32 devices in a mesh: exp: 8 (over z, y), fsdp: 4 (over x, core).
Axes of the slice: x: 2, y: 2, z: 4, core: 2. Of those that a mesh axis runs over, the one named last changes fastest.
Arguments:
- tokens: bfloat16 [12288, 768], P(('exp', 'fsdp')), may hold values from -6 to 6
- cotangent: bfloat16 [12288, 768], P(('exp', 'fsdp')), may hold values from -6 to 6
- segments: int32 [12288], P('exp'), may hold values from 0 to 31, as said below
- routes: int32 [12288, 2], P(('exp', 'fsdp')), may hold values from 0 to 15, as said below
- slots: int32 [12288, 2], P(('exp', 'fsdp')), may hold values from 0 to 95, as said below
- attention_gain: bfloat16 [768], P(('exp', 'fsdp')), may hold values from 0.5 to 1.5
- mixture_gain: bfloat16 [768], P(('exp', 'fsdp')), may hold values from 0.5 to 1.5
- attention_in: bfloat16 [768, 2304], P(('exp', 'fsdp')), may hold values from -0.21875 to 0.21875
- attention_out: bfloat16 [768, 768], P(('exp', 'fsdp')), may hold values from -1.75 to 1.75
- router_weight: bfloat16 [768, 16], P(('exp', 'fsdp')), may hold values from -1 to 1
- position_table: bfloat16 [256, 12], P(('exp', 'fsdp')), may hold values from -4 to 4
- expert_up: bfloat16 [16, 768, 3072], P('exp', 'fsdp'), may hold values from -0.21875 to 0.21875
- expert_down: bfloat16 [16, 3072, 768], P('exp', 'fsdp'), may hold values from -0.109375 to 0.109375
Outputs:
- layer_output: bfloat16 [12288, 768], P(('exp', 'fsdp'))
- balance_loss: float32 [], replicated
- grad_tokens: float32 [12288, 768], P(('exp', 'fsdp'))
- grad_attention_gain: float32 [768], P(('exp', 'fsdp'))
- grad_mixture_gain: float32 [768], P(('exp', 'fsdp'))
- grad_attention_in: float32 [768, 2304], P(('exp', 'fsdp'))
- grad_attention_out: float32 [768, 768], P(('exp', 'fsdp'))
- grad_router_weight: float32 [768, 16], P(('exp', 'fsdp'))
- grad_position_table: float32 [256, 12], P(('exp', 'fsdp'))
- grad_expert_up: float32 [16, 768, 3072], P('exp', 'fsdp')
- grad_expert_down: float32 [16, 3072, 768], P('exp', 'fsdp')
The draws below stay inside these ranges and needn't reach their ends.
Inputs may be any that keep to these rules, and one draw needn't show every extreme that they name: segments never fall; token p of sequence s (the 1536 tokens from s * 1536 on) has 4 * s plus the number of its sequence's document starts after the first token at or before p, of which there are at most three; in every draw one sequence other than the last is a single document. `routes`: each token names two different experts; among the 384 tokens of one device no expert is named more than 96 times, and one expert, the same on every device, is named exactly 96 times on every device. slots[t, k] counts the earlier pairs (token, choice) of the same device, in the order of tokens and then choices, that name the expert routes[t, k].
All inputs are finite; a program needn't handle non-finite values.
Results may differ from the reference program's by a relative error of at most 0.014.
Values may be sent and summed in bfloat16 or wider, within the bound.
A program may use at most 192 MiB of HBM per device.

```python
import jax
import jax.numpy as jnp
from jax import lax

D = 768
HEADS = 12
HEAD_DIM = 64
FF = 3072
TOP = 2
WINDOW = 1024
BUCKETS = 256
TOK_DEV = 384
EXPERTS = 16
CAP = 96
LENGTH = 1536
TOKENS = 12288


def expert_order(key):
    return jax.random.permutation(jax.random.fold_in(key, 11), EXPERTS).astype(jnp.int32)


def route_table(key):
    blocks = TOK_DEV * 0 + TOKENS // TOK_DEV
    half_capacity = CAP // 2
    pair_count = EXPERTS // 2
    order = expert_order(key)
    draw_keys = jax.random.split(key, 4)
    jitter = jax.random.randint(draw_keys[0], (blocks, pair_count), -1, 2)
    block_range = jnp.arange(blocks, dtype=jnp.int32)[:, None]
    trend = -half_capacity + 2 * half_capacity * block_range // max(blocks - 1, 1)
    load_moves = jnp.clip(trend + jitter, -half_capacity, half_capacity)
    load_moves = load_moves.at[:, 0].set(half_capacity)
    load_counts = jnp.stack([half_capacity + load_moves, half_capacity - load_moves], axis=2)
    load_counts = load_counts.at[0, 0, 1].set(1)
    load_counts = load_counts.at[0, 1, 0].set(half_capacity - 1)
    load_counts = load_counts.at[0, 1, 1].set(half_capacity)
    load_counts = load_counts.reshape(blocks, EXPERTS)
    bounds = jnp.cumsum(load_counts, axis=1)
    positions = jnp.arange(2 * TOK_DEV, dtype=jnp.int32)
    labels = jnp.sum((bounds[:, None, :] <= positions[None, :, None]).astype(jnp.int32), axis=2)
    named_experts = order[labels]
    picks = jnp.stack([named_experts[:, :TOK_DEV], named_experts[:, TOK_DEV:]], axis=2)
    token_keys = jax.random.split(draw_keys[3], blocks)
    token_order = jax.vmap(lambda block_key: jax.random.permutation(block_key, TOK_DEV))(token_keys).astype(jnp.int32)
    picks = jnp.take_along_axis(picks, token_order[:, :, None], axis=1)
    flat_routes = picks.reshape(blocks, 2 * TOK_DEV)
    route_select = (flat_routes[:, :, None] == jnp.arange(EXPERTS, dtype=jnp.int32)[None, None, :]).astype(jnp.int32)
    earlier = jnp.cumsum(route_select, axis=1) - route_select
    slot_values = jnp.sum(earlier * route_select, axis=2)
    return (picks.reshape(TOKENS, 2).astype(jnp.int32), slot_values.reshape(TOKENS, 2).astype(jnp.int32))


def draw_routes(key, part):
    return route_table(key)[0]


def draw_slots(key, part):
    return route_table(key)[1]


def column_scales(key, high, low_scale):
    order = expert_order(key)
    rank = jnp.argsort(order).astype(jnp.int32)
    return jnp.where(rank % 2 == 0, high, low_scale).astype(jnp.float32)


def draw_router_weight(key, part):
    scales = column_scales(key, 1.0, 0.35)
    key = jax.random.fold_in(key, 5)
    values = jnp.clip(jax.random.normal(key, (D, EXPERTS), jnp.float32), -3.0, 3.0)
    return (values * scales[None, :] * D ** (-0.5)).astype(jnp.bfloat16)


def draw_segments(key, part):
    key = jax.random.fold_in(key, 7)
    sequences = TOKENS // LENGTH
    cut_key, pick_key = jax.random.split(key)
    cuts = jax.random.randint(cut_key, (sequences, 3), 1, LENGTH)
    single = jax.random.randint(pick_key, (), 0, sequences - 1)
    cuts = jnp.where((jnp.arange(sequences, dtype=jnp.int32) == single)[:, None], LENGTH, cuts)
    positions = jnp.arange(LENGTH, dtype=jnp.int32)
    inside = jnp.sum((positions[None, :, None] >= cuts[:, None, :]).astype(jnp.int32), axis=2)
    return (inside + 4 * jnp.arange(sequences, dtype=jnp.int32)[:, None]).reshape(TOKENS).astype(jnp.int32)


def block_levels(rng, shape, shards, smallest, largest):
    loudness = 1.0
    for dim, blocks in shards:
        heights = jax.random.uniform(jax.random.fold_in(jax.random.fold_in(rng, 6), dim), (blocks,), jnp.float32, smallest / len(shards), largest / len(shards))
        loudness = loudness * jnp.repeat(jnp.exp(heights), shape[dim] // blocks).reshape((-1,) + (1,) * (len(shape) - 1 - dim))
    return loudness


def bell_draw(rng, shape, deviation, reach, cuts=(), kind=jnp.bfloat16):
    drawn = jax.random.normal(rng, shape, jnp.float32) * deviation
    if len(cuts) > 0:
        drawn = block_levels(rng, shape, cuts, -0.22, 0.18) * drawn
    return jnp.clip(drawn, min=-reach, max=reach).astype(kind)


def setup_inputs(seed: int = 0) -> dict:
    seeds = jax.random.split(jax.random.key(seed), 14)
    return {
        "tokens": bell_draw(seeds[0], (TOKENS, D), 1.0, 6.0, ((0, 32),)),
        "cotangent": bell_draw(seeds[1], (TOKENS, D), 1.0, 6.0, ((0, 32),)),
        "segments": draw_segments(jax.random.fold_in(seeds[13], 71), 0),
        "routes": draw_routes(jax.random.fold_in(seeds[13], 71), 0),
        "slots": draw_slots(jax.random.fold_in(seeds[13], 71), 0),
        "attention_gain": jnp.clip(1.0 + 0.1 * jax.random.normal(seeds[5], (D,), jnp.float32), 0.5, 1.5).astype(jnp.bfloat16),
        "mixture_gain": jnp.clip(1.0 + 0.1 * jax.random.normal(seeds[6], (D,), jnp.float32), 0.5, 1.5).astype(jnp.bfloat16),
        "attention_in": bell_draw(seeds[7], (D, 3 * D), D ** -0.5, 0.21875, ((0, 32),)),
        "attention_out": bell_draw(seeds[8], (D, D), (max(D * 16 // WINDOW, 1)) ** -0.5, 1.75, ((0, 32),)),
        "router_weight": draw_router_weight(jax.random.fold_in(seeds[13], 71), 0),
        "position_table": bell_draw(seeds[10], (BUCKETS, HEADS), 1.0, 4.0, ((0, 32),)),
        "expert_up": bell_draw(seeds[11], (EXPERTS, D, FF), D ** -0.5, 0.21875, ((0, 8), (1, 4))),
        "expert_down": bell_draw(seeds[12], (EXPERTS, FF, D), FF ** -0.5, 0.109375, ((0, 8), (1, 4))),
    }


AUX_WEIGHT = 0.01
EPSILON = 1e-06
MASKED = -1e+30

@jax.custom_vjp
def low(v):
    return lax.optimization_barrier(v.astype(jnp.bfloat16)).astype(jnp.float32)

@jax.custom_vjp
def low_back(v):
    return v

def low_keep(v):
    return (low(v), None)

def low_pass(kept, grad):
    return (grad,)

def back_keep(v):
    return (v, None)

def back_low(kept, grad):
    return (low(grad),)
low.defvjp(low_keep, low_pass)
low_back.defvjp(back_keep, back_low)

def product(left_side, right_side):
    return jnp.dot(left_side, right_side, precision=lax.Precision.HIGHEST)

def rms_scale(values):
    return lax.rsqrt(lax.optimization_barrier(jnp.mean(values * values, axis=-1, keepdims=True)) + EPSILON)

def bucket_index(distance):
    near_count = BUCKETS // 2
    spread = max(WINDOW - near_count, 1)
    far_bucket = near_count + jnp.maximum(distance - near_count, 0) * (BUCKETS - near_count) // spread
    return jnp.where(distance < near_count, distance, far_bucket)

def attend_block(query_block, key_block, value_block, query_segments, key_segments, table):
    distance = jnp.arange(query_block.shape[0], dtype=jnp.int32)[:, None] - jnp.arange(key_block.shape[0], dtype=jnp.int32)[None, :] + WINDOW
    allowed = (distance >= 0) & (distance < WINDOW) & (query_segments[:, None] == key_segments[None, :])
    biases = jnp.transpose(table[bucket_index(jnp.clip(distance, 0, WINDOW - 1))], (2, 0, 1))
    scores = jnp.einsum('qhd,khd->hqk', query_block, key_block, precision=lax.Precision.HIGHEST) * HEAD_DIM ** (-0.5) + biases
    scores = jnp.where(allowed[None], low_back(scores), MASKED)
    shifted = jnp.exp(scores - lax.optimization_barrier(jnp.max(scores, axis=-1, keepdims=True)))
    weights = shifted / lax.optimization_barrier(jnp.sum(shifted, axis=-1, keepdims=True))
    return jnp.einsum('hqk,khd->qhd', low(weights), value_block, precision=lax.Precision.HIGHEST)

def attend_sequence(query_seq, key_seq, value_seq, seq_segments, table):
    block_rows = min(TOK_DEV, 512)
    key_rows = WINDOW + block_rows
    padded_keys = jnp.concatenate([jnp.zeros((WINDOW, HEADS, HEAD_DIM), jnp.float32), key_seq])
    padded_values = jnp.concatenate([jnp.zeros((WINDOW, HEADS, HEAD_DIM), jnp.float32), value_seq])
    padded_segments = jnp.concatenate([jnp.full((WINDOW,), -1, jnp.int32), seq_segments.astype(jnp.int32)])

    def one_block(row_start):
        return attend_block(lax.dynamic_slice_in_dim(query_seq, row_start, block_rows, 0), lax.dynamic_slice_in_dim(padded_keys, row_start, key_rows, 0), lax.dynamic_slice_in_dim(padded_values, row_start, key_rows, 0), lax.dynamic_slice_in_dim(padded_segments, row_start + WINDOW, block_rows, 0), lax.dynamic_slice_in_dim(padded_segments, row_start, key_rows, 0), table)
    starts = jnp.arange(LENGTH // block_rows, dtype=jnp.int32) * block_rows
    return lax.map(jax.checkpoint(one_block), starts).reshape(LENGTH, HEADS, HEAD_DIM)

def layer_forward(inputs, attention_gain, mixture_gain, attention_in, attention_out, router_weight, position_table, expert_up, expert_down, segments, routes, slots):
    normed = low(inputs * rms_scale(inputs) * attention_gain)
    projected = low_back(low(product(normed, attention_in)))
    sequences = TOKENS // LENGTH
    shaped = projected.reshape(sequences, LENGTH, 3, HEADS, HEAD_DIM)

    def per_sequence(bundle):
        return attend_sequence(bundle[0][:, 0], bundle[0][:, 1], bundle[0][:, 2], bundle[1], position_table)
    context = lax.map(per_sequence, (shaped, segments.reshape(sequences, LENGTH)))
    attended = low_back(low(context.reshape(TOKENS, D)))
    hidden_state = inputs + low_back(product(attended, attention_out))
    routed = low(hidden_state * rms_scale(hidden_state) * mixture_gain)
    logits = low_back(product(routed, router_weight))
    probabilities = jax.nn.softmax(logits, axis=-1)
    chosen = jnp.take_along_axis(probabilities, routes, axis=1)
    gate_values = chosen / lax.optimization_barrier(jnp.sum(chosen, axis=1, keepdims=True))
    columns = (jnp.arange(TOKENS, dtype=jnp.int32) // TOK_DEV)[:, None] * CAP + slots
    buffers = jnp.zeros((EXPERTS, TOKENS // TOK_DEV * CAP, D), jnp.float32)
    buffers = low_back(buffers.at[routes, columns].add(jnp.broadcast_to(routed[:, None, :], (TOKENS, TOP, D))))

    def expert_apply(operands):
        expert_rows, first_weight, second_weight = operands
        expert_hidden = low_back(product(expert_rows, first_weight))
        activated = low(jax.nn.gelu(expert_hidden, approximate=False))
        return low_back(low(product(activated, second_weight)))
    returned = lax.map(jax.checkpoint(expert_apply), (buffers, expert_up, expert_down))
    mixture = lax.optimization_barrier(jnp.sum(gate_values[:, :, None] * returned[routes, columns], axis=1))
    counts = lax.optimization_barrier(jnp.sum((routes[:, :, None] == jnp.arange(EXPERTS, dtype=jnp.int32)[None, None, :]).astype(jnp.float32), axis=(0, 1)))
    balance = EXPERTS * jnp.sum(counts / (TOKENS * TOP) * lax.optimization_barrier(jnp.mean(probabilities, axis=0)))
    return (hidden_state + mixture, balance)

def reference(tokens, cotangent, segments, routes, slots, attention_gain, mixture_gain, attention_in, attention_out, router_weight, position_table, expert_up, expert_down):
    floats = tuple((array.astype(jnp.float32) for array in (tokens, attention_gain, mixture_gain, attention_in, attention_out, router_weight, position_table, expert_up, expert_down)))

    def forward_only(*values):
        return layer_forward(*values, segments, routes, slots)
    (outputs, balance), pullback = jax.vjp(forward_only, *floats)
    gradients = pullback((cotangent.astype(jnp.float32), jnp.asarray(AUX_WEIGHT, jnp.float32)))
    return (outputs.astype(jnp.bfloat16), balance, gradients[0], gradients[1], gradients[2], gradients[3], gradients[4], gradients[5], gradients[6], gradients[7], gradients[8])
```

```python
from functools import partial

import jax
import jax.numpy as jnp
from jax import lax
from jax.experimental import pallas as pl
from jax.experimental.pallas import tpu as pltpu
from jax.sharding import PartitionSpec as P

WINDOW = 1024
BUCKETS = 256

EPSILON = 1e-06
AUX_WEIGHT = 0.01
MASKED = -1e30
QUERY_BLOCK = 256
SKEW = 128
VMEM_BYTES = 58 * 1024 * 1024
MESH = pl.DeviceIdType.MESH
F32 = jnp.float32
BF16 = jnp.bfloat16


def params(**kwargs):
    return pltpu.CompilerParams(vmem_limit_bytes=VMEM_BYTES, **kwargs)


def shape_of(shape, dtype):
    return jax.ShapeDtypeStruct(shape, dtype)


def whole(shape):
    return pl.BlockSpec(shape, lambda *_: (0,) * len(shape))


def contract_last(left_side, right_side):
    return lax.dot_general(
        left_side, right_side, (((1,), (1,)), ((), ())), preferred_element_type=F32
    )


def matmul(left_side, right_side):
    return jnp.dot(left_side, right_side, preferred_element_type=F32)


def turned(value):
    return value.astype(F32).T


def bucket_index(distance):
    near_count = BUCKETS // 2
    spread = max(WINDOW - near_count, 1)
    far_bucket = (
        near_count + jnp.maximum(distance - near_count, 0) * (BUCKETS - near_count) // spread
    )
    return jnp.where(distance < near_count, distance, far_bucket)


def exchange(modes, arrays, collective_id):
    exp_size, fsdp_size = lax.axis_size("exp"), lax.axis_size("fsdp")
    sizes = {"all": exp_size * fsdp_size, "exp": exp_size, "fsdp": fsdp_size}
    count = len(modes)
    out_shapes = []
    for (group, kind), array in zip(modes, arrays):
        plane = array.shape if kind == "whole" else array.shape[1:]
        out_shapes.append(shape_of((sizes[group],) + plane, array.dtype))
    groups = [group for group, _ in modes]
    greeted = ["all"] if "all" in groups else sorted(set(groups))

    def kernel(*refs):
        sources, targets = refs[:count], refs[count : 2 * count]
        send_sem, recv_sem, own_sem = refs[2 * count :]
        exp_index, fsdp_index = lax.axis_index("exp"), lax.axis_index("fsdp")
        places = {
            "all": exp_index * fsdp_size + fsdp_index,
            "exp": exp_index,
            "fsdp": fsdp_index,
        }

        def device(group, place):
            if group == "all":
                return (place // fsdp_size, place % fsdp_size)
            if group == "exp":
                return (place, fsdp_index)
            return (exp_index, place)

        def plane(index, place):
            kind = modes[index][1]
            if kind == "whole":
                return sources[index]
            if kind == "plane":
                return sources[index].at[place]
            return sources[index].at[place % fsdp_size]

        def copy(index, hop):
            group = modes[index][0]
            size = sizes[group]
            to = (places[group] + hop) % size
            return pltpu.make_async_remote_copy(
                src_ref=plane(index, to),
                dst_ref=targets[index].at[places[group]],
                send_sem=send_sem.at[index, hop],
                recv_sem=recv_sem.at[index, hop],
                device_id=device(group, to),
                device_id_type=MESH,
            )

        def arrival(index, hop):
            group = modes[index][0]
            size = sizes[group]
            source = (places[group] + size - hop) % size
            return pltpu.make_async_remote_copy(
                src_ref=plane(index, source),
                dst_ref=targets[index].at[source],
                send_sem=send_sem.at[index, hop],
                recv_sem=recv_sem.at[index, hop],
                device_id=device(group, source),
                device_id_type=MESH,
            )

        barrier = pltpu.get_barrier_semaphore()
        total = 0
        for group in greeted:
            size = sizes[group]

            def greet(hop, carry, group=group, size=size):
                to = (places[group] + hop) % size
                pl.semaphore_signal(
                    barrier, inc=1, device_id=device(group, to), device_id_type=MESH
                )
                return carry

            lax.fori_loop(1, size, greet, 0)
            total += size - 1
        pl.semaphore_wait(barrier, total)

        own = []
        for index in range(count):
            group = modes[index][0]

            def begin(hop, carry, index=index):
                copy(index, hop).start()
                return carry

            lax.fori_loop(1, sizes[group], begin, 0)
            own.append(
                pltpu.make_async_copy(
                    plane(index, places[group]),
                    targets[index].at[places[group]],
                    own_sem.at[index],
                )
            )
            own[-1].start()
        for index in range(count):
            group = modes[index][0]

            def finish(hop, carry, index=index):
                copy(index, hop).wait_send()
                arrival(index, hop).wait_recv()
                return carry

            lax.fori_loop(1, sizes[group], finish, 0)
            own[index].wait()

    most = max(sizes[group] for group in groups)
    return pl.pallas_call(
        kernel,
        out_shape=tuple(out_shapes),
        in_specs=[pl.BlockSpec(memory_space=pl.ANY)] * count,
        out_specs=tuple([pl.BlockSpec(memory_space=pl.ANY)] * count),
        scratch_shapes=[
            pltpu.SemaphoreType.DMA((count, most)),
            pltpu.SemaphoreType.DMA((count, most)),
            pltpu.SemaphoreType.DMA((count,)),
        ],
        compiler_params=pltpu.CompilerParams(collective_id=collective_id, has_side_effects=True),
        name=f"exchange_{collective_id}",
    )(*arrays)


def project_kernel(
    tokens, weight, segments, normed, query_t, key_n, query_n, value_n, key_t, value_t, weight_t,
    *, heads, width,
):
    @pl.when(pl.program_id(0) == 0)
    def _():
        weight_t[...] = turned(weight[...]).astype(BF16)

    inputs = tokens[0].astype(F32)
    scale = lax.rsqrt(jnp.mean(inputs * inputs, axis=1, keepdims=True) + EPSILON)
    low = (inputs * scale).astype(BF16)
    normed[...] = low
    rows = low.shape[0]
    projected = contract_last(weight_t[...], low).astype(BF16).astype(F32)
    document = segments[...] % 4
    places = lax.broadcasted_iota(jnp.int32, (8, rows), 0)
    same = places == document
    hot = jnp.where(same, 1.0, 0.0)
    barred = jnp.where(same | (places >= 4), 0.0, MASKED)
    filler = jnp.zeros((SKEW - 8 - width, rows), F32)
    for head in range(heads):
        query = projected[head * width : (head + 1) * width] * width ** (-0.5)
        key = projected[(heads + head) * width : (heads + head + 1) * width]
        value = projected[(2 * heads + head) * width : (2 * heads + head + 1) * width]
        query_t[head] = jnp.concatenate([query, barred, filler], axis=0).astype(BF16)
        key_n[head] = jnp.concatenate([key, hot, filler], axis=0).T.astype(BF16)
        query_n[head] = query.T.astype(BF16)
        value_n[head] = value.T.astype(BF16)
        key_t[head] = key.astype(BF16)
        value_t[head] = value.astype(BF16)


def spans(length):
    for query_start in range(0, length, QUERY_BLOCK):
        key_start = max(0, query_start - WINDOW)
        yield query_start, key_start, query_start + QUERY_BLOCK - key_start


def spread_bias(bias, skew):
    skew[...] = pltpu.roll(
        jnp.broadcast_to(bias[0], skew.shape), 0, 1, stride=1, stride_axis=0
    )


def attend_kernel(query_t, key_n, value_t, bias, context, context_high, log_total, skew, scores, *, rows):
    spread_bias(bias, skew)
    for query_start, key_start, key_count in spans(query_t.shape[2]):
        queries = slice(query_start, query_start + QUERY_BLOCK)
        keys = slice(key_start, key_start + key_count)
        raw = matmul(key_n[0, keys, :], query_t[0, :, queries])
        for start in range(0, key_count, SKEW):
            offset = query_start - key_start - start + SKEW
            scores[start : start + SKEW, :] = (
                raw[start : start + SKEW] + skew[:, offset : offset + QUERY_BLOCK]
            )
        high = jnp.max(scores[:key_count, :], axis=0, keepdims=True)
        weights = jnp.exp(scores[:key_count, :] - high)
        total = jnp.sum(weights, axis=0, keepdims=True)
        gathered = matmul(value_t[0, :, keys], weights.astype(BF16)) / total
        context_high[0, :, queries] = gathered
        log_total[0, :, queries] = high + jnp.log(total)
        for start in range(0, QUERY_BLOCK, 128):
            place = query_start + start
            context[place // rows, :, place % rows : place % rows + 128] = gathered[
                :, start : start + 128
            ].astype(BF16)


def attend_back_kernel(
    query_t, key_n, query_n, value_n, key_t, grad_t, grad_n, context_high, log_total, bias,
    grad_projected, grad_bias, skew, grad_skew, grad_key, grad_value, *, scale,
):
    spread_bias(bias, skew)
    grad_skew[...] = jnp.zeros_like(grad_skew)
    grad_key[...] = jnp.zeros_like(grad_key)
    grad_value[...] = jnp.zeros_like(grad_value)
    inner = jnp.sum(grad_t[0].astype(F32) * context_high[0], axis=0, keepdims=True)
    for query_start, key_start, key_count in spans(query_t.shape[2]):
        queries = slice(query_start, query_start + QUERY_BLOCK)
        keys = slice(key_start, key_start + key_count)
        raw = matmul(key_n[0, keys, :], query_t[0, :, queries])
        grad_weights = matmul(value_n[0, keys, :], grad_t[0, :, queries])
        weights_low, grad_low = [], []
        for start in range(0, key_count, SKEW):
            offset = query_start - key_start - start + SKEW
            part = slice(start, start + SKEW)
            weights = jnp.exp(
                raw[part] + skew[:, offset : offset + QUERY_BLOCK] - log_total[0, :, queries]
            )
            grad_scores = weights * (grad_weights[part] - inner[:, queries])
            grad_skew[:, offset : offset + QUERY_BLOCK] += grad_scores
            weights_low.append(weights.astype(BF16))
            grad_low.append(grad_scores.astype(BF16))
        weights_low = jnp.concatenate(weights_low, axis=0)
        grad_low = jnp.concatenate(grad_low, axis=0)
        grad_projected[0, 0, :, queries] = (matmul(key_t[0, :, keys], grad_low) * scale).astype(BF16)
        grad_key[keys, :] += matmul(grad_low, query_n[0, queries, :])
        grad_value[keys, :] += matmul(weights_low, grad_n[0, queries, :])
    grad_projected[1, 0] = grad_key[...].T.astype(BF16)
    grad_projected[2, 0] = grad_value[...].T.astype(BF16)
    count = SKEW
    span = skew.shape[1]
    while count > 8:
        count //= 2
        grad_skew[:count, :] += pltpu.roll(grad_skew[count : 2 * count, :], span - count, 1)
    summed = grad_skew[0:1, :]
    for row in range(1, 8):
        summed = summed + pltpu.roll(grad_skew[row : row + 1, :], span - row, 1)
    grad_bias[0] = summed


def route_kernel(
    tokens, attended_t, attention_out, gain, router, routes, positions, position_rows,
    hidden, routed, probabilities, gates, outgoing, slot_gates, attended, *, experts,
):
    rows = tokens.shape[0]
    attended_low = turned(attended_t[...]).astype(BF16)
    attended[...] = attended_low
    hidden_state = tokens[...].astype(F32) + matmul(attended_low, attention_out[...])
    hidden[...] = hidden_state
    scale = lax.rsqrt(jnp.mean(hidden_state * hidden_state, axis=1, keepdims=True) + EPSILON)
    low = (hidden_state * scale * gain[...]).astype(BF16)
    routed[...] = low
    logits = matmul(low, router[...])
    lanes = lax.broadcasted_iota(jnp.int32, logits.shape, 1)
    logits = jnp.where(lanes < experts, logits, MASKED)
    powers = jnp.exp(logits - jnp.max(logits, axis=1, keepdims=True))
    powers = powers / jnp.sum(powers, axis=1, keepdims=True)
    probabilities[...] = powers
    chosen = [
        jnp.sum(jnp.where(lanes == routes[:, k : k + 1], powers, 0.0), axis=1, keepdims=True)
        for k in range(2)
    ]
    total = chosen[0] + chosen[1]
    gate_values = [chosen[k] / total for k in range(2)]
    pair = lax.broadcasted_iota(jnp.int32, (rows, 2), 1)
    gates[...] = jnp.where(pair == 0, gate_values[0], gate_values[1])
    slot_count = outgoing.shape[0]
    slot_lanes = lax.broadcasted_iota(jnp.int32, (rows, slot_count), 1)
    by_slot = jnp.zeros((rows, slot_count), F32)
    for k in range(2):
        by_slot = by_slot + jnp.where(slot_lanes == positions[:, k : k + 1], gate_values[k], 0.0)
    slot_gates[...] = jnp.sum(by_slot, axis=0, keepdims=True)
    select_rows(outgoing, position_rows, low)


def select_rows(outgoing, position_rows, values):
    slot_count, rows = outgoing.shape[0], values.shape[0]
    for start in range(0, slot_count, rows):
        slots = lax.broadcasted_iota(jnp.int32, (rows, rows), 0) + start
        picked = (slots == position_rows[0:1, :]) | (slots == position_rows[1:2, :])
        outgoing[start : start + rows, :] = matmul(
            jnp.where(picked, 1.0, 0.0).astype(BF16), values
        ).astype(BF16)


def select_kernel(values, position_rows, outgoing):
    select_rows(outgoing, position_rows, values[...])


def gelu_parts(value):
    magnitude = jnp.abs(value)
    power = jnp.exp(value * value * -0.5)
    step = 1.0 / (1.0 + (0.3275911 * 0.7071067811865476) * magnitude)
    series = step * (
        0.127414796
        + step * (-0.142248368 + step * (0.7107068705 + step * (-0.7265760135 + step * 0.5307027145)))
    )
    tail = series * power
    normal = jnp.where(value < 0.0, tail, 1.0 - tail)
    return value * normal, normal + value * power * 0.3989422804014327


def expert_kernel(
    owners, rows_in, cotangent, gates, *refs, shards,
):
    ups, downs = refs[:shards], refs[shards : 2 * shards]
    half = shards // 2
    rest = refs[2 * shards :]
    rows_out, grad_rows, grad_gates, up_keep, up_give, down_keep, down_give = rest[:7]
    up_all, down_all, rows_t, slot_t, slot_grad, total, grad_total, grad_up = rest[7:]
    step = pl.program_id(0)
    blocks, capacity, model_width = rows_in.shape[0], rows_in.shape[2], rows_in.shape[3]
    count = blocks * capacity
    depth = ups[0].shape[0]
    rows = rows_in[:, 0].reshape(count, model_width)

    @pl.when(step == 0)
    def _():
        rows_t[...] = turned(rows).astype(BF16)
        slot_values = gates[...] * cotangent[0].astype(F32)
        slot_grad[...] = slot_values.astype(BF16)
        slot_t[...] = slot_values.T.astype(BF16)
        total[...] = jnp.zeros_like(total)
        grad_total[...] = jnp.zeros_like(grad_total)

    for shard in range(shards):
        start = pl.multiple_of(owners[shard] * depth, 16)
        up_all[pl.ds(start, depth), :] = ups[shard][...]

        @pl.when(step == shard)
        def _(shard=shard):
            down_all[...] = downs[shard][...]

    up, down = up_all[...], down_all[...]
    hidden = matmul(rows, up)
    grad_active = contract_last(slot_grad[...], down)
    activated, slope = gelu_parts(hidden)
    active_low = activated.astype(BF16)
    grad_hidden = (grad_active * slope).astype(BF16)
    total[...] += matmul(active_low, down)
    grad_total[...] += contract_last(grad_hidden, up)
    grad_up[...] = matmul(rows_t[...], grad_hidden).astype(BF16)
    grad_down = matmul(slot_t[...], active_low).T.astype(BF16)
    for shard in range(shards):
        start = pl.multiple_of(owners[shard] * depth, 16)
        target = up_keep if shard < half else up_give
        target[shard % half] = grad_up[pl.ds(start, depth), :]

    @pl.when(step < half)
    def _():
        down_keep[0] = grad_down

    @pl.when(step >= half)
    def _():
        down_give[0] = grad_down

    @pl.when(step == shards - 1)
    def _():
        low = total[...].astype(BF16)
        rows_out[...] = low.reshape(rows_out.shape)
        grad_rows[...] = grad_total[...].astype(BF16).reshape(grad_rows.shape)
        grad_gates[...] = jnp.sum(low.astype(F32) * cotangent[0].astype(F32), axis=1, keepdims=True)


def run_expert(expert, owners, incoming, cotangent, gates, ups, downs):
    shards = len(ups)
    half = shards // 2
    blocks, _, capacity, model_width = incoming.shape
    depth, hidden_width = ups[0].shape
    part = downs[0].shape[0]
    count = blocks * capacity
    grid_spec = pltpu.PrefetchScalarGridSpec(
        num_scalar_prefetch=1,
        grid=(shards,),
        in_specs=[
            pl.BlockSpec((blocks, 1, capacity, model_width), lambda s, o: (0, expert, 0, 0)),
            pl.BlockSpec((1, count, model_width), lambda s, o: (expert, 0, 0)),
            pl.BlockSpec((count, 1), lambda s, o: (0, 0)),
        ]
        + [pl.BlockSpec((depth, part), lambda s, o: (0, o[s]))] * shards
        + [pl.BlockSpec((part, model_width), lambda s, o: (0, 0))] * shards,
        out_specs=[
            pl.BlockSpec((blocks, capacity, model_width), lambda s, o: (0, 0, 0)),
            pl.BlockSpec((blocks, capacity, model_width), lambda s, o: (0, 0, 0)),
            pl.BlockSpec((count, 1), lambda s, o: (0, 0)),
            pl.BlockSpec((half, depth, part), lambda s, o: (0, 0, o[s])),
            pl.BlockSpec((half, depth, part), lambda s, o: (0, 0, o[s])),
            pl.BlockSpec((1, part, model_width), lambda s, o: (jnp.minimum(s, half - 1), 0, 0)),
            pl.BlockSpec((1, part, model_width), lambda s, o: (jnp.maximum(s - half, 0), 0, 0)),
        ],
        scratch_shapes=[
            pltpu.VMEM((model_width, part), BF16),
            pltpu.VMEM((part, model_width), BF16),
            pltpu.VMEM((model_width, count), BF16),
            pltpu.VMEM((model_width, count), BF16),
            pltpu.VMEM((count, model_width), BF16),
            pltpu.VMEM((count, model_width), F32),
            pltpu.VMEM((count, model_width), F32),
            pltpu.VMEM((model_width, part), BF16),
        ],
    )
    flops = 12 * count * model_width * hidden_width
    return pl.pallas_call(
        partial(expert_kernel, shards=shards),
        grid_spec=grid_spec,
        out_shape=(
            shape_of((blocks, capacity, model_width), BF16),
            shape_of((blocks, capacity, model_width), BF16),
            shape_of((count, 1), F32),
            shape_of((half, depth, hidden_width), BF16),
            shape_of((half, depth, hidden_width), BF16),
            shape_of((half, part, model_width), BF16),
            shape_of((half, part, model_width), BF16),
        ),
        compiler_params=params(),
        cost_estimate=pl.CostEstimate(
            flops=flops, bytes_accessed=24 * 1024 * 1024, transcendentals=count * hidden_width
        ),
        name=f"expert_{expert}",
    )(owners, incoming, cotangent, gates, *ups, *downs)


def unroute_kernel(
    hidden, cotangent, routed, probabilities, gates, attended, router, attention_out, gain, routes,
    counts, positions, *refs, experts, local, token_total,
):
    slots, slot_gates = refs[:local], refs[local : 2 * local]
    grad_hidden, grad_branch, small = refs[2 * local :]
    rows = hidden.shape[0]
    lanes = lax.broadcasted_iota(jnp.int32, probabilities.shape, 1)
    grad_output = cotangent[...].astype(F32)
    slot_count = slots[0].shape[0]
    slot_lanes = lax.broadcasted_iota(jnp.int32, (rows, slot_count), 1)
    grad_routed = jnp.zeros(hidden.shape, F32)
    grad_gates = [jnp.zeros((rows, 1), F32), jnp.zeros((rows, 1), F32)]
    for index in range(local):
        picks = [
            slot_lanes == positions[:, 2 * index + k : 2 * index + k + 1] for k in range(2)
        ]
        grad_routed = grad_routed + matmul(
            jnp.where(picks[0] | picks[1], 1.0, 0.0).astype(BF16), slots[index][...]
        )
        for k in range(2):
            grad_gates[k] = grad_gates[k] + jnp.sum(
                jnp.where(picks[k], slot_gates[index][...], 0.0), axis=1, keepdims=True
            )
    powers = probabilities[...]
    picked = [lanes == routes[:, k : k + 1] for k in range(2)]
    chosen_total = sum(
        jnp.sum(jnp.where(picked[k], powers, 0.0), axis=1, keepdims=True) for k in range(2)
    )
    weighted = grad_gates[0] * gates[:, 0:1] + grad_gates[1] * gates[:, 1:2]
    grad_mass = (AUX_WEIGHT * experts / (2.0 * token_total * token_total)) * counts[...]
    for k in range(2):
        grad_mass = grad_mass + jnp.where(picked[k], (grad_gates[k] - weighted) / chosen_total, 0.0)
    grad_logits = powers * (grad_mass - jnp.sum(powers * grad_mass, axis=1, keepdims=True))
    small[...] = matmul(grad_logits.T.astype(BF16), routed[...]).T
    grad_routed = grad_routed + contract_last(grad_logits.astype(BF16), router[...])
    hidden_state = hidden[...]
    scale = lax.rsqrt(jnp.mean(hidden_state * hidden_state, axis=1, keepdims=True) + EPSILON)
    normed = hidden_state * scale
    product = grad_routed * normed
    gain_lanes = lax.broadcasted_iota(jnp.int32, small.shape, 1)
    gain_grad = jnp.sum(product, axis=0, keepdims=True)
    gain_grad = jnp.broadcast_to(gain_grad, (small.shape[1], gain_grad.shape[1])).T
    small[...] = jnp.where(gain_lanes == experts, gain_grad, small[...])
    gains = gain[...]
    grad = scale * (
        grad_routed * gains - normed * jnp.mean(product * gains, axis=1, keepdims=True)
    ) + grad_output
    grad_hidden[...] = grad
    grad_branch[...] = grad.astype(BF16)


def context_grad_kernel(grad_branch, attention_out, context, grad_t, grad_n, grad_out, *, heads, width):
    @pl.when(pl.program_id(0) == 0)
    def _():
        grad_out[...] = jnp.zeros_like(grad_out)

    branch = grad_branch[0]
    grad = contract_last(attention_out[...], branch).astype(BF16)
    for head in range(heads):
        part = grad[head * width : (head + 1) * width]
        grad_t[head] = part
        grad_n[head] = turned(part).astype(BF16)
    grad_out[...] += matmul(context[0], branch)


def project_back_kernel(grad_projected, normed, weight, grad_first, grad_weight, total):
    step = pl.program_id(0)

    @pl.when(step == 0)
    def _():
        total[...] = jnp.zeros_like(total)

    grad = grad_projected[...]
    grad_first[0] = matmul(weight[...], grad).astype(BF16)
    total[...] += matmul(grad, normed[...])

    @pl.when(step == pl.num_programs(0) - 1)
    def _():
        grad_weight[...] = total[...].T.astype(BF16)


def mixture_kernel(hidden, gates, positions, *refs, local):
    slots, output = refs[:local], refs[local]
    rows = hidden.shape[0]
    slot_count = slots[0].shape[0]
    slot_lanes = lax.broadcasted_iota(jnp.int32, (rows, slot_count), 1)
    total = hidden[...]
    for k in range(2):
        picked = jnp.zeros(hidden.shape, F32)
        for index in range(local):
            pick = slot_lanes == positions[:, 2 * index + k : 2 * index + k + 1]
            picked = picked + matmul(jnp.where(pick, 1.0, 0.0).astype(BF16), slots[index][...])
        total = total + gates[:, k : k + 1] * picked
    output[...] = total.astype(BF16)


def finish_kernel(parts, tokens, grad_hidden, grad_tokens):
    total = jnp.sum(parts[...].astype(F32), axis=0).T
    inputs = tokens[...].astype(F32)
    scale = lax.rsqrt(jnp.mean(inputs * inputs, axis=1, keepdims=True) + EPSILON)
    normed = inputs * scale
    grad_tokens[...] = grad_hidden[...] + scale * (
        total - normed * jnp.mean(total * normed, axis=1, keepdims=True)
    )


def over_x(array, hop):
    fsdp_size = lax.axis_size("fsdp")
    return lax.ppermute(array, "fsdp", [(i, (i + 2 * hop) % fsdp_size) for i in range(fsdp_size)])


def over_core(array):
    return lax.ppermute(array, "fsdp", [(i, i ^ 1) for i in range(lax.axis_size("fsdp"))])


def on_device(
    tokens,
    cotangent,
    segments,
    routes,
    slots,
    attention_gain,
    mixture_gain,
    attention_in,
    attention_out,
    router_weight,
    position_table,
    expert_up,
    expert_down,
):
    exp_size, fsdp_size = lax.axis_size("exp"), lax.axis_size("fsdp")
    chips = fsdp_size // 2
    device_count = exp_size * fsdp_size
    fsdp_index = lax.axis_index("fsdp")
    rows, model_width = tokens.shape
    length = rows * fsdp_size
    head_count = position_table.shape[1]
    width = model_width // head_count
    heads = -(-head_count // fsdp_size)
    padded_heads = heads * fsdp_size
    slice_width = 3 * heads * width
    feature_rows, bucket_rows = attention_in.shape[0], position_table.shape[0]
    experts = router_weight.shape[1]
    local = expert_up.shape[0]
    capacity = 4 * rows // experts
    token_total = rows * device_count
    span = WINDOW + 2 * SKEW + QUERY_BLOCK

    gained_in = (attention_gain.astype(F32)[:, None] * attention_in.astype(F32)).astype(BF16)
    planes = jnp.pad(
        gained_in.reshape(feature_rows, 3, head_count, width),
        ((0, 0), (0, 0), (0, padded_heads - head_count), (0, 0)),
    )
    planes = planes.reshape(feature_rows, 3, fsdp_size, heads * width).transpose(2, 0, 1, 3)
    planes = planes.reshape(fsdp_size, feature_rows, slice_width)
    small_rows = -(-(feature_rows + bucket_rows) // 16) * 16
    small = jnp.zeros((small_rows, 128), BF16)
    small = small.at[:feature_rows, :experts].set(router_weight)
    small = small.at[:feature_rows, experts].set(mixture_gain)
    small = small.at[feature_rows : feature_rows + bucket_rows, :head_count].set(position_table)
    expert_range = jnp.arange(128, dtype=jnp.int32)
    own_counts = jnp.sum((routes.reshape(-1, 1) == expert_range[None, :]).astype(F32), axis=0)
    own_counts = jnp.broadcast_to(own_counts[None, :], (8, 128))

    all_tokens, all_planes, all_small, all_counts = exchange(
        [("fsdp", "whole"), ("all", "column"), ("all", "whole"), ("all", "whole")],
        [tokens, planes, small, own_counts],
        0,
    )
    full_out = lax.all_gather(attention_out, ("exp", "fsdp"), axis=0, tiled=True)

    expert_shards = []
    held = (expert_up, expert_down, all_counts)
    expert_up_late, expert_down_late, all_counts = lax.optimization_barrier(held)
    for index in range(local):
        up_shards = [expert_up_late[index]]
        down_shards = [expert_down_late[index]]
        for hop in range(1, chips):
            up_shards.append(over_x(up_shards[0], -hop))
            down_shards.append(over_x(down_shards[0], -hop))
        up_shards = up_shards + [over_core(shard) for shard in up_shards]
        down_shards = down_shards + [over_core(shard) for shard in down_shards]
        expert_shards.append((up_shards, down_shards))
    chip_index, core_index = fsdp_index // 2, fsdp_index % 2
    owners = jnp.stack(
        [
            ((chip_index + hop) % chips) * 2 + (core_index + core) % 2
            for core in range(2)
            for hop in range(chips)
        ]
    ).astype(jnp.int32)

    positions = routes * capacity + slots
    position_rows = positions.T
    late_cotangent, position_rows, all_counts = lax.optimization_barrier(
        (cotangent, position_rows, all_counts)
    )
    cotangent_slots = pl.pallas_call(
        select_kernel,
        out_shape=shape_of((experts * capacity, model_width), BF16),
        compiler_params=params(),
        name="select_cotangent",
    )(late_cotangent, position_rows)
    cotangent_in = lax.all_to_all(
        cotangent_slots.reshape(experts, capacity, model_width),
        "exp", split_axis=0, concat_axis=1, tiled=True,
    )

    weight = all_planes.reshape(model_width, slice_width)
    steps = fsdp_size
    head_t = lambda size: pl.BlockSpec((heads, size, rows), lambda s: (0, 0, s))
    head_n = lambda size: pl.BlockSpec((heads, rows, size), lambda s: (0, s, 0))
    normed, query_t, key_n, query_n, value_n, key_t, value_t = pl.pallas_call(
        partial(project_kernel, heads=heads, width=width),
        grid=(steps,),
        in_specs=[
            pl.BlockSpec((1, rows, model_width), lambda s: (s, 0, 0)),
            whole((model_width, slice_width)),
            pl.BlockSpec((1, rows), lambda s: (0, s)),
        ],
        out_specs=[
            pl.BlockSpec((rows, model_width), lambda s: (s, 0)),
            head_t(SKEW), head_n(SKEW), head_n(width), head_n(width), head_t(width), head_t(width),
        ],
        out_shape=(
            shape_of((length, model_width), BF16),
            shape_of((heads, SKEW, length), BF16),
            shape_of((heads, length, SKEW), BF16),
            shape_of((heads, length, width), BF16),
            shape_of((heads, length, width), BF16),
            shape_of((heads, width, length), BF16),
            shape_of((heads, width, length), BF16),
        ),
        scratch_shapes=[pltpu.VMEM((slice_width, model_width), BF16)],
        compiler_params=params(),
        name="project",
    )(all_tokens, weight, segments.reshape(1, length))

    table = all_small[:, feature_rows : feature_rows + bucket_rows, :head_count]
    table = table.reshape(BUCKETS, head_count)
    table = jnp.pad(table, ((0, 0), (0, padded_heads - head_count)))
    table = lax.dynamic_slice_in_dim(table, fsdp_index * heads, heads, axis=1)
    distance = jnp.arange(span, dtype=jnp.int32) - SKEW
    reachable = (distance >= 0) & (distance < WINDOW)
    bucket_select = (
        (bucket_index(distance)[None, :] == jnp.arange(BUCKETS, dtype=jnp.int32)[:, None])
        & reachable[None, :]
    )
    bias = lax.dot_general(
        table, bucket_select.astype(BF16), (((0,), (0,)), ((), ())), preferred_element_type=F32
    )
    bias = jnp.where(reachable[None, :], bias, MASKED).reshape(heads, 1, span)

    by_head = lambda *size: pl.BlockSpec((1,) + size, lambda h: (h, 0, 0))
    context, context_high, log_total = pl.pallas_call(
        partial(attend_kernel, rows=rows),
        grid=(heads,),
        in_specs=[
            by_head(SKEW, length), by_head(length, SKEW), by_head(width, length), by_head(1, span),
        ],
        out_specs=[
            pl.BlockSpec((fsdp_size, width, rows), lambda h: (0, h, 0)),
            by_head(width, length),
            by_head(1, length),
        ],
        out_shape=(
            shape_of((fsdp_size, heads * width, rows), BF16),
            shape_of((heads, width, length), F32),
            shape_of((heads, 1, length), F32),
        ),
        scratch_shapes=[
            pltpu.VMEM((SKEW, span), F32),
            pltpu.VMEM((WINDOW + QUERY_BLOCK, QUERY_BLOCK), F32),
        ],
        compiler_params=params(),
        name="attend",
    )(query_t, key_n, value_t, bias)

    (attended_t,) = exchange([("fsdp", "plane")], [context], 1)
    attended_t = attended_t.reshape(padded_heads * width, rows)[:model_width]

    router = all_small[:, :feature_rows, :].reshape(model_width, 128)
    gain = router[:, experts].astype(F32).reshape(1, model_width)
    router = jnp.where(expert_range[None, :] < experts, router, jnp.zeros((), BF16))
    hidden, routed, probabilities, gates, outgoing, slot_gates, attended = pl.pallas_call(
        partial(route_kernel, experts=experts),
        out_shape=(
            shape_of((rows, model_width), F32),
            shape_of((rows, model_width), BF16),
            shape_of((rows, 128), F32),
            shape_of((rows, 2), F32),
            shape_of((experts * capacity, model_width), BF16),
            shape_of((1, experts * capacity), F32),
            shape_of((rows, model_width), BF16),
        ),
        compiler_params=params(),
        name="route",
    )(tokens, attended_t, full_out, gain, router, routes, positions, position_rows)

    gate_planes = jnp.broadcast_to(
        slot_gates.reshape(exp_size, 1, local * capacity), (exp_size, 8, local * capacity)
    )
    incoming, gates_in = exchange(
        [("exp", "plane"), ("exp", "plane")],
        [outgoing.reshape(exp_size, local * capacity, model_width), gate_planes],
        2,
    )
    incoming = incoming.reshape(exp_size, local, capacity, model_width)
    gates_in = gates_in[:, 0].reshape(exp_size, local, capacity)

    outs, grads, gate_grads, up_grads, down_grads = [], [], [], [], []
    for index in range(local):
        ups, downs = expert_shards[index]
        out, grad, gate_grad, up_keep, up_give, down_keep, down_give = run_expert(
            index, owners, incoming, cotangent_in,
            gates_in[:, index].reshape(exp_size * capacity, 1), ups, downs,
        )
        outs.append(out)
        grads.append(grad)
        gate_grads.append(
            jnp.broadcast_to(gate_grad.reshape(exp_size, 1, capacity), (exp_size, 8, capacity))
        )
        for keep, give, sums in ((up_keep, up_give, up_grads), (down_keep, down_give, down_grads)):
            taken = over_core(give)
            first = keep[0].astype(F32) + taken[0].astype(F32)
            for hop in range(1, chips):
                passing = (keep[hop].astype(F32) + taken[hop].astype(F32)).astype(BF16)
                first = first + over_x(passing, hop).astype(F32)
            sums.append(first)

    returned = exchange([("exp", "plane")] * (2 * local), grads + gate_grads, 3)
    grad_slots = [part.reshape(exp_size * capacity, model_width) for part in returned[:local]]
    grad_slot_gates = [part[:, 0].reshape(1, exp_size * capacity) for part in returned[local:]]

    members = routes // local
    local_positions = []
    for index in range(local):
        local_positions.append(
            jnp.where(routes % local == index, members * capacity + slots, -1)
        )
    local_positions = jnp.concatenate(local_positions, axis=1)
    counts = jnp.sum(all_counts[:, 0, :], axis=0, keepdims=True)
    grad_hidden, grad_branch, small_grad = pl.pallas_call(
        partial(unroute_kernel, experts=experts, local=local, token_total=token_total),
        out_shape=(
            shape_of((rows, model_width), F32),
            shape_of((rows, model_width), BF16),
            shape_of((model_width, 128), F32),
        ),
        compiler_params=params(),
        name="unroute",
    )(
        hidden, cotangent, routed, probabilities, gates, attended, router, full_out, gain, routes,
        counts, local_positions, *grad_slots, *grad_slot_gates,
    )

    out_slots = [
        lax.all_to_all(out, "exp", split_axis=0, concat_axis=0, tiled=True).reshape(
            exp_size * capacity, model_width
        )
        for out in outs
    ]
    layer_output = pl.pallas_call(
        partial(mixture_kernel, local=local),
        out_shape=shape_of((rows, model_width), BF16),
        compiler_params=params(),
        name="mixture",
    )(hidden, gates, local_positions, *out_slots)

    (all_branch,) = exchange([("fsdp", "whole")], [grad_branch], 4)
    padded_out = jnp.pad(full_out, ((0, padded_heads * width - model_width), (0, 0)))
    own_out = lax.dynamic_slice_in_dim(padded_out, fsdp_index * heads * width, heads * width)
    grad_t, grad_n, out_grad = pl.pallas_call(
        partial(context_grad_kernel, heads=heads, width=width),
        grid=(steps,),
        in_specs=[
            pl.BlockSpec((1, rows, model_width), lambda s: (s, 0, 0)),
            whole((heads * width, model_width)),
            pl.BlockSpec((1, heads * width, rows), lambda s: (s, 0, 0)),
        ],
        out_specs=[head_t(width), head_n(width), whole((heads * width, model_width))],
        out_shape=(
            shape_of((heads, width, length), BF16),
            shape_of((heads, length, width), BF16),
            shape_of((heads * width, model_width), F32),
        ),
        compiler_params=params(),
        name="context_grad",
    )(all_branch, own_out, context)

    grad_projected, grad_bias = pl.pallas_call(
        partial(attend_back_kernel, scale=width ** (-0.5)),
        grid=(heads,),
        in_specs=[
            by_head(SKEW, length), by_head(length, SKEW), by_head(length, width),
            by_head(length, width), by_head(width, length), by_head(width, length),
            by_head(length, width), by_head(width, length), by_head(1, length), by_head(1, span),
        ],
        out_specs=[
            pl.BlockSpec((3, 1, width, length), lambda h: (0, h, 0, 0)),
            by_head(1, span),
        ],
        out_shape=(
            shape_of((3, heads, width, length), BF16),
            shape_of((heads, 1, span), F32),
        ),
        scratch_shapes=[
            pltpu.VMEM((SKEW, span), F32),
            pltpu.VMEM((SKEW, span), F32),
            pltpu.VMEM((length, width), F32),
            pltpu.VMEM((length, width), F32),
        ],
        compiler_params=params(),
        name="attend_back",
    )(query_t, key_n, query_n, value_n, key_t, grad_t, grad_n, context_high, log_total, bias)
    grad_projected = grad_projected.reshape(slice_width, length)

    grad_first, grad_weight = pl.pallas_call(
        project_back_kernel,
        grid=(steps,),
        in_specs=[
            pl.BlockSpec((slice_width, rows), lambda s: (0, s)),
            pl.BlockSpec((rows, model_width), lambda s: (s, 0)),
            whole((model_width, slice_width)),
        ],
        out_specs=[
            pl.BlockSpec((1, model_width, rows), lambda s: (s, 0, 0)),
            whole((model_width, slice_width)),
        ],
        out_shape=(
            shape_of((fsdp_size, model_width, rows), BF16),
            shape_of((model_width, slice_width), BF16),
        ),
        scratch_shapes=[pltpu.VMEM((slice_width, model_width), F32)],
        compiler_params=params(),
        name="project_back",
    )(grad_projected, normed, weight)

    table_grad = lax.dot_general(
        bucket_select.astype(F32), grad_bias.reshape(heads, span), (((1,), (1,)), ((), ())),
        precision=lax.Precision.HIGHEST, preferred_element_type=F32,
    )
    table_grad = lax.dynamic_update_slice(
        jnp.zeros((BUCKETS, 128), F32), table_grad, (jnp.int32(0), fsdp_index * heads)
    )
    small_planes = jnp.concatenate(
        [
            small_grad.reshape(device_count, feature_rows, 128),
            table_grad.reshape(device_count, bucket_rows, 128),
        ],
        axis=1,
    )
    small_planes = jnp.pad(
        small_planes, ((0, 0), (0, small_rows - feature_rows - bucket_rows), (0, 0))
    ).astype(BF16)
    out_planes = lax.dynamic_update_slice(
        jnp.zeros((padded_heads * width, model_width), BF16),
        out_grad.astype(BF16),
        (fsdp_index * heads * width, jnp.int32(0)),
    )[:model_width].reshape(device_count, feature_rows, model_width)
    mass = jnp.broadcast_to(jnp.sum(probabilities, axis=0, keepdims=True), (8, 128))
    first_parts, in_parts, out_parts, small_parts, mass_parts = exchange(
        [("fsdp", "plane"), ("all", "plane"), ("all", "plane"), ("all", "plane"), ("all", "whole")],
        [
            grad_first,
            grad_weight.reshape(device_count, feature_rows, slice_width),
            out_planes,
            small_planes,
            mass,
        ],
        5,
    )
    grad_tokens = pl.pallas_call(
        finish_kernel,
        out_shape=shape_of((rows, model_width), F32),
        compiler_params=params(),
        name="finish",
    )(first_parts, tokens, grad_hidden)

    in_sum = jnp.sum(
        in_parts.astype(F32).reshape(exp_size, fsdp_size, feature_rows, slice_width), axis=0
    )
    in_sum = in_sum.reshape(fsdp_size, feature_rows, 3, heads * width).transpose(1, 2, 0, 3)
    in_sum = in_sum.reshape(feature_rows, 3, padded_heads * width)[:, :, :model_width]
    in_sum = in_sum.reshape(feature_rows, 3 * model_width)
    attention_gain_grad = jnp.sum(in_sum * attention_in.astype(F32), axis=1)
    in_grad = in_sum * attention_gain.astype(F32)[:, None]
    out_sum = jnp.sum(out_parts.astype(F32), axis=0)
    small_sum = jnp.sum(small_parts.astype(F32), axis=0)
    router_grad = small_sum[:feature_rows, :experts]
    mixture_gain_grad = small_sum[:feature_rows, experts]
    table_sum = small_sum[feature_rows : feature_rows + bucket_rows, :head_count]
    global_mass = jnp.sum(mass_parts[:, 0, :], axis=0)
    balance = experts * jnp.sum(
        counts[0] / (token_total * 2) * global_mass / token_total
    )
    return (
        layer_output,
        balance,
        grad_tokens,
        attention_gain_grad,
        mixture_gain_grad,
        in_grad,
        out_sum,
        router_grad,
        table_sum,
        jnp.stack(up_grads),
        jnp.stack(down_grads),
    )


def solution(mesh):
    in_specs = (
        P(("exp", "fsdp"), None),
        P(("exp", "fsdp"), None),
        P("exp"),
        P(("exp", "fsdp"), None),
        P(("exp", "fsdp"), None),
        P(("exp", "fsdp")),
        P(("exp", "fsdp")),
        P(("exp", "fsdp"), None),
        P(("exp", "fsdp"), None),
        P(("exp", "fsdp"), None),
        P(("exp", "fsdp"), None),
        P("exp", "fsdp", None),
        P("exp", "fsdp", None),
    )
    out_specs = (
        P(("exp", "fsdp"), None),
        P(),
        P(("exp", "fsdp"), None),
        P(("exp", "fsdp")),
        P(("exp", "fsdp")),
        P(("exp", "fsdp"), None),
        P(("exp", "fsdp"), None),
        P(("exp", "fsdp"), None),
        P(("exp", "fsdp"), None),
        P("exp", "fsdp", None),
        P("exp", "fsdp", None),
    )
    return jax.shard_map(
        on_device, mesh=mesh, in_specs=in_specs, out_specs=out_specs, check_vma=False
    )
```

```python
from functools import partial

import jax
import jax.numpy as jnp
from jax import lax
from jax.experimental import pallas as pl
from jax.experimental.pallas import tpu as pltpu
from jax.sharding import PartitionSpec as P

WINDOW = 1024
BUCKETS = 256

EPSILON = 1e-06
AUX_WEIGHT = 0.01
MASKED = -1e30
QUERY_BLOCK = 256
SKEW = 128
VMEM_BYTES = 58 * 1024 * 1024
MESH = pl.DeviceIdType.MESH
F32 = jnp.float32
BF16 = jnp.bfloat16


def params(**kwargs):
    return pltpu.CompilerParams(vmem_limit_bytes=VMEM_BYTES, **kwargs)


def shape_of(shape, dtype):
    return jax.ShapeDtypeStruct(shape, dtype)


def whole(shape):
    return pl.BlockSpec(shape, lambda *_: (0,) * len(shape))


def contract_last(left_side, right_side):
    return lax.dot_general(
        left_side, right_side, (((1,), (1,)), ((), ())), preferred_element_type=F32
    )


def matmul(left_side, right_side):
    return jnp.dot(left_side, right_side, preferred_element_type=F32)


def turned(value):
    return value.astype(F32).T


def bucket_index(distance):
    near_count = BUCKETS // 2
    spread = max(WINDOW - near_count, 1)
    far_bucket = (
        near_count + jnp.maximum(distance - near_count, 0) * (BUCKETS - near_count) // spread
    )
    return jnp.where(distance < near_count, distance, far_bucket)

def hint(micros):
    return pl.CostEstimate(flops=int(micros * 1.0e9), bytes_accessed=1024, transcendentals=0)


class Grid:
    def __init__(self):
        self.exp_size, self.fsdp_size = lax.axis_size("exp"), lax.axis_size("fsdp")
        self.device_count = self.exp_size * self.fsdp_size
        self.y_size = max(
            y for y in range(1, self.exp_size + 1) if self.exp_size % y == 0 and 2 * y * y <= self.exp_size
        ) if self.exp_size > 1 else 1
        self.z_size = self.exp_size // self.y_size
        self.x_size = self.fsdp_size // 2

    def here(self):
        self.exp, self.fsdp = lax.axis_index("exp"), lax.axis_index("fsdp")
        self.z, self.y = self.exp // self.y_size, self.exp % self.y_size
        self.x, self.core = self.fsdp // 2, self.fsdp % 2
        self.linear = self.exp * self.fsdp_size + self.fsdp
        return self

    def at(self, z=None, y=None, fsdp=None):
        z = self.z if z is None else z
        y = self.y if y is None else y
        return (z * self.y_size + y, self.fsdp if fsdp is None else fsdp)

    def x_from(self, hop):
        return ((self.x + self.x_size + hop) % self.x_size) * 2 + self.core

    def sibling(self, fsdp):
        return fsdp + 1 - 2 * (fsdp % 2)


class Links:
    def __init__(self, send, receive):
        self.send, self.receive, self.used = send, receive, 0

    def copy(self, source, target, device, landing):
        index = self.used
        self.used += 1
        going = pltpu.make_async_remote_copy(
            src_ref=source, dst_ref=target, send_sem=self.send.at[index],
            recv_sem=self.receive.at[index], device_id=device, device_id_type=MESH,
        )
        coming = pltpu.make_async_remote_copy(
            src_ref=landing, dst_ref=landing, send_sem=self.send.at[index],
            recv_sem=self.receive.at[index], device_id=device, device_id_type=MESH,
        )
        return going, coming


def greet(devices):
    barrier = pltpu.get_barrier_semaphore()
    for device in devices:
        pl.semaphore_signal(barrier, inc=1, device_id=device, device_id_type=MESH)
    pl.semaphore_wait(barrier, len(devices))


def chip_peers(grid):
    peers = [(grid.exp, grid.sibling(grid.fsdp))]
    return peers + [(grid.exp, grid.x_from(hop)) for hop in range(1, grid.x_size)]


class ChipGather:
    def __init__(self, grid, links, own_sem, source, target):
        self.grid, self.links, self.target = grid, links, target
        self.own = pltpu.make_async_copy(source, target.at[grid.fsdp], own_sem)
        sibling = grid.sibling(grid.fsdp)
        self.along_x, self.across = [], []
        for hop in range(1, grid.x_size):
            self.along_x.append(
                links.copy(
                    source, target.at[grid.fsdp], (grid.exp, grid.x_from(hop)),
                    target.at[grid.x_from(-hop)],
                )
            )
        self.across.append(
            links.copy(source, target.at[grid.fsdp], (grid.exp, sibling), target.at[sibling])
        )

    def start(self):
        for going, _ in self.along_x + self.across:
            going.start()
        self.own.start()

    def forward(self):
        grid = self.grid
        for hop in range(1, grid.x_size):
            self.along_x[hop - 1][1].wait_recv()
            held = grid.x_from(-hop)
            other = grid.sibling(held)
            self.across.append(
                self.links.copy(
                    self.target.at[held], self.target.at[held],
                    (grid.exp, grid.sibling(grid.fsdp)), self.target.at[other],
                )
            )
            self.across[-1][0].start()

    def finish(self):
        for _, coming in self.across:
            coming.wait_recv()
        for going, _ in self.along_x + self.across:
            going.wait_send()
        self.own.wait()


class Exchange:
    def __init__(self, grid, axis, links, own_sems, pairs):
        size = grid.exp_size if axis == "exp" else grid.fsdp_size
        place = grid.exp if axis == "exp" else grid.fsdp
        device = (lambda to: (to, grid.fsdp)) if axis == "exp" else (lambda to: (grid.exp, to))
        self.peers = [device((place + hop) % size) for hop in range(1, size)]
        self.copies, self.own = [], []
        for index, (source, target) in enumerate(pairs):
            for hop in range(1, size):
                to, origin = (place + hop) % size, (place + size - hop) % size
                self.copies.append(
                    links.copy(source(to), target.at[place], device(to), target.at[origin])
                )
            self.own.append(
                pltpu.make_async_copy(source(place), target.at[place], own_sems.at[index])
            )

    def start(self):
        for going, _ in self.copies:
            going.start()
        for own in self.own:
            own.start()

    def finish(self):
        for going, coming in self.copies:
            coming.wait_recv()
            going.wait_send()
        for own in self.own:
            own.wait()


ANYWHERE = pl.BlockSpec(memory_space=pl.ANY)
IN_VMEM = pl.BlockSpec(memory_space=pltpu.VMEM)


def dma_sems(count):
    return pltpu.SemaphoreType.DMA((count,))


def exchange(axis, arrays, collective_id, micros):
    grid = Grid()
    size = grid.exp_size if axis == "exp" else grid.fsdp_size
    count = len(arrays)
    parts = [part for _, part in arrays]

    def kernel(*refs):
        sources, targets = refs[:count], refs[count : 2 * count]
        send, receive, own = refs[2 * count :]
        place = grid.here()
        pairs = [
            (partial(plane_of, source, part), target)
            for source, part, target in zip(sources, parts, targets)
        ]
        work = Exchange(place, axis, Links(send, receive), own, pairs)
        greet(work.peers)
        work.start()
        work.finish()

    return pl.pallas_call(
        kernel,
        out_shape=tuple(
            shape_of((size,) + array.shape[(1 if part is None else 2) :], array.dtype)
            for array, part in arrays
        ),
        in_specs=[ANYWHERE] * count,
        out_specs=tuple([ANYWHERE] * count),
        scratch_shapes=[dma_sems(count * size), dma_sems(count * size), dma_sems(count)],
        compiler_params=pltpu.CompilerParams(collective_id=collective_id, has_side_effects=True),
        cost_estimate=hint(micros),
        name=f"exchange_{collective_id}",
    )(*[array for array, _ in arrays])


def plane_of(source, part, to):
    return source.at[to] if part is None else source.at[to, part]


def gather_rows(array, collective_id, micros):
    grid = Grid()

    def kernel(source, target, send, receive, own):
        place = grid.here()
        work = ChipGather(place, Links(send, receive), own.at[0], source, target)
        greet(chip_peers(place))
        work.start()
        work.forward()
        work.finish()

    return pl.pallas_call(
        kernel,
        out_shape=shape_of((grid.fsdp_size,) + array.shape, array.dtype),
        in_specs=[ANYWHERE],
        out_specs=ANYWHERE,
        scratch_shapes=[dma_sems(2 * grid.fsdp_size), dma_sems(2 * grid.fsdp_size), dma_sems(1)],
        compiler_params=pltpu.CompilerParams(collective_id=collective_id, has_side_effects=True),
        cost_estimate=hint(micros),
        name=f"gather_{collective_id}",
    )(array)


class Lanes:
    def __init__(self, heads, width, padded_heads, experts):
        self.weights = 3 * heads * width
        self.base = self.weights // 128 * 128
        self.router = self.weights - self.base
        self.gain = self.router + experts
        self.table = self.gain + 1
        self.count = self.table + padded_heads
        self.width = -(-(self.weights + 2 * experts + 1 + padded_heads) // 128) * 128
        self.extra = self.width - self.base
        self.shift = self.count - self.router


def bucket_rows_select(features, feature_rows, bucket_rows, span):
    row = lax.broadcasted_iota(jnp.int32, (features, 1), 0)
    within = lax.rem(row, feature_rows)
    bucket = jnp.where(
        within < bucket_rows, lax.div(row, feature_rows) * bucket_rows + within, -1
    )
    distance = lax.broadcasted_iota(jnp.int32, (1, span), 1) - SKEW
    near = BUCKETS // 2
    spread = max(WINDOW - near, 1)
    far = near + lax.div(jnp.maximum(distance - near, 0) * (BUCKETS - near), spread)
    wanted = jnp.where(distance < near, distance, far)
    reachable = (distance >= 0) & (distance < WINDOW)
    wanted = jnp.where(reachable, wanted, -2)
    return jnp.where(bucket == wanted, 1.0, 0.0).astype(BF16), reachable


def start_kernel(
    tokens, cotangent, routes, slots, attention_gain, mixture_gain, attention_in, router, table,
    expert_up, expert_down, *refs, lanes, heads, width, head_count, experts, capacity, local, pair,
):
    all_tokens, all_planes, cotangent_slots, position_rows = refs[:4]
    shards = [refs[4 + index * pair : 4 + (index + 1) * pair] for index in range(local)]
    planes, send, receive, own, split = refs[4 + local * pair :]
    grid = Grid().here()
    links = Links(send, receive)
    z_size, y_size, fsdp_size = grid.z_size, grid.y_size, grid.fsdp_size
    columns = [
        grid.at(z=(grid.z + hop) % z_size, fsdp=(grid.fsdp + turn) % fsdp_size)
        for hop in range(z_size)
        for turn in range(fsdp_size)
        if hop or turn
    ]
    rows_y = [grid.at(y=(grid.y + hop) % y_size) for hop in range(1, y_size)]
    gathered = ChipGather(grid, links, own.at[0], tokens, all_tokens)
    greet(columns + rows_y)
    gathered.start()

    part = expert_down.shape[1]
    depth = expert_up.shape[1]
    splits = []
    for index in range(local):
        for block in range(fsdp_size):
            splits.append(
                pltpu.make_async_copy(
                    expert_up.at[index, :, pl.ds(block * part, part)],
                    pair_view(
                        shards[index], 0, (), (pl.ds(block * depth, depth), slice(None))
                    ),
                    split.at[len(splits)],
                )
            )
        splits.append(
            pltpu.make_async_copy(
                expert_down.at[index], pair_view(shards[index], 1, (), ()), split.at[len(splits)]
            )
        )
    for copy in splits:
        copy.start()

    feature_rows, bucket_rows = attention_in.shape[0], table.shape[0]
    model_width = head_count * width
    gained = attention_in[...].astype(F32) * attention_gain[...].astype(F32)
    expert_lanes = lax.broadcasted_iota(jnp.int32, (routes.shape[0], experts), 1)
    named = jnp.zeros((routes.shape[0], experts), F32)
    for k in range(2):
        named = named + jnp.where(expert_lanes == routes[:, k : k + 1], 1.0, 0.0)
    named = jnp.sum(named, axis=0, keepdims=True)

    def fill(value, rows, size):
        value = value.astype(F32)
        if value.shape[1] < size:
            value = jnp.concatenate(
                [value, jnp.zeros((value.shape[0], size - value.shape[1]), F32)], axis=1
            )
        if value.shape[0] < rows:
            value = jnp.concatenate([value, jnp.zeros((rows - value.shape[0], size), F32)], axis=0)
        return value

    pieces = [
        router[...].astype(F32),
        mixture_gain[...].astype(F32),
        fill(table[...], feature_rows, heads * fsdp_size),
        fill(named, feature_rows, experts),
    ]
    taken = sum(piece.shape[1] for piece in pieces)
    if lanes.width > lanes.weights + taken:
        pieces.append(jnp.zeros((feature_rows, lanes.width - lanes.weights - taken), F32))
    for place in range(fsdp_size):
        first, last = place * heads * width, min((place + 1) * heads * width, model_width)
        own_pieces = []
        for kind in range(3):
            if last > first:
                own_pieces.append(gained[:, kind * model_width + first : kind * model_width + last])
            if last - first < heads * width:
                own_pieces.append(
                    jnp.zeros((feature_rows, heads * width - max(last - first, 0)), F32)
                )
        planes[place] = jnp.concatenate(own_pieces + pieces, axis=1).astype(BF16)
    arrivals = [[] for _ in range(z_size)]
    sent = []
    for hop in range(z_size):
        for turn in range(fsdp_size):
            if hop == 0 and turn == 0:
                continue
            to = (grid.fsdp + turn) % fsdp_size
            origin = (grid.fsdp + fsdp_size - turn) % fsdp_size
            going, coming = links.copy(
                planes.at[to],
                all_planes.at[grid.z, grid.y, grid.fsdp],
                grid.at(z=(grid.z + hop) % z_size, fsdp=to),
                all_planes.at[(grid.z + z_size - hop) % z_size, grid.y, origin],
            )
            going.start()
            sent.append(going)
            arrivals[hop].append(coming)
    kept = pltpu.make_async_copy(
        planes.at[grid.fsdp], all_planes.at[grid.z, grid.y, grid.fsdp], own.at[1]
    )
    kept.start()

    place = routes[...].astype(F32) * capacity + slots[...].astype(F32)
    row_count = place.shape[0]
    lane = lax.broadcasted_iota(jnp.int32, (row_count, 128), 1)
    spread = jnp.where(lane == 0, place[:, 0:1], jnp.where(lane == 1, place[:, 1:2], 0.0)).T[:8]
    position_rows[...] = spread
    gathered.forward()
    select_rows(cotangent_slots, spread, cotangent[...])

    forwarded = []
    for hop in range(z_size):
        held = (grid.z + z_size - hop) % z_size
        for coming in arrivals[hop]:
            coming.wait_recv()
        if hop == 0:
            kept.wait()
        for turn in range(1, y_size):
            going, coming = links.copy(
                all_planes.at[held, grid.y],
                all_planes.at[held, grid.y],
                grid.at(y=(grid.y + turn) % y_size),
                all_planes.at[held, (grid.y + y_size - turn) % y_size],
            )
            going.start()
            forwarded.append((going, coming))
    for going, coming in forwarded:
        coming.wait_recv()
        going.wait_send()
    for going in sent:
        going.wait_send()
    gathered.finish()
    for copy in splits:
        copy.wait()


def project_kernel(
    tokens, plane, segments, normed, query_t, key_n, query_n, value_n, key_t, value_t, bias, counts,
    weight_t, table_t, *, heads, width, lanes, feature_rows, bucket_rows,
):
    @pl.when(pl.program_id(0) == 0)
    def _():
        weight_t[...] = turned(plane[:, : lanes.weights]).astype(BF16)
        extra = plane[:, lanes.base :]
        span = bias.shape[2]
        select, reachable = bucket_rows_select(plane.shape[0], feature_rows, bucket_rows, span)
        table_t[...] = lax.dot_general(
            extra, select, (((0,), (0,)), ((), ())), preferred_element_type=F32
        )
        first = lanes.table + lax.axis_index("fsdp") * heads
        for head in range(heads):
            bias[head] = jnp.where(reachable, table_t[pl.ds(first + head, 1), :], MASKED)
        summed = jnp.sum(extra.astype(F32), axis=0, keepdims=True)
        counts[...] = pltpu.roll(
            jnp.broadcast_to(summed, counts.shape), lanes.extra - lanes.shift, 1
        )

    inputs = tokens[0].astype(F32)
    scale = lax.rsqrt(jnp.mean(inputs * inputs, axis=1, keepdims=True) + EPSILON)
    low = (inputs * scale).astype(BF16)
    normed[...] = low
    rows = low.shape[0]
    projected = contract_last(weight_t[...], low).astype(BF16).astype(F32)
    document = segments[...] % 4
    places = lax.broadcasted_iota(jnp.int32, (8, rows), 0)
    same = places == document
    hot = jnp.where(same, 1.0, 0.0)
    barred = jnp.where(same | (places >= 4), 0.0, MASKED)
    filler = jnp.zeros((SKEW - 8 - width, rows), F32)
    for head in range(heads):
        query = projected[head * width : (head + 1) * width] * width ** (-0.5)
        key = projected[(heads + head) * width : (heads + head + 1) * width]
        value = projected[(2 * heads + head) * width : (2 * heads + head + 1) * width]
        query_t[head] = jnp.concatenate([query, barred, filler], axis=0).astype(BF16)
        key_n[head] = jnp.concatenate([key, hot, filler], axis=0).T.astype(BF16)
        query_n[head] = query.T.astype(BF16)
        value_n[head] = value.T.astype(BF16)
        key_t[head] = key.astype(BF16)
        value_t[head] = value.astype(BF16)


def spans(length):
    for query_start in range(0, length, QUERY_BLOCK):
        key_start = max(0, query_start - WINDOW)
        yield query_start, key_start, query_start + QUERY_BLOCK - key_start


def spread_bias(bias, skew):
    skew[...] = pltpu.roll(
        jnp.broadcast_to(bias[0], skew.shape), 0, 1, stride=1, stride_axis=0
    )


def attend_kernel(query_t, key_n, value_t, bias, context, context_high, log_total, skew, scores, *, rows):
    spread_bias(bias, skew)
    for query_start, key_start, key_count in spans(query_t.shape[2]):
        queries = slice(query_start, query_start + QUERY_BLOCK)
        keys = slice(key_start, key_start + key_count)
        raw = matmul(key_n[0, keys, :], query_t[0, :, queries])
        for start in range(0, key_count, SKEW):
            offset = query_start - key_start - start + SKEW
            scores[start : start + SKEW, :] = (
                raw[start : start + SKEW] + skew[:, offset : offset + QUERY_BLOCK]
            )
        high = jnp.max(scores[:key_count, :], axis=0, keepdims=True)
        weights = jnp.exp(scores[:key_count, :] - high)
        total = jnp.sum(weights, axis=0, keepdims=True)
        gathered = matmul(value_t[0, :, keys], weights.astype(BF16)) / total
        context_high[0, :, queries] = gathered
        log_total[0, :, queries] = high + jnp.log(total)
        for start in range(0, QUERY_BLOCK, 128):
            place = query_start + start
            context[place // rows, :, place % rows : place % rows + 128] = gathered[
                :, start : start + 128
            ].astype(BF16)


def attend_back_kernel(
    query_t, key_n, query_n, value_n, key_t, grad_t, grad_n, context_high, log_total, bias,
    grad_projected, grad_bias, skew, grad_skew, grad_key, grad_value, *, scale,
):
    spread_bias(bias, skew)
    grad_skew[...] = jnp.zeros_like(grad_skew)
    grad_key[...] = jnp.zeros_like(grad_key)
    grad_value[...] = jnp.zeros_like(grad_value)
    inner = jnp.sum(grad_t[0].astype(F32) * context_high[0], axis=0, keepdims=True)
    for query_start, key_start, key_count in spans(query_t.shape[2]):
        queries = slice(query_start, query_start + QUERY_BLOCK)
        keys = slice(key_start, key_start + key_count)
        raw = matmul(key_n[0, keys, :], query_t[0, :, queries])
        grad_weights = matmul(value_n[0, keys, :], grad_t[0, :, queries])
        weights_low, grad_low = [], []
        for start in range(0, key_count, SKEW):
            offset = query_start - key_start - start + SKEW
            part = slice(start, start + SKEW)
            weights = jnp.exp(
                raw[part] + skew[:, offset : offset + QUERY_BLOCK] - log_total[0, :, queries]
            )
            grad_scores = weights * (grad_weights[part] - inner[:, queries])
            grad_skew[:, offset : offset + QUERY_BLOCK] += grad_scores
            weights_low.append(weights.astype(BF16))
            grad_low.append(grad_scores.astype(BF16))
        weights_low = jnp.concatenate(weights_low, axis=0)
        grad_low = jnp.concatenate(grad_low, axis=0)
        grad_projected[0, 0, :, queries] = (matmul(key_t[0, :, keys], grad_low) * scale).astype(BF16)
        grad_key[keys, :] += matmul(grad_low, query_n[0, queries, :])
        grad_value[keys, :] += matmul(weights_low, grad_n[0, queries, :])
    grad_projected[1, 0] = grad_key[...].T.astype(BF16)
    grad_projected[2, 0] = grad_value[...].T.astype(BF16)
    count = SKEW
    span = skew.shape[1]
    while count > 8:
        count //= 2
        grad_skew[:count, :] += pltpu.roll(grad_skew[count : 2 * count, :], span - count, 1)
    summed = grad_skew[0:1, :]
    for row in range(1, 8):
        summed = summed + pltpu.roll(grad_skew[row : row + 1, :], span - row, 1)
    grad_bias[0] = summed

def expert_lane(shape, lanes):
    return lax.broadcasted_iota(jnp.int32, shape, 1) - lanes.router


def route_kernel(
    tokens, attended_t, attention_out, plane, routes, slots, position_rows,
    hidden, routed, probabilities, gates, outgoing, slot_gates, *, experts, lanes, capacity,
):
    rows, model_width = tokens.shape
    attended_low = turned(attended_t[:model_width]).astype(BF16)
    hidden_state = tokens[...].astype(F32) + matmul(attended_low, attention_out[...])
    hidden[...] = hidden_state
    scale = lax.rsqrt(jnp.mean(hidden_state * hidden_state, axis=1, keepdims=True) + EPSILON)
    extra = plane[:, lanes.base :]
    gain = extra.astype(F32).T[lanes.gain : lanes.gain + 1]
    low = (hidden_state * scale * gain).astype(BF16)
    routed[...] = low
    logits = matmul(low, extra)
    lane = expert_lane(logits.shape, lanes)
    logits = jnp.where((lane >= 0) & (lane < experts), logits, MASKED)
    powers = jnp.exp(logits - jnp.max(logits, axis=1, keepdims=True))
    powers = powers / jnp.sum(powers, axis=1, keepdims=True)
    probabilities[...] = powers
    chosen = [
        jnp.sum(jnp.where(lane == routes[:, k : k + 1], powers, 0.0), axis=1, keepdims=True)
        for k in range(2)
    ]
    total = chosen[0] + chosen[1]
    gate_values = [chosen[k] / total for k in range(2)]
    pair = lax.broadcasted_iota(jnp.int32, (rows, 2), 1)
    gates[...] = jnp.where(pair == 0, gate_values[0], gate_values[1])
    members, _, gate_lanes = slot_gates.shape
    member_slots = experts // members * capacity
    slot_lanes = lax.broadcasted_iota(jnp.int32, (rows, gate_lanes), 1)
    inside = slot_lanes < member_slots
    places = routes[...] * capacity + slots[...]
    for member in range(members):
        by_slot = jnp.zeros((rows, gate_lanes), F32)
        for k in range(2):
            hit = (slot_lanes + member * member_slots == places[:, k : k + 1]) & inside
            by_slot = by_slot + jnp.where(hit, gate_values[k], 0.0)
        slot_gates[member] = jnp.broadcast_to(
            jnp.sum(by_slot, axis=0, keepdims=True), slot_gates.shape[1:]
        )
    select_rows(outgoing, position_rows[...], low)


def select_rows(outgoing, position_rows, values):
    slot_count, rows = outgoing.shape[0], values.shape[0]
    for start in range(0, slot_count, rows):
        slots = (lax.broadcasted_iota(jnp.int32, (rows, rows), 0) + start).astype(F32)
        picked = (slots == position_rows[0:1, :]) | (slots == position_rows[1:2, :])
        outgoing[start : start + rows, :] = matmul(
            jnp.where(picked, 1.0, 0.0).astype(BF16), values
        ).astype(BF16)


def gelu_parts(value):
    magnitude = jnp.abs(value)
    power = jnp.exp(value * value * -0.5)
    step = 1.0 / (1.0 + (0.3275911 * 0.7071067811865476) * magnitude)
    series = step * (
        0.127414796
        + step * (-0.142248368 + step * (0.7107068705 + step * (-0.7265760135 + step * 0.5307027145)))
    )
    tail = series * power
    normal = jnp.where(value < 0.0, tail, 1.0 - tail)
    return value * normal, normal + value * power * 0.3989422804014327


def pair_view(pair, which, lead, rest):
    if len(pair) == 1:
        return pair[0].at[(*lead, which, *rest)]
    index = (*lead, *rest)
    return pair[which].at[index] if index else pair[which]


def expert_kernel(
    rows_in, cotangent, gates, *refs, shards, index, parts, pair,
):
    half = shards // 2
    moved = len(parts)
    pairs = [refs[shard * pair : (shard + 1) * pair] for shard in range(shards)]
    sources = refs[shards * pair : shards * pair + moved]
    rest = refs[shards * pair + moved :]
    rows_out, grad_rows, grad_gates = rest[:3]
    keep, give = rest[3 : 3 + pair], rest[3 + pair : 3 + 2 * pair]
    rest = rest[3 + 2 * pair :]
    targets = rest[:moved]
    (
        up_all, down_all, rows_t, slot_t, slot_grad, total, grad_total, grad_up, grad_down,
        fetch_sem, store_sem, send, receive, own_sem,
    ) = rest[moved:]
    step = pl.program_id(0)
    grid = Grid().here()
    work = Exchange(
        grid, "exp", Links(send, receive), own_sem,
        [
            (partial(plane_of, source, part), target)
            for source, part, target in zip(sources, parts, targets)
        ],
    )
    blocks, capacity, model_width = rows_in.shape
    count = blocks * capacity
    depth = model_width // shards

    def owner(place):
        return ((grid.x + place % half) % half) * 2 + (grid.core + place // half) % 2

    def fetches(place, slot):
        column = pl.multiple_of(owner(place) * depth, 16)
        return [
            pltpu.make_async_copy(
                pair_view(pairs[shard], 0, (), (pl.ds(column, depth), slice(None))),
                up_all.at[slot, pl.ds(pl.multiple_of(owner(shard) * depth, 16), depth), :],
                fetch_sem.at[slot, shard],
            )
            for shard in range(shards)
        ]

    def fetch_down(shard, slot):
        return pltpu.make_async_copy(
            pair_view(pairs[shard], 1, (), ()), down_all.at[slot], fetch_sem.at[slot, shards]
        )

    def start_fetch(place, slot):
        for copy in fetches(place, slot):
            copy.start()
        for shard in range(shards):

            @pl.when(place == shard)
            def _(shard=shard):
                fetch_down(shard, slot).start()

    def stores(place, slot):
        column = pl.multiple_of(owner(place) * depth, 16)
        return [
            pltpu.make_async_copy(
                grad_up.at[slot, pl.ds(pl.multiple_of(owner(shard) * depth, 16), depth), :],
                pair_view(
                    keep if shard < half else give, 0, (shard % half,),
                    (pl.ds(column, depth), slice(None)),
                ),
                store_sem.at[slot, shard],
            )
            for shard in range(shards)
        ]

    def store_down(place, slot, target):
        return pltpu.make_async_copy(
            grad_down.at[slot], pair_view(target, 1, (place % half,), ()), store_sem.at[slot, shards]
        )

    def start_store(place, slot):
        for copy in stores(place, slot):
            copy.start()

        @pl.when(place < half)
        def _():
            store_down(place, slot, keep).start()

        @pl.when(place >= half)
        def _():
            store_down(place, slot, give).start()

    def wait_store(place, slot):
        for copy in stores(place, slot):
            copy.wait()
        store_down(place, slot, keep).wait()

    slot = step % 2

    @pl.when(step == 0)
    def _():
        start_fetch(0, 0)
        greet(work.peers)
        work.start()
        rows = rows_in[...].reshape(count, model_width)
        rows_t[...] = turned(rows).astype(BF16)
        columns = gates[:, 0, :].T
        for block in range(blocks):
            part = slice(block * capacity, (block + 1) * capacity)
            gate = columns[index * capacity : (index + 1) * capacity, block : block + 1]
            slot_grad[part, :] = (gate * cotangent[0, part, :].astype(F32)).astype(BF16)
        slot_t[...] = turned(slot_grad[...]).astype(BF16)
        total[...] = jnp.zeros_like(total)
        grad_total[...] = jnp.zeros_like(grad_total)

    @pl.when(step + 1 < shards)
    def _():
        start_fetch(step + 1, 1 - slot)

    for copy in fetches(step, slot):
        copy.wait()
    fetch_down(0, slot).wait()
    rows = rows_in[...].reshape(count, model_width)
    up, down = up_all[slot], down_all[slot]
    blocks_of = [slice(start, start + 256) for start in range(0, count, 256)]
    raw = [None] * len(blocks_of)
    active, grad_hidden = [], []
    raw[0] = (matmul(rows[blocks_of[0]], up), contract_last(slot_grad[blocks_of[0], :], down))
    for number, block in enumerate(blocks_of):
        if number + 1 < len(blocks_of):
            after = blocks_of[number + 1]
            raw[number + 1] = (matmul(rows[after], up), contract_last(slot_grad[after, :], down))
        hidden, grad_active = raw[number]
        activated, slope = gelu_parts(hidden)
        active.append(activated.astype(BF16))
        grad_hidden.append((grad_active * slope).astype(BF16))
        total[block, :] += matmul(active[number], down)
        grad_total[block, :] += contract_last(grad_hidden[number], up)
    active = jnp.concatenate(active, axis=0)
    grad_hidden = jnp.concatenate(grad_hidden, axis=0)

    @pl.when(step >= 2)
    def _():
        wait_store(step - 2, slot)

    grad_up[slot] = matmul(rows_t[...], grad_hidden).astype(BF16)
    grad_down[slot] = matmul(slot_t[...], active).T.astype(BF16)
    start_store(step, slot)

    @pl.when(step == shards - 1)
    def _():
        low = total[...].astype(BF16)
        rows_out[...] = low.reshape(rows_out.shape)
        grad_rows[...] = grad_total[...].astype(BF16).reshape(grad_rows.shape)
        product = low.astype(F32) * cotangent[0].astype(F32)
        ones = jnp.ones((8, model_width), F32)
        for block in range(blocks):
            grad_gates[block] = lax.dot_general(
                ones, product[block * capacity : (block + 1) * capacity],
                (((1,), (1,)), ((), ())), precision=lax.Precision.HIGHEST,
                preferred_element_type=F32,
            )
        wait_store(step - 1, 1 - slot)
        wait_store(step, slot)
        work.finish()


def run_expert(index, incoming, cotangent, gates, shards_in, moved, collective_id):
    grid = Grid()
    shards, pair = len(shards_in), len(shards_in[0])
    half = shards // 2
    blocks, capacity, model_width = incoming.shape
    part = shards_in[0][-1].shape[-2]
    count = blocks * capacity
    extra = len(moved)
    copies = max(extra * grid.exp_size, 1)
    grads = [shape_of((half,) + array.shape, BF16) for array in shards_in[0]]
    outputs = pl.pallas_call(
        partial(
            expert_kernel, shards=shards, index=index, parts=[place for _, place in moved], pair=pair
        ),
        grid=(shards,),
        in_specs=[
            whole(incoming.shape),
            pl.BlockSpec((1, count, model_width), lambda s: (index, 0, 0)),
            whole(gates.shape),
        ]
        + [ANYWHERE] * (pair * shards + extra),
        out_specs=tuple(
            [
                whole((blocks, capacity, model_width)),
                whole((blocks, capacity, model_width)),
                whole((blocks, 8, capacity)),
            ]
            + [ANYWHERE] * (2 * pair + extra)
        ),
        scratch_shapes=[
            pltpu.VMEM((2, model_width, part), BF16),
            pltpu.VMEM((2, part, model_width), BF16),
            pltpu.VMEM((model_width, count), BF16),
            pltpu.VMEM((model_width, count), BF16),
            pltpu.VMEM((count, model_width), BF16),
            pltpu.VMEM((count, model_width), F32),
            pltpu.VMEM((count, model_width), F32),
            pltpu.VMEM((2, model_width, part), BF16),
            pltpu.VMEM((2, part, model_width), BF16),
            pltpu.SemaphoreType.DMA((2, shards + 1)),
            pltpu.SemaphoreType.DMA((2, shards + 1)),
            dma_sems(copies),
            dma_sems(copies),
            dma_sems(max(extra, 1)),
        ],
        out_shape=tuple(
            [
                shape_of((blocks, capacity, model_width), BF16),
                shape_of((blocks, capacity, model_width), BF16),
                shape_of((blocks, 8, capacity), F32),
            ]
            + grads
            + grads
            + [
                shape_of((grid.exp_size,) + array.shape[(1 if place is None else 2) :], array.dtype)
                for array, place in moved
            ]
        ),
        compiler_params=params(collective_id=collective_id, has_side_effects=True),
        cost_estimate=hint(35),
        name=f"expert_{index}",
    )(
        incoming, cotangent, gates,
        *[array for shard in shards_in for array in shard],
        *[array for array, _ in moved],
    )
    return (
        outputs[:3], outputs[3 : 3 + pair], outputs[3 + pair : 3 + 2 * pair], outputs[3 + 2 * pair :]
    )


def local_picks(routes, slots, capacity, local, index, slot_count):
    member, which = lax.div(routes, local), lax.rem(routes, local)
    places = jnp.where(which == index, member * capacity + slots, -1)
    lane = lax.broadcasted_iota(jnp.int32, (routes.shape[0], slot_count), 1)
    return [lane == places[:, k : k + 1] for k in range(2)]


def unroute_kernel(
    hidden, cotangent, routed, probabilities, gates, plane, routes, slots, counts, *refs,
    experts, local, token_total, lanes,
):
    grads, gate_grads = refs[:local], refs[local : 2 * local]
    grad_hidden, grad_branch, small = refs[2 * local :]
    rows = hidden.shape[0]
    members, capacity, model_width = grads[0].shape
    grad_output = cotangent[...].astype(F32)
    grad_routed = jnp.zeros(hidden.shape, F32)
    grad_gates = [jnp.zeros((rows, 1), F32), jnp.zeros((rows, 1), F32)]
    member, which = lax.div(routes[...], local), lax.rem(routes[...], local)
    lane = lax.broadcasted_iota(jnp.int32, (rows, capacity), 1)
    for index in range(local):
        picks = local_picks(routes[...], slots[...], capacity, local, index, members * capacity)
        grad_routed = grad_routed + matmul(
            jnp.where(picks[0] | picks[1], 1.0, 0.0).astype(BF16),
            grads[index][...].reshape(members * capacity, model_width),
        )
        for place in range(members):
            spots = jnp.where((which == index) & (member == place), slots[...], -1)
            for k in range(2):
                grad_gates[k] = grad_gates[k] + jnp.sum(
                    jnp.where(lane == spots[:, k : k + 1], gate_grads[index][place, 0:1, :], 0.0),
                    axis=1, keepdims=True,
                )
    powers = probabilities[...]
    lane = expert_lane(powers.shape, lanes)
    inside = (lane >= 0) & (lane < experts)
    picked = [lane == routes[:, k : k + 1] for k in range(2)]
    chosen_total = sum(
        jnp.sum(jnp.where(picked[k], powers, 0.0), axis=1, keepdims=True) for k in range(2)
    )
    weighted = grad_gates[0] * gates[:, 0:1] + grad_gates[1] * gates[:, 1:2]
    grad_mass = (AUX_WEIGHT * experts / (2.0 * token_total * token_total)) * counts[0:1, :]
    grad_mass = jnp.where(inside, grad_mass, 0.0)
    for k in range(2):
        grad_mass = grad_mass + jnp.where(picked[k], (grad_gates[k] - weighted) / chosen_total, 0.0)
    grad_logits = powers * (grad_mass - jnp.sum(powers * grad_mass, axis=1, keepdims=True))
    extra = plane[:, lanes.base :]
    grad_routed = grad_routed + contract_last(grad_logits.astype(BF16), extra)
    hidden_state = hidden[...]
    scale = lax.rsqrt(jnp.mean(hidden_state * hidden_state, axis=1, keepdims=True) + EPSILON)
    normed = hidden_state * scale
    product = grad_routed * normed
    gain_grad = jnp.sum(product, axis=0, keepdims=True)
    small_t = matmul(grad_logits.T.astype(BF16), routed[...])
    row = lax.broadcasted_iota(jnp.int32, small_t.shape, 0)
    small_t = jnp.where(row == lanes.gain, gain_grad, small_t)
    small[...] = small_t.T
    gains = extra.astype(F32).T[lanes.gain : lanes.gain + 1]
    grad = scale * (
        grad_routed * gains - normed * jnp.mean(product * gains, axis=1, keepdims=True)
    ) + grad_output
    grad_hidden[...] = grad
    grad_branch[...] = grad.astype(BF16)


def context_grad_kernel(
    fsdp_index, grad_branch, attention_out, context, grad_t, grad_n, grad_out, total, *, heads, width
):
    @pl.when(pl.program_id(0) == 0)
    def _():
        total[...] = jnp.zeros_like(total)

    branch = grad_branch[0]
    grad = contract_last(attention_out[...], branch).astype(BF16)
    for head in range(heads):
        part = grad[head * width : (head + 1) * width]
        grad_t[head] = part
        grad_n[head] = turned(part).astype(BF16)
    total[...] += matmul(context[0], branch)

    @pl.when(pl.program_id(0) == pl.num_programs(0) - 1)
    def _():
        grad_out[...] = total[...].astype(BF16)


def project_back_kernel(
    grad_projected, normed, plane, small, probabilities, grad_bias, grad_first, grad_plane, total,
    bias_t, *, lanes, heads, feature_rows, bucket_rows,
):
    step = pl.program_id(0)

    @pl.when(step == 0)
    def _():
        total[...] = jnp.zeros_like(total)

    grad = grad_projected[...]
    grad_first[0] = matmul(plane[:, : lanes.weights], grad).astype(BF16)
    total[: lanes.weights, :] += matmul(grad, normed[...])

    @pl.when(step == pl.num_programs(0) - 1)
    def _():
        grad_plane[...] = total[...].T.astype(BF16)
        span = grad_bias.shape[2]
        select, _ = bucket_rows_select(plane.shape[0], feature_rows, bucket_rows, span)
        bias_t[...] = jnp.zeros_like(bias_t)
        first = lanes.table + lax.axis_index("fsdp") * heads
        for head in range(heads):
            bias_t[pl.ds(first + head, 1), :] = grad_bias[head]
        high = bias_t[...].astype(BF16)
        rest = (bias_t[...] - high.astype(F32)).astype(BF16)
        table = contract_last(select, high) + contract_last(select, rest)
        mass = jnp.sum(probabilities[...], axis=0, keepdims=True)
        mass = pltpu.roll(jnp.broadcast_to(mass, (8, lanes.extra)), lanes.shift, 1)[0:1]
        lane = lax.broadcasted_iota(jnp.int32, table.shape, 1)
        row = lax.broadcasted_iota(jnp.int32, table.shape, 0)
        is_small = (lane >= lanes.router) & (lane < lanes.table)
        is_mass = (lane >= lanes.count) & (lax.rem(row, feature_rows) == 0)
        extra = table + jnp.where(is_small, small[...], 0.0) + jnp.where(is_mass, mass, 0.0)
        grad_plane[:, lanes.base :] = (total[lanes.base :, :].T + extra).astype(BF16)


def last_kernel(
    first, planes, out_grad, first_parts, plane_parts, out_parts,
    first_in, first_sum, planes_in, plane_sum, send, receive, own, *, spread_out,
):
    grid = Grid().here()
    links = Links(send, receive)
    z_size, y_size, x_size, fsdp_size = grid.z_size, grid.y_size, grid.x_size, grid.fsdp_size
    exp_size = grid.exp_size
    sibling = grid.sibling(grid.fsdp)
    near = [
        grid.at(z=(grid.z + hop) % z_size, fsdp=(grid.fsdp + turn) % fsdp_size)
        for hop in range(z_size)
        for turn in range(fsdp_size)
        if hop or turn
    ]
    beside = [grid.at(y=(grid.y + hop) % y_size) for hop in range(1, y_size)]

    per_sender = grid.device_count if spread_out else exp_size
    base = 0 if spread_out else grid.fsdp * exp_size
    out_sends = []
    for number in range(per_sender):
        to = base + number
        out_sends.append((to, number))
    if spread_out:
        out_origins = [(origin, origin) for origin in range(grid.device_count)]
    else:
        out_origins = [
            (member * fsdp_size + grid.linear // exp_size, member) for member in range(exp_size)
        ]
    own_slot = grid.linear if spread_out else grid.exp
    out_base = links.used
    links.used += per_sender

    def place_of(linear):
        return (linear // fsdp_size, linear % fsdp_size)

    def out_copy(to, number, slot):
        return pltpu.make_async_remote_copy(
            src_ref=out_grad.at[number], dst_ref=out_parts.at[slot],
            send_sem=send.at[out_base + number], recv_sem=receive.at[out_base + slot],
            device_id=place_of(to), device_id_type=MESH,
        )

    barrier = pltpu.get_barrier_semaphore()
    for device in near + beside:
        pl.semaphore_signal(barrier, inc=1, device_id=device, device_id_type=MESH)
    for origin, _ in out_origins:

        @pl.when(origin != grid.linear)
        def _(origin=origin):
            pl.semaphore_signal(
                barrier, inc=1, device_id=place_of(origin), device_id_type=MESH
            )

    to_self = (
        1 if spread_out else jnp.where(grid.linear // exp_size == grid.fsdp, 1, 0)
    )
    pl.semaphore_wait(barrier, len(near) + len(beside) + per_sender - to_self)

    first_copies = []
    for hop in range(x_size):
        mine = grid.x_from(hop)
        first_copies.append(
            links.copy(
                first.at[grid.sibling(mine)], first_in.at[hop], (grid.exp, sibling), first_in.at[hop]
            )
        )
        first_copies[-1][0].start()
    beside_copies = []
    for hop in range(1, y_size):
        to = (grid.y + hop) % y_size
        beside_copies.append(
            links.copy(
                planes.at[:, to], planes_in.at[hop - 1], grid.at(y=to), planes_in.at[hop - 1]
            )
        )
        beside_copies[-1][0].start()
    for to, number in out_sends:

        @pl.when(to != grid.linear)
        def _(to=to, number=number):
            out_copy(to, number, own_slot).start()

        @pl.when(to == grid.linear)
        def _(number=number):
            pltpu.make_async_copy(out_grad.at[number], out_parts.at[own_slot], own.at[0]).start()

    along_x = []
    for hop in range(x_size):
        first_copies[hop][1].wait_recv()
        summed = first[grid.x_from(hop)].astype(F32) + first_in[hop].astype(F32)
        if hop == 0:
            first_parts[0] = summed.astype(BF16)
        else:
            first_sum[hop - 1] = summed.astype(BF16)
            along_x.append(
                links.copy(
                    first_sum.at[hop - 1], first_parts.at[hop], (grid.exp, grid.x_from(hop)),
                    first_parts.at[hop],
                )
            )
            along_x[-1][0].start()
    for going, coming in beside_copies:
        coming.wait_recv()
    along_z = []
    for hop in list(range(1, z_size)) + [0]:
        to_z = (grid.z + hop) % z_size
        summed = planes[to_z, grid.y].astype(F32)
        for other in range(y_size - 1):
            summed = summed + planes_in[other, to_z].astype(F32)
        plane_sum[hop] = summed.astype(BF16)
        for turn in range(fsdp_size):
            if hop == 0 and turn == 0:
                continue
            to = (grid.fsdp + turn) % fsdp_size
            origin = (grid.fsdp + fsdp_size - turn) % fsdp_size
            along_z.append(
                links.copy(
                    plane_sum.at[hop, to],
                    plane_parts.at[hop, grid.fsdp],
                    grid.at(z=to_z, fsdp=to),
                    plane_parts.at[hop, origin],
                )
            )
            along_z[-1][0].start()
    kept = pltpu.make_async_copy(
        plane_sum.at[0, grid.fsdp], plane_parts.at[0, grid.fsdp], own.at[1]
    )
    kept.start()
    for going, coming in along_x + along_z:
        coming.wait_recv()
    for going, _ in first_copies + beside_copies + along_x + along_z:
        going.wait_send()
    kept.wait()
    for origin, slot in out_origins:

        @pl.when(origin != grid.linear)
        def _(origin=origin, slot=slot):
            out_copy(origin, 0, slot).wait_recv()

    for to, number in out_sends:

        @pl.when(to != grid.linear)
        def _(to=to, number=number):
            out_copy(to, number, own_slot).wait_send()

        @pl.when(to == grid.linear)
        def _(number=number):
            pltpu.make_async_copy(out_grad.at[number], out_parts.at[own_slot], own.at[0]).wait()


def mixture_kernel(hidden, gates, routes, slots, *refs, local):
    rows_in, output = refs[:local], refs[local]
    members, capacity, model_width = rows_in[0].shape
    total = hidden[...]
    picked = [jnp.zeros(hidden.shape, F32), jnp.zeros(hidden.shape, F32)]
    for index in range(local):
        picks = local_picks(routes[...], slots[...], capacity, local, index, members * capacity)
        values = rows_in[index][...].reshape(members * capacity, model_width)
        for k in range(2):
            picked[k] = picked[k] + matmul(jnp.where(picks[k], 1.0, 0.0).astype(BF16), values)
    for k in range(2):
        total = total + gates[:, k : k + 1] * picked[k]
    output[...] = total.astype(BF16)


def finish_kernel(
    first_parts, plane_parts, out_parts, tokens, grad_hidden, attention_in, attention_gain, counts,
    grad_tokens, grad_gain, grad_in, grad_out, small, balance,
    *, lanes, heads, width, head_count, experts, token_total,
):
    total = jnp.sum(first_parts[...].astype(F32), axis=0).T
    inputs = tokens[...].astype(F32)
    scale = lax.rsqrt(jnp.mean(inputs * inputs, axis=1, keepdims=True) + EPSILON)
    normed = inputs * scale
    grad_tokens[...] = grad_hidden[...] + scale * (
        total - normed * jnp.mean(total * normed, axis=1, keepdims=True)
    )
    fsdp_size = plane_parts.shape[1]
    model_width = head_count * width
    summed = jnp.sum(plane_parts[...].astype(F32), axis=0)
    sums = [summed[place] for place in range(fsdp_size)]
    columns = []
    for kind in range(3):
        pieces = [
            sums[place][:, kind * heads * width : (kind + 1) * heads * width]
            for place in range(fsdp_size)
        ]
        columns.append(jnp.concatenate(pieces, axis=1)[:, :model_width])
    gathered = jnp.concatenate(columns, axis=1)
    grad_gain[...] = jnp.sum(gathered * attention_in[...].astype(F32), axis=1, keepdims=True)
    grad_in[...] = gathered * attention_gain[...].astype(F32)
    grad_out[...] = jnp.sum(out_parts[...].astype(F32), axis=0)
    extra = sum(part[:, lanes.base :] for part in sums)
    small[...] = extra
    mass = jnp.broadcast_to(extra[0:1], (8, lanes.extra))
    mass = pltpu.roll(mass, lanes.extra - lanes.shift, 1)
    lane = expert_lane(mass.shape, lanes)
    terms = jnp.where((lane >= 0) & (lane < experts), mass * counts[...], 0.0)[0:1]
    balance[...] = jnp.sum(terms, axis=1, keepdims=True) * (
        experts / (2.0 * token_total * token_total)
    )


def sum_kernel(*refs, local, terms):
    outputs = refs[2 * local * terms :]
    for which in range(2):
        for index in range(local):
            first = (index * 2 + which) * terms
            shape = outputs[which].shape[1:]
            total = refs[first][...].reshape(shape).astype(F32)
            for ref in refs[first + 1 : first + terms]:
                total = total + ref[...].reshape(shape).astype(F32)
            outputs[which][index] = total


def sum_grads(groups, up_shape, down_shape, blocks):
    local = len(groups)
    depth, part = up_shape[1], down_shape[1]
    block_rows = (depth, part // blocks)
    widths = (part, down_shape[2])
    arrays, specs = [], []
    for keep, taken, passed in groups:
        for which in range(2):
            size = (block_rows[which], widths[which])
            for pair in (keep, taken):
                if len(pair) == 1:
                    arrays.append(pair[0])
                    specs.append(
                        pl.BlockSpec((1, 1) + size, lambda c, which=which: (0, which, c, 0))
                    )
                else:
                    arrays.append(pair[which])
                    specs.append(pl.BlockSpec((1,) + size, lambda c: (0, c, 0)))
            for pair in passed:
                if len(pair) == 1:
                    arrays.append(pair[0])
                    specs.append(pl.BlockSpec((1,) + size, lambda c, which=which: (which, c, 0)))
                else:
                    arrays.append(pair[which])
                    specs.append(pl.BlockSpec(size, lambda c: (c, 0)))
    return pl.pallas_call(
        partial(sum_kernel, local=local, terms=len(arrays) // (2 * local)),
        grid=(blocks,),
        in_specs=specs,
        out_specs=[
            pl.BlockSpec((local, depth, part), lambda c: (0, 0, c)),
            pl.BlockSpec((local, part // blocks, down_shape[2]), lambda c: (0, c, 0)),
        ],
        out_shape=(shape_of(up_shape, F32), shape_of(down_shape, F32)),
        compiler_params=params(),
        cost_estimate=hint(8),
        name="sum_grads",
    )(*arrays)


def over_x(array, hop):
    fsdp_size = lax.axis_size("fsdp")
    return lax.ppermute(array, "fsdp", [(i, (i + 2 * hop) % fsdp_size) for i in range(fsdp_size)])


def over_core(array):
    return lax.ppermute(array, "fsdp", [(i, i ^ 1) for i in range(lax.axis_size("fsdp"))])


def on_device(
    tokens,
    cotangent,
    segments,
    routes,
    slots,
    attention_gain,
    mixture_gain,
    attention_in,
    attention_out,
    router_weight,
    position_table,
    expert_up,
    expert_down,
):
    grid = Grid()
    exp_size, fsdp_size, chips = grid.exp_size, grid.fsdp_size, grid.x_size
    device_count = grid.device_count
    fsdp_index = lax.axis_index("fsdp")
    rows, model_width = tokens.shape
    length = rows * fsdp_size
    head_count = position_table.shape[1]
    width = model_width // head_count
    heads = -(-head_count // fsdp_size)
    padded_heads = heads * fsdp_size
    feature_rows, bucket_rows = attention_in.shape[0], position_table.shape[0]
    experts = router_weight.shape[1]
    local = expert_up.shape[0]
    capacity = 4 * rows // experts
    token_total = rows * device_count
    span = WINDOW + 2 * SKEW + QUERY_BLOCK
    lanes = Lanes(heads, width, padded_heads, experts)
    part = expert_down.shape[1]
    pair = 1 if part == model_width else 2
    gain_column = attention_gain.reshape(feature_rows, 1)

    shard_shapes = [shape_of((model_width, part), BF16), shape_of((part, model_width), BF16)]
    if pair == 1:
        shard_shapes = [shape_of((2, model_width, part), BF16)]
    copies = 2 * fsdp_size + grid.z_size * fsdp_size + grid.z_size * grid.y_size
    started = pl.pallas_call(
        partial(
            start_kernel, lanes=lanes, heads=heads, width=width, head_count=head_count,
            experts=experts, capacity=capacity, local=local, pair=pair,
        ),
        out_shape=tuple(
            [
                shape_of((fsdp_size, rows, model_width), BF16),
                shape_of((grid.z_size, grid.y_size, fsdp_size, feature_rows, lanes.width), BF16),
                shape_of((experts * capacity, model_width), BF16),
                shape_of((8, rows), F32),
            ]
            + shard_shapes * local
        ),
        in_specs=[ANYWHERE] + [IN_VMEM] * 8 + [ANYWHERE] * 2,
        out_specs=tuple([ANYWHERE, ANYWHERE, IN_VMEM, IN_VMEM] + [ANYWHERE] * (pair * local)),
        scratch_shapes=[
            pltpu.VMEM((fsdp_size, feature_rows, lanes.width), BF16),
            dma_sems(copies),
            dma_sems(copies),
            dma_sems(2),
            dma_sems(local * (fsdp_size + 1)),
        ],
        compiler_params=params(collective_id=0, has_side_effects=True),
        cost_estimate=hint(20),
        name="start",
    )(
        tokens, cotangent, routes, slots, gain_column, mixture_gain.reshape(feature_rows, 1),
        attention_in, router_weight, position_table, expert_up, expert_down,
    )
    all_tokens, all_planes, cotangent_slots, position_rows = started[:4]
    own_shards = [started[4 + index * pair : 4 + (index + 1) * pair] for index in range(local)]
    plane = all_planes.reshape(model_width, lanes.width)
    full_out = lax.all_gather(attention_out, ("exp", "fsdp"), axis=0, tiled=True)

    def along_x(shard):
        return [tuple(over_x(array, -hop) for array in shard) for hop in range(1, chips)]

    def across(shards):
        return [tuple(over_core(array) for array in shard) for shard in shards]

    near_first = along_x(own_shards[0])
    across_own = across([own_shards[0]])
    cotangent_in = lax.all_to_all(
        cotangent_slots.reshape(experts, capacity, model_width),
        "exp", split_axis=0, concat_axis=1, tiled=True,
    )

    head_t = lambda size: pl.BlockSpec((heads, size, rows), lambda s, *_: (0, 0, s))
    head_n = lambda size: pl.BlockSpec((heads, rows, size), lambda s, *_: (0, s, 0))
    normed, query_t, key_n, query_n, value_n, key_t, value_t, bias, counts = pl.pallas_call(
        partial(
            project_kernel, heads=heads, width=width, lanes=lanes, feature_rows=feature_rows,
            bucket_rows=bucket_rows,
        ),
        grid=(fsdp_size,),
        in_specs=[
            pl.BlockSpec((1, rows, model_width), lambda s: (s, 0, 0)),
            whole((model_width, lanes.width)),
            pl.BlockSpec((1, rows), lambda s: (0, s)),
        ],
        out_specs=[
            pl.BlockSpec((rows, model_width), lambda s: (s, 0)),
            head_t(SKEW), head_n(SKEW), head_n(width), head_n(width), head_t(width), head_t(width),
            whole((heads, 1, span)),
            whole((8, lanes.extra)),
        ],
        out_shape=(
            shape_of((length, model_width), BF16),
            shape_of((heads, SKEW, length), BF16),
            shape_of((heads, length, SKEW), BF16),
            shape_of((heads, length, width), BF16),
            shape_of((heads, length, width), BF16),
            shape_of((heads, width, length), BF16),
            shape_of((heads, width, length), BF16),
            shape_of((heads, 1, span), F32),
            shape_of((8, lanes.extra), F32),
        ),
        scratch_shapes=[
            pltpu.VMEM((lanes.weights, model_width), BF16),
            pltpu.VMEM((lanes.extra, span), F32),
        ],
        compiler_params=params(),
        cost_estimate=hint(8),
        name="project",
    )(all_tokens, plane, segments.reshape(1, length))

    by_head = lambda *size: pl.BlockSpec((1,) + size, lambda h: (h, 0, 0))
    context, context_high, log_total = pl.pallas_call(
        partial(attend_kernel, rows=rows),
        grid=(heads,),
        in_specs=[
            by_head(SKEW, length), by_head(length, SKEW), by_head(width, length), by_head(1, span),
        ],
        out_specs=[
            pl.BlockSpec((fsdp_size, width, rows), lambda h: (0, h, 0)),
            by_head(width, length),
            by_head(1, length),
        ],
        out_shape=(
            shape_of((fsdp_size, heads * width, rows), BF16),
            shape_of((heads, width, length), F32),
            shape_of((heads, 1, length), F32),
        ),
        scratch_shapes=[
            pltpu.VMEM((SKEW, span), F32),
            pltpu.VMEM((WINDOW + QUERY_BLOCK, QUERY_BLOCK), F32),
        ],
        compiler_params=params(),
        cost_estimate=hint(13),
        name="attend",
    )(query_t, key_n, value_t, bias)

    (attended_t,) = exchange("fsdp", [(context, None)], 1, 9)
    attended_t = attended_t.reshape(padded_heads * width, rows)

    gate_lanes = -(-local * capacity // 128) * 128
    hidden, routed, probabilities, gates, outgoing, slot_gates = pl.pallas_call(
        partial(route_kernel, experts=experts, lanes=lanes, capacity=capacity),
        out_shape=(
            shape_of((rows, model_width), F32),
            shape_of((rows, model_width), BF16),
            shape_of((rows, lanes.extra), F32),
            shape_of((rows, 2), F32),
            shape_of((experts * capacity, model_width), BF16),
            shape_of((exp_size, 8, gate_lanes), F32),
        ),
        compiler_params=params(),
        cost_estimate=hint(7),
        name="route",
    )(tokens, attended_t, full_out, plane, routes, slots, position_rows)

    near_first, outgoing, later_shards = lax.optimization_barrier(
        (near_first, outgoing, own_shards[1:])
    )
    expert_shards = [[own_shards[0]] + near_first + across_own + across(near_first)]
    near_later = [along_x(shard) for shard in later_shards]
    across_later = [across([shard]) for shard in later_shards]

    outgoing = outgoing.reshape(exp_size, local, capacity, model_width)
    incoming, gates_in = exchange("exp", [(outgoing, 0), (slot_gates, None)], 2, 28)

    outs, keeps, gives, returned, takens = [], [], [], [], []
    moved = []
    for index in range(local):
        if index > 0:
            near, incoming = lax.optimization_barrier((near_later[index - 1], incoming))
            expert_shards.append(
                [later_shards[index - 1]] + near + across_later[index - 1] + across(near)
            )
        carried = list(moved)
        if index + 1 < local:
            carried.append((outgoing, index + 1))
        (out, grad, gate_grad), keep, give, arrived = run_expert(
            index, incoming, cotangent_in, gates_in, expert_shards[index], carried, 3 + index
        )
        if index + 1 < local:
            incoming = arrived[-1]
            arrived = arrived[:-1]
        if index > 0:
            returned.append(arrived)
        moved = [(grad, None), (gate_grad, None)]
        outs.append(out)
        keeps.append(keep)
        takens.append(tuple(over_core(array) for array in give))

    def pass_on(index, after):
        keep, taken, after = lax.optimization_barrier((keeps[index], takens[index], after))
        passed = []
        for hop in range(1, chips):
            passed.append(
                tuple(
                    over_x((mine[hop].astype(F32) + theirs[hop].astype(F32)).astype(BF16), hop)
                    for mine, theirs in zip(keep, taken)
                )
            )
        return (keep, taken, passed), after

    groups = []
    for index in range(local - 1):
        group, last_grad = pass_on(index, moved[0][0])
        moved[0] = (last_grad, None)
        groups.append(group)
    returned.append(exchange("exp", moved, 3 + local, 28))
    group, returned[-1] = pass_on(local - 1, returned[-1])
    groups.append(group)

    grad_hidden, grad_branch, small = pl.pallas_call(
        partial(
            unroute_kernel, experts=experts, local=local, token_total=token_total, lanes=lanes
        ),
        out_shape=(
            shape_of((rows, model_width), F32),
            shape_of((rows, model_width), BF16),
            shape_of((model_width, lanes.extra), F32),
        ),
        compiler_params=params(),
        cost_estimate=hint(7),
        name="unroute",
    )(
        hidden, cotangent, routed, probabilities, gates, plane, routes, slots, counts,
        *[part[0] for part in returned], *[part[1] for part in returned],
    )

    outs, grad_branch = lax.optimization_barrier((outs, grad_branch))
    out_rows = lax.all_to_all(
        jnp.stack(outs, axis=1), "exp", split_axis=0, concat_axis=0, tiled=True
    )

    all_branch = gather_rows(grad_branch, 4 + local, 15)
    padded_out = full_out
    if padded_heads > head_count:
        padded_out = jnp.pad(full_out, ((0, padded_heads * width - model_width), (0, 0)))
    grad_t, grad_n, out_grad = pl.pallas_call(
        partial(context_grad_kernel, heads=heads, width=width),
        grid_spec=pltpu.PrefetchScalarGridSpec(
            num_scalar_prefetch=1,
            grid=(fsdp_size,),
            in_specs=[
                pl.BlockSpec((1, rows, model_width), lambda s, f: (s, 0, 0)),
                pl.BlockSpec((heads * width, model_width), lambda s, f: (f[0], 0)),
                pl.BlockSpec((1, heads * width, rows), lambda s, f: (s, 0, 0)),
            ],
            out_specs=[head_t(width), head_n(width), whole((heads * width, model_width))],
            scratch_shapes=[pltpu.VMEM((heads * width, model_width), F32)],
        ),
        out_shape=(
            shape_of((heads, width, length), BF16),
            shape_of((heads, length, width), BF16),
            shape_of((heads * width, model_width), BF16),
        ),
        compiler_params=params(),
        cost_estimate=hint(5),
        name="context_grad",
    )(fsdp_index.reshape(1), all_branch, padded_out, context)

    grad_projected, grad_bias = pl.pallas_call(
        partial(attend_back_kernel, scale=width ** (-0.5)),
        grid=(heads,),
        in_specs=[
            by_head(SKEW, length), by_head(length, SKEW), by_head(length, width),
            by_head(length, width), by_head(width, length), by_head(width, length),
            by_head(length, width), by_head(width, length), by_head(1, length), by_head(1, span),
        ],
        out_specs=[
            pl.BlockSpec((3, 1, width, length), lambda h: (0, h, 0, 0)),
            by_head(1, span),
        ],
        out_shape=(
            shape_of((3, heads, width, length), BF16),
            shape_of((heads, 1, span), F32),
        ),
        scratch_shapes=[
            pltpu.VMEM((SKEW, span), F32),
            pltpu.VMEM((SKEW, span), F32),
            pltpu.VMEM((length, width), F32),
            pltpu.VMEM((length, width), F32),
        ],
        compiler_params=params(),
        cost_estimate=hint(15),
        name="attend_back",
    )(query_t, key_n, query_n, value_n, key_t, grad_t, grad_n, context_high, log_total, bias)
    grad_projected = grad_projected.reshape(lanes.weights, length)

    grad_first, grad_plane = pl.pallas_call(
        partial(
            project_back_kernel, lanes=lanes, heads=heads, feature_rows=feature_rows,
            bucket_rows=bucket_rows,
        ),
        grid=(fsdp_size,),
        in_specs=[
            pl.BlockSpec((lanes.weights, rows), lambda s: (0, s)),
            pl.BlockSpec((rows, model_width), lambda s: (s, 0)),
            whole((model_width, lanes.width)),
            whole((model_width, lanes.extra)),
            whole((rows, lanes.extra)),
            whole((heads, 1, span)),
        ],
        out_specs=[
            pl.BlockSpec((1, model_width, rows), lambda s: (s, 0, 0)),
            whole((model_width, lanes.width)),
        ],
        out_shape=(
            shape_of((fsdp_size, model_width, rows), BF16),
            shape_of((model_width, lanes.width), BF16),
        ),
        scratch_shapes=[
            pltpu.VMEM((lanes.width, model_width), F32),
            pltpu.VMEM((lanes.extra, span), F32),
        ],
        compiler_params=params(),
        cost_estimate=hint(9),
        name="project_back",
    )(grad_projected, normed, plane, small, probabilities, grad_bias)

    spread_out = heads * width * fsdp_size != model_width
    if spread_out:
        out_grad = lax.dynamic_update_slice(
            jnp.zeros((padded_heads * width, model_width), BF16), out_grad,
            (fsdp_index * heads * width, jnp.int32(0)),
        )[:model_width]
    out_grad = out_grad.reshape(-1, feature_rows, model_width)
    out_count = device_count if spread_out else exp_size
    plane_shape = (grid.z_size, grid.y_size, fsdp_size, feature_rows, lanes.width)
    parts_shape = (grid.z_size, fsdp_size, feature_rows, lanes.width)
    copies = 2 * fsdp_size + grid.z_size * fsdp_size + grid.y_size + out_count
    first_parts, plane_parts, out_parts = pl.pallas_call(
        partial(last_kernel, spread_out=spread_out),
        out_shape=(
            shape_of((chips, model_width, rows), BF16),
            shape_of(parts_shape, BF16),
            shape_of((out_count, feature_rows, model_width), BF16),
        ),
        in_specs=[IN_VMEM] * 3,
        out_specs=(IN_VMEM, ANYWHERE, ANYWHERE),
        scratch_shapes=[
            pltpu.VMEM((chips, model_width, rows), BF16),
            pltpu.VMEM((max(chips - 1, 1), model_width, rows), BF16),
            pltpu.VMEM((max(grid.y_size - 1, 1),) + parts_shape, BF16),
            pltpu.VMEM(parts_shape, BF16),
            dma_sems(copies),
            dma_sems(copies),
            dma_sems(2),
        ],
        compiler_params=params(collective_id=5 + local, has_side_effects=True),
        cost_estimate=hint(30),
        name="last",
    )(grad_first, grad_plane.reshape(plane_shape), out_grad)

    grad_tokens, gain_grad, in_grad, out_sum, small_sum, balance = pl.pallas_call(
        partial(
            finish_kernel, lanes=lanes, heads=heads, width=width, head_count=head_count,
            experts=experts, token_total=token_total,
        ),
        out_shape=(
            shape_of((rows, model_width), F32),
            shape_of((feature_rows, 1), F32),
            shape_of((feature_rows, 3 * model_width), F32),
            shape_of((feature_rows, model_width), F32),
            shape_of((feature_rows, lanes.extra), F32),
            shape_of((1, 1), F32),
        ),
        compiler_params=params(),
        cost_estimate=hint(6),
        name="finish",
    )(first_parts, plane_parts, out_parts, tokens, grad_hidden, attention_in, gain_column, counts)

    layer_output = pl.pallas_call(
        partial(mixture_kernel, local=local),
        out_shape=shape_of((rows, model_width), BF16),
        compiler_params=params(),
        cost_estimate=hint(5),
        name="mixture",
    )(hidden, gates, routes, slots, *[out_rows[:, index] for index in range(local)])

    up_grad, down_grad = sum_grads(groups, expert_up.shape, expert_down.shape, fsdp_size)
    return (
        layer_output,
        balance.reshape(()),
        grad_tokens,
        gain_grad.reshape(feature_rows),
        small_sum[:, lanes.gain],
        in_grad,
        out_sum,
        small_sum[:, lanes.router : lanes.router + experts],
        small_sum[:bucket_rows, lanes.table : lanes.table + head_count],
        up_grad,
        down_grad,
    )


def solution(mesh):
    in_specs = (
        P(("exp", "fsdp"), None),
        P(("exp", "fsdp"), None),
        P("exp"),
        P(("exp", "fsdp"), None),
        P(("exp", "fsdp"), None),
        P(("exp", "fsdp")),
        P(("exp", "fsdp")),
        P(("exp", "fsdp"), None),
        P(("exp", "fsdp"), None),
        P(("exp", "fsdp"), None),
        P(("exp", "fsdp"), None),
        P("exp", "fsdp", None),
        P("exp", "fsdp", None),
    )
    out_specs = (
        P(("exp", "fsdp"), None),
        P(),
        P(("exp", "fsdp"), None),
        P(("exp", "fsdp")),
        P(("exp", "fsdp")),
        P(("exp", "fsdp"), None),
        P(("exp", "fsdp"), None),
        P(("exp", "fsdp"), None),
        P(("exp", "fsdp"), None),
        P("exp", "fsdp", None),
        P("exp", "fsdp", None),
    )
    return jax.shard_map(
        on_device, mesh=mesh, in_specs=in_specs, out_specs=out_specs, check_vma=False
    )
```

```python
from functools import partial

import jax
import jax.numpy as jnp
from jax import lax
from jax.experimental import pallas as pl
from jax.experimental.pallas import tpu as pltpu
from jax.sharding import PartitionSpec as P

WINDOW = 1024
BUCKETS = 256

EPSILON = 1e-06
AUX_WEIGHT = 0.01
MASKED = -1e30
QUERY_BLOCK = 256
SKEW = 128
VMEM_BYTES = 58 * 1024 * 1024
MESH = pl.DeviceIdType.MESH
F32 = jnp.float32
BF16 = jnp.bfloat16


def params(**kwargs):
    return pltpu.CompilerParams(vmem_limit_bytes=VMEM_BYTES, **kwargs)


def shape_of(shape, dtype):
    return jax.ShapeDtypeStruct(shape, dtype)


def whole(shape):
    return pl.BlockSpec(shape, lambda *_: (0,) * len(shape))


def contract_last(left_side, right_side):
    return lax.dot_general(
        left_side, right_side, (((1,), (1,)), ((), ())), preferred_element_type=F32
    )


def matmul(left_side, right_side):
    return jnp.dot(left_side, right_side, preferred_element_type=F32)


def turned(value):
    return value.astype(F32).T


def bucket_index(distance):
    near_count = BUCKETS // 2
    spread = max(WINDOW - near_count, 1)
    far_bucket = (
        near_count + jnp.maximum(distance - near_count, 0) * (BUCKETS - near_count) // spread
    )
    return jnp.where(distance < near_count, distance, far_bucket)

def hint(micros):
    return pl.CostEstimate(flops=int(micros * 1.0e9), bytes_accessed=1024, transcendentals=0)


class Grid:
    def __init__(self):
        self.exp_size, self.fsdp_size = lax.axis_size("exp"), lax.axis_size("fsdp")
        self.device_count = self.exp_size * self.fsdp_size
        self.y_size = max(
            y for y in range(1, self.exp_size + 1) if self.exp_size % y == 0 and 2 * y * y <= self.exp_size
        ) if self.exp_size > 1 else 1
        self.z_size = self.exp_size // self.y_size
        self.x_size = self.fsdp_size // 2

    def here(self):
        self.exp, self.fsdp = lax.axis_index("exp"), lax.axis_index("fsdp")
        self.z, self.y = self.exp // self.y_size, self.exp % self.y_size
        self.x, self.core = self.fsdp // 2, self.fsdp % 2
        self.linear = self.exp * self.fsdp_size + self.fsdp
        return self

    def at(self, z=None, y=None, fsdp=None):
        z = self.z if z is None else z
        y = self.y if y is None else y
        return (z * self.y_size + y, self.fsdp if fsdp is None else fsdp)

    def x_from(self, hop):
        return ((self.x + self.x_size + hop) % self.x_size) * 2 + self.core

    def sibling(self, fsdp):
        return fsdp + 1 - 2 * (fsdp % 2)


class Links:
    def __init__(self, send, receive):
        self.send, self.receive, self.used = send, receive, 0

    def copy(self, source, target, device, landing):
        index = self.used
        self.used += 1
        going = pltpu.make_async_remote_copy(
            src_ref=source, dst_ref=target, send_sem=self.send.at[index],
            recv_sem=self.receive.at[index], device_id=device, device_id_type=MESH,
        )
        coming = pltpu.make_async_remote_copy(
            src_ref=landing, dst_ref=landing, send_sem=self.send.at[index],
            recv_sem=self.receive.at[index], device_id=device, device_id_type=MESH,
        )
        return going, coming


def greet(devices):
    barrier = pltpu.get_barrier_semaphore()
    for device in devices:
        pl.semaphore_signal(barrier, inc=1, device_id=device, device_id_type=MESH)
    pl.semaphore_wait(barrier, len(devices))


def chip_peers(grid):
    peers = [(grid.exp, grid.sibling(grid.fsdp))]
    return peers + [(grid.exp, grid.x_from(hop)) for hop in range(1, grid.x_size)]


class ChipGather:
    def __init__(self, grid, links, own_sem, source, target):
        self.grid, self.links, self.target = grid, links, target
        self.own = pltpu.make_async_copy(source, target.at[grid.fsdp], own_sem)
        sibling = grid.sibling(grid.fsdp)
        self.along_x, self.across = [], []
        for hop in range(1, grid.x_size):
            self.along_x.append(
                links.copy(
                    source, target.at[grid.fsdp], (grid.exp, grid.x_from(hop)),
                    target.at[grid.x_from(-hop)],
                )
            )
        self.across.append(
            links.copy(source, target.at[grid.fsdp], (grid.exp, sibling), target.at[sibling])
        )

    def start(self):
        for going, _ in self.along_x + self.across:
            going.start()
        self.own.start()

    def forward(self):
        grid = self.grid
        for hop in range(1, grid.x_size):
            self.along_x[hop - 1][1].wait_recv()
            held = grid.x_from(-hop)
            other = grid.sibling(held)
            self.across.append(
                self.links.copy(
                    self.target.at[held], self.target.at[held],
                    (grid.exp, grid.sibling(grid.fsdp)), self.target.at[other],
                )
            )
            self.across[-1][0].start()

    def finish(self):
        for _, coming in self.across:
            coming.wait_recv()
        for going, _ in self.along_x + self.across:
            going.wait_send()
        self.own.wait()


class Exchange:
    def __init__(self, grid, axis, links, own_sems, pairs):
        size = grid.exp_size if axis == "exp" else grid.fsdp_size
        place = grid.exp if axis == "exp" else grid.fsdp
        device = (lambda to: (to, grid.fsdp)) if axis == "exp" else (lambda to: (grid.exp, to))
        self.peers = [device((place + hop) % size) for hop in range(1, size)]
        self.copies, self.own = [], []
        for index, (source, target) in enumerate(pairs):
            for hop in range(1, size):
                to, origin = (place + hop) % size, (place + size - hop) % size
                self.copies.append(
                    links.copy(source(to), target.at[place], device(to), target.at[origin])
                )
            self.own.append(
                pltpu.make_async_copy(source(place), target.at[place], own_sems.at[index])
            )

    def start(self):
        for going, _ in self.copies:
            going.start()
        for own in self.own:
            own.start()

    def finish(self):
        for going, coming in self.copies:
            coming.wait_recv()
            going.wait_send()
        for own in self.own:
            own.wait()


ANYWHERE = pl.BlockSpec(memory_space=pl.ANY)
IN_VMEM = pl.BlockSpec(memory_space=pltpu.VMEM)


def dma_sems(count):
    return pltpu.SemaphoreType.DMA((count,))


def exchange(axis, arrays, collective_id, micros):
    grid = Grid()
    size = grid.exp_size if axis == "exp" else grid.fsdp_size
    count = len(arrays)
    parts = [part for _, part in arrays]

    def kernel(*refs):
        sources, targets = refs[:count], refs[count : 2 * count]
        send, receive, own = refs[2 * count :]
        place = grid.here()
        pairs = [
            (partial(plane_of, source, part), target)
            for source, part, target in zip(sources, parts, targets)
        ]
        work = Exchange(place, axis, Links(send, receive), own, pairs)
        greet(work.peers)
        work.start()
        work.finish()

    return pl.pallas_call(
        kernel,
        out_shape=tuple(
            shape_of((size,) + array.shape[(1 if part is None else 2) :], array.dtype)
            for array, part in arrays
        ),
        in_specs=[ANYWHERE] * count,
        out_specs=tuple([ANYWHERE] * count),
        scratch_shapes=[dma_sems(count * size), dma_sems(count * size), dma_sems(count)],
        compiler_params=pltpu.CompilerParams(collective_id=collective_id, has_side_effects=True),
        cost_estimate=hint(micros),
        name=f"exchange_{collective_id}",
    )(*[array for array, _ in arrays])


def plane_of(source, part, to):
    return source.at[to] if part is None else source.at[to, part]


def gather_rows(array, collective_id, micros):
    grid = Grid()

    def kernel(source, target, send, receive, own):
        place = grid.here()
        work = ChipGather(place, Links(send, receive), own.at[0], source, target)
        greet(chip_peers(place))
        work.start()
        work.forward()
        work.finish()

    return pl.pallas_call(
        kernel,
        out_shape=shape_of((grid.fsdp_size,) + array.shape, array.dtype),
        in_specs=[ANYWHERE],
        out_specs=ANYWHERE,
        scratch_shapes=[dma_sems(2 * grid.fsdp_size), dma_sems(2 * grid.fsdp_size), dma_sems(1)],
        compiler_params=pltpu.CompilerParams(collective_id=collective_id, has_side_effects=True),
        cost_estimate=hint(micros),
        name=f"gather_{collective_id}",
    )(array)


class Lanes:
    def __init__(self, heads, width, padded_heads, experts):
        self.weights = 3 * heads * width
        self.base = self.weights // 128 * 128
        self.router = self.weights - self.base
        self.gain = self.router + experts
        self.table = self.gain + 1
        self.count = self.table + padded_heads
        self.width = -(-(self.weights + 2 * experts + 1 + padded_heads) // 128) * 128
        self.extra = self.width - self.base
        self.shift = self.count - self.router


def bucket_rows_select(features, feature_rows, bucket_rows, span):
    row = lax.broadcasted_iota(jnp.int32, (features, 1), 0)
    within = lax.rem(row, feature_rows)
    bucket = jnp.where(
        within < bucket_rows, lax.div(row, feature_rows) * bucket_rows + within, -1
    )
    distance = lax.broadcasted_iota(jnp.int32, (1, span), 1) - SKEW
    near = BUCKETS // 2
    spread = max(WINDOW - near, 1)
    far = near + lax.div(jnp.maximum(distance - near, 0) * (BUCKETS - near), spread)
    wanted = jnp.where(distance < near, distance, far)
    reachable = (distance >= 0) & (distance < WINDOW)
    wanted = jnp.where(reachable, wanted, -2)
    return jnp.where(bucket == wanted, 1.0, 0.0).astype(BF16), reachable


def as_column(row, size):
    row_place = lax.broadcasted_iota(jnp.int32, (size, size), 0)
    lane = lax.broadcasted_iota(jnp.int32, (size, size), 1)
    spread = jnp.broadcast_to(row.astype(F32), (size, size))
    return jnp.sum(jnp.where(row_place == lane, spread, 0.0), axis=1, keepdims=True)


def padded_rows(value, rows):
    if value.shape[0] == rows:
        return value
    return jnp.concatenate([value, jnp.zeros((rows - value.shape[0], value.shape[1]), F32)], axis=0)


def padded_lanes(value, lanes):
    if value.shape[1] == lanes:
        return value
    return jnp.concatenate([value, jnp.zeros((value.shape[0], lanes - value.shape[1]), F32)], axis=1)


class Wide:
    def __init__(self, grid, links, own_sem, source, target):
        self.grid, self.links, self.target = grid, links, target
        self.own = pltpu.make_async_copy(
            source, target.at[grid.z, grid.y, grid.x, grid.core], own_sem
        )
        self.stages = []
        stage = []
        for hop in range(1, grid.z_size):
            stage.append(
                links.copy(
                    source, target.at[grid.z, grid.y, grid.x, grid.core],
                    grid.at(z=(grid.z + hop) % grid.z_size),
                    target.at[(grid.z + grid.z_size - hop) % grid.z_size, grid.y, grid.x, grid.core],
                )
            )
        self.stages.append(stage)

    def start(self):
        self.own.start()
        for going, _ in self.stages[0]:
            going.start()

    def turn(self, axis):
        grid, target = self.grid, self.target
        for _, coming in self.stages[-1]:
            coming.wait_recv()
        stage = []
        if axis == "y":
            self.own.wait()
            held = target.at[:, grid.y, grid.x, grid.core]
            for hop in range(1, grid.y_size):
                origin = (grid.y + grid.y_size - hop) % grid.y_size
                stage.append(
                    self.links.copy(
                        held, held, grid.at(y=(grid.y + hop) % grid.y_size),
                        target.at[:, origin, grid.x, grid.core],
                    )
                )
        elif axis == "x":
            held = target.at[:, :, grid.x, grid.core]
            for hop in range(1, grid.x_size):
                origin = (grid.x + grid.x_size - hop) % grid.x_size
                stage.append(
                    self.links.copy(
                        held, held, (grid.exp, grid.x_from(hop)), target.at[:, :, origin, grid.core]
                    )
                )
        else:
            held = target.at[:, :, :, grid.core]
            stage.append(
                self.links.copy(
                    held, held, (grid.exp, grid.sibling(grid.fsdp)), target.at[:, :, :, 1 - grid.core]
                )
            )
        for going, _ in stage:
            going.start()
        self.stages.append(stage)

    def finish(self):
        for _, coming in self.stages[-1]:
            coming.wait_recv()
        for stage in self.stages:
            for going, _ in stage:
                going.wait_send()


def start_kernel(
    tokens, cotangent, routes_t, slots_t, attention_gain, mixture_gain, attention_in, router_t, table,
    attention_out, expert_up, expert_down, *refs, lanes, heads, width, head_count, experts, capacity,
    local,
):
    all_tokens, all_planes, cotangent_slots, position_rows, columns, full_out = refs[:6]
    shards = refs[6 : 6 + 2 * local]
    others = refs[6 + 2 * local : 6 + 4 * local]
    planes, up_stage, down_stage, send, receive, own, fetch, split = refs[6 + 4 * local :]
    grid = Grid().here()
    links = Links(send, receive)
    z_size, y_size, fsdp_size = grid.z_size, grid.y_size, grid.fsdp_size
    near = [
        grid.at(z=(grid.z + hop) % z_size, fsdp=(grid.fsdp + turn) % fsdp_size)
        for hop in range(z_size)
        for turn in range(fsdp_size)
        if hop or turn
    ]
    beside = [grid.at(y=(grid.y + hop) % y_size) for hop in range(1, y_size)]
    gathered = ChipGather(grid, links, own.at[0], tokens, all_tokens)
    widely = Wide(grid, links, own.at[2], attention_out, full_out)
    part = expert_down.shape[1]
    depth = expert_up.shape[1]
    fetches = []
    for index in range(local):
        fetches.append(
            pltpu.make_async_copy(expert_up.at[index], up_stage.at[index], fetch.at[2 * index])
        )
        fetches.append(
            pltpu.make_async_copy(
                expert_down.at[index], down_stage.at[index], fetch.at[2 * index + 1]
            )
        )
    greet(near + beside)
    gathered.start()
    widely.start()
    for copy in fetches:
        copy.start()

    feature_rows = attention_in.shape[0]
    model_width = head_count * width
    gained = attention_in[...].astype(F32) * as_column(attention_gain[...], feature_rows)
    route_rows, slot_rows = routes_t[...].astype(F32), slots_t[...].astype(F32)
    columns[...] = padded_rows(jnp.concatenate([route_rows, slot_rows], axis=0), 128).T
    row_count = columns.shape[0]
    expert_lanes = lax.broadcasted_iota(jnp.int32, (row_count, experts), 1).astype(F32)
    named = jnp.zeros((row_count, experts), F32)
    for k in range(2):
        named = named + jnp.where(expert_lanes == columns[:, k : k + 1], 1.0, 0.0)
    named = jnp.sum(named, axis=0, keepdims=True)
    place = lax.broadcasted_iota(jnp.int32, (feature_rows, feature_rows), 0)
    same = place == lax.broadcasted_iota(jnp.int32, (feature_rows, feature_rows), 1)
    router = contract_last(jnp.where(same, 1.0, 0.0).astype(BF16), router_t[...])
    pieces = [
        router,
        as_column(mixture_gain[...], feature_rows),
        padded_rows(padded_lanes(table[...].astype(F32), heads * fsdp_size), feature_rows),
        padded_rows(named, feature_rows),
    ]
    taken = sum(piece.shape[1] for piece in pieces)
    if lanes.width > lanes.weights + taken:
        pieces.append(jnp.zeros((feature_rows, lanes.width - lanes.weights - taken), F32))
    for place in range(fsdp_size):
        first, last = place * heads * width, min((place + 1) * heads * width, model_width)
        own_pieces = []
        for kind in range(3):
            if last > first:
                own_pieces.append(gained[:, kind * model_width + first : kind * model_width + last])
            if last - first < heads * width:
                own_pieces.append(
                    jnp.zeros((feature_rows, heads * width - max(last - first, 0)), F32)
                )
        planes[place] = jnp.concatenate(own_pieces + pieces, axis=1).astype(BF16)
    arrivals = [[] for _ in range(z_size)]
    sent = []
    for hop in range(z_size):
        for turn in range(fsdp_size):
            if hop == 0 and turn == 0:
                continue
            to = (grid.fsdp + turn) % fsdp_size
            origin = (grid.fsdp + fsdp_size - turn) % fsdp_size
            going, coming = links.copy(
                planes.at[to],
                all_planes.at[grid.z, grid.y, grid.fsdp],
                grid.at(z=(grid.z + hop) % z_size, fsdp=to),
                all_planes.at[(grid.z + z_size - hop) % z_size, grid.y, origin],
            )
            going.start()
            sent.append(going)
            arrivals[hop].append(coming)
    kept = pltpu.make_async_copy(
        planes.at[grid.fsdp], all_planes.at[grid.z, grid.y, grid.fsdp], own.at[1]
    )
    kept.start()
    widely.turn("y")

    for copy in fetches:
        copy.wait()
    splits, swapped = [], []
    for index in range(local):
        stores = [
            (
                up_stage.at[index, :, pl.ds(block * part, part)],
                lambda pair, block=block: pair[0].at[pl.ds(block * depth, depth), :],
            )
            for block in range(fsdp_size)
        ]
        stores.append((down_stage.at[index], lambda pair: pair[1]))
        here = shards[2 * index : 2 * index + 2]
        there = others[2 * index : 2 * index + 2]
        for source, view in stores:
            splits.append(pltpu.make_async_copy(source, view(here), split.at[len(splits)]))
            splits[-1].start()
            swapped.append(
                links.copy(
                    source, view(there), (grid.exp, grid.sibling(grid.fsdp)), view(there)
                )
            )
            swapped[-1][0].start()

    place = route_rows * capacity + slot_rows
    position_rows[...] = padded_rows(place, 8)
    select_rows(cotangent_slots, place, cotangent[...])

    forwarded = []
    for hop in range(z_size):
        held = (grid.z + z_size - hop) % z_size
        for coming in arrivals[hop]:
            coming.wait_recv()
        if hop == 0:
            kept.wait()
        for turn in range(1, y_size):
            going, coming = links.copy(
                all_planes.at[held, grid.y],
                all_planes.at[held, grid.y],
                grid.at(y=(grid.y + turn) % y_size),
                all_planes.at[held, (grid.y + y_size - turn) % y_size],
            )
            going.start()
            forwarded.append((going, coming))
        if hop == 0:
            widely.turn("x")
    gathered.forward()
    widely.turn("core")
    for going, coming in forwarded + swapped:
        coming.wait_recv()
        going.wait_send()
    for going in sent:
        going.wait_send()
    gathered.finish()
    widely.finish()
    for copy in splits:
        copy.wait()


def project_kernel(
    tokens, plane, segments, normed, query_t, key_n, query_n, value_n, key_t, value_t, bias, counts,
    weight_t, table_t, *, heads, width, lanes, feature_rows, bucket_rows,
):
    @pl.when(pl.program_id(0) == 0)
    def _():
        weight_t[...] = turned(plane[:, : lanes.weights]).astype(BF16)
        extra = plane[:, lanes.base :]
        span = bias.shape[2]
        select, reachable = bucket_rows_select(plane.shape[0], feature_rows, bucket_rows, span)
        table_t[...] = lax.dot_general(
            extra, select, (((0,), (0,)), ((), ())), preferred_element_type=F32
        )
        first = lanes.table + lax.axis_index("fsdp") * heads
        for head in range(heads):
            bias[head] = jnp.where(reachable, table_t[pl.ds(first + head, 1), :], MASKED)
        summed = jnp.sum(extra.astype(F32), axis=0, keepdims=True)
        counts[...] = pltpu.roll(
            jnp.broadcast_to(summed, counts.shape), lanes.extra - lanes.shift, 1
        )

    inputs = tokens[0].astype(F32)
    scale = lax.rsqrt(jnp.mean(inputs * inputs, axis=1, keepdims=True) + EPSILON)
    low = (inputs * scale).astype(BF16)
    normed[...] = low
    rows = low.shape[0]
    projected = contract_last(weight_t[...], low).astype(BF16).astype(F32)
    document = segments[...] % 4
    places = lax.broadcasted_iota(jnp.int32, (8, rows), 0)
    same = places == document
    hot = jnp.where(same, 1.0, 0.0)
    barred = jnp.where(same | (places >= 4), 0.0, MASKED)
    filler = jnp.zeros((SKEW - 8 - width, rows), F32)
    for head in range(heads):
        query = projected[head * width : (head + 1) * width] * width ** (-0.5)
        key = projected[(heads + head) * width : (heads + head + 1) * width]
        value = projected[(2 * heads + head) * width : (2 * heads + head + 1) * width]
        query_t[head] = jnp.concatenate([query, barred, filler], axis=0).astype(BF16)
        key_n[head] = jnp.concatenate([key, hot, filler], axis=0).T.astype(BF16)
        query_n[head] = query.T.astype(BF16)
        value_n[head] = value.T.astype(BF16)
        key_t[head] = key.astype(BF16)
        value_t[head] = value.astype(BF16)


def spans(length):
    for query_start in range(0, length, QUERY_BLOCK):
        key_start = max(0, query_start - WINDOW)
        yield query_start, key_start, query_start + QUERY_BLOCK - key_start


def spread_bias(bias, skew):
    skew[...] = pltpu.roll(
        jnp.broadcast_to(bias[0], skew.shape), 0, 1, stride=1, stride_axis=0
    )


def attend_kernel(query_t, key_n, value_t, bias, context, context_high, log_total, skew, scores, *, rows):
    spread_bias(bias, skew)
    for query_start, key_start, key_count in spans(query_t.shape[2]):
        queries = slice(query_start, query_start + QUERY_BLOCK)
        keys = slice(key_start, key_start + key_count)
        raw = matmul(key_n[0, keys, :], query_t[0, :, queries])
        for start in range(0, key_count, SKEW):
            offset = query_start - key_start - start + SKEW
            scores[start : start + SKEW, :] = (
                raw[start : start + SKEW] + skew[:, offset : offset + QUERY_BLOCK]
            )
        high = jnp.max(scores[:key_count, :], axis=0, keepdims=True)
        weights = jnp.exp(scores[:key_count, :] - high)
        total = jnp.sum(weights, axis=0, keepdims=True)
        gathered = matmul(value_t[0, :, keys], weights.astype(BF16)) / total
        context_high[0, :, queries] = gathered
        log_total[0, :, queries] = high + jnp.log(total)
        for start in range(0, QUERY_BLOCK, 128):
            place = query_start + start
            context[place // rows, :, place % rows : place % rows + 128] = gathered[
                :, start : start + 128
            ].astype(BF16)


def attend_back_kernel(
    query_t, key_n, query_n, value_n, key_t, grad_t, grad_n, context_high, log_total, bias,
    grad_projected, grad_bias, skew, grad_skew, grad_key, grad_value, *, scale,
):
    spread_bias(bias, skew)
    grad_skew[...] = jnp.zeros_like(grad_skew)
    grad_key[...] = jnp.zeros_like(grad_key)
    grad_value[...] = jnp.zeros_like(grad_value)
    inner = jnp.sum(grad_t[0].astype(F32) * context_high[0], axis=0, keepdims=True)
    for query_start, key_start, key_count in spans(query_t.shape[2]):
        queries = slice(query_start, query_start + QUERY_BLOCK)
        keys = slice(key_start, key_start + key_count)
        raw = matmul(key_n[0, keys, :], query_t[0, :, queries])
        grad_weights = matmul(value_n[0, keys, :], grad_t[0, :, queries])
        weights_low, grad_low = [], []
        for start in range(0, key_count, SKEW):
            offset = query_start - key_start - start + SKEW
            part = slice(start, start + SKEW)
            weights = jnp.exp(
                raw[part] + skew[:, offset : offset + QUERY_BLOCK] - log_total[0, :, queries]
            )
            grad_scores = weights * (grad_weights[part] - inner[:, queries])
            grad_skew[:, offset : offset + QUERY_BLOCK] += grad_scores
            weights_low.append(weights.astype(BF16))
            grad_low.append(grad_scores.astype(BF16))
        weights_low = jnp.concatenate(weights_low, axis=0)
        grad_low = jnp.concatenate(grad_low, axis=0)
        grad_projected[0, 0, :, queries] = (matmul(key_t[0, :, keys], grad_low) * scale).astype(BF16)
        grad_key[keys, :] += matmul(grad_low, query_n[0, queries, :])
        grad_value[keys, :] += matmul(weights_low, grad_n[0, queries, :])
    grad_projected[1, 0] = grad_key[...].T.astype(BF16)
    grad_projected[2, 0] = grad_value[...].T.astype(BF16)
    count = SKEW
    span = skew.shape[1]
    while count > 8:
        count //= 2
        grad_skew[:count, :] += pltpu.roll(grad_skew[count : 2 * count, :], span - count, 1)
    summed = grad_skew[0:1, :]
    for row in range(1, 8):
        summed = summed + pltpu.roll(grad_skew[row : row + 1, :], span - row, 1)
    grad_bias[0] = summed

def expert_lane(shape, lanes):
    return lax.broadcasted_iota(jnp.int32, shape, 1) - lanes.router


def int_columns(columns):
    values = columns[:, 0:4].astype(jnp.int32)
    return values[:, 0:2], values[:, 2:4]


def route_kernel(
    tokens, attended_t, attention_out, plane, columns, position_rows,
    hidden, routed, probabilities, gates, outgoing, slot_gates, *, experts, lanes, capacity,
):
    rows, model_width = tokens.shape
    routes, slots = int_columns(columns)
    attended_low = turned(attended_t[:model_width]).astype(BF16)
    hidden_state = tokens[...].astype(F32) + matmul(attended_low, attention_out[...])
    hidden[...] = hidden_state
    scale = lax.rsqrt(jnp.mean(hidden_state * hidden_state, axis=1, keepdims=True) + EPSILON)
    extra = plane[:, lanes.base :]
    gain = extra.astype(F32).T[lanes.gain : lanes.gain + 1]
    low = (hidden_state * scale * gain).astype(BF16)
    routed[...] = low
    logits = matmul(low, extra)
    lane = expert_lane(logits.shape, lanes)
    logits = jnp.where((lane >= 0) & (lane < experts), logits, MASKED)
    powers = jnp.exp(logits - jnp.max(logits, axis=1, keepdims=True))
    powers = powers / jnp.sum(powers, axis=1, keepdims=True)
    probabilities[...] = powers
    chosen = [
        jnp.sum(jnp.where(lane == routes[:, k : k + 1], powers, 0.0), axis=1, keepdims=True)
        for k in range(2)
    ]
    total = chosen[0] + chosen[1]
    gate_values = [chosen[k] / total for k in range(2)]
    pair = lax.broadcasted_iota(jnp.int32, (rows, 2), 1)
    gates[...] = jnp.where(pair == 0, gate_values[0], gate_values[1])
    members, _, gate_lanes = slot_gates.shape
    member_slots = experts // members * capacity
    slot_lanes = lax.broadcasted_iota(jnp.int32, (rows, gate_lanes), 1)
    inside = slot_lanes < member_slots
    places = routes * capacity + slots
    for member in range(members):
        by_slot = jnp.zeros((rows, gate_lanes), F32)
        for k in range(2):
            hit = (slot_lanes + member * member_slots == places[:, k : k + 1]) & inside
            by_slot = by_slot + jnp.where(hit, gate_values[k], 0.0)
        slot_gates[member] = jnp.broadcast_to(
            jnp.sum(by_slot, axis=0, keepdims=True), slot_gates.shape[1:]
        )
    select_rows(outgoing, position_rows[...], low)


def select_rows(outgoing, position_rows, values):
    slot_count, rows = outgoing.shape[0], values.shape[0]
    for start in range(0, slot_count, rows):
        slots = (lax.broadcasted_iota(jnp.int32, (rows, rows), 0) + start).astype(F32)
        picked = (slots == position_rows[0:1, :]) | (slots == position_rows[1:2, :])
        outgoing[start : start + rows, :] = matmul(
            jnp.where(picked, 1.0, 0.0).astype(BF16), values
        ).astype(BF16)


def gelu_parts(value):
    magnitude = jnp.abs(value)
    power = jnp.exp(value * value * -0.5)
    step = 1.0 / (1.0 + (0.3275911 * 0.7071067811865476) * magnitude)
    series = step * (
        0.127414796
        + step * (-0.142248368 + step * (0.7107068705 + step * (-0.7265760135 + step * 0.5307027145)))
    )
    tail = series * power
    normal = jnp.where(value < 0.0, tail, 1.0 - tail)
    return value * normal, normal + value * power * 0.3989422804014327


def expert_kernel(rows_in, cotangent, gates, *refs, shards, index, parts):
    half = shards // 2
    moved = len(parts)
    ups = list(refs[:shards])
    downs = list(refs[shards : 2 * shards - (half - 1)])
    refs = refs[2 * shards - (half - 1) :]
    sources, refs = refs[:moved], refs[moved:]
    outs_before, refs = refs[: min(index, 1)], refs[min(index, 1) :]
    rows_out, grad_rows, grad_gates, up_keep, up_taken, down_keep, down_taken = refs[:7]
    far_downs, refs = refs[7 : 7 + half - 1], refs[7 + half - 1 :]
    targets, refs = refs[:moved], refs[moved:]
    (
        up_all, down_all, rows_t, slot_t, slot_grad, total, grad_total, grad_up, grad_down,
        fetch_sem, store_sem, store_there, stored_here, send, receive, own_sem,
    ) = refs
    step = pl.program_id(0)
    grid = Grid().here()
    links = Links(send, receive)
    sibling = (grid.exp, grid.sibling(grid.fsdp))
    work = Exchange(
        grid, "exp", links, own_sem,
        [
            (partial(plane_of, source, part), target)
            for source, part, target in zip(sources, parts, targets)
        ],
    )
    across = [
        links.copy(downs[1 + number], far, sibling, far) for number, far in enumerate(far_downs)
    ]
    downs = downs + list(far_downs)
    blocks, capacity, model_width = rows_in.shape
    count = blocks * capacity
    depth = model_width // shards

    def owner(place):
        return ((grid.x + place % half) % half) * 2 + (grid.core + place // half) % 2

    def rows_of(place):
        return pl.ds(pl.multiple_of(owner(place) * depth, 16), depth)

    def fetches(place, slot):
        return [
            pltpu.make_async_copy(
                ups[shard].at[rows_of(place), :], up_all.at[slot, rows_of(shard), :],
                fetch_sem.at[slot, shard],
            )
            for shard in range(shards)
        ]

    def fetch_down(shard, slot):
        return pltpu.make_async_copy(downs[shard], down_all.at[slot], fetch_sem.at[slot, shards])

    def start_fetch(place, slot):
        for copy in fetches(place, slot):
            copy.start()
        for shard in range(shards):

            @pl.when(place == shard)
            def _(shard=shard):
                if shard > half:
                    across[shard - half - 1][1].wait_recv()
                fetch_down(shard, slot).start()

    def keep_stores(place, slot):
        return [
            pltpu.make_async_copy(
                grad_up.at[slot, rows_of(shard), :], up_keep.at[shard, rows_of(place), :],
                store_sem.at[slot, shard],
            )
            for shard in range(half)
        ]

    def give_stores(place, slot):
        return [
            pltpu.make_async_remote_copy(
                src_ref=grad_up.at[slot, rows_of(half + hop), :],
                dst_ref=up_taken.at[hop, rows_of(place), :],
                send_sem=store_there.at[slot, hop], recv_sem=stored_here.at[place, hop],
                device_id=sibling, device_id_type=MESH,
            )
            for hop in range(half)
        ]

    def down_store(place, slot):
        return pltpu.make_async_copy(
            grad_down.at[slot], down_keep.at[place % half], store_sem.at[slot, half]
        )

    def down_give(place, slot):
        return pltpu.make_async_remote_copy(
            src_ref=grad_down.at[slot], dst_ref=down_taken.at[place % half],
            send_sem=store_there.at[slot, half], recv_sem=stored_here.at[place, half],
            device_id=sibling, device_id_type=MESH,
        )

    def start_store(place, slot):
        for copy in keep_stores(place, slot) + give_stores(place, slot):
            copy.start()

        @pl.when(place < half)
        def _():
            down_store(place, slot).start()

        @pl.when(place >= half)
        def _():
            down_give(place, slot).start()

    def wait_store(place, slot):
        for copy in keep_stores(place, slot):
            copy.wait()
        for copy in give_stores(place, slot):
            copy.wait_send()

        @pl.when(place < half)
        def _():
            down_store(place, slot).wait()

        @pl.when(place >= half)
        def _():
            down_give(place, slot).wait_send()

    slot = step % 2

    @pl.when(step == 0)
    def _():
        start_fetch(0, 0)
        greet(work.peers + [sibling])
        for going, _ in across:
            going.start()
        work.start()
        rows = rows_in[...].reshape(count, model_width)
        rows_t[...] = turned(rows).astype(BF16)
        columns = gates[:, 0, :].T
        for block in range(blocks):
            part = slice(block * capacity, (block + 1) * capacity)
            gate = columns[index * capacity : (index + 1) * capacity, block : block + 1]
            slot_grad[part, :] = (gate * cotangent[block, 0].astype(F32)).astype(BF16)
        slot_t[...] = turned(slot_grad[...]).astype(BF16)
        total[...] = jnp.zeros_like(total)
        grad_total[...] = jnp.zeros_like(grad_total)

    @pl.when(step + 1 < shards)
    def _():
        start_fetch(step + 1, 1 - slot)

    for copy in fetches(step, slot):
        copy.wait()
    fetch_down(0, slot).wait()
    rows = rows_in[...].reshape(count, model_width)
    up, down = up_all[slot], down_all[slot]
    blocks_of = [slice(start, start + 256) for start in range(0, count, 256)]
    raw = [None] * len(blocks_of)
    active, grad_hidden = [], []
    raw[0] = (matmul(rows[blocks_of[0]], up), contract_last(slot_grad[blocks_of[0], :], down))
    for number, block in enumerate(blocks_of):
        if number + 1 < len(blocks_of):
            after = blocks_of[number + 1]
            raw[number + 1] = (matmul(rows[after], up), contract_last(slot_grad[after, :], down))
        hidden, grad_active = raw[number]
        activated, slope = gelu_parts(hidden)
        active.append(activated.astype(BF16))
        grad_hidden.append((grad_active * slope).astype(BF16))
        total[block, :] += matmul(active[number], down)
        grad_total[block, :] += contract_last(grad_hidden[number], up)
    active = jnp.concatenate(active, axis=0)
    grad_hidden = jnp.concatenate(grad_hidden, axis=0)

    @pl.when(step >= 2)
    def _():
        wait_store(step - 2, slot)

    grad_up[slot] = matmul(rows_t[...], grad_hidden).astype(BF16)
    grad_down[slot] = matmul(slot_t[...], active).T.astype(BF16)
    start_store(step, slot)

    @pl.when(step == shards - 1)
    def _():
        low = total[...].astype(BF16)
        for before in outs_before:
            rows_out[:, :index] = before[...]
        rows_out[:, index] = low.reshape(blocks, capacity, model_width)
        grad_rows[...] = grad_total[...].astype(BF16).reshape(grad_rows.shape)
        ones = jnp.ones((8, model_width), F32)
        for block in range(blocks):
            product = low[block * capacity : (block + 1) * capacity].astype(F32) * cotangent[
                block, 0
            ].astype(F32)
            grad_gates[block] = lax.dot_general(
                ones, product, (((1,), (1,)), ((), ())), precision=lax.Precision.HIGHEST,
                preferred_element_type=F32,
            )
        if shards > 1:
            wait_store(step - 1, 1 - slot)
        wait_store(step, slot)
        for place in range(shards):
            for copy in give_stores(place, 0):
                copy.wait_recv()
            if place >= half:
                down_give(place, 0).wait_recv()
        for going, _ in across:
            going.wait_send()
        work.finish()


def run_expert(index, incoming, cotangent, gates, ups, downs, moved, outs_before, collective_id):
    grid = Grid()
    shards = len(ups)
    half = shards // 2
    blocks, capacity, model_width = incoming.shape
    part = downs[0].shape[0]
    count = blocks * capacity
    extra = len(moved)
    copies = extra * grid.exp_size + half
    before = [] if outs_before is None else [outs_before]
    outputs = pl.pallas_call(
        partial(expert_kernel, shards=shards, index=index, parts=[place for _, place in moved]),
        grid=(shards,),
        in_specs=[
            whole(incoming.shape),
            pl.BlockSpec((blocks, 1, capacity, model_width), lambda s: (0, index, 0, 0)),
            whole(gates.shape),
        ]
        + [ANYWHERE] * (len(ups) + len(downs) + extra)
        + [whole(array.shape) for array in before],
        out_specs=tuple(
            [
                whole((blocks, index + 1, capacity, model_width)),
                whole((blocks, capacity, model_width)),
                whole((blocks, 8, capacity)),
            ]
            + [ANYWHERE] * (4 + half - 1 + extra)
        ),
        scratch_shapes=[
            pltpu.VMEM((2, model_width, part), BF16),
            pltpu.VMEM((2, part, model_width), BF16),
            pltpu.VMEM((model_width, count), BF16),
            pltpu.VMEM((model_width, count), BF16),
            pltpu.VMEM((count, model_width), BF16),
            pltpu.VMEM((count, model_width), F32),
            pltpu.VMEM((count, model_width), F32),
            pltpu.VMEM((2, model_width, part), BF16),
            pltpu.VMEM((2, part, model_width), BF16),
            pltpu.SemaphoreType.DMA((2, shards + 1)),
            pltpu.SemaphoreType.DMA((2, half + 1)),
            pltpu.SemaphoreType.DMA((2, half + 1)),
            pltpu.SemaphoreType.DMA((shards, half + 1)),
            dma_sems(copies),
            dma_sems(copies),
            dma_sems(max(extra, 1)),
        ],
        out_shape=tuple(
            [
                shape_of((blocks, index + 1, capacity, model_width), BF16),
                shape_of((blocks, capacity, model_width), BF16),
                shape_of((blocks, 8, capacity), F32),
            ]
            + [shape_of((half, model_width, part), BF16)] * 2
            + [shape_of((half, part, model_width), BF16)] * 2
            + [shape_of((part, model_width), BF16)] * (half - 1)
            + [
                shape_of((grid.exp_size,) + array.shape[(1 if place is None else 2) :], array.dtype)
                for array, place in moved
            ]
        ),
        compiler_params=params(collective_id=collective_id, has_side_effects=True),
        cost_estimate=hint(35),
        name=f"expert_{index}",
    )(incoming, cotangent, gates, *ups, *downs, *[array for array, _ in moved], *before)
    up_keep, up_taken, down_keep, down_taken = outputs[3:7]
    return outputs[:3], ((up_keep, up_taken), (down_keep, down_taken)), outputs[7 + half - 1 :]


def local_picks(routes, slots, capacity, local, index, slot_count):
    member, which = lax.div(routes, local), lax.rem(routes, local)
    places = jnp.where(which == index, member * capacity + slots, -1)
    lane = lax.broadcasted_iota(jnp.int32, (routes.shape[0], slot_count), 1)
    return [lane == places[:, k : k + 1] for k in range(2)]


def unroute_kernel(
    hidden, cotangent, routed, probabilities, gates, plane, columns, counts, *refs,
    experts, local, token_total, lanes,
):
    grads, gate_grads = refs[:local], refs[local : 2 * local]
    grad_hidden, grad_branch, small = refs[2 * local :]
    rows = hidden.shape[0]
    members, capacity, model_width = grads[0].shape
    grad_output = cotangent[...].astype(F32)
    grad_routed = jnp.zeros(hidden.shape, F32)
    found = [jnp.zeros((rows, capacity), F32), jnp.zeros((rows, capacity), F32)]
    routes, slots = int_columns(columns)
    member, which = lax.div(routes, local), lax.rem(routes, local)
    lane = lax.broadcasted_iota(jnp.int32, (rows, capacity), 1)
    for index in range(local):
        picks = local_picks(routes, slots, capacity, local, index, members * capacity)
        grad_routed = grad_routed + matmul(
            jnp.where(picks[0] | picks[1], 1.0, 0.0).astype(BF16),
            grads[index][...].reshape(members * capacity, model_width),
        )
        for place in range(members):
            spots = jnp.where((which == index) & (member == place), slots, -1)
            for k in range(2):
                found[k] = found[k] + jnp.where(
                    lane == spots[:, k : k + 1], gate_grads[index][place, 0:1, :], 0.0
                )
    grad_gates = [jnp.sum(found[k], axis=1, keepdims=True) for k in range(2)]
    powers = probabilities[...]
    lane = expert_lane(powers.shape, lanes)
    inside = (lane >= 0) & (lane < experts)
    picked = [lane == routes[:, k : k + 1] for k in range(2)]
    chosen_total = sum(
        jnp.sum(jnp.where(picked[k], powers, 0.0), axis=1, keepdims=True) for k in range(2)
    )
    weighted = grad_gates[0] * gates[:, 0:1] + grad_gates[1] * gates[:, 1:2]
    grad_mass = (AUX_WEIGHT * experts / (2.0 * token_total * token_total)) * counts[0:1, :]
    grad_mass = jnp.where(inside, grad_mass, 0.0)
    for k in range(2):
        grad_mass = grad_mass + jnp.where(picked[k], (grad_gates[k] - weighted) / chosen_total, 0.0)
    grad_logits = powers * (grad_mass - jnp.sum(powers * grad_mass, axis=1, keepdims=True))
    extra = plane[:, lanes.base :]
    grad_routed = grad_routed + contract_last(grad_logits.astype(BF16), extra)
    hidden_state = hidden[...]
    scale = lax.rsqrt(jnp.mean(hidden_state * hidden_state, axis=1, keepdims=True) + EPSILON)
    normed = hidden_state * scale
    product = grad_routed * normed
    gain_grad = jnp.sum(product, axis=0, keepdims=True)
    small_t = matmul(grad_logits.T.astype(BF16), routed[...])
    row = lax.broadcasted_iota(jnp.int32, small_t.shape, 0)
    small_t = jnp.where(row == lanes.gain, gain_grad, small_t)
    small[...] = small_t.T
    gains = extra.astype(F32).T[lanes.gain : lanes.gain + 1]
    grad = scale * (
        grad_routed * gains - normed * jnp.mean(product * gains, axis=1, keepdims=True)
    ) + grad_output
    grad_hidden[...] = grad
    grad_branch[...] = grad.astype(BF16)


def context_grad_kernel(
    fsdp_index, grad_branch, attention_out, context, grad_t, grad_n, grad_out, total, *, heads, width
):
    @pl.when(pl.program_id(0) == 0)
    def _():
        total[...] = jnp.zeros_like(total)

    branch = grad_branch[0]
    grad = contract_last(attention_out[...], branch).astype(BF16)
    for head in range(heads):
        part = grad[head * width : (head + 1) * width]
        grad_t[head] = part
        grad_n[head] = turned(part).astype(BF16)
    total[...] += matmul(context[0], branch)

    @pl.when(pl.program_id(0) == pl.num_programs(0) - 1)
    def _():
        grad_out[...] = total[...].astype(BF16)


def project_back_kernel(
    grad_projected, normed, plane, small, probabilities, grad_bias, grad_first, grad_plane, total,
    bias_t, *, lanes, heads, feature_rows, bucket_rows,
):
    step = pl.program_id(0)

    @pl.when(step == 0)
    def _():
        total[...] = jnp.zeros_like(total)

    grad = grad_projected[...]
    grad_first[0] = matmul(plane[:, : lanes.weights], grad).astype(BF16)
    total[: lanes.weights, :] += matmul(grad, normed[...])

    @pl.when(step == pl.num_programs(0) - 1)
    def _():
        grad_plane[...] = total[...].T.astype(BF16)
        span = grad_bias.shape[2]
        select, _ = bucket_rows_select(plane.shape[0], feature_rows, bucket_rows, span)
        bias_t[...] = jnp.zeros_like(bias_t)
        first = lanes.table + lax.axis_index("fsdp") * heads
        for head in range(heads):
            bias_t[pl.ds(first + head, 1), :] = grad_bias[head]
        high = bias_t[...].astype(BF16)
        rest = (bias_t[...] - high.astype(F32)).astype(BF16)
        table = contract_last(select, high) + contract_last(select, rest)
        mass = jnp.sum(probabilities[...], axis=0, keepdims=True)
        mass = pltpu.roll(jnp.broadcast_to(mass, (8, lanes.extra)), lanes.shift, 1)[0:1]
        lane = lax.broadcasted_iota(jnp.int32, table.shape, 1)
        row = lax.broadcasted_iota(jnp.int32, table.shape, 0)
        is_small = (lane >= lanes.router) & (lane < lanes.table)
        is_mass = (lane >= lanes.count) & (lax.rem(row, feature_rows) == 0)
        extra = table + jnp.where(is_small, small[...], 0.0) + jnp.where(is_mass, mass, 0.0)
        grad_plane[:, lanes.base :] = (total[lanes.base :, :].T + extra).astype(BF16)


def last_kernel(
    first, planes, out_grad, first_parts, plane_parts, out_parts,
    first_in, first_sum, planes_in, plane_sum, send, receive, own, *, spread_out,
):
    grid = Grid().here()
    links = Links(send, receive)
    z_size, y_size, x_size, fsdp_size = grid.z_size, grid.y_size, grid.x_size, grid.fsdp_size
    exp_size = grid.exp_size
    sibling = grid.sibling(grid.fsdp)
    near = [
        grid.at(z=(grid.z + hop) % z_size, fsdp=(grid.fsdp + turn) % fsdp_size)
        for hop in range(z_size)
        for turn in range(fsdp_size)
        if hop or turn
    ]
    beside = [grid.at(y=(grid.y + hop) % y_size) for hop in range(1, y_size)]

    per_sender = grid.device_count if spread_out else exp_size
    base = 0 if spread_out else grid.fsdp * exp_size
    out_sends = []
    for number in range(per_sender):
        to = base + number
        out_sends.append((to, number))
    if spread_out:
        out_origins = [(origin, origin) for origin in range(grid.device_count)]
    else:
        out_origins = [
            (member * fsdp_size + grid.linear // exp_size, member) for member in range(exp_size)
        ]
    own_slot = grid.linear if spread_out else grid.exp
    out_base = links.used
    links.used += per_sender

    def place_of(linear):
        return (linear // fsdp_size, linear % fsdp_size)

    def out_copy(to, number, slot):
        return pltpu.make_async_remote_copy(
            src_ref=out_grad.at[number], dst_ref=out_parts.at[slot],
            send_sem=send.at[out_base + number], recv_sem=receive.at[out_base + slot],
            device_id=place_of(to), device_id_type=MESH,
        )

    barrier = pltpu.get_barrier_semaphore()
    for device in near + beside:
        pl.semaphore_signal(barrier, inc=1, device_id=device, device_id_type=MESH)
    for origin, _ in out_origins:

        @pl.when(origin != grid.linear)
        def _(origin=origin):
            pl.semaphore_signal(
                barrier, inc=1, device_id=place_of(origin), device_id_type=MESH
            )

    to_self = (
        1 if spread_out else jnp.where(grid.linear // exp_size == grid.fsdp, 1, 0)
    )
    pl.semaphore_wait(barrier, len(near) + len(beside) + per_sender - to_self)

    first_copies = []
    for hop in range(x_size):
        mine = grid.x_from(hop)
        first_copies.append(
            links.copy(
                first.at[grid.sibling(mine)], first_in.at[hop], (grid.exp, sibling), first_in.at[hop]
            )
        )
        first_copies[-1][0].start()
    beside_copies = []
    for hop in range(1, y_size):
        to = (grid.y + hop) % y_size
        beside_copies.append(
            links.copy(
                planes.at[:, to], planes_in.at[hop - 1], grid.at(y=to), planes_in.at[hop - 1]
            )
        )
        beside_copies[-1][0].start()
    for to, number in out_sends:

        @pl.when(to != grid.linear)
        def _(to=to, number=number):
            out_copy(to, number, own_slot).start()

        @pl.when(to == grid.linear)
        def _(number=number):
            pltpu.make_async_copy(out_grad.at[number], out_parts.at[own_slot], own.at[0]).start()

    along_x = []
    for hop in range(x_size):
        first_copies[hop][1].wait_recv()
        summed = first[grid.x_from(hop)].astype(F32) + first_in[hop].astype(F32)
        if hop == 0:
            first_parts[0] = summed.astype(BF16)
        else:
            first_sum[hop - 1] = summed.astype(BF16)
            along_x.append(
                links.copy(
                    first_sum.at[hop - 1], first_parts.at[hop], (grid.exp, grid.x_from(hop)),
                    first_parts.at[hop],
                )
            )
            along_x[-1][0].start()
    for going, coming in beside_copies:
        coming.wait_recv()
    along_z = []
    for hop in list(range(1, z_size)) + [0]:
        to_z = (grid.z + hop) % z_size
        summed = planes[to_z, grid.y].astype(F32)
        for other in range(y_size - 1):
            summed = summed + planes_in[other, to_z].astype(F32)
        plane_sum[hop] = summed.astype(BF16)
        for turn in range(fsdp_size):
            if hop == 0 and turn == 0:
                continue
            to = (grid.fsdp + turn) % fsdp_size
            origin = (grid.fsdp + fsdp_size - turn) % fsdp_size
            along_z.append(
                links.copy(
                    plane_sum.at[hop, to],
                    plane_parts.at[hop, grid.fsdp],
                    grid.at(z=to_z, fsdp=to),
                    plane_parts.at[hop, origin],
                )
            )
            along_z[-1][0].start()
    kept = pltpu.make_async_copy(
        plane_sum.at[0, grid.fsdp], plane_parts.at[0, grid.fsdp], own.at[1]
    )
    kept.start()
    for going, coming in along_x + along_z:
        coming.wait_recv()
    for going, _ in first_copies + beside_copies + along_x + along_z:
        going.wait_send()
    kept.wait()
    for origin, slot in out_origins:

        @pl.when(origin != grid.linear)
        def _(origin=origin, slot=slot):
            out_copy(origin, 0, slot).wait_recv()

    for to, number in out_sends:

        @pl.when(to != grid.linear)
        def _(to=to, number=number):
            out_copy(to, number, own_slot).wait_send()

        @pl.when(to == grid.linear)
        def _(number=number):
            pltpu.make_async_copy(out_grad.at[number], out_parts.at[own_slot], own.at[0]).wait()


def mixture_kernel(hidden, gates, columns, rows_in, output, *, local):
    members, _, capacity, model_width = rows_in.shape
    routes, slots = int_columns(columns)
    total = hidden[...]
    picked = [jnp.zeros(hidden.shape, F32), jnp.zeros(hidden.shape, F32)]
    for index in range(local):
        picks = local_picks(routes, slots, capacity, local, index, members * capacity)
        values = rows_in[:, index].reshape(members * capacity, model_width)
        for k in range(2):
            picked[k] = picked[k] + matmul(jnp.where(picks[k], 1.0, 0.0).astype(BF16), values)
    for k in range(2):
        total = total + gates[:, k : k + 1] * picked[k]
    output[...] = total.astype(BF16)


def finish_kernel(
    first_parts, plane_parts, out_parts, tokens, grad_hidden, attention_in, attention_gain, counts,
    grad_tokens, grad_gain, grad_in, grad_out, grad_mixture, grad_router, grad_table, balance,
    *, lanes, heads, width, head_count, experts, token_total,
):
    total = jnp.sum(first_parts[...].astype(F32), axis=0).T
    inputs = tokens[...].astype(F32)
    scale = lax.rsqrt(jnp.mean(inputs * inputs, axis=1, keepdims=True) + EPSILON)
    normed = inputs * scale
    grad_tokens[...] = grad_hidden[...] + scale * (
        total - normed * jnp.mean(total * normed, axis=1, keepdims=True)
    )
    fsdp_size = plane_parts.shape[1]
    model_width = head_count * width
    summed = jnp.sum(plane_parts[...].astype(F32), axis=0)
    sums = [summed[place] for place in range(fsdp_size)]
    columns = []
    for kind in range(3):
        pieces = [
            sums[place][:, kind * heads * width : (kind + 1) * heads * width]
            for place in range(fsdp_size)
        ]
        columns.append(jnp.concatenate(pieces, axis=1)[:, :model_width])
    gathered = jnp.concatenate(columns, axis=1)
    feature_rows = gathered.shape[0]
    gain = jnp.sum(gathered * attention_in[...].astype(F32), axis=1, keepdims=True)
    gain = padded_rows(jnp.broadcast_to(gain, (feature_rows, 128)), 128).T
    grad_gain[...] = gain[0:1, :feature_rows]
    grad_in[...] = gathered * as_column(attention_gain[...], feature_rows)
    grad_out[...] = jnp.sum(out_parts[...].astype(F32), axis=0)
    extra = sum(part[:, lanes.base :] for part in sums)
    extra_t = padded_rows(extra, 128).T
    grad_mixture[...] = extra_t[lanes.gain : lanes.gain + 1, :feature_rows]
    grad_router[...] = extra_t[lanes.router : lanes.router + experts, :feature_rows]
    grad_table[...] = extra[: grad_table.shape[0], lanes.table : lanes.table + head_count]
    mass = jnp.broadcast_to(extra[0:1], (8, lanes.extra))
    mass = pltpu.roll(mass, lanes.extra - lanes.shift, 1)
    lane = expert_lane(mass.shape, lanes)
    terms = jnp.where((lane >= 0) & (lane < experts), mass * counts[...], 0.0)[0:1]
    balance[...] = jnp.sum(terms, axis=1, keepdims=True) * (
        experts / (2.0 * token_total * token_total)
    )


def sum_kernel(*refs, local, terms):
    outputs = refs[2 * local * terms :]
    for which in range(2):
        for index in range(local):
            first = (index * 2 + which) * terms
            shape = outputs[which].shape[1:]
            total = refs[first][...].reshape(shape).astype(F32)
            for ref in refs[first + 1 : first + terms]:
                total = total + ref[...].reshape(shape).astype(F32)
            outputs[which][index] = total


def sum_grads(groups, up_shape, down_shape, blocks):
    local = len(groups)
    depth, part = up_shape[1], down_shape[1]
    sizes = ((depth, part), (part // blocks, down_shape[2]))
    arrays, specs = [], []
    for group in groups:
        for size, (keep, taken, passed) in zip(sizes, group):
            for array in (keep, taken):
                arrays.append(array)
                specs.append(pl.BlockSpec((1,) + size, lambda c: (0, c, 0)))
            for array in passed:
                arrays.append(array)
                specs.append(pl.BlockSpec(size, lambda c: (c, 0)))
    return pl.pallas_call(
        partial(sum_kernel, local=local, terms=len(arrays) // (2 * local)),
        grid=(blocks,),
        in_specs=specs,
        out_specs=[
            pl.BlockSpec((local, depth, part), lambda c: (0, 0, c)),
            pl.BlockSpec((local, part // blocks, down_shape[2]), lambda c: (0, c, 0)),
        ],
        out_shape=(shape_of(up_shape, F32), shape_of(down_shape, F32)),
        compiler_params=params(),
        cost_estimate=hint(8),
        name="sum_grads",
    )(*arrays)


def over_x(array, hop):
    fsdp_size = lax.axis_size("fsdp")
    return lax.ppermute(array, "fsdp", [(i, (i + 2 * hop) % fsdp_size) for i in range(fsdp_size)])


def over_core(array):
    return lax.ppermute(array, "fsdp", [(i, i ^ 1) for i in range(lax.axis_size("fsdp"))])


def on_device(
    tokens,
    cotangent,
    segments,
    routes,
    slots,
    attention_gain,
    mixture_gain,
    attention_in,
    attention_out,
    router_weight,
    position_table,
    expert_up,
    expert_down,
):
    grid = Grid()
    exp_size, fsdp_size, chips = grid.exp_size, grid.fsdp_size, grid.x_size
    device_count = grid.device_count
    fsdp_index = lax.axis_index("fsdp")
    rows, model_width = tokens.shape
    length = rows * fsdp_size
    head_count = position_table.shape[1]
    width = model_width // head_count
    heads = -(-head_count // fsdp_size)
    padded_heads = heads * fsdp_size
    feature_rows, bucket_rows = attention_in.shape[0], position_table.shape[0]
    experts = router_weight.shape[1]
    local = expert_up.shape[0]
    capacity = 4 * rows // experts
    token_total = rows * device_count
    span = WINDOW + 2 * SKEW + QUERY_BLOCK
    lanes = Lanes(heads, width, padded_heads, experts)
    part = expert_down.shape[1]
    gain_row = attention_gain.reshape(1, feature_rows)

    shard_shapes = [shape_of((model_width, part), BF16), shape_of((part, model_width), BF16)]
    copies = (
        2 * fsdp_size + grid.z_size * fsdp_size + grid.z_size * grid.y_size
        + grid.z_size + grid.y_size + grid.x_size + 1 + local * (fsdp_size + 1)
    )
    started = pl.pallas_call(
        partial(
            start_kernel, lanes=lanes, heads=heads, width=width, head_count=head_count,
            experts=experts, capacity=capacity, local=local,
        ),
        out_shape=tuple(
            [
                shape_of((fsdp_size, rows, model_width), BF16),
                shape_of((grid.z_size, grid.y_size, fsdp_size, feature_rows, lanes.width), BF16),
                shape_of((experts * capacity, model_width), BF16),
                shape_of((8, rows), F32),
                shape_of((rows, 128), F32),
                shape_of((grid.z_size, grid.y_size, chips, 2, feature_rows, model_width), BF16),
            ]
            + shard_shapes * (2 * local)
        ),
        in_specs=[ANYWHERE] + [IN_VMEM] * 8 + [ANYWHERE] * 3,
        out_specs=tuple(
            [ANYWHERE, ANYWHERE, IN_VMEM, IN_VMEM, IN_VMEM, ANYWHERE] + [ANYWHERE] * (4 * local)
        ),
        scratch_shapes=[
            pltpu.VMEM((fsdp_size, feature_rows, lanes.width), BF16),
            pltpu.VMEM(expert_up.shape, BF16),
            pltpu.VMEM(expert_down.shape, BF16),
            dma_sems(copies),
            dma_sems(copies),
            dma_sems(3),
            dma_sems(2 * local),
            dma_sems(local * (fsdp_size + 1)),
        ],
        compiler_params=params(collective_id=0, has_side_effects=True),
        cost_estimate=hint(20),
        name="start",
    )(
        tokens, cotangent, routes.T, slots.T, gain_row, mixture_gain.reshape(1, feature_rows),
        attention_in, router_weight.T, position_table, attention_out, expert_up, expert_down,
    )
    all_tokens, all_planes, cotangent_slots, position_rows, columns, full_out = started[:6]
    own_shards = [started[6 + 2 * index : 8 + 2 * index] for index in range(local)]
    other_shards = [
        started[6 + 2 * (local + index) : 8 + 2 * (local + index)] for index in range(local)
    ]
    plane = all_planes.reshape(model_width, lanes.width)
    full_out = full_out.reshape(model_width, model_width)

    def along_x(array):
        return [over_x(array, -hop) for hop in range(1, chips)]

    near_up, near_down = [None] * local, [None] * local
    near_up[0] = along_x(own_shards[0][0])
    cotangent_in = lax.all_to_all(
        cotangent_slots.reshape(exp_size, local * capacity, model_width),
        "exp", split_axis=0, concat_axis=0, tiled=True,
    ).reshape(exp_size, local, capacity, model_width)

    head_t = lambda size: pl.BlockSpec((heads, size, rows), lambda s, *_: (0, 0, s))
    head_n = lambda size: pl.BlockSpec((heads, rows, size), lambda s, *_: (0, s, 0))
    normed, query_t, key_n, query_n, value_n, key_t, value_t, bias, counts = pl.pallas_call(
        partial(
            project_kernel, heads=heads, width=width, lanes=lanes, feature_rows=feature_rows,
            bucket_rows=bucket_rows,
        ),
        grid=(fsdp_size,),
        in_specs=[
            pl.BlockSpec((1, rows, model_width), lambda s: (s, 0, 0)),
            whole((model_width, lanes.width)),
            pl.BlockSpec((1, rows), lambda s: (0, s)),
        ],
        out_specs=[
            pl.BlockSpec((rows, model_width), lambda s: (s, 0)),
            head_t(SKEW), head_n(SKEW), head_n(width), head_n(width), head_t(width), head_t(width),
            whole((heads, 1, span)),
            whole((8, lanes.extra)),
        ],
        out_shape=(
            shape_of((length, model_width), BF16),
            shape_of((heads, SKEW, length), BF16),
            shape_of((heads, length, SKEW), BF16),
            shape_of((heads, length, width), BF16),
            shape_of((heads, length, width), BF16),
            shape_of((heads, width, length), BF16),
            shape_of((heads, width, length), BF16),
            shape_of((heads, 1, span), F32),
            shape_of((8, lanes.extra), F32),
        ),
        scratch_shapes=[
            pltpu.VMEM((lanes.weights, model_width), BF16),
            pltpu.VMEM((lanes.extra, span), F32),
        ],
        compiler_params=params(),
        cost_estimate=hint(8),
        name="project",
    )(all_tokens, plane, segments.reshape(1, length))

    by_head = lambda *size: pl.BlockSpec((1,) + size, lambda h: (h, 0, 0))
    context, context_high, log_total = pl.pallas_call(
        partial(attend_kernel, rows=rows),
        grid=(heads,),
        in_specs=[
            by_head(SKEW, length), by_head(length, SKEW), by_head(width, length), by_head(1, span),
        ],
        out_specs=[
            pl.BlockSpec((fsdp_size, width, rows), lambda h: (0, h, 0)),
            by_head(width, length),
            by_head(1, length),
        ],
        out_shape=(
            shape_of((fsdp_size, heads * width, rows), BF16),
            shape_of((heads, width, length), F32),
            shape_of((heads, 1, length), F32),
        ),
        scratch_shapes=[
            pltpu.VMEM((SKEW, span), F32),
            pltpu.VMEM((WINDOW + QUERY_BLOCK, QUERY_BLOCK), F32),
        ],
        compiler_params=params(),
        cost_estimate=hint(13),
        name="attend",
    )(query_t, key_n, value_t, bias)

    (attended_t,) = exchange("fsdp", [(context, None)], 1, 9)
    own_down, near_up[0], attended_t = lax.optimization_barrier(
        (own_shards[0][1], near_up[0], attended_t)
    )
    near_down[0] = along_x(own_down)
    far_up = [[over_core(array) for array in near_up[0]]]
    attended_t = attended_t.reshape(padded_heads * width, rows)

    gate_lanes = -(-local * capacity // 128) * 128
    hidden, routed, probabilities, gates, outgoing, slot_gates = pl.pallas_call(
        partial(route_kernel, experts=experts, lanes=lanes, capacity=capacity),
        out_shape=(
            shape_of((rows, model_width), F32),
            shape_of((rows, model_width), BF16),
            shape_of((rows, lanes.extra), F32),
            shape_of((rows, 2), F32),
            shape_of((experts * capacity, model_width), BF16),
            shape_of((exp_size, 8, gate_lanes), F32),
        ),
        compiler_params=params(),
        cost_estimate=hint(7),
        name="route",
    )(tokens, attended_t, full_out, plane, columns, position_rows)

    later = [own_shards[index] for index in range(1, local)]
    outgoing, later = lax.optimization_barrier((outgoing, later))
    for index in range(1, local):
        near_up[index], near_down[index] = [along_x(array) for array in later[index - 1]]
    outgoing = outgoing.reshape(exp_size, local, capacity, model_width)
    incoming, gates_in = exchange("exp", [(outgoing, 0), (slot_gates, None)], 2, 28)

    def pass_on(keep, taken):
        return [
            over_x((keep[hop].astype(F32) + taken[hop].astype(F32)).astype(BF16), hop)
            for hop in range(1, chips)
        ]

    returned, groups, moved, outs, later_pass = [], [], [], None, None
    for index in range(local):
        if index > 0:
            near_up[index], incoming = lax.optimization_barrier((near_up[index], incoming))
            far_up.append([over_core(array) for array in near_up[index]])
        carried = list(moved)
        if index + 1 < local:
            carried.append((outgoing, index + 1))
        (outs, grad, gate_grad), sums, arrived = run_expert(
            index, incoming, cotangent_in, gates_in,
            [own_shards[index][0]] + near_up[index] + [other_shards[index][0]] + far_up[index],
            [own_shards[index][1]] + near_down[index] + [other_shards[index][1]],
            carried, outs, 3 + index,
        )
        if index + 1 < local:
            incoming = arrived[-1]
            arrived = arrived[:-1]
        if index > 0:
            returned.append(arrived)
        moved = [(grad, None), (gate_grad, None)]
        if index + 1 < local:
            sums, incoming = lax.optimization_barrier((sums, incoming))
            groups.append([(keep, taken, pass_on(keep, taken)) for keep, taken in sums])

    (up_keep, up_taken), (down_keep, down_taken) = sums
    up_keep, up_taken, last_grad = lax.optimization_barrier((up_keep, up_taken, moved[0][0]))
    up_passed = pass_on(up_keep, up_taken)
    returned.append(exchange("exp", [(last_grad, None), moved[1]], 3 + local, 28))

    outs, returned = lax.optimization_barrier((outs, returned))
    out_rows = lax.all_to_all(outs, "exp", split_axis=0, concat_axis=0, tiled=True)

    grad_hidden, grad_branch, small = pl.pallas_call(
        partial(
            unroute_kernel, experts=experts, local=local, token_total=token_total, lanes=lanes
        ),
        out_shape=(
            shape_of((rows, model_width), F32),
            shape_of((rows, model_width), BF16),
            shape_of((model_width, lanes.extra), F32),
        ),
        compiler_params=params(),
        cost_estimate=hint(7),
        name="unroute",
    )(
        hidden, cotangent, routed, probabilities, gates, plane, columns, counts,
        *[part[0] for part in returned], *[part[1] for part in returned],
    )

    up_passed, grad_branch = lax.optimization_barrier((up_passed, grad_branch))
    all_branch = gather_rows(grad_branch, 4 + local, 15)
    down_keep, down_taken, all_branch = lax.optimization_barrier(
        (down_keep, down_taken, all_branch)
    )
    groups.append(
        [(up_keep, up_taken, up_passed), (down_keep, down_taken, pass_on(down_keep, down_taken))]
    )
    padded_out = full_out
    if padded_heads > head_count:
        padded_out = jnp.pad(full_out, ((0, padded_heads * width - model_width), (0, 0)))
    grad_t, grad_n, out_grad = pl.pallas_call(
        partial(context_grad_kernel, heads=heads, width=width),
        grid_spec=pltpu.PrefetchScalarGridSpec(
            num_scalar_prefetch=1,
            grid=(fsdp_size,),
            in_specs=[
                pl.BlockSpec((1, rows, model_width), lambda s, f: (s, 0, 0)),
                pl.BlockSpec((heads * width, model_width), lambda s, f: (f[0], 0)),
                pl.BlockSpec((1, heads * width, rows), lambda s, f: (s, 0, 0)),
            ],
            out_specs=[head_t(width), head_n(width), whole((heads * width, model_width))],
            scratch_shapes=[pltpu.VMEM((heads * width, model_width), F32)],
        ),
        out_shape=(
            shape_of((heads, width, length), BF16),
            shape_of((heads, length, width), BF16),
            shape_of((heads * width, model_width), BF16),
        ),
        compiler_params=params(),
        cost_estimate=hint(5),
        name="context_grad",
    )(fsdp_index.reshape(1), all_branch, padded_out, context)

    grad_projected, grad_bias = pl.pallas_call(
        partial(attend_back_kernel, scale=width ** (-0.5)),
        grid=(heads,),
        in_specs=[
            by_head(SKEW, length), by_head(length, SKEW), by_head(length, width),
            by_head(length, width), by_head(width, length), by_head(width, length),
            by_head(length, width), by_head(width, length), by_head(1, length), by_head(1, span),
        ],
        out_specs=[
            pl.BlockSpec((3, 1, width, length), lambda h: (0, h, 0, 0)),
            by_head(1, span),
        ],
        out_shape=(
            shape_of((3, heads, width, length), BF16),
            shape_of((heads, 1, span), F32),
        ),
        scratch_shapes=[
            pltpu.VMEM((SKEW, span), F32),
            pltpu.VMEM((SKEW, span), F32),
            pltpu.VMEM((length, width), F32),
            pltpu.VMEM((length, width), F32),
        ],
        compiler_params=params(),
        cost_estimate=hint(15),
        name="attend_back",
    )(query_t, key_n, query_n, value_n, key_t, grad_t, grad_n, context_high, log_total, bias)
    grad_projected = grad_projected.reshape(lanes.weights, length)

    grad_first, grad_plane = pl.pallas_call(
        partial(
            project_back_kernel, lanes=lanes, heads=heads, feature_rows=feature_rows,
            bucket_rows=bucket_rows,
        ),
        grid=(fsdp_size,),
        in_specs=[
            pl.BlockSpec((lanes.weights, rows), lambda s: (0, s)),
            pl.BlockSpec((rows, model_width), lambda s: (s, 0)),
            whole((model_width, lanes.width)),
            whole((model_width, lanes.extra)),
            whole((rows, lanes.extra)),
            whole((heads, 1, span)),
        ],
        out_specs=[
            pl.BlockSpec((1, model_width, rows), lambda s: (s, 0, 0)),
            whole((model_width, lanes.width)),
        ],
        out_shape=(
            shape_of((fsdp_size, model_width, rows), BF16),
            shape_of((model_width, lanes.width), BF16),
        ),
        scratch_shapes=[
            pltpu.VMEM((lanes.width, model_width), F32),
            pltpu.VMEM((lanes.extra, span), F32),
        ],
        compiler_params=params(),
        cost_estimate=hint(9),
        name="project_back",
    )(grad_projected, normed, plane, small, probabilities, grad_bias)

    out_rows, grad_first = lax.optimization_barrier((out_rows, grad_first))
    spread_out = heads * width * fsdp_size != model_width
    if spread_out:
        out_grad = lax.dynamic_update_slice(
            jnp.zeros((padded_heads * width, model_width), BF16), out_grad,
            (fsdp_index * heads * width, jnp.int32(0)),
        )[:model_width]
    out_grad = out_grad.reshape(-1, feature_rows, model_width)
    out_count = device_count if spread_out else exp_size
    plane_shape = (grid.z_size, grid.y_size, fsdp_size, feature_rows, lanes.width)
    parts_shape = (grid.z_size, fsdp_size, feature_rows, lanes.width)
    copies = 2 * fsdp_size + grid.z_size * fsdp_size + grid.y_size + out_count
    first_parts, plane_parts, out_parts = pl.pallas_call(
        partial(last_kernel, spread_out=spread_out),
        out_shape=(
            shape_of((chips, model_width, rows), BF16),
            shape_of(parts_shape, BF16),
            shape_of((out_count, feature_rows, model_width), BF16),
        ),
        in_specs=[IN_VMEM] * 3,
        out_specs=(IN_VMEM, ANYWHERE, ANYWHERE),
        scratch_shapes=[
            pltpu.VMEM((chips, model_width, rows), BF16),
            pltpu.VMEM((max(chips - 1, 1), model_width, rows), BF16),
            pltpu.VMEM((max(grid.y_size - 1, 1),) + parts_shape, BF16),
            pltpu.VMEM(parts_shape, BF16),
            dma_sems(copies),
            dma_sems(copies),
            dma_sems(2),
        ],
        compiler_params=params(collective_id=5 + local, has_side_effects=True),
        cost_estimate=hint(30),
        name="last",
    )(grad_first, grad_plane.reshape(plane_shape), out_grad)

    (
        grad_tokens, gain_grad, in_grad, out_sum, mixture_gain_grad, router_grad, table_grad, balance,
    ) = pl.pallas_call(
        partial(
            finish_kernel, lanes=lanes, heads=heads, width=width, head_count=head_count,
            experts=experts, token_total=token_total,
        ),
        out_shape=(
            shape_of((rows, model_width), F32),
            shape_of((1, feature_rows), F32),
            shape_of((feature_rows, 3 * model_width), F32),
            shape_of((feature_rows, model_width), F32),
            shape_of((1, feature_rows), F32),
            shape_of((experts, feature_rows), F32),
            shape_of((bucket_rows, head_count), F32),
            shape_of((1, 1), F32),
        ),
        compiler_params=params(),
        cost_estimate=hint(6),
        name="finish",
    )(first_parts, plane_parts, out_parts, tokens, grad_hidden, attention_in, gain_row, counts)

    layer_output = pl.pallas_call(
        partial(mixture_kernel, local=local),
        out_shape=shape_of((rows, model_width), BF16),
        compiler_params=params(),
        cost_estimate=hint(5),
        name="mixture",
    )(hidden, gates, columns, out_rows)

    up_grad, down_grad = sum_grads(groups, expert_up.shape, expert_down.shape, fsdp_size)
    return (
        layer_output,
        balance.reshape(()),
        grad_tokens,
        gain_grad.reshape(feature_rows),
        mixture_gain_grad.reshape(feature_rows),
        in_grad,
        out_sum,
        router_grad.T,
        table_grad,
        up_grad,
        down_grad,
    )


def solution(mesh):
    in_specs = (
        P(("exp", "fsdp"), None),
        P(("exp", "fsdp"), None),
        P("exp"),
        P(("exp", "fsdp"), None),
        P(("exp", "fsdp"), None),
        P(("exp", "fsdp")),
        P(("exp", "fsdp")),
        P(("exp", "fsdp"), None),
        P(("exp", "fsdp"), None),
        P(("exp", "fsdp"), None),
        P(("exp", "fsdp"), None),
        P("exp", "fsdp", None),
        P("exp", "fsdp", None),
    )
    out_specs = (
        P(("exp", "fsdp"), None),
        P(),
        P(("exp", "fsdp"), None),
        P(("exp", "fsdp")),
        P(("exp", "fsdp")),
        P(("exp", "fsdp"), None),
        P(("exp", "fsdp"), None),
        P(("exp", "fsdp"), None),
        P(("exp", "fsdp"), None),
        P("exp", "fsdp", None),
        P("exp", "fsdp", None),
    )
    return jax.shard_map(
        on_device, mesh=mesh, in_specs=in_specs, out_specs=out_specs, check_vma=False
    )
```

```python
from functools import partial

import jax
import jax.numpy as jnp
from jax import lax
from jax.experimental import pallas as pl
from jax.experimental.pallas import tpu as pltpu
from jax.sharding import PartitionSpec as P

WINDOW = 1024
BUCKETS = 256

EPSILON = 1e-06
AUX_WEIGHT = 0.01
MASKED = -1e30
QUERY_BLOCK = 256
SKEW = 128
VMEM_BYTES = 58 * 1024 * 1024
MESH = pl.DeviceIdType.MESH
F32 = jnp.float32
BF16 = jnp.bfloat16


def params(**kwargs):
    return pltpu.CompilerParams(vmem_limit_bytes=VMEM_BYTES, **kwargs)


def shape_of(shape, dtype):
    return jax.ShapeDtypeStruct(shape, dtype)


def whole(shape):
    return pl.BlockSpec(shape, lambda *_: (0,) * len(shape))


def contract_last(left_side, right_side):
    return lax.dot_general(
        left_side, right_side, (((1,), (1,)), ((), ())), preferred_element_type=F32
    )


def matmul(left_side, right_side):
    return jnp.dot(left_side, right_side, preferred_element_type=F32)


def turned(value):
    return value.astype(F32).T


def bucket_index(distance):
    near_count = BUCKETS // 2
    spread = max(WINDOW - near_count, 1)
    far_bucket = (
        near_count + jnp.maximum(distance - near_count, 0) * (BUCKETS - near_count) // spread
    )
    return jnp.where(distance < near_count, distance, far_bucket)

def hint(micros):
    return pl.CostEstimate(flops=int(micros * 1.0e9), bytes_accessed=1024, transcendentals=0)


class Grid:
    def __init__(self):
        self.exp_size, self.fsdp_size = lax.axis_size("exp"), lax.axis_size("fsdp")
        self.device_count = self.exp_size * self.fsdp_size
        self.y_size = max(
            y for y in range(1, self.exp_size + 1) if self.exp_size % y == 0 and 2 * y * y <= self.exp_size
        ) if self.exp_size > 1 else 1
        self.z_size = self.exp_size // self.y_size
        self.x_size = self.fsdp_size // 2

    def here(self):
        self.exp, self.fsdp = lax.axis_index("exp"), lax.axis_index("fsdp")
        self.z, self.y = self.exp // self.y_size, self.exp % self.y_size
        self.x, self.core = self.fsdp // 2, self.fsdp % 2
        self.linear = self.exp * self.fsdp_size + self.fsdp
        return self

    def at(self, z=None, y=None, fsdp=None):
        z = self.z if z is None else z
        y = self.y if y is None else y
        return (z * self.y_size + y, self.fsdp if fsdp is None else fsdp)

    def x_from(self, hop):
        return ((self.x + self.x_size + hop) % self.x_size) * 2 + self.core

    def sibling(self, fsdp):
        return fsdp + 1 - 2 * (fsdp % 2)


class Links:
    def __init__(self, send, receive):
        self.send, self.receive, self.used = send, receive, 0

    def copy(self, source, target, device, landing):
        index = self.used
        self.used += 1
        going = pltpu.make_async_remote_copy(
            src_ref=source, dst_ref=target, send_sem=self.send.at[index],
            recv_sem=self.receive.at[index], device_id=device, device_id_type=MESH,
        )
        coming = pltpu.make_async_remote_copy(
            src_ref=landing, dst_ref=landing, send_sem=self.send.at[index],
            recv_sem=self.receive.at[index], device_id=device, device_id_type=MESH,
        )
        return going, coming


def greet(devices):
    barrier = pltpu.get_barrier_semaphore()
    for device in devices:
        pl.semaphore_signal(barrier, inc=1, device_id=device, device_id_type=MESH)
    pl.semaphore_wait(barrier, len(devices))


def chip_peers(grid):
    peers = [(grid.exp, grid.sibling(grid.fsdp))]
    return peers + [(grid.exp, grid.x_from(hop)) for hop in range(1, grid.x_size)]


class ChipGather:
    def __init__(self, grid, links, own_sem, source, target):
        self.grid, self.links, self.target = grid, links, target
        self.own = pltpu.make_async_copy(source, target.at[grid.fsdp], own_sem)
        sibling = grid.sibling(grid.fsdp)
        self.along_x, self.across = [], []
        for hop in range(1, grid.x_size):
            self.along_x.append(
                links.copy(
                    source, target.at[grid.fsdp], (grid.exp, grid.x_from(hop)),
                    target.at[grid.x_from(-hop)],
                )
            )
        self.across.append(
            links.copy(source, target.at[grid.fsdp], (grid.exp, sibling), target.at[sibling])
        )

    def start(self):
        for going, _ in self.along_x + self.across:
            going.start()
        self.own.start()

    def forward(self):
        grid = self.grid
        for hop in range(1, grid.x_size):
            self.along_x[hop - 1][1].wait_recv()
            held = grid.x_from(-hop)
            other = grid.sibling(held)
            self.across.append(
                self.links.copy(
                    self.target.at[held], self.target.at[held],
                    (grid.exp, grid.sibling(grid.fsdp)), self.target.at[other],
                )
            )
            self.across[-1][0].start()

    def finish(self):
        for _, coming in self.across:
            coming.wait_recv()
        for going, _ in self.along_x + self.across:
            going.wait_send()
        self.own.wait()


class Exchange:
    def __init__(self, grid, axis, links, own_sems, pairs):
        size = grid.exp_size if axis == "exp" else grid.fsdp_size
        place = grid.exp if axis == "exp" else grid.fsdp
        device = (lambda to: (to, grid.fsdp)) if axis == "exp" else (lambda to: (grid.exp, to))
        self.peers = [device((place + hop) % size) for hop in range(1, size)]
        self.copies, self.own = [], []
        for index, (source, target) in enumerate(pairs):
            for hop in range(1, size):
                to, origin = (place + hop) % size, (place + size - hop) % size
                self.copies.append(
                    links.copy(source(to), target.at[place], device(to), target.at[origin])
                )
            self.own.append(
                pltpu.make_async_copy(source(place), target.at[place], own_sems.at[index])
            )

    def start(self):
        for going, _ in self.copies:
            going.start()
        for own in self.own:
            own.start()

    def finish(self):
        for going, coming in self.copies:
            coming.wait_recv()
            going.wait_send()
        for own in self.own:
            own.wait()


ANYWHERE = pl.BlockSpec(memory_space=pl.ANY)
IN_VMEM = pl.BlockSpec(memory_space=pltpu.VMEM)


def dma_sems(count):
    return pltpu.SemaphoreType.DMA((count,))


def exchange(axis, arrays, collective_id, micros):
    grid = Grid()
    size = grid.exp_size if axis == "exp" else grid.fsdp_size
    count = len(arrays)
    parts = [part for _, part in arrays]

    def kernel(*refs):
        sources, targets = refs[:count], refs[count : 2 * count]
        send, receive, own = refs[2 * count :]
        place = grid.here()
        pairs = [
            (partial(plane_of, source, part), target)
            for source, part, target in zip(sources, parts, targets)
        ]
        work = Exchange(place, axis, Links(send, receive), own, pairs)
        greet(work.peers)
        work.start()
        work.finish()

    return pl.pallas_call(
        kernel,
        out_shape=tuple(
            shape_of((size,) + array.shape[(1 if part is None else 2) :], array.dtype)
            for array, part in arrays
        ),
        in_specs=[ANYWHERE] * count,
        out_specs=tuple([ANYWHERE] * count),
        scratch_shapes=[dma_sems(count * size), dma_sems(count * size), dma_sems(count)],
        compiler_params=pltpu.CompilerParams(collective_id=collective_id, has_side_effects=True),
        cost_estimate=hint(micros),
        name=f"exchange_{collective_id}",
    )(*[array for array, _ in arrays])


def plane_of(source, part, to):
    return source.at[to] if part is None else source.at[to, part]


def gather_rows(array, collective_id, micros):
    grid = Grid()

    def kernel(source, target, send, receive, own):
        place = grid.here()
        work = ChipGather(place, Links(send, receive), own.at[0], source, target)
        greet(chip_peers(place))
        work.start()
        work.forward()
        work.finish()

    return pl.pallas_call(
        kernel,
        out_shape=shape_of((grid.fsdp_size,) + array.shape, array.dtype),
        in_specs=[ANYWHERE],
        out_specs=ANYWHERE,
        scratch_shapes=[dma_sems(2 * grid.fsdp_size), dma_sems(2 * grid.fsdp_size), dma_sems(1)],
        compiler_params=pltpu.CompilerParams(collective_id=collective_id, has_side_effects=True),
        cost_estimate=hint(micros),
        name=f"gather_{collective_id}",
    )(array)


class Lanes:
    def __init__(self, heads, width, padded_heads, experts):
        self.weights = 3 * heads * width
        self.base = self.weights // 128 * 128
        self.router = self.weights - self.base
        self.gain = self.router + experts
        self.table = self.gain + 1
        self.count = self.table + padded_heads
        self.width = -(-(self.weights + 2 * experts + 1 + padded_heads) // 128) * 128
        self.extra = self.width - self.base
        self.shift = self.count - self.router


def bucket_rows_select(features, feature_rows, bucket_rows, span):
    row = lax.broadcasted_iota(jnp.int32, (features, 1), 0)
    within = lax.rem(row, feature_rows)
    bucket = jnp.where(
        within < bucket_rows, lax.div(row, feature_rows) * bucket_rows + within, -1
    )
    distance = lax.broadcasted_iota(jnp.int32, (1, span), 1) - SKEW
    near = BUCKETS // 2
    spread = max(WINDOW - near, 1)
    far = near + lax.div(jnp.maximum(distance - near, 0) * (BUCKETS - near), spread)
    wanted = jnp.where(distance < near, distance, far)
    reachable = (distance >= 0) & (distance < WINDOW)
    wanted = jnp.where(reachable, wanted, -2)
    return jnp.where(bucket == wanted, 1.0, 0.0).astype(BF16), reachable


def as_column(row, size):
    row_place = lax.broadcasted_iota(jnp.int32, (size, size), 0)
    lane = lax.broadcasted_iota(jnp.int32, (size, size), 1)
    spread = jnp.broadcast_to(row.astype(F32), (size, size))
    return jnp.sum(jnp.where(row_place == lane, spread, 0.0), axis=1, keepdims=True)


def padded_rows(value, rows):
    if value.shape[0] == rows:
        return value
    return jnp.concatenate([value, jnp.zeros((rows - value.shape[0], value.shape[1]), F32)], axis=0)


def padded_lanes(value, lanes):
    if value.shape[1] == lanes:
        return value
    return jnp.concatenate([value, jnp.zeros((value.shape[0], lanes - value.shape[1]), F32)], axis=1)


class Wide:
    def __init__(self, grid, links, own_sem, source, target):
        self.grid, self.links, self.target = grid, links, target
        self.own = pltpu.make_async_copy(
            source, target.at[grid.z, grid.y, grid.x, grid.core], own_sem
        )
        self.stages = []
        stage = []
        for hop in range(1, grid.z_size):
            stage.append(
                links.copy(
                    source, target.at[grid.z, grid.y, grid.x, grid.core],
                    grid.at(z=(grid.z + hop) % grid.z_size),
                    target.at[(grid.z + grid.z_size - hop) % grid.z_size, grid.y, grid.x, grid.core],
                )
            )
        self.stages.append(stage)

    def start(self):
        self.own.start()
        for going, _ in self.stages[0]:
            going.start()

    def turn(self, axis):
        grid, target = self.grid, self.target
        for _, coming in self.stages[-1]:
            coming.wait_recv()
        stage = []
        if axis == "y":
            self.own.wait()
            held = target.at[:, grid.y, grid.x, grid.core]
            for hop in range(1, grid.y_size):
                origin = (grid.y + grid.y_size - hop) % grid.y_size
                stage.append(
                    self.links.copy(
                        held, held, grid.at(y=(grid.y + hop) % grid.y_size),
                        target.at[:, origin, grid.x, grid.core],
                    )
                )
        elif axis == "x":
            held = target.at[:, :, grid.x, grid.core]
            for hop in range(1, grid.x_size):
                origin = (grid.x + grid.x_size - hop) % grid.x_size
                stage.append(
                    self.links.copy(
                        held, held, (grid.exp, grid.x_from(hop)), target.at[:, :, origin, grid.core]
                    )
                )
        else:
            held = target.at[:, :, :, grid.core]
            stage.append(
                self.links.copy(
                    held, held, (grid.exp, grid.sibling(grid.fsdp)), target.at[:, :, :, 1 - grid.core]
                )
            )
        for going, _ in stage:
            going.start()
        self.stages.append(stage)

    def finish(self):
        for _, coming in self.stages[-1]:
            coming.wait_recv()
        for stage in self.stages:
            for going, _ in stage:
                going.wait_send()


def start_kernel(
    tokens, cotangent, routes_t, slots_t, attention_gain, mixture_gain, attention_in, router_t, table,
    attention_out, expert_up, expert_down, *refs, lanes, heads, width, head_count, experts, capacity,
    local,
):
    all_tokens, all_planes, cotangent_slots, position_rows, columns, full_out = refs[:6]
    shards = refs[6 : 6 + 2 * local]
    planes, up_stage, down_stage, send, receive, own, fetch, split = refs[6 + 2 * local :]
    grid = Grid().here()
    links = Links(send, receive)
    z_size, y_size, fsdp_size = grid.z_size, grid.y_size, grid.fsdp_size
    near = [
        grid.at(z=(grid.z + hop) % z_size, fsdp=(grid.fsdp + turn) % fsdp_size)
        for hop in range(z_size)
        for turn in range(fsdp_size)
        if hop or turn
    ]
    beside = [grid.at(y=(grid.y + hop) % y_size) for hop in range(1, y_size)]
    gathered = ChipGather(grid, links, own.at[0], tokens, all_tokens)
    widely = Wide(grid, links, own.at[2], attention_out, full_out)
    part = expert_down.shape[1]
    depth = expert_up.shape[1]
    fetches = []
    for index in range(local):
        fetches.append(
            pltpu.make_async_copy(expert_up.at[index], up_stage.at[index], fetch.at[2 * index])
        )
        fetches.append(
            pltpu.make_async_copy(
                expert_down.at[index], down_stage.at[index], fetch.at[2 * index + 1]
            )
        )
    greet(near + beside)
    gathered.start()
    widely.start()
    for copy in fetches:
        copy.start()

    feature_rows = attention_in.shape[0]
    model_width = head_count * width
    gained = attention_in[...].astype(F32) * as_column(attention_gain[...], feature_rows)
    route_rows, slot_rows = routes_t[...].astype(F32), slots_t[...].astype(F32)
    columns[...] = padded_rows(jnp.concatenate([route_rows, slot_rows], axis=0), 128).T
    row_count = columns.shape[0]
    expert_lanes = lax.broadcasted_iota(jnp.int32, (row_count, experts), 1).astype(F32)
    named = jnp.zeros((row_count, experts), F32)
    for k in range(2):
        named = named + jnp.where(expert_lanes == columns[:, k : k + 1], 1.0, 0.0)
    named = jnp.sum(named, axis=0, keepdims=True)
    place = lax.broadcasted_iota(jnp.int32, (feature_rows, feature_rows), 0)
    same = place == lax.broadcasted_iota(jnp.int32, (feature_rows, feature_rows), 1)
    router = contract_last(jnp.where(same, 1.0, 0.0).astype(BF16), router_t[...])
    pieces = [
        router,
        as_column(mixture_gain[...], feature_rows),
        padded_rows(padded_lanes(table[...].astype(F32), heads * fsdp_size), feature_rows),
        padded_rows(named, feature_rows),
    ]
    taken = sum(piece.shape[1] for piece in pieces)
    if lanes.width > lanes.weights + taken:
        pieces.append(jnp.zeros((feature_rows, lanes.width - lanes.weights - taken), F32))
    for place in range(fsdp_size):
        first, last = place * heads * width, min((place + 1) * heads * width, model_width)
        own_pieces = []
        for kind in range(3):
            if last > first:
                own_pieces.append(gained[:, kind * model_width + first : kind * model_width + last])
            if last - first < heads * width:
                own_pieces.append(
                    jnp.zeros((feature_rows, heads * width - max(last - first, 0)), F32)
                )
        planes[place] = jnp.concatenate(own_pieces + pieces, axis=1).astype(BF16)
    arrivals = [[] for _ in range(z_size)]
    sent = []
    for hop in range(z_size):
        for turn in range(fsdp_size):
            if hop == 0 and turn == 0:
                continue
            to = (grid.fsdp + turn) % fsdp_size
            origin = (grid.fsdp + fsdp_size - turn) % fsdp_size
            going, coming = links.copy(
                planes.at[to],
                all_planes.at[grid.z, grid.y, grid.fsdp],
                grid.at(z=(grid.z + hop) % z_size, fsdp=to),
                all_planes.at[(grid.z + z_size - hop) % z_size, grid.y, origin],
            )
            going.start()
            sent.append(going)
            arrivals[hop].append(coming)
    kept = pltpu.make_async_copy(
        planes.at[grid.fsdp], all_planes.at[grid.z, grid.y, grid.fsdp], own.at[1]
    )
    kept.start()
    widely.turn("y")

    for copy in fetches:
        copy.wait()
    splits = []
    for index in range(local):
        up, down = shards[2 * index : 2 * index + 2]
        stores = [
            (
                up_stage.at[index, :, pl.ds(block * part, part)],
                up.at[pl.ds(block * depth, depth), :],
            )
            for block in range(fsdp_size)
        ]
        for source, target in stores + [(down_stage.at[index], down)]:
            splits.append(pltpu.make_async_copy(source, target, split.at[len(splits)]))
            splits[-1].start()

    place = route_rows * capacity + slot_rows
    position_rows[...] = padded_rows(place, 8)
    select_rows(cotangent_slots, place, cotangent[...])

    forwarded = []
    for hop in range(z_size):
        held = (grid.z + z_size - hop) % z_size
        for coming in arrivals[hop]:
            coming.wait_recv()
        if hop == 0:
            kept.wait()
        for turn in range(1, y_size):
            going, coming = links.copy(
                all_planes.at[held, grid.y],
                all_planes.at[held, grid.y],
                grid.at(y=(grid.y + turn) % y_size),
                all_planes.at[held, (grid.y + y_size - turn) % y_size],
            )
            going.start()
            forwarded.append((going, coming))
        if hop == 0:
            widely.turn("x")
    gathered.forward()
    widely.turn("core")
    for going, coming in forwarded:
        coming.wait_recv()
        going.wait_send()
    for going in sent:
        going.wait_send()
    gathered.finish()
    widely.finish()
    for copy in splits:
        copy.wait()


def project_kernel(
    tokens, plane, segments, normed, query_t, key_n, query_n, value_n, key_t, value_t, bias, counts,
    weight_t, table_t, *, heads, width, lanes, feature_rows, bucket_rows,
):
    @pl.when(pl.program_id(0) == 0)
    def _():
        weight_t[...] = turned(plane[:, : lanes.weights]).astype(BF16)
        extra = plane[:, lanes.base :]
        span = bias.shape[2]
        select, reachable = bucket_rows_select(plane.shape[0], feature_rows, bucket_rows, span)
        table_t[...] = lax.dot_general(
            extra, select, (((0,), (0,)), ((), ())), preferred_element_type=F32
        )
        first = lanes.table + lax.axis_index("fsdp") * heads
        for head in range(heads):
            bias[head] = jnp.where(reachable, table_t[pl.ds(first + head, 1), :], MASKED)
        summed = jnp.sum(extra.astype(F32), axis=0, keepdims=True)
        counts[...] = pltpu.roll(
            jnp.broadcast_to(summed, counts.shape), lanes.extra - lanes.shift, 1
        )

    inputs = tokens[0].astype(F32)
    scale = lax.rsqrt(jnp.mean(inputs * inputs, axis=1, keepdims=True) + EPSILON)
    low = (inputs * scale).astype(BF16)
    normed[...] = low
    rows = low.shape[0]
    projected = contract_last(weight_t[...], low).astype(BF16).astype(F32)
    document = segments[...] % 4
    places = lax.broadcasted_iota(jnp.int32, (8, rows), 0)
    same = places == document
    hot = jnp.where(same, 1.0, 0.0)
    barred = jnp.where(same | (places >= 4), 0.0, MASKED)
    filler = jnp.zeros((SKEW - 8 - width, rows), F32)
    for head in range(heads):
        query = projected[head * width : (head + 1) * width] * width ** (-0.5)
        key = projected[(heads + head) * width : (heads + head + 1) * width]
        value = projected[(2 * heads + head) * width : (2 * heads + head + 1) * width]
        query_t[head] = jnp.concatenate([query, barred, filler], axis=0).astype(BF16)
        key_n[head] = jnp.concatenate([key, hot, filler], axis=0).T.astype(BF16)
        query_n[head] = query.T.astype(BF16)
        value_n[head] = value.T.astype(BF16)
        key_t[head] = key.astype(BF16)
        value_t[head] = value.astype(BF16)


def spans(length):
    for query_start in range(0, length, QUERY_BLOCK):
        key_start = max(0, query_start - WINDOW)
        yield query_start, key_start, query_start + QUERY_BLOCK - key_start


def spread_bias(bias, skew):
    skew[...] = pltpu.roll(
        jnp.broadcast_to(bias[0], skew.shape), 0, 1, stride=1, stride_axis=0
    )


def attend_kernel(query_t, key_n, value_t, bias, context, context_high, log_total, skew, scores, *, rows):
    spread_bias(bias, skew)
    for query_start, key_start, key_count in spans(query_t.shape[2]):
        queries = slice(query_start, query_start + QUERY_BLOCK)
        keys = slice(key_start, key_start + key_count)
        raw = matmul(key_n[0, keys, :], query_t[0, :, queries])
        for start in range(0, key_count, SKEW):
            offset = query_start - key_start - start + SKEW
            scores[start : start + SKEW, :] = (
                raw[start : start + SKEW] + skew[:, offset : offset + QUERY_BLOCK]
            )
        high = jnp.max(scores[:key_count, :], axis=0, keepdims=True)
        weights = jnp.exp(scores[:key_count, :] - high)
        total = jnp.sum(weights, axis=0, keepdims=True)
        gathered = matmul(value_t[0, :, keys], weights.astype(BF16)) / total
        context_high[0, :, queries] = gathered
        log_total[0, :, queries] = high + jnp.log(total)
        for start in range(0, QUERY_BLOCK, 128):
            place = query_start + start
            context[place // rows, :, place % rows : place % rows + 128] = gathered[
                :, start : start + 128
            ].astype(BF16)


def attend_back_kernel(
    query_t, key_n, query_n, value_n, key_t, grad_t, grad_n, context_high, log_total, bias,
    grad_projected, grad_bias, skew, grad_skew, grad_key, grad_value, *, scale,
):
    spread_bias(bias, skew)
    grad_skew[...] = jnp.zeros_like(grad_skew)
    grad_key[...] = jnp.zeros_like(grad_key)
    grad_value[...] = jnp.zeros_like(grad_value)
    inner = jnp.sum(grad_t[0].astype(F32) * context_high[0], axis=0, keepdims=True)
    for query_start, key_start, key_count in spans(query_t.shape[2]):
        queries = slice(query_start, query_start + QUERY_BLOCK)
        keys = slice(key_start, key_start + key_count)
        raw = matmul(key_n[0, keys, :], query_t[0, :, queries])
        grad_weights = matmul(value_n[0, keys, :], grad_t[0, :, queries])
        weights_low, grad_low = [], []
        for start in range(0, key_count, SKEW):
            offset = query_start - key_start - start + SKEW
            part = slice(start, start + SKEW)
            weights = jnp.exp(
                raw[part] + skew[:, offset : offset + QUERY_BLOCK] - log_total[0, :, queries]
            )
            grad_scores = weights * (grad_weights[part] - inner[:, queries])
            grad_skew[:, offset : offset + QUERY_BLOCK] += grad_scores
            weights_low.append(weights.astype(BF16))
            grad_low.append(grad_scores.astype(BF16))
        weights_low = jnp.concatenate(weights_low, axis=0)
        grad_low = jnp.concatenate(grad_low, axis=0)
        grad_projected[0, 0, :, queries] = (matmul(key_t[0, :, keys], grad_low) * scale).astype(BF16)
        grad_key[keys, :] += matmul(grad_low, query_n[0, queries, :])
        grad_value[keys, :] += matmul(weights_low, grad_n[0, queries, :])
    grad_projected[1, 0] = grad_key[...].T.astype(BF16)
    grad_projected[2, 0] = grad_value[...].T.astype(BF16)
    count = SKEW
    span = skew.shape[1]
    while count > 8:
        count //= 2
        grad_skew[:count, :] += pltpu.roll(grad_skew[count : 2 * count, :], span - count, 1)
    summed = grad_skew[0:1, :]
    for row in range(1, 8):
        summed = summed + pltpu.roll(grad_skew[row : row + 1, :], span - row, 1)
    grad_bias[0] = summed

def expert_lane(shape, lanes):
    return lax.broadcasted_iota(jnp.int32, shape, 1) - lanes.router


def int_columns(columns):
    values = columns[:, 0:4].astype(jnp.int32)
    return values[:, 0:2], values[:, 2:4]


def route_kernel(
    tokens, attended_t, attention_out, plane, columns, position_rows,
    hidden, routed, probabilities, gates, outgoing, slot_gates, *, experts, lanes, capacity,
):
    rows, model_width = tokens.shape
    routes, slots = int_columns(columns)
    attended_low = turned(attended_t[:model_width]).astype(BF16)
    hidden_state = tokens[...].astype(F32) + matmul(attended_low, attention_out[...])
    hidden[...] = hidden_state
    scale = lax.rsqrt(jnp.mean(hidden_state * hidden_state, axis=1, keepdims=True) + EPSILON)
    extra = plane[:, lanes.base :]
    gain = extra.astype(F32).T[lanes.gain : lanes.gain + 1]
    low = (hidden_state * scale * gain).astype(BF16)
    routed[...] = low
    logits = matmul(low, extra)
    lane = expert_lane(logits.shape, lanes)
    logits = jnp.where((lane >= 0) & (lane < experts), logits, MASKED)
    powers = jnp.exp(logits - jnp.max(logits, axis=1, keepdims=True))
    powers = powers / jnp.sum(powers, axis=1, keepdims=True)
    probabilities[...] = powers
    chosen = [
        jnp.sum(jnp.where(lane == routes[:, k : k + 1], powers, 0.0), axis=1, keepdims=True)
        for k in range(2)
    ]
    total = chosen[0] + chosen[1]
    gate_values = [chosen[k] / total for k in range(2)]
    pair = lax.broadcasted_iota(jnp.int32, (rows, 2), 1)
    gates[...] = jnp.where(pair == 0, gate_values[0], gate_values[1])
    members, _, gate_lanes = slot_gates.shape
    member_slots = experts // members * capacity
    slot_lanes = lax.broadcasted_iota(jnp.int32, (rows, gate_lanes), 1)
    inside = slot_lanes < member_slots
    places = routes * capacity + slots
    for member in range(members):
        by_slot = jnp.zeros((rows, gate_lanes), F32)
        for k in range(2):
            hit = (slot_lanes + member * member_slots == places[:, k : k + 1]) & inside
            by_slot = by_slot + jnp.where(hit, gate_values[k], 0.0)
        slot_gates[member] = jnp.broadcast_to(
            jnp.sum(by_slot, axis=0, keepdims=True), slot_gates.shape[1:]
        )
    select_rows(outgoing, position_rows[...], low)


def select_rows(outgoing, position_rows, values):
    slot_count, rows = outgoing.shape[0], values.shape[0]
    for start in range(0, slot_count, rows):
        slots = (lax.broadcasted_iota(jnp.int32, (rows, rows), 0) + start).astype(F32)
        picked = (slots == position_rows[0:1, :]) | (slots == position_rows[1:2, :])
        outgoing[start : start + rows, :] = matmul(
            jnp.where(picked, 1.0, 0.0).astype(BF16), values
        ).astype(BF16)


def gelu_parts(value):
    magnitude = jnp.abs(value)
    power = jnp.exp(value * value * -0.5)
    step = 1.0 / (1.0 + (0.3275911 * 0.7071067811865476) * magnitude)
    series = step * (
        0.127414796
        + step * (-0.142248368 + step * (0.7107068705 + step * (-0.7265760135 + step * 0.5307027145)))
    )
    tail = series * power
    normal = jnp.where(value < 0.0, tail, 1.0 - tail)
    return value * normal, normal + value * power * 0.3989422804014327


def flipped(place, other, size):
    result, bit = 0, 1
    while bit < size:
        result = result + bit * ((place // bit + other // bit) % 2)
        bit *= 2
    return result


def expert_kernel(*refs, layout, index, local, half, capacity, parts):
    shards = 2 * half
    refs = dict(zip(layout, _grouped(refs, layout)))
    grid = Grid().here()
    z_size, y_size = grid.z_size, grid.y_size
    first, last = index == 0, index == local - 1
    sibling = (grid.exp, grid.sibling(grid.fsdp))
    links = Links(refs["send"][0], refs["receive"][0])
    rows_all, cot, up_all, down_all = (refs[k][0] for k in ("rows_all", "cot", "up_all", "down_all"))
    active, grad_hidden, unscaled = (refs[k][0] for k in ("active", "grad_hidden", "unscaled"))
    gates, gate_column = refs["gates"][0], refs["gate_column"][0]
    rows_t, slot_t, total = (refs[k][0] for k in ("rows_t", "slot_t", "total"))
    grad_up, grad_down = refs["grad_up"][0], refs["grad_down"][0]
    grad_rows, grad_gates = refs["grad_rows"][0], refs["grad_gates"][0]
    keep_up, keep_down = refs["keep_up"], refs["keep_down"]
    taken_up, taken_down = refs["taken_up"], refs["taken_down"]
    load_sem, fetch_sem, store_sem = refs["load_sem"][0], refs["fetch_sem"][0], refs["store_sem"][0]
    store_there, stored_here = refs["store_there"][0], refs["stored_here"][0]
    blocks, _, model_width = rows_all.shape
    part = up_all.shape[2]
    count = blocks * capacity
    depth = model_width // shards
    group_rows = y_size * capacity

    power = z_size & (z_size - 1) == 0

    def source_z(turn):
        return flipped(grid.z, turn, z_size) if power else (grid.z + turn) % z_size

    def target_z(turn):
        return flipped(grid.z, turn, z_size) if power else (grid.z + z_size - turn) % z_size

    def owner(place, core):
        return ((grid.x + place % half) % half) * 2 + (core + place // half) % 2

    def rows_of(place, core=None):
        core = grid.core if core is None else core
        return pl.ds(pl.multiple_of(owner(place, core) * depth, 16), depth)

    loads = [pltpu.make_async_copy(refs["cot_in"][0].at[:, index], cot, load_sem.at[0])]
    if not first:
        loads.append(pltpu.make_async_copy(refs["rows_in"][0], rows_all, load_sem.at[1]))
    my_up, my_down = refs["my_up"], refs["my_down"]
    swapped_up, swapped_down = refs["swapped_up"], refs["swapped_down"]
    local_up = list(enumerate(my_up)) + [(half, array) for array in swapped_up]
    local_down = list(enumerate(my_down)) + [(half, array) for array in swapped_down]
    fetched_up = [
        pltpu.make_async_copy(
            array.at[rows_of(place), :], up_all.at[place, rows_of(shard), :],
            fetch_sem.at[place, number],
        )
        for number, (shard, array) in enumerate(local_up)
        for place in range(shards)
    ]
    fetched_down = {
        shard: pltpu.make_async_copy(
            array, down_all.at[shard], fetch_sem.at[shards + number, 0]
        )
        for number, (shard, array) in enumerate(local_down)
    }
    crossing = [shard for shard in range(half) if half + shard not in dict(local_up)]
    cross_down = {
        half + shard: links.copy(
            my_down[shard], down_all.at[half + shard], sibling, down_all.at[half + shard]
        )
        for shard in crossing
    }
    cross_up = [
        links.copy(
            my_up[shard].at[rows_of(place, 1 - grid.core), :],
            up_all.at[place, rows_of(shard), :], sibling,
            up_all.at[place, rows_of(half + shard), :],
        )
        for shard in crossing
        for place in range(shards)
    ]
    cross_next = [
        links.copy(source, target, sibling, target)
        for source, target in zip(refs["next_mine"], refs["next_swapped"])
    ]
    work = Exchange(
        grid, "exp", links, refs["own_sem"][0],
        [
            (partial(plane_of, source, place), target)
            for source, place, target in zip(refs["moved_from"], parts, refs["moved_to"])
        ],
    )
    gate_work = None
    if first:
        gate_work = Exchange(
            grid, "exp", links, refs["gate_sem"][0],
            [(partial(plane_of, refs["gates_from"][0], None), gates)],
        )

    def member(z, y):
        return z * y_size + y

    def dispatch(turn, hop):
        to = member(target_z(turn), (grid.y + y_size - hop) % y_size)
        origin = member(source_z(turn), (grid.y + hop) % y_size)
        outgoing = refs["outgoing"][0]
        going = pltpu.make_async_remote_copy(
            src_ref=outgoing.at[to, index], dst_ref=rows_all.at[grid.exp],
            send_sem=refs["row_send"][0].at[turn, hop], recv_sem=refs["row_receive"][0].at[turn, hop],
            device_id=(to, grid.fsdp), device_id_type=MESH,
        )
        coming = pltpu.make_async_remote_copy(
            src_ref=rows_all.at[origin], dst_ref=rows_all.at[origin],
            send_sem=refs["row_send"][0].at[turn, hop], recv_sem=refs["row_receive"][0].at[turn, hop],
            device_id=(to, grid.fsdp), device_id_type=MESH,
        )
        return going, coming

    def give_back(turn, hop):
        to = member(source_z(turn), (grid.y + hop) % y_size)
        origin = member(target_z(turn), (grid.y + y_size - hop) % y_size)
        pairs = []
        for number, (held, target) in enumerate(
            ((grad_rows, refs["back_rows"][0]), (grad_gates, refs["back_gates"][0]))
        ):
            sems = dict(
                send_sem=refs["back_send"][0].at[number, turn, hop],
                recv_sem=refs["back_receive"][0].at[number, turn, hop],
                device_id=(to, grid.fsdp), device_id_type=MESH,
            )
            pairs.append(
                (
                    pltpu.make_async_remote_copy(
                        src_ref=held.at[to], dst_ref=target.at[grid.exp], **sems
                    ),
                    pltpu.make_async_remote_copy(
                        src_ref=target.at[origin], dst_ref=target.at[origin], **sems
                    ),
                )
            )
        return pairs

    steps = [(turn, hop) for turn in range(z_size) for hop in range(y_size)]
    own_row = own_back = None
    if first:
        own_row = pltpu.make_async_copy(
            refs["outgoing"][0].at[grid.exp, index], rows_all.at[grid.exp], load_sem.at[1]
        )
    if last:
        own_back = [
            pltpu.make_async_copy(held.at[grid.exp], target.at[grid.exp], load_sem.at[2 + number])
            for number, (held, target) in enumerate(
                ((grad_rows, refs["back_rows"][0]), (grad_gates, refs["back_gates"][0]))
            )
        ]

    for copy in loads:
        copy.start()
    for copy in list(fetched_down.values()) + fetched_up:
        copy.start()
    greet([((grid.exp + hop) % grid.exp_size, grid.fsdp) for hop in range(1, grid.exp_size)] + [sibling])
    if first:
        gate_work.start()
        own_row.start()
        for turn, hop in steps[1:]:
            dispatch(turn, hop)[0].start()
    for going, _ in list(cross_down.values()) + cross_up + cross_next:
        going.start()
    work.start()

    loads[0].wait()
    for place in range(shards):
        if place in fetched_down:
            fetched_down[place].wait()
        else:
            cross_down[place][1].wait_recv()
        unscaled[place] = contract_last(cot[...].reshape(count, model_width), down_all[place])
    if first:
        gate_work.finish()
        gates_out = pltpu.make_async_copy(gates, refs["gates_to"][0], load_sem.at[4])
        gates_out.start()
    columns = gates[:, 0, :].T
    for block in range(blocks):
        piece = slice(block * capacity, (block + 1) * capacity)
        gate = columns[index * capacity : (index + 1) * capacity, block : block + 1]
        gate_column[piece, :] = gate
    slot_t[...] = (gate_column[...] * cot[...].reshape(count, model_width).astype(F32)).T.astype(BF16)
    for copy in fetched_up:
        copy.wait()
    for _, coming in cross_up:
        coming.wait_recv()
    if first:
        own_row.wait()
    else:
        loads[1].wait()

    def group(turn, carry):
        z = source_z(turn)
        if first:
            for hop in range(y_size):
                if hop == 0:

                    @pl.when(turn > 0)
                    def _():
                        dispatch(turn, 0)[1].wait_recv()

                else:
                    dispatch(turn, hop)[1].wait_recv()
        members = pl.ds(z * y_size, y_size)
        span = pl.ds(pl.multiple_of(z * group_rows, 16), group_rows)
        rows = rows_all[members].reshape(group_rows, model_width)
        gate = gate_column[span, :]
        grad = jnp.zeros((group_rows, model_width), F32)
        products = jnp.zeros((group_rows, part), F32)
        ahead = matmul(rows, up_all[0])
        for place in range(shards):
            hidden = ahead
            if place + 1 < shards:
                ahead = matmul(rows, up_all[place + 1])
            base = unscaled[place, span, :]
            activated, slope = gelu_parts(hidden)
            products = products + activated * base
            active[place, span, :] = activated.astype(BF16)
            low = (gate * base * slope).astype(BF16)
            grad_hidden[place, span, :] = low
            grad = grad + contract_last(low, up_all[place])
        grad_rows[members] = grad.astype(BF16).reshape(y_size, capacity, model_width)
        ones = jnp.ones((8, part), F32)
        for hop in range(y_size):
            grad_gates[z * y_size + hop] = lax.dot_general(
                ones, products[hop * capacity : (hop + 1) * capacity], (((1,), (1,)), ((), ())),
                precision=lax.Precision.HIGHEST, preferred_element_type=F32,
            )
        if last:
            for hop in range(y_size):
                if hop == 0:

                    @pl.when(turn > 0)
                    def _():
                        for going, _ in give_back(turn, 0):
                            going.start()

                else:
                    for going, _ in give_back(turn, hop):
                        going.start()
        return carry

    lax.fori_loop(0, z_size, group, 0)
    if last:
        for copy in own_back:
            copy.start()

    rows_t[...] = turned(rows_all[...].reshape(count, model_width)).astype(BF16)
    total[...] = jnp.zeros_like(total)

    def up_target(targets, hop, place):
        if hop == 0:
            return targets[0].at[rows_of(place), :]
        return targets[1].at[hop - 1, rows_of(place), :]

    def keep_stores(place, slot):
        return [
            pltpu.make_async_copy(
                grad_up.at[slot, rows_of(hop), :], up_target(keep_up, hop, place),
                store_sem.at[slot, hop],
            )
            for hop in range(half)
        ]

    def give_stores(place, slot):
        return [
            pltpu.make_async_remote_copy(
                src_ref=grad_up.at[slot, rows_of(half + hop), :],
                dst_ref=up_target(taken_up, hop, place),
                send_sem=store_there.at[slot, hop], recv_sem=stored_here.at[place, hop],
                device_id=sibling, device_id_type=MESH,
            )
            for hop in range(half)
        ]

    def down_store(hop, slot):
        target = keep_down[0] if hop == 0 else keep_down[1].at[hop - 1]
        return pltpu.make_async_copy(grad_down.at[slot], target, store_sem.at[slot, half])

    def down_give(hop, slot):
        target = taken_down[0] if hop == 0 else taken_down[1].at[hop - 1]
        return pltpu.make_async_remote_copy(
            src_ref=grad_down.at[slot], dst_ref=target,
            send_sem=store_there.at[slot, half], recv_sem=stored_here.at[hop, half],
            device_id=sibling, device_id_type=MESH,
        )

    def each_down(place, slot, act):
        for hop in range(half):

            @pl.when(place == hop)
            def _(hop=hop):
                act(down_store(hop, slot), False)

            @pl.when(place == half + hop)
            def _(hop=hop):
                act(down_give(hop, slot), True)

    def start_store(place, slot):
        for copy in keep_stores(place, slot) + give_stores(place, slot):
            copy.start()
        each_down(place, slot, lambda copy, _: copy.start())

    def wait_store(place, slot):
        for copy in keep_stores(place, slot):
            copy.wait()
        for copy in give_stores(place, slot):
            copy.wait_send()
        each_down(place, slot, lambda copy, remote: copy.wait_send() if remote else copy.wait())

    def column(place, carry):
        slot = place % 2
        total[...] += matmul(active[place], down_all[place])

        @pl.when(place >= 2)
        def _():
            wait_store(place - 2, slot)

        grad_up[slot] = matmul(rows_t[...], grad_hidden[place]).astype(BF16)
        grad_down[slot] = matmul(slot_t[...], active[place]).T.astype(BF16)
        start_store(place, slot)
        return carry

    lax.fori_loop(0, shards, column, 0)

    rows_out = refs["rows_out"][0]
    for before in refs["outs_before"]:
        rows_out[:, :index] = before[...]
    rows_out[:, index] = total[...].astype(BF16).reshape(blocks, capacity, model_width)
    for place in range(max(shards - 2, 0), shards):
        wait_store(place, place % 2)
    for place in range(shards):
        for copy in give_stores(place, 0):
            copy.wait_recv()
    for hop in range(half):
        down_give(hop, 0).wait_recv()
    if half > 1:
        refs["pass_up"][0][...] = (
            keep_up[1][...].astype(F32) + taken_up[1][...].astype(F32)
        ).astype(BF16)
        refs["pass_down"][0][...] = (
            keep_down[1][...].astype(F32) + taken_down[1][...].astype(F32)
        ).astype(BF16)
    for going, coming in cross_next:
        coming.wait_recv()
        going.wait_send()
    for going, _ in list(cross_down.values()) + cross_up:
        going.wait_send()
    if first:
        gates_out.wait()
        for turn, hop in steps[1:]:
            dispatch(turn, hop)[0].wait_send()
    work.finish()
    if last:
        for turn, hop in steps[1:]:
            for going, coming in give_back(turn, hop):
                coming.wait_recv()
                going.wait_send()
        for copy in own_back:
            copy.wait()


def _grouped(refs, layout):
    groups, start = [], 0
    for size in layout.values():
        groups.append(refs[start : start + size])
        start += size
    return groups


def run_expert(index, local, outgoing, slot_gates, rows_in, gates, cotangent, ups, downs, swapped,
               next_mine, moved, outs_before, collective_id):
    grid = Grid()
    half = len(ups)
    shards = 2 * half
    first, last = index == 0, index == local - 1
    blocks, _, capacity, model_width = cotangent.shape
    part = downs[0].shape[0]
    count = blocks * capacity
    gate_lanes = slot_gates.shape[2]
    inputs, outputs, scratch = {}, {}, {}
    inputs["cot_in"] = [(cotangent, ANYWHERE)]
    inputs["outgoing"] = [(outgoing, ANYWHERE)] if first else []
    inputs["gates_from"] = [(slot_gates, ANYWHERE)] if first else []
    inputs["rows_in"] = [] if first else [(rows_in, ANYWHERE)]
    if not first:
        inputs["gates"] = [(gates, IN_VMEM)]
    inputs["my_up"] = [(array, ANYWHERE) for array in ups]
    inputs["my_down"] = [(array, ANYWHERE) for array in downs]
    inputs["swapped_up"] = [(array, ANYWHERE) for array in swapped[:1]]
    inputs["swapped_down"] = [(array, ANYWHERE) for array in swapped[1:]]
    inputs["next_mine"] = [(array, ANYWHERE) for array in next_mine]
    inputs["moved_from"] = [(array, ANYWHERE) for array, _ in moved]
    inputs["outs_before"] = [] if outs_before is None else [(outs_before, IN_VMEM)]

    up_shape, down_shape = (model_width, part), (part, model_width)
    outputs["rows_out"] = [(shape_of((blocks, index + 1, capacity, model_width), BF16), IN_VMEM)]
    own_up, own_down = shape_of(up_shape, BF16), shape_of(down_shape, BF16)
    outputs["own"] = [(own_up, ANYWHERE), (own_up, ANYWHERE), (own_down, ANYWHERE), (own_down, ANYWHERE)]
    outputs["pass_up"] = [(shape_of((half - 1,) + up_shape, BF16), IN_VMEM)] if half > 1 else []
    outputs["pass_down"] = [(shape_of((half - 1,) + down_shape, BF16), IN_VMEM)] if half > 1 else []
    outputs["next_swapped"] = [(shape_of(array.shape, BF16), ANYWHERE) for array in next_mine]
    outputs["gates_to"] = [(shape_of(slot_gates.shape, F32), ANYWHERE)] if first else []
    outputs["moved_to"] = [
        (
            shape_of((grid.exp_size,) + array.shape[(1 if place is None else 2) :], array.dtype),
            ANYWHERE,
        )
        for array, place in moved
    ]
    rows_shape, gate_shape = (blocks, capacity, model_width), (blocks, 8, capacity)
    if last:
        outputs["back_rows"] = [(shape_of(rows_shape, BF16), ANYWHERE)]
        outputs["back_gates"] = [(shape_of(gate_shape, F32), ANYWHERE)]
    else:
        outputs["grad_rows"] = [(shape_of(rows_shape, BF16), IN_VMEM)]
        outputs["grad_gates"] = [(shape_of(gate_shape, F32), IN_VMEM)]

    sems = lambda *shape: pltpu.SemaphoreType.DMA(shape)
    scratch["rows_all"] = pltpu.VMEM(rows_shape, BF16)
    scratch["cot"] = pltpu.VMEM(rows_shape, BF16)
    scratch["up_all"] = pltpu.VMEM((shards,) + up_shape, BF16)
    scratch["down_all"] = pltpu.VMEM((shards,) + down_shape, BF16)
    scratch["active"] = pltpu.VMEM((shards, count, part), BF16)
    scratch["grad_hidden"] = pltpu.VMEM((shards, count, part), BF16)
    scratch["unscaled"] = pltpu.VMEM((shards, count, part), F32)
    if first:
        scratch["gates"] = pltpu.VMEM(slot_gates.shape, F32)
        scratch["gate_sem"] = sems(1)
        scratch["row_send"] = sems(grid.z_size, grid.y_size)
        scratch["row_receive"] = sems(grid.z_size, grid.y_size)
    if last:
        scratch["grad_rows"] = pltpu.VMEM(rows_shape, BF16)
        scratch["grad_gates"] = pltpu.VMEM(gate_shape, F32)
        scratch["back_send"] = sems(2, grid.z_size, grid.y_size)
        scratch["back_receive"] = sems(2, grid.z_size, grid.y_size)
    scratch["gate_column"] = pltpu.VMEM((count, 1), F32)
    scratch["rows_t"] = pltpu.VMEM((model_width, count), BF16)
    scratch["slot_t"] = pltpu.VMEM((model_width, count), BF16)
    scratch["total"] = pltpu.VMEM((count, model_width), F32)
    scratch["grad_up"] = pltpu.VMEM((2,) + up_shape, BF16)
    scratch["grad_down"] = pltpu.VMEM((2,) + down_shape, BF16)
    if half > 1:
        for name, shape in (("up", up_shape), ("down", down_shape)):
            scratch["far_keep_" + name] = pltpu.VMEM((half - 1,) + shape, BF16)
            scratch["far_taken_" + name] = pltpu.VMEM((half - 1,) + shape, BF16)
    scratch["load_sem"] = sems(5)
    scratch["fetch_sem"] = sems(2 * shards, half + 1)
    scratch["store_sem"] = sems(2, half + 1)
    scratch["store_there"] = sems(2, half + 1)
    scratch["stored_here"] = sems(shards, half + 1)
    copies = (len(moved) + 1) * grid.exp_size + half * (shards + 1) + len(next_mine)
    scratch["send"] = sems(copies)
    scratch["receive"] = sems(copies)
    scratch["own_sem"] = sems(max(len(moved), 1))

    layout = {name: len(group) for name, group in inputs.items()}
    layout.update({name: len(group) for name, group in outputs.items()})
    layout.update({name: 1 for name in scratch})

    def body(*refs):
        named = dict(zip(layout, _grouped(refs, layout)))
        up_keep, up_taken, down_keep, down_taken = named.pop("own")
        far = lambda name: list(named.pop(name)) if half > 1 else []
        named["keep_up"] = [up_keep] + far("far_keep_up")
        named["taken_up"] = [up_taken] + far("far_taken_up")
        named["keep_down"] = [down_keep] + far("far_keep_down")
        named["taken_down"] = [down_taken] + far("far_taken_down")
        flat = [ref for group in named.values() for ref in group]
        sizes = {name: len(group) for name, group in named.items()}
        expert_kernel(
            *flat, layout=sizes, index=index, local=local, half=half, capacity=capacity,
            parts=[place for _, place in moved],
        )

    results = pl.pallas_call(
        body,
        in_specs=[spec for group in inputs.values() for _, spec in group],
        out_specs=tuple(spec for group in outputs.values() for _, spec in group),
        out_shape=tuple(shape for group in outputs.values() for shape, _ in group),
        scratch_shapes=list(scratch.values()),
        compiler_params=params(collective_id=collective_id, has_side_effects=True),
        cost_estimate=hint(45),
        name=f"expert_{index}",
    )(*[array for group in inputs.values() for array, _ in group])
    return dict(zip(outputs, _grouped(results, {name: len(group) for name, group in outputs.items()})))


def local_picks(routes, slots, capacity, local, index, slot_count):
    member, which = lax.div(routes, local), lax.rem(routes, local)
    places = jnp.where(which == index, member * capacity + slots, -1)
    lane = lax.broadcasted_iota(jnp.int32, (routes.shape[0], slot_count), 1)
    return [lane == places[:, k : k + 1] for k in range(2)]


def unroute_kernel(
    hidden, cotangent, routed, probabilities, gates, plane, columns, counts, *refs,
    experts, local, token_total, lanes,
):
    grads, gate_grads = refs[:local], refs[local : 2 * local]
    grad_hidden, grad_branch, small = refs[2 * local :]
    rows = hidden.shape[0]
    members, capacity, model_width = grads[0].shape
    grad_output = cotangent[...].astype(F32)
    grad_routed = jnp.zeros(hidden.shape, F32)
    found = [jnp.zeros((rows, capacity), F32), jnp.zeros((rows, capacity), F32)]
    routes, slots = int_columns(columns)
    member, which = lax.div(routes, local), lax.rem(routes, local)
    lane = lax.broadcasted_iota(jnp.int32, (rows, capacity), 1)
    for index in range(local):
        picks = local_picks(routes, slots, capacity, local, index, members * capacity)
        grad_routed = grad_routed + matmul(
            jnp.where(picks[0] | picks[1], 1.0, 0.0).astype(BF16),
            grads[index][...].reshape(members * capacity, model_width),
        )
        for place in range(members):
            spots = jnp.where((which == index) & (member == place), slots, -1)
            for k in range(2):
                found[k] = found[k] + jnp.where(
                    lane == spots[:, k : k + 1], gate_grads[index][place, 0:1, :], 0.0
                )
    grad_gates = [jnp.sum(found[k], axis=1, keepdims=True) for k in range(2)]
    powers = probabilities[...]
    lane = expert_lane(powers.shape, lanes)
    inside = (lane >= 0) & (lane < experts)
    picked = [lane == routes[:, k : k + 1] for k in range(2)]
    chosen_total = sum(
        jnp.sum(jnp.where(picked[k], powers, 0.0), axis=1, keepdims=True) for k in range(2)
    )
    weighted = grad_gates[0] * gates[:, 0:1] + grad_gates[1] * gates[:, 1:2]
    grad_mass = (AUX_WEIGHT * experts / (2.0 * token_total * token_total)) * counts[0:1, :]
    grad_mass = jnp.where(inside, grad_mass, 0.0)
    for k in range(2):
        grad_mass = grad_mass + jnp.where(picked[k], (grad_gates[k] - weighted) / chosen_total, 0.0)
    grad_logits = powers * (grad_mass - jnp.sum(powers * grad_mass, axis=1, keepdims=True))
    extra = plane[:, lanes.base :]
    grad_routed = grad_routed + contract_last(grad_logits.astype(BF16), extra)
    hidden_state = hidden[...]
    scale = lax.rsqrt(jnp.mean(hidden_state * hidden_state, axis=1, keepdims=True) + EPSILON)
    normed = hidden_state * scale
    product = grad_routed * normed
    gain_grad = jnp.sum(product, axis=0, keepdims=True)
    small_t = matmul(grad_logits.T.astype(BF16), routed[...])
    row = lax.broadcasted_iota(jnp.int32, small_t.shape, 0)
    small_t = jnp.where(row == lanes.gain, gain_grad, small_t)
    small[...] = small_t.T
    gains = extra.astype(F32).T[lanes.gain : lanes.gain + 1]
    grad = scale * (
        grad_routed * gains - normed * jnp.mean(product * gains, axis=1, keepdims=True)
    ) + grad_output
    grad_hidden[...] = grad
    grad_branch[...] = grad.astype(BF16)


def context_grad_kernel(
    fsdp_index, grad_branch, attention_out, context, grad_t, grad_n, grad_out, total, *, heads, width
):
    @pl.when(pl.program_id(0) == 0)
    def _():
        total[...] = jnp.zeros_like(total)

    branch = grad_branch[0]
    grad = contract_last(attention_out[...], branch).astype(BF16)
    for head in range(heads):
        part = grad[head * width : (head + 1) * width]
        grad_t[head] = part
        grad_n[head] = turned(part).astype(BF16)
    total[...] += matmul(context[0], branch)

    @pl.when(pl.program_id(0) == pl.num_programs(0) - 1)
    def _():
        grad_out[...] = total[...].astype(BF16)


def project_back_kernel(
    grad_projected, normed, plane, small, probabilities, grad_bias, grad_first, grad_plane, total,
    bias_t, *, lanes, heads, feature_rows, bucket_rows,
):
    step = pl.program_id(0)

    @pl.when(step == 0)
    def _():
        total[...] = jnp.zeros_like(total)

    grad = grad_projected[...]
    grad_first[0] = matmul(plane[:, : lanes.weights], grad).astype(BF16)
    total[: lanes.weights, :] += matmul(grad, normed[...])

    @pl.when(step == pl.num_programs(0) - 1)
    def _():
        grad_plane[...] = total[...].T.astype(BF16)
        span = grad_bias.shape[2]
        select, _ = bucket_rows_select(plane.shape[0], feature_rows, bucket_rows, span)
        bias_t[...] = jnp.zeros_like(bias_t)
        first = lanes.table + lax.axis_index("fsdp") * heads
        for head in range(heads):
            bias_t[pl.ds(first + head, 1), :] = grad_bias[head]
        high = bias_t[...].astype(BF16)
        rest = (bias_t[...] - high.astype(F32)).astype(BF16)
        table = contract_last(select, high) + contract_last(select, rest)
        mass = jnp.sum(probabilities[...], axis=0, keepdims=True)
        mass = pltpu.roll(jnp.broadcast_to(mass, (8, lanes.extra)), lanes.shift, 1)[0:1]
        lane = lax.broadcasted_iota(jnp.int32, table.shape, 1)
        row = lax.broadcasted_iota(jnp.int32, table.shape, 0)
        is_small = (lane >= lanes.router) & (lane < lanes.table)
        is_mass = (lane >= lanes.count) & (lax.rem(row, feature_rows) == 0)
        extra = table + jnp.where(is_small, small[...], 0.0) + jnp.where(is_mass, mass, 0.0)
        grad_plane[:, lanes.base :] = (total[lanes.base :, :].T + extra).astype(BF16)


def last_kernel(
    first, planes, out_grad, first_parts, plane_parts, out_parts,
    first_in, first_sum, planes_in, plane_sum, send, receive, own, *, spread_out,
):
    grid = Grid().here()
    links = Links(send, receive)
    z_size, y_size, x_size, fsdp_size = grid.z_size, grid.y_size, grid.x_size, grid.fsdp_size
    exp_size = grid.exp_size
    sibling = grid.sibling(grid.fsdp)
    near = [
        grid.at(z=(grid.z + hop) % z_size, fsdp=(grid.fsdp + turn) % fsdp_size)
        for hop in range(z_size)
        for turn in range(fsdp_size)
        if hop or turn
    ]
    beside = [grid.at(y=(grid.y + hop) % y_size) for hop in range(1, y_size)]

    per_sender = grid.device_count if spread_out else exp_size
    base = 0 if spread_out else grid.fsdp * exp_size
    out_sends = []
    for number in range(per_sender):
        to = base + number
        out_sends.append((to, number))
    if spread_out:
        out_origins = [(origin, origin) for origin in range(grid.device_count)]
    else:
        out_origins = [
            (member * fsdp_size + grid.linear // exp_size, member) for member in range(exp_size)
        ]
    own_slot = grid.linear if spread_out else grid.exp
    out_base = links.used
    links.used += per_sender

    def place_of(linear):
        return (linear // fsdp_size, linear % fsdp_size)

    def out_copy(to, number, slot):
        return pltpu.make_async_remote_copy(
            src_ref=out_grad.at[number], dst_ref=out_parts.at[slot],
            send_sem=send.at[out_base + number], recv_sem=receive.at[out_base + slot],
            device_id=place_of(to), device_id_type=MESH,
        )

    barrier = pltpu.get_barrier_semaphore()
    for device in near + beside:
        pl.semaphore_signal(barrier, inc=1, device_id=device, device_id_type=MESH)
    for origin, _ in out_origins:

        @pl.when(origin != grid.linear)
        def _(origin=origin):
            pl.semaphore_signal(
                barrier, inc=1, device_id=place_of(origin), device_id_type=MESH
            )

    to_self = (
        1 if spread_out else jnp.where(grid.linear // exp_size == grid.fsdp, 1, 0)
    )
    pl.semaphore_wait(barrier, len(near) + len(beside) + per_sender - to_self)

    first_copies = []
    for hop in range(x_size):
        mine = grid.x_from(hop)
        first_copies.append(
            links.copy(
                first.at[grid.sibling(mine)], first_in.at[hop], (grid.exp, sibling), first_in.at[hop]
            )
        )
        first_copies[-1][0].start()
    beside_copies = []
    for hop in range(1, y_size):
        to = (grid.y + hop) % y_size
        beside_copies.append(
            links.copy(
                planes.at[:, to], planes_in.at[hop - 1], grid.at(y=to), planes_in.at[hop - 1]
            )
        )
        beside_copies[-1][0].start()
    for to, number in out_sends:

        @pl.when(to != grid.linear)
        def _(to=to, number=number):
            out_copy(to, number, own_slot).start()

        @pl.when(to == grid.linear)
        def _(number=number):
            pltpu.make_async_copy(out_grad.at[number], out_parts.at[own_slot], own.at[0]).start()

    along_x = []
    for hop in range(x_size):
        first_copies[hop][1].wait_recv()
        summed = first[grid.x_from(hop)].astype(F32) + first_in[hop].astype(F32)
        if hop == 0:
            first_parts[0] = summed.astype(BF16)
        else:
            first_sum[hop - 1] = summed.astype(BF16)
            along_x.append(
                links.copy(
                    first_sum.at[hop - 1], first_parts.at[hop], (grid.exp, grid.x_from(hop)),
                    first_parts.at[hop],
                )
            )
            along_x[-1][0].start()
    for going, coming in beside_copies:
        coming.wait_recv()
    along_z = []
    for hop in list(range(1, z_size)) + [0]:
        to_z = (grid.z + hop) % z_size
        summed = planes[to_z, grid.y].astype(F32)
        for other in range(y_size - 1):
            summed = summed + planes_in[other, to_z].astype(F32)
        plane_sum[hop] = summed.astype(BF16)
        for turn in range(fsdp_size):
            if hop == 0 and turn == 0:
                continue
            to = (grid.fsdp + turn) % fsdp_size
            origin = (grid.fsdp + fsdp_size - turn) % fsdp_size
            along_z.append(
                links.copy(
                    plane_sum.at[hop, to],
                    plane_parts.at[hop, grid.fsdp],
                    grid.at(z=to_z, fsdp=to),
                    plane_parts.at[hop, origin],
                )
            )
            along_z[-1][0].start()
    kept = pltpu.make_async_copy(
        plane_sum.at[0, grid.fsdp], plane_parts.at[0, grid.fsdp], own.at[1]
    )
    kept.start()
    for going, coming in along_x + along_z:
        coming.wait_recv()
    for going, _ in first_copies + beside_copies + along_x + along_z:
        going.wait_send()
    kept.wait()
    for origin, slot in out_origins:

        @pl.when(origin != grid.linear)
        def _(origin=origin, slot=slot):
            out_copy(origin, 0, slot).wait_recv()

    for to, number in out_sends:

        @pl.when(to != grid.linear)
        def _(to=to, number=number):
            out_copy(to, number, own_slot).wait_send()

        @pl.when(to == grid.linear)
        def _(number=number):
            pltpu.make_async_copy(out_grad.at[number], out_parts.at[own_slot], own.at[0]).wait()


def mixture_kernel(hidden, gates, columns, rows_in, output, *, local):
    members, _, capacity, model_width = rows_in.shape
    routes, slots = int_columns(columns)
    total = hidden[...]
    picked = [jnp.zeros(hidden.shape, F32), jnp.zeros(hidden.shape, F32)]
    for index in range(local):
        picks = local_picks(routes, slots, capacity, local, index, members * capacity)
        values = rows_in[:, index].reshape(members * capacity, model_width)
        for k in range(2):
            picked[k] = picked[k] + matmul(jnp.where(picks[k], 1.0, 0.0).astype(BF16), values)
    for k in range(2):
        total = total + gates[:, k : k + 1] * picked[k]
    output[...] = total.astype(BF16)


def finish_kernel(
    first_parts, plane_parts, out_parts, tokens, grad_hidden, attention_in, attention_gain, counts,
    grad_tokens, grad_gain, grad_in, grad_out, grad_mixture, grad_router, grad_table, balance,
    *, lanes, heads, width, head_count, experts, token_total,
):
    total = jnp.sum(first_parts[...].astype(F32), axis=0).T
    inputs = tokens[...].astype(F32)
    scale = lax.rsqrt(jnp.mean(inputs * inputs, axis=1, keepdims=True) + EPSILON)
    normed = inputs * scale
    grad_tokens[...] = grad_hidden[...] + scale * (
        total - normed * jnp.mean(total * normed, axis=1, keepdims=True)
    )
    fsdp_size = plane_parts.shape[1]
    model_width = head_count * width
    summed = jnp.sum(plane_parts[...].astype(F32), axis=0)
    sums = [summed[place] for place in range(fsdp_size)]
    columns = []
    for kind in range(3):
        pieces = [
            sums[place][:, kind * heads * width : (kind + 1) * heads * width]
            for place in range(fsdp_size)
        ]
        columns.append(jnp.concatenate(pieces, axis=1)[:, :model_width])
    gathered = jnp.concatenate(columns, axis=1)
    feature_rows = gathered.shape[0]
    gain = jnp.sum(gathered * attention_in[...].astype(F32), axis=1, keepdims=True)
    gain = padded_rows(jnp.broadcast_to(gain, (feature_rows, 128)), 128).T
    grad_gain[...] = gain[0:1, :feature_rows]
    grad_in[...] = gathered * as_column(attention_gain[...], feature_rows)
    grad_out[...] = jnp.sum(out_parts[...].astype(F32), axis=0)
    extra = sum(part[:, lanes.base :] for part in sums)
    extra_t = padded_rows(extra, 128).T
    grad_mixture[...] = extra_t[lanes.gain : lanes.gain + 1, :feature_rows]
    grad_router[...] = extra_t[lanes.router : lanes.router + experts, :feature_rows]
    grad_table[...] = extra[: grad_table.shape[0], lanes.table : lanes.table + head_count]
    mass = jnp.broadcast_to(extra[0:1], (8, lanes.extra))
    mass = pltpu.roll(mass, lanes.extra - lanes.shift, 1)
    lane = expert_lane(mass.shape, lanes)
    terms = jnp.where((lane >= 0) & (lane < experts), mass * counts[...], 0.0)[0:1]
    balance[...] = jnp.sum(terms, axis=1, keepdims=True) * (
        experts / (2.0 * token_total * token_total)
    )


def sum_kernel(*refs, local, terms):
    outputs = refs[2 * local * terms :]
    for which in range(2):
        for index in range(local):
            first = (index * 2 + which) * terms
            shape = outputs[which].shape[1:]
            total = refs[first][...].reshape(shape).astype(F32)
            for ref in refs[first + 1 : first + terms]:
                total = total + ref[...].reshape(shape).astype(F32)
            outputs[which][index] = total


def sum_grads(groups, up_shape, down_shape, blocks):
    local = len(groups)
    depth, part = up_shape[1], down_shape[1]
    sizes = ((depth, part), (part // blocks, down_shape[2]))
    arrays, specs = [], []
    for group in groups:
        for size, (keep, taken, passed) in zip(sizes, group):
            for array in (keep, taken, *passed):
                arrays.append(array)
                specs.append(pl.BlockSpec(size, lambda c: (c, 0)))
    return pl.pallas_call(
        partial(sum_kernel, local=local, terms=len(arrays) // (2 * local)),
        grid=(blocks,),
        in_specs=specs,
        out_specs=[
            pl.BlockSpec((local, depth, part), lambda c: (0, 0, c)),
            pl.BlockSpec((local, part // blocks, down_shape[2]), lambda c: (0, c, 0)),
        ],
        out_shape=(shape_of(up_shape, F32), shape_of(down_shape, F32)),
        compiler_params=params(),
        cost_estimate=hint(8),
        name="sum_grads",
    )(*arrays)


def over_x(array, hop):
    fsdp_size = lax.axis_size("fsdp")
    return lax.ppermute(array, "fsdp", [(i, (i + 2 * hop) % fsdp_size) for i in range(fsdp_size)])


def over_core(array):
    return lax.ppermute(array, "fsdp", [(i, i ^ 1) for i in range(lax.axis_size("fsdp"))])


def on_device(
    tokens,
    cotangent,
    segments,
    routes,
    slots,
    attention_gain,
    mixture_gain,
    attention_in,
    attention_out,
    router_weight,
    position_table,
    expert_up,
    expert_down,
):
    grid = Grid()
    exp_size, fsdp_size, chips = grid.exp_size, grid.fsdp_size, grid.x_size
    device_count = grid.device_count
    fsdp_index = lax.axis_index("fsdp")
    rows, model_width = tokens.shape
    length = rows * fsdp_size
    head_count = position_table.shape[1]
    width = model_width // head_count
    heads = -(-head_count // fsdp_size)
    padded_heads = heads * fsdp_size
    feature_rows, bucket_rows = attention_in.shape[0], position_table.shape[0]
    experts = router_weight.shape[1]
    local = expert_up.shape[0]
    capacity = 4 * rows // experts
    token_total = rows * device_count
    span = WINDOW + 2 * SKEW + QUERY_BLOCK
    lanes = Lanes(heads, width, padded_heads, experts)
    part = expert_down.shape[1]
    gain_row = attention_gain.reshape(1, feature_rows)

    shard_shapes = [shape_of((model_width, part), BF16), shape_of((part, model_width), BF16)]
    copies = (
        2 * fsdp_size + grid.z_size * fsdp_size + grid.z_size * grid.y_size
        + grid.z_size + grid.y_size + grid.x_size + 1
    )
    started = pl.pallas_call(
        partial(
            start_kernel, lanes=lanes, heads=heads, width=width, head_count=head_count,
            experts=experts, capacity=capacity, local=local,
        ),
        out_shape=tuple(
            [
                shape_of((fsdp_size, rows, model_width), BF16),
                shape_of((grid.z_size, grid.y_size, fsdp_size, feature_rows, lanes.width), BF16),
                shape_of((experts * capacity, model_width), BF16),
                shape_of((8, rows), F32),
                shape_of((rows, 128), F32),
                shape_of((grid.z_size, grid.y_size, chips, 2, feature_rows, model_width), BF16),
            ]
            + shard_shapes * local
        ),
        in_specs=[ANYWHERE] + [IN_VMEM] * 8 + [ANYWHERE] * 3,
        out_specs=tuple(
            [ANYWHERE, ANYWHERE, IN_VMEM, IN_VMEM, IN_VMEM, ANYWHERE] + [ANYWHERE] * (2 * local)
        ),
        scratch_shapes=[
            pltpu.VMEM((fsdp_size, feature_rows, lanes.width), BF16),
            pltpu.VMEM(expert_up.shape, BF16),
            pltpu.VMEM(expert_down.shape, BF16),
            dma_sems(copies),
            dma_sems(copies),
            dma_sems(3),
            dma_sems(2 * local),
            dma_sems(local * (fsdp_size + 1)),
        ],
        compiler_params=params(collective_id=0, has_side_effects=True),
        cost_estimate=hint(20),
        name="start",
    )(
        tokens, cotangent, routes.T, slots.T, gain_row, mixture_gain.reshape(1, feature_rows),
        attention_in, router_weight.T, position_table, attention_out, expert_up, expert_down,
    )
    all_tokens, all_planes, cotangent_slots, position_rows, columns, full_out = started[:6]
    own_shards = [started[6 + 2 * index : 8 + 2 * index] for index in range(local)]
    plane = all_planes.reshape(model_width, lanes.width)
    full_out = full_out.reshape(model_width, model_width)

    def along_x(array):
        return [over_x(array, -hop) for hop in range(1, chips)]

    near_up, near_down = [None] * local, [None] * local
    near_up[0] = along_x(own_shards[0][0])
    cotangent_in = lax.all_to_all(
        cotangent_slots.reshape(exp_size, local * capacity, model_width),
        "exp", split_axis=0, concat_axis=0, tiled=True,
    ).reshape(exp_size, local, capacity, model_width)

    head_t = lambda size: pl.BlockSpec((heads, size, rows), lambda s, *_: (0, 0, s))
    head_n = lambda size: pl.BlockSpec((heads, rows, size), lambda s, *_: (0, s, 0))
    normed, query_t, key_n, query_n, value_n, key_t, value_t, bias, counts = pl.pallas_call(
        partial(
            project_kernel, heads=heads, width=width, lanes=lanes, feature_rows=feature_rows,
            bucket_rows=bucket_rows,
        ),
        grid=(fsdp_size,),
        in_specs=[
            pl.BlockSpec((1, rows, model_width), lambda s: (s, 0, 0)),
            whole((model_width, lanes.width)),
            pl.BlockSpec((1, rows), lambda s: (0, s)),
        ],
        out_specs=[
            pl.BlockSpec((rows, model_width), lambda s: (s, 0)),
            head_t(SKEW), head_n(SKEW), head_n(width), head_n(width), head_t(width), head_t(width),
            whole((heads, 1, span)),
            whole((8, lanes.extra)),
        ],
        out_shape=(
            shape_of((length, model_width), BF16),
            shape_of((heads, SKEW, length), BF16),
            shape_of((heads, length, SKEW), BF16),
            shape_of((heads, length, width), BF16),
            shape_of((heads, length, width), BF16),
            shape_of((heads, width, length), BF16),
            shape_of((heads, width, length), BF16),
            shape_of((heads, 1, span), F32),
            shape_of((8, lanes.extra), F32),
        ),
        scratch_shapes=[
            pltpu.VMEM((lanes.weights, model_width), BF16),
            pltpu.VMEM((lanes.extra, span), F32),
        ],
        compiler_params=params(),
        cost_estimate=hint(8),
        name="project",
    )(all_tokens, plane, segments.reshape(1, length))

    by_head = lambda *size: pl.BlockSpec((1,) + size, lambda h: (h, 0, 0))
    context, context_high, log_total = pl.pallas_call(
        partial(attend_kernel, rows=rows),
        grid=(heads,),
        in_specs=[
            by_head(SKEW, length), by_head(length, SKEW), by_head(width, length), by_head(1, span),
        ],
        out_specs=[
            pl.BlockSpec((fsdp_size, width, rows), lambda h: (0, h, 0)),
            by_head(width, length),
            by_head(1, length),
        ],
        out_shape=(
            shape_of((fsdp_size, heads * width, rows), BF16),
            shape_of((heads, width, length), F32),
            shape_of((heads, 1, length), F32),
        ),
        scratch_shapes=[
            pltpu.VMEM((SKEW, span), F32),
            pltpu.VMEM((WINDOW + QUERY_BLOCK, QUERY_BLOCK), F32),
        ],
        compiler_params=params(),
        cost_estimate=hint(13),
        name="attend",
    )(query_t, key_n, value_t, bias)

    (attended_t,) = exchange("fsdp", [(context, None)], 1, 9)
    own_down, near_up[0], attended_t = lax.optimization_barrier(
        (own_shards[0][1], near_up[0], attended_t)
    )
    near_down[0] = along_x(own_down)
    attended_t = attended_t.reshape(padded_heads * width, rows)

    gate_lanes = -(-local * capacity // 128) * 128
    hidden, routed, probabilities, gates, outgoing, slot_gates = pl.pallas_call(
        partial(route_kernel, experts=experts, lanes=lanes, capacity=capacity),
        out_shape=(
            shape_of((rows, model_width), F32),
            shape_of((rows, model_width), BF16),
            shape_of((rows, lanes.extra), F32),
            shape_of((rows, 2), F32),
            shape_of((experts * capacity, model_width), BF16),
            shape_of((exp_size, 8, gate_lanes), F32),
        ),
        compiler_params=params(),
        cost_estimate=hint(7),
        name="route",
    )(tokens, attended_t, full_out, plane, columns, position_rows)

    later = [own_shards[index] for index in range(1, local)]
    outgoing, later = lax.optimization_barrier((outgoing, later))
    for index in range(1, local):
        near_up[index], near_down[index] = [along_x(array) for array in later[index - 1]]
    outgoing = outgoing.reshape(exp_size, local, capacity, model_width)

    def pass_along(arrays):
        return [over_x(arrays[0][hop - 1], hop) for hop in range(1, chips)]

    returned, groups, moved, outs, rows_in, gates_in, swapped = [], [], [], None, None, None, ()
    for index in range(local):
        final = index == local - 1
        carried = list(moved) if final else list(moved) + [(outgoing, index + 1)]
        result = run_expert(
            index, local, outgoing, slot_gates, rows_in, gates_in, cotangent_in,
            [own_shards[index][0]] + near_up[index], [own_shards[index][1]] + near_down[index],
            swapped, () if final else own_shards[index + 1], carried, outs, 3 + index,
        )
        (outs,) = result["rows_out"]
        if index == 0:
            (gates_in,) = result["gates_to"]
        arrived = list(result["moved_to"])
        if not final:
            rows_in = arrived.pop()
            swapped = result["next_swapped"]
            moved = [(result["grad_rows"][0], None), (result["grad_gates"][0], None)]
        if arrived:
            returned.append(arrived)
        up_keep, up_taken, down_keep, down_taken = result["own"]
        if not final:
            passed = (result["pass_up"], result["pass_down"])
            passed, rows_in = lax.optimization_barrier((passed, rows_in))
            groups.append(
                [
                    (up_keep, up_taken, pass_along(passed[0])),
                    (down_keep, down_taken, pass_along(passed[1])),
                ]
            )
    up_passed = pass_along(result["pass_up"])
    returned.append([result["back_rows"][0], result["back_gates"][0]])
    groups, returned = lax.optimization_barrier((groups, returned))

    outs, returned = lax.optimization_barrier((outs, returned))
    out_rows = lax.all_to_all(outs, "exp", split_axis=0, concat_axis=0, tiled=True)

    grad_hidden, grad_branch, small = pl.pallas_call(
        partial(
            unroute_kernel, experts=experts, local=local, token_total=token_total, lanes=lanes
        ),
        out_shape=(
            shape_of((rows, model_width), F32),
            shape_of((rows, model_width), BF16),
            shape_of((model_width, lanes.extra), F32),
        ),
        compiler_params=params(),
        cost_estimate=hint(7),
        name="unroute",
    )(
        hidden, cotangent, routed, probabilities, gates, plane, columns, counts,
        *[part[0] for part in returned], *[part[1] for part in returned],
    )

    up_passed, grad_branch = lax.optimization_barrier((up_passed, grad_branch))
    all_branch = gather_rows(grad_branch, 4 + local, 15)
    pass_down, all_branch = lax.optimization_barrier((result["pass_down"], all_branch))
    groups.append(
        [(up_keep, up_taken, up_passed), (down_keep, down_taken, pass_along(pass_down))]
    )
    padded_out = full_out
    if padded_heads > head_count:
        padded_out = jnp.pad(full_out, ((0, padded_heads * width - model_width), (0, 0)))
    grad_t, grad_n, out_grad = pl.pallas_call(
        partial(context_grad_kernel, heads=heads, width=width),
        grid_spec=pltpu.PrefetchScalarGridSpec(
            num_scalar_prefetch=1,
            grid=(fsdp_size,),
            in_specs=[
                pl.BlockSpec((1, rows, model_width), lambda s, f: (s, 0, 0)),
                pl.BlockSpec((heads * width, model_width), lambda s, f: (f[0], 0)),
                pl.BlockSpec((1, heads * width, rows), lambda s, f: (s, 0, 0)),
            ],
            out_specs=[head_t(width), head_n(width), whole((heads * width, model_width))],
            scratch_shapes=[pltpu.VMEM((heads * width, model_width), F32)],
        ),
        out_shape=(
            shape_of((heads, width, length), BF16),
            shape_of((heads, length, width), BF16),
            shape_of((heads * width, model_width), BF16),
        ),
        compiler_params=params(),
        cost_estimate=hint(5),
        name="context_grad",
    )(fsdp_index.reshape(1), all_branch, padded_out, context)

    grad_projected, grad_bias = pl.pallas_call(
        partial(attend_back_kernel, scale=width ** (-0.5)),
        grid=(heads,),
        in_specs=[
            by_head(SKEW, length), by_head(length, SKEW), by_head(length, width),
            by_head(length, width), by_head(width, length), by_head(width, length),
            by_head(length, width), by_head(width, length), by_head(1, length), by_head(1, span),
        ],
        out_specs=[
            pl.BlockSpec((3, 1, width, length), lambda h: (0, h, 0, 0)),
            by_head(1, span),
        ],
        out_shape=(
            shape_of((3, heads, width, length), BF16),
            shape_of((heads, 1, span), F32),
        ),
        scratch_shapes=[
            pltpu.VMEM((SKEW, span), F32),
            pltpu.VMEM((SKEW, span), F32),
            pltpu.VMEM((length, width), F32),
            pltpu.VMEM((length, width), F32),
        ],
        compiler_params=params(),
        cost_estimate=hint(15),
        name="attend_back",
    )(query_t, key_n, query_n, value_n, key_t, grad_t, grad_n, context_high, log_total, bias)
    grad_projected = grad_projected.reshape(lanes.weights, length)

    grad_first, grad_plane = pl.pallas_call(
        partial(
            project_back_kernel, lanes=lanes, heads=heads, feature_rows=feature_rows,
            bucket_rows=bucket_rows,
        ),
        grid=(fsdp_size,),
        in_specs=[
            pl.BlockSpec((lanes.weights, rows), lambda s: (0, s)),
            pl.BlockSpec((rows, model_width), lambda s: (s, 0)),
            whole((model_width, lanes.width)),
            whole((model_width, lanes.extra)),
            whole((rows, lanes.extra)),
            whole((heads, 1, span)),
        ],
        out_specs=[
            pl.BlockSpec((1, model_width, rows), lambda s: (s, 0, 0)),
            whole((model_width, lanes.width)),
        ],
        out_shape=(
            shape_of((fsdp_size, model_width, rows), BF16),
            shape_of((model_width, lanes.width), BF16),
        ),
        scratch_shapes=[
            pltpu.VMEM((lanes.width, model_width), F32),
            pltpu.VMEM((lanes.extra, span), F32),
        ],
        compiler_params=params(),
        cost_estimate=hint(9),
        name="project_back",
    )(grad_projected, normed, plane, small, probabilities, grad_bias)

    out_rows, grad_first = lax.optimization_barrier((out_rows, grad_first))
    spread_out = heads * width * fsdp_size != model_width
    if spread_out:
        out_grad = lax.dynamic_update_slice(
            jnp.zeros((padded_heads * width, model_width), BF16), out_grad,
            (fsdp_index * heads * width, jnp.int32(0)),
        )[:model_width]
    out_grad = out_grad.reshape(-1, feature_rows, model_width)
    out_count = device_count if spread_out else exp_size
    plane_shape = (grid.z_size, grid.y_size, fsdp_size, feature_rows, lanes.width)
    parts_shape = (grid.z_size, fsdp_size, feature_rows, lanes.width)
    copies = 2 * fsdp_size + grid.z_size * fsdp_size + grid.y_size + out_count
    first_parts, plane_parts, out_parts = pl.pallas_call(
        partial(last_kernel, spread_out=spread_out),
        out_shape=(
            shape_of((chips, model_width, rows), BF16),
            shape_of(parts_shape, BF16),
            shape_of((out_count, feature_rows, model_width), BF16),
        ),
        in_specs=[IN_VMEM] * 3,
        out_specs=(IN_VMEM, ANYWHERE, ANYWHERE),
        scratch_shapes=[
            pltpu.VMEM((chips, model_width, rows), BF16),
            pltpu.VMEM((max(chips - 1, 1), model_width, rows), BF16),
            pltpu.VMEM((max(grid.y_size - 1, 1),) + parts_shape, BF16),
            pltpu.VMEM(parts_shape, BF16),
            dma_sems(copies),
            dma_sems(copies),
            dma_sems(2),
        ],
        compiler_params=params(collective_id=5 + local, has_side_effects=True),
        cost_estimate=hint(30),
        name="last",
    )(grad_first, grad_plane.reshape(plane_shape), out_grad)

    (
        grad_tokens, gain_grad, in_grad, out_sum, mixture_gain_grad, router_grad, table_grad, balance,
    ) = pl.pallas_call(
        partial(
            finish_kernel, lanes=lanes, heads=heads, width=width, head_count=head_count,
            experts=experts, token_total=token_total,
        ),
        out_shape=(
            shape_of((rows, model_width), F32),
            shape_of((1, feature_rows), F32),
            shape_of((feature_rows, 3 * model_width), F32),
            shape_of((feature_rows, model_width), F32),
            shape_of((1, feature_rows), F32),
            shape_of((experts, feature_rows), F32),
            shape_of((bucket_rows, head_count), F32),
            shape_of((1, 1), F32),
        ),
        compiler_params=params(),
        cost_estimate=hint(6),
        name="finish",
    )(first_parts, plane_parts, out_parts, tokens, grad_hidden, attention_in, gain_row, counts)

    layer_output = pl.pallas_call(
        partial(mixture_kernel, local=local),
        out_shape=shape_of((rows, model_width), BF16),
        compiler_params=params(),
        cost_estimate=hint(5),
        name="mixture",
    )(hidden, gates, columns, out_rows)

    up_grad, down_grad = sum_grads(groups, expert_up.shape, expert_down.shape, fsdp_size)
    return (
        layer_output,
        balance.reshape(()),
        grad_tokens,
        gain_grad.reshape(feature_rows),
        mixture_gain_grad.reshape(feature_rows),
        in_grad,
        out_sum,
        router_grad.T,
        table_grad,
        up_grad,
        down_grad,
    )


def solution(mesh):
    in_specs = (
        P(("exp", "fsdp"), None),
        P(("exp", "fsdp"), None),
        P("exp"),
        P(("exp", "fsdp"), None),
        P(("exp", "fsdp"), None),
        P(("exp", "fsdp")),
        P(("exp", "fsdp")),
        P(("exp", "fsdp"), None),
        P(("exp", "fsdp"), None),
        P(("exp", "fsdp"), None),
        P(("exp", "fsdp"), None),
        P("exp", "fsdp", None),
        P("exp", "fsdp", None),
    )
    out_specs = (
        P(("exp", "fsdp"), None),
        P(),
        P(("exp", "fsdp"), None),
        P(("exp", "fsdp")),
        P(("exp", "fsdp")),
        P(("exp", "fsdp"), None),
        P(("exp", "fsdp"), None),
        P(("exp", "fsdp"), None),
        P(("exp", "fsdp"), None),
        P("exp", "fsdp", None),
        P("exp", "fsdp", None),
    )
    return jax.shard_map(
        on_device, mesh=mesh, in_specs=in_specs, out_specs=out_specs, check_vma=False
    )
```

```python
from functools import partial

import jax
import jax.numpy as jnp
from jax import lax
from jax.experimental import pallas as pl
from jax.experimental.pallas import tpu as pltpu
from jax.sharding import PartitionSpec as P

WINDOW = 1024
BUCKETS = 256

EPSILON = 1e-06
AUX_WEIGHT = 0.01
MASKED = -1e30
QUERY_BLOCK = 256
SKEW = 128
VMEM_BYTES = 58 * 1024 * 1024
MESH = pl.DeviceIdType.MESH
F32 = jnp.float32
BF16 = jnp.bfloat16


def params(**kwargs):
    return pltpu.CompilerParams(vmem_limit_bytes=VMEM_BYTES, **kwargs)


def shape_of(shape, dtype):
    return jax.ShapeDtypeStruct(shape, dtype)


def whole(shape):
    return pl.BlockSpec(shape, lambda *_: (0,) * len(shape))


def contract_last(left_side, right_side):
    return lax.dot_general(
        left_side, right_side, (((1,), (1,)), ((), ())), preferred_element_type=F32
    )


def matmul(left_side, right_side):
    return jnp.dot(left_side, right_side, preferred_element_type=F32)


def turned(value):
    return value.astype(F32).T


def bucket_index(distance):
    near_count = BUCKETS // 2
    spread = max(WINDOW - near_count, 1)
    far_bucket = (
        near_count + jnp.maximum(distance - near_count, 0) * (BUCKETS - near_count) // spread
    )
    return jnp.where(distance < near_count, distance, far_bucket)

def hint(micros):
    return pl.CostEstimate(flops=int(micros * 1.0e9), bytes_accessed=1024, transcendentals=0)


class Grid:
    def __init__(self):
        self.exp_size, self.fsdp_size = lax.axis_size("exp"), lax.axis_size("fsdp")
        self.device_count = self.exp_size * self.fsdp_size
        self.y_size = max(
            y for y in range(1, self.exp_size + 1) if self.exp_size % y == 0 and 2 * y * y <= self.exp_size
        ) if self.exp_size > 1 else 1
        self.z_size = self.exp_size // self.y_size
        self.x_size = self.fsdp_size // 2

    def here(self):
        self.exp, self.fsdp = lax.axis_index("exp"), lax.axis_index("fsdp")
        self.z, self.y = self.exp // self.y_size, self.exp % self.y_size
        self.x, self.core = self.fsdp // 2, self.fsdp % 2
        self.linear = self.exp * self.fsdp_size + self.fsdp
        return self

    def at(self, z=None, y=None, fsdp=None):
        z = self.z if z is None else z
        y = self.y if y is None else y
        return (z * self.y_size + y, self.fsdp if fsdp is None else fsdp)

    def x_from(self, hop):
        return ((self.x + self.x_size + hop) % self.x_size) * 2 + self.core

    def sibling(self, fsdp):
        return fsdp + 1 - 2 * (fsdp % 2)


class Links:
    def __init__(self, send, receive):
        self.send, self.receive, self.used = send, receive, 0

    def copy(self, source, target, device, landing):
        index = self.used
        self.used += 1
        going = pltpu.make_async_remote_copy(
            src_ref=source, dst_ref=target, send_sem=self.send.at[index],
            recv_sem=self.receive.at[index], device_id=device, device_id_type=MESH,
        )
        coming = pltpu.make_async_remote_copy(
            src_ref=landing, dst_ref=landing, send_sem=self.send.at[index],
            recv_sem=self.receive.at[index], device_id=device, device_id_type=MESH,
        )
        return going, coming


def greet(devices):
    barrier = pltpu.get_barrier_semaphore()
    for device in devices:
        pl.semaphore_signal(barrier, inc=1, device_id=device, device_id_type=MESH)
    pl.semaphore_wait(barrier, len(devices))


def chip_peers(grid):
    peers = [(grid.exp, grid.sibling(grid.fsdp))]
    return peers + [(grid.exp, grid.x_from(hop)) for hop in range(1, grid.x_size)]


class ChipGather:
    def __init__(self, grid, links, own_sem, source, target):
        self.grid, self.links, self.target = grid, links, target
        self.own = pltpu.make_async_copy(source, target.at[grid.fsdp], own_sem)
        sibling = grid.sibling(grid.fsdp)
        self.along_x, self.across = [], []
        for hop in range(1, grid.x_size):
            self.along_x.append(
                links.copy(
                    source, target.at[grid.fsdp], (grid.exp, grid.x_from(hop)),
                    target.at[grid.x_from(-hop)],
                )
            )
        self.across.append(
            links.copy(source, target.at[grid.fsdp], (grid.exp, sibling), target.at[sibling])
        )

    def start(self):
        for going, _ in self.along_x + self.across:
            going.start()
        self.own.start()

    def forward(self):
        grid = self.grid
        for hop in range(1, grid.x_size):
            self.along_x[hop - 1][1].wait_recv()
            held = grid.x_from(-hop)
            other = grid.sibling(held)
            self.across.append(
                self.links.copy(
                    self.target.at[held], self.target.at[held],
                    (grid.exp, grid.sibling(grid.fsdp)), self.target.at[other],
                )
            )
            self.across[-1][0].start()

    def finish(self):
        for _, coming in self.across:
            coming.wait_recv()
        for going, _ in self.along_x + self.across:
            going.wait_send()
        self.own.wait()


class Exchange:
    def __init__(self, grid, axis, links, own_sems, pairs):
        size = grid.exp_size if axis == "exp" else grid.fsdp_size
        place = grid.exp if axis == "exp" else grid.fsdp
        device = (lambda to: (to, grid.fsdp)) if axis == "exp" else (lambda to: (grid.exp, to))
        self.peers = [device((place + hop) % size) for hop in range(1, size)]
        self.copies, self.own = [], []
        for index, (source, target) in enumerate(pairs):
            for hop in range(1, size):
                to, origin = (place + hop) % size, (place + size - hop) % size
                self.copies.append(
                    links.copy(source(to), target.at[place], device(to), target.at[origin])
                )
            self.own.append(
                pltpu.make_async_copy(source(place), target.at[place], own_sems.at[index])
            )

    def start(self):
        for going, _ in self.copies:
            going.start()
        for own in self.own:
            own.start()

    def finish(self):
        for going, coming in self.copies:
            coming.wait_recv()
            going.wait_send()
        for own in self.own:
            own.wait()


ANYWHERE = pl.BlockSpec(memory_space=pl.ANY)
IN_VMEM = pl.BlockSpec(memory_space=pltpu.VMEM)


def dma_sems(count):
    return pltpu.SemaphoreType.DMA((count,))


def exchange(axis, arrays, collective_id, micros):
    grid = Grid()
    size = grid.exp_size if axis == "exp" else grid.fsdp_size
    count = len(arrays)
    parts = [part for _, part in arrays]

    def kernel(*refs):
        sources, targets = refs[:count], refs[count : 2 * count]
        send, receive, own = refs[2 * count :]
        place = grid.here()
        pairs = [
            (partial(plane_of, source, part), target)
            for source, part, target in zip(sources, parts, targets)
        ]
        work = Exchange(place, axis, Links(send, receive), own, pairs)
        greet(work.peers)
        work.start()
        work.finish()

    return pl.pallas_call(
        kernel,
        out_shape=tuple(
            shape_of((size,) + array.shape[(1 if part is None else 2) :], array.dtype)
            for array, part in arrays
        ),
        in_specs=[IN_VMEM] * count,
        out_specs=tuple([ANYWHERE] * count),
        scratch_shapes=[dma_sems(count * size), dma_sems(count * size), dma_sems(count)],
        compiler_params=pltpu.CompilerParams(collective_id=collective_id, has_side_effects=True),
        cost_estimate=hint(micros),
        name=f"exchange_{collective_id}",
    )(*[array for array, _ in arrays])


def plane_of(source, part, to):
    return source.at[to] if part is None else source.at[to, part]


def gather_rows(array, collective_id, micros):
    grid = Grid()

    def kernel(source, target, send, receive, own):
        place = grid.here()
        work = ChipGather(place, Links(send, receive), own.at[0], source, target)
        greet(chip_peers(place))
        work.start()
        work.forward()
        work.finish()

    return pl.pallas_call(
        kernel,
        out_shape=shape_of((grid.fsdp_size,) + array.shape, array.dtype),
        in_specs=[IN_VMEM],
        out_specs=ANYWHERE,
        scratch_shapes=[dma_sems(2 * grid.fsdp_size), dma_sems(2 * grid.fsdp_size), dma_sems(1)],
        compiler_params=pltpu.CompilerParams(collective_id=collective_id, has_side_effects=True),
        cost_estimate=hint(micros),
        name=f"gather_{collective_id}",
    )(array)


class Lanes:
    def __init__(self, heads, width, padded_heads, experts):
        self.weights = 3 * heads * width
        self.base = self.weights // 128 * 128
        self.router = self.weights - self.base
        self.gain = self.router + experts
        self.table = self.gain + 1
        self.count = self.table + padded_heads
        self.width = -(-(self.weights + 2 * experts + 1 + padded_heads) // 128) * 128
        self.extra = self.width - self.base
        self.shift = self.count - self.router


def bucket_rows_select(features, feature_rows, bucket_rows, span):
    row = lax.broadcasted_iota(jnp.int32, (features, 1), 0)
    within = lax.rem(row, feature_rows)
    bucket = jnp.where(
        within < bucket_rows, lax.div(row, feature_rows) * bucket_rows + within, -1
    )
    distance = lax.broadcasted_iota(jnp.int32, (1, span), 1) - SKEW
    near = BUCKETS // 2
    spread = max(WINDOW - near, 1)
    far = near + lax.div(jnp.maximum(distance - near, 0) * (BUCKETS - near), spread)
    wanted = jnp.where(distance < near, distance, far)
    reachable = (distance >= 0) & (distance < WINDOW)
    wanted = jnp.where(reachable, wanted, -2)
    return jnp.where(bucket == wanted, 1.0, 0.0).astype(BF16), reachable


def as_column(row, size):
    row_place = lax.broadcasted_iota(jnp.int32, (size, size), 0)
    lane = lax.broadcasted_iota(jnp.int32, (size, size), 1)
    spread = jnp.broadcast_to(row.astype(F32), (size, size))
    return jnp.sum(jnp.where(row_place == lane, spread, 0.0), axis=1, keepdims=True)


def padded_rows(value, rows):
    if value.shape[0] == rows:
        return value
    return jnp.concatenate([value, jnp.zeros((rows - value.shape[0], value.shape[1]), F32)], axis=0)


def padded_lanes(value, lanes):
    if value.shape[1] == lanes:
        return value
    return jnp.concatenate([value, jnp.zeros((value.shape[0], lanes - value.shape[1]), F32)], axis=1)


class Wide:
    def __init__(self, grid, links, own_sem, source, target):
        self.grid, self.links, self.target = grid, links, target
        self.own = pltpu.make_async_copy(
            source, target.at[grid.z, grid.y, grid.x, grid.core], own_sem
        )
        self.stages = []
        stage = []
        for hop in range(1, grid.z_size):
            stage.append(
                links.copy(
                    source, target.at[grid.z, grid.y, grid.x, grid.core],
                    grid.at(z=(grid.z + hop) % grid.z_size),
                    target.at[(grid.z + grid.z_size - hop) % grid.z_size, grid.y, grid.x, grid.core],
                )
            )
        self.stages.append(stage)

    def start(self):
        self.own.start()
        for going, _ in self.stages[0]:
            going.start()

    def turn(self, axis):
        grid, target = self.grid, self.target
        for _, coming in self.stages[-1]:
            coming.wait_recv()
        stage = []
        if axis == "y":
            self.own.wait()
            held = target.at[:, grid.y, grid.x, grid.core]
            for hop in range(1, grid.y_size):
                origin = (grid.y + grid.y_size - hop) % grid.y_size
                stage.append(
                    self.links.copy(
                        held, held, grid.at(y=(grid.y + hop) % grid.y_size),
                        target.at[:, origin, grid.x, grid.core],
                    )
                )
        elif axis == "x":
            held = target.at[:, :, grid.x, grid.core]
            for hop in range(1, grid.x_size):
                origin = (grid.x + grid.x_size - hop) % grid.x_size
                stage.append(
                    self.links.copy(
                        held, held, (grid.exp, grid.x_from(hop)), target.at[:, :, origin, grid.core]
                    )
                )
        else:
            held = target.at[:, :, :, grid.core]
            stage.append(
                self.links.copy(
                    held, held, (grid.exp, grid.sibling(grid.fsdp)), target.at[:, :, :, 1 - grid.core]
                )
            )
        for going, _ in stage:
            going.start()
        self.stages.append(stage)

    def finish(self):
        for _, coming in self.stages[-1]:
            coming.wait_recv()
        for stage in self.stages:
            for going, _ in stage:
                going.wait_send()


def start_kernel(
    tokens, cotangent, routes_t, slots_t, attention_gain, mixture_gain, attention_in, router_t, table,
    attention_out, expert_up, expert_down, *refs, lanes, heads, width, head_count, experts, capacity,
    local,
):
    all_tokens, all_planes, cotangent_slots, position_rows, columns, full_out = refs[:6]
    shards = refs[6 : 6 + 2 * local]
    planes, up_stage, down_stage, send, receive, own, fetch, split = refs[6 + 2 * local :]
    grid = Grid().here()
    links = Links(send, receive)
    z_size, y_size, fsdp_size = grid.z_size, grid.y_size, grid.fsdp_size
    near = [
        grid.at(z=(grid.z + hop) % z_size, fsdp=(grid.fsdp + turn) % fsdp_size)
        for hop in range(z_size)
        for turn in range(fsdp_size)
        if hop or turn
    ]
    beside = [grid.at(y=(grid.y + hop) % y_size) for hop in range(1, y_size)]
    gathered = ChipGather(grid, links, own.at[0], tokens, all_tokens)
    widely = Wide(grid, links, own.at[2], attention_out, full_out)
    part = expert_down.shape[1]
    depth = expert_up.shape[1]
    fetches = []
    for index in range(local):
        fetches.append(
            pltpu.make_async_copy(expert_up.at[index], up_stage.at[index], fetch.at[2 * index])
        )
        fetches.append(
            pltpu.make_async_copy(
                expert_down.at[index], down_stage.at[index], fetch.at[2 * index + 1]
            )
        )
    greet(near + beside)
    gathered.start()
    widely.start()
    for copy in fetches:
        copy.start()

    feature_rows = attention_in.shape[0]
    model_width = head_count * width
    gained = attention_in[...].astype(F32) * as_column(attention_gain[...], feature_rows)
    route_rows, slot_rows = routes_t[...].astype(F32), slots_t[...].astype(F32)
    columns[...] = padded_rows(jnp.concatenate([route_rows, slot_rows], axis=0), 128).T
    row_count = columns.shape[0]
    expert_lanes = lax.broadcasted_iota(jnp.int32, (row_count, experts), 1).astype(F32)
    named = jnp.zeros((row_count, experts), F32)
    for k in range(2):
        named = named + jnp.where(expert_lanes == columns[:, k : k + 1], 1.0, 0.0)
    named = jnp.sum(named, axis=0, keepdims=True)
    place = lax.broadcasted_iota(jnp.int32, (feature_rows, feature_rows), 0)
    same = place == lax.broadcasted_iota(jnp.int32, (feature_rows, feature_rows), 1)
    router = contract_last(jnp.where(same, 1.0, 0.0).astype(BF16), router_t[...])
    pieces = [
        router,
        as_column(mixture_gain[...], feature_rows),
        padded_rows(padded_lanes(table[...].astype(F32), heads * fsdp_size), feature_rows),
        padded_rows(named, feature_rows),
    ]
    taken = sum(piece.shape[1] for piece in pieces)
    if lanes.width > lanes.weights + taken:
        pieces.append(jnp.zeros((feature_rows, lanes.width - lanes.weights - taken), F32))
    for place in range(fsdp_size):
        first, last = place * heads * width, min((place + 1) * heads * width, model_width)
        own_pieces = []
        for kind in range(3):
            if last > first:
                own_pieces.append(gained[:, kind * model_width + first : kind * model_width + last])
            if last - first < heads * width:
                own_pieces.append(
                    jnp.zeros((feature_rows, heads * width - max(last - first, 0)), F32)
                )
        planes[place] = jnp.concatenate(own_pieces + pieces, axis=1).astype(BF16)
    arrivals = [[] for _ in range(z_size)]
    sent = []
    for hop in range(z_size):
        for turn in range(fsdp_size):
            if hop == 0 and turn == 0:
                continue
            to = (grid.fsdp + turn) % fsdp_size
            origin = (grid.fsdp + fsdp_size - turn) % fsdp_size
            going, coming = links.copy(
                planes.at[to],
                all_planes.at[grid.z, grid.y, grid.fsdp],
                grid.at(z=(grid.z + hop) % z_size, fsdp=to),
                all_planes.at[(grid.z + z_size - hop) % z_size, grid.y, origin],
            )
            going.start()
            sent.append(going)
            arrivals[hop].append(coming)
    kept = pltpu.make_async_copy(
        planes.at[grid.fsdp], all_planes.at[grid.z, grid.y, grid.fsdp], own.at[1]
    )
    kept.start()
    widely.turn("y")

    for copy in fetches:
        copy.wait()
    splits = []
    for index in range(local):
        up, down = shards[2 * index : 2 * index + 2]
        stores = [
            (
                up_stage.at[index, :, pl.ds(block * part, part)],
                up.at[pl.ds(block * depth, depth), :],
            )
            for block in range(fsdp_size)
        ]
        for source, target in stores + [(down_stage.at[index], down)]:
            splits.append(pltpu.make_async_copy(source, target, split.at[len(splits)]))
            splits[-1].start()

    place = route_rows * capacity + slot_rows
    position_rows[...] = padded_rows(place, 8)
    select_rows(cotangent_slots, place, cotangent[...])

    forwarded = []
    for hop in range(z_size):
        held = (grid.z + z_size - hop) % z_size
        for coming in arrivals[hop]:
            coming.wait_recv()
        if hop == 0:
            kept.wait()
        for turn in range(1, y_size):
            going, coming = links.copy(
                all_planes.at[held, grid.y],
                all_planes.at[held, grid.y],
                grid.at(y=(grid.y + turn) % y_size),
                all_planes.at[held, (grid.y + y_size - turn) % y_size],
            )
            going.start()
            forwarded.append((going, coming))
        if hop == 0:
            widely.turn("x")
    gathered.forward()
    widely.turn("core")
    for going, coming in forwarded:
        coming.wait_recv()
        going.wait_send()
    for going in sent:
        going.wait_send()
    gathered.finish()
    widely.finish()
    for copy in splits:
        copy.wait()


def project_kernel(
    tokens, plane, segments, normed, query_t, key_n, query_n, value_n, key_t, value_t, bias, counts,
    weight_t, table_t, *, heads, width, lanes, feature_rows, bucket_rows,
):
    @pl.when(pl.program_id(0) == 0)
    def _():
        weight_t[...] = turned(plane[:, : lanes.weights]).astype(BF16)
        extra = plane[:, lanes.base :]
        span = bias.shape[2]
        select, reachable = bucket_rows_select(plane.shape[0], feature_rows, bucket_rows, span)
        table_t[...] = lax.dot_general(
            extra, select, (((0,), (0,)), ((), ())), preferred_element_type=F32
        )
        first = lanes.table + lax.axis_index("fsdp") * heads
        for head in range(heads):
            bias[head] = jnp.where(reachable, table_t[pl.ds(first + head, 1), :], MASKED)
        summed = jnp.sum(extra.astype(F32), axis=0, keepdims=True)
        counts[...] = pltpu.roll(
            jnp.broadcast_to(summed, counts.shape), lanes.extra - lanes.shift, 1
        )

    inputs = tokens[0].astype(F32)
    scale = lax.rsqrt(jnp.mean(inputs * inputs, axis=1, keepdims=True) + EPSILON)
    low = (inputs * scale).astype(BF16)
    normed[...] = low
    rows = low.shape[0]
    projected = contract_last(weight_t[...], low).astype(BF16).astype(F32)
    document = segments[...] % 4
    places = lax.broadcasted_iota(jnp.int32, (8, rows), 0)
    same = places == document
    hot = jnp.where(same, 1.0, 0.0)
    barred = jnp.where(same | (places >= 4), 0.0, MASKED)
    filler = jnp.zeros((SKEW - 8 - width, rows), F32)
    for head in range(heads):
        query = projected[head * width : (head + 1) * width] * width ** (-0.5)
        key = projected[(heads + head) * width : (heads + head + 1) * width]
        value = projected[(2 * heads + head) * width : (2 * heads + head + 1) * width]
        query_t[head] = jnp.concatenate([query, barred, filler], axis=0).astype(BF16)
        key_n[head] = jnp.concatenate([key, hot, filler], axis=0).T.astype(BF16)
        query_n[head] = query.T.astype(BF16)
        value_n[head] = value.T.astype(BF16)
        key_t[head] = key.astype(BF16)
        value_t[head] = value.astype(BF16)


def spans(length):
    for query_start in range(0, length, QUERY_BLOCK):
        key_start = max(0, query_start - WINDOW)
        yield query_start, key_start, query_start + QUERY_BLOCK - key_start


def spread_bias(bias, skew):
    skew[...] = pltpu.roll(
        jnp.broadcast_to(bias[0], skew.shape), 0, 1, stride=1, stride_axis=0
    )


def attend_kernel(query_t, key_n, value_t, bias, context, context_high, log_total, skew, scores, *, rows):
    spread_bias(bias, skew)
    for query_start, key_start, key_count in spans(query_t.shape[2]):
        queries = slice(query_start, query_start + QUERY_BLOCK)
        keys = slice(key_start, key_start + key_count)
        raw = matmul(key_n[0, keys, :], query_t[0, :, queries])
        for start in range(0, key_count, SKEW):
            offset = query_start - key_start - start + SKEW
            scores[start : start + SKEW, :] = (
                raw[start : start + SKEW] + skew[:, offset : offset + QUERY_BLOCK]
            )
        high = jnp.max(scores[:key_count, :], axis=0, keepdims=True)
        weights = jnp.exp(scores[:key_count, :] - high)
        total = jnp.sum(weights, axis=0, keepdims=True)
        gathered = matmul(value_t[0, :, keys], weights.astype(BF16)) / total
        context_high[0, :, queries] = gathered
        log_total[0, :, queries] = high + jnp.log(total)
        for start in range(0, QUERY_BLOCK, 128):
            place = query_start + start
            context[place // rows, :, place % rows : place % rows + 128] = gathered[
                :, start : start + 128
            ].astype(BF16)


def attend_back_kernel(
    query_t, key_n, query_n, value_n, key_t, grad_t, grad_n, context_high, log_total, bias,
    grad_projected, grad_bias, skew, grad_skew, grad_key, grad_value, *, scale,
):
    spread_bias(bias, skew)
    grad_skew[...] = jnp.zeros_like(grad_skew)
    grad_key[...] = jnp.zeros_like(grad_key)
    grad_value[...] = jnp.zeros_like(grad_value)
    inner = jnp.sum(grad_t[0].astype(F32) * context_high[0], axis=0, keepdims=True)
    for query_start, key_start, key_count in spans(query_t.shape[2]):
        queries = slice(query_start, query_start + QUERY_BLOCK)
        keys = slice(key_start, key_start + key_count)
        raw = matmul(key_n[0, keys, :], query_t[0, :, queries])
        grad_weights = matmul(value_n[0, keys, :], grad_t[0, :, queries])
        weights_low, grad_low = [], []
        for start in range(0, key_count, SKEW):
            offset = query_start - key_start - start + SKEW
            part = slice(start, start + SKEW)
            weights = jnp.exp(
                raw[part] + skew[:, offset : offset + QUERY_BLOCK] - log_total[0, :, queries]
            )
            grad_scores = weights * (grad_weights[part] - inner[:, queries])
            grad_skew[:, offset : offset + QUERY_BLOCK] += grad_scores
            weights_low.append(weights.astype(BF16))
            grad_low.append(grad_scores.astype(BF16))
        weights_low = jnp.concatenate(weights_low, axis=0)
        grad_low = jnp.concatenate(grad_low, axis=0)
        grad_projected[0, 0, :, queries] = (matmul(key_t[0, :, keys], grad_low) * scale).astype(BF16)
        grad_key[keys, :] += matmul(grad_low, query_n[0, queries, :])
        grad_value[keys, :] += matmul(weights_low, grad_n[0, queries, :])
    grad_projected[1, 0] = grad_key[...].T.astype(BF16)
    grad_projected[2, 0] = grad_value[...].T.astype(BF16)
    count = SKEW
    span = skew.shape[1]
    while count > 8:
        count //= 2
        grad_skew[:count, :] += pltpu.roll(grad_skew[count : 2 * count, :], span - count, 1)
    summed = grad_skew[0:1, :]
    for row in range(1, 8):
        summed = summed + pltpu.roll(grad_skew[row : row + 1, :], span - row, 1)
    grad_bias[0] = summed

def expert_lane(shape, lanes):
    return lax.broadcasted_iota(jnp.int32, shape, 1) - lanes.router


def int_columns(columns):
    values = columns[:, 0:4].astype(jnp.int32)
    return values[:, 0:2], values[:, 2:4]


def route_kernel(
    tokens, attended_t, attention_out, plane, columns, position_rows,
    hidden, routed, probabilities, gates, outgoing, slot_gates, *, experts, lanes, capacity,
):
    rows, model_width = tokens.shape
    routes, slots = int_columns(columns)
    attended_low = turned(attended_t[:model_width]).astype(BF16)
    hidden_state = tokens[...].astype(F32) + matmul(attended_low, attention_out[...])
    hidden[...] = hidden_state
    scale = lax.rsqrt(jnp.mean(hidden_state * hidden_state, axis=1, keepdims=True) + EPSILON)
    extra = plane[:, lanes.base :]
    gain = extra.astype(F32).T[lanes.gain : lanes.gain + 1]
    low = (hidden_state * scale * gain).astype(BF16)
    routed[...] = low
    logits = matmul(low, extra)
    lane = expert_lane(logits.shape, lanes)
    logits = jnp.where((lane >= 0) & (lane < experts), logits, MASKED)
    powers = jnp.exp(logits - jnp.max(logits, axis=1, keepdims=True))
    powers = powers / jnp.sum(powers, axis=1, keepdims=True)
    probabilities[...] = powers
    chosen = [
        jnp.sum(jnp.where(lane == routes[:, k : k + 1], powers, 0.0), axis=1, keepdims=True)
        for k in range(2)
    ]
    total = chosen[0] + chosen[1]
    gate_values = [chosen[k] / total for k in range(2)]
    pair = lax.broadcasted_iota(jnp.int32, (rows, 2), 1)
    gates[...] = jnp.where(pair == 0, gate_values[0], gate_values[1])
    members, _, gate_lanes = slot_gates.shape
    member_slots = experts // members * capacity
    slot_lanes = lax.broadcasted_iota(jnp.int32, (rows, gate_lanes), 1)
    inside = slot_lanes < member_slots
    places = routes * capacity + slots
    for member in range(members):
        by_slot = jnp.zeros((rows, gate_lanes), F32)
        for k in range(2):
            hit = (slot_lanes + member * member_slots == places[:, k : k + 1]) & inside
            by_slot = by_slot + jnp.where(hit, gate_values[k], 0.0)
        slot_gates[member] = jnp.broadcast_to(
            jnp.sum(by_slot, axis=0, keepdims=True), slot_gates.shape[1:]
        )
    select_rows(outgoing, position_rows[...], low)


def select_rows(outgoing, position_rows, values):
    slot_count, rows = outgoing.shape[0], values.shape[0]
    for start in range(0, slot_count, rows):
        slots = (lax.broadcasted_iota(jnp.int32, (rows, rows), 0) + start).astype(F32)
        picked = (slots == position_rows[0:1, :]) | (slots == position_rows[1:2, :])
        outgoing[start : start + rows, :] = matmul(
            jnp.where(picked, 1.0, 0.0).astype(BF16), values
        ).astype(BF16)


def gelu_parts(value):
    magnitude = jnp.abs(value)
    power = jnp.exp2(value * value * -0.7213475204444817)
    base = 1.0 + (0.3275911 * 0.7071067811865476) * magnitude
    step = pl.reciprocal(base, approx=True)
    step = step * (2.0 - base * step)
    series = step * (
        0.127414796
        + step * (-0.142248368 + step * (0.7107068705 + step * (-0.7265760135 + step * 0.5307027145)))
    )
    tail = series * power
    normal = jnp.where(value < 0.0, tail, 1.0 - tail)
    return value * normal, normal + value * (power * 0.3989422804014327)


def flipped(place, other, size):
    result, bit = 0, 1
    while bit < size:
        result = result + bit * ((place // bit + other // bit) % 2)
        bit *= 2
    return result


def expert_kernel(*refs, layout, index, local, half, capacity, parts):
    shards = 2 * half
    refs = Bag(layout, refs)
    grid = Grid().here()
    z_size, y_size = grid.z_size, grid.y_size
    first, last = index == 0, index == local - 1
    sibling = (grid.exp, grid.sibling(grid.fsdp))
    links = Links(refs.send[0], refs.receive[0])
    rows_all, cot, up_all, down_all = (
        refs.rows_all[0], refs.cot[0], refs.up_all[0], refs.down_all[0]
    )
    active, grad_hidden, unscaled = refs.active[0], refs.grad_hidden[0], refs.unscaled[0]
    gates, gate_column = refs.gates[0], refs.gate_column[0]
    rows_t, slot_t = refs.rows_t[0], refs.slot_t[0]
    grad_up, grad_down = refs.grad_up[0], refs.grad_down[0]
    grad_rows, grad_gates = refs.grad_rows[0], refs.grad_gates[0]
    up_keep, up_taken, down_keep, down_taken = refs.own
    keep_up = [up_keep] + list(refs.far_keep_up)
    taken_up = [up_taken] + list(refs.far_taken_up)
    keep_down = [down_keep] + list(refs.far_keep_down)
    taken_down = [down_taken] + list(refs.far_taken_down)
    load_sem, fetch_sem, store_sem = refs.load_sem[0], refs.fetch_sem[0], refs.store_sem[0]
    store_there, stored_here = refs.store_there[0], refs.stored_here[0]
    pass_sem = refs.pass_sem[0]
    blocks, _, model_width = rows_all.shape
    part = up_all.shape[2]
    count = blocks * capacity
    depth = model_width // shards
    power = z_size & (z_size - 1) == 0
    together = 2 if power and z_size > 1 else 1
    group_rows = together * y_size * capacity

    def source_z(turn):
        return flipped(grid.z, turn, z_size) if power else (grid.z + turn) % z_size

    def target_z(turn):
        return flipped(grid.z, turn, z_size) if power else (grid.z + z_size - turn) % z_size

    def owner(place, core):
        return ((grid.x + place % half) % half) * 2 + (core + place // half) % 2

    def rows_of(place, core=None):
        core = grid.core if core is None else core
        return pl.ds(pl.multiple_of(owner(place, core) * depth, 16), depth)

    loads = [pltpu.make_async_copy(refs.cot_in[0].at[:, index], cot, load_sem.at[0])]
    if not first:
        loads.append(pltpu.make_async_copy(refs.rows_in[0], rows_all, load_sem.at[1]))
    my_up, my_down = refs.my_up, refs.my_down
    swapped_up, swapped_down = refs.swapped_up, refs.swapped_down
    local_up = list(enumerate(my_up)) + [(half, array) for array in swapped_up]
    local_down = list(enumerate(my_down)) + [(half, array) for array in swapped_down]
    fetched_up = [
        pltpu.make_async_copy(
            array.at[rows_of(place), :], up_all.at[place, rows_of(shard), :],
            fetch_sem.at[place, number],
        )
        for number, (shard, array) in enumerate(local_up)
        for place in range(shards)
    ]
    fetched_down = {
        shard: pltpu.make_async_copy(
            array, down_all.at[shard], fetch_sem.at[shards + number, 0]
        )
        for number, (shard, array) in enumerate(local_down)
    }
    crossing = [shard for shard in range(half) if half + shard not in dict(local_up)]
    cross_down = {
        half + shard: links.copy(
            my_down[shard], down_all.at[half + shard], sibling, down_all.at[half + shard]
        )
        for shard in crossing
    }
    cross_up = [
        links.copy(
            my_up[shard].at[rows_of(place, 1 - grid.core), :],
            up_all.at[place, rows_of(shard), :], sibling,
            up_all.at[place, rows_of(half + shard), :],
        )
        for shard in crossing
        for place in range(shards)
    ]
    cross_next = [
        links.copy(source, target, sibling, target)
        for source, target in zip(refs.next_mine, refs.next_swapped)
    ]
    work = Exchange(
        grid, "exp", links, refs.own_sem[0],
        [
            (partial(plane_of, source, place), target)
            for source, place, target in zip(refs.moved_from, parts, refs.moved_to)
        ],
    )
    gate_work = None
    if first:
        gate_work = Exchange(
            grid, "exp", links, refs.gate_sem[0],
            [(partial(plane_of, refs.gates_from[0], None), gates)],
        )

    def member(z, y):
        return z * y_size + y

    def dispatch(turn, hop):
        to = member(target_z(turn), (grid.y + y_size - hop) % y_size)
        origin = member(source_z(turn), (grid.y + hop) % y_size)
        outgoing = refs.outgoing[0]
        going = pltpu.make_async_remote_copy(
            src_ref=outgoing.at[to, index], dst_ref=rows_all.at[grid.exp],
            send_sem=refs.row_send[0].at[turn, hop], recv_sem=refs.row_receive[0].at[turn, hop],
            device_id=(to, grid.fsdp), device_id_type=MESH,
        )
        coming = pltpu.make_async_remote_copy(
            src_ref=rows_all.at[origin], dst_ref=rows_all.at[origin],
            send_sem=refs.row_send[0].at[turn, hop], recv_sem=refs.row_receive[0].at[turn, hop],
            device_id=(to, grid.fsdp), device_id_type=MESH,
        )
        return going, coming

    def give_back(turn, hop):
        to = member(source_z(turn), (grid.y + hop) % y_size)
        origin = member(target_z(turn), (grid.y + y_size - hop) % y_size)
        pairs = []
        for number, (held, target) in enumerate(
            ((grad_rows, refs.back_rows[0]), (grad_gates, refs.back_gates[0]))
        ):
            sems = dict(
                send_sem=refs.back_send[0].at[number, turn, hop],
                recv_sem=refs.back_receive[0].at[number, turn, hop],
                device_id=(to, grid.fsdp), device_id_type=MESH,
            )
            pairs.append(
                (
                    pltpu.make_async_remote_copy(
                        src_ref=held.at[to], dst_ref=target.at[grid.exp], **sems
                    ),
                    pltpu.make_async_remote_copy(
                        src_ref=target.at[origin], dst_ref=target.at[origin], **sems
                    ),
                )
            )
        return pairs

    steps = [(turn, hop) for turn in range(z_size) for hop in range(y_size)]
    own_row = own_back = None
    if first:
        own_row = pltpu.make_async_copy(
            refs.outgoing[0].at[grid.exp, index], rows_all.at[grid.exp], load_sem.at[1]
        )
    if last:
        own_back = [
            pltpu.make_async_copy(held.at[grid.exp], target.at[grid.exp], load_sem.at[2 + number])
            for number, (held, target) in enumerate(
                ((grad_rows, refs.back_rows[0]), (grad_gates, refs.back_gates[0]))
            )
        ]

    for copy in loads:
        copy.start()
    for copy in list(fetched_down.values()) + fetched_up:
        copy.start()
    greet([((grid.exp + hop) % grid.exp_size, grid.fsdp) for hop in range(1, grid.exp_size)] + [sibling])
    if first:
        gate_work.start()
        own_row.start()
        for turn, hop in steps[1:]:
            dispatch(turn, hop)[0].start()
    for going, _ in list(cross_down.values()) + cross_up + cross_next:
        going.start()
    work.start()

    loads[0].wait()
    for place in range(shards):
        if place in fetched_down:
            fetched_down[place].wait()
        else:
            cross_down[place][1].wait_recv()
        unscaled[place] = contract_last(cot[...].reshape(count, model_width), down_all[place])
    if first:
        gate_work.finish()
        gates_out = pltpu.make_async_copy(gates, refs.gates_to[0], load_sem.at[4])
        gates_out.start()
    columns = gates[:, 0, :].T
    for block in range(blocks):
        piece = slice(block * capacity, (block + 1) * capacity)
        gate = columns[index * capacity : (index + 1) * capacity, block : block + 1]
        gate_column[piece, :] = gate
    slot_t[...] = (gate_column[...] * cot[...].reshape(count, model_width).astype(F32)).T.astype(BF16)
    for copy in fetched_up:
        copy.wait()
    for _, coming in cross_up:
        coming.wait_recv()
    if first:
        own_row.wait()
    else:
        loads[1].wait()

    def group(number, carry):
        turns = [number * together + more for more in range(together)]
        if together == 2:
            place_of_group = flipped(grid.z // 2, number, z_size // 2)
        else:
            place_of_group = source_z(number)
        if first:
            for turn in turns:
                for hop in range(y_size):

                    @pl.when(turn + hop > 0)
                    def _(turn=turn, hop=hop):
                        dispatch(turn, hop)[1].wait_recv()

        members = pl.ds(place_of_group * together * y_size, together * y_size)
        span = pl.ds(pl.multiple_of(place_of_group * group_rows, 16), group_rows)
        rows = rows_all[members].reshape(group_rows, model_width)
        gate = gate_column[span, :]
        grad = jnp.zeros((group_rows, model_width), F32)
        products = jnp.zeros((group_rows, part), F32)
        ahead = matmul(rows, up_all[0])
        for place in range(shards):
            hidden = ahead
            if place + 1 < shards:
                ahead = matmul(rows, up_all[place + 1])
            base = unscaled[place, span, :]
            activated, slope = gelu_parts(hidden)
            products = products + activated * base
            active[place, span, :] = activated.astype(BF16)
            low = (gate * base * slope).astype(BF16)
            grad_hidden[place, span, :] = low
            grad = grad + contract_last(low, up_all[place])
        grad_rows[members] = grad.astype(BF16).reshape(together * y_size, capacity, model_width)
        ones = jnp.ones((8, part), F32)
        for hop in range(together * y_size):
            grad_gates[place_of_group * together * y_size + hop] = lax.dot_general(
                ones, products[hop * capacity : (hop + 1) * capacity], (((1,), (1,)), ((), ())),
                precision=lax.Precision.HIGHEST, preferred_element_type=F32,
            )
        if last:
            for turn in turns:
                for hop in range(y_size):

                    @pl.when(turn + hop > 0)
                    def _(turn=turn, hop=hop):
                        for going, _ in give_back(turn, hop):
                            going.start()

        return carry

    lax.fori_loop(0, z_size // together, group, 0)
    if last:
        for copy in own_back:
            copy.start()

    rows_t[...] = turned(rows_all[...].reshape(count, model_width)).astype(BF16)
    total = refs.total[0] if refs.total else unscaled.at[0]
    total[...] = jnp.zeros(total.shape, F32)

    def up_target(targets, hop, place):
        if hop == 0:
            return targets[0].at[rows_of(place), :]
        return targets[1].at[hop - 1, rows_of(place), :]

    def keep_stores(place, slot):
        return [
            pltpu.make_async_copy(
                grad_up.at[slot, rows_of(hop), :], up_target(keep_up, hop, place),
                store_sem.at[slot, hop],
            )
            for hop in range(half)
        ]

    def give_stores(place, slot):
        return [
            pltpu.make_async_remote_copy(
                src_ref=grad_up.at[slot, rows_of(half + hop), :],
                dst_ref=up_target(taken_up, hop, place),
                send_sem=store_there.at[slot, hop], recv_sem=stored_here.at[place, hop],
                device_id=sibling, device_id_type=MESH,
            )
            for hop in range(half)
        ]

    def down_store(hop, slot):
        target = keep_down[0] if hop == 0 else keep_down[1].at[hop - 1]
        return pltpu.make_async_copy(grad_down.at[slot], target, store_sem.at[slot, half])

    def down_give(hop, slot):
        target = taken_down[0] if hop == 0 else taken_down[1].at[hop - 1]
        return pltpu.make_async_remote_copy(
            src_ref=grad_down.at[slot], dst_ref=target,
            send_sem=store_there.at[slot, half], recv_sem=stored_here.at[hop, half],
            device_id=sibling, device_id_type=MESH,
        )

    def each_down(place, slot, act):
        for hop in range(half):

            @pl.when(place == hop)
            def _(hop=hop):
                act(down_store(hop, slot), False)

            @pl.when(place == half + hop)
            def _(hop=hop):
                act(down_give(hop, slot), True)

    def start_store(place, slot):
        for copy in keep_stores(place, slot) + give_stores(place, slot):
            copy.start()
        each_down(place, slot, lambda copy, _: copy.start())

    def wait_store(place, slot):
        for copy in keep_stores(place, slot):
            copy.wait()
        for copy in give_stores(place, slot):
            copy.wait_send()
        each_down(place, slot, lambda copy, remote: copy.wait_send() if remote else copy.wait())

    def column(place, carry):
        slot = place % 2
        total[...] += matmul(active[place], down_all[place])

        @pl.when(place >= 2)
        def _():
            wait_store(place - 2, slot)

        grad_up[slot] = matmul(rows_t[...], grad_hidden[place]).astype(BF16)
        grad_down[slot] = matmul(slot_t[...], active[place]).T.astype(BF16)
        start_store(place, slot)
        return carry

    lax.fori_loop(0, shards, column, 0)

    rows_out = refs.rows_out[0]
    cot[...] = total[...].astype(BF16).reshape(blocks, capacity, model_width)
    out_copies = [pltpu.make_async_copy(cot, rows_out.at[:, index], load_sem.at[0])]
    for before in refs.outs_before:
        out_copies.append(
            pltpu.make_async_copy(before, rows_out.at[:, pl.ds(0, index)], load_sem.at[1])
        )
    for copy in out_copies:
        copy.start()
    for place in range(max(shards - 2, 0), shards):
        wait_store(place, place % 2)
    for place in range(shards):
        for copy in give_stores(place, 0):
            copy.wait_recv()
    for hop in range(half):
        down_give(hop, 0).wait_recv()
    if half > 1:
        for kept, taken, target, sem in (
            (keep_up[1], taken_up[1], refs.pass_up[0], 0),
            (keep_down[1], taken_down[1], refs.pass_down[0], 1),
        ):
            kept[...] = (kept[...].astype(F32) + taken[...].astype(F32)).astype(BF16)
            out_copies.append(pltpu.make_async_copy(kept, target, pass_sem.at[sem]))
            out_copies[-1].start()
    for copy in out_copies:
        copy.wait()
    for going, coming in cross_next:
        coming.wait_recv()
        going.wait_send()
    for going, _ in list(cross_down.values()) + cross_up:
        going.wait_send()
    if first:
        gates_out.wait()
        for turn, hop in steps[1:]:
            dispatch(turn, hop)[0].wait_send()
    work.finish()
    if last:
        for turn, hop in steps[1:]:
            for going, coming in give_back(turn, hop):
                coming.wait_recv()
                going.wait_send()
        for copy in own_back:
            copy.wait()


class Bag:
    def __init__(self, layout, refs):
        start = 0
        for name, size in layout.items():
            setattr(self, name, refs[start : start + size])
            start += size


class Wanted:
    def groups(self):
        return list(self.__dict__.values())

    def layout(self):
        return {name: len(group) for name, group in self.__dict__.items()}


def run_expert(index, local, outgoing, slot_gates, rows_in, gates, cotangent, ups, downs, swapped,
               next_mine, moved, outs_before, collective_id):
    grid = Grid()
    half = len(ups)
    shards = 2 * half
    first, last = index == 0, index == local - 1
    blocks, _, capacity, model_width = cotangent.shape
    part = downs[0].shape[0]
    count = blocks * capacity
    gate_lanes = slot_gates.shape[2]
    inputs, outputs, scratch = Wanted(), Wanted(), Wanted()
    inputs.cot_in = [(cotangent, ANYWHERE)]
    inputs.outgoing = [(outgoing, ANYWHERE)] if first else []
    inputs.gates_from = [(slot_gates, ANYWHERE)] if first else []
    inputs.rows_in = [] if first else [(rows_in, ANYWHERE)]
    if not first:
        inputs.gates = [(gates, IN_VMEM)]
    inputs.my_up = [(array, ANYWHERE) for array in ups]
    inputs.my_down = [(array, ANYWHERE) for array in downs]
    inputs.swapped_up = [(array, ANYWHERE) for array in swapped[:1]]
    inputs.swapped_down = [(array, ANYWHERE) for array in swapped[1:]]
    inputs.next_mine = [(array, ANYWHERE) for array in next_mine]
    inputs.moved_from = [(array, ANYWHERE) for array, _ in moved]
    inputs.outs_before = [] if outs_before is None else [(outs_before, IN_VMEM)]

    up_shape, down_shape = (model_width, part), (part, model_width)
    outputs.rows_out = [(shape_of((blocks, index + 1, capacity, model_width), BF16), ANYWHERE)]
    own_up, own_down = shape_of(up_shape, BF16), shape_of(down_shape, BF16)
    outputs.own = [(own_up, ANYWHERE), (own_up, ANYWHERE), (own_down, ANYWHERE), (own_down, ANYWHERE)]
    outputs.pass_up = [(shape_of((half - 1,) + up_shape, BF16), ANYWHERE)] if half > 1 else []
    outputs.pass_down = [(shape_of((half - 1,) + down_shape, BF16), ANYWHERE)] if half > 1 else []
    outputs.next_swapped = [(shape_of(array.shape, BF16), ANYWHERE) for array in next_mine]
    outputs.gates_to = [(shape_of(slot_gates.shape, F32), ANYWHERE)] if first else []
    outputs.moved_to = [
        (
            shape_of((grid.exp_size,) + array.shape[(1 if place is None else 2) :], array.dtype),
            ANYWHERE,
        )
        for array, place in moved
    ]
    rows_shape, gate_shape = (blocks, capacity, model_width), (blocks, 8, capacity)
    if last:
        outputs.back_rows = [(shape_of(rows_shape, BF16), ANYWHERE)]
        outputs.back_gates = [(shape_of(gate_shape, F32), ANYWHERE)]
    else:
        outputs.grad_rows = [(shape_of(rows_shape, BF16), IN_VMEM)]
        outputs.grad_gates = [(shape_of(gate_shape, F32), IN_VMEM)]

    sems = lambda *shape: pltpu.SemaphoreType.DMA(shape)
    scratch.rows_all = [pltpu.VMEM(rows_shape, BF16)]
    scratch.cot = [pltpu.VMEM(rows_shape, BF16)]
    scratch.up_all = [pltpu.VMEM((shards,) + up_shape, BF16)]
    scratch.down_all = [pltpu.VMEM((shards,) + down_shape, BF16)]
    scratch.active = [pltpu.VMEM((shards, count, part), BF16)]
    scratch.grad_hidden = [pltpu.VMEM((shards, count, part), BF16)]
    scratch.unscaled = [pltpu.VMEM((shards, count, part), F32)]
    if first:
        scratch.gates = [pltpu.VMEM(slot_gates.shape, F32)]
        scratch.gate_sem = [sems(1)]
        scratch.row_send = [sems(grid.z_size, grid.y_size)]
        scratch.row_receive = [sems(grid.z_size, grid.y_size)]
    if last:
        scratch.grad_rows = [pltpu.VMEM(rows_shape, BF16)]
        scratch.grad_gates = [pltpu.VMEM(gate_shape, F32)]
        scratch.back_send = [sems(2, grid.z_size, grid.y_size)]
        scratch.back_receive = [sems(2, grid.z_size, grid.y_size)]
    scratch.gate_column = [pltpu.VMEM((count, 1), F32)]
    scratch.rows_t = [pltpu.VMEM((model_width, count), BF16)]
    scratch.slot_t = [pltpu.VMEM((model_width, count), BF16)]
    scratch.total = [] if part == model_width else [pltpu.VMEM((count, model_width), F32)]
    scratch.grad_up = [pltpu.VMEM((2,) + up_shape, BF16)]
    scratch.grad_down = [pltpu.VMEM((2,) + down_shape, BF16)]
    far_up = [pltpu.VMEM((half - 1,) + up_shape, BF16)] * (1 if half > 1 else 0)
    far_down = [pltpu.VMEM((half - 1,) + down_shape, BF16)] * (1 if half > 1 else 0)
    scratch.far_keep_up, scratch.far_taken_up = far_up, far_up
    scratch.far_keep_down, scratch.far_taken_down = far_down, far_down
    scratch.load_sem = [sems(5)]
    scratch.pass_sem = [sems(2)]
    scratch.fetch_sem = [sems(2 * shards, half + 1)]
    scratch.store_sem = [sems(2, half + 1)]
    scratch.store_there = [sems(2, half + 1)]
    scratch.stored_here = [sems(shards, half + 1)]
    copies = (len(moved) + 1) * grid.exp_size + half * (shards + 1) + len(next_mine)
    scratch.send = [sems(copies)]
    scratch.receive = [sems(copies)]
    scratch.own_sem = [sems(max(len(moved), 1))]

    layout = {**inputs.layout(), **outputs.layout(), **scratch.layout()}

    def body(*refs):
        expert_kernel(
            *refs, layout=layout, index=index, local=local, half=half, capacity=capacity,
            parts=[place for _, place in moved],
        )

    results = pl.pallas_call(
        body,
        in_specs=[spec for group in inputs.groups() for _, spec in group],
        out_specs=tuple(spec for group in outputs.groups() for _, spec in group),
        out_shape=tuple(shape for group in outputs.groups() for shape, _ in group),
        scratch_shapes=[item for group in scratch.groups() for item in group],
        compiler_params=params(collective_id=collective_id, has_side_effects=True),
        cost_estimate=hint(45),
        name=f"expert_{index}",
    )(*[array for group in inputs.groups() for array, _ in group])
    return Bag(outputs.layout(), results)


def local_picks(routes, slots, capacity, local, index, slot_count):
    member, which = lax.div(routes, local), lax.rem(routes, local)
    places = jnp.where(which == index, member * capacity + slots, -1)
    lane = lax.broadcasted_iota(jnp.int32, (routes.shape[0], slot_count), 1)
    return [lane == places[:, k : k + 1] for k in range(2)]


def unroute_kernel(
    hidden, cotangent, routed, probabilities, gates, plane, columns, counts, *refs,
    experts, local, token_total, lanes,
):
    grads, gate_grads = refs[:local], refs[local : 2 * local]
    grad_hidden, grad_branch, small = refs[2 * local :]
    rows = hidden.shape[0]
    members, capacity, model_width = grads[0].shape
    grad_output = cotangent[...].astype(F32)
    grad_routed = jnp.zeros(hidden.shape, F32)
    found = [jnp.zeros((rows, capacity), F32), jnp.zeros((rows, capacity), F32)]
    routes, slots = int_columns(columns)
    member, which = lax.div(routes, local), lax.rem(routes, local)
    lane = lax.broadcasted_iota(jnp.int32, (rows, capacity), 1)
    for index in range(local):
        picks = local_picks(routes, slots, capacity, local, index, members * capacity)
        grad_routed = grad_routed + matmul(
            jnp.where(picks[0] | picks[1], 1.0, 0.0).astype(BF16),
            grads[index][...].reshape(members * capacity, model_width),
        )
        for place in range(members):
            spots = jnp.where((which == index) & (member == place), slots, -1)
            for k in range(2):
                found[k] = found[k] + jnp.where(
                    lane == spots[:, k : k + 1], gate_grads[index][place, 0:1, :], 0.0
                )
    grad_gates = [jnp.sum(found[k], axis=1, keepdims=True) for k in range(2)]
    powers = probabilities[...]
    lane = expert_lane(powers.shape, lanes)
    inside = (lane >= 0) & (lane < experts)
    picked = [lane == routes[:, k : k + 1] for k in range(2)]
    chosen_total = sum(
        jnp.sum(jnp.where(picked[k], powers, 0.0), axis=1, keepdims=True) for k in range(2)
    )
    weighted = grad_gates[0] * gates[:, 0:1] + grad_gates[1] * gates[:, 1:2]
    grad_mass = (AUX_WEIGHT * experts / (2.0 * token_total * token_total)) * counts[0:1, :]
    grad_mass = jnp.where(inside, grad_mass, 0.0)
    for k in range(2):
        grad_mass = grad_mass + jnp.where(picked[k], (grad_gates[k] - weighted) / chosen_total, 0.0)
    grad_logits = powers * (grad_mass - jnp.sum(powers * grad_mass, axis=1, keepdims=True))
    extra = plane[:, lanes.base :]
    grad_routed = grad_routed + contract_last(grad_logits.astype(BF16), extra)
    hidden_state = hidden[...]
    scale = lax.rsqrt(jnp.mean(hidden_state * hidden_state, axis=1, keepdims=True) + EPSILON)
    normed = hidden_state * scale
    product = grad_routed * normed
    gain_grad = jnp.sum(product, axis=0, keepdims=True)
    small_t = matmul(grad_logits.T.astype(BF16), routed[...])
    row = lax.broadcasted_iota(jnp.int32, small_t.shape, 0)
    small_t = jnp.where(row == lanes.gain, gain_grad, small_t)
    small[...] = small_t.T
    gains = extra.astype(F32).T[lanes.gain : lanes.gain + 1]
    grad = scale * (
        grad_routed * gains - normed * jnp.mean(product * gains, axis=1, keepdims=True)
    ) + grad_output
    grad_hidden[...] = grad
    grad_branch[...] = grad.astype(BF16)


def context_grad_kernel(
    fsdp_index, grad_branch, attention_out, context, grad_t, grad_n, grad_out, total, *, heads, width
):
    @pl.when(pl.program_id(0) == 0)
    def _():
        total[...] = jnp.zeros_like(total)

    branch = grad_branch[0]
    grad = contract_last(attention_out[...], branch).astype(BF16)
    for head in range(heads):
        part = grad[head * width : (head + 1) * width]
        grad_t[head] = part
        grad_n[head] = turned(part).astype(BF16)
    total[...] += matmul(context[0], branch)

    @pl.when(pl.program_id(0) == pl.num_programs(0) - 1)
    def _():
        grad_out[...] = total[...].astype(BF16)


def project_back_kernel(
    grad_projected, normed, plane, small, probabilities, grad_bias, grad_first, grad_plane, total,
    bias_t, *, lanes, heads, feature_rows, bucket_rows,
):
    step = pl.program_id(0)

    @pl.when(step == 0)
    def _():
        total[...] = jnp.zeros_like(total)

    grad = grad_projected[...]
    grad_first[0] = matmul(plane[:, : lanes.weights], grad).astype(BF16)
    total[: lanes.weights, :] += matmul(grad, normed[...])

    @pl.when(step == pl.num_programs(0) - 1)
    def _():
        grad_plane[...] = total[...].T.astype(BF16)
        span = grad_bias.shape[2]
        select, _ = bucket_rows_select(plane.shape[0], feature_rows, bucket_rows, span)
        bias_t[...] = jnp.zeros_like(bias_t)
        first = lanes.table + lax.axis_index("fsdp") * heads
        for head in range(heads):
            bias_t[pl.ds(first + head, 1), :] = grad_bias[head]
        high = bias_t[...].astype(BF16)
        rest = (bias_t[...] - high.astype(F32)).astype(BF16)
        table = contract_last(select, high) + contract_last(select, rest)
        mass = jnp.sum(probabilities[...], axis=0, keepdims=True)
        mass = pltpu.roll(jnp.broadcast_to(mass, (8, lanes.extra)), lanes.shift, 1)[0:1]
        lane = lax.broadcasted_iota(jnp.int32, table.shape, 1)
        row = lax.broadcasted_iota(jnp.int32, table.shape, 0)
        is_small = (lane >= lanes.router) & (lane < lanes.table)
        is_mass = (lane >= lanes.count) & (lax.rem(row, feature_rows) == 0)
        extra = table + jnp.where(is_small, small[...], 0.0) + jnp.where(is_mass, mass, 0.0)
        grad_plane[:, lanes.base :] = (total[lanes.base :, :].T + extra).astype(BF16)


def last_kernel(
    first, planes, out_grad, first_parts, plane_parts, out_parts,
    first_in, first_sum, planes_in, plane_sum, send, receive, own, *, spread_out,
):
    grid = Grid().here()
    links = Links(send, receive)
    z_size, y_size, x_size, fsdp_size = grid.z_size, grid.y_size, grid.x_size, grid.fsdp_size
    exp_size = grid.exp_size
    sibling = grid.sibling(grid.fsdp)
    near = [
        grid.at(z=(grid.z + hop) % z_size, fsdp=(grid.fsdp + turn) % fsdp_size)
        for hop in range(z_size)
        for turn in range(fsdp_size)
        if hop or turn
    ]
    beside = [grid.at(y=(grid.y + hop) % y_size) for hop in range(1, y_size)]

    per_sender = grid.device_count if spread_out else exp_size
    base = 0 if spread_out else grid.fsdp * exp_size
    out_sends = []
    for number in range(per_sender):
        to = base + number
        out_sends.append((to, number))
    if spread_out:
        out_origins = [(origin, origin) for origin in range(grid.device_count)]
    else:
        out_origins = [
            (member * fsdp_size + grid.linear // exp_size, member) for member in range(exp_size)
        ]
    own_slot = grid.linear if spread_out else grid.exp
    out_base = links.used
    links.used += per_sender

    def place_of(linear):
        return (linear // fsdp_size, linear % fsdp_size)

    def out_copy(to, number, slot):
        return pltpu.make_async_remote_copy(
            src_ref=out_grad.at[number], dst_ref=out_parts.at[slot],
            send_sem=send.at[out_base + number], recv_sem=receive.at[out_base + slot],
            device_id=place_of(to), device_id_type=MESH,
        )

    barrier = pltpu.get_barrier_semaphore()
    for device in near + beside:
        pl.semaphore_signal(barrier, inc=1, device_id=device, device_id_type=MESH)
    for origin, _ in out_origins:

        @pl.when(origin != grid.linear)
        def _(origin=origin):
            pl.semaphore_signal(
                barrier, inc=1, device_id=place_of(origin), device_id_type=MESH
            )

    to_self = (
        1 if spread_out else jnp.where(grid.linear // exp_size == grid.fsdp, 1, 0)
    )
    pl.semaphore_wait(barrier, len(near) + len(beside) + per_sender - to_self)

    first_copies = []
    for hop in range(x_size):
        mine = grid.x_from(hop)
        first_copies.append(
            links.copy(
                first.at[grid.sibling(mine)], first_in.at[hop], (grid.exp, sibling), first_in.at[hop]
            )
        )
        first_copies[-1][0].start()
    beside_copies = []
    for hop in range(1, y_size):
        to = (grid.y + hop) % y_size
        beside_copies.append(
            links.copy(
                planes.at[:, to], planes_in.at[hop - 1], grid.at(y=to), planes_in.at[hop - 1]
            )
        )
        beside_copies[-1][0].start()
    for to, number in out_sends:

        @pl.when(to != grid.linear)
        def _(to=to, number=number):
            out_copy(to, number, own_slot).start()

        @pl.when(to == grid.linear)
        def _(number=number):
            pltpu.make_async_copy(out_grad.at[number], out_parts.at[own_slot], own.at[0]).start()

    along_x = []
    for hop in range(x_size):
        first_copies[hop][1].wait_recv()
        summed = first[grid.x_from(hop)].astype(F32) + first_in[hop].astype(F32)
        if hop == 0:
            first_parts[0] = summed.astype(BF16)
        else:
            first_sum[hop - 1] = summed.astype(BF16)
            along_x.append(
                links.copy(
                    first_sum.at[hop - 1], first_parts.at[hop], (grid.exp, grid.x_from(hop)),
                    first_parts.at[hop],
                )
            )
            along_x[-1][0].start()
    for going, coming in beside_copies:
        coming.wait_recv()
    along_z = []
    for hop in list(range(1, z_size)) + [0]:
        to_z = (grid.z + hop) % z_size
        summed = planes[to_z, grid.y].astype(F32)
        for other in range(y_size - 1):
            summed = summed + planes_in[other, to_z].astype(F32)
        plane_sum[hop] = summed.astype(BF16)
        for turn in range(fsdp_size):
            if hop == 0 and turn == 0:
                continue
            to = (grid.fsdp + turn) % fsdp_size
            origin = (grid.fsdp + fsdp_size - turn) % fsdp_size
            along_z.append(
                links.copy(
                    plane_sum.at[hop, to],
                    plane_parts.at[hop, grid.fsdp],
                    grid.at(z=to_z, fsdp=to),
                    plane_parts.at[hop, origin],
                )
            )
            along_z[-1][0].start()
    kept = pltpu.make_async_copy(
        plane_sum.at[0, grid.fsdp], plane_parts.at[0, grid.fsdp], own.at[1]
    )
    kept.start()
    for going, coming in along_x + along_z:
        coming.wait_recv()
    for going, _ in first_copies + beside_copies + along_x + along_z:
        going.wait_send()
    kept.wait()
    for origin, slot in out_origins:

        @pl.when(origin != grid.linear)
        def _(origin=origin, slot=slot):
            out_copy(origin, 0, slot).wait_recv()

    for to, number in out_sends:

        @pl.when(to != grid.linear)
        def _(to=to, number=number):
            out_copy(to, number, own_slot).wait_send()

        @pl.when(to == grid.linear)
        def _(number=number):
            pltpu.make_async_copy(out_grad.at[number], out_parts.at[own_slot], own.at[0]).wait()


def mixture_kernel(hidden, gates, columns, rows_in, output, *, local):
    members, _, capacity, model_width = rows_in.shape
    routes, slots = int_columns(columns)
    total = hidden[...]
    picked = [jnp.zeros(hidden.shape, F32), jnp.zeros(hidden.shape, F32)]
    for index in range(local):
        picks = local_picks(routes, slots, capacity, local, index, members * capacity)
        values = rows_in[:, index].reshape(members * capacity, model_width)
        for k in range(2):
            picked[k] = picked[k] + matmul(jnp.where(picks[k], 1.0, 0.0).astype(BF16), values)
    for k in range(2):
        total = total + gates[:, k : k + 1] * picked[k]
    output[...] = total.astype(BF16)


def finish_kernel(
    first_parts, plane_parts, out_parts, tokens, grad_hidden, attention_in, attention_gain, counts,
    grad_tokens, grad_gain, grad_in, grad_out, grad_mixture, grad_router, grad_table, balance,
    *, lanes, heads, width, head_count, experts, token_total,
):
    total = jnp.sum(first_parts[...].astype(F32), axis=0).T
    inputs = tokens[...].astype(F32)
    scale = lax.rsqrt(jnp.mean(inputs * inputs, axis=1, keepdims=True) + EPSILON)
    normed = inputs * scale
    grad_tokens[...] = grad_hidden[...] + scale * (
        total - normed * jnp.mean(total * normed, axis=1, keepdims=True)
    )
    fsdp_size = plane_parts.shape[1]
    model_width = head_count * width
    summed = jnp.sum(plane_parts[...].astype(F32), axis=0)
    sums = [summed[place] for place in range(fsdp_size)]
    columns = []
    for kind in range(3):
        pieces = [
            sums[place][:, kind * heads * width : (kind + 1) * heads * width]
            for place in range(fsdp_size)
        ]
        columns.append(jnp.concatenate(pieces, axis=1)[:, :model_width])
    gathered = jnp.concatenate(columns, axis=1)
    feature_rows = gathered.shape[0]
    gain = jnp.sum(gathered * attention_in[...].astype(F32), axis=1, keepdims=True)
    gain = padded_rows(jnp.broadcast_to(gain, (feature_rows, 128)), 128).T
    grad_gain[...] = gain[0:1, :feature_rows]
    grad_in[...] = gathered * as_column(attention_gain[...], feature_rows)
    grad_out[...] = jnp.sum(out_parts[...].astype(F32), axis=0)
    extra = sum(part[:, lanes.base :] for part in sums)
    extra_t = padded_rows(extra, 128).T
    grad_mixture[...] = extra_t[lanes.gain : lanes.gain + 1, :feature_rows]
    grad_router[...] = extra_t[lanes.router : lanes.router + experts, :feature_rows]
    grad_table[...] = extra[: grad_table.shape[0], lanes.table : lanes.table + head_count]
    mass = jnp.broadcast_to(extra[0:1], (8, lanes.extra))
    mass = pltpu.roll(mass, lanes.extra - lanes.shift, 1)
    lane = expert_lane(mass.shape, lanes)
    terms = jnp.where((lane >= 0) & (lane < experts), mass * counts[...], 0.0)[0:1]
    balance[...] = jnp.sum(terms, axis=1, keepdims=True) * (
        experts / (2.0 * token_total * token_total)
    )


def sum_kernel(*refs, local, terms):
    outputs = refs[2 * local * terms :]
    for which in range(2):
        for index in range(local):
            first = (index * 2 + which) * terms
            shape = outputs[which].shape[1:]
            total = refs[first][...].reshape(shape).astype(F32)
            for ref in refs[first + 1 : first + terms]:
                total = total + ref[...].reshape(shape).astype(F32)
            outputs[which][index] = total


def sum_grads(groups, up_shape, down_shape, blocks):
    local = len(groups)
    depth, part = up_shape[1], down_shape[1]
    sizes = ((depth, part), (part // blocks, down_shape[2]))
    arrays, specs = [], []
    for group in groups:
        for size, (keep, taken, passed) in zip(sizes, group):
            for array in (keep, taken, *passed):
                arrays.append(array)
                specs.append(pl.BlockSpec(size, lambda c: (c, 0)))
    return pl.pallas_call(
        partial(sum_kernel, local=local, terms=len(arrays) // (2 * local)),
        grid=(blocks,),
        in_specs=specs,
        out_specs=[
            pl.BlockSpec((local, depth, part), lambda c: (0, 0, c)),
            pl.BlockSpec((local, part // blocks, down_shape[2]), lambda c: (0, c, 0)),
        ],
        out_shape=(shape_of(up_shape, F32), shape_of(down_shape, F32)),
        compiler_params=params(),
        cost_estimate=hint(8),
        name="sum_grads",
    )(*arrays)


def over_x(array, hop):
    fsdp_size = lax.axis_size("fsdp")
    return lax.ppermute(array, "fsdp", [(i, (i + 2 * hop) % fsdp_size) for i in range(fsdp_size)])


def over_core(array):
    return lax.ppermute(array, "fsdp", [(i, i ^ 1) for i in range(lax.axis_size("fsdp"))])


def on_device(
    tokens,
    cotangent,
    segments,
    routes,
    slots,
    attention_gain,
    mixture_gain,
    attention_in,
    attention_out,
    router_weight,
    position_table,
    expert_up,
    expert_down,
):
    grid = Grid()
    exp_size, fsdp_size, chips = grid.exp_size, grid.fsdp_size, grid.x_size
    device_count = grid.device_count
    fsdp_index = lax.axis_index("fsdp")
    rows, model_width = tokens.shape
    length = rows * fsdp_size
    head_count = position_table.shape[1]
    width = model_width // head_count
    heads = -(-head_count // fsdp_size)
    padded_heads = heads * fsdp_size
    feature_rows, bucket_rows = attention_in.shape[0], position_table.shape[0]
    experts = router_weight.shape[1]
    local = expert_up.shape[0]
    capacity = 4 * rows // experts
    token_total = rows * device_count
    span = WINDOW + 2 * SKEW + QUERY_BLOCK
    lanes = Lanes(heads, width, padded_heads, experts)
    part = expert_down.shape[1]
    gain_row = attention_gain.reshape(1, feature_rows)

    shard_shapes = [shape_of((model_width, part), BF16), shape_of((part, model_width), BF16)]
    copies = (
        2 * fsdp_size + grid.z_size * fsdp_size + grid.z_size * grid.y_size
        + grid.z_size + grid.y_size + grid.x_size + 1
    )
    started = pl.pallas_call(
        partial(
            start_kernel, lanes=lanes, heads=heads, width=width, head_count=head_count,
            experts=experts, capacity=capacity, local=local,
        ),
        out_shape=tuple(
            [
                shape_of((fsdp_size, rows, model_width), BF16),
                shape_of((grid.z_size, grid.y_size, fsdp_size, feature_rows, lanes.width), BF16),
                shape_of((experts * capacity, model_width), BF16),
                shape_of((8, rows), F32),
                shape_of((rows, 128), F32),
                shape_of((grid.z_size, grid.y_size, chips, 2, feature_rows, model_width), BF16),
            ]
            + shard_shapes * local
        ),
        in_specs=[IN_VMEM] * 10 + [ANYWHERE] * 2,
        out_specs=tuple(
            [ANYWHERE, ANYWHERE, IN_VMEM, IN_VMEM, IN_VMEM, ANYWHERE] + [ANYWHERE] * (2 * local)
        ),
        scratch_shapes=[
            pltpu.VMEM((fsdp_size, feature_rows, lanes.width), BF16),
            pltpu.VMEM(expert_up.shape, BF16),
            pltpu.VMEM(expert_down.shape, BF16),
            dma_sems(copies),
            dma_sems(copies),
            dma_sems(3),
            dma_sems(2 * local),
            dma_sems(local * (fsdp_size + 1)),
        ],
        compiler_params=params(collective_id=0, has_side_effects=True),
        cost_estimate=hint(20),
        name="start",
    )(
        tokens, cotangent, routes.T, slots.T, gain_row, mixture_gain.reshape(1, feature_rows),
        attention_in, router_weight.T, position_table, attention_out, expert_up, expert_down,
    )
    all_tokens, all_planes, cotangent_slots, position_rows, columns, full_out = started[:6]
    own_shards = [started[6 + 2 * index : 8 + 2 * index] for index in range(local)]
    plane = all_planes.reshape(model_width, lanes.width)
    full_out = full_out.reshape(model_width, model_width)

    def along_x(array):
        return [over_x(array, -hop) for hop in range(1, chips)]

    near_up, near_down = [None] * local, [None] * local
    near_up[0] = along_x(own_shards[0][0])
    cotangent_in = lax.all_to_all(
        cotangent_slots.reshape(exp_size, local * capacity, model_width),
        "exp", split_axis=0, concat_axis=0, tiled=True,
    ).reshape(exp_size, local, capacity, model_width)

    head_t = lambda size: pl.BlockSpec((heads, size, rows), lambda s, *_: (0, 0, s))
    head_n = lambda size: pl.BlockSpec((heads, rows, size), lambda s, *_: (0, s, 0))
    normed, query_t, key_n, query_n, value_n, key_t, value_t, bias, counts = pl.pallas_call(
        partial(
            project_kernel, heads=heads, width=width, lanes=lanes, feature_rows=feature_rows,
            bucket_rows=bucket_rows,
        ),
        grid=(fsdp_size,),
        in_specs=[
            pl.BlockSpec((1, rows, model_width), lambda s: (s, 0, 0)),
            whole((model_width, lanes.width)),
            pl.BlockSpec((1, rows), lambda s: (0, s)),
        ],
        out_specs=[
            pl.BlockSpec((rows, model_width), lambda s: (s, 0)),
            head_t(SKEW), head_n(SKEW), head_n(width), head_n(width), head_t(width), head_t(width),
            whole((heads, 1, span)),
            whole((8, lanes.extra)),
        ],
        out_shape=(
            shape_of((length, model_width), BF16),
            shape_of((heads, SKEW, length), BF16),
            shape_of((heads, length, SKEW), BF16),
            shape_of((heads, length, width), BF16),
            shape_of((heads, length, width), BF16),
            shape_of((heads, width, length), BF16),
            shape_of((heads, width, length), BF16),
            shape_of((heads, 1, span), F32),
            shape_of((8, lanes.extra), F32),
        ),
        scratch_shapes=[
            pltpu.VMEM((lanes.weights, model_width), BF16),
            pltpu.VMEM((lanes.extra, span), F32),
        ],
        compiler_params=params(),
        cost_estimate=hint(8),
        name="project",
    )(all_tokens, plane, segments.reshape(1, length))

    by_head = lambda *size: pl.BlockSpec((1,) + size, lambda h: (h, 0, 0))
    context, context_high, log_total = pl.pallas_call(
        partial(attend_kernel, rows=rows),
        grid=(heads,),
        in_specs=[
            by_head(SKEW, length), by_head(length, SKEW), by_head(width, length), by_head(1, span),
        ],
        out_specs=[
            pl.BlockSpec((fsdp_size, width, rows), lambda h: (0, h, 0)),
            by_head(width, length),
            by_head(1, length),
        ],
        out_shape=(
            shape_of((fsdp_size, heads * width, rows), BF16),
            shape_of((heads, width, length), F32),
            shape_of((heads, 1, length), F32),
        ),
        scratch_shapes=[
            pltpu.VMEM((SKEW, span), F32),
            pltpu.VMEM((WINDOW + QUERY_BLOCK, QUERY_BLOCK), F32),
        ],
        compiler_params=params(),
        cost_estimate=hint(13),
        name="attend",
    )(query_t, key_n, value_t, bias)

    (attended_t,) = exchange("fsdp", [(context, None)], 1, 9)
    own_down, near_up[0], attended_t = lax.optimization_barrier(
        (own_shards[0][1], near_up[0], attended_t)
    )
    near_down[0] = along_x(own_down)
    attended_t = attended_t.reshape(padded_heads * width, rows)

    gate_lanes = -(-local * capacity // 128) * 128
    hidden, routed, probabilities, gates, outgoing, slot_gates = pl.pallas_call(
        partial(route_kernel, experts=experts, lanes=lanes, capacity=capacity),
        out_shape=(
            shape_of((rows, model_width), F32),
            shape_of((rows, model_width), BF16),
            shape_of((rows, lanes.extra), F32),
            shape_of((rows, 2), F32),
            shape_of((experts * capacity, model_width), BF16),
            shape_of((exp_size, 8, gate_lanes), F32),
        ),
        compiler_params=params(),
        cost_estimate=hint(7),
        name="route",
    )(tokens, attended_t, full_out, plane, columns, position_rows)

    later = [own_shards[index] for index in range(1, local)]
    outgoing, later = lax.optimization_barrier((outgoing, later))
    for index in range(1, local):
        near_up[index], near_down[index] = [along_x(array) for array in later[index - 1]]
    outgoing = outgoing.reshape(exp_size, local, capacity, model_width)

    def pass_along(arrays):
        return [over_x(arrays[0][hop - 1], hop) for hop in range(1, chips)]

    returned, groups, moved, outs, rows_in, gates_in, swapped = [], [], [], None, None, None, ()
    for index in range(local):
        final = index == local - 1
        carried = list(moved) if final else list(moved) + [(outgoing, index + 1)]
        result = run_expert(
            index, local, outgoing, slot_gates, rows_in, gates_in, cotangent_in,
            [own_shards[index][0]] + near_up[index], [own_shards[index][1]] + near_down[index],
            swapped, () if final else own_shards[index + 1], carried, outs, 3 + index,
        )
        (outs,) = result.rows_out
        if index == 0:
            (gates_in,) = result.gates_to
        arrived = list(result.moved_to)
        if not final:
            rows_in = arrived.pop()
            swapped = result.next_swapped
            moved = [(result.grad_rows[0], None), (result.grad_gates[0], None)]
        if arrived:
            returned.append(arrived)
        up_keep, up_taken, down_keep, down_taken = result.own
        if not final:
            passed = (result.pass_up, result.pass_down)
            passed, rows_in = lax.optimization_barrier((passed, rows_in))
            groups.append(
                [
                    (up_keep, up_taken, pass_along(passed[0])),
                    (down_keep, down_taken, pass_along(passed[1])),
                ]
            )
    returned.append([result.back_rows[0], result.back_gates[0]])
    groups, returned = lax.optimization_barrier((groups, returned))

    outs, returned = lax.optimization_barrier((outs, returned))
    out_rows = lax.all_to_all(outs, "exp", split_axis=0, concat_axis=0, tiled=True)

    grad_hidden, grad_branch, small = pl.pallas_call(
        partial(
            unroute_kernel, experts=experts, local=local, token_total=token_total, lanes=lanes
        ),
        out_shape=(
            shape_of((rows, model_width), F32),
            shape_of((rows, model_width), BF16),
            shape_of((model_width, lanes.extra), F32),
        ),
        compiler_params=params(),
        cost_estimate=hint(1),
        name="unroute",
    )(
        hidden, cotangent, routed, probabilities, gates, plane, columns, counts,
        *[part[0] for part in returned], *[part[1] for part in returned],
    )

    all_branch = gather_rows(grad_branch, 4 + local, 1)
    passed, all_branch = lax.optimization_barrier(((result.pass_up, result.pass_down), all_branch))
    groups.append(
        [
            (up_keep, up_taken, pass_along(passed[0])),
            (down_keep, down_taken, pass_along(passed[1])),
        ]
    )
    padded_out = full_out
    if padded_heads > head_count:
        padded_out = jnp.pad(full_out, ((0, padded_heads * width - model_width), (0, 0)))
    grad_t, grad_n, out_grad = pl.pallas_call(
        partial(context_grad_kernel, heads=heads, width=width),
        grid_spec=pltpu.PrefetchScalarGridSpec(
            num_scalar_prefetch=1,
            grid=(fsdp_size,),
            in_specs=[
                pl.BlockSpec((1, rows, model_width), lambda s, f: (s, 0, 0)),
                pl.BlockSpec((heads * width, model_width), lambda s, f: (f[0], 0)),
                pl.BlockSpec((1, heads * width, rows), lambda s, f: (s, 0, 0)),
            ],
            out_specs=[head_t(width), head_n(width), whole((heads * width, model_width))],
            scratch_shapes=[pltpu.VMEM((heads * width, model_width), F32)],
        ),
        out_shape=(
            shape_of((heads, width, length), BF16),
            shape_of((heads, length, width), BF16),
            shape_of((heads * width, model_width), BF16),
        ),
        compiler_params=params(),
        cost_estimate=hint(1),
        name="context_grad",
    )(fsdp_index.reshape(1), all_branch, padded_out, context)

    grad_projected, grad_bias = pl.pallas_call(
        partial(attend_back_kernel, scale=width ** (-0.5)),
        grid=(heads,),
        in_specs=[
            by_head(SKEW, length), by_head(length, SKEW), by_head(length, width),
            by_head(length, width), by_head(width, length), by_head(width, length),
            by_head(length, width), by_head(width, length), by_head(1, length), by_head(1, span),
        ],
        out_specs=[
            pl.BlockSpec((3, 1, width, length), lambda h: (0, h, 0, 0)),
            by_head(1, span),
        ],
        out_shape=(
            shape_of((3, heads, width, length), BF16),
            shape_of((heads, 1, span), F32),
        ),
        scratch_shapes=[
            pltpu.VMEM((SKEW, span), F32),
            pltpu.VMEM((SKEW, span), F32),
            pltpu.VMEM((length, width), F32),
            pltpu.VMEM((length, width), F32),
        ],
        compiler_params=params(),
        cost_estimate=hint(1),
        name="attend_back",
    )(query_t, key_n, query_n, value_n, key_t, grad_t, grad_n, context_high, log_total, bias)
    grad_projected = grad_projected.reshape(lanes.weights, length)

    grad_first, grad_plane = pl.pallas_call(
        partial(
            project_back_kernel, lanes=lanes, heads=heads, feature_rows=feature_rows,
            bucket_rows=bucket_rows,
        ),
        grid=(fsdp_size,),
        in_specs=[
            pl.BlockSpec((lanes.weights, rows), lambda s: (0, s)),
            pl.BlockSpec((rows, model_width), lambda s: (s, 0)),
            whole((model_width, lanes.width)),
            whole((model_width, lanes.extra)),
            whole((rows, lanes.extra)),
            whole((heads, 1, span)),
        ],
        out_specs=[
            pl.BlockSpec((1, model_width, rows), lambda s: (s, 0, 0)),
            whole((model_width, lanes.width)),
        ],
        out_shape=(
            shape_of((fsdp_size, model_width, rows), BF16),
            shape_of((model_width, lanes.width), BF16),
        ),
        scratch_shapes=[
            pltpu.VMEM((lanes.width, model_width), F32),
            pltpu.VMEM((lanes.extra, span), F32),
        ],
        compiler_params=params(),
        cost_estimate=hint(1),
        name="project_back",
    )(grad_projected, normed, plane, small, probabilities, grad_bias)

    out_rows, groups, grad_first = lax.optimization_barrier((out_rows, groups, grad_first))
    spread_out = heads * width * fsdp_size != model_width
    if spread_out:
        out_grad = lax.dynamic_update_slice(
            jnp.zeros((padded_heads * width, model_width), BF16), out_grad,
            (fsdp_index * heads * width, jnp.int32(0)),
        )[:model_width]
    out_grad = out_grad.reshape(-1, feature_rows, model_width)
    out_count = device_count if spread_out else exp_size
    plane_shape = (grid.z_size, grid.y_size, fsdp_size, feature_rows, lanes.width)
    parts_shape = (grid.z_size, fsdp_size, feature_rows, lanes.width)
    copies = 2 * fsdp_size + grid.z_size * fsdp_size + grid.y_size + out_count
    first_parts, plane_parts, out_parts = pl.pallas_call(
        partial(last_kernel, spread_out=spread_out),
        out_shape=(
            shape_of((chips, model_width, rows), BF16),
            shape_of(parts_shape, BF16),
            shape_of((out_count, feature_rows, model_width), BF16),
        ),
        in_specs=[IN_VMEM] * 3,
        out_specs=(IN_VMEM, ANYWHERE, ANYWHERE),
        scratch_shapes=[
            pltpu.VMEM((chips, model_width, rows), BF16),
            pltpu.VMEM((max(chips - 1, 1), model_width, rows), BF16),
            pltpu.VMEM((max(grid.y_size - 1, 1),) + parts_shape, BF16),
            pltpu.VMEM(parts_shape, BF16),
            dma_sems(copies),
            dma_sems(copies),
            dma_sems(2),
        ],
        compiler_params=params(collective_id=5 + local, has_side_effects=True),
        cost_estimate=hint(30),
        name="last",
    )(grad_first, grad_plane.reshape(plane_shape), out_grad)

    (
        grad_tokens, gain_grad, in_grad, out_sum, mixture_gain_grad, router_grad, table_grad, balance,
    ) = pl.pallas_call(
        partial(
            finish_kernel, lanes=lanes, heads=heads, width=width, head_count=head_count,
            experts=experts, token_total=token_total,
        ),
        out_shape=(
            shape_of((rows, model_width), F32),
            shape_of((1, feature_rows), F32),
            shape_of((feature_rows, 3 * model_width), F32),
            shape_of((feature_rows, model_width), F32),
            shape_of((1, feature_rows), F32),
            shape_of((experts, feature_rows), F32),
            shape_of((bucket_rows, head_count), F32),
            shape_of((1, 1), F32),
        ),
        compiler_params=params(),
        cost_estimate=hint(6),
        name="finish",
    )(first_parts, plane_parts, out_parts, tokens, grad_hidden, attention_in, gain_row, counts)

    layer_output = pl.pallas_call(
        partial(mixture_kernel, local=local),
        out_shape=shape_of((rows, model_width), BF16),
        compiler_params=params(),
        cost_estimate=hint(5),
        name="mixture",
    )(hidden, gates, columns, out_rows)

    up_grad, down_grad = sum_grads(groups, expert_up.shape, expert_down.shape, fsdp_size)
    return (
        layer_output,
        balance.reshape(()),
        grad_tokens,
        gain_grad.reshape(feature_rows),
        mixture_gain_grad.reshape(feature_rows),
        in_grad,
        out_sum,
        router_grad.T,
        table_grad,
        up_grad,
        down_grad,
    )


def solution(mesh):
    in_specs = (
        P(("exp", "fsdp"), None),
        P(("exp", "fsdp"), None),
        P("exp"),
        P(("exp", "fsdp"), None),
        P(("exp", "fsdp"), None),
        P(("exp", "fsdp")),
        P(("exp", "fsdp")),
        P(("exp", "fsdp"), None),
        P(("exp", "fsdp"), None),
        P(("exp", "fsdp"), None),
        P(("exp", "fsdp"), None),
        P("exp", "fsdp", None),
        P("exp", "fsdp", None),
    )
    out_specs = (
        P(("exp", "fsdp"), None),
        P(),
        P(("exp", "fsdp"), None),
        P(("exp", "fsdp")),
        P(("exp", "fsdp")),
        P(("exp", "fsdp"), None),
        P(("exp", "fsdp"), None),
        P(("exp", "fsdp"), None),
        P(("exp", "fsdp"), None),
        P("exp", "fsdp", None),
        P("exp", "fsdp", None),
    )
    return jax.shard_map(
        on_device, mesh=mesh, in_specs=in_specs, out_specs=out_specs, check_vma=False
    )
```

```python
from functools import partial

import jax
import jax.numpy as jnp
from jax import lax
from jax.experimental import pallas as pl
from jax.experimental.pallas import tpu as pltpu
from jax.sharding import PartitionSpec as P

WINDOW = 1024
BUCKETS = 256

EPSILON = 1e-06
AUX_WEIGHT = 0.01
MASKED = -1e30
QUERY_BLOCK = 256
SKEW = 128
VMEM_BYTES = 58 * 1024 * 1024
MESH = pl.DeviceIdType.MESH
F32 = jnp.float32
BF16 = jnp.bfloat16


def params(**kwargs):
    return pltpu.CompilerParams(vmem_limit_bytes=VMEM_BYTES, **kwargs)


def shape_of(shape, dtype):
    return jax.ShapeDtypeStruct(shape, dtype)


def whole(shape):
    return pl.BlockSpec(shape, lambda *_: (0,) * len(shape))


def contract_last(left_side, right_side):
    return lax.dot_general(
        left_side, right_side, (((1,), (1,)), ((), ())), preferred_element_type=F32
    )


def matmul(left_side, right_side):
    return jnp.dot(left_side, right_side, preferred_element_type=F32)


def turned(value):
    return value.astype(F32).T


def bucket_index(distance):
    near_count = BUCKETS // 2
    spread = max(WINDOW - near_count, 1)
    far_bucket = (
        near_count + jnp.maximum(distance - near_count, 0) * (BUCKETS - near_count) // spread
    )
    return jnp.where(distance < near_count, distance, far_bucket)

def hint(micros):
    return pl.CostEstimate(flops=int(micros * 1.0e9), bytes_accessed=1024, transcendentals=0)


class Grid:
    def __init__(self):
        self.exp_size, self.fsdp_size = lax.axis_size("exp"), lax.axis_size("fsdp")
        self.device_count = self.exp_size * self.fsdp_size
        self.y_size = max(
            y for y in range(1, self.exp_size + 1) if self.exp_size % y == 0 and 2 * y * y <= self.exp_size
        ) if self.exp_size > 1 else 1
        self.z_size = self.exp_size // self.y_size
        self.x_size = self.fsdp_size // 2

    def here(self):
        self.exp, self.fsdp = lax.axis_index("exp"), lax.axis_index("fsdp")
        self.z, self.y = self.exp // self.y_size, self.exp % self.y_size
        self.x, self.core = self.fsdp // 2, self.fsdp % 2
        self.linear = self.exp * self.fsdp_size + self.fsdp
        return self

    def at(self, z=None, y=None, fsdp=None):
        z = self.z if z is None else z
        y = self.y if y is None else y
        return (z * self.y_size + y, self.fsdp if fsdp is None else fsdp)

    def x_from(self, hop):
        return ((self.x + self.x_size + hop) % self.x_size) * 2 + self.core

    def sibling(self, fsdp):
        return fsdp + 1 - 2 * (fsdp % 2)


class Links:
    def __init__(self, send, receive):
        self.send, self.receive, self.used = send, receive, 0

    def copy(self, source, target, device, landing):
        index = self.used
        self.used += 1
        going = pltpu.make_async_remote_copy(
            src_ref=source, dst_ref=target, send_sem=self.send.at[index],
            recv_sem=self.receive.at[index], device_id=device, device_id_type=MESH,
        )
        coming = pltpu.make_async_remote_copy(
            src_ref=landing, dst_ref=landing, send_sem=self.send.at[index],
            recv_sem=self.receive.at[index], device_id=device, device_id_type=MESH,
        )
        return going, coming


def greet(devices):
    barrier = pltpu.get_barrier_semaphore()
    for device in devices:
        pl.semaphore_signal(barrier, inc=1, device_id=device, device_id_type=MESH)
    pl.semaphore_wait(barrier, len(devices))


def chip_peers(grid):
    peers = [(grid.exp, grid.sibling(grid.fsdp))]
    return peers + [(grid.exp, grid.x_from(hop)) for hop in range(1, grid.x_size)]


class ChipGather:
    def __init__(self, grid, links, own_sem, source, target):
        self.grid, self.links, self.target = grid, links, target
        self.own = pltpu.make_async_copy(source, target.at[grid.fsdp], own_sem)
        sibling = grid.sibling(grid.fsdp)
        self.along_x, self.across = [], []
        for hop in range(1, grid.x_size):
            self.along_x.append(
                links.copy(
                    source, target.at[grid.fsdp], (grid.exp, grid.x_from(hop)),
                    target.at[grid.x_from(-hop)],
                )
            )
        self.across.append(
            links.copy(source, target.at[grid.fsdp], (grid.exp, sibling), target.at[sibling])
        )

    def start(self):
        for going, _ in self.along_x + self.across:
            going.start()
        self.own.start()

    def forward(self):
        grid = self.grid
        for hop in range(1, grid.x_size):
            self.along_x[hop - 1][1].wait_recv()
            held = grid.x_from(-hop)
            other = grid.sibling(held)
            self.across.append(
                self.links.copy(
                    self.target.at[held], self.target.at[held],
                    (grid.exp, grid.sibling(grid.fsdp)), self.target.at[other],
                )
            )
            self.across[-1][0].start()

    def finish(self):
        for _, coming in self.across:
            coming.wait_recv()
        for going, _ in self.along_x + self.across:
            going.wait_send()
        self.own.wait()


class Exchange:
    def __init__(self, grid, axis, links, own_sems, pairs):
        size = grid.exp_size if axis == "exp" else grid.fsdp_size
        place = grid.exp if axis == "exp" else grid.fsdp
        device = (lambda to: (to, grid.fsdp)) if axis == "exp" else (lambda to: (grid.exp, to))
        self.peers = [device((place + hop) % size) for hop in range(1, size)]
        self.copies, self.own = [], []
        for index, (source, target) in enumerate(pairs):
            for hop in range(1, size):
                to, origin = (place + hop) % size, (place + size - hop) % size
                self.copies.append(
                    links.copy(source(to), target.at[place], device(to), target.at[origin])
                )
            self.own.append(
                pltpu.make_async_copy(source(place), target.at[place], own_sems.at[index])
            )

    def start(self):
        for going, _ in self.copies:
            going.start()
        for own in self.own:
            own.start()

    def finish(self):
        for going, coming in self.copies:
            coming.wait_recv()
            going.wait_send()
        for own in self.own:
            own.wait()


ANYWHERE = pl.BlockSpec(memory_space=pl.ANY)
IN_VMEM = pl.BlockSpec(memory_space=pltpu.VMEM)


def dma_sems(count):
    return pltpu.SemaphoreType.DMA((count,))


def exchange(axis, arrays, collective_id, micros):
    grid = Grid()
    size = grid.exp_size if axis == "exp" else grid.fsdp_size
    count = len(arrays)
    parts = [part for _, part in arrays]

    def kernel(*refs):
        sources, targets = refs[:count], refs[count : 2 * count]
        send, receive, own = refs[2 * count :]
        place = grid.here()
        pairs = [
            (partial(plane_of, source, part), target)
            for source, part, target in zip(sources, parts, targets)
        ]
        work = Exchange(place, axis, Links(send, receive), own, pairs)
        greet(work.peers)
        work.start()
        work.finish()

    return pl.pallas_call(
        kernel,
        out_shape=tuple(
            shape_of((size,) + array.shape[(1 if part is None else 2) :], array.dtype)
            for array, part in arrays
        ),
        in_specs=[IN_VMEM] * count,
        out_specs=tuple([ANYWHERE] * count),
        scratch_shapes=[dma_sems(count * size), dma_sems(count * size), dma_sems(count)],
        compiler_params=pltpu.CompilerParams(collective_id=collective_id, has_side_effects=True),
        cost_estimate=hint(micros),
        name=f"exchange_{collective_id}",
    )(*[array for array, _ in arrays])


def plane_of(source, part, to):
    return source.at[to] if part is None else source.at[to, part]


def gather_rows(array, collective_id, micros):
    grid = Grid()

    def kernel(source, target, send, receive, own):
        place = grid.here()
        work = ChipGather(place, Links(send, receive), own.at[0], source, target)
        greet(chip_peers(place))
        work.start()
        work.forward()
        work.finish()

    return pl.pallas_call(
        kernel,
        out_shape=shape_of((grid.fsdp_size,) + array.shape, array.dtype),
        in_specs=[IN_VMEM],
        out_specs=ANYWHERE,
        scratch_shapes=[dma_sems(2 * grid.fsdp_size), dma_sems(2 * grid.fsdp_size), dma_sems(1)],
        compiler_params=pltpu.CompilerParams(collective_id=collective_id, has_side_effects=True),
        cost_estimate=hint(micros),
        name=f"gather_{collective_id}",
    )(array)


class Lanes:
    def __init__(self, heads, width, padded_heads, experts):
        self.weights = 3 * heads * width
        self.base = self.weights // 128 * 128
        self.router = self.weights - self.base
        self.gain = self.router + experts
        self.table = self.gain + 1
        self.count = self.table + padded_heads
        self.width = -(-(self.weights + 2 * experts + 1 + padded_heads) // 128) * 128
        self.extra = self.width - self.base
        self.shift = self.count - self.router


def bucket_rows_select(features, feature_rows, bucket_rows, span):
    row = lax.broadcasted_iota(jnp.int32, (features, 1), 0)
    within = lax.rem(row, feature_rows)
    bucket = jnp.where(
        within < bucket_rows, lax.div(row, feature_rows) * bucket_rows + within, -1
    )
    distance = lax.broadcasted_iota(jnp.int32, (1, span), 1) - SKEW
    near = BUCKETS // 2
    spread = max(WINDOW - near, 1)
    far = near + lax.div(jnp.maximum(distance - near, 0) * (BUCKETS - near), spread)
    wanted = jnp.where(distance < near, distance, far)
    reachable = (distance >= 0) & (distance < WINDOW)
    wanted = jnp.where(reachable, wanted, -2)
    return jnp.where(bucket == wanted, 1.0, 0.0).astype(BF16), reachable


def as_column(row, size):
    row_place = lax.broadcasted_iota(jnp.int32, (size, size), 0)
    lane = lax.broadcasted_iota(jnp.int32, (size, size), 1)
    spread = jnp.broadcast_to(row.astype(F32), (size, size))
    return jnp.sum(jnp.where(row_place == lane, spread, 0.0), axis=1, keepdims=True)


def padded_rows(value, rows):
    if value.shape[0] == rows:
        return value
    return jnp.concatenate([value, jnp.zeros((rows - value.shape[0], value.shape[1]), F32)], axis=0)


def padded_lanes(value, lanes):
    if value.shape[1] == lanes:
        return value
    return jnp.concatenate([value, jnp.zeros((value.shape[0], lanes - value.shape[1]), F32)], axis=1)


class Wide:
    def __init__(self, grid, links, own_sem, source, target):
        self.grid, self.links, self.target = grid, links, target
        self.own = pltpu.make_async_copy(
            source, target.at[grid.z, grid.y, grid.x, grid.core], own_sem
        )
        stage = []
        for hop in range(1, grid.x_size):
            origin = (grid.x + grid.x_size - hop) % grid.x_size
            stage.append(
                links.copy(
                    source, target.at[grid.z, grid.y, grid.x, grid.core],
                    (grid.exp, grid.x_from(hop)), target.at[grid.z, grid.y, origin, grid.core],
                )
            )
        self.stages = [stage]

    def start(self):
        self.own.start()
        for going, _ in self.stages[0]:
            going.start()

    def turn(self, axis):
        grid, target = self.grid, self.target
        for _, coming in self.stages[-1]:
            coming.wait_recv()
        stage = []
        if axis == 0:
            self.own.wait()
            held = target.at[grid.z, grid.y, :, grid.core]
            for hop in range(1, grid.z_size):
                origin = (grid.z + grid.z_size - hop) % grid.z_size
                stage.append(
                    self.links.copy(
                        held, held, grid.at(z=(grid.z + hop) % grid.z_size),
                        target.at[origin, grid.y, :, grid.core],
                    )
                )
        elif axis == 1:
            held = target.at[:, grid.y, :, grid.core]
            for hop in range(1, grid.y_size):
                origin = (grid.y + grid.y_size - hop) % grid.y_size
                stage.append(
                    self.links.copy(
                        held, held, grid.at(y=(grid.y + hop) % grid.y_size),
                        target.at[:, origin, :, grid.core],
                    )
                )
        else:
            held = target.at[:, :, :, grid.core]
            stage.append(
                self.links.copy(
                    held, held, (grid.exp, grid.sibling(grid.fsdp)), target.at[:, :, :, 1 - grid.core]
                )
            )
        for going, _ in stage:
            going.start()
        self.stages.append(stage)

    def finish(self):
        for _, coming in self.stages[-1]:
            coming.wait_recv()
        for stage in self.stages:
            for going, _ in stage:
                going.wait_send()


def start_kernel(
    tokens, cotangent, routes_t, slots_t, attention_gain, mixture_gain, attention_in, router_t, table,
    attention_out, expert_up, expert_down, *refs, lanes, heads, width, head_count, experts, capacity,
    local,
):
    all_tokens, all_planes, cotangent_slots, position_rows, columns, full_out = refs[:6]
    shards = refs[6 : 6 + 2 * local]
    planes, up_stage, down_stage, send, receive, own, fetch, split = refs[6 + 2 * local :]
    grid = Grid().here()
    links = Links(send, receive)
    z_size, y_size, fsdp_size = grid.z_size, grid.y_size, grid.fsdp_size
    near = [
        (grid.exp, (grid.fsdp + turn) % fsdp_size) for turn in range(1, fsdp_size)
    ] + [grid.at(z=(grid.z + hop) % z_size) for hop in range(1, z_size)]
    beside = [grid.at(y=(grid.y + hop) % y_size) for hop in range(1, y_size)]
    gathered = ChipGather(grid, links, own.at[0], tokens, all_tokens)
    widely = Wide(grid, links, own.at[2], attention_out, full_out)
    part = expert_down.shape[1]
    depth = expert_up.shape[1]
    fetches = []
    for index in range(local):
        fetches.append(
            pltpu.make_async_copy(expert_up.at[index], up_stage.at[index], fetch.at[2 * index])
        )
        fetches.append(
            pltpu.make_async_copy(
                expert_down.at[index], down_stage.at[index], fetch.at[2 * index + 1]
            )
        )
    greet(near + beside)
    widely.start()
    for copy in fetches:
        copy.start()

    feature_rows = attention_in.shape[0]
    model_width = head_count * width
    gained = attention_in[...].astype(F32) * as_column(attention_gain[...], feature_rows)
    route_rows, slot_rows = routes_t[...].astype(F32), slots_t[...].astype(F32)
    columns[...] = padded_rows(jnp.concatenate([route_rows, slot_rows], axis=0), 128).T
    row_count = columns.shape[0]
    expert_lanes = lax.broadcasted_iota(jnp.int32, (row_count, experts), 1).astype(F32)
    named = jnp.zeros((row_count, experts), F32)
    for k in range(2):
        named = named + jnp.where(expert_lanes == columns[:, k : k + 1], 1.0, 0.0)
    named = jnp.sum(named, axis=0, keepdims=True)
    place = lax.broadcasted_iota(jnp.int32, (feature_rows, feature_rows), 0)
    same = place == lax.broadcasted_iota(jnp.int32, (feature_rows, feature_rows), 1)
    router = contract_last(jnp.where(same, 1.0, 0.0).astype(BF16), router_t[...])
    pieces = [
        router,
        as_column(mixture_gain[...], feature_rows),
        padded_rows(padded_lanes(table[...].astype(F32), heads * fsdp_size), feature_rows),
        padded_rows(named, feature_rows),
    ]
    taken = sum(piece.shape[1] for piece in pieces)
    if lanes.width > lanes.weights + taken:
        pieces.append(jnp.zeros((feature_rows, lanes.width - lanes.weights - taken), F32))
    for place in range(fsdp_size):
        first, last = place * heads * width, min((place + 1) * heads * width, model_width)
        own_pieces = []
        for kind in range(3):
            if last > first:
                own_pieces.append(gained[:, kind * model_width + first : kind * model_width + last])
            if last - first < heads * width:
                own_pieces.append(
                    jnp.zeros((feature_rows, heads * width - max(last - first, 0)), F32)
                )
        planes[place] = jnp.concatenate(own_pieces + pieces, axis=1).astype(BF16)
    placed = []
    for turn in range(1, fsdp_size):
        to = (grid.fsdp + turn) % fsdp_size
        origin = (grid.fsdp + fsdp_size - turn) % fsdp_size
        placed.append(
            links.copy(
                planes.at[to], all_planes.at[grid.z, grid.y, grid.fsdp], (grid.exp, to),
                all_planes.at[grid.z, grid.y, origin],
            )
        )
        placed[-1][0].start()
    kept = pltpu.make_async_copy(
        planes.at[grid.fsdp], all_planes.at[grid.z, grid.y, grid.fsdp], own.at[1]
    )
    kept.start()
    gathered.start()
    for _, coming in placed:
        coming.wait_recv()
    kept.wait()

    def over_y(z):
        for turn in range(1, y_size):
            forwarded.append(
                links.copy(
                    all_planes.at[z, grid.y],
                    all_planes.at[z, grid.y],
                    grid.at(y=(grid.y + turn) % y_size),
                    all_planes.at[z, (grid.y + y_size - turn) % y_size],
                )
            )
            forwarded[-1][0].start()

    along_z, forwarded = [], []
    for hop in range(1, z_size):
        along_z.append(
            links.copy(
                all_planes.at[grid.z, grid.y],
                all_planes.at[grid.z, grid.y],
                grid.at(z=(grid.z + hop) % z_size),
                all_planes.at[(grid.z + z_size - hop) % z_size, grid.y],
            )
        )
        along_z[-1][0].start()
    over_y(grid.z)
    widely.turn(0)

    for copy in fetches:
        copy.wait()
    splits = []
    for index in range(local):
        up, down = shards[2 * index : 2 * index + 2]
        stores = [
            (
                up_stage.at[index, :, pl.ds(block * part, part)],
                up.at[pl.ds(block * depth, depth), :],
            )
            for block in range(fsdp_size)
        ]
        for source, target in stores + [(down_stage.at[index], down)]:
            splits.append(pltpu.make_async_copy(source, target, split.at[len(splits)]))
            splits[-1].start()

    place = route_rows * capacity + slot_rows
    position_rows[...] = padded_rows(place, 8)
    select_rows(cotangent_slots, place, cotangent[...])

    for hop in range(1, z_size):
        along_z[hop - 1][1].wait_recv()
        over_y((grid.z + z_size - hop) % z_size)
    widely.turn(1)
    gathered.forward()
    widely.turn(2)
    for going, coming in forwarded:
        coming.wait_recv()
        going.wait_send()
    for going, _ in placed + along_z:
        going.wait_send()
    gathered.finish()
    widely.finish()
    for copy in splits:
        copy.wait()


def project_kernel(
    tokens, plane, segments, normed, query_t, key_n, query_n, value_n, key_t, value_t, bias, counts,
    weight_t, table_t, *, heads, width, lanes, feature_rows, bucket_rows,
):
    @pl.when(pl.program_id(0) == 0)
    def _():
        weight_t[...] = turned(plane[:, : lanes.weights]).astype(BF16)
        extra = plane[:, lanes.base :]
        span = bias.shape[2]
        select, reachable = bucket_rows_select(plane.shape[0], feature_rows, bucket_rows, span)
        table_t[...] = lax.dot_general(
            extra, select, (((0,), (0,)), ((), ())), preferred_element_type=F32
        )
        first = lanes.table + lax.axis_index("fsdp") * heads
        for head in range(heads):
            bias[head] = jnp.where(reachable, table_t[pl.ds(first + head, 1), :], MASKED)
        summed = jnp.sum(extra.astype(F32), axis=0, keepdims=True)
        counts[...] = pltpu.roll(
            jnp.broadcast_to(summed, counts.shape), lanes.extra - lanes.shift, 1
        )

    inputs = tokens[0].astype(F32)
    scale = lax.rsqrt(jnp.mean(inputs * inputs, axis=1, keepdims=True) + EPSILON)
    low = (inputs * scale).astype(BF16)
    normed[...] = low
    rows = low.shape[0]
    projected = contract_last(weight_t[...], low).astype(BF16).astype(F32)
    document = segments[...] % 4
    places = lax.broadcasted_iota(jnp.int32, (8, rows), 0)
    same = places == document
    hot = jnp.where(same, 1.0, 0.0)
    barred = jnp.where(same | (places >= 4), 0.0, MASKED)
    filler = jnp.zeros((SKEW - 8 - width, rows), F32)
    for head in range(heads):
        query = projected[head * width : (head + 1) * width] * width ** (-0.5)
        key = projected[(heads + head) * width : (heads + head + 1) * width]
        value = projected[(2 * heads + head) * width : (2 * heads + head + 1) * width]
        query_t[head] = jnp.concatenate([query, barred, filler], axis=0).astype(BF16)
        key_n[head] = jnp.concatenate([key, hot, filler], axis=0).T.astype(BF16)
        query_n[head] = query.T.astype(BF16)
        value_n[head] = value.T.astype(BF16)
        key_t[head] = key.astype(BF16)
        value_t[head] = value.astype(BF16)


def spans(length):
    for query_start in range(0, length, QUERY_BLOCK):
        key_start = max(0, query_start - WINDOW)
        yield query_start, key_start, query_start + QUERY_BLOCK - key_start


def spread_bias(bias, skew):
    skew[...] = pltpu.roll(
        jnp.broadcast_to(bias[0], skew.shape), 0, 1, stride=1, stride_axis=0
    )


def attend_kernel(query_t, key_n, value_t, bias, context, context_high, log_total, skew, scores, *, rows):
    spread_bias(bias, skew)
    for query_start, key_start, key_count in spans(query_t.shape[2]):
        queries = slice(query_start, query_start + QUERY_BLOCK)
        keys = slice(key_start, key_start + key_count)
        raw = matmul(key_n[0, keys, :], query_t[0, :, queries])
        for start in range(0, key_count, SKEW):
            offset = query_start - key_start - start + SKEW
            scores[start : start + SKEW, :] = (
                raw[start : start + SKEW] + skew[:, offset : offset + QUERY_BLOCK]
            )
        high = jnp.max(scores[:key_count, :], axis=0, keepdims=True)
        weights = jnp.exp(scores[:key_count, :] - high)
        total = jnp.sum(weights, axis=0, keepdims=True)
        gathered = matmul(value_t[0, :, keys], weights.astype(BF16)) / total
        context_high[0, :, queries] = gathered
        log_total[0, :, queries] = high + jnp.log(total)
        for start in range(0, QUERY_BLOCK, 128):
            place = query_start + start
            context[place // rows, :, place % rows : place % rows + 128] = gathered[
                :, start : start + 128
            ].astype(BF16)


def attend_back_kernel(
    query_t, key_n, query_n, value_n, key_t, grad_t, grad_n, context_high, log_total, bias,
    grad_projected, grad_bias, skew, grad_skew, grad_key, grad_value, *, scale,
):
    spread_bias(bias, skew)
    grad_skew[...] = jnp.zeros_like(grad_skew)
    grad_key[...] = jnp.zeros_like(grad_key)
    grad_value[...] = jnp.zeros_like(grad_value)
    inner = jnp.sum(grad_t[0].astype(F32) * context_high[0], axis=0, keepdims=True)
    for query_start, key_start, key_count in spans(query_t.shape[2]):
        queries = slice(query_start, query_start + QUERY_BLOCK)
        keys = slice(key_start, key_start + key_count)
        raw = matmul(key_n[0, keys, :], query_t[0, :, queries])
        grad_weights = matmul(value_n[0, keys, :], grad_t[0, :, queries])
        weights_low, grad_low = [], []
        for start in range(0, key_count, SKEW):
            offset = query_start - key_start - start + SKEW
            part = slice(start, start + SKEW)
            weights = jnp.exp(
                raw[part] + skew[:, offset : offset + QUERY_BLOCK] - log_total[0, :, queries]
            )
            grad_scores = weights * (grad_weights[part] - inner[:, queries])
            grad_skew[:, offset : offset + QUERY_BLOCK] += grad_scores
            weights_low.append(weights.astype(BF16))
            grad_low.append(grad_scores.astype(BF16))
        weights_low = jnp.concatenate(weights_low, axis=0)
        grad_low = jnp.concatenate(grad_low, axis=0)
        grad_projected[0, 0, :, queries] = (matmul(key_t[0, :, keys], grad_low) * scale).astype(BF16)
        grad_key[keys, :] += matmul(grad_low, query_n[0, queries, :])
        grad_value[keys, :] += matmul(weights_low, grad_n[0, queries, :])
    grad_projected[1, 0] = grad_key[...].T.astype(BF16)
    grad_projected[2, 0] = grad_value[...].T.astype(BF16)
    count = SKEW
    span = skew.shape[1]
    while count > 8:
        count //= 2
        grad_skew[:count, :] += pltpu.roll(grad_skew[count : 2 * count, :], span - count, 1)
    summed = grad_skew[0:1, :]
    for row in range(1, 8):
        summed = summed + pltpu.roll(grad_skew[row : row + 1, :], span - row, 1)
    grad_bias[0] = summed

def expert_lane(shape, lanes):
    return lax.broadcasted_iota(jnp.int32, shape, 1) - lanes.router


def int_columns(columns):
    values = columns[:, 0:4].astype(jnp.int32)
    return values[:, 0:2], values[:, 2:4]


def route_kernel(
    tokens, attended_t, attention_out, plane, columns, position_rows,
    hidden, routed, probabilities, gates, outgoing, slot_gates, *, experts, lanes, capacity,
):
    rows, model_width = tokens.shape
    routes, slots = int_columns(columns)
    attended_low = turned(attended_t[:model_width]).astype(BF16)
    hidden_state = tokens[...].astype(F32) + matmul(attended_low, attention_out[...])
    hidden[...] = hidden_state
    scale = lax.rsqrt(jnp.mean(hidden_state * hidden_state, axis=1, keepdims=True) + EPSILON)
    extra = plane[:, lanes.base :]
    gain = extra.astype(F32).T[lanes.gain : lanes.gain + 1]
    low = (hidden_state * scale * gain).astype(BF16)
    routed[...] = low
    logits = matmul(low, extra)
    lane = expert_lane(logits.shape, lanes)
    logits = jnp.where((lane >= 0) & (lane < experts), logits, MASKED)
    powers = jnp.exp(logits - jnp.max(logits, axis=1, keepdims=True))
    powers = powers / jnp.sum(powers, axis=1, keepdims=True)
    probabilities[...] = powers
    chosen = [
        jnp.sum(jnp.where(lane == routes[:, k : k + 1], powers, 0.0), axis=1, keepdims=True)
        for k in range(2)
    ]
    total = chosen[0] + chosen[1]
    gate_values = [chosen[k] / total for k in range(2)]
    pair = lax.broadcasted_iota(jnp.int32, (rows, 2), 1)
    gates[...] = jnp.where(pair == 0, gate_values[0], gate_values[1])
    members, _, gate_lanes = slot_gates.shape
    member_slots = experts // members * capacity
    slot_lanes = lax.broadcasted_iota(jnp.int32, (rows, gate_lanes), 1)
    inside = slot_lanes < member_slots
    places = routes * capacity + slots
    for member in range(members):
        by_slot = jnp.zeros((rows, gate_lanes), F32)
        for k in range(2):
            hit = (slot_lanes + member * member_slots == places[:, k : k + 1]) & inside
            by_slot = by_slot + jnp.where(hit, gate_values[k], 0.0)
        slot_gates[member] = jnp.broadcast_to(
            jnp.sum(by_slot, axis=0, keepdims=True), slot_gates.shape[1:]
        )
    select_rows(outgoing, position_rows[...], low)


def select_rows(outgoing, position_rows, values):
    slot_count, rows = outgoing.shape[0], values.shape[0]
    for start in range(0, slot_count, rows):
        slots = (lax.broadcasted_iota(jnp.int32, (rows, rows), 0) + start).astype(F32)
        picked = (slots == position_rows[0:1, :]) | (slots == position_rows[1:2, :])
        outgoing[start : start + rows, :] = matmul(
            jnp.where(picked, 1.0, 0.0).astype(BF16), values
        ).astype(BF16)


def gelu_parts(value):
    magnitude = jnp.abs(value)
    power = jnp.exp2(value * value * -0.7213475204444817)
    base = 1.0 + (0.3275911 * 0.7071067811865476) * magnitude
    step = pl.reciprocal(base, approx=True)
    step = step * (2.0 - base * step)
    series = step * (
        0.127414796
        + step * (-0.142248368 + step * (0.7107068705 + step * (-0.7265760135 + step * 0.5307027145)))
    )
    tail = series * power
    normal = jnp.where(value < 0.0, tail, 1.0 - tail)
    return value * normal, normal + value * (power * 0.3989422804014327)


def flipped(place, other, size):
    result, bit = 0, 1
    while bit < size:
        result = result + bit * ((place // bit + other // bit) % 2)
        bit *= 2
    return result


def expert_kernel(*refs, layout, index, local, half, capacity, parts):
    shards = 2 * half
    refs = Bag(layout, refs)
    grid = Grid().here()
    z_size, y_size = grid.z_size, grid.y_size
    first, last = False, index == local - 1
    sibling = (grid.exp, grid.sibling(grid.fsdp))
    links = Links(refs.send[0], refs.receive[0])
    rows_all, cot, up_all, down_all = (
        refs.rows_all[0], refs.cot[0], refs.up_all[0], refs.down_all[0]
    )
    active, grad_hidden, unscaled = refs.active[0], refs.grad_hidden[0], refs.unscaled[0]
    gates, gate_column = refs.gates[0], refs.gate_column[0]
    rows_t, slot_t = refs.rows_t[0], refs.slot_t[0]
    grad_up, grad_down = refs.grad_up[0], refs.grad_down[0]
    grad_rows, grad_gates = refs.grad_rows[0], refs.grad_gates[0]
    up_keep, up_taken, down_keep, down_taken = refs.own
    keep_up = [up_keep] + list(refs.far_keep_up)
    taken_up = [up_taken] + list(refs.far_taken_up)
    keep_down = [down_keep] + list(refs.far_keep_down)
    taken_down = [down_taken] + list(refs.far_taken_down)
    load_sem, fetch_sem, store_sem = refs.load_sem[0], refs.fetch_sem[0], refs.store_sem[0]
    store_there, stored_here = refs.store_there[0], refs.stored_here[0]
    pass_sem = refs.pass_sem[0]
    blocks, _, model_width = rows_all.shape
    part = up_all.shape[2]
    count = blocks * capacity
    depth = model_width // shards
    power = z_size & (z_size - 1) == 0
    together = 2 if power and z_size > 1 else 1
    group_rows = together * y_size * capacity

    def source_z(turn):
        return flipped(grid.z, turn, z_size) if power else (grid.z + turn) % z_size

    def target_z(turn):
        return flipped(grid.z, turn, z_size) if power else (grid.z + z_size - turn) % z_size

    def owner(place, core):
        return ((grid.x + place % half) % half) * 2 + (core + place // half) % 2

    def rows_of(place, core=None):
        core = grid.core if core is None else core
        return pl.ds(pl.multiple_of(owner(place, core) * depth, 16), depth)

    loads = [pltpu.make_async_copy(refs.cot_in[0].at[:, index], cot, load_sem.at[0])]
    if not first:
        loads.append(pltpu.make_async_copy(refs.rows_in[0], rows_all, load_sem.at[1]))
    my_up, my_down = refs.my_up, refs.my_down
    swapped_up, swapped_down = refs.swapped_up, refs.swapped_down
    local_up = list(enumerate(my_up)) + [(half, array) for array in swapped_up]
    local_down = list(enumerate(my_down)) + [(half, array) for array in swapped_down]
    fetched_up = [
        pltpu.make_async_copy(
            array.at[rows_of(place), :], up_all.at[place, rows_of(shard), :],
            fetch_sem.at[place, number],
        )
        for number, (shard, array) in enumerate(local_up)
        for place in range(shards)
    ]
    fetched_down = {
        shard: pltpu.make_async_copy(
            array, down_all.at[shard], fetch_sem.at[shards + number, 0]
        )
        for number, (shard, array) in enumerate(local_down)
    }
    crossing = [shard for shard in range(half) if half + shard not in dict(local_up)]
    cross_down = {
        half + shard: links.copy(
            my_down[shard], down_all.at[half + shard], sibling, down_all.at[half + shard]
        )
        for shard in crossing
    }
    cross_up = [
        links.copy(
            my_up[shard].at[rows_of(place, 1 - grid.core), :],
            up_all.at[place, rows_of(shard), :], sibling,
            up_all.at[place, rows_of(half + shard), :],
        )
        for shard in crossing
        for place in range(shards)
    ]
    cross_next = [
        links.copy(source, target, sibling, target)
        for source, target in zip(refs.next_mine, refs.next_swapped)
    ]
    work = Exchange(
        grid, "exp", links, refs.own_sem[0],
        [
            (partial(plane_of, source, place), target)
            for source, place, target in zip(refs.moved_from, parts, refs.moved_to)
        ],
    )
    gate_work = None
    if first:
        gate_work = Exchange(
            grid, "exp", links, refs.gate_sem[0],
            [(partial(plane_of, refs.gates_from[0], None), gates)],
        )

    def member(z, y):
        return z * y_size + y

    def dispatch(turn, hop):
        to = member(target_z(turn), (grid.y + y_size - hop) % y_size)
        origin = member(source_z(turn), (grid.y + hop) % y_size)
        outgoing = refs.outgoing[0]
        going = pltpu.make_async_remote_copy(
            src_ref=outgoing.at[to, index], dst_ref=rows_all.at[grid.exp],
            send_sem=refs.row_send[0].at[turn, hop], recv_sem=refs.row_receive[0].at[turn, hop],
            device_id=(to, grid.fsdp), device_id_type=MESH,
        )
        coming = pltpu.make_async_remote_copy(
            src_ref=rows_all.at[origin], dst_ref=rows_all.at[origin],
            send_sem=refs.row_send[0].at[turn, hop], recv_sem=refs.row_receive[0].at[turn, hop],
            device_id=(to, grid.fsdp), device_id_type=MESH,
        )
        return going, coming

    def give_back(turn, hop):
        to = member(source_z(turn), (grid.y + hop) % y_size)
        origin = member(target_z(turn), (grid.y + y_size - hop) % y_size)
        pairs = []
        for number, (held, target) in enumerate(
            ((grad_rows, refs.back_rows[0]), (grad_gates, refs.back_gates[0]))
        ):
            sems = dict(
                send_sem=refs.back_send[0].at[number, turn, hop],
                recv_sem=refs.back_receive[0].at[number, turn, hop],
                device_id=(to, grid.fsdp), device_id_type=MESH,
            )
            pairs.append(
                (
                    pltpu.make_async_remote_copy(
                        src_ref=held.at[to], dst_ref=target.at[grid.exp], **sems
                    ),
                    pltpu.make_async_remote_copy(
                        src_ref=target.at[origin], dst_ref=target.at[origin], **sems
                    ),
                )
            )
        return pairs

    steps = [(turn, hop) for turn in range(z_size) for hop in range(y_size)]
    own_row = own_back = None
    if first:
        own_row = pltpu.make_async_copy(
            refs.outgoing[0].at[grid.exp, index], rows_all.at[grid.exp], load_sem.at[1]
        )
    if last:
        own_back = [
            pltpu.make_async_copy(held.at[grid.exp], target.at[grid.exp], load_sem.at[2 + number])
            for number, (held, target) in enumerate(
                ((grad_rows, refs.back_rows[0]), (grad_gates, refs.back_gates[0]))
            )
        ]

    for copy in loads:
        copy.start()
    for copy in list(fetched_down.values()) + fetched_up:
        copy.start()
    greet([((grid.exp + hop) % grid.exp_size, grid.fsdp) for hop in range(1, grid.exp_size)] + [sibling])
    if first:
        gate_work.start()
        own_row.start()
        for turn, hop in steps[1:]:
            dispatch(turn, hop)[0].start()
    for going, _ in list(cross_down.values()) + cross_up + cross_next:
        going.start()
    work.start()

    loads[0].wait()
    for place in range(shards):
        if place in fetched_down:
            fetched_down[place].wait()
        else:
            cross_down[place][1].wait_recv()
        unscaled[place] = contract_last(cot[...].reshape(count, model_width), down_all[place])
    if first:
        gate_work.finish()
        gates_out = pltpu.make_async_copy(gates, refs.gates_to[0], load_sem.at[4])
        gates_out.start()
    columns = gates[:, 0, :].T
    for block in range(blocks):
        piece = slice(block * capacity, (block + 1) * capacity)
        gate = columns[index * capacity : (index + 1) * capacity, block : block + 1]
        gate_column[piece, :] = gate
    slot_t[...] = (gate_column[...] * cot[...].reshape(count, model_width).astype(F32)).T.astype(BF16)
    for copy in fetched_up:
        copy.wait()
    for _, coming in cross_up:
        coming.wait_recv()
    if first:
        own_row.wait()
    else:
        loads[1].wait()

    def group(number, carry):
        turns = [number * together + more for more in range(together)]
        if together == 2:
            place_of_group = flipped(grid.z // 2, number, z_size // 2)
        else:
            place_of_group = source_z(number)
        if first:
            for turn in turns:
                for hop in range(y_size):

                    @pl.when(turn + hop > 0)
                    def _(turn=turn, hop=hop):
                        dispatch(turn, hop)[1].wait_recv()

        members = pl.ds(place_of_group * together * y_size, together * y_size)
        span = pl.ds(pl.multiple_of(place_of_group * group_rows, 16), group_rows)
        rows = rows_all[members].reshape(group_rows, model_width)
        gate = gate_column[span, :]
        grad = jnp.zeros((group_rows, model_width), F32)
        products = jnp.zeros((group_rows, part), F32)
        ahead = matmul(rows, up_all[0])
        for place in range(shards):
            hidden = ahead
            if place + 1 < shards:
                ahead = matmul(rows, up_all[place + 1])
            base = unscaled[place, span, :]
            activated, slope = gelu_parts(hidden)
            products = products + activated * base
            active[place, span, :] = activated.astype(BF16)
            low = (gate * base * slope).astype(BF16)
            grad_hidden[place, span, :] = low
            grad = grad + contract_last(low, up_all[place])
        grad_rows[members] = grad.astype(BF16).reshape(together * y_size, capacity, model_width)
        ones = jnp.ones((8, part), F32)
        for hop in range(together * y_size):
            grad_gates[place_of_group * together * y_size + hop] = lax.dot_general(
                ones, products[hop * capacity : (hop + 1) * capacity], (((1,), (1,)), ((), ())),
                precision=lax.Precision.HIGHEST, preferred_element_type=F32,
            )
        if last:
            for turn in turns:
                for hop in range(y_size):

                    @pl.when(turn + hop > 0)
                    def _(turn=turn, hop=hop):
                        for going, _ in give_back(turn, hop):
                            going.start()

        return carry

    lax.fori_loop(0, z_size // together, group, 0)
    if last:
        for copy in own_back:
            copy.start()

    rows_t[...] = turned(rows_all[...].reshape(count, model_width)).astype(BF16)
    total = refs.total[0] if refs.total else unscaled.at[0]
    total[...] = jnp.zeros(total.shape, F32)

    def up_target(targets, hop, place):
        if hop == 0:
            return targets[0].at[rows_of(place), :]
        return targets[1].at[hop - 1, rows_of(place), :]

    def keep_stores(place, slot):
        return [
            pltpu.make_async_copy(
                grad_up.at[slot, rows_of(hop), :], up_target(keep_up, hop, place),
                store_sem.at[slot, hop],
            )
            for hop in range(half)
        ]

    def give_stores(place, slot):
        return [
            pltpu.make_async_remote_copy(
                src_ref=grad_up.at[slot, rows_of(half + hop), :],
                dst_ref=up_target(taken_up, hop, place),
                send_sem=store_there.at[slot, hop], recv_sem=stored_here.at[place, hop],
                device_id=sibling, device_id_type=MESH,
            )
            for hop in range(half)
        ]

    def down_store(hop, slot):
        target = keep_down[0] if hop == 0 else keep_down[1].at[hop - 1]
        return pltpu.make_async_copy(grad_down.at[slot], target, store_sem.at[slot, half])

    def down_give(hop, slot):
        target = taken_down[0] if hop == 0 else taken_down[1].at[hop - 1]
        return pltpu.make_async_remote_copy(
            src_ref=grad_down.at[slot], dst_ref=target,
            send_sem=store_there.at[slot, half], recv_sem=stored_here.at[hop, half],
            device_id=sibling, device_id_type=MESH,
        )

    def each_down(place, slot, act):
        for hop in range(half):

            @pl.when(place == hop)
            def _(hop=hop):
                act(down_store(hop, slot), False)

            @pl.when(place == half + hop)
            def _(hop=hop):
                act(down_give(hop, slot), True)

    def start_store(place, slot):
        for copy in keep_stores(place, slot) + give_stores(place, slot):
            copy.start()
        each_down(place, slot, lambda copy, _: copy.start())

    def wait_store(place, slot):
        for copy in keep_stores(place, slot):
            copy.wait()
        for copy in give_stores(place, slot):
            copy.wait_send()
        each_down(place, slot, lambda copy, remote: copy.wait_send() if remote else copy.wait())

    def column(place, carry):
        slot = place % 2
        total[...] += matmul(active[place], down_all[place])

        @pl.when(place >= 2)
        def _():
            wait_store(place - 2, slot)

        grad_up[slot] = matmul(rows_t[...], grad_hidden[place]).astype(BF16)
        grad_down[slot] = matmul(slot_t[...], active[place]).T.astype(BF16)
        start_store(place, slot)
        return carry

    lax.fori_loop(0, shards, column, 0)

    rows_out = refs.rows_out[0]
    cot[...] = total[...].astype(BF16).reshape(blocks, capacity, model_width)
    out_copies = [pltpu.make_async_copy(cot, rows_out.at[:, index], load_sem.at[0])]
    for before in refs.outs_before:
        out_copies.append(
            pltpu.make_async_copy(before, rows_out.at[:, pl.ds(0, index)], load_sem.at[1])
        )
    for copy in out_copies:
        copy.start()
    for place in range(max(shards - 2, 0), shards):
        wait_store(place, place % 2)
    for place in range(shards):
        for copy in give_stores(place, 0):
            copy.wait_recv()
    for hop in range(half):
        down_give(hop, 0).wait_recv()
    if half > 1:
        for kept, taken, target, sem in (
            (keep_up[1], taken_up[1], refs.pass_up[0], 0),
            (keep_down[1], taken_down[1], refs.pass_down[0], 1),
        ):
            kept[...] = (kept[...].astype(F32) + taken[...].astype(F32)).astype(BF16)
            out_copies.append(pltpu.make_async_copy(kept, target, pass_sem.at[sem]))
            out_copies[-1].start()
    for copy in out_copies:
        copy.wait()
    for going, coming in cross_next:
        coming.wait_recv()
        going.wait_send()
    for going, _ in list(cross_down.values()) + cross_up:
        going.wait_send()
    if first:
        gates_out.wait()
        for turn, hop in steps[1:]:
            dispatch(turn, hop)[0].wait_send()
    work.finish()
    if last:
        for turn, hop in steps[1:]:
            for going, coming in give_back(turn, hop):
                coming.wait_recv()
                going.wait_send()
        for copy in own_back:
            copy.wait()


class Bag:
    def __init__(self, layout, refs):
        start = 0
        for name, size in layout.items():
            setattr(self, name, refs[start : start + size])
            start += size


class Wanted:
    def groups(self):
        return list(self.__dict__.values())

    def layout(self):
        return {name: len(group) for name, group in self.__dict__.items()}


def run_expert(index, local, outgoing, slot_gates, rows_in, gates, cotangent, ups, downs, swapped,
               next_mine, moved, outs_before, collective_id):
    grid = Grid()
    half = len(ups)
    shards = 2 * half
    first, last = False, index == local - 1
    blocks, _, capacity, model_width = cotangent.shape
    part = downs[0].shape[0]
    count = blocks * capacity
    gate_lanes = slot_gates.shape[2]
    inputs, outputs, scratch = Wanted(), Wanted(), Wanted()
    inputs.cot_in = [(cotangent, ANYWHERE)]
    inputs.outgoing = [(outgoing, ANYWHERE)] if first else []
    inputs.gates_from = [(slot_gates, ANYWHERE)] if first else []
    inputs.rows_in = [] if first else [(rows_in, ANYWHERE)]
    if not first:
        inputs.gates = [(gates, IN_VMEM)]
    inputs.my_up = [(array, ANYWHERE) for array in ups]
    inputs.my_down = [(array, ANYWHERE) for array in downs]
    inputs.swapped_up = [(array, ANYWHERE) for array in swapped[:1]]
    inputs.swapped_down = [(array, ANYWHERE) for array in swapped[1:]]
    inputs.next_mine = [(array, ANYWHERE) for array in next_mine]
    inputs.moved_from = [(array, ANYWHERE) for array, _ in moved]
    inputs.outs_before = [] if outs_before is None else [(outs_before, IN_VMEM)]

    up_shape, down_shape = (model_width, part), (part, model_width)
    outputs.rows_out = [(shape_of((blocks, index + 1, capacity, model_width), BF16), ANYWHERE)]
    own_up, own_down = shape_of(up_shape, BF16), shape_of(down_shape, BF16)
    outputs.own = [(own_up, ANYWHERE), (own_up, ANYWHERE), (own_down, ANYWHERE), (own_down, ANYWHERE)]
    outputs.pass_up = [(shape_of((half - 1,) + up_shape, BF16), ANYWHERE)] if half > 1 else []
    outputs.pass_down = [(shape_of((half - 1,) + down_shape, BF16), ANYWHERE)] if half > 1 else []
    outputs.next_swapped = [(shape_of(array.shape, BF16), ANYWHERE) for array in next_mine]
    outputs.gates_to = [(shape_of(slot_gates.shape, F32), ANYWHERE)] if first else []
    outputs.moved_to = [
        (
            shape_of((grid.exp_size,) + array.shape[(1 if place is None else 2) :], array.dtype),
            ANYWHERE,
        )
        for array, place in moved
    ]
    rows_shape, gate_shape = (blocks, capacity, model_width), (blocks, 8, capacity)
    if last:
        outputs.back_rows = [(shape_of(rows_shape, BF16), ANYWHERE)]
        outputs.back_gates = [(shape_of(gate_shape, F32), ANYWHERE)]
    else:
        outputs.grad_rows = [(shape_of(rows_shape, BF16), IN_VMEM)]
        outputs.grad_gates = [(shape_of(gate_shape, F32), IN_VMEM)]

    sems = lambda *shape: pltpu.SemaphoreType.DMA(shape)
    scratch.rows_all = [pltpu.VMEM(rows_shape, BF16)]
    scratch.cot = [pltpu.VMEM(rows_shape, BF16)]
    scratch.up_all = [pltpu.VMEM((shards,) + up_shape, BF16)]
    scratch.down_all = [pltpu.VMEM((shards,) + down_shape, BF16)]
    scratch.active = [pltpu.VMEM((shards, count, part), BF16)]
    scratch.grad_hidden = [pltpu.VMEM((shards, count, part), BF16)]
    scratch.unscaled = [pltpu.VMEM((shards, count, part), F32)]
    if first:
        scratch.gates = [pltpu.VMEM(slot_gates.shape, F32)]
        scratch.gate_sem = [sems(1)]
        scratch.row_send = [sems(grid.z_size, grid.y_size)]
        scratch.row_receive = [sems(grid.z_size, grid.y_size)]
    if last:
        scratch.grad_rows = [pltpu.VMEM(rows_shape, BF16)]
        scratch.grad_gates = [pltpu.VMEM(gate_shape, F32)]
        scratch.back_send = [sems(2, grid.z_size, grid.y_size)]
        scratch.back_receive = [sems(2, grid.z_size, grid.y_size)]
    scratch.gate_column = [pltpu.VMEM((count, 1), F32)]
    scratch.rows_t = [pltpu.VMEM((model_width, count), BF16)]
    scratch.slot_t = [pltpu.VMEM((model_width, count), BF16)]
    scratch.total = [] if part == model_width else [pltpu.VMEM((count, model_width), F32)]
    scratch.grad_up = [pltpu.VMEM((2,) + up_shape, BF16)]
    scratch.grad_down = [pltpu.VMEM((2,) + down_shape, BF16)]
    far_up = [pltpu.VMEM((half - 1,) + up_shape, BF16)] * (1 if half > 1 else 0)
    far_down = [pltpu.VMEM((half - 1,) + down_shape, BF16)] * (1 if half > 1 else 0)
    scratch.far_keep_up, scratch.far_taken_up = far_up, far_up
    scratch.far_keep_down, scratch.far_taken_down = far_down, far_down
    scratch.load_sem = [sems(5)]
    scratch.pass_sem = [sems(2)]
    scratch.fetch_sem = [sems(2 * shards, half + 1)]
    scratch.store_sem = [sems(2, half + 1)]
    scratch.store_there = [sems(2, half + 1)]
    scratch.stored_here = [sems(shards, half + 1)]
    copies = (len(moved) + 1) * grid.exp_size + half * (shards + 1) + len(next_mine)
    scratch.send = [sems(copies)]
    scratch.receive = [sems(copies)]
    scratch.own_sem = [sems(max(len(moved), 1))]

    layout = {**inputs.layout(), **outputs.layout(), **scratch.layout()}

    def body(*refs):
        expert_kernel(
            *refs, layout=layout, index=index, local=local, half=half, capacity=capacity,
            parts=[place for _, place in moved],
        )

    results = pl.pallas_call(
        body,
        in_specs=[spec for group in inputs.groups() for _, spec in group],
        out_specs=tuple(spec for group in outputs.groups() for _, spec in group),
        out_shape=tuple(shape for group in outputs.groups() for shape, _ in group),
        scratch_shapes=[item for group in scratch.groups() for item in group],
        compiler_params=params(collective_id=collective_id, has_side_effects=True),
        cost_estimate=hint(45),
        name=f"expert_{index}",
    )(*[array for group in inputs.groups() for array, _ in group])
    return Bag(outputs.layout(), results)


def local_picks(routes, slots, capacity, local, index, slot_count):
    member, which = lax.div(routes, local), lax.rem(routes, local)
    places = jnp.where(which == index, member * capacity + slots, -1)
    lane = lax.broadcasted_iota(jnp.int32, (routes.shape[0], slot_count), 1)
    return [lane == places[:, k : k + 1] for k in range(2)]


def unroute_kernel(
    hidden, cotangent, routed, probabilities, gates, plane, columns, counts, *refs,
    experts, local, token_total, lanes,
):
    grads, gate_grads = refs[:local], refs[local : 2 * local]
    grad_hidden, grad_branch, small = refs[2 * local :]
    rows = hidden.shape[0]
    members, capacity, model_width = grads[0].shape
    grad_output = cotangent[...].astype(F32)
    grad_routed = jnp.zeros(hidden.shape, F32)
    found = [jnp.zeros((rows, capacity), F32), jnp.zeros((rows, capacity), F32)]
    routes, slots = int_columns(columns)
    member, which = lax.div(routes, local), lax.rem(routes, local)
    lane = lax.broadcasted_iota(jnp.int32, (rows, capacity), 1)
    for index in range(local):
        picks = local_picks(routes, slots, capacity, local, index, members * capacity)
        grad_routed = grad_routed + matmul(
            jnp.where(picks[0] | picks[1], 1.0, 0.0).astype(BF16),
            grads[index][...].reshape(members * capacity, model_width),
        )
        for place in range(members):
            spots = jnp.where((which == index) & (member == place), slots, -1)
            for k in range(2):
                found[k] = found[k] + jnp.where(
                    lane == spots[:, k : k + 1], gate_grads[index][place, 0:1, :], 0.0
                )
    grad_gates = [jnp.sum(found[k], axis=1, keepdims=True) for k in range(2)]
    powers = probabilities[...]
    lane = expert_lane(powers.shape, lanes)
    inside = (lane >= 0) & (lane < experts)
    picked = [lane == routes[:, k : k + 1] for k in range(2)]
    chosen_total = sum(
        jnp.sum(jnp.where(picked[k], powers, 0.0), axis=1, keepdims=True) for k in range(2)
    )
    weighted = grad_gates[0] * gates[:, 0:1] + grad_gates[1] * gates[:, 1:2]
    grad_mass = (AUX_WEIGHT * experts / (2.0 * token_total * token_total)) * counts[0:1, :]
    grad_mass = jnp.where(inside, grad_mass, 0.0)
    for k in range(2):
        grad_mass = grad_mass + jnp.where(picked[k], (grad_gates[k] - weighted) / chosen_total, 0.0)
    grad_logits = powers * (grad_mass - jnp.sum(powers * grad_mass, axis=1, keepdims=True))
    extra = plane[:, lanes.base :]
    grad_routed = grad_routed + contract_last(grad_logits.astype(BF16), extra)
    hidden_state = hidden[...]
    scale = lax.rsqrt(jnp.mean(hidden_state * hidden_state, axis=1, keepdims=True) + EPSILON)
    normed = hidden_state * scale
    product = grad_routed * normed
    gain_grad = jnp.sum(product, axis=0, keepdims=True)
    small_t = matmul(grad_logits.T.astype(BF16), routed[...])
    row = lax.broadcasted_iota(jnp.int32, small_t.shape, 0)
    small_t = jnp.where(row == lanes.gain, gain_grad, small_t)
    small[...] = small_t.T
    gains = extra.astype(F32).T[lanes.gain : lanes.gain + 1]
    grad = scale * (
        grad_routed * gains - normed * jnp.mean(product * gains, axis=1, keepdims=True)
    ) + grad_output
    grad_hidden[...] = grad
    grad_branch[...] = grad.astype(BF16)


def context_grad_kernel(
    fsdp_index, grad_branch, attention_out, context, grad_t, grad_n, grad_out, total, *, heads, width
):
    @pl.when(pl.program_id(0) == 0)
    def _():
        total[...] = jnp.zeros_like(total)

    branch = grad_branch[0]
    grad = contract_last(attention_out[...], branch).astype(BF16)
    for head in range(heads):
        part = grad[head * width : (head + 1) * width]
        grad_t[head] = part
        grad_n[head] = turned(part).astype(BF16)
    total[...] += matmul(context[0], branch)

    @pl.when(pl.program_id(0) == pl.num_programs(0) - 1)
    def _():
        grad_out[...] = total[...].astype(BF16)


def project_back_kernel(
    grad_projected, normed, plane, small, probabilities, grad_bias, grad_first, grad_plane, total,
    bias_t, *, lanes, heads, feature_rows, bucket_rows,
):
    step = pl.program_id(0)

    @pl.when(step == 0)
    def _():
        total[...] = jnp.zeros_like(total)

    grad = grad_projected[...]
    grad_first[0] = matmul(plane[:, : lanes.weights], grad).astype(BF16)
    total[: lanes.weights, :] += matmul(grad, normed[...])

    @pl.when(step == pl.num_programs(0) - 1)
    def _():
        grad_plane[...] = total[...].T.astype(BF16)
        span = grad_bias.shape[2]
        select, _ = bucket_rows_select(plane.shape[0], feature_rows, bucket_rows, span)
        bias_t[...] = jnp.zeros_like(bias_t)
        first = lanes.table + lax.axis_index("fsdp") * heads
        for head in range(heads):
            bias_t[pl.ds(first + head, 1), :] = grad_bias[head]
        high = bias_t[...].astype(BF16)
        rest = (bias_t[...] - high.astype(F32)).astype(BF16)
        table = contract_last(select, high) + contract_last(select, rest)
        mass = jnp.sum(probabilities[...], axis=0, keepdims=True)
        mass = pltpu.roll(jnp.broadcast_to(mass, (8, lanes.extra)), lanes.shift, 1)[0:1]
        lane = lax.broadcasted_iota(jnp.int32, table.shape, 1)
        row = lax.broadcasted_iota(jnp.int32, table.shape, 0)
        is_small = (lane >= lanes.router) & (lane < lanes.table)
        is_mass = (lane >= lanes.count) & (lax.rem(row, feature_rows) == 0)
        extra = table + jnp.where(is_small, small[...], 0.0) + jnp.where(is_mass, mass, 0.0)
        grad_plane[:, lanes.base :] = (total[lanes.base :, :].T + extra).astype(BF16)


def last_kernel(
    first, planes, out_grad, first_parts, plane_parts, out_parts,
    first_in, first_sum, planes_in, plane_sum, along_in, reduced, send, receive, own, *, spread_out,
):
    grid = Grid().here()
    links = Links(send, receive)
    z_size, y_size, x_size, fsdp_size = grid.z_size, grid.y_size, grid.x_size, grid.fsdp_size
    exp_size = grid.exp_size
    sibling = grid.sibling(grid.fsdp)
    near = [
        (grid.exp, (grid.fsdp + turn) % fsdp_size) for turn in range(1, fsdp_size)
    ] + [grid.at(z=(grid.z + hop) % z_size) for hop in range(1, z_size)]
    beside = [grid.at(y=(grid.y + hop) % y_size) for hop in range(1, y_size)]

    per_sender = grid.device_count if spread_out else exp_size
    base = 0 if spread_out else grid.fsdp * exp_size
    out_sends = []
    for number in range(per_sender):
        to = base + number
        out_sends.append((to, number))
    if spread_out:
        out_origins = [(origin, origin) for origin in range(grid.device_count)]
    else:
        out_origins = [
            (member * fsdp_size + grid.linear // exp_size, member) for member in range(exp_size)
        ]
    own_slot = grid.linear if spread_out else grid.exp
    out_base = links.used
    links.used += per_sender

    def place_of(linear):
        return (linear // fsdp_size, linear % fsdp_size)

    def out_copy(to, number, slot):
        return pltpu.make_async_remote_copy(
            src_ref=out_grad.at[number], dst_ref=out_parts.at[slot],
            send_sem=send.at[out_base + number], recv_sem=receive.at[out_base + slot],
            device_id=place_of(to), device_id_type=MESH,
        )

    barrier = pltpu.get_barrier_semaphore()
    for device in near + beside:
        pl.semaphore_signal(barrier, inc=1, device_id=device, device_id_type=MESH)
    for origin, _ in out_origins:

        @pl.when(origin != grid.linear)
        def _(origin=origin):
            pl.semaphore_signal(
                barrier, inc=1, device_id=place_of(origin), device_id_type=MESH
            )

    to_self = (
        1 if spread_out else jnp.where(grid.linear // exp_size == grid.fsdp, 1, 0)
    )
    pl.semaphore_wait(barrier, len(near) + len(beside) + per_sender - to_self)

    first_copies = []
    for hop in range(x_size):
        mine = grid.x_from(hop)
        first_copies.append(
            links.copy(
                first.at[grid.sibling(mine)], first_in.at[hop], (grid.exp, sibling), first_in.at[hop]
            )
        )
        first_copies[-1][0].start()
    z_hops = list(range(1, z_size)) + [0]
    beside_copies = []
    for z_hop in z_hops:
        beside_copies.append([])
        for hop in range(1, y_size):
            to = (grid.y + hop) % y_size
            landing = planes_in.at[hop - 1, z_hop]
            beside_copies[-1].append(
                links.copy(
                    planes.at[(grid.z + z_hop) % z_size, to], landing, grid.at(y=to), landing
                )
            )
            beside_copies[-1][-1][0].start()
    for to, number in out_sends:

        @pl.when(to != grid.linear)
        def _(to=to, number=number):
            out_copy(to, number, own_slot).start()

        @pl.when(to == grid.linear)
        def _(number=number):
            pltpu.make_async_copy(out_grad.at[number], out_parts.at[own_slot], own.at[0]).start()

    along_x = []
    for hop in range(x_size):
        first_copies[hop][1].wait_recv()
        summed = first[grid.x_from(hop)].astype(F32) + first_in[hop].astype(F32)
        if hop == 0:
            first_parts[0] = summed.astype(BF16)
        else:
            first_sum[hop - 1] = summed.astype(BF16)
            along_x.append(
                links.copy(
                    first_sum.at[hop - 1], first_parts.at[hop], (grid.exp, grid.x_from(hop)),
                    first_parts.at[hop],
                )
            )
            along_x[-1][0].start()
    along_z = []
    for z_hop, copies in zip(z_hops, beside_copies):
        to_z = (grid.z + z_hop) % z_size
        summed = planes[to_z, grid.y].astype(F32)
        for number, (_, coming) in enumerate(copies):
            coming.wait_recv()
            summed = summed + planes_in[number, z_hop].astype(F32)
        plane_sum[z_hop] = summed.astype(BF16)
        if z_hop > 0:
            along_z.append(
                links.copy(
                    plane_sum.at[z_hop], along_in.at[z_hop - 1], grid.at(z=to_z),
                    along_in.at[z_hop - 1],
                )
            )
            along_z[-1][0].start()
    summed = plane_sum[0].astype(F32)
    for number, (_, coming) in enumerate(along_z):
        coming.wait_recv()
        summed = summed + along_in[number].astype(F32)
    reduced[...] = summed.astype(BF16)
    placed = []
    for turn in range(1, fsdp_size):
        to = (grid.fsdp + turn) % fsdp_size
        origin = (grid.fsdp + fsdp_size - turn) % fsdp_size
        placed.append(
            links.copy(
                reduced.at[to], plane_parts.at[grid.fsdp], (grid.exp, to), plane_parts.at[origin]
            )
        )
        placed[-1][0].start()
    kept = pltpu.make_async_copy(reduced.at[grid.fsdp], plane_parts.at[grid.fsdp], own.at[1])
    kept.start()
    for going, coming in along_x + placed:
        coming.wait_recv()
    for going, _ in first_copies + along_x + along_z + placed:
        going.wait_send()
    for copies in beside_copies:
        for going, _ in copies:
            going.wait_send()
    kept.wait()
    for origin, slot in out_origins:

        @pl.when(origin != grid.linear)
        def _(origin=origin, slot=slot):
            out_copy(origin, 0, slot).wait_recv()

    for to, number in out_sends:

        @pl.when(to != grid.linear)
        def _(to=to, number=number):
            out_copy(to, number, own_slot).wait_send()

        @pl.when(to == grid.linear)
        def _(number=number):
            pltpu.make_async_copy(out_grad.at[number], out_parts.at[own_slot], own.at[0]).wait()


def mixture_kernel(hidden, gates, columns, rows_in, output, *, local):
    members, _, capacity, model_width = rows_in.shape
    routes, slots = int_columns(columns)
    total = hidden[...]
    picked = [jnp.zeros(hidden.shape, F32), jnp.zeros(hidden.shape, F32)]
    for index in range(local):
        picks = local_picks(routes, slots, capacity, local, index, members * capacity)
        values = rows_in[:, index].reshape(members * capacity, model_width)
        for k in range(2):
            picked[k] = picked[k] + matmul(jnp.where(picks[k], 1.0, 0.0).astype(BF16), values)
    for k in range(2):
        total = total + gates[:, k : k + 1] * picked[k]
    output[...] = total.astype(BF16)


def finish_kernel(
    first_parts, plane_parts, out_parts, tokens, grad_hidden, attention_in, attention_gain, counts,
    grad_tokens, grad_gain, grad_in, grad_out, grad_mixture, grad_router, grad_table, balance,
    *, lanes, heads, width, head_count, experts, token_total,
):
    total = jnp.sum(first_parts[...].astype(F32), axis=0).T
    inputs = tokens[...].astype(F32)
    scale = lax.rsqrt(jnp.mean(inputs * inputs, axis=1, keepdims=True) + EPSILON)
    normed = inputs * scale
    grad_tokens[...] = grad_hidden[...] + scale * (
        total - normed * jnp.mean(total * normed, axis=1, keepdims=True)
    )
    fsdp_size = plane_parts.shape[0]
    model_width = head_count * width
    sums = [plane_parts[place].astype(F32) for place in range(fsdp_size)]
    columns = []
    for kind in range(3):
        pieces = [
            sums[place][:, kind * heads * width : (kind + 1) * heads * width]
            for place in range(fsdp_size)
        ]
        columns.append(jnp.concatenate(pieces, axis=1)[:, :model_width])
    gathered = jnp.concatenate(columns, axis=1)
    feature_rows = gathered.shape[0]
    gain = jnp.sum(gathered * attention_in[...].astype(F32), axis=1, keepdims=True)
    gain = padded_rows(jnp.broadcast_to(gain, (feature_rows, 128)), 128).T
    grad_gain[...] = gain[0:1, :feature_rows]
    grad_in[...] = gathered * as_column(attention_gain[...], feature_rows)
    grad_out[...] = jnp.sum(out_parts[...].astype(F32), axis=0)
    extra = sum(part[:, lanes.base :] for part in sums)
    extra_t = padded_rows(extra, 128).T
    grad_mixture[...] = extra_t[lanes.gain : lanes.gain + 1, :feature_rows]
    grad_router[...] = extra_t[lanes.router : lanes.router + experts, :feature_rows]
    grad_table[...] = extra[: grad_table.shape[0], lanes.table : lanes.table + head_count]
    mass = jnp.broadcast_to(extra[0:1], (8, lanes.extra))
    mass = pltpu.roll(mass, lanes.extra - lanes.shift, 1)
    lane = expert_lane(mass.shape, lanes)
    terms = jnp.where((lane >= 0) & (lane < experts), mass * counts[...], 0.0)[0:1]
    balance[...] = jnp.sum(terms, axis=1, keepdims=True) * (
        experts / (2.0 * token_total * token_total)
    )


def sum_kernel(*refs, local, terms):
    outputs = refs[2 * local * terms :]
    for which in range(2):
        for index in range(local):
            first = (index * 2 + which) * terms
            shape = outputs[which].shape[1:]
            total = refs[first][...].reshape(shape).astype(F32)
            for ref in refs[first + 1 : first + terms]:
                total = total + ref[...].reshape(shape).astype(F32)
            outputs[which][index] = total


def sum_grads(groups, up_shape, down_shape, blocks):
    local = len(groups)
    depth, part = up_shape[1], down_shape[1]
    sizes = ((depth, part), (part // blocks, down_shape[2]))
    arrays, specs = [], []
    for group in groups:
        for size, (keep, taken, passed) in zip(sizes, group):
            for array in (keep, taken, *passed):
                arrays.append(array)
                specs.append(pl.BlockSpec(size, lambda c: (c, 0)))
    return pl.pallas_call(
        partial(sum_kernel, local=local, terms=len(arrays) // (2 * local)),
        grid=(blocks,),
        in_specs=specs,
        out_specs=[
            pl.BlockSpec((local, depth, part), lambda c: (0, 0, c)),
            pl.BlockSpec((local, part // blocks, down_shape[2]), lambda c: (0, c, 0)),
        ],
        out_shape=(shape_of(up_shape, F32), shape_of(down_shape, F32)),
        compiler_params=params(),
        cost_estimate=hint(8),
        name="sum_grads",
    )(*arrays)


def over_x(array, hop):
    fsdp_size = lax.axis_size("fsdp")
    return lax.ppermute(array, "fsdp", [(i, (i + 2 * hop) % fsdp_size) for i in range(fsdp_size)])


def over_core(array):
    return lax.ppermute(array, "fsdp", [(i, i ^ 1) for i in range(lax.axis_size("fsdp"))])


def on_device(
    tokens,
    cotangent,
    segments,
    routes,
    slots,
    attention_gain,
    mixture_gain,
    attention_in,
    attention_out,
    router_weight,
    position_table,
    expert_up,
    expert_down,
):
    grid = Grid()
    exp_size, fsdp_size, chips = grid.exp_size, grid.fsdp_size, grid.x_size
    device_count = grid.device_count
    fsdp_index = lax.axis_index("fsdp")
    rows, model_width = tokens.shape
    length = rows * fsdp_size
    head_count = position_table.shape[1]
    width = model_width // head_count
    heads = -(-head_count // fsdp_size)
    padded_heads = heads * fsdp_size
    feature_rows, bucket_rows = attention_in.shape[0], position_table.shape[0]
    experts = router_weight.shape[1]
    local = expert_up.shape[0]
    capacity = 4 * rows // experts
    token_total = rows * device_count
    span = WINDOW + 2 * SKEW + QUERY_BLOCK
    lanes = Lanes(heads, width, padded_heads, experts)
    part = expert_down.shape[1]
    gain_row = attention_gain.reshape(1, feature_rows)

    shard_shapes = [shape_of((model_width, part), BF16), shape_of((part, model_width), BF16)]
    copies = (
        4 * fsdp_size + grid.z_size + grid.z_size * grid.y_size
        + grid.z_size + grid.y_size + grid.x_size + 1
    )
    started = pl.pallas_call(
        partial(
            start_kernel, lanes=lanes, heads=heads, width=width, head_count=head_count,
            experts=experts, capacity=capacity, local=local,
        ),
        out_shape=tuple(
            [
                shape_of((fsdp_size, rows, model_width), BF16),
                shape_of((grid.z_size, grid.y_size, fsdp_size, feature_rows, lanes.width), BF16),
                shape_of((experts * capacity, model_width), BF16),
                shape_of((8, rows), F32),
                shape_of((rows, 128), F32),
                shape_of((grid.z_size, grid.y_size, chips, 2, feature_rows, model_width), BF16),
            ]
            + shard_shapes * local
        ),
        in_specs=[IN_VMEM] * 10 + [ANYWHERE] * 2,
        out_specs=tuple(
            [ANYWHERE, ANYWHERE, IN_VMEM, IN_VMEM, IN_VMEM, ANYWHERE] + [ANYWHERE] * (2 * local)
        ),
        scratch_shapes=[
            pltpu.VMEM((fsdp_size, feature_rows, lanes.width), BF16),
            pltpu.VMEM(expert_up.shape, BF16),
            pltpu.VMEM(expert_down.shape, BF16),
            dma_sems(copies),
            dma_sems(copies),
            dma_sems(3),
            dma_sems(2 * local),
            dma_sems(local * (fsdp_size + 1)),
        ],
        compiler_params=params(collective_id=0, has_side_effects=True),
        cost_estimate=hint(20),
        name="start",
    )(
        tokens, cotangent, routes.T, slots.T, gain_row, mixture_gain.reshape(1, feature_rows),
        attention_in, router_weight.T, position_table, attention_out, expert_up, expert_down,
    )
    all_tokens, all_planes, cotangent_slots, position_rows, columns, full_out = started[:6]
    own_shards = [started[6 + 2 * index : 8 + 2 * index] for index in range(local)]
    plane = all_planes.reshape(model_width, lanes.width)
    full_out = full_out.reshape(model_width, model_width)

    def along_x(array):
        return [over_x(array, -hop) for hop in range(1, chips)]

    near_up, near_down = [None] * local, [None] * local
    near_up[0] = along_x(own_shards[0][0])
    cotangent_in = lax.all_to_all(
        cotangent_slots.reshape(exp_size, local * capacity, model_width),
        "exp", split_axis=0, concat_axis=0, tiled=True,
    ).reshape(exp_size, local, capacity, model_width)

    head_t = lambda size: pl.BlockSpec((heads, size, rows), lambda s, *_: (0, 0, s))
    head_n = lambda size: pl.BlockSpec((heads, rows, size), lambda s, *_: (0, s, 0))
    normed, query_t, key_n, query_n, value_n, key_t, value_t, bias, counts = pl.pallas_call(
        partial(
            project_kernel, heads=heads, width=width, lanes=lanes, feature_rows=feature_rows,
            bucket_rows=bucket_rows,
        ),
        grid=(fsdp_size,),
        in_specs=[
            pl.BlockSpec((1, rows, model_width), lambda s: (s, 0, 0)),
            whole((model_width, lanes.width)),
            pl.BlockSpec((1, rows), lambda s: (0, s)),
        ],
        out_specs=[
            pl.BlockSpec((rows, model_width), lambda s: (s, 0)),
            head_t(SKEW), head_n(SKEW), head_n(width), head_n(width), head_t(width), head_t(width),
            whole((heads, 1, span)),
            whole((8, lanes.extra)),
        ],
        out_shape=(
            shape_of((length, model_width), BF16),
            shape_of((heads, SKEW, length), BF16),
            shape_of((heads, length, SKEW), BF16),
            shape_of((heads, length, width), BF16),
            shape_of((heads, length, width), BF16),
            shape_of((heads, width, length), BF16),
            shape_of((heads, width, length), BF16),
            shape_of((heads, 1, span), F32),
            shape_of((8, lanes.extra), F32),
        ),
        scratch_shapes=[
            pltpu.VMEM((lanes.weights, model_width), BF16),
            pltpu.VMEM((lanes.extra, span), F32),
        ],
        compiler_params=params(),
        cost_estimate=hint(8),
        name="project",
    )(all_tokens, plane, segments.reshape(1, length))

    by_head = lambda *size: pl.BlockSpec((1,) + size, lambda h: (h, 0, 0))
    context, context_high, log_total = pl.pallas_call(
        partial(attend_kernel, rows=rows),
        grid=(heads,),
        in_specs=[
            by_head(SKEW, length), by_head(length, SKEW), by_head(width, length), by_head(1, span),
        ],
        out_specs=[
            pl.BlockSpec((fsdp_size, width, rows), lambda h: (0, h, 0)),
            by_head(width, length),
            by_head(1, length),
        ],
        out_shape=(
            shape_of((fsdp_size, heads * width, rows), BF16),
            shape_of((heads, width, length), F32),
            shape_of((heads, 1, length), F32),
        ),
        scratch_shapes=[
            pltpu.VMEM((SKEW, span), F32),
            pltpu.VMEM((WINDOW + QUERY_BLOCK, QUERY_BLOCK), F32),
        ],
        compiler_params=params(),
        cost_estimate=hint(13),
        name="attend",
    )(query_t, key_n, value_t, bias)

    (attended_t,) = exchange("fsdp", [(context, None)], 1, 9)
    own_down, near_up[0], attended_t = lax.optimization_barrier(
        (own_shards[0][1], near_up[0], attended_t)
    )
    near_down[0] = along_x(own_down)
    attended_t = attended_t.reshape(padded_heads * width, rows)

    gate_lanes = -(-local * capacity // 128) * 128
    hidden, routed, probabilities, gates, outgoing, slot_gates = pl.pallas_call(
        partial(route_kernel, experts=experts, lanes=lanes, capacity=capacity),
        out_shape=(
            shape_of((rows, model_width), F32),
            shape_of((rows, model_width), BF16),
            shape_of((rows, lanes.extra), F32),
            shape_of((rows, 2), F32),
            shape_of((experts * capacity, model_width), BF16),
            shape_of((exp_size, 8, gate_lanes), F32),
        ),
        compiler_params=params(),
        cost_estimate=hint(7),
        name="route",
    )(tokens, attended_t, full_out, plane, columns, position_rows)

    later = [own_shards[index] for index in range(1, local)]
    outgoing, later = lax.optimization_barrier((outgoing, later))
    for index in range(1, local):
        near_up[index], near_down[index] = [along_x(array) for array in later[index - 1]]
    outgoing = outgoing.reshape(exp_size, local, capacity, model_width)

    def pass_along(arrays):
        return [over_x(arrays[0][hop - 1], hop) for hop in range(1, chips)]

    rows_in, gates_in = exchange("exp", [(outgoing, 0), (slot_gates, None)], 2, 28)
    returned, groups, moved, outs, swapped = [], [], [], None, ()
    for index in range(local):
        final = index == local - 1
        carried = list(moved) if final else list(moved) + [(outgoing, index + 1)]
        result = run_expert(
            index, local, outgoing, slot_gates, rows_in, gates_in, cotangent_in,
            [own_shards[index][0]] + near_up[index], [own_shards[index][1]] + near_down[index],
            swapped, () if final else own_shards[index + 1], carried, outs, 3 + index,
        )
        (outs,) = result.rows_out
        arrived = list(result.moved_to)
        if not final:
            rows_in = arrived.pop()
            swapped = result.next_swapped
            moved = [(result.grad_rows[0], None), (result.grad_gates[0], None)]
        if arrived:
            returned.append(arrived)
        up_keep, up_taken, down_keep, down_taken = result.own
        if not final:
            passed = (result.pass_up, result.pass_down)
            passed, rows_in = lax.optimization_barrier((passed, rows_in))
            groups.append(
                [
                    (up_keep, up_taken, pass_along(passed[0])),
                    (down_keep, down_taken, pass_along(passed[1])),
                ]
            )
    returned.append([result.back_rows[0], result.back_gates[0]])
    groups, returned = lax.optimization_barrier((groups, returned))

    outs, returned = lax.optimization_barrier((outs, returned))
    out_rows = lax.all_to_all(outs, "exp", split_axis=0, concat_axis=0, tiled=True)

    grad_hidden, grad_branch, small = pl.pallas_call(
        partial(
            unroute_kernel, experts=experts, local=local, token_total=token_total, lanes=lanes
        ),
        out_shape=(
            shape_of((rows, model_width), F32),
            shape_of((rows, model_width), BF16),
            shape_of((model_width, lanes.extra), F32),
        ),
        compiler_params=params(),
        cost_estimate=hint(1),
        name="unroute",
    )(
        hidden, cotangent, routed, probabilities, gates, plane, columns, counts,
        *[part[0] for part in returned], *[part[1] for part in returned],
    )

    all_branch = gather_rows(grad_branch, 4 + local, 1)
    passed, all_branch = lax.optimization_barrier(((result.pass_up, result.pass_down), all_branch))
    groups.append(
        [
            (up_keep, up_taken, pass_along(passed[0])),
            (down_keep, down_taken, pass_along(passed[1])),
        ]
    )
    padded_out = full_out
    if padded_heads > head_count:
        padded_out = jnp.pad(full_out, ((0, padded_heads * width - model_width), (0, 0)))
    grad_t, grad_n, out_grad = pl.pallas_call(
        partial(context_grad_kernel, heads=heads, width=width),
        grid_spec=pltpu.PrefetchScalarGridSpec(
            num_scalar_prefetch=1,
            grid=(fsdp_size,),
            in_specs=[
                pl.BlockSpec((1, rows, model_width), lambda s, f: (s, 0, 0)),
                pl.BlockSpec((heads * width, model_width), lambda s, f: (f[0], 0)),
                pl.BlockSpec((1, heads * width, rows), lambda s, f: (s, 0, 0)),
            ],
            out_specs=[head_t(width), head_n(width), whole((heads * width, model_width))],
            scratch_shapes=[pltpu.VMEM((heads * width, model_width), F32)],
        ),
        out_shape=(
            shape_of((heads, width, length), BF16),
            shape_of((heads, length, width), BF16),
            shape_of((heads * width, model_width), BF16),
        ),
        compiler_params=params(),
        cost_estimate=hint(1),
        name="context_grad",
    )(fsdp_index.reshape(1), all_branch, padded_out, context)

    grad_projected, grad_bias = pl.pallas_call(
        partial(attend_back_kernel, scale=width ** (-0.5)),
        grid=(heads,),
        in_specs=[
            by_head(SKEW, length), by_head(length, SKEW), by_head(length, width),
            by_head(length, width), by_head(width, length), by_head(width, length),
            by_head(length, width), by_head(width, length), by_head(1, length), by_head(1, span),
        ],
        out_specs=[
            pl.BlockSpec((3, 1, width, length), lambda h: (0, h, 0, 0)),
            by_head(1, span),
        ],
        out_shape=(
            shape_of((3, heads, width, length), BF16),
            shape_of((heads, 1, span), F32),
        ),
        scratch_shapes=[
            pltpu.VMEM((SKEW, span), F32),
            pltpu.VMEM((SKEW, span), F32),
            pltpu.VMEM((length, width), F32),
            pltpu.VMEM((length, width), F32),
        ],
        compiler_params=params(),
        cost_estimate=hint(1),
        name="attend_back",
    )(query_t, key_n, query_n, value_n, key_t, grad_t, grad_n, context_high, log_total, bias)
    grad_projected = grad_projected.reshape(lanes.weights, length)

    grad_first, grad_plane = pl.pallas_call(
        partial(
            project_back_kernel, lanes=lanes, heads=heads, feature_rows=feature_rows,
            bucket_rows=bucket_rows,
        ),
        grid=(fsdp_size,),
        in_specs=[
            pl.BlockSpec((lanes.weights, rows), lambda s: (0, s)),
            pl.BlockSpec((rows, model_width), lambda s: (s, 0)),
            whole((model_width, lanes.width)),
            whole((model_width, lanes.extra)),
            whole((rows, lanes.extra)),
            whole((heads, 1, span)),
        ],
        out_specs=[
            pl.BlockSpec((1, model_width, rows), lambda s: (s, 0, 0)),
            whole((model_width, lanes.width)),
        ],
        out_shape=(
            shape_of((fsdp_size, model_width, rows), BF16),
            shape_of((model_width, lanes.width), BF16),
        ),
        scratch_shapes=[
            pltpu.VMEM((lanes.width, model_width), F32),
            pltpu.VMEM((lanes.extra, span), F32),
        ],
        compiler_params=params(),
        cost_estimate=hint(1),
        name="project_back",
    )(grad_projected, normed, plane, small, probabilities, grad_bias)

    out_rows, grad_first = lax.optimization_barrier((out_rows, grad_first))
    spread_out = heads * width * fsdp_size != model_width
    if spread_out:
        out_grad = lax.dynamic_update_slice(
            jnp.zeros((padded_heads * width, model_width), BF16), out_grad,
            (fsdp_index * heads * width, jnp.int32(0)),
        )[:model_width]
    out_grad = out_grad.reshape(-1, feature_rows, model_width)
    out_count = device_count if spread_out else exp_size
    plane_shape = (grid.z_size, grid.y_size, fsdp_size, feature_rows, lanes.width)
    parts_shape = (fsdp_size, feature_rows, lanes.width)
    copies = 3 * fsdp_size + grid.z_size * grid.y_size + grid.z_size + out_count
    first_parts, plane_parts, out_parts = pl.pallas_call(
        partial(last_kernel, spread_out=spread_out),
        out_shape=(
            shape_of((chips, model_width, rows), BF16),
            shape_of(parts_shape, BF16),
            shape_of((out_count, feature_rows, model_width), BF16),
        ),
        in_specs=[IN_VMEM] * 3,
        out_specs=(IN_VMEM, ANYWHERE, ANYWHERE),
        scratch_shapes=[
            pltpu.VMEM((chips, model_width, rows), BF16),
            pltpu.VMEM((max(chips - 1, 1), model_width, rows), BF16),
            pltpu.VMEM((max(grid.y_size - 1, 1), grid.z_size) + parts_shape, BF16),
            pltpu.VMEM((grid.z_size,) + parts_shape, BF16),
            pltpu.VMEM((max(grid.z_size - 1, 1),) + parts_shape, BF16),
            pltpu.VMEM(parts_shape, BF16),
            dma_sems(copies),
            dma_sems(copies),
            dma_sems(2),
        ],
        compiler_params=params(collective_id=5 + local, has_side_effects=True),
        cost_estimate=hint(1),
        name="last",
    )(grad_first, grad_plane.reshape(plane_shape), out_grad)

    groups, first_parts = lax.optimization_barrier((groups, first_parts))
    (
        grad_tokens, gain_grad, in_grad, out_sum, mixture_gain_grad, router_grad, table_grad, balance,
    ) = pl.pallas_call(
        partial(
            finish_kernel, lanes=lanes, heads=heads, width=width, head_count=head_count,
            experts=experts, token_total=token_total,
        ),
        out_shape=(
            shape_of((rows, model_width), F32),
            shape_of((1, feature_rows), F32),
            shape_of((feature_rows, 3 * model_width), F32),
            shape_of((feature_rows, model_width), F32),
            shape_of((1, feature_rows), F32),
            shape_of((experts, feature_rows), F32),
            shape_of((bucket_rows, head_count), F32),
            shape_of((1, 1), F32),
        ),
        compiler_params=params(),
        cost_estimate=hint(6),
        name="finish",
    )(first_parts, plane_parts, out_parts, tokens, grad_hidden, attention_in, gain_row, counts)

    layer_output = pl.pallas_call(
        partial(mixture_kernel, local=local),
        out_shape=shape_of((rows, model_width), BF16),
        compiler_params=params(),
        cost_estimate=hint(5),
        name="mixture",
    )(hidden, gates, columns, out_rows)

    up_grad, down_grad = sum_grads(groups, expert_up.shape, expert_down.shape, fsdp_size)
    return (
        layer_output,
        balance.reshape(()),
        grad_tokens,
        gain_grad.reshape(feature_rows),
        mixture_gain_grad.reshape(feature_rows),
        in_grad,
        out_sum,
        router_grad.T,
        table_grad,
        up_grad,
        down_grad,
    )


def solution(mesh):
    in_specs = (
        P(("exp", "fsdp"), None),
        P(("exp", "fsdp"), None),
        P("exp"),
        P(("exp", "fsdp"), None),
        P(("exp", "fsdp"), None),
        P(("exp", "fsdp")),
        P(("exp", "fsdp")),
        P(("exp", "fsdp"), None),
        P(("exp", "fsdp"), None),
        P(("exp", "fsdp"), None),
        P(("exp", "fsdp"), None),
        P("exp", "fsdp", None),
        P("exp", "fsdp", None),
    )
    out_specs = (
        P(("exp", "fsdp"), None),
        P(),
        P(("exp", "fsdp"), None),
        P(("exp", "fsdp")),
        P(("exp", "fsdp")),
        P(("exp", "fsdp"), None),
        P(("exp", "fsdp"), None),
        P(("exp", "fsdp"), None),
        P(("exp", "fsdp"), None),
        P("exp", "fsdp", None),
        P("exp", "fsdp", None),
    )
    return jax.shard_map(
        on_device, mesh=mesh, in_specs=in_specs, out_specs=out_specs, check_vma=False
    )
```

```python
from functools import partial

import jax
import jax.numpy as jnp
from jax import lax
from jax.experimental import pallas as pl
from jax.experimental.pallas import tpu as pltpu
from jax.sharding import PartitionSpec as P

WINDOW = 1024
BUCKETS = 256

EPSILON = 1e-06
AUX_WEIGHT = 0.01
MASKED = -1e30
QUERY_BLOCK = 256
SKEW = 128
VMEM_BYTES = 58 * 1024 * 1024
MESH = pl.DeviceIdType.MESH
F32 = jnp.float32
BF16 = jnp.bfloat16


def params(**kwargs):
    return pltpu.CompilerParams(vmem_limit_bytes=VMEM_BYTES, **kwargs)


def shape_of(shape, dtype):
    return jax.ShapeDtypeStruct(shape, dtype)


def whole(shape):
    return pl.BlockSpec(shape, lambda *_: (0,) * len(shape))


def contract_last(left_side, right_side):
    return lax.dot_general(
        left_side, right_side, (((1,), (1,)), ((), ())), preferred_element_type=F32
    )


def contract_first(left_side, right_side):
    return lax.dot_general(
        left_side, right_side, (((0,), (0,)), ((), ())), preferred_element_type=F32
    )


def matmul(left_side, right_side):
    return jnp.dot(left_side, right_side, preferred_element_type=F32)


def turned(value):
    return value.astype(F32).T


def bucket_index(distance):
    near_count = BUCKETS // 2
    spread = max(WINDOW - near_count, 1)
    far_bucket = (
        near_count + jnp.maximum(distance - near_count, 0) * (BUCKETS - near_count) // spread
    )
    return jnp.where(distance < near_count, distance, far_bucket)

def hint(micros):
    return pl.CostEstimate(flops=int(micros * 1.0e9), bytes_accessed=1024, transcendentals=0)


class Grid:
    def __init__(self):
        self.exp_size, self.fsdp_size = lax.axis_size("exp"), lax.axis_size("fsdp")
        self.device_count = self.exp_size * self.fsdp_size
        self.y_size = max(
            y for y in range(1, self.exp_size + 1) if self.exp_size % y == 0 and 2 * y * y <= self.exp_size
        ) if self.exp_size > 1 else 1
        self.z_size = self.exp_size // self.y_size
        self.x_size = self.fsdp_size // 2

    def here(self):
        self.exp, self.fsdp = lax.axis_index("exp"), lax.axis_index("fsdp")
        self.z, self.y = self.exp // self.y_size, self.exp % self.y_size
        self.x, self.core = self.fsdp // 2, self.fsdp % 2
        self.linear = self.exp * self.fsdp_size + self.fsdp
        return self

    def at(self, z=None, y=None, fsdp=None):
        z = self.z if z is None else z
        y = self.y if y is None else y
        return (z * self.y_size + y, self.fsdp if fsdp is None else fsdp)

    def x_from(self, hop):
        return ((self.x + self.x_size + hop) % self.x_size) * 2 + self.core

    def sibling(self, fsdp):
        return fsdp + 1 - 2 * (fsdp % 2)


class Links:
    def __init__(self, send, receive):
        self.send, self.receive, self.used = send, receive, 0

    def copy(self, source, target, device, landing):
        index = self.used
        self.used += 1
        going = pltpu.make_async_remote_copy(
            src_ref=source, dst_ref=target, send_sem=self.send.at[index],
            recv_sem=self.receive.at[index], device_id=device, device_id_type=MESH,
        )
        coming = pltpu.make_async_remote_copy(
            src_ref=landing, dst_ref=landing, send_sem=self.send.at[index],
            recv_sem=self.receive.at[index], device_id=device, device_id_type=MESH,
        )
        return going, coming


def greet(devices):
    barrier = pltpu.get_barrier_semaphore()
    for device in devices:
        pl.semaphore_signal(barrier, inc=1, device_id=device, device_id_type=MESH)
    pl.semaphore_wait(barrier, len(devices))


def chip_peers(grid):
    peers = [(grid.exp, grid.sibling(grid.fsdp))]
    return peers + [(grid.exp, grid.x_from(hop)) for hop in range(1, grid.x_size)]


class ChipGather:
    def __init__(self, grid, links, own_sem, source, target):
        self.grid, self.links, self.target = grid, links, target
        self.own = pltpu.make_async_copy(source, target.at[grid.fsdp], own_sem)
        sibling = grid.sibling(grid.fsdp)
        self.along_x, self.across = [], []
        for hop in range(1, grid.x_size):
            self.along_x.append(
                links.copy(
                    source, target.at[grid.fsdp], (grid.exp, grid.x_from(hop)),
                    target.at[grid.x_from(-hop)],
                )
            )
        self.across.append(
            links.copy(source, target.at[grid.fsdp], (grid.exp, sibling), target.at[sibling])
        )

    def start(self):
        for going, _ in self.along_x + self.across:
            going.start()
        self.own.start()

    def forward(self):
        grid = self.grid
        for hop in range(1, grid.x_size):
            self.along_x[hop - 1][1].wait_recv()
            held = grid.x_from(-hop)
            other = grid.sibling(held)
            self.across.append(
                self.links.copy(
                    self.target.at[held], self.target.at[held],
                    (grid.exp, grid.sibling(grid.fsdp)), self.target.at[other],
                )
            )
            self.across[-1][0].start()

    def finish(self):
        for _, coming in self.across:
            coming.wait_recv()
        for going, _ in self.along_x + self.across:
            going.wait_send()
        self.own.wait()


class Exchange:
    def __init__(self, grid, axis, links, own_sems, pairs):
        size = grid.exp_size if axis == "exp" else grid.fsdp_size
        place = grid.exp if axis == "exp" else grid.fsdp
        device = (lambda to: (to, grid.fsdp)) if axis == "exp" else (lambda to: (grid.exp, to))
        self.peers = [device((place + hop) % size) for hop in range(1, size)]
        self.copies, self.own = [], []
        for index, (source, target) in enumerate(pairs):
            for hop in range(1, size):
                to, origin = (place + hop) % size, (place + size - hop) % size
                self.copies.append(
                    links.copy(source(to), target.at[place], device(to), target.at[origin])
                )
            self.own.append(
                pltpu.make_async_copy(source(place), target.at[place], own_sems.at[index])
            )

    def start(self):
        for going, _ in self.copies:
            going.start()
        for own in self.own:
            own.start()

    def finish(self):
        for going, coming in self.copies:
            coming.wait_recv()
            going.wait_send()
        for own in self.own:
            own.wait()


ANYWHERE = pl.BlockSpec(memory_space=pl.ANY)
IN_VMEM = pl.BlockSpec(memory_space=pltpu.VMEM)


def dma_sems(count):
    return pltpu.SemaphoreType.DMA((count,))


def exchange(axis, arrays, collective_id, micros, across=()):
    grid = Grid()
    size = grid.exp_size if axis == "exp" else grid.fsdp_size
    count, crossing = len(arrays), len(across)
    parts = [part for _, part in arrays]

    def kernel(*refs):
        sources, over = refs[:count], refs[count : count + crossing]
        refs = refs[count + crossing :]
        targets, landed = refs[:count], refs[count : count + crossing]
        send, receive, own = refs[count + crossing :]
        place = grid.here()
        links = Links(send, receive)
        sibling = (place.exp, place.sibling(place.fsdp))
        pairs = [
            (partial(plane_of, source, part), target)
            for source, part, target in zip(sources, parts, targets)
        ]
        work = Exchange(place, axis, links, own, pairs)
        swaps = [
            links.copy(source, target, sibling, target) for source, target in zip(over, landed)
        ]
        greet(work.peers + ([sibling] if swaps and axis == "exp" else []))
        work.start()
        for going, _ in swaps:
            going.start()
        work.finish()
        for going, coming in swaps:
            coming.wait_recv()
            going.wait_send()

    return pl.pallas_call(
        kernel,
        out_shape=tuple(
            [
                shape_of((size,) + array.shape[(1 if part is None else 2) :], array.dtype)
                for array, part in arrays
            ]
            + [shape_of(array.shape, array.dtype) for array in across]
        ),
        in_specs=[IN_VMEM] * count + [ANYWHERE] * crossing,
        out_specs=tuple([ANYWHERE] * (count + crossing)),
        scratch_shapes=[
            dma_sems(count * size + crossing), dma_sems(count * size + crossing), dma_sems(count),
        ],
        compiler_params=params(collective_id=collective_id, has_side_effects=True),
        cost_estimate=hint(micros),
        name=f"exchange_{collective_id}",
    )(*[array for array, _ in arrays], *across)


def plane_of(source, part, to):
    return source.at[to] if part is None else source.at[to, part]


def gather_rows(array, collective_id, micros):
    grid = Grid()

    def kernel(source, target, send, receive, own):
        place = grid.here()
        work = ChipGather(place, Links(send, receive), own.at[0], source, target)
        greet(chip_peers(place))
        work.start()
        work.forward()
        work.finish()

    return pl.pallas_call(
        kernel,
        out_shape=shape_of((grid.fsdp_size,) + array.shape, array.dtype),
        in_specs=[IN_VMEM],
        out_specs=ANYWHERE,
        scratch_shapes=[dma_sems(2 * grid.fsdp_size), dma_sems(2 * grid.fsdp_size), dma_sems(1)],
        compiler_params=pltpu.CompilerParams(collective_id=collective_id, has_side_effects=True),
        cost_estimate=hint(micros),
        name=f"gather_{collective_id}",
    )(array)


class Lanes:
    def __init__(self, heads, width, padded_heads, experts):
        self.weights = 3 * heads * width
        self.base = self.weights // 128 * 128
        self.router = self.weights - self.base
        self.gain = self.router + experts
        self.table = self.gain + 1
        self.count = self.table + padded_heads
        self.width = -(-(self.weights + 2 * experts + 1 + padded_heads) // 128) * 128
        self.extra = self.width - self.base
        self.shift = self.count - self.router


def bucket_rows_select(features, feature_rows, bucket_rows, span):
    row = lax.broadcasted_iota(jnp.int32, (features, 1), 0)
    within = lax.rem(row, feature_rows)
    bucket = jnp.where(
        within < bucket_rows, lax.div(row, feature_rows) * bucket_rows + within, -1
    )
    distance = lax.broadcasted_iota(jnp.int32, (1, span), 1) - SKEW
    near = BUCKETS // 2
    spread = max(WINDOW - near, 1)
    far = near + lax.div(jnp.maximum(distance - near, 0) * (BUCKETS - near), spread)
    wanted = jnp.where(distance < near, distance, far)
    reachable = (distance >= 0) & (distance < WINDOW)
    wanted = jnp.where(reachable, wanted, -2)
    return jnp.where(bucket == wanted, 1.0, 0.0).astype(BF16), reachable


def as_column(row, size):
    row_place = lax.broadcasted_iota(jnp.int32, (size, size), 0)
    lane = lax.broadcasted_iota(jnp.int32, (size, size), 1)
    spread = jnp.broadcast_to(row.astype(F32), (size, size))
    return jnp.sum(jnp.where(row_place == lane, spread, 0.0), axis=1, keepdims=True)


def padded_rows(value, rows):
    if value.shape[0] == rows:
        return value
    return jnp.concatenate([value, jnp.zeros((rows - value.shape[0], value.shape[1]), F32)], axis=0)


def padded_lanes(value, lanes):
    if value.shape[1] == lanes:
        return value
    return jnp.concatenate([value, jnp.zeros((value.shape[0], lanes - value.shape[1]), F32)], axis=1)


class Wide:
    def __init__(self, grid, links, own_sem, source, target):
        self.grid, self.links, self.target = grid, links, target
        self.own = pltpu.make_async_copy(
            source, target.at[grid.z, grid.y, grid.x, grid.core], own_sem
        )
        stage = []
        for hop in range(1, grid.z_size):
            origin = (grid.z + grid.z_size - hop) % grid.z_size
            stage.append(
                links.copy(
                    source, target.at[grid.z, grid.y, grid.x, grid.core],
                    grid.at(z=(grid.z + hop) % grid.z_size),
                    target.at[origin, grid.y, grid.x, grid.core],
                )
            )
        self.stages = [stage]

    def start(self):
        self.own.start()
        for going, _ in self.stages[0]:
            going.start()

    def turn(self, axis):
        grid, target = self.grid, self.target
        for _, coming in self.stages[-1]:
            coming.wait_recv()
        stage = []
        if axis == 0:
            self.own.wait()
            held = target.at[:, grid.y, grid.x, grid.core]
            for hop in range(1, grid.y_size):
                origin = (grid.y + grid.y_size - hop) % grid.y_size
                stage.append(
                    self.links.copy(
                        held, held, grid.at(y=(grid.y + hop) % grid.y_size),
                        target.at[:, origin, grid.x, grid.core],
                    )
                )
        elif axis == 1:
            held = target.at[:, :, grid.x, grid.core]
            for hop in range(1, grid.x_size):
                origin = (grid.x + grid.x_size - hop) % grid.x_size
                stage.append(
                    self.links.copy(
                        held, held, (grid.exp, grid.x_from(hop)),
                        target.at[:, :, origin, grid.core],
                    )
                )
        else:
            held = target.at[:, :, :, grid.core]
            stage.append(
                self.links.copy(
                    held, held, (grid.exp, grid.sibling(grid.fsdp)), target.at[:, :, :, 1 - grid.core]
                )
            )
        for going, _ in stage:
            going.start()
        self.stages.append(stage)

    def finish(self):
        for _, coming in self.stages[-1]:
            coming.wait_recv()
        for stage in self.stages:
            for going, _ in stage:
                going.wait_send()


def start_kernel(
    tokens, cotangent, routes_t, slots_t, attention_gain, mixture_gain, attention_in, router_t, table,
    attention_out, expert_up, expert_down, *refs, lanes, heads, width, head_count, experts, capacity,
    local,
):
    all_tokens, all_planes, cotangent_slots, position_rows, columns, full_out = refs[:6]
    shards = refs[6 : 6 + 2 * local]
    planes, up_stage, down_stage, send, receive, own, fetch, split = refs[6 + 2 * local :]
    grid = Grid().here()
    links = Links(send, receive)
    z_size, y_size, fsdp_size = grid.z_size, grid.y_size, grid.fsdp_size
    near = [
        (grid.exp, (grid.fsdp + turn) % fsdp_size) for turn in range(1, fsdp_size)
    ] + [grid.at(z=(grid.z + hop) % z_size) for hop in range(1, z_size)]
    beside = [grid.at(y=(grid.y + hop) % y_size) for hop in range(1, y_size)]
    gathered = ChipGather(grid, links, own.at[0], tokens, all_tokens)
    widely = Wide(grid, links, own.at[2], attention_out, full_out)
    part = expert_down.shape[1]
    depth = expert_up.shape[1]
    fetches = []
    for index in range(local):
        fetches.append(
            pltpu.make_async_copy(expert_up.at[index], up_stage.at[index], fetch.at[2 * index])
        )
        fetches.append(
            pltpu.make_async_copy(
                expert_down.at[index], down_stage.at[index], fetch.at[2 * index + 1]
            )
        )
    greet(near + beside)
    widely.start()
    for copy in fetches:
        copy.start()

    feature_rows = attention_in.shape[0]
    model_width = head_count * width
    gained = attention_in[...].astype(F32) * as_column(attention_gain[...], feature_rows)
    route_rows, slot_rows = routes_t[...].astype(F32), slots_t[...].astype(F32)
    columns[...] = padded_rows(jnp.concatenate([route_rows, slot_rows], axis=0), 128).T
    row_count = columns.shape[0]
    expert_lanes = lax.broadcasted_iota(jnp.int32, (row_count, experts), 1).astype(F32)
    named = jnp.zeros((row_count, experts), F32)
    for k in range(2):
        named = named + jnp.where(expert_lanes == columns[:, k : k + 1], 1.0, 0.0)
    named = jnp.sum(named, axis=0, keepdims=True)
    place = lax.broadcasted_iota(jnp.int32, (feature_rows, feature_rows), 0)
    same = place == lax.broadcasted_iota(jnp.int32, (feature_rows, feature_rows), 1)
    router = contract_last(jnp.where(same, 1.0, 0.0).astype(BF16), router_t[...])
    pieces = [
        router,
        as_column(mixture_gain[...], feature_rows),
        padded_rows(padded_lanes(table[...].astype(F32), heads * fsdp_size), feature_rows),
        padded_rows(named, feature_rows),
    ]
    taken = sum(piece.shape[1] for piece in pieces)
    if lanes.width > lanes.weights + taken:
        pieces.append(jnp.zeros((feature_rows, lanes.width - lanes.weights - taken), F32))
    for place in range(fsdp_size):
        first, last = place * heads * width, min((place + 1) * heads * width, model_width)
        own_pieces = []
        for kind in range(3):
            if last > first:
                own_pieces.append(gained[:, kind * model_width + first : kind * model_width + last])
            if last - first < heads * width:
                own_pieces.append(
                    jnp.zeros((feature_rows, heads * width - max(last - first, 0)), F32)
                )
        planes[place] = jnp.concatenate(own_pieces + pieces, axis=1).astype(BF16)
    placed = []
    for turn in range(1, fsdp_size):
        to = (grid.fsdp + turn) % fsdp_size
        origin = (grid.fsdp + fsdp_size - turn) % fsdp_size
        placed.append(
            links.copy(
                planes.at[to], all_planes.at[grid.z, grid.y, grid.fsdp], (grid.exp, to),
                all_planes.at[grid.z, grid.y, origin],
            )
        )
        placed[-1][0].start()
    kept = pltpu.make_async_copy(
        planes.at[grid.fsdp], all_planes.at[grid.z, grid.y, grid.fsdp], own.at[1]
    )
    kept.start()
    gathered.start()
    for _, coming in placed:
        coming.wait_recv()
    kept.wait()

    def over_y(z):
        for turn in range(1, y_size):
            forwarded.append(
                links.copy(
                    all_planes.at[z, grid.y],
                    all_planes.at[z, grid.y],
                    grid.at(y=(grid.y + turn) % y_size),
                    all_planes.at[z, (grid.y + y_size - turn) % y_size],
                )
            )
            forwarded[-1][0].start()

    along_z, forwarded = [], []
    for hop in range(1, z_size):
        along_z.append(
            links.copy(
                all_planes.at[grid.z, grid.y],
                all_planes.at[grid.z, grid.y],
                grid.at(z=(grid.z + hop) % z_size),
                all_planes.at[(grid.z + z_size - hop) % z_size, grid.y],
            )
        )
        along_z[-1][0].start()
    over_y(grid.z)
    widely.turn(0)

    for copy in fetches:
        copy.wait()
    splits = []
    for index in range(local):
        up, down = shards[2 * index : 2 * index + 2]
        stores = [
            (
                up_stage.at[index, :, pl.ds(block * part, part)],
                up.at[pl.ds(block * depth, depth), :],
            )
            for block in range(fsdp_size)
        ]
        for source, target in stores + [(down_stage.at[index], down)]:
            splits.append(pltpu.make_async_copy(source, target, split.at[len(splits)]))
            splits[-1].start()

    widely.turn(1)

    place = route_rows * capacity + slot_rows
    position_rows[...] = padded_rows(place, 8)
    select_rows(cotangent_slots, place, cotangent[...])

    for hop in range(1, z_size):
        along_z[hop - 1][1].wait_recv()
        over_y((grid.z + z_size - hop) % z_size)
    gathered.forward()
    widely.turn(2)
    for going, coming in forwarded:
        coming.wait_recv()
        going.wait_send()
    for going, _ in placed + along_z:
        going.wait_send()
    gathered.finish()
    widely.finish()
    for copy in splits:
        copy.wait()


def project_kernel(
    tokens, plane, segments, normed, query_t, key_n, query_n, value_n, key_t, value_t, bias, counts,
    weight_t, table_t, *, heads, width, lanes, feature_rows, bucket_rows,
):
    @pl.when(pl.program_id(0) == 0)
    def _():
        weight_t[...] = turned(plane[:, : lanes.weights]).astype(BF16)
        extra = plane[:, lanes.base :]
        span = bias.shape[2]
        select, reachable = bucket_rows_select(plane.shape[0], feature_rows, bucket_rows, span)
        table_t[...] = lax.dot_general(
            extra, select, (((0,), (0,)), ((), ())), preferred_element_type=F32
        )
        first = lanes.table + lax.axis_index("fsdp") * heads
        for head in range(heads):
            bias[head] = jnp.where(reachable, table_t[pl.ds(first + head, 1), :], MASKED)
        summed = jnp.sum(extra.astype(F32), axis=0, keepdims=True)
        counts[...] = pltpu.roll(
            jnp.broadcast_to(summed, counts.shape), lanes.extra - lanes.shift, 1
        )

    inputs = tokens[0].astype(F32)
    scale = lax.rsqrt(jnp.mean(inputs * inputs, axis=1, keepdims=True) + EPSILON)
    low = (inputs * scale).astype(BF16)
    normed[...] = low
    rows = low.shape[0]
    projected = contract_last(weight_t[...], low).astype(BF16).astype(F32)
    document = segments[...] % 4
    places = lax.broadcasted_iota(jnp.int32, (8, rows), 0)
    same = places == document
    hot = jnp.where(same, 1.0, 0.0)
    barred = jnp.where(same | (places >= 4), 0.0, MASKED)
    filler = jnp.zeros((SKEW - 8 - width, rows), F32)
    for head in range(heads):
        query = projected[head * width : (head + 1) * width] * width ** (-0.5)
        key = projected[(heads + head) * width : (heads + head + 1) * width]
        value = projected[(2 * heads + head) * width : (2 * heads + head + 1) * width]
        query_t[head] = jnp.concatenate([query, barred, filler], axis=0).astype(BF16)
        key_n[head] = jnp.concatenate([key, hot, filler], axis=0).T.astype(BF16)
        query_n[head] = query.T.astype(BF16)
        value_n[head] = value.T.astype(BF16)
        key_t[head] = key.astype(BF16)
        value_t[head] = value.astype(BF16)


def spans(length):
    for query_start in range(0, length, QUERY_BLOCK):
        key_start = max(0, query_start - WINDOW)
        yield query_start, key_start, query_start + QUERY_BLOCK - key_start


def spread_bias(bias, skew):
    skew[...] = pltpu.roll(
        jnp.broadcast_to(bias[0], skew.shape), 0, 1, stride=1, stride_axis=0
    )


def attend_kernel(query_t, key_n, value_t, bias, context, context_high, log_total, skew, scores, *, rows):
    spread_bias(bias, skew)
    for query_start, key_start, key_count in spans(query_t.shape[2]):
        queries = slice(query_start, query_start + QUERY_BLOCK)
        keys = slice(key_start, key_start + key_count)
        raw = matmul(key_n[0, keys, :], query_t[0, :, queries])
        for start in range(0, key_count, SKEW):
            offset = query_start - key_start - start + SKEW
            scores[start : start + SKEW, :] = (
                raw[start : start + SKEW] + skew[:, offset : offset + QUERY_BLOCK]
            )
        high = jnp.max(scores[:key_count, :], axis=0, keepdims=True)
        weights = jnp.exp(scores[:key_count, :] - high)
        total = jnp.sum(weights, axis=0, keepdims=True)
        gathered = matmul(value_t[0, :, keys], weights.astype(BF16)) / total
        context_high[0, :, queries] = gathered
        log_total[0, :, queries] = high + jnp.log(total)
        for start in range(0, QUERY_BLOCK, 128):
            place = query_start + start
            context[place // rows, :, place % rows : place % rows + 128] = gathered[
                :, start : start + 128
            ].astype(BF16)


def attend_back_kernel(
    query_t, key_n, query_n, value_n, key_t, grad_t, grad_n, context_high, log_total, bias,
    grad_projected, grad_bias, skew, grad_skew, grad_key, grad_value, *, scale,
):
    spread_bias(bias, skew)
    grad_skew[...] = jnp.zeros_like(grad_skew)
    grad_key[...] = jnp.zeros_like(grad_key)
    grad_value[...] = jnp.zeros_like(grad_value)
    inner = jnp.sum(grad_t[0].astype(F32) * context_high[0], axis=0, keepdims=True)
    for query_start, key_start, key_count in spans(query_t.shape[2]):
        queries = slice(query_start, query_start + QUERY_BLOCK)
        keys = slice(key_start, key_start + key_count)
        raw = matmul(key_n[0, keys, :], query_t[0, :, queries])
        grad_weights = matmul(value_n[0, keys, :], grad_t[0, :, queries])
        weights_low, grad_low = [], []
        for start in range(0, key_count, SKEW):
            offset = query_start - key_start - start + SKEW
            part = slice(start, start + SKEW)
            weights = jnp.exp(
                raw[part] + skew[:, offset : offset + QUERY_BLOCK] - log_total[0, :, queries]
            )
            grad_scores = weights * (grad_weights[part] - inner[:, queries])
            grad_skew[:, offset : offset + QUERY_BLOCK] += grad_scores
            weights_low.append(weights.astype(BF16))
            grad_low.append(grad_scores.astype(BF16))
        weights_low = jnp.concatenate(weights_low, axis=0)
        grad_low = jnp.concatenate(grad_low, axis=0)
        grad_projected[0, 0, :, queries] = (matmul(key_t[0, :, keys], grad_low) * scale).astype(BF16)
        grad_key[keys, :] += matmul(grad_low, query_n[0, queries, :])
        grad_value[keys, :] += matmul(weights_low, grad_n[0, queries, :])
    grad_projected[1, 0] = grad_key[...].T.astype(BF16)
    grad_projected[2, 0] = grad_value[...].T.astype(BF16)
    count = SKEW
    span = skew.shape[1]
    while count > 8:
        count //= 2
        grad_skew[:count, :] += pltpu.roll(grad_skew[count : 2 * count, :], span - count, 1)
    summed = grad_skew[0:1, :]
    for row in range(1, 8):
        summed = summed + pltpu.roll(grad_skew[row : row + 1, :], span - row, 1)
    grad_bias[0] = summed

def expert_lane(shape, lanes):
    return lax.broadcasted_iota(jnp.int32, shape, 1) - lanes.router


def int_columns(columns):
    values = columns[:, 0:4].astype(jnp.int32)
    return values[:, 0:2], values[:, 2:4]


def route_kernel(
    tokens, attended_t, attention_out, plane, columns, position_rows,
    hidden, routed, probabilities, gates, outgoing, slot_gates, *, experts, lanes, capacity,
):
    rows, model_width = tokens.shape
    routes, slots = int_columns(columns)
    attended_low = turned(attended_t[:model_width]).astype(BF16)
    hidden_state = tokens[...].astype(F32) + matmul(attended_low, attention_out[...])
    hidden[...] = hidden_state
    scale = lax.rsqrt(jnp.mean(hidden_state * hidden_state, axis=1, keepdims=True) + EPSILON)
    extra = plane[:, lanes.base :]
    gain = extra.astype(F32).T[lanes.gain : lanes.gain + 1]
    low = (hidden_state * scale * gain).astype(BF16)
    routed[...] = low
    logits = matmul(low, extra)
    lane = expert_lane(logits.shape, lanes)
    logits = jnp.where((lane >= 0) & (lane < experts), logits, MASKED)
    powers = jnp.exp(logits - jnp.max(logits, axis=1, keepdims=True))
    powers = powers / jnp.sum(powers, axis=1, keepdims=True)
    probabilities[...] = powers
    chosen = [
        jnp.sum(jnp.where(lane == routes[:, k : k + 1], powers, 0.0), axis=1, keepdims=True)
        for k in range(2)
    ]
    total = chosen[0] + chosen[1]
    gate_values = [chosen[k] / total for k in range(2)]
    pair = lax.broadcasted_iota(jnp.int32, (rows, 2), 1)
    gates[...] = jnp.where(pair == 0, gate_values[0], gate_values[1])
    members, _, gate_lanes = slot_gates.shape
    member_slots = experts // members * capacity
    slot_lanes = lax.broadcasted_iota(jnp.int32, (rows, gate_lanes), 1)
    inside = slot_lanes < member_slots
    places = routes * capacity + slots
    for member in range(members):
        by_slot = jnp.zeros((rows, gate_lanes), F32)
        for k in range(2):
            hit = (slot_lanes + member * member_slots == places[:, k : k + 1]) & inside
            by_slot = by_slot + jnp.where(hit, gate_values[k], 0.0)
        slot_gates[member] = jnp.broadcast_to(
            jnp.sum(by_slot, axis=0, keepdims=True), slot_gates.shape[1:]
        )
    select_rows(outgoing, position_rows[...], low)


def select_rows(outgoing, position_rows, values):
    slot_count, rows = outgoing.shape[0], values.shape[0]
    for start in range(0, slot_count, rows):
        slots = (lax.broadcasted_iota(jnp.int32, (rows, rows), 0) + start).astype(F32)
        picked = (slots == position_rows[0:1, :]) | (slots == position_rows[1:2, :])
        outgoing[start : start + rows, :] = matmul(
            jnp.where(picked, 1.0, 0.0).astype(BF16), values
        ).astype(BF16)


def gelu_parts(value):
    magnitude = jnp.abs(value)
    power = jnp.exp2(value * value * -0.7213475204444817)
    base = 1.0 + (0.3275911 * 0.7071067811865476) * magnitude
    step = pl.reciprocal(base, approx=True)
    step = step * (2.0 - base * step)
    series = step * (
        0.127414796
        + step * (-0.142248368 + step * (0.7107068705 + step * (-0.7265760135 + step * 0.5307027145)))
    )
    tail = series * power
    normal = jnp.where(value < 0.0, tail, 1.0 - tail)
    return value * normal, normal + value * (power * 0.3989422804014327)


def flipped(place, other, size):
    result, bit = 0, 1
    while bit < size:
        result = result + bit * ((place // bit + other // bit) % 2)
        bit *= 2
    return result


def expert_kernel(*refs, layout, index, local, half, capacity, parts):
    shards = 2 * half
    refs = Bag(layout, refs)
    grid = Grid().here()
    z_size, y_size = grid.z_size, grid.y_size
    first, last = False, index == local - 1
    sibling = (grid.exp, grid.sibling(grid.fsdp))
    links = Links(refs.send[0], refs.receive[0])
    rows_all, cot, up_all, down_all = (
        refs.rows_all[0], refs.cot[0], refs.up_all[0], refs.down_all[0]
    )
    active, grad_hidden, unscaled = refs.active[0], refs.grad_hidden[0], refs.unscaled[0]
    gates, gate_column = refs.gates[0], refs.gate_column[0]
    rows_t, slot_grad = refs.rows_t[0], refs.slot_grad[0]
    grad_up, grad_down = refs.grad_up[0], refs.grad_down[0]
    grad_rows, grad_gates = refs.grad_rows[0], refs.grad_gates[0]
    up_keep, up_taken, down_keep, down_taken = refs.own
    keep_up = [up_keep] + list(refs.far_keep_up)
    taken_up = [up_taken] + list(refs.far_taken_up)
    keep_down = [down_keep] + list(refs.far_keep_down)
    taken_down = [down_taken] + list(refs.far_taken_down)
    load_sem, fetch_sem, store_sem = refs.load_sem[0], refs.fetch_sem[0], refs.store_sem[0]
    store_there, stored_here = refs.store_there[0], refs.stored_here[0]
    pass_sem = refs.pass_sem[0]
    blocks, _, model_width = rows_all.shape
    part = up_all.shape[2]
    count = blocks * capacity
    depth = model_width // shards
    power = z_size & (z_size - 1) == 0
    together = 2 if power and z_size > 1 else 1
    group_rows = together * y_size * capacity

    def source_z(turn):
        return flipped(grid.z, turn, z_size) if power else (grid.z + turn) % z_size

    def target_z(turn):
        return flipped(grid.z, turn, z_size) if power else (grid.z + z_size - turn) % z_size

    def owner(place, core):
        return ((grid.x + place % half) % half) * 2 + (core + place // half) % 2

    def rows_of(place, core=None):
        core = grid.core if core is None else core
        return pl.ds(pl.multiple_of(owner(place, core) * depth, 16), depth)

    loads = [pltpu.make_async_copy(refs.cot_in[0].at[:, index], cot, load_sem.at[0])]
    if not first:
        loads.append(pltpu.make_async_copy(refs.rows_in[0], rows_all, load_sem.at[1]))
    my_up, my_down = refs.my_up, refs.my_down
    swapped_up, swapped_down = refs.swapped_up, refs.swapped_down
    local_up = list(enumerate(my_up)) + [
        (half + number, array) for number, array in enumerate(swapped_up)
    ]
    local_down = list(enumerate(my_down)) + [
        (half + number, array) for number, array in enumerate(swapped_down)
    ]
    fetched_up = [
        pltpu.make_async_copy(
            array.at[rows_of(place), :], up_all.at[place, rows_of(shard), :],
            fetch_sem.at[place, number],
        )
        for number, (shard, array) in enumerate(local_up)
        for place in range(shards)
    ]
    fetched_down = {
        shard: pltpu.make_async_copy(
            array, down_all.at[shard], fetch_sem.at[shards + number, 0]
        )
        for number, (shard, array) in enumerate(local_down)
    }
    cross_down = {
        half + shard: links.copy(
            my_down[shard], down_all.at[half + shard], sibling, down_all.at[half + shard]
        )
        for shard in range(len(swapped_down), half)
    }
    cross_up = [
        links.copy(
            my_up[shard].at[rows_of(place, 1 - grid.core), :],
            up_all.at[place, rows_of(shard), :], sibling,
            up_all.at[place, rows_of(half + shard), :],
        )
        for shard in range(len(swapped_up), half)
        for place in range(shards)
    ]
    cross_next = [
        links.copy(source, target, sibling, target)
        for source, target in zip(refs.next_mine, refs.next_swapped)
    ]
    work = Exchange(
        grid, "exp", links, refs.own_sem[0],
        [
            (partial(plane_of, source, place), target)
            for source, place, target in zip(refs.moved_from, parts, refs.moved_to)
        ],
    )
    gate_work = None
    if first:
        gate_work = Exchange(
            grid, "exp", links, refs.gate_sem[0],
            [(partial(plane_of, refs.gates_from[0], None), gates)],
        )

    def member(z, y):
        return z * y_size + y

    def dispatch(turn, hop):
        to = member(target_z(turn), (grid.y + y_size - hop) % y_size)
        origin = member(source_z(turn), (grid.y + hop) % y_size)
        outgoing = refs.outgoing[0]
        going = pltpu.make_async_remote_copy(
            src_ref=outgoing.at[to, index], dst_ref=rows_all.at[grid.exp],
            send_sem=refs.row_send[0].at[turn, hop], recv_sem=refs.row_receive[0].at[turn, hop],
            device_id=(to, grid.fsdp), device_id_type=MESH,
        )
        coming = pltpu.make_async_remote_copy(
            src_ref=rows_all.at[origin], dst_ref=rows_all.at[origin],
            send_sem=refs.row_send[0].at[turn, hop], recv_sem=refs.row_receive[0].at[turn, hop],
            device_id=(to, grid.fsdp), device_id_type=MESH,
        )
        return going, coming

    def give_back(turn, hop):
        to = member(source_z(turn), (grid.y + hop) % y_size)
        origin = member(target_z(turn), (grid.y + y_size - hop) % y_size)
        pairs = []
        for number, (held, target) in enumerate(
            ((grad_rows, refs.back_rows[0]), (grad_gates, refs.back_gates[0]))
        ):
            sems = dict(
                send_sem=refs.back_send[0].at[number, turn, hop],
                recv_sem=refs.back_receive[0].at[number, turn, hop],
                device_id=(to, grid.fsdp), device_id_type=MESH,
            )
            pairs.append(
                (
                    pltpu.make_async_remote_copy(
                        src_ref=held.at[to], dst_ref=target.at[grid.exp], **sems
                    ),
                    pltpu.make_async_remote_copy(
                        src_ref=target.at[origin], dst_ref=target.at[origin], **sems
                    ),
                )
            )
        return pairs

    steps = [(turn, hop) for turn in range(z_size) for hop in range(y_size)]
    own_row = own_back = None
    if first:
        own_row = pltpu.make_async_copy(
            refs.outgoing[0].at[grid.exp, index], rows_all.at[grid.exp], load_sem.at[1]
        )
    if last:
        own_back = [
            pltpu.make_async_copy(held.at[grid.exp], target.at[grid.exp], load_sem.at[2 + number])
            for number, (held, target) in enumerate(
                ((grad_rows, refs.back_rows[0]), (grad_gates, refs.back_gates[0]))
            )
        ]

    for copy in loads:
        copy.start()
    for copy in list(fetched_down.values()) + fetched_up:
        copy.start()
    greet([((grid.exp + hop) % grid.exp_size, grid.fsdp) for hop in range(1, grid.exp_size)] + [sibling])
    if first:
        gate_work.start()
        own_row.start()
        for turn, hop in steps[1:]:
            dispatch(turn, hop)[0].start()
    for going, _ in list(cross_down.values()) + cross_up + cross_next:
        going.start()
    work.start()

    loads[0].wait()
    for place in range(shards):
        if place in fetched_down:
            fetched_down[place].wait()
        else:
            cross_down[place][1].wait_recv()
        unscaled[place] = contract_last(cot[...].reshape(count, model_width), down_all[place])
    if first:
        gate_work.finish()
        gates_out = pltpu.make_async_copy(gates, refs.gates_to[0], load_sem.at[4])
        gates_out.start()
    columns = gates[:, 0, :].T
    for block in range(blocks):
        piece = slice(block * capacity, (block + 1) * capacity)
        gate = columns[index * capacity : (index + 1) * capacity, block : block + 1]
        gate_column[piece, :] = gate
    slot_grad[...] = (
        gate_column[...] * cot[...].reshape(count, model_width).astype(F32)
    ).astype(BF16)
    for copy in fetched_up:
        copy.wait()
    for _, coming in cross_up:
        coming.wait_recv()
    if first:
        own_row.wait()
    else:
        loads[1].wait()

    def group(number, carry):
        turns = [number * together + more for more in range(together)]
        if together == 2:
            place_of_group = flipped(grid.z // 2, number, z_size // 2)
        else:
            place_of_group = source_z(number)
        if first:
            for turn in turns:
                for hop in range(y_size):

                    @pl.when(turn + hop > 0)
                    def _(turn=turn, hop=hop):
                        dispatch(turn, hop)[1].wait_recv()

        members = pl.ds(place_of_group * together * y_size, together * y_size)
        span = pl.ds(pl.multiple_of(place_of_group * group_rows, 16), group_rows)
        rows = rows_all[members].reshape(group_rows, model_width)
        gate = gate_column[span, :]
        grad = jnp.zeros((group_rows, model_width), F32)
        products = jnp.zeros((group_rows, part), F32)
        ahead = matmul(rows, up_all[0])
        for place in range(shards):
            hidden = ahead
            if place + 1 < shards:
                ahead = matmul(rows, up_all[place + 1])
            base = unscaled[place, span, :]
            activated, slope = gelu_parts(hidden)
            products = products + activated * base
            active[place, span, :] = activated.astype(BF16)
            low = (gate * base * slope).astype(BF16)
            grad_hidden[place, span, :] = low
            grad = grad + contract_last(low, up_all[place])
        grad_rows[members] = grad.astype(BF16).reshape(together * y_size, capacity, model_width)
        ones = jnp.ones((8, part), F32)
        for hop in range(together * y_size):
            grad_gates[place_of_group * together * y_size + hop] = lax.dot_general(
                ones, products[hop * capacity : (hop + 1) * capacity], (((1,), (1,)), ((), ())),
                precision=lax.Precision.HIGHEST, preferred_element_type=F32,
            )
        if last:
            for turn in turns:
                for hop in range(y_size):

                    @pl.when(turn + hop > 0)
                    def _(turn=turn, hop=hop):
                        for going, _ in give_back(turn, hop):
                            going.start()

        return carry

    lax.fori_loop(0, z_size // together, group, 0)
    if last:
        for copy in own_back:
            copy.start()

    rows_t[...] = turned(rows_all[...].reshape(count, model_width)).astype(BF16)
    total = refs.total[0] if refs.total else unscaled.at[0]
    total[...] = jnp.zeros(total.shape, F32)

    def up_target(targets, hop, place):
        if hop == 0:
            return targets[0].at[rows_of(place), :]
        return targets[1].at[hop - 1, rows_of(place), :]

    def keep_stores(place, slot):
        return [
            pltpu.make_async_copy(
                grad_up.at[slot, rows_of(hop), :], up_target(keep_up, hop, place),
                store_sem.at[slot, hop],
            )
            for hop in range(half)
        ]

    def give_stores(place, slot):
        return [
            pltpu.make_async_remote_copy(
                src_ref=grad_up.at[slot, rows_of(half + hop), :],
                dst_ref=up_target(taken_up, hop, place),
                send_sem=store_there.at[slot, hop], recv_sem=stored_here.at[place, hop],
                device_id=sibling, device_id_type=MESH,
            )
            for hop in range(half)
        ]

    def down_store(hop, slot):
        target = keep_down[0] if hop == 0 else keep_down[1].at[hop - 1]
        return pltpu.make_async_copy(grad_down.at[slot], target, store_sem.at[slot, half])

    def down_give(hop, slot):
        target = taken_down[0] if hop == 0 else taken_down[1].at[hop - 1]
        return pltpu.make_async_remote_copy(
            src_ref=grad_down.at[slot], dst_ref=target,
            send_sem=store_there.at[slot, half], recv_sem=stored_here.at[hop, half],
            device_id=sibling, device_id_type=MESH,
        )

    def each_down(place, slot, act):
        for hop in range(half):

            @pl.when(place == hop)
            def _(hop=hop):
                act(down_store(hop, slot), False)

            @pl.when(place == half + hop)
            def _(hop=hop):
                act(down_give(hop, slot), True)

    def start_store(place, slot):
        for copy in keep_stores(place, slot) + give_stores(place, slot):
            copy.start()
        each_down(place, slot, lambda copy, _: copy.start())

    def wait_store(place, slot):
        for copy in keep_stores(place, slot):
            copy.wait()
        for copy in give_stores(place, slot):
            copy.wait_send()
        each_down(place, slot, lambda copy, remote: copy.wait_send() if remote else copy.wait())

    def column(place, carry):
        slot = place % 2
        total[...] += matmul(active[place], down_all[place])

        @pl.when(place >= 2)
        def _():
            wait_store(place - 2, slot)

        grad_up[slot] = matmul(rows_t[...], grad_hidden[place]).astype(BF16)
        grad_down[slot] = contract_first(active[place], slot_grad[...]).astype(BF16)
        start_store(place, slot)
        return carry

    lax.fori_loop(0, shards, column, 0)

    rows_out = refs.rows_out[0]
    cot[...] = total[...].astype(BF16).reshape(blocks, capacity, model_width)
    out_copies = [pltpu.make_async_copy(cot, rows_out.at[:, index], load_sem.at[0])]
    for before in refs.outs_before:
        out_copies.append(
            pltpu.make_async_copy(before, rows_out.at[:, pl.ds(0, index)], load_sem.at[1])
        )
    for copy in out_copies:
        copy.start()
    for place in range(max(shards - 2, 0), shards):
        wait_store(place, place % 2)
    for place in range(shards):
        for copy in give_stores(place, 0):
            copy.wait_recv()
    for hop in range(half):
        down_give(hop, 0).wait_recv()
    if half > 1:
        for kept, taken, target, sem in (
            (keep_up[1], taken_up[1], refs.pass_up[0], 0),
            (keep_down[1], taken_down[1], refs.pass_down[0], 1),
        ):
            kept[...] = (kept[...].astype(F32) + taken[...].astype(F32)).astype(BF16)
            out_copies.append(pltpu.make_async_copy(kept, target, pass_sem.at[sem]))
            out_copies[-1].start()
    for copy in out_copies:
        copy.wait()
    for going, coming in cross_next:
        coming.wait_recv()
        going.wait_send()
    for going, _ in list(cross_down.values()) + cross_up:
        going.wait_send()
    if first:
        gates_out.wait()
        for turn, hop in steps[1:]:
            dispatch(turn, hop)[0].wait_send()
    work.finish()
    if last:
        for turn, hop in steps[1:]:
            for going, coming in give_back(turn, hop):
                coming.wait_recv()
                going.wait_send()
        for copy in own_back:
            copy.wait()


class Bag:
    def __init__(self, layout, refs):
        start = 0
        for name, size in layout.items():
            setattr(self, name, refs[start : start + size])
            start += size


class Wanted:
    def groups(self):
        return list(self.__dict__.values())

    def layout(self):
        return {name: len(group) for name, group in self.__dict__.items()}


def run_expert(index, local, outgoing, slot_gates, rows_in, gates, cotangent, ups, downs, swapped,
               next_mine, moved, outs_before, collective_id):
    grid = Grid()
    half = len(ups)
    shards = 2 * half
    first, last = False, index == local - 1
    blocks, _, capacity, model_width = cotangent.shape
    part = downs[0].shape[0]
    count = blocks * capacity
    gate_lanes = slot_gates.shape[2]
    inputs, outputs, scratch = Wanted(), Wanted(), Wanted()
    inputs.cot_in = [(cotangent, ANYWHERE)]
    inputs.outgoing = [(outgoing, ANYWHERE)] if first else []
    inputs.gates_from = [(slot_gates, ANYWHERE)] if first else []
    inputs.rows_in = [] if first else [(rows_in, ANYWHERE)]
    if not first:
        inputs.gates = [(gates, IN_VMEM)]
    inputs.my_up = [(array, ANYWHERE) for array in ups]
    inputs.my_down = [(array, ANYWHERE) for array in downs]
    inputs.swapped_up = [(array, ANYWHERE) for array in swapped[0]]
    inputs.swapped_down = [(array, ANYWHERE) for array in swapped[1]]
    inputs.next_mine = [(array, ANYWHERE) for array in next_mine]
    inputs.moved_from = [(array, ANYWHERE) for array, _ in moved]
    inputs.outs_before = [] if outs_before is None else [(outs_before, IN_VMEM)]

    up_shape, down_shape = (model_width, part), (part, model_width)
    outputs.rows_out = [(shape_of((blocks, index + 1, capacity, model_width), BF16), ANYWHERE)]
    own_up, own_down = shape_of(up_shape, BF16), shape_of(down_shape, BF16)
    outputs.own = [(own_up, ANYWHERE), (own_up, ANYWHERE), (own_down, ANYWHERE), (own_down, ANYWHERE)]
    outputs.pass_up = [(shape_of((half - 1,) + up_shape, BF16), ANYWHERE)] if half > 1 else []
    outputs.pass_down = [(shape_of((half - 1,) + down_shape, BF16), ANYWHERE)] if half > 1 else []
    outputs.next_swapped = [(shape_of(array.shape, BF16), ANYWHERE) for array in next_mine]
    outputs.gates_to = [(shape_of(slot_gates.shape, F32), ANYWHERE)] if first else []
    outputs.moved_to = [
        (
            shape_of((grid.exp_size,) + array.shape[(1 if place is None else 2) :], array.dtype),
            ANYWHERE,
        )
        for array, place in moved
    ]
    rows_shape, gate_shape = (blocks, capacity, model_width), (blocks, 8, capacity)
    if last:
        outputs.back_rows = [(shape_of(rows_shape, BF16), ANYWHERE)]
        outputs.back_gates = [(shape_of(gate_shape, F32), ANYWHERE)]
    else:
        outputs.grad_rows = [(shape_of(rows_shape, BF16), IN_VMEM)]
        outputs.grad_gates = [(shape_of(gate_shape, F32), IN_VMEM)]

    sems = lambda *shape: pltpu.SemaphoreType.DMA(shape)
    scratch.rows_all = [pltpu.VMEM(rows_shape, BF16)]
    scratch.cot = [pltpu.VMEM(rows_shape, BF16)]
    scratch.up_all = [pltpu.VMEM((shards,) + up_shape, BF16)]
    scratch.down_all = [pltpu.VMEM((shards,) + down_shape, BF16)]
    scratch.active = [pltpu.VMEM((shards, count, part), BF16)]
    scratch.grad_hidden = [pltpu.VMEM((shards, count, part), BF16)]
    scratch.unscaled = [pltpu.VMEM((shards, count, part), F32)]
    if first:
        scratch.gates = [pltpu.VMEM(slot_gates.shape, F32)]
        scratch.gate_sem = [sems(1)]
        scratch.row_send = [sems(grid.z_size, grid.y_size)]
        scratch.row_receive = [sems(grid.z_size, grid.y_size)]
    if last:
        scratch.grad_rows = [pltpu.VMEM(rows_shape, BF16)]
        scratch.grad_gates = [pltpu.VMEM(gate_shape, F32)]
        scratch.back_send = [sems(2, grid.z_size, grid.y_size)]
        scratch.back_receive = [sems(2, grid.z_size, grid.y_size)]
    scratch.gate_column = [pltpu.VMEM((count, 1), F32)]
    scratch.rows_t = [pltpu.VMEM((model_width, count), BF16)]
    scratch.slot_grad = [pltpu.VMEM((count, model_width), BF16)]
    scratch.total = [] if part == model_width else [pltpu.VMEM((count, model_width), F32)]
    scratch.grad_up = [pltpu.VMEM((2,) + up_shape, BF16)]
    scratch.grad_down = [pltpu.VMEM((2,) + down_shape, BF16)]
    far_up = [pltpu.VMEM((half - 1,) + up_shape, BF16)] * (1 if half > 1 else 0)
    far_down = [pltpu.VMEM((half - 1,) + down_shape, BF16)] * (1 if half > 1 else 0)
    scratch.far_keep_up, scratch.far_taken_up = far_up, far_up
    scratch.far_keep_down, scratch.far_taken_down = far_down, far_down
    scratch.load_sem = [sems(5)]
    scratch.pass_sem = [sems(2)]
    scratch.fetch_sem = [sems(2 * shards, shards)]
    scratch.store_sem = [sems(2, half + 1)]
    scratch.store_there = [sems(2, half + 1)]
    scratch.stored_here = [sems(shards, half + 1)]
    copies = (len(moved) + 1) * grid.exp_size + half * (shards + 1) + len(next_mine)
    scratch.send = [sems(copies)]
    scratch.receive = [sems(copies)]
    scratch.own_sem = [sems(max(len(moved), 1))]

    layout = {**inputs.layout(), **outputs.layout(), **scratch.layout()}

    def body(*refs):
        expert_kernel(
            *refs, layout=layout, index=index, local=local, half=half, capacity=capacity,
            parts=[place for _, place in moved],
        )

    results = pl.pallas_call(
        body,
        in_specs=[spec for group in inputs.groups() for _, spec in group],
        out_specs=tuple(spec for group in outputs.groups() for _, spec in group),
        out_shape=tuple(shape for group in outputs.groups() for shape, _ in group),
        scratch_shapes=[item for group in scratch.groups() for item in group],
        compiler_params=params(collective_id=collective_id, has_side_effects=True),
        cost_estimate=hint(45),
        name=f"expert_{index}",
    )(*[array for group in inputs.groups() for array, _ in group])
    return Bag(outputs.layout(), results)


def local_picks(routes, slots, capacity, local, index, slot_count):
    member, which = lax.div(routes, local), lax.rem(routes, local)
    places = jnp.where(which == index, member * capacity + slots, -1)
    lane = lax.broadcasted_iota(jnp.int32, (routes.shape[0], slot_count), 1)
    return [lane == places[:, k : k + 1] for k in range(2)]


def unroute_kernel(
    hidden, cotangent, routed, probabilities, gates, plane, columns, counts, *refs,
    experts, local, token_total, lanes,
):
    grads, gate_grads = refs[:local], refs[local : 2 * local]
    grad_hidden, grad_branch, small = refs[2 * local :]
    rows = hidden.shape[0]
    members, capacity, model_width = grads[0].shape
    grad_output = cotangent[...].astype(F32)
    grad_routed = jnp.zeros(hidden.shape, F32)
    found = [jnp.zeros((rows, capacity), F32), jnp.zeros((rows, capacity), F32)]
    routes, slots = int_columns(columns)
    member, which = lax.div(routes, local), lax.rem(routes, local)
    lane = lax.broadcasted_iota(jnp.int32, (rows, capacity), 1)
    for index in range(local):
        picks = local_picks(routes, slots, capacity, local, index, members * capacity)
        grad_routed = grad_routed + matmul(
            jnp.where(picks[0] | picks[1], 1.0, 0.0).astype(BF16),
            grads[index][...].reshape(members * capacity, model_width),
        )
        for place in range(members):
            spots = jnp.where((which == index) & (member == place), slots, -1)
            for k in range(2):
                found[k] = found[k] + jnp.where(
                    lane == spots[:, k : k + 1], gate_grads[index][place, 0:1, :], 0.0
                )
    grad_gates = [jnp.sum(found[k], axis=1, keepdims=True) for k in range(2)]
    powers = probabilities[...]
    lane = expert_lane(powers.shape, lanes)
    inside = (lane >= 0) & (lane < experts)
    picked = [lane == routes[:, k : k + 1] for k in range(2)]
    chosen_total = sum(
        jnp.sum(jnp.where(picked[k], powers, 0.0), axis=1, keepdims=True) for k in range(2)
    )
    weighted = grad_gates[0] * gates[:, 0:1] + grad_gates[1] * gates[:, 1:2]
    grad_mass = (AUX_WEIGHT * experts / (2.0 * token_total * token_total)) * counts[0:1, :]
    grad_mass = jnp.where(inside, grad_mass, 0.0)
    for k in range(2):
        grad_mass = grad_mass + jnp.where(picked[k], (grad_gates[k] - weighted) / chosen_total, 0.0)
    grad_logits = powers * (grad_mass - jnp.sum(powers * grad_mass, axis=1, keepdims=True))
    extra = plane[:, lanes.base :]
    grad_routed = grad_routed + contract_last(grad_logits.astype(BF16), extra)
    hidden_state = hidden[...]
    scale = lax.rsqrt(jnp.mean(hidden_state * hidden_state, axis=1, keepdims=True) + EPSILON)
    normed = hidden_state * scale
    product = grad_routed * normed
    gain_grad = jnp.sum(product, axis=0, keepdims=True)
    small_t = matmul(grad_logits.T.astype(BF16), routed[...])
    row = lax.broadcasted_iota(jnp.int32, small_t.shape, 0)
    small_t = jnp.where(row == lanes.gain, gain_grad, small_t)
    small[...] = small_t.T
    gains = extra.astype(F32).T[lanes.gain : lanes.gain + 1]
    grad = scale * (
        grad_routed * gains - normed * jnp.mean(product * gains, axis=1, keepdims=True)
    ) + grad_output
    grad_hidden[...] = grad
    grad_branch[...] = grad.astype(BF16)


def context_grad_kernel(
    fsdp_index, grad_branch, attention_out, context, grad_t, grad_n, grad_out, total, *, heads, width
):
    @pl.when(pl.program_id(0) == 0)
    def _():
        total[...] = jnp.zeros_like(total)

    branch = grad_branch[0]
    grad = contract_last(attention_out[...], branch).astype(BF16)
    for head in range(heads):
        part = grad[head * width : (head + 1) * width]
        grad_t[head] = part
        grad_n[head] = turned(part).astype(BF16)
    total[...] += matmul(context[0], branch)

    @pl.when(pl.program_id(0) == pl.num_programs(0) - 1)
    def _():
        grad_out[...] = total[...].astype(BF16)


def project_back_kernel(
    grad_projected, normed, plane, small, probabilities, grad_bias, grad_first, grad_plane, total,
    bias_t, *, lanes, heads, feature_rows, bucket_rows,
):
    step = pl.program_id(0)

    @pl.when(step == 0)
    def _():
        total[...] = jnp.zeros_like(total)

    grad = grad_projected[...]
    grad_first[0] = matmul(plane[:, : lanes.weights], grad).astype(BF16)
    total[: lanes.weights, :] += matmul(grad, normed[...])

    @pl.when(step == pl.num_programs(0) - 1)
    def _():
        grad_plane[...] = total[...].T.astype(BF16)
        span = grad_bias.shape[2]
        select, _ = bucket_rows_select(plane.shape[0], feature_rows, bucket_rows, span)
        bias_t[...] = jnp.zeros_like(bias_t)
        first = lanes.table + lax.axis_index("fsdp") * heads
        for head in range(heads):
            bias_t[pl.ds(first + head, 1), :] = grad_bias[head]
        high = bias_t[...].astype(BF16)
        rest = (bias_t[...] - high.astype(F32)).astype(BF16)
        table = contract_last(select, high) + contract_last(select, rest)
        mass = jnp.sum(probabilities[...], axis=0, keepdims=True)
        mass = pltpu.roll(jnp.broadcast_to(mass, (8, lanes.extra)), lanes.shift, 1)[0:1]
        lane = lax.broadcasted_iota(jnp.int32, table.shape, 1)
        row = lax.broadcasted_iota(jnp.int32, table.shape, 0)
        is_small = (lane >= lanes.router) & (lane < lanes.table)
        is_mass = (lane >= lanes.count) & (lax.rem(row, feature_rows) == 0)
        extra = table + jnp.where(is_small, small[...], 0.0) + jnp.where(is_mass, mass, 0.0)
        grad_plane[:, lanes.base :] = (total[lanes.base :, :].T + extra).astype(BF16)


def last_kernel(
    first, planes, out_grad, first_parts, plane_parts, out_parts,
    first_in, first_sum, planes_in, plane_sum, along_in, reduced, send, receive, own, *, spread_out,
):
    grid = Grid().here()
    links = Links(send, receive)
    z_size, y_size, x_size, fsdp_size = grid.z_size, grid.y_size, grid.x_size, grid.fsdp_size
    exp_size = grid.exp_size
    sibling = grid.sibling(grid.fsdp)
    near = [
        (grid.exp, (grid.fsdp + turn) % fsdp_size) for turn in range(1, fsdp_size)
    ] + [grid.at(z=(grid.z + hop) % z_size) for hop in range(1, z_size)]
    beside = [grid.at(y=(grid.y + hop) % y_size) for hop in range(1, y_size)]

    per_sender = grid.device_count if spread_out else exp_size
    base = 0 if spread_out else grid.fsdp * exp_size
    out_sends = []
    for number in range(per_sender):
        to = base + number
        out_sends.append((to, number))
    if spread_out:
        out_origins = [(origin, origin) for origin in range(grid.device_count)]
    else:
        out_origins = [
            (member * fsdp_size + grid.linear // exp_size, member) for member in range(exp_size)
        ]
    own_slot = grid.linear if spread_out else grid.exp
    out_base = links.used
    links.used += per_sender

    def place_of(linear):
        return (linear // fsdp_size, linear % fsdp_size)

    def out_copy(to, number, slot):
        return pltpu.make_async_remote_copy(
            src_ref=out_grad.at[number], dst_ref=out_parts.at[slot],
            send_sem=send.at[out_base + number], recv_sem=receive.at[out_base + slot],
            device_id=place_of(to), device_id_type=MESH,
        )

    barrier = pltpu.get_barrier_semaphore()
    for device in near + beside:
        pl.semaphore_signal(barrier, inc=1, device_id=device, device_id_type=MESH)
    for origin, _ in out_origins:

        @pl.when(origin != grid.linear)
        def _(origin=origin):
            pl.semaphore_signal(
                barrier, inc=1, device_id=place_of(origin), device_id_type=MESH
            )

    to_self = (
        1 if spread_out else jnp.where(grid.linear // exp_size == grid.fsdp, 1, 0)
    )
    pl.semaphore_wait(barrier, len(near) + len(beside) + per_sender - to_self)

    first_copies = []
    for hop in range(x_size):
        mine = grid.x_from(hop)
        first_copies.append(
            links.copy(
                first.at[grid.sibling(mine)], first_in.at[hop], (grid.exp, sibling), first_in.at[hop]
            )
        )
        first_copies[-1][0].start()
    z_hops = list(range(1, z_size)) + [0]
    beside_copies = []
    for z_hop in z_hops:
        beside_copies.append([])
        for hop in range(1, y_size):
            to = (grid.y + hop) % y_size
            landing = planes_in.at[hop - 1, z_hop]
            beside_copies[-1].append(
                links.copy(
                    planes.at[(grid.z + z_hop) % z_size, to], landing, grid.at(y=to), landing
                )
            )
            beside_copies[-1][-1][0].start()
    for to, number in out_sends:

        @pl.when(to != grid.linear)
        def _(to=to, number=number):
            out_copy(to, number, own_slot).start()

        @pl.when(to == grid.linear)
        def _(number=number):
            pltpu.make_async_copy(out_grad.at[number], out_parts.at[own_slot], own.at[0]).start()

    along_x = []
    for hop in range(x_size):
        first_copies[hop][1].wait_recv()
        summed = first[grid.x_from(hop)].astype(F32) + first_in[hop].astype(F32)
        if hop == 0:
            first_parts[0] = summed.astype(BF16)
        else:
            first_sum[hop - 1] = summed.astype(BF16)
            along_x.append(
                links.copy(
                    first_sum.at[hop - 1], first_parts.at[hop], (grid.exp, grid.x_from(hop)),
                    first_parts.at[hop],
                )
            )
            along_x[-1][0].start()
    along_z = []
    for z_hop, copies in zip(z_hops, beside_copies):
        to_z = (grid.z + z_hop) % z_size
        summed = planes[to_z, grid.y].astype(F32)
        for number, (_, coming) in enumerate(copies):
            coming.wait_recv()
            summed = summed + planes_in[number, z_hop].astype(F32)
        plane_sum[z_hop] = summed.astype(BF16)
        if z_hop > 0:
            along_z.append(
                links.copy(
                    plane_sum.at[z_hop], along_in.at[z_hop - 1], grid.at(z=to_z),
                    along_in.at[z_hop - 1],
                )
            )
            along_z[-1][0].start()
    summed = plane_sum[0].astype(F32)
    for number, (_, coming) in enumerate(along_z):
        coming.wait_recv()
        summed = summed + along_in[number].astype(F32)
    reduced[...] = summed.astype(BF16)
    placed = []
    for turn in range(1, fsdp_size):
        to = (grid.fsdp + turn) % fsdp_size
        origin = (grid.fsdp + fsdp_size - turn) % fsdp_size
        placed.append(
            links.copy(
                reduced.at[to], plane_parts.at[grid.fsdp], (grid.exp, to), plane_parts.at[origin]
            )
        )
        placed[-1][0].start()
    kept = pltpu.make_async_copy(reduced.at[grid.fsdp], plane_parts.at[grid.fsdp], own.at[1])
    kept.start()
    for going, coming in along_x + placed:
        coming.wait_recv()
    for going, _ in first_copies + along_x + along_z + placed:
        going.wait_send()
    for copies in beside_copies:
        for going, _ in copies:
            going.wait_send()
    kept.wait()
    for origin, slot in out_origins:

        @pl.when(origin != grid.linear)
        def _(origin=origin, slot=slot):
            out_copy(origin, 0, slot).wait_recv()

    for to, number in out_sends:

        @pl.when(to != grid.linear)
        def _(to=to, number=number):
            out_copy(to, number, own_slot).wait_send()

        @pl.when(to == grid.linear)
        def _(number=number):
            pltpu.make_async_copy(out_grad.at[number], out_parts.at[own_slot], own.at[0]).wait()


def mixture_kernel(hidden, gates, columns, rows_in, output, *, local):
    members, _, capacity, model_width = rows_in.shape
    routes, slots = int_columns(columns)
    total = hidden[...]
    picked = [jnp.zeros(hidden.shape, F32), jnp.zeros(hidden.shape, F32)]
    for index in range(local):
        picks = local_picks(routes, slots, capacity, local, index, members * capacity)
        values = rows_in[:, index].reshape(members * capacity, model_width)
        for k in range(2):
            picked[k] = picked[k] + matmul(jnp.where(picks[k], 1.0, 0.0).astype(BF16), values)
    for k in range(2):
        total = total + gates[:, k : k + 1] * picked[k]
    output[...] = total.astype(BF16)


def finish_kernel(
    first_parts, plane_parts, out_parts, tokens, grad_hidden, attention_in, attention_gain, counts,
    grad_tokens, grad_gain, grad_in, grad_out, grad_mixture, grad_router, grad_table, balance,
    *, lanes, heads, width, head_count, experts, token_total,
):
    total = jnp.sum(first_parts[...].astype(F32), axis=0).T
    inputs = tokens[...].astype(F32)
    scale = lax.rsqrt(jnp.mean(inputs * inputs, axis=1, keepdims=True) + EPSILON)
    normed = inputs * scale
    grad_tokens[...] = grad_hidden[...] + scale * (
        total - normed * jnp.mean(total * normed, axis=1, keepdims=True)
    )
    fsdp_size = plane_parts.shape[0]
    model_width = head_count * width
    sums = [plane_parts[place].astype(F32) for place in range(fsdp_size)]
    columns = []
    for kind in range(3):
        pieces = [
            sums[place][:, kind * heads * width : (kind + 1) * heads * width]
            for place in range(fsdp_size)
        ]
        columns.append(jnp.concatenate(pieces, axis=1)[:, :model_width])
    gathered = jnp.concatenate(columns, axis=1)
    feature_rows = gathered.shape[0]
    gain = jnp.sum(gathered * attention_in[...].astype(F32), axis=1, keepdims=True)
    gain = padded_rows(jnp.broadcast_to(gain, (feature_rows, 128)), 128).T
    grad_gain[...] = gain[0:1, :feature_rows]
    grad_in[...] = gathered * as_column(attention_gain[...], feature_rows)
    grad_out[...] = jnp.sum(out_parts[...].astype(F32), axis=0)
    extra = sum(part[:, lanes.base :] for part in sums)
    extra_t = padded_rows(extra, 128).T
    grad_mixture[...] = extra_t[lanes.gain : lanes.gain + 1, :feature_rows]
    grad_router[...] = extra_t[lanes.router : lanes.router + experts, :feature_rows]
    grad_table[...] = extra[: grad_table.shape[0], lanes.table : lanes.table + head_count]
    mass = jnp.broadcast_to(extra[0:1], (8, lanes.extra))
    mass = pltpu.roll(mass, lanes.extra - lanes.shift, 1)
    lane = expert_lane(mass.shape, lanes)
    terms = jnp.where((lane >= 0) & (lane < experts), mass * counts[...], 0.0)[0:1]
    balance[...] = jnp.sum(terms, axis=1, keepdims=True) * (
        experts / (2.0 * token_total * token_total)
    )


def sum_kernel(*refs, local, terms):
    outputs = refs[2 * local * terms :]
    for which in range(2):
        for index in range(local):
            first = (index * 2 + which) * terms
            shape = outputs[which].shape[1:]
            total = refs[first][...].reshape(shape).astype(F32)
            for ref in refs[first + 1 : first + terms]:
                total = total + ref[...].reshape(shape).astype(F32)
            outputs[which][index] = total


def sum_grads(groups, up_shape, down_shape, blocks):
    local = len(groups)
    depth, part = up_shape[1], down_shape[1]
    sizes = ((depth, part), (part // blocks, down_shape[2]))
    arrays, specs = [], []
    for group in groups:
        for size, (keep, taken, passed) in zip(sizes, group):
            for array in (keep, taken, *passed):
                arrays.append(array)
                specs.append(pl.BlockSpec(size, lambda c: (c, 0)))
    return pl.pallas_call(
        partial(sum_kernel, local=local, terms=len(arrays) // (2 * local)),
        grid=(blocks,),
        in_specs=specs,
        out_specs=[
            pl.BlockSpec((local, depth, part), lambda c: (0, 0, c)),
            pl.BlockSpec((local, part // blocks, down_shape[2]), lambda c: (0, c, 0)),
        ],
        out_shape=(shape_of(up_shape, F32), shape_of(down_shape, F32)),
        compiler_params=params(),
        cost_estimate=hint(8),
        name="sum_grads",
    )(*arrays)


def over_x(array, hop):
    fsdp_size = lax.axis_size("fsdp")
    return lax.ppermute(array, "fsdp", [(i, (i + 2 * hop) % fsdp_size) for i in range(fsdp_size)])


def over_core(array):
    return lax.ppermute(array, "fsdp", [(i, i ^ 1) for i in range(lax.axis_size("fsdp"))])


def on_device(
    tokens,
    cotangent,
    segments,
    routes,
    slots,
    attention_gain,
    mixture_gain,
    attention_in,
    attention_out,
    router_weight,
    position_table,
    expert_up,
    expert_down,
):
    grid = Grid()
    exp_size, fsdp_size, chips = grid.exp_size, grid.fsdp_size, grid.x_size
    device_count = grid.device_count
    fsdp_index = lax.axis_index("fsdp")
    rows, model_width = tokens.shape
    length = rows * fsdp_size
    head_count = position_table.shape[1]
    width = model_width // head_count
    heads = -(-head_count // fsdp_size)
    padded_heads = heads * fsdp_size
    feature_rows, bucket_rows = attention_in.shape[0], position_table.shape[0]
    experts = router_weight.shape[1]
    local = expert_up.shape[0]
    capacity = 4 * rows // experts
    token_total = rows * device_count
    span = WINDOW + 2 * SKEW + QUERY_BLOCK
    lanes = Lanes(heads, width, padded_heads, experts)
    part = expert_down.shape[1]
    gain_row = attention_gain.reshape(1, feature_rows)

    shard_shapes = [shape_of((model_width, part), BF16), shape_of((part, model_width), BF16)]
    copies = (
        4 * fsdp_size + grid.z_size + grid.z_size * grid.y_size
        + grid.z_size + grid.y_size + grid.x_size + 1
    )
    started = pl.pallas_call(
        partial(
            start_kernel, lanes=lanes, heads=heads, width=width, head_count=head_count,
            experts=experts, capacity=capacity, local=local,
        ),
        out_shape=tuple(
            [
                shape_of((fsdp_size, rows, model_width), BF16),
                shape_of((grid.z_size, grid.y_size, fsdp_size, feature_rows, lanes.width), BF16),
                shape_of((experts * capacity, model_width), BF16),
                shape_of((8, rows), F32),
                shape_of((rows, 128), F32),
                shape_of((grid.z_size, grid.y_size, chips, 2, feature_rows, model_width), BF16),
            ]
            + shard_shapes * local
        ),
        in_specs=[IN_VMEM] * 10 + [ANYWHERE] * 2,
        out_specs=tuple(
            [ANYWHERE, ANYWHERE, IN_VMEM, IN_VMEM, IN_VMEM, ANYWHERE] + [ANYWHERE] * (2 * local)
        ),
        scratch_shapes=[
            pltpu.VMEM((fsdp_size, feature_rows, lanes.width), BF16),
            pltpu.VMEM(expert_up.shape, BF16),
            pltpu.VMEM(expert_down.shape, BF16),
            dma_sems(copies),
            dma_sems(copies),
            dma_sems(3),
            dma_sems(2 * local),
            dma_sems(local * (fsdp_size + 1)),
        ],
        compiler_params=params(collective_id=0, has_side_effects=True),
        cost_estimate=hint(20),
        name="start",
    )(
        tokens, cotangent, routes.T, slots.T, gain_row, mixture_gain.reshape(1, feature_rows),
        attention_in, router_weight.T, position_table, attention_out, expert_up, expert_down,
    )
    all_tokens, all_planes, cotangent_slots, position_rows, columns, full_out = started[:6]
    own_shards = [started[6 + 2 * index : 8 + 2 * index] for index in range(local)]
    plane = all_planes.reshape(model_width, lanes.width)
    full_out = full_out.reshape(model_width, model_width)

    def along_x(array):
        return [over_x(array, -hop) for hop in range(1, chips)]

    near_up, near_down = [None] * local, [None] * local
    near_up[0] = along_x(own_shards[0][0])
    cotangent_in = lax.all_to_all(
        cotangent_slots.reshape(exp_size, local * capacity, model_width),
        "exp", split_axis=0, concat_axis=0, tiled=True,
    ).reshape(exp_size, local, capacity, model_width)

    head_t = lambda size: pl.BlockSpec((heads, size, rows), lambda s, *_: (0, 0, s))
    head_n = lambda size: pl.BlockSpec((heads, rows, size), lambda s, *_: (0, s, 0))
    normed, query_t, key_n, query_n, value_n, key_t, value_t, bias, counts = pl.pallas_call(
        partial(
            project_kernel, heads=heads, width=width, lanes=lanes, feature_rows=feature_rows,
            bucket_rows=bucket_rows,
        ),
        grid=(fsdp_size,),
        in_specs=[
            pl.BlockSpec((1, rows, model_width), lambda s: (s, 0, 0)),
            whole((model_width, lanes.width)),
            pl.BlockSpec((1, rows), lambda s: (0, s)),
        ],
        out_specs=[
            pl.BlockSpec((rows, model_width), lambda s: (s, 0)),
            head_t(SKEW), head_n(SKEW), head_n(width), head_n(width), head_t(width), head_t(width),
            whole((heads, 1, span)),
            whole((8, lanes.extra)),
        ],
        out_shape=(
            shape_of((length, model_width), BF16),
            shape_of((heads, SKEW, length), BF16),
            shape_of((heads, length, SKEW), BF16),
            shape_of((heads, length, width), BF16),
            shape_of((heads, length, width), BF16),
            shape_of((heads, width, length), BF16),
            shape_of((heads, width, length), BF16),
            shape_of((heads, 1, span), F32),
            shape_of((8, lanes.extra), F32),
        ),
        scratch_shapes=[
            pltpu.VMEM((lanes.weights, model_width), BF16),
            pltpu.VMEM((lanes.extra, span), F32),
        ],
        compiler_params=params(),
        cost_estimate=hint(8),
        name="project",
    )(all_tokens, plane, segments.reshape(1, length))

    by_head = lambda *size: pl.BlockSpec((1,) + size, lambda h: (h, 0, 0))
    context, context_high, log_total = pl.pallas_call(
        partial(attend_kernel, rows=rows),
        grid=(heads,),
        in_specs=[
            by_head(SKEW, length), by_head(length, SKEW), by_head(width, length), by_head(1, span),
        ],
        out_specs=[
            pl.BlockSpec((fsdp_size, width, rows), lambda h: (0, h, 0)),
            by_head(width, length),
            by_head(1, length),
        ],
        out_shape=(
            shape_of((fsdp_size, heads * width, rows), BF16),
            shape_of((heads, width, length), F32),
            shape_of((heads, 1, length), F32),
        ),
        scratch_shapes=[
            pltpu.VMEM((SKEW, span), F32),
            pltpu.VMEM((WINDOW + QUERY_BLOCK, QUERY_BLOCK), F32),
        ],
        compiler_params=params(),
        cost_estimate=hint(13),
        name="attend",
    )(query_t, key_n, value_t, bias)

    (attended_t,) = exchange("fsdp", [(context, None)], 1, 9)
    own_down, near_up[0], attended_t = lax.optimization_barrier(
        (own_shards[0][1], near_up[0], attended_t)
    )
    near_down[0] = along_x(own_down)
    attended_t = attended_t.reshape(padded_heads * width, rows)

    gate_lanes = -(-local * capacity // 128) * 128
    hidden, routed, probabilities, gates, outgoing, slot_gates = pl.pallas_call(
        partial(route_kernel, experts=experts, lanes=lanes, capacity=capacity),
        out_shape=(
            shape_of((rows, model_width), F32),
            shape_of((rows, model_width), BF16),
            shape_of((rows, lanes.extra), F32),
            shape_of((rows, 2), F32),
            shape_of((experts * capacity, model_width), BF16),
            shape_of((exp_size, 8, gate_lanes), F32),
        ),
        compiler_params=params(),
        cost_estimate=hint(7),
        name="route",
    )(tokens, attended_t, full_out, plane, columns, position_rows)

    later = [own_shards[index] for index in range(1, local)]
    outgoing, later = lax.optimization_barrier((outgoing, later))
    for index in range(1, local):
        near_up[index], near_down[index] = [along_x(array) for array in later[index - 1]]
    outgoing = outgoing.reshape(exp_size, local, capacity, model_width)

    def pass_along(arrays):
        return [over_x(arrays[0][hop - 1], hop) for hop in range(1, chips)]

    ready = [own_shards[0][0]] + near_up[0] + [own_shards[0][1]]
    rows_in, gates_in, *crossed = exchange(
        "exp", [(outgoing, 0), (slot_gates, None)], 2, 28, across=ready
    )
    swapped = (crossed[:-1], crossed[-1:])
    returned, groups, moved, outs = [], [], [], None
    for index in range(local):
        final = index == local - 1
        carried = list(moved) if final else list(moved) + [(outgoing, index + 1)]
        result = run_expert(
            index, local, outgoing, slot_gates, rows_in, gates_in, cotangent_in,
            [own_shards[index][0]] + near_up[index], [own_shards[index][1]] + near_down[index],
            swapped, () if final else own_shards[index + 1], carried, outs, 3 + index,
        )
        (outs,) = result.rows_out
        arrived = list(result.moved_to)
        if not final:
            rows_in = arrived.pop()
            swapped = (result.next_swapped[:1], result.next_swapped[1:])
            moved = [(result.grad_rows[0], None), (result.grad_gates[0], None)]
        if arrived:
            returned.append(arrived)
        up_keep, up_taken, down_keep, down_taken = result.own
        if not final:
            passed = (result.pass_up, result.pass_down)
            passed, rows_in = lax.optimization_barrier((passed, rows_in))
            groups.append(
                [
                    (up_keep, up_taken, pass_along(passed[0])),
                    (down_keep, down_taken, pass_along(passed[1])),
                ]
            )
    returned.append([result.back_rows[0], result.back_gates[0]])
    groups, returned = lax.optimization_barrier((groups, returned))

    outs, returned = lax.optimization_barrier((outs, returned))
    out_rows = lax.all_to_all(outs, "exp", split_axis=0, concat_axis=0, tiled=True)

    grad_hidden, grad_branch, small = pl.pallas_call(
        partial(
            unroute_kernel, experts=experts, local=local, token_total=token_total, lanes=lanes
        ),
        out_shape=(
            shape_of((rows, model_width), F32),
            shape_of((rows, model_width), BF16),
            shape_of((model_width, lanes.extra), F32),
        ),
        compiler_params=params(),
        cost_estimate=hint(1),
        name="unroute",
    )(
        hidden, cotangent, routed, probabilities, gates, plane, columns, counts,
        *[part[0] for part in returned], *[part[1] for part in returned],
    )

    all_branch = gather_rows(grad_branch, 4 + local, 1)
    pass_down, all_branch = lax.optimization_barrier((result.pass_down, all_branch))
    groups.append(
        [
            (up_keep, up_taken, pass_along(result.pass_up)),
            (down_keep, down_taken, pass_along(pass_down)),
        ]
    )
    padded_out = full_out
    if padded_heads > head_count:
        padded_out = jnp.pad(full_out, ((0, padded_heads * width - model_width), (0, 0)))
    grad_t, grad_n, out_grad = pl.pallas_call(
        partial(context_grad_kernel, heads=heads, width=width),
        grid_spec=pltpu.PrefetchScalarGridSpec(
            num_scalar_prefetch=1,
            grid=(fsdp_size,),
            in_specs=[
                pl.BlockSpec((1, rows, model_width), lambda s, f: (s, 0, 0)),
                pl.BlockSpec((heads * width, model_width), lambda s, f: (f[0], 0)),
                pl.BlockSpec((1, heads * width, rows), lambda s, f: (s, 0, 0)),
            ],
            out_specs=[head_t(width), head_n(width), whole((heads * width, model_width))],
            scratch_shapes=[pltpu.VMEM((heads * width, model_width), F32)],
        ),
        out_shape=(
            shape_of((heads, width, length), BF16),
            shape_of((heads, length, width), BF16),
            shape_of((heads * width, model_width), BF16),
        ),
        compiler_params=params(),
        cost_estimate=hint(1),
        name="context_grad",
    )(fsdp_index.reshape(1), all_branch, padded_out, context)

    grad_projected, grad_bias = pl.pallas_call(
        partial(attend_back_kernel, scale=width ** (-0.5)),
        grid=(heads,),
        in_specs=[
            by_head(SKEW, length), by_head(length, SKEW), by_head(length, width),
            by_head(length, width), by_head(width, length), by_head(width, length),
            by_head(length, width), by_head(width, length), by_head(1, length), by_head(1, span),
        ],
        out_specs=[
            pl.BlockSpec((3, 1, width, length), lambda h: (0, h, 0, 0)),
            by_head(1, span),
        ],
        out_shape=(
            shape_of((3, heads, width, length), BF16),
            shape_of((heads, 1, span), F32),
        ),
        scratch_shapes=[
            pltpu.VMEM((SKEW, span), F32),
            pltpu.VMEM((SKEW, span), F32),
            pltpu.VMEM((length, width), F32),
            pltpu.VMEM((length, width), F32),
        ],
        compiler_params=params(),
        cost_estimate=hint(1),
        name="attend_back",
    )(query_t, key_n, query_n, value_n, key_t, grad_t, grad_n, context_high, log_total, bias)
    grad_projected = grad_projected.reshape(lanes.weights, length)

    grad_first, grad_plane = pl.pallas_call(
        partial(
            project_back_kernel, lanes=lanes, heads=heads, feature_rows=feature_rows,
            bucket_rows=bucket_rows,
        ),
        grid=(fsdp_size,),
        in_specs=[
            pl.BlockSpec((lanes.weights, rows), lambda s: (0, s)),
            pl.BlockSpec((rows, model_width), lambda s: (s, 0)),
            whole((model_width, lanes.width)),
            whole((model_width, lanes.extra)),
            whole((rows, lanes.extra)),
            whole((heads, 1, span)),
        ],
        out_specs=[
            pl.BlockSpec((1, model_width, rows), lambda s: (s, 0, 0)),
            whole((model_width, lanes.width)),
        ],
        out_shape=(
            shape_of((fsdp_size, model_width, rows), BF16),
            shape_of((model_width, lanes.width), BF16),
        ),
        scratch_shapes=[
            pltpu.VMEM((lanes.width, model_width), F32),
            pltpu.VMEM((lanes.extra, span), F32),
        ],
        compiler_params=params(),
        cost_estimate=hint(1),
        name="project_back",
    )(grad_projected, normed, plane, small, probabilities, grad_bias)

    out_rows, grad_first = lax.optimization_barrier((out_rows, grad_first))
    spread_out = heads * width * fsdp_size != model_width
    if spread_out:
        out_grad = lax.dynamic_update_slice(
            jnp.zeros((padded_heads * width, model_width), BF16), out_grad,
            (fsdp_index * heads * width, jnp.int32(0)),
        )[:model_width]
    out_grad = out_grad.reshape(-1, feature_rows, model_width)
    out_count = device_count if spread_out else exp_size
    plane_shape = (grid.z_size, grid.y_size, fsdp_size, feature_rows, lanes.width)
    parts_shape = (fsdp_size, feature_rows, lanes.width)
    copies = 3 * fsdp_size + grid.z_size * grid.y_size + grid.z_size + out_count
    first_parts, plane_parts, out_parts = pl.pallas_call(
        partial(last_kernel, spread_out=spread_out),
        out_shape=(
            shape_of((chips, model_width, rows), BF16),
            shape_of(parts_shape, BF16),
            shape_of((out_count, feature_rows, model_width), BF16),
        ),
        in_specs=[IN_VMEM] * 3,
        out_specs=(IN_VMEM, ANYWHERE, ANYWHERE),
        scratch_shapes=[
            pltpu.VMEM((chips, model_width, rows), BF16),
            pltpu.VMEM((max(chips - 1, 1), model_width, rows), BF16),
            pltpu.VMEM((max(grid.y_size - 1, 1), grid.z_size) + parts_shape, BF16),
            pltpu.VMEM((grid.z_size,) + parts_shape, BF16),
            pltpu.VMEM((max(grid.z_size - 1, 1),) + parts_shape, BF16),
            pltpu.VMEM(parts_shape, BF16),
            dma_sems(copies),
            dma_sems(copies),
            dma_sems(2),
        ],
        compiler_params=params(collective_id=5 + local, has_side_effects=True),
        cost_estimate=hint(1),
        name="last",
    )(grad_first, grad_plane.reshape(plane_shape), out_grad)

    groups, first_parts = lax.optimization_barrier((groups, first_parts))
    (
        grad_tokens, gain_grad, in_grad, out_sum, mixture_gain_grad, router_grad, table_grad, balance,
    ) = pl.pallas_call(
        partial(
            finish_kernel, lanes=lanes, heads=heads, width=width, head_count=head_count,
            experts=experts, token_total=token_total,
        ),
        out_shape=(
            shape_of((rows, model_width), F32),
            shape_of((1, feature_rows), F32),
            shape_of((feature_rows, 3 * model_width), F32),
            shape_of((feature_rows, model_width), F32),
            shape_of((1, feature_rows), F32),
            shape_of((experts, feature_rows), F32),
            shape_of((bucket_rows, head_count), F32),
            shape_of((1, 1), F32),
        ),
        compiler_params=params(),
        cost_estimate=hint(6),
        name="finish",
    )(first_parts, plane_parts, out_parts, tokens, grad_hidden, attention_in, gain_row, counts)

    layer_output = pl.pallas_call(
        partial(mixture_kernel, local=local),
        out_shape=shape_of((rows, model_width), BF16),
        compiler_params=params(),
        cost_estimate=hint(5),
        name="mixture",
    )(hidden, gates, columns, out_rows)

    up_grad, down_grad = sum_grads(groups, expert_up.shape, expert_down.shape, fsdp_size)
    return (
        layer_output,
        balance.reshape(()),
        grad_tokens,
        gain_grad.reshape(feature_rows),
        mixture_gain_grad.reshape(feature_rows),
        in_grad,
        out_sum,
        router_grad.T,
        table_grad,
        up_grad,
        down_grad,
    )


def solution(mesh):
    in_specs = (
        P(("exp", "fsdp"), None),
        P(("exp", "fsdp"), None),
        P("exp"),
        P(("exp", "fsdp"), None),
        P(("exp", "fsdp"), None),
        P(("exp", "fsdp")),
        P(("exp", "fsdp")),
        P(("exp", "fsdp"), None),
        P(("exp", "fsdp"), None),
        P(("exp", "fsdp"), None),
        P(("exp", "fsdp"), None),
        P("exp", "fsdp", None),
        P("exp", "fsdp", None),
    )
    out_specs = (
        P(("exp", "fsdp"), None),
        P(),
        P(("exp", "fsdp"), None),
        P(("exp", "fsdp")),
        P(("exp", "fsdp")),
        P(("exp", "fsdp"), None),
        P(("exp", "fsdp"), None),
        P(("exp", "fsdp"), None),
        P(("exp", "fsdp"), None),
        P("exp", "fsdp", None),
        P("exp", "fsdp", None),
    )
    return jax.shard_map(
        on_device, mesh=mesh, in_specs=in_specs, out_specs=out_specs, check_vma=False
    )
```

```python
from functools import partial

import jax
import jax.numpy as jnp
from jax import lax
from jax.experimental import pallas as pl
from jax.experimental.pallas import tpu as pltpu
from jax.sharding import PartitionSpec as P

WINDOW = 1024
BUCKETS = 256

EPSILON = 1e-06
AUX_WEIGHT = 0.01
MASKED = -1e30
QUERY_BLOCK = 256
SKEW = 128
VMEM_BYTES = 58 * 1024 * 1024
MESH = pl.DeviceIdType.MESH
F32 = jnp.float32
BF16 = jnp.bfloat16


def params(**kwargs):
    return pltpu.CompilerParams(vmem_limit_bytes=VMEM_BYTES, **kwargs)


def shape_of(shape, dtype):
    return jax.ShapeDtypeStruct(shape, dtype)


def whole(shape):
    return pl.BlockSpec(shape, lambda *_: (0,) * len(shape))


def contract_last(left_side, right_side):
    return lax.dot_general(
        left_side, right_side, (((1,), (1,)), ((), ())), preferred_element_type=F32
    )


def contract_first(left_side, right_side):
    return lax.dot_general(
        left_side, right_side, (((0,), (0,)), ((), ())), preferred_element_type=F32
    )


def matmul(left_side, right_side):
    return jnp.dot(left_side, right_side, preferred_element_type=F32)


def turned(value):
    return value.astype(F32).T


def bucket_index(distance):
    near_count = BUCKETS // 2
    spread = max(WINDOW - near_count, 1)
    far_bucket = (
        near_count + jnp.maximum(distance - near_count, 0) * (BUCKETS - near_count) // spread
    )
    return jnp.where(distance < near_count, distance, far_bucket)

def hint(micros):
    return pl.CostEstimate(flops=int(micros * 1.0e9), bytes_accessed=1024, transcendentals=0)


class Grid:
    def __init__(self):
        self.exp_size, self.fsdp_size = lax.axis_size("exp"), lax.axis_size("fsdp")
        self.device_count = self.exp_size * self.fsdp_size
        self.y_size = max(
            y for y in range(1, self.exp_size + 1) if self.exp_size % y == 0 and 2 * y * y <= self.exp_size
        ) if self.exp_size > 1 else 1
        self.z_size = self.exp_size // self.y_size
        self.x_size = self.fsdp_size // 2

    def here(self):
        self.exp, self.fsdp = lax.axis_index("exp"), lax.axis_index("fsdp")
        self.z, self.y = self.exp // self.y_size, self.exp % self.y_size
        self.x, self.core = self.fsdp // 2, self.fsdp % 2
        self.linear = self.exp * self.fsdp_size + self.fsdp
        return self

    def at(self, z=None, y=None, fsdp=None):
        z = self.z if z is None else z
        y = self.y if y is None else y
        return (z * self.y_size + y, self.fsdp if fsdp is None else fsdp)

    def x_from(self, hop):
        return ((self.x + self.x_size + hop) % self.x_size) * 2 + self.core

    def sibling(self, fsdp):
        return fsdp + 1 - 2 * (fsdp % 2)


class Links:
    def __init__(self, send, receive):
        self.send, self.receive, self.used = send, receive, 0

    def copy(self, source, target, device, landing):
        index = self.used
        self.used += 1
        going = pltpu.make_async_remote_copy(
            src_ref=source, dst_ref=target, send_sem=self.send.at[index],
            recv_sem=self.receive.at[index], device_id=device, device_id_type=MESH,
        )
        coming = pltpu.make_async_remote_copy(
            src_ref=landing, dst_ref=landing, send_sem=self.send.at[index],
            recv_sem=self.receive.at[index], device_id=device, device_id_type=MESH,
        )
        return going, coming


def greet(devices):
    barrier = pltpu.get_barrier_semaphore()
    for device in devices:
        pl.semaphore_signal(barrier, inc=1, device_id=device, device_id_type=MESH)
    pl.semaphore_wait(barrier, len(devices))


def chip_peers(grid):
    peers = [(grid.exp, grid.sibling(grid.fsdp))]
    return peers + [(grid.exp, grid.x_from(hop)) for hop in range(1, grid.x_size)]


class ChipGather:
    def __init__(self, grid, links, own_sem, source, target):
        self.grid, self.links, self.target = grid, links, target
        self.own = pltpu.make_async_copy(source, target.at[grid.fsdp], own_sem)
        sibling = grid.sibling(grid.fsdp)
        self.along_x, self.across = [], []
        for hop in range(1, grid.x_size):
            self.along_x.append(
                links.copy(
                    source, target.at[grid.fsdp], (grid.exp, grid.x_from(hop)),
                    target.at[grid.x_from(-hop)],
                )
            )
        self.across.append(
            links.copy(source, target.at[grid.fsdp], (grid.exp, sibling), target.at[sibling])
        )

    def start(self):
        for going, _ in self.along_x + self.across:
            going.start()
        self.own.start()

    def forward(self):
        grid = self.grid
        for hop in range(1, grid.x_size):
            self.along_x[hop - 1][1].wait_recv()
            held = grid.x_from(-hop)
            other = grid.sibling(held)
            self.across.append(
                self.links.copy(
                    self.target.at[held], self.target.at[held],
                    (grid.exp, grid.sibling(grid.fsdp)), self.target.at[other],
                )
            )
            self.across[-1][0].start()

    def finish(self):
        for _, coming in self.across:
            coming.wait_recv()
        for going, _ in self.along_x + self.across:
            going.wait_send()
        self.own.wait()


class Exchange:
    def __init__(self, grid, axis, links, own_sems, pairs):
        size = grid.exp_size if axis == "exp" else grid.fsdp_size
        place = grid.exp if axis == "exp" else grid.fsdp
        device = (lambda to: (to, grid.fsdp)) if axis == "exp" else (lambda to: (grid.exp, to))
        self.peers = [device((place + hop) % size) for hop in range(1, size)]
        self.copies, self.own = [], []
        for index, (source, target) in enumerate(pairs):
            for hop in range(1, size):
                to, origin = (place + hop) % size, (place + size - hop) % size
                self.copies.append(
                    links.copy(source(to), target.at[place], device(to), target.at[origin])
                )
            self.own.append(
                pltpu.make_async_copy(source(place), target.at[place], own_sems.at[index])
            )

    def start(self):
        for going, _ in self.copies:
            going.start()
        for own in self.own:
            own.start()

    def finish(self):
        for going, coming in self.copies:
            coming.wait_recv()
            going.wait_send()
        for own in self.own:
            own.wait()


ANYWHERE = pl.BlockSpec(memory_space=pl.ANY)
IN_VMEM = pl.BlockSpec(memory_space=pltpu.VMEM)


def dma_sems(count):
    return pltpu.SemaphoreType.DMA((count,))


def exchange(axis, arrays, collective_id, micros, across=()):
    grid = Grid()
    size = grid.exp_size if axis == "exp" else grid.fsdp_size
    count, crossing = len(arrays), len(across)
    parts = [part for _, part in arrays]

    def kernel(*refs):
        sources, over = refs[:count], refs[count : count + crossing]
        refs = refs[count + crossing :]
        targets, landed = refs[:count], refs[count : count + crossing]
        send, receive, own = refs[count + crossing :]
        place = grid.here()
        links = Links(send, receive)
        sibling = (place.exp, place.sibling(place.fsdp))
        pairs = [
            (partial(plane_of, source, part), target)
            for source, part, target in zip(sources, parts, targets)
        ]
        work = Exchange(place, axis, links, own, pairs)
        swaps = [
            links.copy(source, target, sibling, target) for source, target in zip(over, landed)
        ]
        greet(work.peers + ([sibling] if swaps and axis == "exp" else []))
        work.start()
        for going, _ in swaps:
            going.start()
        work.finish()
        for going, coming in swaps:
            coming.wait_recv()
            going.wait_send()

    return pl.pallas_call(
        kernel,
        out_shape=tuple(
            [
                shape_of((size,) + array.shape[(1 if part is None else 2) :], array.dtype)
                for array, part in arrays
            ]
            + [shape_of(array.shape, array.dtype) for array in across]
        ),
        in_specs=[IN_VMEM] * count + [ANYWHERE] * crossing,
        out_specs=tuple([ANYWHERE] * (count + crossing)),
        scratch_shapes=[
            dma_sems(count * size + crossing), dma_sems(count * size + crossing), dma_sems(count),
        ],
        compiler_params=params(collective_id=collective_id, has_side_effects=True),
        cost_estimate=hint(micros),
        name=f"exchange_{collective_id}",
    )(*[array for array, _ in arrays], *across)


def plane_of(source, part, to):
    return source.at[to] if part is None else source.at[to, part]


def gather_rows(array, collective_id, micros):
    grid = Grid()

    def kernel(source, target, send, receive, own):
        place = grid.here()
        work = ChipGather(place, Links(send, receive), own.at[0], source, target)
        greet(chip_peers(place))
        work.start()
        work.forward()
        work.finish()

    return pl.pallas_call(
        kernel,
        out_shape=shape_of((grid.fsdp_size,) + array.shape, array.dtype),
        in_specs=[IN_VMEM],
        out_specs=ANYWHERE,
        scratch_shapes=[dma_sems(2 * grid.fsdp_size), dma_sems(2 * grid.fsdp_size), dma_sems(1)],
        compiler_params=pltpu.CompilerParams(collective_id=collective_id, has_side_effects=True),
        cost_estimate=hint(micros),
        name=f"gather_{collective_id}",
    )(array)


class Lanes:
    def __init__(self, heads, width, padded_heads, experts):
        self.weights = 3 * heads * width
        self.base = self.weights // 128 * 128
        self.router = self.weights - self.base
        self.gain = self.router + experts
        self.table = self.gain + 1
        self.count = self.table + padded_heads
        self.width = -(-(self.weights + 2 * experts + 1 + padded_heads) // 128) * 128
        self.extra = self.width - self.base
        self.shift = self.count - self.router


def bucket_rows_select(features, feature_rows, bucket_rows, span):
    row = lax.broadcasted_iota(jnp.int32, (features, 1), 0)
    within = lax.rem(row, feature_rows)
    bucket = jnp.where(
        within < bucket_rows, lax.div(row, feature_rows) * bucket_rows + within, -1
    )
    distance = lax.broadcasted_iota(jnp.int32, (1, span), 1) - SKEW
    near = BUCKETS // 2
    spread = max(WINDOW - near, 1)
    far = near + lax.div(jnp.maximum(distance - near, 0) * (BUCKETS - near), spread)
    wanted = jnp.where(distance < near, distance, far)
    reachable = (distance >= 0) & (distance < WINDOW)
    wanted = jnp.where(reachable, wanted, -2)
    return jnp.where(bucket == wanted, 1.0, 0.0).astype(BF16), reachable


def as_column(row, size):
    row_place = lax.broadcasted_iota(jnp.int32, (size, size), 0)
    lane = lax.broadcasted_iota(jnp.int32, (size, size), 1)
    spread = jnp.broadcast_to(row.astype(F32), (size, size))
    return jnp.sum(jnp.where(row_place == lane, spread, 0.0), axis=1, keepdims=True)


def padded_rows(value, rows):
    if value.shape[0] == rows:
        return value
    return jnp.concatenate([value, jnp.zeros((rows - value.shape[0], value.shape[1]), F32)], axis=0)


def padded_lanes(value, lanes):
    if value.shape[1] == lanes:
        return value
    return jnp.concatenate([value, jnp.zeros((value.shape[0], lanes - value.shape[1]), F32)], axis=1)


class Wide:
    def __init__(self, grid, links, own_sem, source, target):
        self.grid, self.links, self.target = grid, links, target
        self.own = pltpu.make_async_copy(
            source, target.at[grid.z, grid.y, grid.x, grid.core], own_sem
        )
        stage = []
        for hop in range(1, grid.z_size):
            origin = (grid.z + grid.z_size - hop) % grid.z_size
            stage.append(
                links.copy(
                    source, target.at[grid.z, grid.y, grid.x, grid.core],
                    grid.at(z=(grid.z + hop) % grid.z_size),
                    target.at[origin, grid.y, grid.x, grid.core],
                )
            )
        self.stages = [stage]

    def start(self):
        self.own.start()
        for going, _ in self.stages[0]:
            going.start()

    def turn(self, axis):
        grid, target = self.grid, self.target
        for _, coming in self.stages[-1]:
            coming.wait_recv()
        stage = []
        if axis == 0:
            self.own.wait()
            held = target.at[:, grid.y, grid.x, grid.core]
            for hop in range(1, grid.y_size):
                origin = (grid.y + grid.y_size - hop) % grid.y_size
                stage.append(
                    self.links.copy(
                        held, held, grid.at(y=(grid.y + hop) % grid.y_size),
                        target.at[:, origin, grid.x, grid.core],
                    )
                )
        elif axis == 1:
            held = target.at[:, :, grid.x, grid.core]
            for hop in range(1, grid.x_size):
                origin = (grid.x + grid.x_size - hop) % grid.x_size
                stage.append(
                    self.links.copy(
                        held, held, (grid.exp, grid.x_from(hop)),
                        target.at[:, :, origin, grid.core],
                    )
                )
        else:
            held = target.at[:, :, :, grid.core]
            stage.append(
                self.links.copy(
                    held, held, (grid.exp, grid.sibling(grid.fsdp)), target.at[:, :, :, 1 - grid.core]
                )
            )
        for going, _ in stage:
            going.start()
        self.stages.append(stage)

    def finish(self):
        for _, coming in self.stages[-1]:
            coming.wait_recv()
        for stage in self.stages:
            for going, _ in stage:
                going.wait_send()


def start_kernel(
    tokens, cotangent, routes_t, slots_t, attention_gain, mixture_gain, attention_in, router_t, table,
    attention_out, expert_up, expert_down, *refs, lanes, heads, width, head_count, experts, capacity,
    local, late,
):
    all_tokens, all_planes, cotangent_early, position_rows, columns, full_out = refs[:6]
    cotangent_late, refs = refs[6 : 6 + late], refs[6 + late :]
    shards = refs[: 2 * local]
    planes, up_stage, down_stage, send, receive, own, fetch, split = refs[2 * local :]
    grid = Grid().here()
    links = Links(send, receive)
    z_size, y_size, fsdp_size = grid.z_size, grid.y_size, grid.fsdp_size
    near = [
        (grid.exp, (grid.fsdp + turn) % fsdp_size) for turn in range(1, fsdp_size)
    ] + [grid.at(z=(grid.z + hop) % z_size) for hop in range(1, z_size)]
    beside = [grid.at(y=(grid.y + hop) % y_size) for hop in range(1, y_size)]
    gathered = ChipGather(grid, links, own.at[0], tokens, all_tokens)
    widely = Wide(grid, links, own.at[2], attention_out, full_out)
    part = expert_down.shape[1]
    depth = expert_up.shape[1]
    fetches = []
    for index in range(local):
        fetches.append(
            pltpu.make_async_copy(expert_up.at[index], up_stage.at[index], fetch.at[2 * index])
        )
        fetches.append(
            pltpu.make_async_copy(
                expert_down.at[index], down_stage.at[index], fetch.at[2 * index + 1]
            )
        )
    greet(near + beside)
    widely.start()
    for copy in fetches:
        copy.start()

    feature_rows = attention_in.shape[0]
    model_width = head_count * width
    gained = attention_in[...].astype(F32) * as_column(attention_gain[...], feature_rows)
    route_rows, slot_rows = routes_t[...].astype(F32), slots_t[...].astype(F32)
    columns[...] = padded_rows(jnp.concatenate([route_rows, slot_rows], axis=0), 128).T
    row_count = columns.shape[0]
    expert_lanes = lax.broadcasted_iota(jnp.int32, (row_count, experts), 1).astype(F32)
    named = jnp.zeros((row_count, experts), F32)
    for k in range(2):
        named = named + jnp.where(expert_lanes == columns[:, k : k + 1], 1.0, 0.0)
    named = jnp.sum(named, axis=0, keepdims=True)
    place = lax.broadcasted_iota(jnp.int32, (feature_rows, feature_rows), 0)
    same = place == lax.broadcasted_iota(jnp.int32, (feature_rows, feature_rows), 1)
    router = contract_last(jnp.where(same, 1.0, 0.0).astype(BF16), router_t[...])
    pieces = [
        router,
        as_column(mixture_gain[...], feature_rows),
        padded_rows(padded_lanes(table[...].astype(F32), heads * fsdp_size), feature_rows),
        padded_rows(named, feature_rows),
    ]
    taken = sum(piece.shape[1] for piece in pieces)
    if lanes.width > lanes.weights + taken:
        pieces.append(jnp.zeros((feature_rows, lanes.width - lanes.weights - taken), F32))
    for place in range(fsdp_size):
        first, last = place * heads * width, min((place + 1) * heads * width, model_width)
        own_pieces = []
        for kind in range(3):
            if last > first:
                own_pieces.append(gained[:, kind * model_width + first : kind * model_width + last])
            if last - first < heads * width:
                own_pieces.append(
                    jnp.zeros((feature_rows, heads * width - max(last - first, 0)), F32)
                )
        planes[place] = jnp.concatenate(own_pieces + pieces, axis=1).astype(BF16)
    placed = []
    for turn in range(1, fsdp_size):
        to = (grid.fsdp + turn) % fsdp_size
        origin = (grid.fsdp + fsdp_size - turn) % fsdp_size
        placed.append(
            links.copy(
                planes.at[to], all_planes.at[grid.z, grid.y, grid.fsdp], (grid.exp, to),
                all_planes.at[grid.z, grid.y, origin],
            )
        )
        placed[-1][0].start()
    kept = pltpu.make_async_copy(
        planes.at[grid.fsdp], all_planes.at[grid.z, grid.y, grid.fsdp], own.at[1]
    )
    kept.start()
    gathered.start()
    for _, coming in placed:
        coming.wait_recv()
    kept.wait()

    def over_y(z):
        for turn in range(1, y_size):
            forwarded.append(
                links.copy(
                    all_planes.at[z, grid.y],
                    all_planes.at[z, grid.y],
                    grid.at(y=(grid.y + turn) % y_size),
                    all_planes.at[z, (grid.y + y_size - turn) % y_size],
                )
            )
            forwarded[-1][0].start()

    along_z, forwarded = [], []
    for hop in range(1, z_size):
        along_z.append(
            links.copy(
                all_planes.at[grid.z, grid.y],
                all_planes.at[grid.z, grid.y],
                grid.at(z=(grid.z + hop) % z_size),
                all_planes.at[(grid.z + z_size - hop) % z_size, grid.y],
            )
        )
        along_z[-1][0].start()
    over_y(grid.z)
    widely.turn(0)

    for copy in fetches:
        copy.wait()
    splits = []
    for index in range(local):
        up, down = shards[2 * index : 2 * index + 2]
        stores = [
            (
                up_stage.at[index, :, pl.ds(block * part, part)],
                up.at[pl.ds(block * depth, depth), :],
            )
            for block in range(fsdp_size)
        ]
        for source, target in stores + [(down_stage.at[index], down)]:
            splits.append(pltpu.make_async_copy(source, target, split.at[len(splits)]))
            splits[-1].start()

    widely.turn(1)

    place = route_rows * capacity + slot_rows
    position_rows[...] = padded_rows(place, 8)
    select_rows([cotangent_early] + list(cotangent_late), place, cotangent[...])

    for hop in range(1, z_size):
        along_z[hop - 1][1].wait_recv()
        over_y((grid.z + z_size - hop) % z_size)
    gathered.forward()
    widely.turn(2)
    for going, coming in forwarded:
        coming.wait_recv()
        going.wait_send()
    for going, _ in placed + along_z:
        going.wait_send()
    gathered.finish()
    widely.finish()
    for copy in splits:
        copy.wait()


def project_kernel(
    tokens, plane, segments, normed, query_t, key_n, query_n, value_n, key_t, value_t, bias, counts,
    weight_t, table_t, *, heads, width, lanes, feature_rows, bucket_rows,
):
    @pl.when(pl.program_id(0) == 0)
    def _():
        weight_t[...] = turned(plane[:, : lanes.weights]).astype(BF16)
        extra = plane[:, lanes.base :]
        span = bias.shape[2]
        select, reachable = bucket_rows_select(plane.shape[0], feature_rows, bucket_rows, span)
        table_t[...] = lax.dot_general(
            extra, select, (((0,), (0,)), ((), ())), preferred_element_type=F32
        )
        first = lanes.table + lax.axis_index("fsdp") * heads
        for head in range(heads):
            bias[head] = jnp.where(reachable, table_t[pl.ds(first + head, 1), :], MASKED)
        summed = jnp.sum(extra.astype(F32), axis=0, keepdims=True)
        counts[...] = pltpu.roll(
            jnp.broadcast_to(summed, counts.shape), lanes.extra - lanes.shift, 1
        )

    inputs = tokens[0].astype(F32)
    scale = lax.rsqrt(jnp.mean(inputs * inputs, axis=1, keepdims=True) + EPSILON)
    low = (inputs * scale).astype(BF16)
    normed[...] = low
    rows = low.shape[0]
    projected = contract_last(weight_t[...], low).astype(BF16).astype(F32)
    document = segments[...] % 4
    places = lax.broadcasted_iota(jnp.int32, (8, rows), 0)
    same = places == document
    hot = jnp.where(same, 1.0, 0.0)
    barred = jnp.where(same | (places >= 4), 0.0, MASKED)
    filler = jnp.zeros((SKEW - 8 - width, rows), F32)
    for head in range(heads):
        query = projected[head * width : (head + 1) * width] * width ** (-0.5)
        key = projected[(heads + head) * width : (heads + head + 1) * width]
        value = projected[(2 * heads + head) * width : (2 * heads + head + 1) * width]
        query_t[head] = jnp.concatenate([query, barred, filler], axis=0).astype(BF16)
        key_n[head] = jnp.concatenate([key, hot, filler], axis=0).T.astype(BF16)
        query_n[head] = query.T.astype(BF16)
        value_n[head] = value.T.astype(BF16)
        key_t[head] = key.astype(BF16)
        value_t[head] = value.astype(BF16)


def spans(length):
    for query_start in range(0, length, QUERY_BLOCK):
        key_start = max(0, query_start - WINDOW)
        yield query_start, key_start, query_start + QUERY_BLOCK - key_start


def spread_bias(bias, skew):
    skew[...] = pltpu.roll(
        jnp.broadcast_to(bias[0], skew.shape), 0, 1, stride=1, stride_axis=0
    )


def attend_kernel(query_t, key_n, value_t, bias, context, context_high, log_total, skew, scores, *, rows):
    spread_bias(bias, skew)
    for query_start, key_start, key_count in spans(query_t.shape[2]):
        queries = slice(query_start, query_start + QUERY_BLOCK)
        keys = slice(key_start, key_start + key_count)
        raw = matmul(key_n[0, keys, :], query_t[0, :, queries])
        for start in range(0, key_count, SKEW):
            offset = query_start - key_start - start + SKEW
            scores[start : start + SKEW, :] = (
                raw[start : start + SKEW] + skew[:, offset : offset + QUERY_BLOCK]
            )
        high = jnp.max(scores[:key_count, :], axis=0, keepdims=True)
        weights = jnp.exp(scores[:key_count, :] - high)
        total = jnp.sum(weights, axis=0, keepdims=True)
        gathered = matmul(value_t[0, :, keys], weights.astype(BF16)) / total
        context_high[0, :, queries] = gathered
        log_total[0, :, queries] = high + jnp.log(total)
        for start in range(0, QUERY_BLOCK, 128):
            place = query_start + start
            context[place // rows, :, place % rows : place % rows + 128] = gathered[
                :, start : start + 128
            ].astype(BF16)


def attend_back_kernel(
    query_t, key_n, query_n, value_n, key_t, grad_t, grad_n, context_high, log_total, bias,
    grad_projected, grad_bias, skew, grad_skew, grad_key, grad_value, *, scale,
):
    spread_bias(bias, skew)
    grad_skew[...] = jnp.zeros_like(grad_skew)
    grad_key[...] = jnp.zeros_like(grad_key)
    grad_value[...] = jnp.zeros_like(grad_value)
    inner = jnp.sum(grad_t[0].astype(F32) * context_high[0], axis=0, keepdims=True)
    for query_start, key_start, key_count in spans(query_t.shape[2]):
        queries = slice(query_start, query_start + QUERY_BLOCK)
        keys = slice(key_start, key_start + key_count)
        raw = matmul(key_n[0, keys, :], query_t[0, :, queries])
        grad_weights = matmul(value_n[0, keys, :], grad_t[0, :, queries])
        weights_low, grad_low = [], []
        for start in range(0, key_count, SKEW):
            offset = query_start - key_start - start + SKEW
            part = slice(start, start + SKEW)
            weights = jnp.exp(
                raw[part] + skew[:, offset : offset + QUERY_BLOCK] - log_total[0, :, queries]
            )
            grad_scores = weights * (grad_weights[part] - inner[:, queries])
            grad_skew[:, offset : offset + QUERY_BLOCK] += grad_scores
            weights_low.append(weights.astype(BF16))
            grad_low.append(grad_scores.astype(BF16))
        weights_low = jnp.concatenate(weights_low, axis=0)
        grad_low = jnp.concatenate(grad_low, axis=0)
        grad_projected[0, 0, :, queries] = (matmul(key_t[0, :, keys], grad_low) * scale).astype(BF16)
        grad_key[keys, :] += matmul(grad_low, query_n[0, queries, :])
        grad_value[keys, :] += matmul(weights_low, grad_n[0, queries, :])
    grad_projected[1, 0] = grad_key[...].T.astype(BF16)
    grad_projected[2, 0] = grad_value[...].T.astype(BF16)
    count = SKEW
    span = skew.shape[1]
    while count > 8:
        count //= 2
        grad_skew[:count, :] += pltpu.roll(grad_skew[count : 2 * count, :], span - count, 1)
    summed = grad_skew[0:1, :]
    for row in range(1, 8):
        summed = summed + pltpu.roll(grad_skew[row : row + 1, :], span - row, 1)
    grad_bias[0] = summed

def expert_lane(shape, lanes):
    return lax.broadcasted_iota(jnp.int32, shape, 1) - lanes.router


def int_columns(columns):
    values = columns[:, 0:4].astype(jnp.int32)
    return values[:, 0:2], values[:, 2:4]


def route_kernel(
    tokens, attended_t, attention_out, plane, columns, position_rows,
    hidden, routed, probabilities, gates, outgoing, slot_gates, *, experts, lanes, capacity,
):
    rows, model_width = tokens.shape
    routes, slots = int_columns(columns)
    attended_low = turned(attended_t[:model_width]).astype(BF16)
    hidden_state = tokens[...].astype(F32) + matmul(attended_low, attention_out[...])
    hidden[...] = hidden_state
    scale = lax.rsqrt(jnp.mean(hidden_state * hidden_state, axis=1, keepdims=True) + EPSILON)
    extra = plane[:, lanes.base :]
    gain = extra.astype(F32).T[lanes.gain : lanes.gain + 1]
    low = (hidden_state * scale * gain).astype(BF16)
    routed[...] = low
    logits = matmul(low, extra)
    lane = expert_lane(logits.shape, lanes)
    logits = jnp.where((lane >= 0) & (lane < experts), logits, MASKED)
    powers = jnp.exp(logits - jnp.max(logits, axis=1, keepdims=True))
    powers = powers / jnp.sum(powers, axis=1, keepdims=True)
    probabilities[...] = powers
    chosen = [
        jnp.sum(jnp.where(lane == routes[:, k : k + 1], powers, 0.0), axis=1, keepdims=True)
        for k in range(2)
    ]
    total = chosen[0] + chosen[1]
    gate_values = [chosen[k] / total for k in range(2)]
    pair = lax.broadcasted_iota(jnp.int32, (rows, 2), 1)
    gates[...] = jnp.where(pair == 0, gate_values[0], gate_values[1])
    members, _, gate_lanes = slot_gates.shape
    member_slots = experts // members * capacity
    slot_lanes = lax.broadcasted_iota(jnp.int32, (rows, gate_lanes), 1)
    inside = slot_lanes < member_slots
    places = routes * capacity + slots
    for member in range(members):
        by_slot = jnp.zeros((rows, gate_lanes), F32)
        for k in range(2):
            hit = (slot_lanes + member * member_slots == places[:, k : k + 1]) & inside
            by_slot = by_slot + jnp.where(hit, gate_values[k], 0.0)
        slot_gates[member] = jnp.broadcast_to(
            jnp.sum(by_slot, axis=0, keepdims=True), slot_gates.shape[1:]
        )
    select_rows([outgoing], position_rows[...], low)


def select_rows(outgoing, position_rows, values):
    rows = values.shape[0]
    sizes = [array.shape[1] for array in outgoing]
    for member in range(outgoing[0].shape[0]):
        slots = lax.broadcasted_iota(jnp.int32, (sum(sizes), rows), 0) + member * sum(sizes)
        slots = slots.astype(F32)
        picked = (slots == position_rows[0:1, :]) | (slots == position_rows[1:2, :])
        found = matmul(jnp.where(picked, 1.0, 0.0).astype(BF16), values).astype(BF16)
        first = 0
        for array, size in zip(outgoing, sizes):
            array[member] = found[first : first + size]
            first += size


def gelu_parts(value):
    magnitude = jnp.abs(value)
    power = jnp.exp2(value * value * -0.7213475204444817)
    base = 1.0 + (0.3275911 * 0.7071067811865476) * magnitude
    step = pl.reciprocal(base, approx=True)
    step = step * (2.0 - base * step)
    series = step * (
        0.127414796
        + step * (-0.142248368 + step * (0.7107068705 + step * (-0.7265760135 + step * 0.5307027145)))
    )
    tail = series * power
    normal = jnp.where(value < 0.0, tail, 1.0 - tail)
    return value * normal, normal + value * (power * 0.3989422804014327)


def flipped(place, other, size):
    result, bit = 0, 1
    while bit < size:
        result = result + bit * ((place // bit + other // bit) % 2)
        bit *= 2
    return result


def expert_kernel(*refs, layout, index, local, half, capacity, parts):
    shards = 2 * half
    refs = Bag(layout, refs)
    grid = Grid().here()
    z_size, y_size = grid.z_size, grid.y_size
    last = index == local - 1
    sibling = (grid.exp, grid.sibling(grid.fsdp))
    links = Links(refs.send[0], refs.receive[0])
    rows_all, cot, up_all, down_all = (
        refs.rows_all[0], refs.cot[0], refs.up_all[0], refs.down_all[0]
    )
    total = refs.total[0]
    if last:
        active, grad_hidden, unscaled = refs.active[0], refs.grad_hidden[0], refs.unscaled[0]
    else:
        grad_total = refs.grad_total[0]
    gates, gate_column = refs.gates[0], refs.gate_column[0]
    rows_t, slot_grad = refs.rows_t[0], refs.slot_grad[0]
    grad_up, grad_down = refs.grad_up[0], refs.grad_down[0]
    grad_rows, grad_gates = refs.grad_rows[0], refs.grad_gates[0]
    up_keep, up_taken, down_keep, down_taken = refs.own
    keep_up = [up_keep] + list(refs.far_keep_up)
    taken_up = [up_taken] + list(refs.far_taken_up)
    keep_down = [down_keep] + list(refs.far_keep_down)
    taken_down = [down_taken] + list(refs.far_taken_down)
    load_sem, fetch_sem, store_sem = refs.load_sem[0], refs.fetch_sem[0], refs.store_sem[0]
    store_there, stored_here = refs.store_there[0], refs.stored_here[0]
    pass_sem = refs.pass_sem[0]
    blocks, _, model_width = rows_all.shape
    part = up_all.shape[2]
    count = blocks * capacity
    depth = model_width // shards
    power = z_size & (z_size - 1) == 0
    together = 2 if power and z_size > 1 else 1
    group_rows = together * y_size * capacity

    def source_z(turn):
        return flipped(grid.z, turn, z_size) if power else (grid.z + turn) % z_size

    def target_z(turn):
        return flipped(grid.z, turn, z_size) if power else (grid.z + z_size - turn) % z_size

    def owner(place, core):
        return ((grid.x + place % half) % half) * 2 + (core + place // half) % 2

    def rows_of(place, core=None):
        core = grid.core if core is None else core
        return pl.ds(pl.multiple_of(owner(place, core) * depth, 16), depth)

    loads = [pltpu.make_async_copy(refs.rows_in[0], rows_all, load_sem.at[1])]
    late_count = 0
    if last and refs.cot_late:
        late_count = refs.cot_late[0].shape[1]
        loads.append(
            pltpu.make_async_copy(
                refs.cot_late[0], cot.at[:, pl.ds(capacity - late_count, late_count)], load_sem.at[4]
            )
        )
    loads.append(
        pltpu.make_async_copy(
            refs.cot_in[0].at[:, pl.ds(index * capacity, capacity - late_count)],
            cot.at[:, pl.ds(0, capacity - late_count)], load_sem.at[0],
        )
    )
    my_up, my_down = refs.my_up, refs.my_down
    swapped_up, swapped_down = refs.swapped_up, refs.swapped_down
    local_up = list(enumerate(my_up)) + [
        (half + number, array) for number, array in enumerate(swapped_up)
    ]
    local_down = list(enumerate(my_down)) + [
        (half + number, array) for number, array in enumerate(swapped_down)
    ]
    fetched_up = [
        pltpu.make_async_copy(
            array.at[rows_of(place), :], up_all.at[place, rows_of(shard), :],
            fetch_sem.at[place, number],
        )
        for number, (shard, array) in enumerate(local_up)
        for place in range(shards)
    ]
    fetched_down = {
        shard: pltpu.make_async_copy(
            array, down_all.at[shard], fetch_sem.at[shards + number, 0]
        )
        for number, (shard, array) in enumerate(local_down)
    }
    cross_down = {
        half + shard: links.copy(
            my_down[shard], down_all.at[half + shard], sibling, down_all.at[half + shard]
        )
        for shard in range(len(swapped_down), half)
    }
    cross_up = [
        links.copy(
            my_up[shard].at[rows_of(place, 1 - grid.core), :],
            up_all.at[place, rows_of(shard), :], sibling,
            up_all.at[place, rows_of(half + shard), :],
        )
        for shard in range(len(swapped_up), half)
        for place in range(shards)
    ]
    cross_next = [
        links.copy(source, target, sibling, target)
        for source, target in zip(refs.next_mine, refs.next_swapped)
    ]
    work = Exchange(
        grid, "exp", links, refs.own_sem[0],
        [
            (partial(plane_of, source, place), target)
            for source, place, target in zip(refs.moved_from, parts, refs.moved_to)
        ],
    )
    def member(z, y):
        return z * y_size + y

    def give_back(turn, hop):
        to = member(source_z(turn), (grid.y + hop) % y_size)
        origin = member(target_z(turn), (grid.y + y_size - hop) % y_size)
        pairs = []
        for number, (held, target) in enumerate(
            ((grad_rows, refs.back_rows[0]), (grad_gates, refs.back_gates[0]))
        ):
            sems = dict(
                send_sem=refs.back_send[0].at[number, turn, hop],
                recv_sem=refs.back_receive[0].at[number, turn, hop],
                device_id=(to, grid.fsdp), device_id_type=MESH,
            )
            pairs.append(
                (
                    pltpu.make_async_remote_copy(
                        src_ref=held.at[to], dst_ref=target.at[grid.exp], **sems
                    ),
                    pltpu.make_async_remote_copy(
                        src_ref=target.at[origin], dst_ref=target.at[origin], **sems
                    ),
                )
            )
        return pairs

    steps = [(turn, hop) for turn in range(z_size) for hop in range(y_size)]
    own_back = []
    if last:
        own_back = [
            pltpu.make_async_copy(held.at[grid.exp], target.at[grid.exp], load_sem.at[2 + number])
            for number, (held, target) in enumerate(
                ((grad_rows, refs.back_rows[0]), (grad_gates, refs.back_gates[0]))
            )
        ]

    for copy in loads:
        copy.start()
    for copy in list(fetched_down.values()) + fetched_up:
        copy.start()
    greet(
        [((grid.exp + hop) % grid.exp_size, grid.fsdp) for hop in range(1, grid.exp_size)]
        + chip_peers(grid)
    )
    for going, _ in list(cross_down.values()) + cross_up + cross_next:
        going.start()
    work.start()

    def place_at(position):
        hop = (position // 2 + 1) % half
        return hop + half * (1 - position % 2)

    def slot_rows():
        columns = gates[:, 0, :].T
        for block in range(blocks):
            piece = slice(block * capacity, (block + 1) * capacity)
            gate = columns[index * capacity : (index + 1) * capacity, block : block + 1]
            gate_column[piece, :] = gate
        slot_grad[...] = (
            gate_column[...] * cot[...].reshape(count, model_width).astype(F32)
        ).astype(BF16)

    def wait_down(place):
        if place in fetched_down:
            fetched_down[place].wait()
        else:
            cross_down[place][1].wait_recv()

    def wait_up():
        for copy in fetched_up:
            copy.wait()
        for _, coming in cross_up:
            coming.wait_recv()

    def folded(value):
        return sum(value[:, start : start + 128] for start in range(0, value.shape[1], 128))

    def gate_rows(found, block):
        ones = jnp.ones((8, 128), F32)
        grad_gates[block] = lax.dot_general(
            ones, found, (((1,), (1,)), ((), ())), precision=lax.Precision.HIGHEST,
            preferred_element_type=F32,
        )

    def up_target(targets, hop, place):
        if hop == 0:
            return targets[0].at[rows_of(place), :]
        return targets[1].at[hop - 1, rows_of(place), :]

    def keep_stores(place, slot):
        return [
            pltpu.make_async_copy(
                grad_up.at[slot, rows_of(hop), :], up_target(keep_up, hop, place),
                store_sem.at[slot, hop],
            )
            for hop in range(half)
        ]

    def give_stores(place, slot):
        return [
            pltpu.make_async_remote_copy(
                src_ref=grad_up.at[slot, rows_of(half + hop), :],
                dst_ref=up_target(taken_up, hop, place),
                send_sem=store_there.at[slot, hop], recv_sem=stored_here.at[place, hop],
                device_id=sibling, device_id_type=MESH,
            )
            for hop in range(half)
        ]

    def down_store(slot):
        return pltpu.make_async_copy(grad_down.at[slot], keep_down[0], store_sem.at[slot, half])

    def down_give(hop, slot):
        target = taken_down[0] if hop == 0 else taken_down[1].at[hop - 1]
        return pltpu.make_async_remote_copy(
            src_ref=grad_down.at[slot], dst_ref=target,
            send_sem=store_there.at[slot, half], recv_sem=stored_here.at[hop, half],
            device_id=sibling, device_id_type=MESH,
        )

    def start_store(place, slot):
        for copy in keep_stores(place, slot) + give_stores(place, slot):
            copy.start()

        @pl.when(place == 0)
        def _():
            down_store(slot).start()

        for hop in range(half):

            @pl.when(place == half + hop)
            def _(hop=hop):
                down_give(hop, slot).start()

            if hop > 0:

                @pl.when(place == hop)
                def _(hop=hop):
                    keep_down[1][hop - 1] = grad_down[slot]

    def wait_store(place, slot):
        for copy in keep_stores(place, slot):
            copy.wait()
        for copy in give_stores(place, slot):
            copy.wait_send()

        @pl.when(place == 0)
        def _():
            down_store(slot).wait()

        for hop in range(half):

            @pl.when(place == half + hop)
            def _(hop=hop):
                down_give(hop, slot).wait_send()

    early_rows = part // 2
    early = [
        links.copy(
            keep_down[1].at[hop - 1, pl.ds(0, early_rows), :], refs.early_down[0].at[hop - 1],
            (grid.exp, grid.x_from(hop)), refs.early_down[0].at[hop - 1],
        )
        for hop in range(1, half)
    ]

    def pass_early():
        for hop in range(1, half):
            down_give(hop, 0).wait_recv()
            keep_down[1][hop - 1] = (
                keep_down[1][hop - 1].astype(F32) + taken_down[1][hop - 1].astype(F32)
            ).astype(BF16)
            early[hop - 1][0].start()

    def fused(position, carry):
        place, slot = place_at(position), position % 2
        if half > 1:

            @pl.when(position == shards - 2)
            def _():
                pass_early()

        up, down = up_all[place], down_all[place]
        rows = rows_all[...].reshape(count, model_width)
        pieces = [slice(start, start + 256) for start in range(0, count, 256)]

        def products_of(piece):
            return matmul(rows[piece], up), contract_last(slot_grad[piece, :], down)

        raw = products_of(pieces[0])
        active_low, grad_low = [], []
        for number, piece in enumerate(pieces):
            hidden, grad_active = raw
            if number + 1 < len(pieces):
                raw = products_of(pieces[number + 1])
            activated, slope = gelu_parts(hidden)
            active_low.append(activated.astype(BF16))
            grad_low.append((grad_active * slope).astype(BF16))
            total[piece, :] += matmul(active_low[number], down)
            grad_total[piece, :] += contract_last(grad_low[number], up)
        active_low = jnp.concatenate(active_low, axis=0)
        grad_low = jnp.concatenate(grad_low, axis=0)

        @pl.when(position >= 2)
        def _():
            wait_store(place_at(position - 2), slot)

        grad_up[slot] = matmul(rows_t[...], grad_low).astype(BF16)
        grad_down[slot] = contract_first(active_low, slot_grad[...]).astype(BF16)
        start_store(place, slot)
        return carry

    def group(number, carry):
        turns = [number * together + more for more in range(together)]
        if together == 2:
            place_of_group = flipped(grid.z // 2, number, z_size // 2)
        else:
            place_of_group = source_z(number)
        members = pl.ds(place_of_group * together * y_size, together * y_size)
        span = pl.ds(pl.multiple_of(place_of_group * group_rows, 16), group_rows)
        rows = rows_all[members].reshape(group_rows, model_width)
        gate = gate_column[span, :]
        grad = jnp.zeros((group_rows, model_width), F32)
        products = jnp.zeros((group_rows, 128), F32)
        ahead = matmul(rows, up_all[0])
        for place in range(shards):
            hidden = ahead
            if place + 1 < shards:
                ahead = matmul(rows, up_all[place + 1])
            base = unscaled[place, span, :].astype(F32)
            activated, slope = gelu_parts(hidden)
            products = products + folded(activated * base)
            active_low = activated.astype(BF16)
            active[place, span, :] = active_low
            low = (gate * base * slope).astype(BF16)
            grad_hidden[place, span, :] = low
            grad = grad + contract_last(low, up_all[place])
            total[span, :] += matmul(active_low, down_all[place])
        grad_rows[members] = grad.astype(BF16).reshape(together * y_size, capacity, model_width)
        for hop in range(together * y_size):
            gate_rows(
                products[hop * capacity : (hop + 1) * capacity],
                place_of_group * together * y_size + hop,
            )
        for turn in turns:
            for hop in range(y_size):

                @pl.when(turn + hop > 0)
                def _(turn=turn, hop=hop):
                    for going, _ in give_back(turn, hop):
                        going.start()

        return carry

    def column(position, carry):
        place, slot = place_at(position), position % 2
        if half > 1:

            @pl.when(position == shards - 1)
            def _():
                pass_early()

        @pl.when(position >= 2)
        def _():
            wait_store(place_at(position - 2), slot)

        grad_up[slot] = matmul(rows_t[...], grad_hidden[place]).astype(BF16)
        grad_down[slot] = contract_first(active[place], slot_grad[...]).astype(BF16)
        start_store(place, slot)
        return carry

    for copy in loads[1:]:
        copy.wait()
    total[...] = jnp.zeros_like(total)
    slot_rows()
    if last:
        for place in range(shards):
            wait_down(place)
            unscaled[place] = contract_last(
                cot[...].reshape(count, model_width), down_all[place]
            ).astype(BF16)
        loads[0].wait()
        wait_up()
        lax.fori_loop(0, z_size // together, group, 0)
        for copy in own_back:
            copy.start()
        rows_t[...] = turned(rows_all[...].reshape(count, model_width)).astype(BF16)
        lax.fori_loop(0, shards, column, 0)
    else:
        loads[0].wait()
        rows_t[...] = turned(rows_all[...].reshape(count, model_width)).astype(BF16)
        grad_total[...] = jnp.zeros_like(grad_total)
        wait_up()
        for place in range(shards):
            wait_down(place)
        lax.fori_loop(0, shards, fused, 0)
        grad_rows[...] = grad_total[...].astype(BF16).reshape(grad_rows.shape)
        for block in range(blocks):
            rows = total[block * capacity : (block + 1) * capacity, :].astype(BF16).astype(F32)
            gate_rows(folded(rows * cot[block].astype(F32)), block)

    rows_out = refs.rows_out[0]
    cot[...] = total[...].astype(BF16).reshape(blocks, capacity, model_width)
    out_copies = [pltpu.make_async_copy(cot, rows_out.at[:, index], load_sem.at[0])]
    for before in refs.outs_before:
        out_copies.append(
            pltpu.make_async_copy(before, rows_out.at[:, pl.ds(0, index)], load_sem.at[1])
        )
    for copy in out_copies:
        copy.start()
    for position in range(max(shards - 2, 0), shards):
        wait_store(place_at(position), position % 2)
    for place in range(shards):
        for copy in give_stores(place, 0):
            copy.wait_recv()
    down_give(0, 0).wait_recv()
    if half > 1:
        keep_up[1][...] = (keep_up[1][...].astype(F32) + taken_up[1][...].astype(F32)).astype(BF16)
        for source, target, number in (
            (keep_up[1], refs.pass_up[0], 0),
            (keep_down[1].at[:, pl.ds(early_rows, part - early_rows), :], refs.pass_down[0], 1),
        ):
            out_copies.append(pltpu.make_async_copy(source, target, pass_sem.at[number]))
            out_copies[-1].start()
    for copy in out_copies:
        copy.wait()
    for going, coming in early:
        coming.wait_recv()
        going.wait_send()
    for going, coming in cross_next:
        coming.wait_recv()
        going.wait_send()
    for going, _ in list(cross_down.values()) + cross_up:
        going.wait_send()
    work.finish()
    if last:
        for turn, hop in steps[1:]:
            for going, coming in give_back(turn, hop):
                coming.wait_recv()
                going.wait_send()
        for copy in own_back:
            copy.wait()


class Bag:
    def __init__(self, layout, refs):
        start = 0
        for name, size in layout.items():
            setattr(self, name, refs[start : start + size])
            start += size


class Wanted:
    def groups(self):
        return list(self.__dict__.values())

    def layout(self):
        return {name: len(group) for name, group in self.__dict__.items()}


def run_expert(index, local, rows_in, gates, cotangent, cotangent_late, ups, downs, swapped, next_mine,
               moved, outs_before, collective_id):
    grid = Grid()
    half = len(ups)
    shards = 2 * half
    last = index == local - 1
    blocks, capacity, model_width = rows_in.shape
    part = downs[0].shape[0]
    count = blocks * capacity
    inputs, outputs, scratch = Wanted(), Wanted(), Wanted()
    inputs.cot_in = [(cotangent, ANYWHERE)]
    inputs.cot_late = [(array, ANYWHERE) for array in cotangent_late]
    inputs.rows_in = [(rows_in, ANYWHERE)]
    inputs.gates = [(gates, IN_VMEM)]
    inputs.my_up = [(array, ANYWHERE) for array in ups]
    inputs.my_down = [(array, ANYWHERE) for array in downs]
    inputs.swapped_up = [(array, ANYWHERE) for array in swapped[0]]
    inputs.swapped_down = [(array, ANYWHERE) for array in swapped[1]]
    inputs.next_mine = [(array, ANYWHERE) for array in next_mine]
    inputs.moved_from = [(array, ANYWHERE) for array, _ in moved]
    inputs.outs_before = [] if outs_before is None else [(outs_before, IN_VMEM)]

    up_shape, down_shape = (model_width, part), (part, model_width)
    outputs.rows_out = [(shape_of((blocks, index + 1, capacity, model_width), BF16), ANYWHERE)]
    own_up, own_down = shape_of(up_shape, BF16), shape_of(down_shape, BF16)
    outputs.own = [(own_up, ANYWHERE), (own_up, ANYWHERE), (own_down, ANYWHERE), (own_down, ANYWHERE)]
    outputs.pass_up = [(shape_of((half - 1,) + up_shape, BF16), ANYWHERE)] if half > 1 else []
    late_down = (half - 1, part - part // 2, model_width)
    early_down = (half - 1, part // 2, model_width)
    outputs.pass_down = [(shape_of(late_down, BF16), ANYWHERE)] if half > 1 else []
    outputs.early_down = [(shape_of(early_down, BF16), ANYWHERE)] if half > 1 else []
    outputs.next_swapped = [(shape_of(array.shape, BF16), ANYWHERE) for array in next_mine]
    outputs.moved_to = [
        (
            shape_of((grid.exp_size,) + array.shape[(1 if place is None else 2) :], array.dtype),
            ANYWHERE,
        )
        for array, place in moved
    ]
    rows_shape, gate_shape = (blocks, capacity, model_width), (blocks, 8, capacity)
    if last:
        outputs.back_rows = [(shape_of(rows_shape, BF16), ANYWHERE)]
        outputs.back_gates = [(shape_of(gate_shape, F32), ANYWHERE)]
    else:
        outputs.grad_rows = [(shape_of(rows_shape, BF16), IN_VMEM)]
        outputs.grad_gates = [(shape_of(gate_shape, F32), IN_VMEM)]

    sems = lambda *shape: pltpu.SemaphoreType.DMA(shape)
    scratch.rows_all = [pltpu.VMEM(rows_shape, BF16)]
    scratch.cot = [pltpu.VMEM(rows_shape, BF16)]
    scratch.up_all = [pltpu.VMEM((shards,) + up_shape, BF16)]
    scratch.down_all = [pltpu.VMEM((shards,) + down_shape, BF16)]
    scratch.total = [pltpu.VMEM((count, model_width), F32)]
    if last:
        scratch.active = [pltpu.VMEM((shards, count, part), BF16)]
        scratch.grad_hidden = [pltpu.VMEM((shards, count, part), BF16)]
        scratch.unscaled = [pltpu.VMEM((shards, count, part), BF16)]
    else:
        scratch.grad_total = [pltpu.VMEM((count, model_width), F32)]
    if last:
        scratch.grad_rows = [pltpu.VMEM(rows_shape, BF16)]
        scratch.grad_gates = [pltpu.VMEM(gate_shape, F32)]
        scratch.back_send = [sems(2, grid.z_size, grid.y_size)]
        scratch.back_receive = [sems(2, grid.z_size, grid.y_size)]
    scratch.gate_column = [pltpu.VMEM((count, 1), F32)]
    scratch.rows_t = [pltpu.VMEM((model_width, count), BF16)]
    scratch.slot_grad = [pltpu.VMEM((count, model_width), BF16)]
    scratch.grad_up = [pltpu.VMEM((2,) + up_shape, BF16)]
    scratch.grad_down = [pltpu.VMEM((2,) + down_shape, BF16)]
    far_up = [pltpu.VMEM((half - 1,) + up_shape, BF16)] * (1 if half > 1 else 0)
    far_down = [pltpu.VMEM((half - 1,) + down_shape, BF16)] * (1 if half > 1 else 0)
    scratch.far_keep_up, scratch.far_taken_up = far_up, far_up
    scratch.far_keep_down, scratch.far_taken_down = far_down, far_down
    scratch.load_sem = [sems(5)]
    scratch.pass_sem = [sems(2)]
    scratch.fetch_sem = [sems(2 * shards, shards)]
    scratch.store_sem = [sems(2, half + 1)]
    scratch.store_there = [sems(2, half + 1)]
    scratch.stored_here = [sems(shards, half + 1)]
    copies = len(moved) * grid.exp_size + half * (shards + 2) + len(next_mine)
    scratch.send = [sems(copies)]
    scratch.receive = [sems(copies)]
    scratch.own_sem = [sems(max(len(moved), 1))]

    layout = {**inputs.layout(), **outputs.layout(), **scratch.layout()}

    def body(*refs):
        expert_kernel(
            *refs, layout=layout, index=index, local=local, half=half, capacity=capacity,
            parts=[place for _, place in moved],
        )

    results = pl.pallas_call(
        body,
        in_specs=[spec for group in inputs.groups() for _, spec in group],
        out_specs=tuple(spec for group in outputs.groups() for _, spec in group),
        out_shape=tuple(shape for group in outputs.groups() for shape, _ in group),
        scratch_shapes=[item for group in scratch.groups() for item in group],
        compiler_params=params(collective_id=collective_id, has_side_effects=True),
        cost_estimate=hint(45),
        name=f"expert_{index}",
    )(*[array for group in inputs.groups() for array, _ in group])
    return Bag(outputs.layout(), results)


def local_picks(routes, slots, capacity, local, index, slot_count):
    member, which = lax.div(routes, local), lax.rem(routes, local)
    places = jnp.where(which == index, member * capacity + slots, -1)
    lane = lax.broadcasted_iota(jnp.int32, (routes.shape[0], slot_count), 1)
    return [lane == places[:, k : k + 1] for k in range(2)]


def unroute_kernel(
    hidden, cotangent, routed, probabilities, gates, plane, columns, counts, *refs,
    experts, local, token_total, lanes,
):
    grads, gate_grads = refs[:local], refs[local : 2 * local]
    grad_hidden, grad_branch, small = refs[2 * local :]
    rows = hidden.shape[0]
    members, capacity, model_width = grads[0].shape
    grad_output = cotangent[...].astype(F32)
    grad_routed = jnp.zeros(hidden.shape, F32)
    found = [jnp.zeros((rows, capacity), F32), jnp.zeros((rows, capacity), F32)]
    routes, slots = int_columns(columns)
    member, which = lax.div(routes, local), lax.rem(routes, local)
    lane = lax.broadcasted_iota(jnp.int32, (rows, capacity), 1)
    for index in range(local):
        picks = local_picks(routes, slots, capacity, local, index, members * capacity)
        grad_routed = grad_routed + matmul(
            jnp.where(picks[0] | picks[1], 1.0, 0.0).astype(BF16),
            grads[index][...].reshape(members * capacity, model_width),
        )
        for place in range(members):
            spots = jnp.where((which == index) & (member == place), slots, -1)
            for k in range(2):
                found[k] = found[k] + jnp.where(
                    lane == spots[:, k : k + 1], gate_grads[index][place, 0:1, :], 0.0
                )
    grad_gates = [jnp.sum(found[k], axis=1, keepdims=True) for k in range(2)]
    powers = probabilities[...]
    lane = expert_lane(powers.shape, lanes)
    inside = (lane >= 0) & (lane < experts)
    picked = [lane == routes[:, k : k + 1] for k in range(2)]
    chosen_total = sum(
        jnp.sum(jnp.where(picked[k], powers, 0.0), axis=1, keepdims=True) for k in range(2)
    )
    weighted = grad_gates[0] * gates[:, 0:1] + grad_gates[1] * gates[:, 1:2]
    grad_mass = (AUX_WEIGHT * experts / (2.0 * token_total * token_total)) * counts[0:1, :]
    grad_mass = jnp.where(inside, grad_mass, 0.0)
    for k in range(2):
        grad_mass = grad_mass + jnp.where(picked[k], (grad_gates[k] - weighted) / chosen_total, 0.0)
    grad_logits = powers * (grad_mass - jnp.sum(powers * grad_mass, axis=1, keepdims=True))
    extra = plane[:, lanes.base :]
    grad_routed = grad_routed + contract_last(grad_logits.astype(BF16), extra)
    hidden_state = hidden[...]
    scale = lax.rsqrt(jnp.mean(hidden_state * hidden_state, axis=1, keepdims=True) + EPSILON)
    normed = hidden_state * scale
    product = grad_routed * normed
    gain_grad = jnp.sum(product, axis=0, keepdims=True)
    small_t = matmul(grad_logits.T.astype(BF16), routed[...])
    row = lax.broadcasted_iota(jnp.int32, small_t.shape, 0)
    small_t = jnp.where(row == lanes.gain, gain_grad, small_t)
    small[...] = small_t.T
    gains = extra.astype(F32).T[lanes.gain : lanes.gain + 1]
    grad = scale * (
        grad_routed * gains - normed * jnp.mean(product * gains, axis=1, keepdims=True)
    ) + grad_output
    grad_hidden[...] = grad
    grad_branch[...] = grad.astype(BF16)


def context_grad_kernel(
    fsdp_index, grad_branch, attention_out, context, grad_t, grad_n, grad_out, total, *, heads, width
):
    @pl.when(pl.program_id(0) == 0)
    def _():
        total[...] = jnp.zeros_like(total)

    branch = grad_branch[0]
    grad = contract_last(attention_out[...], branch).astype(BF16)
    for head in range(heads):
        part = grad[head * width : (head + 1) * width]
        grad_t[head] = part
        grad_n[head] = turned(part).astype(BF16)
    total[...] += matmul(context[0], branch)

    @pl.when(pl.program_id(0) == pl.num_programs(0) - 1)
    def _():
        grad_out[...] = total[...].astype(BF16)


def project_back_kernel(
    grad_projected, normed, plane, small, probabilities, grad_bias, grad_first, grad_plane, total,
    bias_t, *, lanes, heads, feature_rows, bucket_rows,
):
    step = pl.program_id(0)

    @pl.when(step == 0)
    def _():
        total[...] = jnp.zeros_like(total)

    grad = grad_projected[...]
    grad_first[0] = matmul(plane[:, : lanes.weights], grad).astype(BF16)
    total[: lanes.weights, :] += matmul(grad, normed[...])

    @pl.when(step == pl.num_programs(0) - 1)
    def _():
        grad_plane[...] = total[...].T.astype(BF16)
        span = grad_bias.shape[2]
        select, _ = bucket_rows_select(plane.shape[0], feature_rows, bucket_rows, span)
        bias_t[...] = jnp.zeros_like(bias_t)
        first = lanes.table + lax.axis_index("fsdp") * heads
        for head in range(heads):
            bias_t[pl.ds(first + head, 1), :] = grad_bias[head]
        high = bias_t[...].astype(BF16)
        rest = (bias_t[...] - high.astype(F32)).astype(BF16)
        table = contract_last(select, high) + contract_last(select, rest)
        mass = jnp.sum(probabilities[...], axis=0, keepdims=True)
        mass = pltpu.roll(jnp.broadcast_to(mass, (8, lanes.extra)), lanes.shift, 1)[0:1]
        lane = lax.broadcasted_iota(jnp.int32, table.shape, 1)
        row = lax.broadcasted_iota(jnp.int32, table.shape, 0)
        is_small = (lane >= lanes.router) & (lane < lanes.table)
        is_mass = (lane >= lanes.count) & (lax.rem(row, feature_rows) == 0)
        extra = table + jnp.where(is_small, small[...], 0.0) + jnp.where(is_mass, mass, 0.0)
        grad_plane[:, lanes.base :] = (total[lanes.base :, :].T + extra).astype(BF16)


def last_kernel(
    first, planes, out_grad, first_parts, plane_parts, out_parts,
    first_in, first_sum, planes_in, plane_sum, along_in, reduced, send, receive, own, *, spread_out,
):
    grid = Grid().here()
    links = Links(send, receive)
    z_size, y_size, x_size, fsdp_size = grid.z_size, grid.y_size, grid.x_size, grid.fsdp_size
    exp_size = grid.exp_size
    sibling = grid.sibling(grid.fsdp)
    near = [
        (grid.exp, (grid.fsdp + turn) % fsdp_size) for turn in range(1, fsdp_size)
    ] + [grid.at(z=(grid.z + hop) % z_size) for hop in range(1, z_size)]
    beside = [grid.at(y=(grid.y + hop) % y_size) for hop in range(1, y_size)]

    per_sender = grid.device_count if spread_out else exp_size
    base = 0 if spread_out else grid.fsdp * exp_size
    out_sends = []
    for number in range(per_sender):
        to = base + number
        out_sends.append((to, number))
    if spread_out:
        out_origins = [(origin, origin) for origin in range(grid.device_count)]
    else:
        out_origins = [
            (member * fsdp_size + grid.linear // exp_size, member) for member in range(exp_size)
        ]
    own_slot = grid.linear if spread_out else grid.exp
    out_base = links.used
    links.used += per_sender

    def place_of(linear):
        return (linear // fsdp_size, linear % fsdp_size)

    def out_copy(to, number, slot):
        return pltpu.make_async_remote_copy(
            src_ref=out_grad.at[number], dst_ref=out_parts.at[slot],
            send_sem=send.at[out_base + number], recv_sem=receive.at[out_base + slot],
            device_id=place_of(to), device_id_type=MESH,
        )

    barrier = pltpu.get_barrier_semaphore()
    for device in near + beside:
        pl.semaphore_signal(barrier, inc=1, device_id=device, device_id_type=MESH)
    for origin, _ in out_origins:

        @pl.when(origin != grid.linear)
        def _(origin=origin):
            pl.semaphore_signal(
                barrier, inc=1, device_id=place_of(origin), device_id_type=MESH
            )

    to_self = (
        1 if spread_out else jnp.where(grid.linear // exp_size == grid.fsdp, 1, 0)
    )
    pl.semaphore_wait(barrier, len(near) + len(beside) + per_sender - to_self)

    first_copies = []
    for hop in range(x_size):
        mine = grid.x_from(hop)
        first_copies.append(
            links.copy(
                first.at[grid.sibling(mine)], first_in.at[hop], (grid.exp, sibling), first_in.at[hop]
            )
        )
        first_copies[-1][0].start()
    z_hops = list(range(1, z_size)) + [0]
    beside_copies = []
    for z_hop in z_hops:
        beside_copies.append([])
        for hop in range(1, y_size):
            to = (grid.y + hop) % y_size
            landing = planes_in.at[hop - 1, z_hop]
            beside_copies[-1].append(
                links.copy(
                    planes.at[(grid.z + z_hop) % z_size, to], landing, grid.at(y=to), landing
                )
            )
            beside_copies[-1][-1][0].start()
    for to, number in out_sends:

        @pl.when(to != grid.linear)
        def _(to=to, number=number):
            out_copy(to, number, own_slot).start()

        @pl.when(to == grid.linear)
        def _(number=number):
            pltpu.make_async_copy(out_grad.at[number], out_parts.at[own_slot], own.at[0]).start()

    along_x = []
    for hop in range(x_size):
        first_copies[hop][1].wait_recv()
        summed = first[grid.x_from(hop)].astype(F32) + first_in[hop].astype(F32)
        if hop == 0:
            first_parts[0] = summed.astype(BF16)
        else:
            first_sum[hop - 1] = summed.astype(BF16)
            along_x.append(
                links.copy(
                    first_sum.at[hop - 1], first_parts.at[hop], (grid.exp, grid.x_from(hop)),
                    first_parts.at[hop],
                )
            )
            along_x[-1][0].start()
    along_z = []
    for z_hop, copies in zip(z_hops, beside_copies):
        to_z = (grid.z + z_hop) % z_size
        summed = planes[to_z, grid.y].astype(F32)
        for number, (_, coming) in enumerate(copies):
            coming.wait_recv()
            summed = summed + planes_in[number, z_hop].astype(F32)
        plane_sum[z_hop] = summed.astype(BF16)
        if z_hop > 0:
            along_z.append(
                links.copy(
                    plane_sum.at[z_hop], along_in.at[z_hop - 1], grid.at(z=to_z),
                    along_in.at[z_hop - 1],
                )
            )
            along_z[-1][0].start()
    summed = plane_sum[0].astype(F32)
    for number, (_, coming) in enumerate(along_z):
        coming.wait_recv()
        summed = summed + along_in[number].astype(F32)
    reduced[...] = summed.astype(BF16)
    placed = []
    for turn in range(1, fsdp_size):
        to = (grid.fsdp + turn) % fsdp_size
        origin = (grid.fsdp + fsdp_size - turn) % fsdp_size
        placed.append(
            links.copy(
                reduced.at[to], plane_parts.at[grid.fsdp], (grid.exp, to), plane_parts.at[origin]
            )
        )
        placed[-1][0].start()
    kept = pltpu.make_async_copy(reduced.at[grid.fsdp], plane_parts.at[grid.fsdp], own.at[1])
    kept.start()
    for going, coming in along_x + placed:
        coming.wait_recv()
    for going, _ in first_copies + along_x + along_z + placed:
        going.wait_send()
    for copies in beside_copies:
        for going, _ in copies:
            going.wait_send()
    kept.wait()
    for origin, slot in out_origins:

        @pl.when(origin != grid.linear)
        def _(origin=origin, slot=slot):
            out_copy(origin, 0, slot).wait_recv()

    for to, number in out_sends:

        @pl.when(to != grid.linear)
        def _(to=to, number=number):
            out_copy(to, number, own_slot).wait_send()

        @pl.when(to == grid.linear)
        def _(number=number):
            pltpu.make_async_copy(out_grad.at[number], out_parts.at[own_slot], own.at[0]).wait()


def mixture_kernel(hidden, gates, columns, rows_in, output, *, local):
    members, _, capacity, model_width = rows_in.shape
    routes, slots = int_columns(columns)
    total = hidden[...]
    picked = [jnp.zeros(hidden.shape, F32), jnp.zeros(hidden.shape, F32)]
    for index in range(local):
        picks = local_picks(routes, slots, capacity, local, index, members * capacity)
        values = rows_in[:, index].reshape(members * capacity, model_width)
        for k in range(2):
            picked[k] = picked[k] + matmul(jnp.where(picks[k], 1.0, 0.0).astype(BF16), values)
    for k in range(2):
        total = total + gates[:, k : k + 1] * picked[k]
    output[...] = total.astype(BF16)


def finish_kernel(
    first_parts, plane_parts, out_parts, tokens, grad_hidden, attention_in, attention_gain, counts,
    grad_tokens, grad_gain, grad_in, grad_out, grad_mixture, grad_router, grad_table, balance,
    *, lanes, heads, width, head_count, experts, token_total,
):
    total = jnp.sum(first_parts[...].astype(F32), axis=0).T
    inputs = tokens[...].astype(F32)
    scale = lax.rsqrt(jnp.mean(inputs * inputs, axis=1, keepdims=True) + EPSILON)
    normed = inputs * scale
    grad_tokens[...] = grad_hidden[...] + scale * (
        total - normed * jnp.mean(total * normed, axis=1, keepdims=True)
    )
    fsdp_size = plane_parts.shape[0]
    model_width = head_count * width
    sums = [plane_parts[place].astype(F32) for place in range(fsdp_size)]
    columns = []
    for kind in range(3):
        pieces = [
            sums[place][:, kind * heads * width : (kind + 1) * heads * width]
            for place in range(fsdp_size)
        ]
        columns.append(jnp.concatenate(pieces, axis=1)[:, :model_width])
    gathered = jnp.concatenate(columns, axis=1)
    feature_rows = gathered.shape[0]
    gain = jnp.sum(gathered * attention_in[...].astype(F32), axis=1, keepdims=True)
    gain = padded_rows(jnp.broadcast_to(gain, (feature_rows, 128)), 128).T
    grad_gain[...] = gain[0:1, :feature_rows]
    grad_in[...] = gathered * as_column(attention_gain[...], feature_rows)
    grad_out[...] = jnp.sum(out_parts[...].astype(F32), axis=0)
    extra = sum(part[:, lanes.base :] for part in sums)
    extra_t = padded_rows(extra, 128).T
    grad_mixture[...] = extra_t[lanes.gain : lanes.gain + 1, :feature_rows]
    grad_router[...] = extra_t[lanes.router : lanes.router + experts, :feature_rows]
    grad_table[...] = extra[: grad_table.shape[0], lanes.table : lanes.table + head_count]
    mass = jnp.broadcast_to(extra[0:1], (8, lanes.extra))
    mass = pltpu.roll(mass, lanes.extra - lanes.shift, 1)
    lane = expert_lane(mass.shape, lanes)
    terms = jnp.where((lane >= 0) & (lane < experts), mass * counts[...], 0.0)[0:1]
    balance[...] = jnp.sum(terms, axis=1, keepdims=True) * (
        experts / (2.0 * token_total * token_total)
    )


def sum_kernel(*refs, layout, local):
    outputs = refs[len(layout) :]
    early_blocks = pl.num_programs(0) // 2
    totals = {}
    number = 0
    while number < len(layout):
        index, which, halves = layout[number]
        shape = outputs[which].shape[1:]
        value = refs[number][...].reshape(shape).astype(F32)
        if halves:
            rest = refs[number + 1][...].reshape(shape).astype(F32)
            value = jnp.where(pl.program_id(0) < early_blocks, value, rest)
            number += 1
        totals[index, which] = totals[index, which] + value if (index, which) in totals else value
        number += 1
    for (index, which), total in totals.items():
        outputs[which][index] = total


def sum_grads(groups, up_shape, down_shape, blocks):
    local = len(groups)
    depth, part = up_shape[1], down_shape[1]
    sizes = ((depth, part), (part // blocks, down_shape[2]))
    arrays, specs, layout = [], [], []
    early = blocks // 2
    for index, group in enumerate(groups):
        for which, (size, (keep, taken, passed)) in enumerate(zip(sizes, group)):
            for array in (keep, taken, *passed):
                if isinstance(array, tuple):
                    arrays.extend(array)
                    specs.append(pl.BlockSpec(size, lambda c: (jnp.minimum(c, early - 1), 0)))
                    specs.append(pl.BlockSpec(size, lambda c: (jnp.maximum(c - early, 0), 0)))
                    layout.extend([(index, which, True)] * 2)
                else:
                    arrays.append(array)
                    specs.append(pl.BlockSpec(size, lambda c: (c, 0)))
                    layout.append((index, which, False))
    return pl.pallas_call(
        partial(sum_kernel, layout=layout, local=local),
        grid=(blocks,),
        in_specs=specs,
        out_specs=[
            pl.BlockSpec((local, depth, part), lambda c: (0, 0, c)),
            pl.BlockSpec((local, part // blocks, down_shape[2]), lambda c: (0, c, 0)),
        ],
        out_shape=(shape_of(up_shape, F32), shape_of(down_shape, F32)),
        compiler_params=params(),
        cost_estimate=hint(8),
        name="sum_grads",
    )(*arrays)


def over_x(array, hop):
    fsdp_size = lax.axis_size("fsdp")
    return lax.ppermute(array, "fsdp", [(i, (i + 2 * hop) % fsdp_size) for i in range(fsdp_size)])


def over_core(array):
    return lax.ppermute(array, "fsdp", [(i, i ^ 1) for i in range(lax.axis_size("fsdp"))])


def on_device(
    tokens,
    cotangent,
    segments,
    routes,
    slots,
    attention_gain,
    mixture_gain,
    attention_in,
    attention_out,
    router_weight,
    position_table,
    expert_up,
    expert_down,
):
    grid = Grid()
    exp_size, fsdp_size, chips = grid.exp_size, grid.fsdp_size, grid.x_size
    device_count = grid.device_count
    fsdp_index = lax.axis_index("fsdp")
    rows, model_width = tokens.shape
    length = rows * fsdp_size
    head_count = position_table.shape[1]
    width = model_width // head_count
    heads = -(-head_count // fsdp_size)
    padded_heads = heads * fsdp_size
    feature_rows, bucket_rows = attention_in.shape[0], position_table.shape[0]
    experts = router_weight.shape[1]
    local = expert_up.shape[0]
    capacity = 4 * rows // experts
    token_total = rows * device_count
    span = WINDOW + 2 * SKEW + QUERY_BLOCK
    lanes = Lanes(heads, width, padded_heads, experts)
    part = expert_down.shape[1]
    gain_row = attention_gain.reshape(1, feature_rows)
    late_rows = capacity // 2 // 16 * 16 if local > 1 else 0
    late = 1 if late_rows else 0

    shard_shapes = [shape_of((model_width, part), BF16), shape_of((part, model_width), BF16)]
    copies = (
        4 * fsdp_size + grid.z_size + grid.z_size * grid.y_size
        + grid.z_size + grid.y_size + grid.x_size + 1
    )
    started = pl.pallas_call(
        partial(
            start_kernel, lanes=lanes, heads=heads, width=width, head_count=head_count,
            experts=experts, capacity=capacity, local=local, late=late,
        ),
        out_shape=tuple(
            [
                shape_of((fsdp_size, rows, model_width), BF16),
                shape_of((grid.z_size, grid.y_size, fsdp_size, feature_rows, lanes.width), BF16),
                shape_of((exp_size, local * capacity - late_rows, model_width), BF16),
                shape_of((8, rows), F32),
                shape_of((rows, 128), F32),
                shape_of((grid.z_size, grid.y_size, chips, 2, feature_rows, model_width), BF16),
            ]
            + [shape_of((exp_size, late_rows, model_width), BF16)] * late
            + shard_shapes * local
        ),
        in_specs=[IN_VMEM] * 10 + [ANYWHERE] * 2,
        out_specs=tuple(
            [ANYWHERE, ANYWHERE, IN_VMEM, IN_VMEM, IN_VMEM, ANYWHERE]
            + [IN_VMEM] * late
            + [ANYWHERE] * (2 * local)
        ),
        scratch_shapes=[
            pltpu.VMEM((fsdp_size, feature_rows, lanes.width), BF16),
            pltpu.VMEM(expert_up.shape, BF16),
            pltpu.VMEM(expert_down.shape, BF16),
            dma_sems(copies),
            dma_sems(copies),
            dma_sems(3),
            dma_sems(2 * local),
            dma_sems(local * (fsdp_size + 1)),
        ],
        compiler_params=params(collective_id=0, has_side_effects=True),
        cost_estimate=hint(20),
        name="start",
    )(
        tokens, cotangent, routes.T, slots.T, gain_row, mixture_gain.reshape(1, feature_rows),
        attention_in, router_weight.T, position_table, attention_out, expert_up, expert_down,
    )
    all_tokens, all_planes, cotangent_early, position_rows, columns, full_out = started[:6]
    cotangent_late, started = started[6 : 6 + late], started[6 + late :]
    own_shards = [started[2 * index : 2 * index + 2] for index in range(local)]
    plane = all_planes.reshape(model_width, lanes.width)
    full_out = full_out.reshape(model_width, model_width)

    def along_x(array):
        return [over_x(array, -hop) for hop in range(1, chips)]

    near_up, near_down = [None] * local, [None] * local
    near_up[0] = along_x(own_shards[0][0])
    cotangent_in = lax.all_to_all(
        cotangent_early, "exp", split_axis=0, concat_axis=0, tiled=True
    )

    head_t = lambda size: pl.BlockSpec((heads, size, rows), lambda s, *_: (0, 0, s))
    head_n = lambda size: pl.BlockSpec((heads, rows, size), lambda s, *_: (0, s, 0))
    normed, query_t, key_n, query_n, value_n, key_t, value_t, bias, counts = pl.pallas_call(
        partial(
            project_kernel, heads=heads, width=width, lanes=lanes, feature_rows=feature_rows,
            bucket_rows=bucket_rows,
        ),
        grid=(fsdp_size,),
        in_specs=[
            pl.BlockSpec((1, rows, model_width), lambda s: (s, 0, 0)),
            whole((model_width, lanes.width)),
            pl.BlockSpec((1, rows), lambda s: (0, s)),
        ],
        out_specs=[
            pl.BlockSpec((rows, model_width), lambda s: (s, 0)),
            head_t(SKEW), head_n(SKEW), head_n(width), head_n(width), head_t(width), head_t(width),
            whole((heads, 1, span)),
            whole((8, lanes.extra)),
        ],
        out_shape=(
            shape_of((length, model_width), BF16),
            shape_of((heads, SKEW, length), BF16),
            shape_of((heads, length, SKEW), BF16),
            shape_of((heads, length, width), BF16),
            shape_of((heads, length, width), BF16),
            shape_of((heads, width, length), BF16),
            shape_of((heads, width, length), BF16),
            shape_of((heads, 1, span), F32),
            shape_of((8, lanes.extra), F32),
        ),
        scratch_shapes=[
            pltpu.VMEM((lanes.weights, model_width), BF16),
            pltpu.VMEM((lanes.extra, span), F32),
        ],
        compiler_params=params(),
        cost_estimate=hint(8),
        name="project",
    )(all_tokens, plane, segments.reshape(1, length))

    by_head = lambda *size: pl.BlockSpec((1,) + size, lambda h: (h, 0, 0))
    context, context_high, log_total = pl.pallas_call(
        partial(attend_kernel, rows=rows),
        grid=(heads,),
        in_specs=[
            by_head(SKEW, length), by_head(length, SKEW), by_head(width, length), by_head(1, span),
        ],
        out_specs=[
            pl.BlockSpec((fsdp_size, width, rows), lambda h: (0, h, 0)),
            by_head(width, length),
            by_head(1, length),
        ],
        out_shape=(
            shape_of((fsdp_size, heads * width, rows), BF16),
            shape_of((heads, width, length), F32),
            shape_of((heads, 1, length), F32),
        ),
        scratch_shapes=[
            pltpu.VMEM((SKEW, span), F32),
            pltpu.VMEM((WINDOW + QUERY_BLOCK, QUERY_BLOCK), F32),
        ],
        compiler_params=params(),
        cost_estimate=hint(13),
        name="attend",
    )(query_t, key_n, value_t, bias)

    (attended_t,) = exchange("fsdp", [(context, None)], 1, 9)
    own_down, near_up[0], attended_t = lax.optimization_barrier(
        (own_shards[0][1], near_up[0], attended_t)
    )
    near_down[0] = along_x(own_down)
    attended_t = attended_t.reshape(padded_heads * width, rows)

    gate_lanes = -(-local * capacity // 128) * 128
    hidden, routed, probabilities, gates, outgoing, slot_gates = pl.pallas_call(
        partial(route_kernel, experts=experts, lanes=lanes, capacity=capacity),
        out_shape=(
            shape_of((rows, model_width), F32),
            shape_of((rows, model_width), BF16),
            shape_of((rows, lanes.extra), F32),
            shape_of((rows, 2), F32),
            shape_of((exp_size, local * capacity, model_width), BF16),
            shape_of((exp_size, 8, gate_lanes), F32),
        ),
        compiler_params=params(),
        cost_estimate=hint(7),
        name="route",
    )(tokens, attended_t, full_out, plane, columns, position_rows)

    later = [own_shards[index] for index in range(1, local)]
    outgoing, later = lax.optimization_barrier((outgoing, later))
    for index in range(1, local):
        near_up[index], near_down[index] = [along_x(array) for array in later[index - 1]]
    outgoing = outgoing.reshape(exp_size, local, capacity, model_width)

    def down_parts(early, rest):
        return [(early[0][hop], rest[hop]) for hop in range(chips - 1)]

    def pass_along(arrays):
        return [over_x(arrays[0][hop - 1], hop) for hop in range(1, chips)]

    ready = [own_shards[0][0]] + near_up[0] + [own_shards[0][1]]
    rows_in, gates_in, *crossed = exchange(
        "exp", [(outgoing, 0), (slot_gates, None)], 2, 28, across=ready
    )
    swapped = (crossed[:-1], crossed[-1:])
    returned, groups, moved, outs = [], [], [], None
    late_rows_in = ()
    for index in range(local):
        final = index == local - 1
        carried = list(moved)
        if not final:
            carried.append((outgoing, index + 1))
        if index == 0 and late:
            carried.append((cotangent_late[0], None))
        result = run_expert(
            index, local, rows_in, gates_in, cotangent_in, late_rows_in if final else (),
            [own_shards[index][0]] + near_up[index], [own_shards[index][1]] + near_down[index],
            swapped, () if final else own_shards[index + 1], carried, outs, 3 + index,
        )
        (outs,) = result.rows_out
        arrived = list(result.moved_to)
        if index == 0 and late:
            late_rows_in = (arrived.pop(),)
        if not final:
            rows_in = arrived.pop()
            swapped = (result.next_swapped[:1], result.next_swapped[1:])
            moved = [(result.grad_rows[0], None), (result.grad_gates[0], None)]
        if arrived:
            returned.append(arrived)
        up_keep, up_taken, down_keep, down_taken = result.own
        if not final:
            passed = (result.pass_up, result.pass_down)
            passed, rows_in = lax.optimization_barrier((passed, rows_in))
            groups.append(
                [
                    (up_keep, up_taken, pass_along(passed[0])),
                    (down_keep, down_taken, down_parts(result.early_down, pass_along(passed[1]))),
                ]
            )
    returned.append([result.back_rows[0], result.back_gates[0]])
    groups, returned = lax.optimization_barrier((groups, returned))

    outs, returned = lax.optimization_barrier((outs, returned))
    out_rows = lax.all_to_all(outs, "exp", split_axis=0, concat_axis=0, tiled=True)

    grad_hidden, grad_branch, small = pl.pallas_call(
        partial(
            unroute_kernel, experts=experts, local=local, token_total=token_total, lanes=lanes
        ),
        out_shape=(
            shape_of((rows, model_width), F32),
            shape_of((rows, model_width), BF16),
            shape_of((model_width, lanes.extra), F32),
        ),
        compiler_params=params(),
        cost_estimate=hint(1),
        name="unroute",
    )(
        hidden, cotangent, routed, probabilities, gates, plane, columns, counts,
        *[part[0] for part in returned], *[part[1] for part in returned],
    )

    all_branch = gather_rows(grad_branch, 4 + local, 1)
    pass_up, all_branch = lax.optimization_barrier((result.pass_up, all_branch))
    groups.append(
        [
            (up_keep, up_taken, pass_along(pass_up)),
            (down_keep, down_taken, down_parts(result.early_down, pass_along(result.pass_down))),
        ]
    )
    padded_out = full_out
    if padded_heads > head_count:
        padded_out = jnp.pad(full_out, ((0, padded_heads * width - model_width), (0, 0)))
    grad_t, grad_n, out_grad = pl.pallas_call(
        partial(context_grad_kernel, heads=heads, width=width),
        grid_spec=pltpu.PrefetchScalarGridSpec(
            num_scalar_prefetch=1,
            grid=(fsdp_size,),
            in_specs=[
                pl.BlockSpec((1, rows, model_width), lambda s, f: (s, 0, 0)),
                pl.BlockSpec((heads * width, model_width), lambda s, f: (f[0], 0)),
                pl.BlockSpec((1, heads * width, rows), lambda s, f: (s, 0, 0)),
            ],
            out_specs=[head_t(width), head_n(width), whole((heads * width, model_width))],
            scratch_shapes=[pltpu.VMEM((heads * width, model_width), F32)],
        ),
        out_shape=(
            shape_of((heads, width, length), BF16),
            shape_of((heads, length, width), BF16),
            shape_of((heads * width, model_width), BF16),
        ),
        compiler_params=params(),
        cost_estimate=hint(1),
        name="context_grad",
    )(fsdp_index.reshape(1), all_branch, padded_out, context)

    grad_projected, grad_bias = pl.pallas_call(
        partial(attend_back_kernel, scale=width ** (-0.5)),
        grid=(heads,),
        in_specs=[
            by_head(SKEW, length), by_head(length, SKEW), by_head(length, width),
            by_head(length, width), by_head(width, length), by_head(width, length),
            by_head(length, width), by_head(width, length), by_head(1, length), by_head(1, span),
        ],
        out_specs=[
            pl.BlockSpec((3, 1, width, length), lambda h: (0, h, 0, 0)),
            by_head(1, span),
        ],
        out_shape=(
            shape_of((3, heads, width, length), BF16),
            shape_of((heads, 1, span), F32),
        ),
        scratch_shapes=[
            pltpu.VMEM((SKEW, span), F32),
            pltpu.VMEM((SKEW, span), F32),
            pltpu.VMEM((length, width), F32),
            pltpu.VMEM((length, width), F32),
        ],
        compiler_params=params(),
        cost_estimate=hint(1),
        name="attend_back",
    )(query_t, key_n, query_n, value_n, key_t, grad_t, grad_n, context_high, log_total, bias)
    grad_projected = grad_projected.reshape(lanes.weights, length)

    grad_first, grad_plane = pl.pallas_call(
        partial(
            project_back_kernel, lanes=lanes, heads=heads, feature_rows=feature_rows,
            bucket_rows=bucket_rows,
        ),
        grid=(fsdp_size,),
        in_specs=[
            pl.BlockSpec((lanes.weights, rows), lambda s: (0, s)),
            pl.BlockSpec((rows, model_width), lambda s: (s, 0)),
            whole((model_width, lanes.width)),
            whole((model_width, lanes.extra)),
            whole((rows, lanes.extra)),
            whole((heads, 1, span)),
        ],
        out_specs=[
            pl.BlockSpec((1, model_width, rows), lambda s: (s, 0, 0)),
            whole((model_width, lanes.width)),
        ],
        out_shape=(
            shape_of((fsdp_size, model_width, rows), BF16),
            shape_of((model_width, lanes.width), BF16),
        ),
        scratch_shapes=[
            pltpu.VMEM((lanes.width, model_width), F32),
            pltpu.VMEM((lanes.extra, span), F32),
        ],
        compiler_params=params(),
        cost_estimate=hint(1),
        name="project_back",
    )(grad_projected, normed, plane, small, probabilities, grad_bias)

    out_rows, grad_first = lax.optimization_barrier((out_rows, grad_first))
    spread_out = heads * width * fsdp_size != model_width
    if spread_out:
        out_grad = lax.dynamic_update_slice(
            jnp.zeros((padded_heads * width, model_width), BF16), out_grad,
            (fsdp_index * heads * width, jnp.int32(0)),
        )[:model_width]
    out_grad = out_grad.reshape(-1, feature_rows, model_width)
    out_count = device_count if spread_out else exp_size
    plane_shape = (grid.z_size, grid.y_size, fsdp_size, feature_rows, lanes.width)
    parts_shape = (fsdp_size, feature_rows, lanes.width)
    copies = 3 * fsdp_size + grid.z_size * grid.y_size + grid.z_size + out_count
    first_parts, plane_parts, out_parts = pl.pallas_call(
        partial(last_kernel, spread_out=spread_out),
        out_shape=(
            shape_of((chips, model_width, rows), BF16),
            shape_of(parts_shape, BF16),
            shape_of((out_count, feature_rows, model_width), BF16),
        ),
        in_specs=[IN_VMEM] * 3,
        out_specs=(IN_VMEM, ANYWHERE, ANYWHERE),
        scratch_shapes=[
            pltpu.VMEM((chips, model_width, rows), BF16),
            pltpu.VMEM((max(chips - 1, 1), model_width, rows), BF16),
            pltpu.VMEM((max(grid.y_size - 1, 1), grid.z_size) + parts_shape, BF16),
            pltpu.VMEM((grid.z_size,) + parts_shape, BF16),
            pltpu.VMEM((max(grid.z_size - 1, 1),) + parts_shape, BF16),
            pltpu.VMEM(parts_shape, BF16),
            dma_sems(copies),
            dma_sems(copies),
            dma_sems(2),
        ],
        compiler_params=params(collective_id=5 + local, has_side_effects=True),
        cost_estimate=hint(1),
        name="last",
    )(grad_first, grad_plane.reshape(plane_shape), out_grad)

    groups, first_parts = lax.optimization_barrier((groups, first_parts))
    (
        grad_tokens, gain_grad, in_grad, out_sum, mixture_gain_grad, router_grad, table_grad, balance,
    ) = pl.pallas_call(
        partial(
            finish_kernel, lanes=lanes, heads=heads, width=width, head_count=head_count,
            experts=experts, token_total=token_total,
        ),
        out_shape=(
            shape_of((rows, model_width), F32),
            shape_of((1, feature_rows), F32),
            shape_of((feature_rows, 3 * model_width), F32),
            shape_of((feature_rows, model_width), F32),
            shape_of((1, feature_rows), F32),
            shape_of((experts, feature_rows), F32),
            shape_of((bucket_rows, head_count), F32),
            shape_of((1, 1), F32),
        ),
        compiler_params=params(),
        cost_estimate=hint(6),
        name="finish",
    )(first_parts, plane_parts, out_parts, tokens, grad_hidden, attention_in, gain_row, counts)

    layer_output = pl.pallas_call(
        partial(mixture_kernel, local=local),
        out_shape=shape_of((rows, model_width), BF16),
        compiler_params=params(),
        cost_estimate=hint(5),
        name="mixture",
    )(hidden, gates, columns, out_rows)

    up_grad, down_grad = sum_grads(groups, expert_up.shape, expert_down.shape, fsdp_size)
    return (
        layer_output,
        balance.reshape(()),
        grad_tokens,
        gain_grad.reshape(feature_rows),
        mixture_gain_grad.reshape(feature_rows),
        in_grad,
        out_sum,
        router_grad.T,
        table_grad,
        up_grad,
        down_grad,
    )


def solution(mesh):
    in_specs = (
        P(("exp", "fsdp"), None),
        P(("exp", "fsdp"), None),
        P("exp"),
        P(("exp", "fsdp"), None),
        P(("exp", "fsdp"), None),
        P(("exp", "fsdp")),
        P(("exp", "fsdp")),
        P(("exp", "fsdp"), None),
        P(("exp", "fsdp"), None),
        P(("exp", "fsdp"), None),
        P(("exp", "fsdp"), None),
        P("exp", "fsdp", None),
        P("exp", "fsdp", None),
    )
    out_specs = (
        P(("exp", "fsdp"), None),
        P(),
        P(("exp", "fsdp"), None),
        P(("exp", "fsdp")),
        P(("exp", "fsdp")),
        P(("exp", "fsdp"), None),
        P(("exp", "fsdp"), None),
        P(("exp", "fsdp"), None),
        P(("exp", "fsdp"), None),
        P("exp", "fsdp", None),
        P("exp", "fsdp", None),
    )
    return jax.shard_map(
        on_device, mesh=mesh, in_specs=in_specs, out_specs=out_specs, check_vma=False
    )
```

```python
from functools import partial

import jax
import jax.numpy as jnp
from jax import lax
from jax.experimental import pallas as pl
from jax.experimental.pallas import tpu as pltpu
from jax.sharding import PartitionSpec as P

WINDOW = 1024
BUCKETS = 256

EPSILON = 1e-06
AUX_WEIGHT = 0.01
MASKED = -1e30
QUERY_BLOCK = 256
SKEW = 128
VMEM_BYTES = 58 * 1024 * 1024
MESH = pl.DeviceIdType.MESH
F32 = jnp.float32
BF16 = jnp.bfloat16


def params(**kwargs):
    return pltpu.CompilerParams(vmem_limit_bytes=VMEM_BYTES, **kwargs)


def shape_of(shape, dtype):
    return jax.ShapeDtypeStruct(shape, dtype)


def whole(shape):
    return pl.BlockSpec(shape, lambda *_: (0,) * len(shape))


def contract_last(left_side, right_side):
    return lax.dot_general(
        left_side, right_side, (((1,), (1,)), ((), ())), preferred_element_type=F32
    )


def matmul(left_side, right_side):
    return jnp.dot(left_side, right_side, preferred_element_type=F32)


def turned(value):
    return value.astype(F32).T


def bucket_index(distance):
    near_count = BUCKETS // 2
    spread = max(WINDOW - near_count, 1)
    far_bucket = (
        near_count + jnp.maximum(distance - near_count, 0) * (BUCKETS - near_count) // spread
    )
    return jnp.where(distance < near_count, distance, far_bucket)

def hint(micros):
    return pl.CostEstimate(flops=int(micros * 1.0e9), bytes_accessed=1024, transcendentals=0)


class Grid:
    def __init__(self):
        self.exp_size, self.fsdp_size = lax.axis_size("exp"), lax.axis_size("fsdp")
        self.device_count = self.exp_size * self.fsdp_size
        self.y_size = max(
            y for y in range(1, self.exp_size + 1) if self.exp_size % y == 0 and 2 * y * y <= self.exp_size
        ) if self.exp_size > 1 else 1
        self.z_size = self.exp_size // self.y_size
        self.x_size = self.fsdp_size // 2

    def here(self):
        self.exp, self.fsdp = lax.axis_index("exp"), lax.axis_index("fsdp")
        self.z, self.y = self.exp // self.y_size, self.exp % self.y_size
        self.x, self.core = self.fsdp // 2, self.fsdp % 2
        self.linear = self.exp * self.fsdp_size + self.fsdp
        return self

    def at(self, z=None, y=None, fsdp=None):
        z = self.z if z is None else z
        y = self.y if y is None else y
        return (z * self.y_size + y, self.fsdp if fsdp is None else fsdp)

    def x_from(self, hop):
        return ((self.x + self.x_size + hop) % self.x_size) * 2 + self.core

    def sibling(self, fsdp):
        return fsdp + 1 - 2 * (fsdp % 2)


class Links:
    def __init__(self, send, receive):
        self.send, self.receive, self.used = send, receive, 0

    def copy(self, source, target, device, landing):
        index = self.used
        self.used += 1
        going = pltpu.make_async_remote_copy(
            src_ref=source, dst_ref=target, send_sem=self.send.at[index],
            recv_sem=self.receive.at[index], device_id=device, device_id_type=MESH,
        )
        coming = pltpu.make_async_remote_copy(
            src_ref=landing, dst_ref=landing, send_sem=self.send.at[index],
            recv_sem=self.receive.at[index], device_id=device, device_id_type=MESH,
        )
        return going, coming


def greet(devices):
    barrier = pltpu.get_barrier_semaphore()
    for device in devices:
        pl.semaphore_signal(barrier, inc=1, device_id=device, device_id_type=MESH)
    pl.semaphore_wait(barrier, len(devices))


def chip_peers(grid):
    peers = [(grid.exp, grid.sibling(grid.fsdp))]
    return peers + [(grid.exp, grid.x_from(hop)) for hop in range(1, grid.x_size)]


class ChipGather:
    def __init__(self, grid, links, own_sem, source, target):
        self.grid, self.links, self.target = grid, links, target
        self.own = pltpu.make_async_copy(source, target.at[grid.fsdp], own_sem)
        sibling = grid.sibling(grid.fsdp)
        self.along_x, self.across = [], []
        for hop in range(1, grid.x_size):
            self.along_x.append(
                links.copy(
                    source, target.at[grid.fsdp], (grid.exp, grid.x_from(hop)),
                    target.at[grid.x_from(-hop)],
                )
            )
        self.across.append(
            links.copy(source, target.at[grid.fsdp], (grid.exp, sibling), target.at[sibling])
        )

    def start(self):
        for going, _ in self.along_x + self.across:
            going.start()
        self.own.start()

    def forward(self):
        grid = self.grid
        for hop in range(1, grid.x_size):
            self.along_x[hop - 1][1].wait_recv()
            held = grid.x_from(-hop)
            other = grid.sibling(held)
            self.across.append(
                self.links.copy(
                    self.target.at[held], self.target.at[held],
                    (grid.exp, grid.sibling(grid.fsdp)), self.target.at[other],
                )
            )
            self.across[-1][0].start()

    def finish(self):
        for _, coming in self.across:
            coming.wait_recv()
        for going, _ in self.along_x + self.across:
            going.wait_send()
        self.own.wait()


class Exchange:
    def __init__(self, grid, axis, links, own_sems, pairs):
        size = grid.exp_size if axis == "exp" else grid.fsdp_size
        place = grid.exp if axis == "exp" else grid.fsdp
        device = (lambda to: (to, grid.fsdp)) if axis == "exp" else (lambda to: (grid.exp, to))
        self.peers = [device((place + hop) % size) for hop in range(1, size)]
        self.copies, self.own = [], []
        for index, (source, target) in enumerate(pairs):
            for hop in range(1, size):
                to, origin = (place + hop) % size, (place + size - hop) % size
                self.copies.append(
                    links.copy(source(to), target.at[place], device(to), target.at[origin])
                )
            self.own.append(
                pltpu.make_async_copy(source(place), target.at[place], own_sems.at[index])
            )

    def start(self):
        for going, _ in self.copies:
            going.start()
        for own in self.own:
            own.start()

    def finish(self):
        for going, coming in self.copies:
            coming.wait_recv()
            going.wait_send()
        for own in self.own:
            own.wait()


ANYWHERE = pl.BlockSpec(memory_space=pl.ANY)
IN_VMEM = pl.BlockSpec(memory_space=pltpu.VMEM)


def dma_sems(count):
    return pltpu.SemaphoreType.DMA((count,))


def exchange(axis, arrays, collective_id, micros, across=()):
    grid = Grid()
    size = grid.exp_size if axis == "exp" else grid.fsdp_size
    count, crossing = len(arrays), len(across)
    parts = [part for _, part in arrays]

    def kernel(*refs):
        sources, over = refs[:count], refs[count : count + crossing]
        refs = refs[count + crossing :]
        targets, landed = refs[:count], refs[count : count + crossing]
        send, receive, own = refs[count + crossing :]
        place = grid.here()
        links = Links(send, receive)
        sibling = (place.exp, place.sibling(place.fsdp))
        pairs = [
            (partial(plane_of, source, part), target)
            for source, part, target in zip(sources, parts, targets)
        ]
        work = Exchange(place, axis, links, own, pairs)
        swaps = [
            links.copy(source, target, sibling, target) for source, target in zip(over, landed)
        ]
        greet(work.peers + ([sibling] if swaps and axis == "exp" else []))
        work.start()
        for going, _ in swaps:
            going.start()
        work.finish()
        for going, coming in swaps:
            coming.wait_recv()
            going.wait_send()

    return pl.pallas_call(
        kernel,
        out_shape=tuple(
            [
                shape_of((size,) + array.shape[(1 if part is None else 2) :], array.dtype)
                for array, part in arrays
            ]
            + [shape_of(array.shape, array.dtype) for array in across]
        ),
        in_specs=[IN_VMEM] * count + [ANYWHERE] * crossing,
        out_specs=tuple([ANYWHERE] * (count + crossing)),
        scratch_shapes=[
            dma_sems(count * size + crossing), dma_sems(count * size + crossing), dma_sems(count),
        ],
        compiler_params=params(collective_id=collective_id, has_side_effects=True),
        cost_estimate=hint(micros),
        name=f"exchange_{collective_id}",
    )(*[array for array, _ in arrays], *across)


def plane_of(source, part, to):
    return source.at[to] if part is None else source.at[to, part]


class Lanes:
    def __init__(self, heads, width, padded_heads, experts):
        self.weights = 3 * heads * width
        self.base = self.weights // 128 * 128
        self.router = self.weights - self.base
        self.gain = self.router + experts
        self.table = self.gain + 1
        self.count = self.table + padded_heads
        self.width = -(-(self.weights + 2 * experts + 1 + padded_heads) // 128) * 128
        self.extra = self.width - self.base
        self.shift = self.count - self.router


def bucket_rows_select(features, feature_rows, bucket_rows, span):
    row = lax.broadcasted_iota(jnp.int32, (features, 1), 0)
    within = lax.rem(row, feature_rows)
    bucket = jnp.where(
        within < bucket_rows, lax.div(row, feature_rows) * bucket_rows + within, -1
    )
    distance = lax.broadcasted_iota(jnp.int32, (1, span), 1) - SKEW
    near = BUCKETS // 2
    spread = max(WINDOW - near, 1)
    far = near + lax.div(jnp.maximum(distance - near, 0) * (BUCKETS - near), spread)
    wanted = jnp.where(distance < near, distance, far)
    reachable = (distance >= 0) & (distance < WINDOW)
    wanted = jnp.where(reachable, wanted, -2)
    return jnp.where(bucket == wanted, 1.0, 0.0).astype(BF16), reachable


def as_column(row, size):
    row_place = lax.broadcasted_iota(jnp.int32, (size, size), 0)
    lane = lax.broadcasted_iota(jnp.int32, (size, size), 1)
    spread = jnp.broadcast_to(row.astype(F32), (size, size))
    return jnp.sum(jnp.where(row_place == lane, spread, 0.0), axis=1, keepdims=True)


def padded_rows(value, rows):
    if value.shape[0] == rows:
        return value
    return jnp.concatenate([value, jnp.zeros((rows - value.shape[0], value.shape[1]), F32)], axis=0)


def padded_lanes(value, lanes):
    if value.shape[1] == lanes:
        return value
    return jnp.concatenate([value, jnp.zeros((value.shape[0], lanes - value.shape[1]), F32)], axis=1)


class Wide:
    def __init__(self, grid, links, own_sem, source, target):
        self.grid, self.links, self.target = grid, links, target
        self.own = pltpu.make_async_copy(
            source, target.at[grid.z, grid.y, grid.x, grid.core], own_sem
        )
        stage = []
        for hop in range(1, grid.z_size):
            origin = (grid.z + grid.z_size - hop) % grid.z_size
            stage.append(
                links.copy(
                    source, target.at[grid.z, grid.y, grid.x, grid.core],
                    grid.at(z=(grid.z + hop) % grid.z_size),
                    target.at[origin, grid.y, grid.x, grid.core],
                )
            )
        self.stages = [stage]

    def start(self):
        self.own.start()
        for going, _ in self.stages[0]:
            going.start()

    def turn(self, axis):
        grid, target = self.grid, self.target
        for _, coming in self.stages[-1]:
            coming.wait_recv()
        stage = []
        if axis == 0:
            self.own.wait()
            held = target.at[:, grid.y, grid.x, grid.core]
            for hop in range(1, grid.y_size):
                origin = (grid.y + grid.y_size - hop) % grid.y_size
                stage.append(
                    self.links.copy(
                        held, held, grid.at(y=(grid.y + hop) % grid.y_size),
                        target.at[:, origin, grid.x, grid.core],
                    )
                )
        elif axis == 1:
            held = target.at[:, :, grid.x, grid.core]
            for hop in range(1, grid.x_size):
                origin = (grid.x + grid.x_size - hop) % grid.x_size
                stage.append(
                    self.links.copy(
                        held, held, (grid.exp, grid.x_from(hop)),
                        target.at[:, :, origin, grid.core],
                    )
                )
        else:
            held = target.at[:, :, :, grid.core]
            stage.append(
                self.links.copy(
                    held, held, (grid.exp, grid.sibling(grid.fsdp)), target.at[:, :, :, 1 - grid.core]
                )
            )
        for going, _ in stage:
            going.start()
        self.stages.append(stage)

    def finish(self):
        for _, coming in self.stages[-1]:
            coming.wait_recv()
        for stage in self.stages:
            for going, _ in stage:
                going.wait_send()


def start_kernel(
    tokens, cotangent, routes_t, slots_t, attention_gain, mixture_gain, attention_in, router_t, table,
    attention_out, expert_up, expert_down, *refs, lanes, heads, width, head_count, experts, capacity,
    local, late,
):
    all_tokens, all_planes, cotangent_early, position_rows, columns, full_out = refs[:6]
    cotangent_late, refs = refs[6 : 6 + late], refs[6 + late :]
    shards = refs[: 2 * local]
    planes, up_stage, down_stage, send, receive, own, fetch, split = refs[2 * local :]
    grid = Grid().here()
    links = Links(send, receive)
    z_size, y_size, fsdp_size = grid.z_size, grid.y_size, grid.fsdp_size
    near = [
        (grid.exp, (grid.fsdp + turn) % fsdp_size) for turn in range(1, fsdp_size)
    ] + [grid.at(z=(grid.z + hop) % z_size) for hop in range(1, z_size)]
    beside = [grid.at(y=(grid.y + hop) % y_size) for hop in range(1, y_size)]
    gathered = ChipGather(grid, links, own.at[0], tokens, all_tokens)
    widely = Wide(grid, links, own.at[2], attention_out, full_out)
    part = expert_down.shape[1]
    depth = expert_up.shape[1]
    fetches = []
    for index in range(local):
        fetches.append(
            pltpu.make_async_copy(expert_up.at[index], up_stage.at[index], fetch.at[2 * index])
        )
        fetches.append(
            pltpu.make_async_copy(
                expert_down.at[index], down_stage.at[index], fetch.at[2 * index + 1]
            )
        )
    greet(near + beside)
    widely.start()
    for copy in fetches:
        copy.start()

    feature_rows = attention_in.shape[0]
    model_width = head_count * width
    gained = attention_in[...].astype(F32) * as_column(attention_gain[...], feature_rows)
    route_rows, slot_rows = routes_t[...].astype(F32), slots_t[...].astype(F32)
    columns[...] = padded_rows(jnp.concatenate([route_rows, slot_rows], axis=0), 128).T
    row_count = columns.shape[0]
    expert_lanes = lax.broadcasted_iota(jnp.int32, (row_count, experts), 1).astype(F32)
    named = jnp.zeros((row_count, experts), F32)
    for k in range(2):
        named = named + jnp.where(expert_lanes == columns[:, k : k + 1], 1.0, 0.0)
    named = jnp.sum(named, axis=0, keepdims=True)
    place = lax.broadcasted_iota(jnp.int32, (feature_rows, feature_rows), 0)
    same = place == lax.broadcasted_iota(jnp.int32, (feature_rows, feature_rows), 1)
    router = contract_last(jnp.where(same, 1.0, 0.0).astype(BF16), router_t[...])
    pieces = [
        router,
        as_column(mixture_gain[...], feature_rows),
        padded_rows(padded_lanes(table[...].astype(F32), heads * fsdp_size), feature_rows),
        padded_rows(named, feature_rows),
    ]
    taken = sum(piece.shape[1] for piece in pieces)
    if lanes.width > lanes.weights + taken:
        pieces.append(jnp.zeros((feature_rows, lanes.width - lanes.weights - taken), F32))
    for place in range(fsdp_size):
        first, last = place * heads * width, min((place + 1) * heads * width, model_width)
        own_pieces = []
        for kind in range(3):
            if last > first:
                own_pieces.append(gained[:, kind * model_width + first : kind * model_width + last])
            if last - first < heads * width:
                own_pieces.append(
                    jnp.zeros((feature_rows, heads * width - max(last - first, 0)), F32)
                )
        planes[place] = jnp.concatenate(own_pieces + pieces, axis=1).astype(BF16)
    placed = []
    for turn in range(1, fsdp_size):
        to = (grid.fsdp + turn) % fsdp_size
        origin = (grid.fsdp + fsdp_size - turn) % fsdp_size
        placed.append(
            links.copy(
                planes.at[to], all_planes.at[grid.z, grid.y, grid.fsdp], (grid.exp, to),
                all_planes.at[grid.z, grid.y, origin],
            )
        )
        placed[-1][0].start()
    kept = pltpu.make_async_copy(
        planes.at[grid.fsdp], all_planes.at[grid.z, grid.y, grid.fsdp], own.at[1]
    )
    kept.start()
    gathered.start()
    for _, coming in placed:
        coming.wait_recv()
    kept.wait()

    def over_y(z):
        for turn in range(1, y_size):
            forwarded.append(
                links.copy(
                    all_planes.at[z, grid.y],
                    all_planes.at[z, grid.y],
                    grid.at(y=(grid.y + turn) % y_size),
                    all_planes.at[z, (grid.y + y_size - turn) % y_size],
                )
            )
            forwarded[-1][0].start()

    along_z, forwarded = [], []
    for hop in range(1, z_size):
        along_z.append(
            links.copy(
                all_planes.at[grid.z, grid.y],
                all_planes.at[grid.z, grid.y],
                grid.at(z=(grid.z + hop) % z_size),
                all_planes.at[(grid.z + z_size - hop) % z_size, grid.y],
            )
        )
        along_z[-1][0].start()
    over_y(grid.z)
    widely.turn(0)

    for copy in fetches:
        copy.wait()
    splits = []
    for index in range(local):
        up, down = shards[2 * index : 2 * index + 2]
        stores = [
            (
                up_stage.at[index, :, pl.ds(block * part, part)],
                up.at[pl.ds(block * depth, depth), :],
            )
            for block in range(fsdp_size)
        ]
        for source, target in stores + [(down_stage.at[index], down)]:
            splits.append(pltpu.make_async_copy(source, target, split.at[len(splits)]))
            splits[-1].start()

    widely.turn(1)

    place = route_rows * capacity + slot_rows
    position_rows[...] = padded_rows(place, 8)
    select_rows([cotangent_early] + list(cotangent_late), place, cotangent[...])

    for hop in range(1, z_size):
        along_z[hop - 1][1].wait_recv()
        over_y((grid.z + z_size - hop) % z_size)
    gathered.forward()
    widely.turn(2)
    for going, coming in forwarded:
        coming.wait_recv()
        going.wait_send()
    for going, _ in placed + along_z:
        going.wait_send()
    gathered.finish()
    widely.finish()
    for copy in splits:
        copy.wait()


def project_kernel(
    tokens, plane, segments, normed, query_t, key_n, query_n, value_n, key_t, value_t, bias, counts,
    weight_t, table_t, *, heads, width, lanes, feature_rows, bucket_rows,
):
    @pl.when(pl.program_id(0) == 0)
    def _():
        weight_t[...] = turned(plane[:, : lanes.weights]).astype(BF16)
        extra = plane[:, lanes.base :]
        span = bias.shape[2]
        select, reachable = bucket_rows_select(plane.shape[0], feature_rows, bucket_rows, span)
        table_t[...] = lax.dot_general(
            extra, select, (((0,), (0,)), ((), ())), preferred_element_type=F32
        )
        first = lanes.table + lax.axis_index("fsdp") * heads
        for head in range(heads):
            bias[head] = jnp.where(reachable, table_t[pl.ds(first + head, 1), :], MASKED)
        summed = jnp.sum(extra.astype(F32), axis=0, keepdims=True)
        counts[...] = pltpu.roll(
            jnp.broadcast_to(summed, counts.shape), lanes.extra - lanes.shift, 1
        )

    inputs = tokens[0].astype(F32)
    scale = lax.rsqrt(jnp.mean(inputs * inputs, axis=1, keepdims=True) + EPSILON)
    low = (inputs * scale).astype(BF16)
    normed[...] = low
    rows = low.shape[0]
    projected = contract_last(weight_t[...], low).astype(BF16).astype(F32)
    document = segments[...] % 4
    places = lax.broadcasted_iota(jnp.int32, (8, rows), 0)
    same = places == document
    hot = jnp.where(same, 1.0, 0.0)
    barred = jnp.where(same | (places >= 4), 0.0, MASKED)
    filler = jnp.zeros((SKEW - 8 - width, rows), F32)
    for head in range(heads):
        query = projected[head * width : (head + 1) * width] * width ** (-0.5)
        key = projected[(heads + head) * width : (heads + head + 1) * width]
        value = projected[(2 * heads + head) * width : (2 * heads + head + 1) * width]
        query_t[head] = jnp.concatenate([query, barred, filler], axis=0).astype(BF16)
        key_n[head] = jnp.concatenate([key, hot, filler], axis=0).T.astype(BF16)
        query_n[head] = query.T.astype(BF16)
        value_n[head] = value.T.astype(BF16)
        key_t[head] = key.astype(BF16)
        value_t[head] = value.astype(BF16)


def spans(length):
    for query_start in range(0, length, QUERY_BLOCK):
        key_start = max(0, query_start - WINDOW)
        yield query_start, key_start, query_start + QUERY_BLOCK - key_start


def spread_bias(bias, skew):
    skew[...] = pltpu.roll(
        jnp.broadcast_to(bias[0], skew.shape), 0, 1, stride=1, stride_axis=0
    )


def attend_kernel(query_t, key_n, value_t, bias, context, context_high, log_total, skew, scores, *, rows):
    spread_bias(bias, skew)
    for query_start, key_start, key_count in spans(query_t.shape[2]):
        queries = slice(query_start, query_start + QUERY_BLOCK)
        keys = slice(key_start, key_start + key_count)
        raw = matmul(key_n[0, keys, :], query_t[0, :, queries])
        for start in range(0, key_count, SKEW):
            offset = query_start - key_start - start + SKEW
            scores[start : start + SKEW, :] = (
                raw[start : start + SKEW] + skew[:, offset : offset + QUERY_BLOCK]
            )
        high = jnp.max(scores[:key_count, :], axis=0, keepdims=True)
        weights = jnp.exp(scores[:key_count, :] - high)
        total = jnp.sum(weights, axis=0, keepdims=True)
        gathered = matmul(value_t[0, :, keys], weights.astype(BF16)) / total
        context_high[0, :, queries] = gathered
        log_total[0, :, queries] = high + jnp.log(total)
        for start in range(0, QUERY_BLOCK, 128):
            place = query_start + start
            context[place // rows, :, place % rows : place % rows + 128] = gathered[
                :, start : start + 128
            ].astype(BF16)


def attend_back_kernel(
    query_t, key_n, query_n, value_n, key_t, grad_t, grad_n, context_high, log_total, bias,
    grad_projected, grad_bias, skew, grad_skew, grad_key, grad_value, *, scale,
):
    spread_bias(bias, skew)
    grad_skew[...] = jnp.zeros_like(grad_skew)
    grad_key[...] = jnp.zeros_like(grad_key)
    grad_value[...] = jnp.zeros_like(grad_value)
    inner = jnp.sum(grad_t[0].astype(F32) * context_high[0], axis=0, keepdims=True)
    for query_start, key_start, key_count in spans(query_t.shape[2]):
        queries = slice(query_start, query_start + QUERY_BLOCK)
        keys = slice(key_start, key_start + key_count)
        raw = matmul(key_n[0, keys, :], query_t[0, :, queries])
        grad_weights = matmul(value_n[0, keys, :], grad_t[0, :, queries])
        weights_low, grad_low = [], []
        for start in range(0, key_count, SKEW):
            offset = query_start - key_start - start + SKEW
            part = slice(start, start + SKEW)
            weights = jnp.exp(
                raw[part] + skew[:, offset : offset + QUERY_BLOCK] - log_total[0, :, queries]
            )
            grad_scores = weights * (grad_weights[part] - inner[:, queries])
            grad_skew[:, offset : offset + QUERY_BLOCK] += grad_scores
            weights_low.append(weights.astype(BF16))
            grad_low.append(grad_scores.astype(BF16))
        weights_low = jnp.concatenate(weights_low, axis=0)
        grad_low = jnp.concatenate(grad_low, axis=0)
        grad_projected[0, 0, :, queries] = (matmul(key_t[0, :, keys], grad_low) * scale).astype(BF16)
        grad_key[keys, :] += matmul(grad_low, query_n[0, queries, :])
        grad_value[keys, :] += matmul(weights_low, grad_n[0, queries, :])
    grad_projected[1, 0] = grad_key[...].T.astype(BF16)
    grad_projected[2, 0] = grad_value[...].T.astype(BF16)
    count = SKEW
    span = skew.shape[1]
    while count > 8:
        count //= 2
        grad_skew[:count, :] += pltpu.roll(grad_skew[count : 2 * count, :], span - count, 1)
    summed = grad_skew[0:1, :]
    for row in range(1, 8):
        summed = summed + pltpu.roll(grad_skew[row : row + 1, :], span - row, 1)
    grad_bias[0] = summed

def expert_lane(shape, lanes):
    return lax.broadcasted_iota(jnp.int32, shape, 1) - lanes.router


def int_columns(columns):
    values = columns[:, 0:4].astype(jnp.int32)
    return values[:, 0:2], values[:, 2:4]


def route_kernel(
    tokens, attended_t, attention_out, plane, columns, position_rows,
    hidden, routed, probabilities, gates, outgoing, slot_gates, *, experts, lanes, capacity,
):
    rows, model_width = tokens.shape
    routes, slots = int_columns(columns)
    attended_low = turned(attended_t[:model_width]).astype(BF16)
    hidden_state = tokens[...].astype(F32) + matmul(attended_low, attention_out[...])
    hidden[...] = hidden_state
    scale = lax.rsqrt(jnp.mean(hidden_state * hidden_state, axis=1, keepdims=True) + EPSILON)
    extra = plane[:, lanes.base :]
    gain = extra.astype(F32).T[lanes.gain : lanes.gain + 1]
    low = (hidden_state * scale * gain).astype(BF16)
    routed[...] = low
    logits = matmul(low, extra)
    lane = expert_lane(logits.shape, lanes)
    logits = jnp.where((lane >= 0) & (lane < experts), logits, MASKED)
    powers = jnp.exp(logits - jnp.max(logits, axis=1, keepdims=True))
    powers = powers / jnp.sum(powers, axis=1, keepdims=True)
    probabilities[...] = powers
    chosen = [
        jnp.sum(jnp.where(lane == routes[:, k : k + 1], powers, 0.0), axis=1, keepdims=True)
        for k in range(2)
    ]
    total = chosen[0] + chosen[1]
    gate_values = [chosen[k] / total for k in range(2)]
    pair = lax.broadcasted_iota(jnp.int32, (rows, 2), 1)
    gates[...] = jnp.where(pair == 0, gate_values[0], gate_values[1])
    members, _, gate_lanes = slot_gates.shape
    member_slots = experts // members * capacity
    slot_lanes = lax.broadcasted_iota(jnp.int32, (rows, gate_lanes), 1)
    inside = slot_lanes < member_slots
    places = routes * capacity + slots
    for member in range(members):
        by_slot = jnp.zeros((rows, gate_lanes), F32)
        for k in range(2):
            hit = (slot_lanes + member * member_slots == places[:, k : k + 1]) & inside
            by_slot = by_slot + jnp.where(hit, gate_values[k], 0.0)
        slot_gates[member] = jnp.broadcast_to(
            jnp.sum(by_slot, axis=0, keepdims=True), slot_gates.shape[1:]
        )
    select_rows([outgoing], position_rows[...], low)


def select_rows(outgoing, position_rows, values):
    rows = values.shape[0]
    sizes = [array.shape[1] for array in outgoing]
    for member in range(outgoing[0].shape[0]):
        slots = lax.broadcasted_iota(jnp.int32, (sum(sizes), rows), 0) + member * sum(sizes)
        slots = slots.astype(F32)
        picked = (slots == position_rows[0:1, :]) | (slots == position_rows[1:2, :])
        found = matmul(jnp.where(picked, 1.0, 0.0).astype(BF16), values).astype(BF16)
        first = 0
        for array, size in zip(outgoing, sizes):
            array[member] = found[first : first + size]
            first += size


def gelu_parts(value):
    magnitude = jnp.abs(value)
    power = jnp.exp2(value * value * -0.7213475204444817)
    base = 1.0 + (0.3275911 * 0.7071067811865476) * magnitude
    step = pl.reciprocal(base, approx=True)
    step = step * (2.0 - base * step)
    series = step * (
        0.127414796
        + step * (-0.142248368 + step * (0.7107068705 + step * (-0.7265760135 + step * 0.5307027145)))
    )
    tail = series * power
    normal = jnp.where(value < 0.0, tail, 1.0 - tail)
    return value * normal, normal + value * (power * 0.3989422804014327)


def flipped(place, other, size):
    result, bit = 0, 1
    while bit < size:
        result = result + bit * ((place // bit + other // bit) % 2)
        bit *= 2
    return result


def expert_kernel(*refs, layout, index, local, half, capacity, parts):
    shards = 2 * half
    refs = Bag(layout, refs)
    grid = Grid().here()
    z_size, y_size = grid.z_size, grid.y_size
    last = index == local - 1
    sibling = (grid.exp, grid.sibling(grid.fsdp))
    links = Links(refs.send[0], refs.receive[0])
    rows_all, cot, up_all, down_all = (
        refs.rows_all[0], refs.cot[0], refs.up_all[0], refs.down_all[0]
    )
    total = refs.total[0]
    if last:
        active, grad_hidden, unscaled = refs.active[0], refs.grad_hidden[0], refs.unscaled[0]
    else:
        grad_total, slot_grad = refs.grad_total[0], refs.slot_grad[0]
    gates, gate_column = refs.gates[0], refs.gate_column[0]
    rows_t, slot_t = refs.rows_t[0], refs.slot_t[0]
    grad_up, grad_down = refs.grad_up[0], refs.grad_down[0]
    grad_rows, grad_gates = refs.grad_rows[0], refs.grad_gates[0]
    up_keep, up_taken, down_keep, down_taken = refs.own
    keep_up = [up_keep] + list(refs.far_keep_up)
    taken_up = [up_taken] + list(refs.far_taken_up)
    keep_down = [down_keep] + list(refs.far_keep_down)
    taken_down = [down_taken] + list(refs.far_taken_down)
    load_sem, fetch_sem, store_sem = refs.load_sem[0], refs.fetch_sem[0], refs.store_sem[0]
    store_there, stored_here = refs.store_there[0], refs.stored_here[0]
    pass_sem = refs.pass_sem[0]
    blocks, _, model_width = rows_all.shape
    part = up_all.shape[2]
    count = blocks * capacity
    depth = model_width // shards
    power = z_size & (z_size - 1) == 0
    together = 2 if power and z_size > 1 else 1
    group_rows = together * y_size * capacity

    def source_z(turn):
        return flipped(grid.z, turn, z_size) if power else (grid.z + turn) % z_size

    def target_z(turn):
        return flipped(grid.z, turn, z_size) if power else (grid.z + z_size - turn) % z_size

    def owner(place, core):
        return ((grid.x + place % half) % half) * 2 + (core + place // half) % 2

    def rows_of(place, core=None):
        core = grid.core if core is None else core
        return pl.ds(pl.multiple_of(owner(place, core) * depth, 16), depth)

    loads = [pltpu.make_async_copy(refs.rows_in[0], rows_all, load_sem.at[1])]
    late_count = 0
    if last and refs.cot_late:
        late_count = refs.cot_late[0].shape[1]
        loads.append(
            pltpu.make_async_copy(
                refs.cot_late[0], cot.at[:, pl.ds(capacity - late_count, late_count)], load_sem.at[4]
            )
        )
    loads.append(
        pltpu.make_async_copy(
            refs.cot_in[0].at[:, pl.ds(index * capacity, capacity - late_count)],
            cot.at[:, pl.ds(0, capacity - late_count)], load_sem.at[0],
        )
    )
    my_up, my_down = refs.my_up, refs.my_down
    swapped_up, swapped_down = refs.swapped_up, refs.swapped_down
    local_up = list(enumerate(my_up)) + [
        (half + number, array) for number, array in enumerate(swapped_up)
    ]
    local_down = list(enumerate(my_down)) + [
        (half + number, array) for number, array in enumerate(swapped_down)
    ]

    def fetch_up(place):
        return [
            pltpu.make_async_copy(
                array.at[rows_of(place), :], up_all.at[place, rows_of(shard), :],
                fetch_sem.at[place, number],
            )
            for number, (shard, array) in enumerate(local_up)
        ]

    fetched_down = {
        shard: pltpu.make_async_copy(
            array, down_all.at[shard], fetch_sem.at[shards + number, 0]
        )
        for number, (shard, array) in enumerate(local_down)
    }
    cross_down = {
        half + shard: links.copy(
            my_down[shard], down_all.at[half + shard], sibling, down_all.at[half + shard]
        )
        for shard in range(len(swapped_down), half)
    }
    cross_up = [
        links.copy(
            my_up[shard].at[rows_of(place, 1 - grid.core), :],
            up_all.at[place, rows_of(shard), :], sibling,
            up_all.at[place, rows_of(half + shard), :],
        )
        for shard in range(len(swapped_up), half)
        for place in range(shards)
    ]
    cross_next = [
        links.copy(source, target, sibling, target)
        for source, target in zip(refs.next_mine, refs.next_swapped)
    ]
    work = Exchange(
        grid, "exp", links, refs.own_sem[0],
        [
            (partial(plane_of, source, place), target)
            for source, place, target in zip(refs.moved_from, parts, refs.moved_to)
        ],
    )
    def member(z, y):
        return z * y_size + y

    def give_back(turn, hop):
        to = member(source_z(turn), (grid.y + hop) % y_size)
        origin = member(target_z(turn), (grid.y + y_size - hop) % y_size)
        pairs = []
        for number, (held, target) in enumerate(
            ((grad_rows, refs.back_rows[0]), (grad_gates, refs.back_gates[0]))
        ):
            sems = dict(
                send_sem=refs.back_send[0].at[number, turn, hop],
                recv_sem=refs.back_receive[0].at[number, turn, hop],
                device_id=(to, grid.fsdp), device_id_type=MESH,
            )
            pairs.append(
                (
                    pltpu.make_async_remote_copy(
                        src_ref=held.at[to], dst_ref=target.at[grid.exp], **sems
                    ),
                    pltpu.make_async_remote_copy(
                        src_ref=target.at[origin], dst_ref=target.at[origin], **sems
                    ),
                )
            )
        return pairs

    steps = [(turn, hop) for turn in range(z_size) for hop in range(y_size)]
    own_back = []
    if last:
        own_back = [
            pltpu.make_async_copy(held.at[grid.exp], target.at[grid.exp], load_sem.at[2 + number])
            for number, (held, target) in enumerate(
                ((grad_rows, refs.back_rows[0]), (grad_gates, refs.back_gates[0]))
            )
        ]

    for copy in loads:
        copy.start()
    order = list(range(shards))
    if not last:
        order = [(pair + 1) % half + side * half for pair in range(half) for side in (1, 0)]
    if last:
        for copy in fetched_down.values():
            copy.start()
    for place in order:
        if not last and place in fetched_down:
            fetched_down[place].start()
        for copy in fetch_up(place):
            copy.start()
    greet(
        [((grid.exp + hop) % grid.exp_size, grid.fsdp) for hop in range(1, grid.exp_size)]
        + chip_peers(grid)
    )
    for going, _ in list(cross_down.values()) + cross_up + cross_next:
        going.start()
    work.start()

    def place_at(position):
        hop = (position // 2 + 1) % half
        return hop + half * (1 - position % 2)

    def slot_rows():
        columns = gates[:, 0, :].T
        for block in range(blocks):
            piece = slice(block * capacity, (block + 1) * capacity)
            gate = columns[index * capacity : (index + 1) * capacity, block : block + 1]
            gate_column[piece, :] = gate
        slot_values = gate_column[...] * cot[...].reshape(count, model_width).astype(F32)
        slot_t[...] = slot_values.T.astype(BF16)
        if not last:
            slot_grad[...] = slot_values.astype(BF16)

    def wait_down(place):
        if place in fetched_down:
            fetched_down[place].wait()
        else:
            cross_down[place][1].wait_recv()

    def wait_crossed():
        for _, coming in cross_up:
            coming.wait_recv()

    def folded(value):
        return sum(value[:, start : start + 128] for start in range(0, value.shape[1], 128))

    def gate_rows(found, block):
        ones = jnp.ones((8, 128), F32)
        grad_gates[block] = lax.dot_general(
            ones, found, (((1,), (1,)), ((), ())), precision=lax.Precision.HIGHEST,
            preferred_element_type=F32,
        )

    def up_target(targets, hop, place):
        if hop == 0:
            return targets[0].at[rows_of(place), :]
        return targets[1].at[hop - 1, rows_of(place), :]

    def keep_stores(place, slot):
        return [
            pltpu.make_async_copy(
                grad_up.at[slot, rows_of(hop), :], up_target(keep_up, hop, place),
                store_sem.at[slot, hop],
            )
            for hop in range(half)
        ]

    def give_stores(place, slot):
        return [
            pltpu.make_async_remote_copy(
                src_ref=grad_up.at[slot, rows_of(half + hop), :],
                dst_ref=up_target(taken_up, hop, place),
                send_sem=store_there.at[slot, hop], recv_sem=stored_here.at[place, hop],
                device_id=sibling, device_id_type=MESH,
            )
            for hop in range(half)
        ]

    def down_store(slot):
        return pltpu.make_async_copy(grad_down.at[slot], keep_down[0], store_sem.at[slot, half])

    def down_give(hop, slot):
        target = taken_down[0] if hop == 0 else taken_down[1].at[hop - 1]
        return pltpu.make_async_remote_copy(
            src_ref=grad_down.at[slot], dst_ref=target,
            send_sem=store_there.at[slot, half], recv_sem=stored_here.at[hop, half],
            device_id=sibling, device_id_type=MESH,
        )

    def start_store(place, slot):
        for copy in keep_stores(place, slot) + give_stores(place, slot):
            copy.start()

        @pl.when(place == 0)
        def _():
            down_store(slot).start()

        for hop in range(half):

            @pl.when(place == half + hop)
            def _(hop=hop):
                down_give(hop, slot).start()

            if hop > 0:

                @pl.when(place == hop)
                def _(hop=hop):
                    keep_down[1][hop - 1] = grad_down[slot]

    def wait_store(place, slot):
        for copy in keep_stores(place, slot):
            copy.wait()
        for copy in give_stores(place, slot):
            copy.wait_send()

        @pl.when(place == 0)
        def _():
            down_store(slot).wait()

        for hop in range(half):

            @pl.when(place == half + hop)
            def _(hop=hop):
                down_give(hop, slot).wait_send()

    early_rows = part // 2
    early = [
        links.copy(
            keep_down[1].at[hop - 1, pl.ds(0, early_rows), :], refs.early_down[0].at[hop - 1],
            (grid.exp, grid.x_from(hop)), refs.early_down[0].at[hop - 1],
        )
        for hop in range(1, half)
    ]

    def pass_early():
        for hop in range(1, half):
            down_give(hop, 0).wait_recv()
            keep_down[1][hop - 1] = (
                keep_down[1][hop - 1].astype(F32) + taken_down[1][hop - 1].astype(F32)
            ).astype(BF16)
            early[hop - 1][0].start()

    def fused(position, carry):
        place, slot = place_at(position), position % 2
        if half > 1:

            @pl.when(position == shards - 2)
            def _():
                pass_early()

        for copy in fetch_up(place):
            copy.wait()
        for which in range(shards):

            @pl.when(place == which)
            def _(which=which):
                wait_down(which)

        up, down = up_all[place], down_all[place]
        rows = rows_all[...].reshape(count, model_width)
        pieces = [slice(start, start + 256) for start in range(0, count, 256)]

        def products_of(piece):
            return matmul(rows[piece], up), contract_last(slot_grad[piece, :], down)

        raw = products_of(pieces[0])
        active_low, grad_low = [], []
        for number, piece in enumerate(pieces):
            hidden, grad_active = raw
            if number + 1 < len(pieces):
                raw = products_of(pieces[number + 1])
            activated, slope = gelu_parts(hidden)
            active_low.append(activated.astype(BF16))
            grad_low.append((grad_active * slope).astype(BF16))
            total[piece, :] += matmul(active_low[number], down)
            grad_total[piece, :] += contract_last(grad_low[number], up)
        active_low = jnp.concatenate(active_low, axis=0)
        grad_low = jnp.concatenate(grad_low, axis=0)

        @pl.when(position >= 2)
        def _():
            wait_store(place_at(position - 2), slot)

        grad_up[slot] = matmul(rows_t[...], grad_low).astype(BF16)
        grad_down[slot] = matmul(slot_t[...], active_low).T.astype(BF16)
        start_store(place, slot)
        return carry

    def group(number, carry):
        turns = [number * together + more for more in range(together)]
        if together == 2:
            place_of_group = flipped(grid.z // 2, number, z_size // 2)
        else:
            place_of_group = source_z(number)
        members = pl.ds(place_of_group * together * y_size, together * y_size)
        span = pl.ds(pl.multiple_of(place_of_group * group_rows, 16), group_rows)
        rows = rows_all[members].reshape(group_rows, model_width)
        gate = gate_column[span, :]
        grad = jnp.zeros((group_rows, model_width), F32)
        products = jnp.zeros((group_rows, 128), F32)
        ahead = matmul(rows, up_all[0])
        for place in range(shards):
            hidden = ahead
            if place + 1 < shards:
                ahead = matmul(rows, up_all[place + 1])
            base = unscaled[place, span, :].astype(F32)
            activated, slope = gelu_parts(hidden)
            products = products + folded(activated * base)
            active_low = activated.astype(BF16)
            active[place, span, :] = active_low
            low = (gate * base * slope).astype(BF16)
            grad_hidden[place, span, :] = low
            grad = grad + contract_last(low, up_all[place])
            total[span, :] += matmul(active_low, down_all[place])
        grad_rows[members] = grad.astype(BF16).reshape(together * y_size, capacity, model_width)
        for hop in range(together * y_size):
            gate_rows(
                products[hop * capacity : (hop + 1) * capacity],
                place_of_group * together * y_size + hop,
            )
        for turn in turns:
            for hop in range(y_size):

                @pl.when(turn + hop > 0)
                def _(turn=turn, hop=hop):
                    for going, _ in give_back(turn, hop):
                        going.start()

        return carry

    def column(position, carry):
        place, slot = place_at(position), position % 2
        if half > 1:

            @pl.when(position == shards - 1)
            def _():
                pass_early()

        @pl.when(position >= 2)
        def _():
            wait_store(place_at(position - 2), slot)

        grad_up[slot] = matmul(rows_t[...], grad_hidden[place]).astype(BF16)
        grad_down[slot] = matmul(slot_t[...], active[place]).T.astype(BF16)
        start_store(place, slot)
        return carry

    for copy in loads[1:]:
        copy.wait()
    total[...] = jnp.zeros_like(total)
    slot_rows()
    if last:
        for place in range(shards):
            wait_down(place)
            unscaled[place] = contract_last(
                cot[...].reshape(count, model_width), down_all[place]
            ).astype(BF16)
        loads[0].wait()
        for place in range(shards):
            for copy in fetch_up(place):
                copy.wait()
        wait_crossed()
        lax.fori_loop(0, z_size // together, group, 0)
        for copy in own_back:
            copy.start()
        rows_t[...] = turned(rows_all[...].reshape(count, model_width)).astype(BF16)
        lax.fori_loop(0, shards, column, 0)
    else:
        loads[0].wait()
        rows_t[...] = turned(rows_all[...].reshape(count, model_width)).astype(BF16)
        grad_total[...] = jnp.zeros_like(grad_total)
        wait_crossed()
        lax.fori_loop(0, shards, fused, 0)
        grad_rows[...] = grad_total[...].astype(BF16).reshape(grad_rows.shape)
        for block in range(blocks):
            rows = total[block * capacity : (block + 1) * capacity, :].astype(BF16).astype(F32)
            gate_rows(folded(rows * cot[block].astype(F32)), block)

    rows_out = refs.rows_out[0]
    cot[...] = total[...].astype(BF16).reshape(blocks, capacity, model_width)
    out_copies = [pltpu.make_async_copy(cot, rows_out.at[:, index], load_sem.at[0])]
    for before in refs.outs_before:
        out_copies.append(
            pltpu.make_async_copy(before, rows_out.at[:, pl.ds(0, index)], load_sem.at[1])
        )
    for copy in out_copies:
        copy.start()
    for position in range(max(shards - 2, 0), shards):
        wait_store(place_at(position), position % 2)
    for place in range(shards):
        for copy in give_stores(place, 0):
            copy.wait_recv()
    down_give(0, 0).wait_recv()
    if half > 1:
        keep_up[1][...] = (keep_up[1][...].astype(F32) + taken_up[1][...].astype(F32)).astype(BF16)
        for source, target, number in (
            (keep_up[1], refs.pass_up[0], 0),
            (keep_down[1].at[:, pl.ds(early_rows, part - early_rows), :], refs.pass_down[0], 1),
        ):
            out_copies.append(pltpu.make_async_copy(source, target, pass_sem.at[number]))
            out_copies[-1].start()
    for copy in out_copies:
        copy.wait()
    for going, coming in early:
        coming.wait_recv()
        going.wait_send()
    for going, coming in cross_next:
        coming.wait_recv()
        going.wait_send()
    for going, _ in list(cross_down.values()) + cross_up:
        going.wait_send()
    work.finish()
    if last:
        for turn, hop in steps[1:]:
            for going, coming in give_back(turn, hop):
                coming.wait_recv()
                going.wait_send()
        for copy in own_back:
            copy.wait()


class Bag:
    def __init__(self, layout, refs):
        start = 0
        for name, size in layout.items():
            setattr(self, name, refs[start : start + size])
            start += size


class Wanted:
    def groups(self):
        return list(self.__dict__.values())

    def layout(self):
        return {name: len(group) for name, group in self.__dict__.items()}


def run_expert(index, local, rows_in, gates, cotangent, cotangent_late, ups, downs, swapped, next_mine,
               moved, outs_before, collective_id):
    grid = Grid()
    half = len(ups)
    shards = 2 * half
    last = index == local - 1
    blocks, capacity, model_width = rows_in.shape
    part = downs[0].shape[0]
    count = blocks * capacity
    inputs, outputs, scratch = Wanted(), Wanted(), Wanted()
    inputs.cot_in = [(cotangent, ANYWHERE)]
    inputs.cot_late = [(array, ANYWHERE) for array in cotangent_late]
    inputs.rows_in = [(rows_in, ANYWHERE)]
    inputs.gates = [(gates, IN_VMEM)]
    inputs.my_up = [(array, ANYWHERE) for array in ups]
    inputs.my_down = [(array, ANYWHERE) for array in downs]
    inputs.swapped_up = [(array, ANYWHERE) for array in swapped[0]]
    inputs.swapped_down = [(array, ANYWHERE) for array in swapped[1]]
    inputs.next_mine = [(array, ANYWHERE) for array in next_mine]
    inputs.moved_from = [(array, ANYWHERE) for array, _ in moved]
    inputs.outs_before = [] if outs_before is None else [(outs_before, IN_VMEM)]

    up_shape, down_shape = (model_width, part), (part, model_width)
    outputs.rows_out = [(shape_of((blocks, index + 1, capacity, model_width), BF16), ANYWHERE)]
    own_up, own_down = shape_of(up_shape, BF16), shape_of(down_shape, BF16)
    outputs.own = [(own_up, ANYWHERE), (own_up, ANYWHERE), (own_down, ANYWHERE), (own_down, ANYWHERE)]
    outputs.pass_up = [(shape_of((half - 1,) + up_shape, BF16), ANYWHERE)] if half > 1 else []
    late_down = (half - 1, part - part // 2, model_width)
    early_down = (half - 1, part // 2, model_width)
    outputs.pass_down = [(shape_of(late_down, BF16), ANYWHERE)] if half > 1 else []
    outputs.early_down = [(shape_of(early_down, BF16), ANYWHERE)] if half > 1 else []
    outputs.next_swapped = [(shape_of(array.shape, BF16), ANYWHERE) for array in next_mine]
    outputs.moved_to = [
        (
            shape_of((grid.exp_size,) + array.shape[(1 if place is None else 2) :], array.dtype),
            ANYWHERE,
        )
        for array, place in moved
    ]
    rows_shape, gate_shape = (blocks, capacity, model_width), (blocks, 8, capacity)
    if last:
        outputs.back_rows = [(shape_of(rows_shape, BF16), ANYWHERE)]
        outputs.back_gates = [(shape_of(gate_shape, F32), ANYWHERE)]
    else:
        outputs.grad_rows = [(shape_of(rows_shape, BF16), IN_VMEM)]
        outputs.grad_gates = [(shape_of(gate_shape, F32), IN_VMEM)]

    sems = lambda *shape: pltpu.SemaphoreType.DMA(shape)
    scratch.rows_all = [pltpu.VMEM(rows_shape, BF16)]
    scratch.cot = [pltpu.VMEM(rows_shape, BF16)]
    scratch.up_all = [pltpu.VMEM((shards,) + up_shape, BF16)]
    scratch.down_all = [pltpu.VMEM((shards,) + down_shape, BF16)]
    scratch.total = [pltpu.VMEM((count, model_width), F32)]
    if last:
        scratch.active = [pltpu.VMEM((shards, count, part), BF16)]
        scratch.grad_hidden = [pltpu.VMEM((shards, count, part), BF16)]
        scratch.unscaled = [pltpu.VMEM((shards, count, part), BF16)]
    else:
        scratch.grad_total = [pltpu.VMEM((count, model_width), F32)]
        scratch.slot_grad = [pltpu.VMEM((count, model_width), BF16)]
    if last:
        scratch.grad_rows = [pltpu.VMEM(rows_shape, BF16)]
        scratch.grad_gates = [pltpu.VMEM(gate_shape, F32)]
        scratch.back_send = [sems(2, grid.z_size, grid.y_size)]
        scratch.back_receive = [sems(2, grid.z_size, grid.y_size)]
    scratch.gate_column = [pltpu.VMEM((count, 1), F32)]
    scratch.rows_t = [pltpu.VMEM((model_width, count), BF16)]
    scratch.slot_t = [pltpu.VMEM((model_width, count), BF16)]
    scratch.grad_up = [pltpu.VMEM((2,) + up_shape, BF16)]
    scratch.grad_down = [pltpu.VMEM((2,) + down_shape, BF16)]
    far_up = [pltpu.VMEM((half - 1,) + up_shape, BF16)] * (1 if half > 1 else 0)
    far_down = [pltpu.VMEM((half - 1,) + down_shape, BF16)] * (1 if half > 1 else 0)
    scratch.far_keep_up, scratch.far_taken_up = far_up, far_up
    scratch.far_keep_down, scratch.far_taken_down = far_down, far_down
    scratch.load_sem = [sems(5)]
    scratch.pass_sem = [sems(2)]
    scratch.fetch_sem = [sems(2 * shards, shards)]
    scratch.store_sem = [sems(2, half + 1)]
    scratch.store_there = [sems(2, half + 1)]
    scratch.stored_here = [sems(shards, half + 1)]
    copies = len(moved) * grid.exp_size + half * (shards + 2) + len(next_mine)
    scratch.send = [sems(copies)]
    scratch.receive = [sems(copies)]
    scratch.own_sem = [sems(max(len(moved), 1))]

    layout = {**inputs.layout(), **outputs.layout(), **scratch.layout()}

    def body(*refs):
        expert_kernel(
            *refs, layout=layout, index=index, local=local, half=half, capacity=capacity,
            parts=[place for _, place in moved],
        )

    results = pl.pallas_call(
        body,
        in_specs=[spec for group in inputs.groups() for _, spec in group],
        out_specs=tuple(spec for group in outputs.groups() for _, spec in group),
        out_shape=tuple(shape for group in outputs.groups() for shape, _ in group),
        scratch_shapes=[item for group in scratch.groups() for item in group],
        compiler_params=params(collective_id=collective_id, has_side_effects=True),
        cost_estimate=hint(45),
        name=f"expert_{index}",
    )(*[array for group in inputs.groups() for array, _ in group])
    return Bag(outputs.layout(), results)


def local_picks(routes, slots, capacity, local, index, slot_count):
    member, which = lax.div(routes, local), lax.rem(routes, local)
    places = jnp.where(which == index, member * capacity + slots, -1)
    lane = lax.broadcasted_iota(jnp.int32, (routes.shape[0], slot_count), 1)
    return [lane == places[:, k : k + 1] for k in range(2)]


def unroute_kernel(
    hidden, cotangent, routed, probabilities, gates, plane, columns, counts, attention_out, context,
    *refs, experts, local, token_total, lanes, heads, width,
):
    grads, gate_grads = refs[:local], refs[local : 2 * local]
    (
        grad_hidden, small, grad_t, grad_n, grad_out, branches, own_out, total, send, receive, own_sem,
    ) = refs[2 * local :]
    grid = Grid().here()
    links = Links(send, receive)
    rows, model_width = hidden.shape
    members, capacity = grads[0].shape[0], grads[0].shape[1]
    head_rows = heads * width
    fetch = pltpu.make_async_copy(
        attention_out.at[pl.ds(pl.multiple_of(grid.fsdp * head_rows, 16), head_rows), :], own_out,
        own_sem.at[0],
    )
    fetch.start()
    greet(chip_peers(grid))
    extra = plane[:, lanes.base :]
    gains = extra.astype(F32).T[lanes.gain : lanes.gain + 1]
    half_rows = rows // 2
    sibling = grid.sibling(grid.fsdp)
    small_t = jnp.zeros((lanes.extra, model_width), F32)
    gain_grad = jnp.zeros((1, model_width), F32)
    along_x, across = [], []
    for half in range(2):
        here = slice(half * half_rows, (half + 1) * half_rows)
        grad_output = cotangent[here, :].astype(F32)
        routes = columns[here, 0:2].astype(jnp.int32)
        slots = columns[here, 2:4].astype(jnp.int32)
        member, which = lax.div(routes, local), lax.rem(routes, local)
        lane = lax.broadcasted_iota(jnp.int32, (half_rows, capacity), 1)
        grad_routed = jnp.zeros((half_rows, model_width), F32)
        found = [jnp.zeros((half_rows, capacity), F32), jnp.zeros((half_rows, capacity), F32)]
        for index in range(local):
            picks = local_picks(routes, slots, capacity, local, index, members * capacity)
            grad_routed = grad_routed + matmul(
                jnp.where(picks[0] | picks[1], 1.0, 0.0).astype(BF16),
                grads[index][...].reshape(members * capacity, model_width),
            )
            for place in range(members):
                spots = jnp.where((which == index) & (member == place), slots, -1)
                for k in range(2):
                    found[k] = found[k] + jnp.where(
                        lane == spots[:, k : k + 1], gate_grads[index][place, 0:1, :], 0.0
                    )
        grad_gates = [jnp.sum(found[k], axis=1, keepdims=True) for k in range(2)]
        powers = probabilities[here, :]
        lane = expert_lane(powers.shape, lanes)
        inside = (lane >= 0) & (lane < experts)
        picked = [lane == routes[:, k : k + 1] for k in range(2)]
        chosen_total = sum(
            jnp.sum(jnp.where(picked[k], powers, 0.0), axis=1, keepdims=True) for k in range(2)
        )
        weighted = grad_gates[0] * gates[here, 0:1] + grad_gates[1] * gates[here, 1:2]
        grad_mass = (AUX_WEIGHT * experts / (2.0 * token_total * token_total)) * counts[0:1, :]
        grad_mass = jnp.where(inside, grad_mass, 0.0)
        for k in range(2):
            grad_mass = grad_mass + jnp.where(
                picked[k], (grad_gates[k] - weighted) / chosen_total, 0.0
            )
        grad_logits = powers * (grad_mass - jnp.sum(powers * grad_mass, axis=1, keepdims=True))
        grad_routed = grad_routed + contract_last(grad_logits.astype(BF16), extra)
        hidden_state = hidden[here, :]
        scale = lax.rsqrt(jnp.mean(hidden_state * hidden_state, axis=1, keepdims=True) + EPSILON)
        normed = hidden_state * scale
        product = grad_routed * normed
        grad = scale * (
            grad_routed * gains - normed * jnp.mean(product * gains, axis=1, keepdims=True)
        ) + grad_output
        grad_hidden[here, :] = grad
        branches[grid.fsdp, here, :] = grad.astype(BF16)
        mine = branches.at[grid.fsdp, here, :]
        for hop in range(1, grid.x_size):
            along_x.append(
                links.copy(
                    mine, mine, (grid.exp, grid.x_from(hop)),
                    branches.at[grid.x_from(-hop), here, :],
                )
            )
            along_x[-1][0].start()
        across.append(
            links.copy(mine, mine, (grid.exp, sibling), branches.at[sibling, here, :])
        )
        across[-1][0].start()
        gain_grad = gain_grad + jnp.sum(product, axis=0, keepdims=True)
        small_t = small_t + matmul(grad_logits.T.astype(BF16), routed[here, :])

    def context_grad(place):
        branch = branches[place]
        grad = contract_last(own_out[...], branch).astype(BF16)
        columns_here = pl.ds(pl.multiple_of(place * rows, 128), rows)
        rows_here = pl.ds(pl.multiple_of(place * rows, 16), rows)
        for head in range(heads):
            piece = grad[head * width : (head + 1) * width]
            grad_t[head, :, columns_here] = piece
            grad_n[head, rows_here, :] = turned(piece).astype(BF16)
        total[...] += matmul(context[place], branch)

    total[...] = jnp.zeros_like(total)
    fetch.wait()
    context_grad(grid.fsdp)
    forwards = []
    for half in range(2):
        here = slice(half * half_rows, (half + 1) * half_rows)
        for hop in range(1, grid.x_size):
            along_x[half * (grid.x_size - 1) + hop - 1][1].wait_recv()
            held = grid.x_from(-hop)
            forwards.append(
                links.copy(
                    branches.at[held, here, :], branches.at[held, here, :], (grid.exp, sibling),
                    branches.at[grid.sibling(held), here, :],
                )
            )
            forwards[-1][0].start()
    row = lax.broadcasted_iota(jnp.int32, small_t.shape, 0)
    small[...] = jnp.where(row == lanes.gain, gain_grad, small_t).T
    for _, coming in across:
        coming.wait_recv()
    context_grad(sibling)
    for hop in range(1, grid.x_size):
        context_grad(grid.x_from(-hop))
    for _, coming in forwards:
        coming.wait_recv()
    for hop in range(1, grid.x_size):
        context_grad(grid.sibling(grid.x_from(-hop)))
    grad_out[...] = total[...].astype(BF16)
    for going, _ in along_x + across + forwards:
        going.wait_send()


def project_back_kernel(
    grad_projected, normed, plane, small, probabilities, grad_bias, grad_first, grad_plane, total,
    bias_t, *, lanes, heads, feature_rows, bucket_rows,
):
    step = pl.program_id(0)

    @pl.when(step == 0)
    def _():
        total[...] = jnp.zeros_like(total)

    grad = grad_projected[...]
    grad_first[0] = matmul(plane[:, : lanes.weights], grad).astype(BF16)
    total[: lanes.weights, :] += matmul(grad, normed[...])

    @pl.when(step == pl.num_programs(0) - 1)
    def _():
        grad_plane[...] = total[...].T.astype(BF16)
        span = grad_bias.shape[2]
        select, _ = bucket_rows_select(plane.shape[0], feature_rows, bucket_rows, span)
        bias_t[...] = jnp.zeros_like(bias_t)
        first = lanes.table + lax.axis_index("fsdp") * heads
        for head in range(heads):
            bias_t[pl.ds(first + head, 1), :] = grad_bias[head]
        high = bias_t[...].astype(BF16)
        rest = (bias_t[...] - high.astype(F32)).astype(BF16)
        table = contract_last(select, high) + contract_last(select, rest)
        mass = jnp.sum(probabilities[...], axis=0, keepdims=True)
        mass = pltpu.roll(jnp.broadcast_to(mass, (8, lanes.extra)), lanes.shift, 1)[0:1]
        lane = lax.broadcasted_iota(jnp.int32, table.shape, 1)
        row = lax.broadcasted_iota(jnp.int32, table.shape, 0)
        is_small = (lane >= lanes.router) & (lane < lanes.table)
        is_mass = (lane >= lanes.count) & (lax.rem(row, feature_rows) == 0)
        extra = table + jnp.where(is_small, small[...], 0.0) + jnp.where(is_mass, mass, 0.0)
        grad_plane[:, lanes.base :] = (total[lanes.base :, :].T + extra).astype(BF16)


def last_kernel(
    first, planes, out_grad, first_parts, plane_parts, out_parts,
    first_in, first_sum, planes_in, plane_sum, along_in, reduced, send, receive, own, *, spread_out,
):
    grid = Grid().here()
    links = Links(send, receive)
    z_size, y_size, x_size, fsdp_size = grid.z_size, grid.y_size, grid.x_size, grid.fsdp_size
    exp_size = grid.exp_size
    sibling = grid.sibling(grid.fsdp)
    near = [
        (grid.exp, (grid.fsdp + turn) % fsdp_size) for turn in range(1, fsdp_size)
    ] + [grid.at(z=(grid.z + hop) % z_size) for hop in range(1, z_size)]
    beside = [grid.at(y=(grid.y + hop) % y_size) for hop in range(1, y_size)]

    per_sender = grid.device_count if spread_out else exp_size
    base = 0 if spread_out else grid.fsdp * exp_size
    out_sends = []
    for number in range(per_sender):
        to = base + number
        out_sends.append((to, number))
    if spread_out:
        out_origins = [(origin, origin) for origin in range(grid.device_count)]
    else:
        out_origins = [
            (member * fsdp_size + grid.linear // exp_size, member) for member in range(exp_size)
        ]
    own_slot = grid.linear if spread_out else grid.exp
    out_base = links.used
    links.used += per_sender

    def place_of(linear):
        return (linear // fsdp_size, linear % fsdp_size)

    def out_copy(to, number, slot):
        return pltpu.make_async_remote_copy(
            src_ref=out_grad.at[number], dst_ref=out_parts.at[slot],
            send_sem=send.at[out_base + number], recv_sem=receive.at[out_base + slot],
            device_id=place_of(to), device_id_type=MESH,
        )

    barrier = pltpu.get_barrier_semaphore()
    for device in near + beside:
        pl.semaphore_signal(barrier, inc=1, device_id=device, device_id_type=MESH)
    for origin, _ in out_origins:

        @pl.when(origin != grid.linear)
        def _(origin=origin):
            pl.semaphore_signal(
                barrier, inc=1, device_id=place_of(origin), device_id_type=MESH
            )

    to_self = (
        1 if spread_out else jnp.where(grid.linear // exp_size == grid.fsdp, 1, 0)
    )
    pl.semaphore_wait(barrier, len(near) + len(beside) + per_sender - to_self)

    first_copies = []
    for hop in range(x_size):
        mine = grid.x_from(hop)
        first_copies.append(
            links.copy(
                first.at[grid.sibling(mine)], first_in.at[hop], (grid.exp, sibling), first_in.at[hop]
            )
        )
        first_copies[-1][0].start()
    z_hops = list(range(1, z_size)) + [0]
    beside_copies = []
    for z_hop in z_hops:
        beside_copies.append([])
        for hop in range(1, y_size):
            to = (grid.y + hop) % y_size
            landing = planes_in.at[hop - 1, z_hop]
            beside_copies[-1].append(
                links.copy(
                    planes.at[(grid.z + z_hop) % z_size, to], landing, grid.at(y=to), landing
                )
            )
            beside_copies[-1][-1][0].start()
    along_x = []
    for hop in range(x_size):
        first_copies[hop][1].wait_recv()
        summed = first[grid.x_from(hop)].astype(F32) + first_in[hop].astype(F32)
        if hop == 0:
            first_parts[0] = summed.astype(BF16)
        else:
            first_sum[hop - 1] = summed.astype(BF16)
            along_x.append(
                links.copy(
                    first_sum.at[hop - 1], first_parts.at[hop], (grid.exp, grid.x_from(hop)),
                    first_parts.at[hop],
                )
            )
            along_x[-1][0].start()
    along_z = []
    for z_hop, copies in zip(z_hops, beside_copies):
        to_z = (grid.z + z_hop) % z_size
        summed = planes[to_z, grid.y].astype(F32)
        for number, (_, coming) in enumerate(copies):
            coming.wait_recv()
            summed = summed + planes_in[number, z_hop].astype(F32)
        plane_sum[z_hop] = summed.astype(BF16)
        if z_hop > 0:
            along_z.append(
                links.copy(
                    plane_sum.at[z_hop], along_in.at[z_hop - 1], grid.at(z=to_z),
                    along_in.at[z_hop - 1],
                )
            )
            along_z[-1][0].start()
    for to, number in out_sends:

        @pl.when(to != grid.linear)
        def _(to=to, number=number):
            out_copy(to, number, own_slot).start()

        @pl.when(to == grid.linear)
        def _(number=number):
            pltpu.make_async_copy(out_grad.at[number], out_parts.at[own_slot], own.at[0]).start()

    summed = plane_sum[0].astype(F32)
    for number, (_, coming) in enumerate(along_z):
        coming.wait_recv()
        summed = summed + along_in[number].astype(F32)
    reduced[...] = summed.astype(BF16)
    placed = []
    for turn in range(1, fsdp_size):
        to = (grid.fsdp + turn) % fsdp_size
        origin = (grid.fsdp + fsdp_size - turn) % fsdp_size
        placed.append(
            links.copy(
                reduced.at[to], plane_parts.at[grid.fsdp], (grid.exp, to), plane_parts.at[origin]
            )
        )
        placed[-1][0].start()
    kept = pltpu.make_async_copy(reduced.at[grid.fsdp], plane_parts.at[grid.fsdp], own.at[1])
    kept.start()
    for going, coming in along_x + placed:
        coming.wait_recv()
    for going, _ in first_copies + along_x + along_z + placed:
        going.wait_send()
    for copies in beside_copies:
        for going, _ in copies:
            going.wait_send()
    kept.wait()
    for origin, slot in out_origins:

        @pl.when(origin != grid.linear)
        def _(origin=origin, slot=slot):
            out_copy(origin, 0, slot).wait_recv()

    for to, number in out_sends:

        @pl.when(to != grid.linear)
        def _(to=to, number=number):
            out_copy(to, number, own_slot).wait_send()

        @pl.when(to == grid.linear)
        def _(number=number):
            pltpu.make_async_copy(out_grad.at[number], out_parts.at[own_slot], own.at[0]).wait()


def mixture_kernel(hidden, gates, columns, rows_in, output, *, local):
    members, _, capacity, model_width = rows_in.shape
    routes, slots = int_columns(columns)
    total = hidden[...]
    picked = [jnp.zeros(hidden.shape, F32), jnp.zeros(hidden.shape, F32)]
    for index in range(local):
        picks = local_picks(routes, slots, capacity, local, index, members * capacity)
        values = rows_in[:, index].reshape(members * capacity, model_width)
        for k in range(2):
            picked[k] = picked[k] + matmul(jnp.where(picks[k], 1.0, 0.0).astype(BF16), values)
    for k in range(2):
        total = total + gates[:, k : k + 1] * picked[k]
    output[...] = total.astype(BF16)


def finish_kernel(
    first_parts, plane_parts, out_parts, tokens, grad_hidden, attention_in, attention_gain, counts,
    grad_tokens, grad_gain, grad_in, grad_out, grad_mixture, grad_router, grad_table, balance,
    *, lanes, heads, width, head_count, experts, token_total,
):
    total = jnp.sum(first_parts[...].astype(F32), axis=0).T
    inputs = tokens[...].astype(F32)
    scale = lax.rsqrt(jnp.mean(inputs * inputs, axis=1, keepdims=True) + EPSILON)
    normed = inputs * scale
    grad_tokens[...] = grad_hidden[...] + scale * (
        total - normed * jnp.mean(total * normed, axis=1, keepdims=True)
    )
    fsdp_size = plane_parts.shape[0]
    model_width = head_count * width
    sums = [plane_parts[place].astype(F32) for place in range(fsdp_size)]
    columns = []
    for kind in range(3):
        pieces = [
            sums[place][:, kind * heads * width : (kind + 1) * heads * width]
            for place in range(fsdp_size)
        ]
        columns.append(jnp.concatenate(pieces, axis=1)[:, :model_width])
    gathered = jnp.concatenate(columns, axis=1)
    feature_rows = gathered.shape[0]
    gain = jnp.sum(gathered * attention_in[...].astype(F32), axis=1, keepdims=True)
    gain = padded_rows(jnp.broadcast_to(gain, (feature_rows, 128)), 128).T
    grad_gain[...] = gain[0:1, :feature_rows]
    grad_in[...] = gathered * as_column(attention_gain[...], feature_rows)
    grad_out[...] = jnp.sum(out_parts[...].astype(F32), axis=0)
    extra = sum(part[:, lanes.base :] for part in sums)
    extra_t = padded_rows(extra, 128).T
    grad_mixture[...] = extra_t[lanes.gain : lanes.gain + 1, :feature_rows]
    grad_router[...] = extra_t[lanes.router : lanes.router + experts, :feature_rows]
    grad_table[...] = extra[: grad_table.shape[0], lanes.table : lanes.table + head_count]
    mass = jnp.broadcast_to(extra[0:1], (8, lanes.extra))
    mass = pltpu.roll(mass, lanes.extra - lanes.shift, 1)
    lane = expert_lane(mass.shape, lanes)
    terms = jnp.where((lane >= 0) & (lane < experts), mass * counts[...], 0.0)[0:1]
    balance[...] = jnp.sum(terms, axis=1, keepdims=True) * (
        experts / (2.0 * token_total * token_total)
    )


def sum_kernel(*refs, layout, local):
    outputs = refs[len(layout) :]
    early_blocks = pl.num_programs(0) // 2
    totals = {}
    number = 0
    while number < len(layout):
        index, which, halves = layout[number]
        shape = outputs[which].shape[1:]
        value = refs[number][...].reshape(shape).astype(F32)
        if halves:
            rest = refs[number + 1][...].reshape(shape).astype(F32)
            value = jnp.where(pl.program_id(0) < early_blocks, value, rest)
            number += 1
        totals[index, which] = totals[index, which] + value if (index, which) in totals else value
        number += 1
    for (index, which), total in totals.items():
        outputs[which][index] = total


def sum_grads(groups, up_shape, down_shape, blocks):
    local = len(groups)
    depth, part = up_shape[1], down_shape[1]
    sizes = ((depth, part), (part // blocks, down_shape[2]))
    arrays, specs, layout = [], [], []
    early = blocks // 2
    for index, group in enumerate(groups):
        for which, (size, (keep, taken, passed)) in enumerate(zip(sizes, group)):
            for array in (keep, taken, *passed):
                if isinstance(array, tuple):
                    arrays.extend(array)
                    specs.append(pl.BlockSpec(size, lambda c: (jnp.minimum(c, early - 1), 0)))
                    specs.append(pl.BlockSpec(size, lambda c: (jnp.maximum(c - early, 0), 0)))
                    layout.extend([(index, which, True)] * 2)
                else:
                    arrays.append(array)
                    specs.append(pl.BlockSpec(size, lambda c: (c, 0)))
                    layout.append((index, which, False))
    return pl.pallas_call(
        partial(sum_kernel, layout=layout, local=local),
        grid=(blocks,),
        in_specs=specs,
        out_specs=[
            pl.BlockSpec((local, depth, part), lambda c: (0, 0, c)),
            pl.BlockSpec((local, part // blocks, down_shape[2]), lambda c: (0, c, 0)),
        ],
        out_shape=(shape_of(up_shape, F32), shape_of(down_shape, F32)),
        compiler_params=params(),
        cost_estimate=hint(8),
        name="sum_grads",
    )(*arrays)


def over_x(array, hop):
    fsdp_size = lax.axis_size("fsdp")
    return lax.ppermute(array, "fsdp", [(i, (i + 2 * hop) % fsdp_size) for i in range(fsdp_size)])


def over_core(array):
    return lax.ppermute(array, "fsdp", [(i, i ^ 1) for i in range(lax.axis_size("fsdp"))])


def on_device(
    tokens,
    cotangent,
    segments,
    routes,
    slots,
    attention_gain,
    mixture_gain,
    attention_in,
    attention_out,
    router_weight,
    position_table,
    expert_up,
    expert_down,
):
    grid = Grid()
    exp_size, fsdp_size, chips = grid.exp_size, grid.fsdp_size, grid.x_size
    device_count = grid.device_count
    fsdp_index = lax.axis_index("fsdp")
    rows, model_width = tokens.shape
    length = rows * fsdp_size
    head_count = position_table.shape[1]
    width = model_width // head_count
    heads = -(-head_count // fsdp_size)
    padded_heads = heads * fsdp_size
    feature_rows, bucket_rows = attention_in.shape[0], position_table.shape[0]
    experts = router_weight.shape[1]
    local = expert_up.shape[0]
    capacity = 4 * rows // experts
    token_total = rows * device_count
    span = WINDOW + 2 * SKEW + QUERY_BLOCK
    lanes = Lanes(heads, width, padded_heads, experts)
    part = expert_down.shape[1]
    gain_row = attention_gain.reshape(1, feature_rows)
    late_rows = 2 * capacity // 3 if local > 1 and capacity % 48 == 0 else 0
    late = 1 if late_rows else 0

    shard_shapes = [shape_of((model_width, part), BF16), shape_of((part, model_width), BF16)]
    copies = (
        4 * fsdp_size + grid.z_size + grid.z_size * grid.y_size
        + grid.z_size + grid.y_size + grid.x_size + 1
    )
    started = pl.pallas_call(
        partial(
            start_kernel, lanes=lanes, heads=heads, width=width, head_count=head_count,
            experts=experts, capacity=capacity, local=local, late=late,
        ),
        out_shape=tuple(
            [
                shape_of((fsdp_size, rows, model_width), BF16),
                shape_of((grid.z_size, grid.y_size, fsdp_size, feature_rows, lanes.width), BF16),
                shape_of((exp_size, local * capacity - late_rows, model_width), BF16),
                shape_of((8, rows), F32),
                shape_of((rows, 128), F32),
                shape_of((grid.z_size, grid.y_size, chips, 2, feature_rows, model_width), BF16),
            ]
            + [shape_of((exp_size, late_rows, model_width), BF16)] * late
            + shard_shapes * local
        ),
        in_specs=[IN_VMEM] * 10 + [ANYWHERE] * 2,
        out_specs=tuple(
            [ANYWHERE, ANYWHERE, IN_VMEM, IN_VMEM, IN_VMEM, ANYWHERE]
            + [IN_VMEM] * late
            + [ANYWHERE] * (2 * local)
        ),
        scratch_shapes=[
            pltpu.VMEM((fsdp_size, feature_rows, lanes.width), BF16),
            pltpu.VMEM(expert_up.shape, BF16),
            pltpu.VMEM(expert_down.shape, BF16),
            dma_sems(copies),
            dma_sems(copies),
            dma_sems(3),
            dma_sems(2 * local),
            dma_sems(local * (fsdp_size + 1)),
        ],
        compiler_params=params(collective_id=0, has_side_effects=True),
        cost_estimate=hint(20),
        name="start",
    )(
        tokens, cotangent, routes.T, slots.T, gain_row, mixture_gain.reshape(1, feature_rows),
        attention_in, router_weight.T, position_table, attention_out, expert_up, expert_down,
    )
    all_tokens, all_planes, cotangent_early, position_rows, columns, full_out = started[:6]
    cotangent_late, started = started[6 : 6 + late], started[6 + late :]
    own_shards = [started[2 * index : 2 * index + 2] for index in range(local)]
    plane = all_planes.reshape(model_width, lanes.width)
    full_out = full_out.reshape(model_width, model_width)

    def along_x(array):
        return [over_x(array, -hop) for hop in range(1, chips)]

    near_up, near_down = [None] * local, [None] * local
    near_up[0] = along_x(own_shards[0][0])
    cotangent_in = lax.all_to_all(
        cotangent_early, "exp", split_axis=0, concat_axis=0, tiled=True
    )

    head_t = lambda size: pl.BlockSpec((heads, size, rows), lambda s, *_: (0, 0, s))
    head_n = lambda size: pl.BlockSpec((heads, rows, size), lambda s, *_: (0, s, 0))
    normed, query_t, key_n, query_n, value_n, key_t, value_t, bias, counts = pl.pallas_call(
        partial(
            project_kernel, heads=heads, width=width, lanes=lanes, feature_rows=feature_rows,
            bucket_rows=bucket_rows,
        ),
        grid=(fsdp_size,),
        in_specs=[
            pl.BlockSpec((1, rows, model_width), lambda s: (s, 0, 0)),
            whole((model_width, lanes.width)),
            pl.BlockSpec((1, rows), lambda s: (0, s)),
        ],
        out_specs=[
            pl.BlockSpec((rows, model_width), lambda s: (s, 0)),
            head_t(SKEW), head_n(SKEW), head_n(width), head_n(width), head_t(width), head_t(width),
            whole((heads, 1, span)),
            whole((8, lanes.extra)),
        ],
        out_shape=(
            shape_of((length, model_width), BF16),
            shape_of((heads, SKEW, length), BF16),
            shape_of((heads, length, SKEW), BF16),
            shape_of((heads, length, width), BF16),
            shape_of((heads, length, width), BF16),
            shape_of((heads, width, length), BF16),
            shape_of((heads, width, length), BF16),
            shape_of((heads, 1, span), F32),
            shape_of((8, lanes.extra), F32),
        ),
        scratch_shapes=[
            pltpu.VMEM((lanes.weights, model_width), BF16),
            pltpu.VMEM((lanes.extra, span), F32),
        ],
        compiler_params=params(),
        cost_estimate=hint(8),
        name="project",
    )(all_tokens, plane, segments.reshape(1, length))

    by_head = lambda *size: pl.BlockSpec((1,) + size, lambda h: (h, 0, 0))
    context, context_high, log_total = pl.pallas_call(
        partial(attend_kernel, rows=rows),
        grid=(heads,),
        in_specs=[
            by_head(SKEW, length), by_head(length, SKEW), by_head(width, length), by_head(1, span),
        ],
        out_specs=[
            pl.BlockSpec((fsdp_size, width, rows), lambda h: (0, h, 0)),
            by_head(width, length),
            by_head(1, length),
        ],
        out_shape=(
            shape_of((fsdp_size, heads * width, rows), BF16),
            shape_of((heads, width, length), F32),
            shape_of((heads, 1, length), F32),
        ),
        scratch_shapes=[
            pltpu.VMEM((SKEW, span), F32),
            pltpu.VMEM((WINDOW + QUERY_BLOCK, QUERY_BLOCK), F32),
        ],
        compiler_params=params(),
        cost_estimate=hint(13),
        name="attend",
    )(query_t, key_n, value_t, bias)

    (attended_t,) = exchange("fsdp", [(context, None)], 1, 9)
    own_down, near_up[0], attended_t = lax.optimization_barrier(
        (own_shards[0][1], near_up[0], attended_t)
    )
    near_down[0] = along_x(own_down)
    attended_t = attended_t.reshape(padded_heads * width, rows)

    gate_lanes = -(-local * capacity // 128) * 128
    hidden, routed, probabilities, gates, outgoing, slot_gates = pl.pallas_call(
        partial(route_kernel, experts=experts, lanes=lanes, capacity=capacity),
        out_shape=(
            shape_of((rows, model_width), F32),
            shape_of((rows, model_width), BF16),
            shape_of((rows, lanes.extra), F32),
            shape_of((rows, 2), F32),
            shape_of((exp_size, local * capacity, model_width), BF16),
            shape_of((exp_size, 8, gate_lanes), F32),
        ),
        compiler_params=params(),
        cost_estimate=hint(7),
        name="route",
    )(tokens, attended_t, full_out, plane, columns, position_rows)

    later = [own_shards[index] for index in range(1, local)]
    outgoing, later = lax.optimization_barrier((outgoing, later))
    for index in range(1, local):
        near_up[index], near_down[index] = [along_x(array) for array in later[index - 1]]
    outgoing = outgoing.reshape(exp_size, local, capacity, model_width)

    def down_parts(early, rest):
        return [(early[0][hop], rest[hop]) for hop in range(chips - 1)]

    def pass_along(arrays):
        return [over_x(arrays[0][hop - 1], hop) for hop in range(1, chips)]

    ready = [own_shards[0][0]] + near_up[0] + [own_shards[0][1]]
    rows_in, gates_in, *crossed = exchange(
        "exp", [(outgoing, 0), (slot_gates, None)], 2, 28, across=ready
    )
    swapped = (crossed[:-1], crossed[-1:])
    returned, groups, moved, outs = [], [], [], None
    late_rows_in = ()
    for index in range(local):
        final = index == local - 1
        carried = list(moved)
        if not final:
            carried.append((outgoing, index + 1))
        if index == 0 and late:
            carried.append((cotangent_late[0], None))
        result = run_expert(
            index, local, rows_in, gates_in, cotangent_in, late_rows_in if final else (),
            [own_shards[index][0]] + near_up[index], [own_shards[index][1]] + near_down[index],
            swapped, () if final else own_shards[index + 1], carried, outs, 3 + index,
        )
        (outs,) = result.rows_out
        arrived = list(result.moved_to)
        if index == 0 and late:
            late_rows_in = (arrived.pop(),)
        if not final:
            rows_in = arrived.pop()
            swapped = (result.next_swapped[:1], result.next_swapped[1:])
            moved = [(result.grad_rows[0], None), (result.grad_gates[0], None)]
        if arrived:
            returned.append(arrived)
        up_keep, up_taken, down_keep, down_taken = result.own
        if not final:
            passed = (result.pass_up, result.pass_down)
            passed, rows_in = lax.optimization_barrier((passed, rows_in))
            groups.append(
                [
                    (up_keep, up_taken, pass_along(passed[0])),
                    (down_keep, down_taken, down_parts(result.early_down, pass_along(passed[1]))),
                ]
            )
    returned.append([result.back_rows[0], result.back_gates[0]])
    groups, returned = lax.optimization_barrier((groups, returned))

    outs, returned = lax.optimization_barrier((outs, returned))
    out_rows = lax.all_to_all(outs, "exp", split_axis=0, concat_axis=0, tiled=True)

    padded_out = full_out
    if padded_heads > head_count:
        padded_out = jnp.pad(full_out, ((0, padded_heads * width - model_width), (0, 0)))
    copies = 2 * 2 * fsdp_size
    grad_hidden, small, grad_t, grad_n, out_grad = pl.pallas_call(
        partial(
            unroute_kernel, experts=experts, local=local, token_total=token_total, lanes=lanes,
            heads=heads, width=width,
        ),
        out_shape=(
            shape_of((rows, model_width), F32),
            shape_of((model_width, lanes.extra), F32),
            shape_of((heads, width, length), BF16),
            shape_of((heads, length, width), BF16),
            shape_of((heads * width, model_width), BF16),
        ),
        in_specs=[IN_VMEM] * 8 + [ANYWHERE] + [IN_VMEM] * (1 + 2 * local),
        out_specs=tuple([IN_VMEM] * 5),
        scratch_shapes=[
            pltpu.VMEM((fsdp_size, rows, model_width), BF16),
            pltpu.VMEM((heads * width, model_width), BF16),
            pltpu.VMEM((heads * width, model_width), F32),
            dma_sems(copies),
            dma_sems(copies),
            dma_sems(1),
        ],
        compiler_params=params(collective_id=4 + local, has_side_effects=True),
        cost_estimate=hint(1),
        name="unroute",
    )(
        hidden, cotangent, routed, probabilities, gates, plane, columns, counts, padded_out, context,
        *[part[0] for part in returned], *[part[1] for part in returned],
    )
    pass_up, grad_t = lax.optimization_barrier((result.pass_up, grad_t))
    groups.append(
        [
            (up_keep, up_taken, pass_along(pass_up)),
            (down_keep, down_taken, down_parts(result.early_down, pass_along(result.pass_down))),
        ]
    )

    grad_projected, grad_bias = pl.pallas_call(
        partial(attend_back_kernel, scale=width ** (-0.5)),
        grid=(heads,),
        in_specs=[
            by_head(SKEW, length), by_head(length, SKEW), by_head(length, width),
            by_head(length, width), by_head(width, length), by_head(width, length),
            by_head(length, width), by_head(width, length), by_head(1, length), by_head(1, span),
        ],
        out_specs=[
            pl.BlockSpec((3, 1, width, length), lambda h: (0, h, 0, 0)),
            by_head(1, span),
        ],
        out_shape=(
            shape_of((3, heads, width, length), BF16),
            shape_of((heads, 1, span), F32),
        ),
        scratch_shapes=[
            pltpu.VMEM((SKEW, span), F32),
            pltpu.VMEM((SKEW, span), F32),
            pltpu.VMEM((length, width), F32),
            pltpu.VMEM((length, width), F32),
        ],
        compiler_params=params(),
        cost_estimate=hint(1),
        name="attend_back",
    )(query_t, key_n, query_n, value_n, key_t, grad_t, grad_n, context_high, log_total, bias)
    grad_projected = grad_projected.reshape(lanes.weights, length)

    grad_first, grad_plane = pl.pallas_call(
        partial(
            project_back_kernel, lanes=lanes, heads=heads, feature_rows=feature_rows,
            bucket_rows=bucket_rows,
        ),
        grid=(fsdp_size,),
        in_specs=[
            pl.BlockSpec((lanes.weights, rows), lambda s: (0, s)),
            pl.BlockSpec((rows, model_width), lambda s: (s, 0)),
            whole((model_width, lanes.width)),
            whole((model_width, lanes.extra)),
            whole((rows, lanes.extra)),
            whole((heads, 1, span)),
        ],
        out_specs=[
            pl.BlockSpec((1, model_width, rows), lambda s: (s, 0, 0)),
            whole((model_width, lanes.width)),
        ],
        out_shape=(
            shape_of((fsdp_size, model_width, rows), BF16),
            shape_of((model_width, lanes.width), BF16),
        ),
        scratch_shapes=[
            pltpu.VMEM((lanes.width, model_width), F32),
            pltpu.VMEM((lanes.extra, span), F32),
        ],
        compiler_params=params(),
        cost_estimate=hint(1),
        name="project_back",
    )(grad_projected, normed, plane, small, probabilities, grad_bias)

    out_rows, grad_first = lax.optimization_barrier((out_rows, grad_first))
    spread_out = heads * width * fsdp_size != model_width
    if spread_out:
        out_grad = lax.dynamic_update_slice(
            jnp.zeros((padded_heads * width, model_width), BF16), out_grad,
            (fsdp_index * heads * width, jnp.int32(0)),
        )[:model_width]
    out_grad = out_grad.reshape(-1, feature_rows, model_width)
    out_count = device_count if spread_out else exp_size
    plane_shape = (grid.z_size, grid.y_size, fsdp_size, feature_rows, lanes.width)
    parts_shape = (fsdp_size, feature_rows, lanes.width)
    copies = 3 * fsdp_size + grid.z_size * grid.y_size + grid.z_size + out_count
    first_parts, plane_parts, out_parts = pl.pallas_call(
        partial(last_kernel, spread_out=spread_out),
        out_shape=(
            shape_of((chips, model_width, rows), BF16),
            shape_of(parts_shape, BF16),
            shape_of((out_count, feature_rows, model_width), BF16),
        ),
        in_specs=[IN_VMEM] * 3,
        out_specs=(IN_VMEM, ANYWHERE, ANYWHERE),
        scratch_shapes=[
            pltpu.VMEM((chips, model_width, rows), BF16),
            pltpu.VMEM((max(chips - 1, 1), model_width, rows), BF16),
            pltpu.VMEM((max(grid.y_size - 1, 1), grid.z_size) + parts_shape, BF16),
            pltpu.VMEM((grid.z_size,) + parts_shape, BF16),
            pltpu.VMEM((max(grid.z_size - 1, 1),) + parts_shape, BF16),
            pltpu.VMEM(parts_shape, BF16),
            dma_sems(copies),
            dma_sems(copies),
            dma_sems(2),
        ],
        compiler_params=params(collective_id=5 + local, has_side_effects=True),
        cost_estimate=hint(1),
        name="last",
    )(grad_first, grad_plane.reshape(plane_shape), out_grad)

    groups, first_parts = lax.optimization_barrier((groups, first_parts))
    (
        grad_tokens, gain_grad, in_grad, out_sum, mixture_gain_grad, router_grad, table_grad, balance,
    ) = pl.pallas_call(
        partial(
            finish_kernel, lanes=lanes, heads=heads, width=width, head_count=head_count,
            experts=experts, token_total=token_total,
        ),
        out_shape=(
            shape_of((rows, model_width), F32),
            shape_of((1, feature_rows), F32),
            shape_of((feature_rows, 3 * model_width), F32),
            shape_of((feature_rows, model_width), F32),
            shape_of((1, feature_rows), F32),
            shape_of((experts, feature_rows), F32),
            shape_of((bucket_rows, head_count), F32),
            shape_of((1, 1), F32),
        ),
        compiler_params=params(),
        cost_estimate=hint(6),
        name="finish",
    )(first_parts, plane_parts, out_parts, tokens, grad_hidden, attention_in, gain_row, counts)

    layer_output = pl.pallas_call(
        partial(mixture_kernel, local=local),
        out_shape=shape_of((rows, model_width), BF16),
        compiler_params=params(),
        cost_estimate=hint(5),
        name="mixture",
    )(hidden, gates, columns, out_rows)

    up_grad, down_grad = sum_grads(groups, expert_up.shape, expert_down.shape, fsdp_size)
    return (
        layer_output,
        balance.reshape(()),
        grad_tokens,
        gain_grad.reshape(feature_rows),
        mixture_gain_grad.reshape(feature_rows),
        in_grad,
        out_sum,
        router_grad.T,
        table_grad,
        up_grad,
        down_grad,
    )


def solution(mesh):
    in_specs = (
        P(("exp", "fsdp"), None),
        P(("exp", "fsdp"), None),
        P("exp"),
        P(("exp", "fsdp"), None),
        P(("exp", "fsdp"), None),
        P(("exp", "fsdp")),
        P(("exp", "fsdp")),
        P(("exp", "fsdp"), None),
        P(("exp", "fsdp"), None),
        P(("exp", "fsdp"), None),
        P(("exp", "fsdp"), None),
        P("exp", "fsdp", None),
        P("exp", "fsdp", None),
    )
    out_specs = (
        P(("exp", "fsdp"), None),
        P(),
        P(("exp", "fsdp"), None),
        P(("exp", "fsdp")),
        P(("exp", "fsdp")),
        P(("exp", "fsdp"), None),
        P(("exp", "fsdp"), None),
        P(("exp", "fsdp"), None),
        P(("exp", "fsdp"), None),
        P("exp", "fsdp", None),
        P("exp", "fsdp", None),
    )
    return jax.shard_map(
        on_device, mesh=mesh, in_specs=in_specs, out_specs=out_specs, check_vma=False
    )
```

```python
from functools import partial

import jax
import jax.numpy as jnp
from jax import lax
from jax.experimental import pallas as pl
from jax.experimental.pallas import tpu as pltpu
from jax.sharding import PartitionSpec as P

WINDOW = 1024
BUCKETS = 256

EPSILON = 1e-06
AUX_WEIGHT = 0.01
MASKED = -1e30
QUERY_BLOCK = 256
SKEW = 128
VMEM_BYTES = 58 * 1024 * 1024
MESH = pl.DeviceIdType.MESH
F32 = jnp.float32
BF16 = jnp.bfloat16


def params(**kwargs):
    return pltpu.CompilerParams(vmem_limit_bytes=VMEM_BYTES, **kwargs)


def shape_of(shape, dtype):
    return jax.ShapeDtypeStruct(shape, dtype)


def whole(shape):
    return pl.BlockSpec(shape, lambda *_: (0,) * len(shape))


def contract_last(left_side, right_side):
    return lax.dot_general(
        left_side, right_side, (((1,), (1,)), ((), ())), preferred_element_type=F32
    )


def matmul(left_side, right_side):
    return jnp.dot(left_side, right_side, preferred_element_type=F32)


def turned(value):
    return value.astype(F32).T


def bucket_index(distance):
    near_count = BUCKETS // 2
    spread = max(WINDOW - near_count, 1)
    far_bucket = (
        near_count + jnp.maximum(distance - near_count, 0) * (BUCKETS - near_count) // spread
    )
    return jnp.where(distance < near_count, distance, far_bucket)

def hint(micros):
    return pl.CostEstimate(flops=int(micros * 1.0e9), bytes_accessed=1024, transcendentals=0)


class Grid:
    def __init__(self):
        self.exp_size, self.fsdp_size = lax.axis_size("exp"), lax.axis_size("fsdp")
        self.device_count = self.exp_size * self.fsdp_size
        self.y_size = max(
            y for y in range(1, self.exp_size + 1) if self.exp_size % y == 0 and 2 * y * y <= self.exp_size
        ) if self.exp_size > 1 else 1
        self.z_size = self.exp_size // self.y_size
        self.x_size = self.fsdp_size // 2

    def here(self):
        self.exp, self.fsdp = lax.axis_index("exp"), lax.axis_index("fsdp")
        self.z, self.y = self.exp // self.y_size, self.exp % self.y_size
        self.x, self.core = self.fsdp // 2, self.fsdp % 2
        self.linear = self.exp * self.fsdp_size + self.fsdp
        return self

    def at(self, z=None, y=None, fsdp=None):
        z = self.z if z is None else z
        y = self.y if y is None else y
        return (z * self.y_size + y, self.fsdp if fsdp is None else fsdp)

    def x_from(self, hop):
        return ((self.x + self.x_size + hop) % self.x_size) * 2 + self.core

    def sibling(self, fsdp):
        return fsdp + 1 - 2 * (fsdp % 2)


class Links:
    def __init__(self, send, receive):
        self.send, self.receive, self.used = send, receive, 0

    def copy(self, source, target, device, landing):
        index = self.used
        self.used += 1
        going = pltpu.make_async_remote_copy(
            src_ref=source, dst_ref=target, send_sem=self.send.at[index],
            recv_sem=self.receive.at[index], device_id=device, device_id_type=MESH,
        )
        coming = pltpu.make_async_remote_copy(
            src_ref=landing, dst_ref=landing, send_sem=self.send.at[index],
            recv_sem=self.receive.at[index], device_id=device, device_id_type=MESH,
        )
        return going, coming


def greet(devices):
    barrier = pltpu.get_barrier_semaphore()
    for device in devices:
        pl.semaphore_signal(barrier, inc=1, device_id=device, device_id_type=MESH)
    pl.semaphore_wait(barrier, len(devices))


def chip_peers(grid):
    peers = [(grid.exp, grid.sibling(grid.fsdp))]
    return peers + [(grid.exp, grid.x_from(hop)) for hop in range(1, grid.x_size)]


class ChipGather:
    def __init__(self, grid, links, own_sem, source, target):
        self.grid, self.links, self.target = grid, links, target
        self.own = pltpu.make_async_copy(source, target.at[grid.fsdp], own_sem)
        sibling = grid.sibling(grid.fsdp)
        self.along_x, self.across = [], []
        for hop in range(1, grid.x_size):
            self.along_x.append(
                links.copy(
                    source, target.at[grid.fsdp], (grid.exp, grid.x_from(hop)),
                    target.at[grid.x_from(-hop)],
                )
            )
        self.across.append(
            links.copy(source, target.at[grid.fsdp], (grid.exp, sibling), target.at[sibling])
        )

    def start(self):
        for going, _ in self.along_x + self.across:
            going.start()
        self.own.start()

    def forward(self):
        grid = self.grid
        for hop in range(1, grid.x_size):
            self.along_x[hop - 1][1].wait_recv()
            held = grid.x_from(-hop)
            other = grid.sibling(held)
            self.across.append(
                self.links.copy(
                    self.target.at[held], self.target.at[held],
                    (grid.exp, grid.sibling(grid.fsdp)), self.target.at[other],
                )
            )
            self.across[-1][0].start()

    def finish(self):
        for _, coming in self.across:
            coming.wait_recv()
        for going, _ in self.along_x + self.across:
            going.wait_send()
        self.own.wait()


class Exchange:
    def __init__(self, grid, axis, links, own_sems, pairs):
        size = grid.exp_size if axis == "exp" else grid.fsdp_size
        place = grid.exp if axis == "exp" else grid.fsdp
        device = (lambda to: (to, grid.fsdp)) if axis == "exp" else (lambda to: (grid.exp, to))
        self.peers = [device((place + hop) % size) for hop in range(1, size)]
        self.copies, self.own = [], []
        for index, (source, target) in enumerate(pairs):
            for hop in range(1, size):
                to, origin = (place + hop) % size, (place + size - hop) % size
                self.copies.append(
                    links.copy(source(to), target.at[place], device(to), target.at[origin])
                )
            self.own.append(
                pltpu.make_async_copy(source(place), target.at[place], own_sems.at[index])
            )

    def start(self):
        for going, _ in self.copies:
            going.start()
        for own in self.own:
            own.start()

    def finish(self):
        for going, coming in self.copies:
            coming.wait_recv()
            going.wait_send()
        for own in self.own:
            own.wait()


ANYWHERE = pl.BlockSpec(memory_space=pl.ANY)
IN_VMEM = pl.BlockSpec(memory_space=pltpu.VMEM)


def dma_sems(count):
    return pltpu.SemaphoreType.DMA((count,))


def plane_of(source, part, to):
    return source.at[to] if part is None else source.at[to, part]


class Lanes:
    def __init__(self, heads, width, padded_heads, experts):
        self.weights = 3 * heads * width
        self.base = self.weights // 128 * 128
        self.router = self.weights - self.base
        self.gain = self.router + experts
        self.table = self.gain + 1
        self.count = self.table + padded_heads
        self.width = -(-(self.weights + 2 * experts + 1 + padded_heads) // 128) * 128
        self.extra = self.width - self.base
        self.shift = self.count - self.router


def bucket_rows_select(features, feature_rows, bucket_rows, span):
    row = lax.broadcasted_iota(jnp.int32, (features, 1), 0)
    within = lax.rem(row, feature_rows)
    bucket = jnp.where(
        within < bucket_rows, lax.div(row, feature_rows) * bucket_rows + within, -1
    )
    distance = lax.broadcasted_iota(jnp.int32, (1, span), 1) - SKEW
    near = BUCKETS // 2
    spread = max(WINDOW - near, 1)
    far = near + lax.div(jnp.maximum(distance - near, 0) * (BUCKETS - near), spread)
    wanted = jnp.where(distance < near, distance, far)
    reachable = (distance >= 0) & (distance < WINDOW)
    wanted = jnp.where(reachable, wanted, -2)
    return jnp.where(bucket == wanted, 1.0, 0.0).astype(BF16), reachable


def as_column(row, size):
    row_place = lax.broadcasted_iota(jnp.int32, (size, size), 0)
    lane = lax.broadcasted_iota(jnp.int32, (size, size), 1)
    spread = jnp.broadcast_to(row.astype(F32), (size, size))
    return jnp.sum(jnp.where(row_place == lane, spread, 0.0), axis=1, keepdims=True)


def padded_rows(value, rows):
    if value.shape[0] == rows:
        return value
    return jnp.concatenate([value, jnp.zeros((rows - value.shape[0], value.shape[1]), F32)], axis=0)


def padded_lanes(value, lanes):
    if value.shape[1] == lanes:
        return value
    return jnp.concatenate([value, jnp.zeros((value.shape[0], lanes - value.shape[1]), F32)], axis=1)


class Wide:
    def __init__(self, grid, links, own_sem, source, target):
        self.grid, self.links, self.target = grid, links, target
        self.own = pltpu.make_async_copy(
            source, target.at[grid.z, grid.y, grid.x, grid.core], own_sem
        )
        stage = []
        for hop in range(1, grid.z_size):
            origin = (grid.z + grid.z_size - hop) % grid.z_size
            stage.append(
                links.copy(
                    source, target.at[grid.z, grid.y, grid.x, grid.core],
                    grid.at(z=(grid.z + hop) % grid.z_size),
                    target.at[origin, grid.y, grid.x, grid.core],
                )
            )
        self.stages = [stage]

    def start(self):
        self.own.start()
        for going, _ in self.stages[0]:
            going.start()

    def turn(self, axis):
        grid, target = self.grid, self.target
        for _, coming in self.stages[-1]:
            coming.wait_recv()
        stage = []
        if axis == 0:
            self.own.wait()
            held = target.at[:, grid.y, grid.x, grid.core]
            for hop in range(1, grid.y_size):
                origin = (grid.y + grid.y_size - hop) % grid.y_size
                stage.append(
                    self.links.copy(
                        held, held, grid.at(y=(grid.y + hop) % grid.y_size),
                        target.at[:, origin, grid.x, grid.core],
                    )
                )
        elif axis == 1:
            held = target.at[:, :, grid.x, grid.core]
            for hop in range(1, grid.x_size):
                origin = (grid.x + grid.x_size - hop) % grid.x_size
                stage.append(
                    self.links.copy(
                        held, held, (grid.exp, grid.x_from(hop)),
                        target.at[:, :, origin, grid.core],
                    )
                )
        else:
            held = target.at[:, :, :, grid.core]
            stage.append(
                self.links.copy(
                    held, held, (grid.exp, grid.sibling(grid.fsdp)), target.at[:, :, :, 1 - grid.core]
                )
            )
        for going, _ in stage:
            going.start()
        self.stages.append(stage)

    def finish(self):
        for _, coming in self.stages[-1]:
            coming.wait_recv()
        for stage in self.stages:
            for going, _ in stage:
                going.wait_send()


def start_kernel(
    tokens, cotangent, routes_t, slots_t, attention_gain, mixture_gain, attention_in, router_t, table,
    attention_out, expert_up, expert_down, *refs, lanes, heads, width, head_count, experts, capacity,
    local, late,
):
    all_tokens, all_planes, cotangent_early, position_rows, columns, full_out = refs[:6]
    cotangent_late, refs = refs[6 : 6 + late], refs[6 + late :]
    shards = refs[: 2 * local]
    planes, up_stage, down_stage, send, receive, own, fetch, split = refs[2 * local :]
    grid = Grid().here()
    links = Links(send, receive)
    z_size, y_size, fsdp_size = grid.z_size, grid.y_size, grid.fsdp_size
    near = [
        (grid.exp, (grid.fsdp + turn) % fsdp_size) for turn in range(1, fsdp_size)
    ] + [grid.at(z=(grid.z + hop) % z_size) for hop in range(1, z_size)]
    beside = [grid.at(y=(grid.y + hop) % y_size) for hop in range(1, y_size)]
    gathered = ChipGather(grid, links, own.at[0], tokens, all_tokens)
    widely = Wide(grid, links, own.at[2], attention_out, full_out)
    part = expert_down.shape[1]
    depth = expert_up.shape[1]
    fetches = []
    for index in range(local):
        fetches.append(
            pltpu.make_async_copy(expert_up.at[index], up_stage.at[index], fetch.at[2 * index])
        )
        fetches.append(
            pltpu.make_async_copy(
                expert_down.at[index], down_stage.at[index], fetch.at[2 * index + 1]
            )
        )
    greet(near + beside)
    widely.start()
    for copy in fetches:
        copy.start()

    feature_rows = attention_in.shape[0]
    model_width = head_count * width
    gained = attention_in[...].astype(F32) * as_column(attention_gain[...], feature_rows)
    route_rows, slot_rows = routes_t[...].astype(F32), slots_t[...].astype(F32)
    columns[...] = padded_rows(jnp.concatenate([route_rows, slot_rows], axis=0), 128).T
    row_count = columns.shape[0]
    expert_lanes = lax.broadcasted_iota(jnp.int32, (row_count, experts), 1).astype(F32)
    named = jnp.zeros((row_count, experts), F32)
    for k in range(2):
        named = named + jnp.where(expert_lanes == columns[:, k : k + 1], 1.0, 0.0)
    named = jnp.sum(named, axis=0, keepdims=True)
    place = lax.broadcasted_iota(jnp.int32, (feature_rows, feature_rows), 0)
    same = place == lax.broadcasted_iota(jnp.int32, (feature_rows, feature_rows), 1)
    router = contract_last(jnp.where(same, 1.0, 0.0).astype(BF16), router_t[...])
    pieces = [
        router,
        as_column(mixture_gain[...], feature_rows),
        padded_rows(padded_lanes(table[...].astype(F32), heads * fsdp_size), feature_rows),
        padded_rows(named, feature_rows),
    ]
    taken = sum(piece.shape[1] for piece in pieces)
    if lanes.width > lanes.weights + taken:
        pieces.append(jnp.zeros((feature_rows, lanes.width - lanes.weights - taken), F32))
    for place in range(fsdp_size):
        first, last = place * heads * width, min((place + 1) * heads * width, model_width)
        own_pieces = []
        for kind in range(3):
            if last > first:
                own_pieces.append(gained[:, kind * model_width + first : kind * model_width + last])
            if last - first < heads * width:
                own_pieces.append(
                    jnp.zeros((feature_rows, heads * width - max(last - first, 0)), F32)
                )
        planes[place] = jnp.concatenate(own_pieces + pieces, axis=1).astype(BF16)
    placed = []
    for turn in range(1, fsdp_size):
        to = (grid.fsdp + turn) % fsdp_size
        origin = (grid.fsdp + fsdp_size - turn) % fsdp_size
        placed.append(
            links.copy(
                planes.at[to], all_planes.at[grid.z, grid.y, grid.fsdp], (grid.exp, to),
                all_planes.at[grid.z, grid.y, origin],
            )
        )
        placed[-1][0].start()
    kept = pltpu.make_async_copy(
        planes.at[grid.fsdp], all_planes.at[grid.z, grid.y, grid.fsdp], own.at[1]
    )
    kept.start()
    gathered.start()
    for _, coming in placed:
        coming.wait_recv()
    kept.wait()

    def over_y(z):
        for turn in range(1, y_size):
            forwarded.append(
                links.copy(
                    all_planes.at[z, grid.y],
                    all_planes.at[z, grid.y],
                    grid.at(y=(grid.y + turn) % y_size),
                    all_planes.at[z, (grid.y + y_size - turn) % y_size],
                )
            )
            forwarded[-1][0].start()

    along_z, forwarded = [], []
    for hop in range(1, z_size):
        along_z.append(
            links.copy(
                all_planes.at[grid.z, grid.y],
                all_planes.at[grid.z, grid.y],
                grid.at(z=(grid.z + hop) % z_size),
                all_planes.at[(grid.z + z_size - hop) % z_size, grid.y],
            )
        )
        along_z[-1][0].start()
    over_y(grid.z)
    widely.turn(0)

    for copy in fetches:
        copy.wait()
    splits = []
    for index in range(local):
        up, down = shards[2 * index : 2 * index + 2]
        stores = [
            (
                up_stage.at[index, :, pl.ds(block * part, part)],
                up.at[pl.ds(block * depth, depth), :],
            )
            for block in range(fsdp_size)
        ]
        for source, target in stores + [(down_stage.at[index], down)]:
            splits.append(pltpu.make_async_copy(source, target, split.at[len(splits)]))
            splits[-1].start()

    widely.turn(1)

    place = route_rows * capacity + slot_rows
    position_rows[...] = padded_rows(place, 8)
    select_rows([cotangent_early] + list(cotangent_late), place, cotangent[...])

    for hop in range(1, z_size):
        along_z[hop - 1][1].wait_recv()
        over_y((grid.z + z_size - hop) % z_size)
    gathered.forward()
    widely.turn(2)
    for going, coming in forwarded:
        coming.wait_recv()
        going.wait_send()
    for going, _ in placed + along_z:
        going.wait_send()
    gathered.finish()
    widely.finish()
    for copy in splits:
        copy.wait()


def project_kernel(
    tokens, plane, segments, normed, query_t, key_n, query_n, value_n, key_t, value_t, bias, counts,
    weight_t, table_t, *, heads, width, lanes, feature_rows, bucket_rows,
):
    @pl.when(pl.program_id(0) == 0)
    def _():
        weight_t[...] = turned(plane[:, : lanes.weights]).astype(BF16)
        extra = plane[:, lanes.base :]
        span = bias.shape[2]
        select, reachable = bucket_rows_select(plane.shape[0], feature_rows, bucket_rows, span)
        table_t[...] = lax.dot_general(
            extra, select, (((0,), (0,)), ((), ())), preferred_element_type=F32
        )
        first = lanes.table + lax.axis_index("fsdp") * heads
        for head in range(heads):
            bias[head] = jnp.where(reachable, table_t[pl.ds(first + head, 1), :], MASKED)
        summed = jnp.sum(extra.astype(F32), axis=0, keepdims=True)
        counts[...] = pltpu.roll(
            jnp.broadcast_to(summed, counts.shape), lanes.extra - lanes.shift, 1
        )

    inputs = tokens[0].astype(F32)
    scale = lax.rsqrt(jnp.mean(inputs * inputs, axis=1, keepdims=True) + EPSILON)
    low = (inputs * scale).astype(BF16)
    normed[...] = low
    rows = low.shape[0]
    projected = contract_last(weight_t[...], low).astype(BF16).astype(F32)
    document = segments[...] % 4
    places = lax.broadcasted_iota(jnp.int32, (8, rows), 0)
    same = places == document
    hot = jnp.where(same, 1.0, 0.0)
    barred = jnp.where(same | (places >= 4), 0.0, MASKED)
    filler = jnp.zeros((SKEW - 8 - width, rows), F32)
    for head in range(heads):
        query = projected[head * width : (head + 1) * width] * width ** (-0.5)
        key = projected[(heads + head) * width : (heads + head + 1) * width]
        value = projected[(2 * heads + head) * width : (2 * heads + head + 1) * width]
        query_t[head] = jnp.concatenate([query, barred, filler], axis=0).astype(BF16)
        key_n[head] = jnp.concatenate([key, hot, filler], axis=0).T.astype(BF16)
        query_n[head] = query.T.astype(BF16)
        value_n[head] = value.T.astype(BF16)
        key_t[head] = key.astype(BF16)
        value_t[head] = value.astype(BF16)


def spans(length):
    for query_start in range(0, length, QUERY_BLOCK):
        key_start = max(0, query_start - WINDOW)
        yield query_start, key_start, query_start + QUERY_BLOCK - key_start


def spread_bias(bias, skew):
    skew[...] = pltpu.roll(
        jnp.broadcast_to(bias[0], skew.shape), 0, 1, stride=1, stride_axis=0
    )


def attend_kernel(
    query_t, key_n, value_t, bias, context, context_high, log_total, attended, skew, scores, held,
    send, receive, own, *, rows,
):
    head = pl.program_id(0)
    width = value_t.shape[1]
    grid = Grid().here()
    fsdp_size = grid.fsdp_size

    def leave(number):
        place = pl.ds(pl.multiple_of(number * width, 16), width)
        copies = []
        for turn in range(1, fsdp_size):
            to = (grid.fsdp + turn) % fsdp_size
            origin = (grid.fsdp + fsdp_size - turn) % fsdp_size
            sems = dict(
                send_sem=send.at[number, turn], recv_sem=receive.at[number, turn],
                device_id=(grid.exp, to), device_id_type=MESH,
            )
            copies.append(
                (
                    pltpu.make_async_remote_copy(
                        src_ref=held.at[number, to], dst_ref=attended.at[grid.fsdp, place, :], **sems
                    ),
                    pltpu.make_async_remote_copy(
                        src_ref=attended.at[origin, place, :], dst_ref=attended.at[origin, place, :],
                        **sems,
                    ),
                )
            )
        kept = pltpu.make_async_copy(
            held.at[number, grid.fsdp], attended.at[grid.fsdp, place, :], own.at[number]
        )
        return copies, kept

    @pl.when(head == 0)
    def _():
        greet([(grid.exp, (grid.fsdp + turn) % fsdp_size) for turn in range(1, fsdp_size)])

    spread_bias(bias, skew)
    for query_start, key_start, key_count in spans(query_t.shape[2]):
        queries = slice(query_start, query_start + QUERY_BLOCK)
        keys = slice(key_start, key_start + key_count)
        raw = matmul(key_n[0, keys, :], query_t[0, :, queries])
        for start in range(0, key_count, SKEW):
            offset = query_start - key_start - start + SKEW
            scores[start : start + SKEW, :] = (
                raw[start : start + SKEW] + skew[:, offset : offset + QUERY_BLOCK]
            )
        high = jnp.max(scores[:key_count, :], axis=0, keepdims=True)
        weights = jnp.exp(scores[:key_count, :] - high)
        total = jnp.sum(weights, axis=0, keepdims=True)
        gathered = matmul(value_t[0, :, keys], weights.astype(BF16)) / total
        context_high[0, :, queries] = gathered
        log_total[0, :, queries] = high + jnp.log(total)
        for start in range(0, QUERY_BLOCK, 128):
            place = query_start + start
            piece = gathered[:, start : start + 128].astype(BF16)
            context[place // rows, :, place % rows : place % rows + 128] = piece
            held[head, place // rows, :, place % rows : place % rows + 128] = piece
    copies, kept = leave(head)
    for going, _ in copies:
        going.start()
    kept.start()

    @pl.when(head == pl.num_programs(0) - 1)
    def _():
        def finish(number, carry):
            copies, kept = leave(number)
            for going, coming in copies:
                coming.wait_recv()
                going.wait_send()
            kept.wait()
            return carry

        lax.fori_loop(0, pl.num_programs(0), finish, 0)


def attend_back_kernel(
    query_t, key_n, query_n, value_n, key_t, grad_t, grad_n, context_high, log_total, bias,
    grad_projected, grad_bias, skew, grad_skew, grad_key, grad_value, *, scale,
):
    spread_bias(bias, skew)
    grad_skew[...] = jnp.zeros_like(grad_skew)
    grad_key[...] = jnp.zeros_like(grad_key)
    grad_value[...] = jnp.zeros_like(grad_value)
    inner = jnp.sum(grad_t[0].astype(F32) * context_high[0], axis=0, keepdims=True)
    for query_start, key_start, key_count in spans(query_t.shape[2]):
        queries = slice(query_start, query_start + QUERY_BLOCK)
        keys = slice(key_start, key_start + key_count)
        raw = matmul(key_n[0, keys, :], query_t[0, :, queries])
        grad_weights = matmul(value_n[0, keys, :], grad_t[0, :, queries])
        weights_low, grad_low = [], []
        for start in range(0, key_count, SKEW):
            offset = query_start - key_start - start + SKEW
            part = slice(start, start + SKEW)
            weights = jnp.exp(
                raw[part] + skew[:, offset : offset + QUERY_BLOCK] - log_total[0, :, queries]
            )
            grad_scores = weights * (grad_weights[part] - inner[:, queries])
            grad_skew[:, offset : offset + QUERY_BLOCK] += grad_scores
            weights_low.append(weights.astype(BF16))
            grad_low.append(grad_scores.astype(BF16))
        weights_low = jnp.concatenate(weights_low, axis=0)
        grad_low = jnp.concatenate(grad_low, axis=0)
        grad_projected[0, 0, :, queries] = (matmul(key_t[0, :, keys], grad_low) * scale).astype(BF16)
        grad_key[keys, :] += matmul(grad_low, query_n[0, queries, :])
        grad_value[keys, :] += matmul(weights_low, grad_n[0, queries, :])
    grad_projected[1, 0] = grad_key[...].T.astype(BF16)
    grad_projected[2, 0] = grad_value[...].T.astype(BF16)
    count = SKEW
    span = skew.shape[1]
    while count > 8:
        count //= 2
        grad_skew[:count, :] += pltpu.roll(grad_skew[count : 2 * count, :], span - count, 1)
    summed = grad_skew[0:1, :]
    for row in range(1, 8):
        summed = summed + pltpu.roll(grad_skew[row : row + 1, :], span - row, 1)
    grad_bias[0] = summed

def expert_lane(shape, lanes):
    return lax.broadcasted_iota(jnp.int32, shape, 1) - lanes.router


def int_columns(columns):
    values = columns[:, 0:4].astype(jnp.int32)
    return values[:, 0:2], values[:, 2:4]


def route_kernel(
    tokens, attended_t, attention_out, plane, columns, position_rows, *refs,
    experts, lanes, capacity, crossing,
):
    over, refs = refs[:crossing], refs[crossing:]
    hidden, routed, probabilities, gates, outgoing, rows_in, gates_in = refs[:7]
    landed, refs = refs[7 : 7 + crossing], refs[7 + crossing :]
    slot_gates, send, receive, own = refs
    grid = Grid().here()
    links = Links(send, receive)
    exp_size = grid.exp_size
    sibling = (grid.exp, grid.sibling(grid.fsdp))
    greet([((grid.exp + hop) % exp_size, grid.fsdp) for hop in range(1, exp_size)] + [sibling])
    swaps = [links.copy(source, target, sibling, target) for source, target in zip(over, landed)]
    for going, _ in swaps:
        going.start()
    rows, model_width = tokens.shape
    routes, slots = int_columns(columns)
    attended_low = turned(attended_t[:model_width]).astype(BF16)
    hidden_state = tokens[...].astype(F32) + matmul(attended_low, attention_out[...])
    hidden[...] = hidden_state
    scale = lax.rsqrt(jnp.mean(hidden_state * hidden_state, axis=1, keepdims=True) + EPSILON)
    extra = plane[:, lanes.base :]
    gain = extra.astype(F32).T[lanes.gain : lanes.gain + 1]
    low = (hidden_state * scale * gain).astype(BF16)
    routed[...] = low
    member_slots = experts // exp_size * capacity
    work = Exchange(
        grid, "exp", links, own,
        [
            (lambda to: outgoing.at[to, pl.ds(0, capacity), :], rows_in),
            (partial(plane_of, slot_gates, None), gates_in),
        ],
    )
    for hop in list(range(1, exp_size)) + [0]:
        to = (grid.exp + hop) % exp_size
        slot = lax.broadcasted_iota(jnp.int32, (member_slots, rows), 0) + to * member_slots
        slot = slot.astype(F32)
        picked = (slot == position_rows[0:1, :]) | (slot == position_rows[1:2, :])
        outgoing[to] = matmul(jnp.where(picked, 1.0, 0.0).astype(BF16), low).astype(BF16)
        if hop > 0:
            work.copies[hop - 1][0].start()
        else:
            work.own[0].start()
    logits = matmul(low, extra)
    lane = expert_lane(logits.shape, lanes)
    logits = jnp.where((lane >= 0) & (lane < experts), logits, MASKED)
    powers = jnp.exp(logits - jnp.max(logits, axis=1, keepdims=True))
    powers = powers / jnp.sum(powers, axis=1, keepdims=True)
    probabilities[...] = powers
    chosen = [
        jnp.sum(jnp.where(lane == routes[:, k : k + 1], powers, 0.0), axis=1, keepdims=True)
        for k in range(2)
    ]
    total = chosen[0] + chosen[1]
    gate_values = [chosen[k] / total for k in range(2)]
    pair = lax.broadcasted_iota(jnp.int32, (rows, 2), 1)
    gates[...] = jnp.where(pair == 0, gate_values[0], gate_values[1])
    gate_lanes = slot_gates.shape[2]
    slot_lanes = lax.broadcasted_iota(jnp.int32, (rows, gate_lanes), 1)
    inside = slot_lanes < member_slots
    places = routes * capacity + slots
    for member in range(exp_size):
        by_slot = jnp.zeros((rows, gate_lanes), F32)
        for k in range(2):
            hit = (slot_lanes + member * member_slots == places[:, k : k + 1]) & inside
            by_slot = by_slot + jnp.where(hit, gate_values[k], 0.0)
        slot_gates[member] = jnp.broadcast_to(
            jnp.sum(by_slot, axis=0, keepdims=True), slot_gates.shape[1:]
        )
    for going, _ in work.copies[exp_size - 1 :]:
        going.start()
    work.own[1].start()
    work.finish()
    for going, coming in swaps:
        coming.wait_recv()
        going.wait_send()


def select_rows(outgoing, position_rows, values):
    rows = values.shape[0]
    sizes = [array.shape[1] for array in outgoing]
    for member in range(outgoing[0].shape[0]):
        slots = lax.broadcasted_iota(jnp.int32, (sum(sizes), rows), 0) + member * sum(sizes)
        slots = slots.astype(F32)
        picked = (slots == position_rows[0:1, :]) | (slots == position_rows[1:2, :])
        found = matmul(jnp.where(picked, 1.0, 0.0).astype(BF16), values).astype(BF16)
        first = 0
        for array, size in zip(outgoing, sizes):
            array[member] = found[first : first + size]
            first += size


def gelu_parts(value):
    magnitude = jnp.abs(value)
    power = jnp.exp2(value * value * -0.7213475204444817)
    base = 1.0 + (0.3275911 * 0.7071067811865476) * magnitude
    step = pl.reciprocal(base, approx=True)
    step = step * (2.0 - base * step)
    series = step * (
        0.127414796
        + step * (-0.142248368 + step * (0.7107068705 + step * (-0.7265760135 + step * 0.5307027145)))
    )
    tail = series * power
    normal = jnp.where(value < 0.0, tail, 1.0 - tail)
    return value * normal, normal + value * (power * 0.3989422804014327)


def flipped(place, other, size):
    result, bit = 0, 1
    while bit < size:
        result = result + bit * ((place // bit + other // bit) % 2)
        bit *= 2
    return result


def expert_kernel(*refs, layout, index, local, half, capacity, parts):
    shards = 2 * half
    refs = Bag(layout, refs)
    grid = Grid().here()
    z_size, y_size = grid.z_size, grid.y_size
    last = index == local - 1
    sibling = (grid.exp, grid.sibling(grid.fsdp))
    links = Links(refs.send[0], refs.receive[0])
    rows_all, cot, up_all, down_all = (
        refs.rows_all[0], refs.cot[0], refs.up_all[0], refs.down_all[0]
    )
    total = refs.total[0]
    if last:
        active, grad_hidden, unscaled = refs.active[0], refs.grad_hidden[0], refs.unscaled[0]
    else:
        grad_total, slot_grad = refs.grad_total[0], refs.slot_grad[0]
    gates, gate_column = refs.gates[0], refs.gate_column[0]
    rows_t, slot_t = refs.rows_t[0], refs.slot_t[0]
    grad_up, grad_down = refs.grad_up[0], refs.grad_down[0]
    grad_rows, grad_gates = refs.grad_rows[0], refs.grad_gates[0]
    up_keep, up_taken, down_keep, down_taken = refs.own
    keep_up = [up_keep] + list(refs.far_keep_up)
    taken_up = [up_taken] + list(refs.far_taken_up)
    keep_down = [down_keep] + list(refs.far_keep_down)
    taken_down = [down_taken] + list(refs.far_taken_down)
    load_sem, fetch_sem, store_sem = refs.load_sem[0], refs.fetch_sem[0], refs.store_sem[0]
    store_there, stored_here = refs.store_there[0], refs.stored_here[0]
    pass_sem = refs.pass_sem[0]
    blocks, _, model_width = rows_all.shape
    part = up_all.shape[2]
    count = blocks * capacity
    depth = model_width // shards
    power = z_size & (z_size - 1) == 0
    together = 2 if power and z_size > 1 else 1
    group_rows = together * y_size * capacity

    def source_z(turn):
        return flipped(grid.z, turn, z_size) if power else (grid.z + turn) % z_size

    def target_z(turn):
        return flipped(grid.z, turn, z_size) if power else (grid.z + z_size - turn) % z_size

    def owner(place, core):
        return ((grid.x + place % half) % half) * 2 + (core + place // half) % 2

    def rows_of(place, core=None):
        core = grid.core if core is None else core
        return pl.ds(pl.multiple_of(owner(place, core) * depth, 16), depth)

    loads = [pltpu.make_async_copy(refs.rows_in[0], rows_all, load_sem.at[1])]
    late_count = 0
    if last and refs.cot_late:
        late_count = refs.cot_late[0].shape[1]
        loads.append(
            pltpu.make_async_copy(
                refs.cot_late[0], cot.at[:, pl.ds(capacity - late_count, late_count)], load_sem.at[4]
            )
        )
    loads.append(
        pltpu.make_async_copy(
            refs.cot_in[0].at[:, pl.ds(index * capacity, capacity - late_count)],
            cot.at[:, pl.ds(0, capacity - late_count)], load_sem.at[0],
        )
    )
    my_up, my_down = refs.my_up, refs.my_down
    swapped_up, swapped_down = refs.swapped_up, refs.swapped_down
    local_up = list(enumerate(my_up)) + [
        (half + number, array) for number, array in enumerate(swapped_up)
    ]
    local_down = list(enumerate(my_down)) + [
        (half + number, array) for number, array in enumerate(swapped_down)
    ]

    def fetch_up(place):
        return [
            pltpu.make_async_copy(
                array.at[rows_of(place), :], up_all.at[place, rows_of(shard), :],
                fetch_sem.at[place, number],
            )
            for number, (shard, array) in enumerate(local_up)
        ]

    fetched_down = {
        shard: pltpu.make_async_copy(
            array, down_all.at[shard], fetch_sem.at[shards + number, 0]
        )
        for number, (shard, array) in enumerate(local_down)
    }
    cross_down = {
        half + shard: links.copy(
            my_down[shard], down_all.at[half + shard], sibling, down_all.at[half + shard]
        )
        for shard in range(len(swapped_down), half)
    }
    cross_up = [
        links.copy(
            my_up[shard].at[rows_of(place, 1 - grid.core), :],
            up_all.at[place, rows_of(shard), :], sibling,
            up_all.at[place, rows_of(half + shard), :],
        )
        for shard in range(len(swapped_up), half)
        for place in range(shards)
    ]
    cross_next = [
        links.copy(source, target, sibling, target)
        for source, target in zip(refs.next_mine, refs.next_swapped)
    ]
    work = Exchange(
        grid, "exp", links, refs.own_sem[0],
        [
            (partial(plane_of, source, place), target)
            for source, place, target in zip(refs.moved_from, parts, refs.moved_to)
        ],
    )
    def member(z, y):
        return z * y_size + y

    def give_back(turn, hop):
        to = member(source_z(turn), (grid.y + hop) % y_size)
        origin = member(target_z(turn), (grid.y + y_size - hop) % y_size)
        pairs = []
        for number, (held, target) in enumerate(
            ((grad_rows, refs.back_rows[0]), (grad_gates, refs.back_gates[0]))
        ):
            sems = dict(
                send_sem=refs.back_send[0].at[number, turn, hop],
                recv_sem=refs.back_receive[0].at[number, turn, hop],
                device_id=(to, grid.fsdp), device_id_type=MESH,
            )
            pairs.append(
                (
                    pltpu.make_async_remote_copy(
                        src_ref=held.at[to], dst_ref=target.at[grid.exp], **sems
                    ),
                    pltpu.make_async_remote_copy(
                        src_ref=target.at[origin], dst_ref=target.at[origin], **sems
                    ),
                )
            )
        return pairs

    steps = [(turn, hop) for turn in range(z_size) for hop in range(y_size)]
    own_back = []
    if last:
        own_back = [
            pltpu.make_async_copy(held.at[grid.exp], target.at[grid.exp], load_sem.at[2 + number])
            for number, (held, target) in enumerate(
                ((grad_rows, refs.back_rows[0]), (grad_gates, refs.back_gates[0]))
            )
        ]

    for copy in loads:
        copy.start()
    order = list(range(shards))
    if not last:
        order = [(pair + 1) % half + side * half for pair in range(half) for side in (1, 0)]
    if last:
        for copy in fetched_down.values():
            copy.start()
    for place in order:
        if not last and place in fetched_down:
            fetched_down[place].start()
        for copy in fetch_up(place):
            copy.start()
    greet(
        [((grid.exp + hop) % grid.exp_size, grid.fsdp) for hop in range(1, grid.exp_size)]
        + chip_peers(grid)
    )
    for going, _ in list(cross_down.values()) + cross_up + cross_next:
        going.start()
    work.start()

    def place_at(position):
        hop = (position // 2 + 1) % half
        return hop + half * (1 - position % 2)

    def slot_rows():
        columns = gates[:, 0, :].T
        for block in range(blocks):
            piece = slice(block * capacity, (block + 1) * capacity)
            gate = columns[index * capacity : (index + 1) * capacity, block : block + 1]
            gate_column[piece, :] = gate
        slot_values = gate_column[...] * cot[...].reshape(count, model_width).astype(F32)
        slot_t[...] = slot_values.T.astype(BF16)
        if not last:
            slot_grad[...] = slot_values.astype(BF16)

    def wait_down(place):
        if place in fetched_down:
            fetched_down[place].wait()
        else:
            cross_down[place][1].wait_recv()

    def wait_crossed():
        for _, coming in cross_up:
            coming.wait_recv()

    def folded(value):
        return sum(value[:, start : start + 128] for start in range(0, value.shape[1], 128))

    def gate_rows(found, block):
        ones = jnp.ones((8, 128), F32)
        grad_gates[block] = lax.dot_general(
            ones, found, (((1,), (1,)), ((), ())), precision=lax.Precision.HIGHEST,
            preferred_element_type=F32,
        )

    def up_target(targets, hop, place):
        if hop == 0:
            return targets[0].at[rows_of(place), :]
        return targets[1].at[hop - 1, rows_of(place), :]

    def keep_stores(place, slot):
        return [
            pltpu.make_async_copy(
                grad_up.at[slot, rows_of(hop), :], up_target(keep_up, hop, place),
                store_sem.at[slot, hop],
            )
            for hop in range(half)
        ]

    def give_stores(place, slot):
        return [
            pltpu.make_async_remote_copy(
                src_ref=grad_up.at[slot, rows_of(half + hop), :],
                dst_ref=up_target(taken_up, hop, place),
                send_sem=store_there.at[slot, hop], recv_sem=stored_here.at[place, hop],
                device_id=sibling, device_id_type=MESH,
            )
            for hop in range(half)
        ]

    def down_store(slot):
        return pltpu.make_async_copy(grad_down.at[slot], keep_down[0], store_sem.at[slot, half])

    def down_give(hop, slot):
        target = taken_down[0] if hop == 0 else taken_down[1].at[hop - 1]
        return pltpu.make_async_remote_copy(
            src_ref=grad_down.at[slot], dst_ref=target,
            send_sem=store_there.at[slot, half], recv_sem=stored_here.at[hop, half],
            device_id=sibling, device_id_type=MESH,
        )

    def start_store(place, slot):
        for copy in keep_stores(place, slot) + give_stores(place, slot):
            copy.start()

        @pl.when(place == 0)
        def _():
            down_store(slot).start()

        for hop in range(half):

            @pl.when(place == half + hop)
            def _(hop=hop):
                down_give(hop, slot).start()

            if hop > 0:

                @pl.when(place == hop)
                def _(hop=hop):
                    keep_down[1][hop - 1] = grad_down[slot]

    def wait_store(place, slot):
        for copy in keep_stores(place, slot):
            copy.wait()
        for copy in give_stores(place, slot):
            copy.wait_send()

        @pl.when(place == 0)
        def _():
            down_store(slot).wait()

        for hop in range(half):

            @pl.when(place == half + hop)
            def _(hop=hop):
                down_give(hop, slot).wait_send()

    def fused(position, carry):
        place, slot = place_at(position), position % 2
        for copy in fetch_up(place):
            copy.wait()
        for which in range(shards):

            @pl.when(place == which)
            def _(which=which):
                wait_down(which)

        up, down = up_all[place], down_all[place]
        rows = rows_all[...].reshape(count, model_width)
        pieces = [slice(start, start + 256) for start in range(0, count, 256)]

        def products_of(piece):
            return matmul(rows[piece], up), contract_last(slot_grad[piece, :], down)

        raw = products_of(pieces[0])
        active_low, grad_low = [], []
        for number, piece in enumerate(pieces):
            hidden, grad_active = raw
            if number + 1 < len(pieces):
                raw = products_of(pieces[number + 1])
            activated, slope = gelu_parts(hidden)
            active_low.append(activated.astype(BF16))
            grad_low.append((grad_active * slope).astype(BF16))
            total[piece, :] += matmul(active_low[number], down)
            grad_total[piece, :] += contract_last(grad_low[number], up)
        active_low = jnp.concatenate(active_low, axis=0)
        grad_low = jnp.concatenate(grad_low, axis=0)

        @pl.when(position >= 2)
        def _():
            wait_store(place_at(position - 2), slot)

        grad_up[slot] = matmul(rows_t[...], grad_low).astype(BF16)
        grad_down[slot] = matmul(slot_t[...], active_low).T.astype(BF16)
        start_store(place, slot)
        return carry

    def group(number, carry):
        turns = [number * together + more for more in range(together)]
        if together == 2:
            place_of_group = flipped(grid.z // 2, number, z_size // 2)
        else:
            place_of_group = source_z(number)
        members = pl.ds(place_of_group * together * y_size, together * y_size)
        span = pl.ds(pl.multiple_of(place_of_group * group_rows, 16), group_rows)
        rows = rows_all[members].reshape(group_rows, model_width)
        gate = gate_column[span, :]
        grad = jnp.zeros((group_rows, model_width), F32)
        products = jnp.zeros((group_rows, 128), F32)
        ahead = matmul(rows, up_all[0])
        for place in range(shards):
            hidden = ahead
            if place + 1 < shards:
                ahead = matmul(rows, up_all[place + 1])
            base = unscaled[place, span, :].astype(F32)
            activated, slope = gelu_parts(hidden)
            products = products + folded(activated * base)
            active_low = activated.astype(BF16)
            active[place, span, :] = active_low
            low = (gate * base * slope).astype(BF16)
            grad_hidden[place, span, :] = low
            grad = grad + contract_last(low, up_all[place])
            total[span, :] += matmul(active_low, down_all[place])
        grad_rows[members] = grad.astype(BF16).reshape(together * y_size, capacity, model_width)
        for hop in range(together * y_size):
            gate_rows(
                products[hop * capacity : (hop + 1) * capacity],
                place_of_group * together * y_size + hop,
            )
        for turn in turns:
            for hop in range(y_size):

                @pl.when(turn + hop > 0)
                def _(turn=turn, hop=hop):
                    for going, _ in give_back(turn, hop):
                        going.start()

        return carry

    def column(position, carry):
        place, slot = place_at(position), position % 2
        @pl.when(position >= 2)
        def _():
            wait_store(place_at(position - 2), slot)

        grad_up[slot] = matmul(rows_t[...], grad_hidden[place]).astype(BF16)
        grad_down[slot] = matmul(slot_t[...], active[place]).T.astype(BF16)
        start_store(place, slot)
        return carry

    for copy in loads[1:]:
        copy.wait()
    total[...] = jnp.zeros_like(total)
    slot_rows()
    if last:
        for place in range(shards):
            wait_down(place)
            unscaled[place] = contract_last(
                cot[...].reshape(count, model_width), down_all[place]
            ).astype(BF16)
        loads[0].wait()
        for place in range(shards):
            for copy in fetch_up(place):
                copy.wait()
        wait_crossed()
        lax.fori_loop(0, z_size // together, group, 0)
        for copy in own_back:
            copy.start()
        rows_t[...] = turned(rows_all[...].reshape(count, model_width)).astype(BF16)
        lax.fori_loop(0, shards, column, 0)
    else:
        loads[0].wait()
        rows_t[...] = turned(rows_all[...].reshape(count, model_width)).astype(BF16)
        grad_total[...] = jnp.zeros_like(grad_total)
        wait_crossed()
        lax.fori_loop(0, shards, fused, 0)
        grad_rows[...] = grad_total[...].astype(BF16).reshape(grad_rows.shape)
        for block in range(blocks):
            rows = total[block * capacity : (block + 1) * capacity, :].astype(BF16).astype(F32)
            gate_rows(folded(rows * cot[block].astype(F32)), block)

    rows_out = refs.rows_out[0]
    cot[...] = total[...].astype(BF16).reshape(blocks, capacity, model_width)
    out_copies = [pltpu.make_async_copy(cot, rows_out.at[:, index], load_sem.at[0])]
    for before in refs.outs_before:
        out_copies.append(
            pltpu.make_async_copy(before, rows_out.at[:, pl.ds(0, index)], load_sem.at[1])
        )
    for copy in out_copies:
        copy.start()
    for position in range(max(shards - 2, 0), shards):
        wait_store(place_at(position), position % 2)
    for place in range(shards):
        for copy in give_stores(place, 0):
            copy.wait_recv()
    for hop in range(half):
        down_give(hop, 0).wait_recv()
    if half > 1:
        for kept, taken in ((keep_up[1], taken_up[1]), (keep_down[1], taken_down[1])):
            kept[...] = (kept[...].astype(F32) + taken[...].astype(F32)).astype(BF16)
        early_rows = part // 2
        for source, target, number in (
            (keep_up[1], refs.pass_up[0], 0),
            (keep_down[1].at[:, pl.ds(0, early_rows), :], refs.early_down[0], 1),
            (keep_down[1].at[:, pl.ds(early_rows, part - early_rows), :], refs.pass_down[0], 2),
        ):
            out_copies.append(pltpu.make_async_copy(source, target, pass_sem.at[number]))
            out_copies[-1].start()
    for copy in out_copies:
        copy.wait()
    for going, coming in cross_next:
        coming.wait_recv()
        going.wait_send()
    for going, _ in list(cross_down.values()) + cross_up:
        going.wait_send()
    work.finish()
    if last:
        for turn, hop in steps[1:]:
            for going, coming in give_back(turn, hop):
                coming.wait_recv()
                going.wait_send()
        for copy in own_back:
            copy.wait()


class Bag:
    def __init__(self, layout, refs):
        start = 0
        for name, size in layout.items():
            setattr(self, name, refs[start : start + size])
            start += size


class Wanted:
    def groups(self):
        return list(self.__dict__.values())

    def layout(self):
        return {name: len(group) for name, group in self.__dict__.items()}


def run_expert(index, local, rows_in, gates, cotangent, cotangent_late, ups, downs, swapped, next_mine,
               moved, outs_before, collective_id):
    grid = Grid()
    half = len(ups)
    shards = 2 * half
    last = index == local - 1
    blocks, capacity, model_width = rows_in.shape
    part = downs[0].shape[0]
    count = blocks * capacity
    inputs, outputs, scratch = Wanted(), Wanted(), Wanted()
    inputs.cot_in = [(cotangent, ANYWHERE)]
    inputs.cot_late = [(array, ANYWHERE) for array in cotangent_late]
    inputs.rows_in = [(rows_in, ANYWHERE)]
    inputs.gates = [(gates, IN_VMEM)]
    inputs.my_up = [(array, ANYWHERE) for array in ups]
    inputs.my_down = [(array, ANYWHERE) for array in downs]
    inputs.swapped_up = [(array, ANYWHERE) for array in swapped[0]]
    inputs.swapped_down = [(array, ANYWHERE) for array in swapped[1]]
    inputs.next_mine = [(array, ANYWHERE) for array in next_mine]
    inputs.moved_from = [(array, ANYWHERE) for array, _ in moved]
    inputs.outs_before = [] if outs_before is None else [(outs_before, IN_VMEM)]

    up_shape, down_shape = (model_width, part), (part, model_width)
    outputs.rows_out = [(shape_of((blocks, index + 1, capacity, model_width), BF16), ANYWHERE)]
    own_up, own_down = shape_of(up_shape, BF16), shape_of(down_shape, BF16)
    outputs.own = [(own_up, ANYWHERE), (own_up, ANYWHERE), (own_down, ANYWHERE), (own_down, ANYWHERE)]
    outputs.pass_up = [(shape_of((half - 1,) + up_shape, BF16), ANYWHERE)] if half > 1 else []
    late_down = (half - 1, part - part // 2, model_width)
    early_down = (half - 1, part // 2, model_width)
    outputs.pass_down = [(shape_of(late_down, BF16), ANYWHERE)] if half > 1 else []
    outputs.early_down = [(shape_of(early_down, BF16), ANYWHERE)] if half > 1 else []
    outputs.next_swapped = [(shape_of(array.shape, BF16), ANYWHERE) for array in next_mine]
    outputs.moved_to = [
        (
            shape_of((grid.exp_size,) + array.shape[(1 if place is None else 2) :], array.dtype),
            ANYWHERE,
        )
        for array, place in moved
    ]
    rows_shape, gate_shape = (blocks, capacity, model_width), (blocks, 8, capacity)
    if last:
        outputs.back_rows = [(shape_of(rows_shape, BF16), ANYWHERE)]
        outputs.back_gates = [(shape_of(gate_shape, F32), ANYWHERE)]
    else:
        outputs.grad_rows = [(shape_of(rows_shape, BF16), IN_VMEM)]
        outputs.grad_gates = [(shape_of(gate_shape, F32), IN_VMEM)]

    sems = lambda *shape: pltpu.SemaphoreType.DMA(shape)
    scratch.rows_all = [pltpu.VMEM(rows_shape, BF16)]
    scratch.cot = [pltpu.VMEM(rows_shape, BF16)]
    scratch.up_all = [pltpu.VMEM((shards,) + up_shape, BF16)]
    scratch.down_all = [pltpu.VMEM((shards,) + down_shape, BF16)]
    scratch.total = [pltpu.VMEM((count, model_width), F32)]
    if last:
        scratch.active = [pltpu.VMEM((shards, count, part), BF16)]
        scratch.grad_hidden = [pltpu.VMEM((shards, count, part), BF16)]
        scratch.unscaled = [pltpu.VMEM((shards, count, part), BF16)]
    else:
        scratch.grad_total = [pltpu.VMEM((count, model_width), F32)]
        scratch.slot_grad = [pltpu.VMEM((count, model_width), BF16)]
    if last:
        scratch.grad_rows = [pltpu.VMEM(rows_shape, BF16)]
        scratch.grad_gates = [pltpu.VMEM(gate_shape, F32)]
        scratch.back_send = [sems(2, grid.z_size, grid.y_size)]
        scratch.back_receive = [sems(2, grid.z_size, grid.y_size)]
    scratch.gate_column = [pltpu.VMEM((count, 1), F32)]
    scratch.rows_t = [pltpu.VMEM((model_width, count), BF16)]
    scratch.slot_t = [pltpu.VMEM((model_width, count), BF16)]
    scratch.grad_up = [pltpu.VMEM((2,) + up_shape, BF16)]
    scratch.grad_down = [pltpu.VMEM((2,) + down_shape, BF16)]
    far_up = [pltpu.VMEM((half - 1,) + up_shape, BF16)] * (1 if half > 1 else 0)
    far_down = [pltpu.VMEM((half - 1,) + down_shape, BF16)] * (1 if half > 1 else 0)
    scratch.far_keep_up, scratch.far_taken_up = far_up, far_up
    scratch.far_keep_down, scratch.far_taken_down = far_down, far_down
    scratch.load_sem = [sems(5)]
    scratch.pass_sem = [sems(3)]
    scratch.fetch_sem = [sems(2 * shards, shards)]
    scratch.store_sem = [sems(2, half + 1)]
    scratch.store_there = [sems(2, half + 1)]
    scratch.stored_here = [sems(shards, half + 1)]
    copies = len(moved) * grid.exp_size + half * (shards + 2) + len(next_mine)
    scratch.send = [sems(copies)]
    scratch.receive = [sems(copies)]
    scratch.own_sem = [sems(max(len(moved), 1))]

    layout = {**inputs.layout(), **outputs.layout(), **scratch.layout()}

    def body(*refs):
        expert_kernel(
            *refs, layout=layout, index=index, local=local, half=half, capacity=capacity,
            parts=[place for _, place in moved],
        )

    results = pl.pallas_call(
        body,
        in_specs=[spec for group in inputs.groups() for _, spec in group],
        out_specs=tuple(spec for group in outputs.groups() for _, spec in group),
        out_shape=tuple(shape for group in outputs.groups() for shape, _ in group),
        scratch_shapes=[item for group in scratch.groups() for item in group],
        compiler_params=params(collective_id=collective_id, has_side_effects=True),
        cost_estimate=hint(45),
        name=f"expert_{index}",
    )(*[array for group in inputs.groups() for array, _ in group])
    return Bag(outputs.layout(), results)


def local_picks(routes, slots, capacity, local, index, slot_count):
    member, which = lax.div(routes, local), lax.rem(routes, local)
    places = jnp.where(which == index, member * capacity + slots, -1)
    lane = lax.broadcasted_iota(jnp.int32, (routes.shape[0], slot_count), 1)
    return [lane == places[:, k : k + 1] for k in range(2)]


def unroute_kernel(
    hidden, cotangent, routed, probabilities, gates, plane, columns, counts, attention_out, context,
    *refs, experts, local, token_total, lanes, heads, width,
):
    grads, gate_grads = refs[:local], refs[local : 2 * local]
    (
        grad_hidden, small, grad_t, grad_n, grad_out, branches, own_out, total, send, receive, own_sem,
    ) = refs[2 * local :]
    grid = Grid().here()
    links = Links(send, receive)
    rows, model_width = hidden.shape
    members, capacity = grads[0].shape[0], grads[0].shape[1]
    head_rows = heads * width
    fetch = pltpu.make_async_copy(
        attention_out.at[pl.ds(pl.multiple_of(grid.fsdp * head_rows, 16), head_rows), :], own_out,
        own_sem.at[0],
    )
    fetch.start()
    greet(chip_peers(grid))
    extra = plane[:, lanes.base :]
    gains = extra.astype(F32).T[lanes.gain : lanes.gain + 1]
    half_rows = rows // 2
    sibling = grid.sibling(grid.fsdp)
    small_t = jnp.zeros((lanes.extra, model_width), F32)
    gain_grad = jnp.zeros((1, model_width), F32)
    along_x, across = [], []
    for half in range(2):
        here = slice(half * half_rows, (half + 1) * half_rows)
        grad_output = cotangent[here, :].astype(F32)
        routes = columns[here, 0:2].astype(jnp.int32)
        slots = columns[here, 2:4].astype(jnp.int32)
        member, which = lax.div(routes, local), lax.rem(routes, local)
        lane = lax.broadcasted_iota(jnp.int32, (half_rows, capacity), 1)
        grad_routed = jnp.zeros((half_rows, model_width), F32)
        found = [jnp.zeros((half_rows, capacity), F32), jnp.zeros((half_rows, capacity), F32)]
        for index in range(local):
            picks = local_picks(routes, slots, capacity, local, index, members * capacity)
            grad_routed = grad_routed + matmul(
                jnp.where(picks[0] | picks[1], 1.0, 0.0).astype(BF16),
                grads[index][...].reshape(members * capacity, model_width),
            )
            for place in range(members):
                spots = jnp.where((which == index) & (member == place), slots, -1)
                for k in range(2):
                    found[k] = found[k] + jnp.where(
                        lane == spots[:, k : k + 1], gate_grads[index][place, 0:1, :], 0.0
                    )
        grad_gates = [jnp.sum(found[k], axis=1, keepdims=True) for k in range(2)]
        powers = probabilities[here, :]
        lane = expert_lane(powers.shape, lanes)
        inside = (lane >= 0) & (lane < experts)
        picked = [lane == routes[:, k : k + 1] for k in range(2)]
        chosen_total = sum(
            jnp.sum(jnp.where(picked[k], powers, 0.0), axis=1, keepdims=True) for k in range(2)
        )
        weighted = grad_gates[0] * gates[here, 0:1] + grad_gates[1] * gates[here, 1:2]
        grad_mass = (AUX_WEIGHT * experts / (2.0 * token_total * token_total)) * counts[0:1, :]
        grad_mass = jnp.where(inside, grad_mass, 0.0)
        for k in range(2):
            grad_mass = grad_mass + jnp.where(
                picked[k], (grad_gates[k] - weighted) / chosen_total, 0.0
            )
        grad_logits = powers * (grad_mass - jnp.sum(powers * grad_mass, axis=1, keepdims=True))
        grad_routed = grad_routed + contract_last(grad_logits.astype(BF16), extra)
        hidden_state = hidden[here, :]
        scale = lax.rsqrt(jnp.mean(hidden_state * hidden_state, axis=1, keepdims=True) + EPSILON)
        normed = hidden_state * scale
        product = grad_routed * normed
        grad = scale * (
            grad_routed * gains - normed * jnp.mean(product * gains, axis=1, keepdims=True)
        ) + grad_output
        grad_hidden[here, :] = grad
        branches[grid.fsdp, here, :] = grad.astype(BF16)
        mine = branches.at[grid.fsdp, here, :]
        for hop in range(1, grid.x_size):
            along_x.append(
                links.copy(
                    mine, mine, (grid.exp, grid.x_from(hop)),
                    branches.at[grid.x_from(-hop), here, :],
                )
            )
            along_x[-1][0].start()
        across.append(
            links.copy(mine, mine, (grid.exp, sibling), branches.at[sibling, here, :])
        )
        across[-1][0].start()
        gain_grad = gain_grad + jnp.sum(product, axis=0, keepdims=True)
        small_t = small_t + matmul(grad_logits.T.astype(BF16), routed[here, :])

    def context_grad(place):
        branch = branches[place]
        grad = contract_last(own_out[...], branch).astype(BF16)
        columns_here = pl.ds(pl.multiple_of(place * rows, 128), rows)
        rows_here = pl.ds(pl.multiple_of(place * rows, 16), rows)
        for head in range(heads):
            piece = grad[head * width : (head + 1) * width]
            grad_t[head, :, columns_here] = piece
            grad_n[head, rows_here, :] = turned(piece).astype(BF16)
        total[...] += matmul(context[place], branch)

    total[...] = jnp.zeros_like(total)
    fetch.wait()
    context_grad(grid.fsdp)
    forwards = []
    for half in range(2):
        here = slice(half * half_rows, (half + 1) * half_rows)
        for hop in range(1, grid.x_size):
            along_x[half * (grid.x_size - 1) + hop - 1][1].wait_recv()
            held = grid.x_from(-hop)
            forwards.append(
                links.copy(
                    branches.at[held, here, :], branches.at[held, here, :], (grid.exp, sibling),
                    branches.at[grid.sibling(held), here, :],
                )
            )
            forwards[-1][0].start()
    row = lax.broadcasted_iota(jnp.int32, small_t.shape, 0)
    small[...] = jnp.where(row == lanes.gain, gain_grad, small_t).T
    for _, coming in across:
        coming.wait_recv()
    context_grad(sibling)
    for hop in range(1, grid.x_size):
        context_grad(grid.x_from(-hop))
    for _, coming in forwards:
        coming.wait_recv()
    for hop in range(1, grid.x_size):
        context_grad(grid.sibling(grid.x_from(-hop)))
    grad_out[...] = total[...].astype(BF16)
    for going, _ in along_x + across + forwards:
        going.wait_send()


def project_back_kernel(
    grad_projected, normed, plane, small, probabilities, grad_bias, grad_first, grad_plane, total,
    bias_t, *, lanes, heads, feature_rows, bucket_rows,
):
    step = pl.program_id(0)

    @pl.when(step == 0)
    def _():
        total[...] = jnp.zeros_like(total)

    grad = grad_projected[...]
    grad_first[0] = matmul(plane[:, : lanes.weights], grad).astype(BF16)
    total[: lanes.weights, :] += matmul(grad, normed[...])

    @pl.when(step == pl.num_programs(0) - 1)
    def _():
        grad_plane[...] = total[...].T.astype(BF16)
        span = grad_bias.shape[2]
        select, _ = bucket_rows_select(plane.shape[0], feature_rows, bucket_rows, span)
        bias_t[...] = jnp.zeros_like(bias_t)
        first = lanes.table + lax.axis_index("fsdp") * heads
        for head in range(heads):
            bias_t[pl.ds(first + head, 1), :] = grad_bias[head]
        high = bias_t[...].astype(BF16)
        rest = (bias_t[...] - high.astype(F32)).astype(BF16)
        table = contract_last(select, high) + contract_last(select, rest)
        mass = jnp.sum(probabilities[...], axis=0, keepdims=True)
        mass = pltpu.roll(jnp.broadcast_to(mass, (8, lanes.extra)), lanes.shift, 1)[0:1]
        lane = lax.broadcasted_iota(jnp.int32, table.shape, 1)
        row = lax.broadcasted_iota(jnp.int32, table.shape, 0)
        is_small = (lane >= lanes.router) & (lane < lanes.table)
        is_mass = (lane >= lanes.count) & (lax.rem(row, feature_rows) == 0)
        extra = table + jnp.where(is_small, small[...], 0.0) + jnp.where(is_mass, mass, 0.0)
        grad_plane[:, lanes.base :] = (total[lanes.base :, :].T + extra).astype(BF16)


def last_kernel(
    first, planes, out_grad, hidden, gates, columns, rows_back, first_parts, output, plane_parts,
    out_parts, first_in, first_sum, planes_in, plane_sum, along_in, reduced, send, receive, own,
    *, spread_out, local,
):
    grid = Grid().here()
    links = Links(send, receive)
    z_size, y_size, x_size, fsdp_size = grid.z_size, grid.y_size, grid.x_size, grid.fsdp_size
    exp_size = grid.exp_size
    sibling = grid.sibling(grid.fsdp)
    near = [
        (grid.exp, (grid.fsdp + turn) % fsdp_size) for turn in range(1, fsdp_size)
    ] + [grid.at(z=(grid.z + hop) % z_size) for hop in range(1, z_size)]
    beside = [grid.at(y=(grid.y + hop) % y_size) for hop in range(1, y_size)]

    per_sender = grid.device_count if spread_out else exp_size
    base = 0 if spread_out else grid.fsdp * exp_size
    out_sends = []
    for number in range(per_sender):
        to = base + number
        out_sends.append((to, number))
    if spread_out:
        out_origins = [(origin, origin) for origin in range(grid.device_count)]
    else:
        out_origins = [
            (member * fsdp_size + grid.linear // exp_size, member) for member in range(exp_size)
        ]
    own_slot = grid.linear if spread_out else grid.exp
    out_base = links.used
    links.used += per_sender

    def place_of(linear):
        return (linear // fsdp_size, linear % fsdp_size)

    def out_copy(to, number, slot):
        return pltpu.make_async_remote_copy(
            src_ref=out_grad.at[number], dst_ref=out_parts.at[slot],
            send_sem=send.at[out_base + number], recv_sem=receive.at[out_base + slot],
            device_id=place_of(to), device_id_type=MESH,
        )

    barrier = pltpu.get_barrier_semaphore()
    for device in near + beside:
        pl.semaphore_signal(barrier, inc=1, device_id=device, device_id_type=MESH)
    for origin, _ in out_origins:

        @pl.when(origin != grid.linear)
        def _(origin=origin):
            pl.semaphore_signal(
                barrier, inc=1, device_id=place_of(origin), device_id_type=MESH
            )

    to_self = (
        1 if spread_out else jnp.where(grid.linear // exp_size == grid.fsdp, 1, 0)
    )
    pl.semaphore_wait(barrier, len(near) + len(beside) + per_sender - to_self)

    first_copies = []
    for hop in range(x_size):
        mine = grid.x_from(hop)
        first_copies.append(
            links.copy(
                first.at[grid.sibling(mine)], first_in.at[hop], (grid.exp, sibling), first_in.at[hop]
            )
        )
        first_copies[-1][0].start()
    z_hops = list(range(1, z_size)) + [0]
    beside_copies = []
    for z_hop in z_hops:
        beside_copies.append([])
        for hop in range(1, y_size):
            to = (grid.y + hop) % y_size
            landing = planes_in.at[hop - 1, z_hop]
            beside_copies[-1].append(
                links.copy(
                    planes.at[(grid.z + z_hop) % z_size, to], landing, grid.at(y=to), landing
                )
            )
            beside_copies[-1][-1][0].start()
    along_x = []
    for hop in range(x_size):
        first_copies[hop][1].wait_recv()
        summed = first[grid.x_from(hop)].astype(F32) + first_in[hop].astype(F32)
        if hop == 0:
            first_parts[0] = summed.astype(BF16)
        else:
            first_sum[hop - 1] = summed.astype(BF16)
            along_x.append(
                links.copy(
                    first_sum.at[hop - 1], first_parts.at[hop], (grid.exp, grid.x_from(hop)),
                    first_parts.at[hop],
                )
            )
            along_x[-1][0].start()
    along_z = []
    for z_hop, copies in zip(z_hops, beside_copies):
        to_z = (grid.z + z_hop) % z_size
        summed = planes[to_z, grid.y].astype(F32)
        for number, (_, coming) in enumerate(copies):
            coming.wait_recv()
            summed = summed + planes_in[number, z_hop].astype(F32)
        plane_sum[z_hop] = summed.astype(BF16)
        if z_hop > 0:
            along_z.append(
                links.copy(
                    plane_sum.at[z_hop], along_in.at[z_hop - 1], grid.at(z=to_z),
                    along_in.at[z_hop - 1],
                )
            )
            along_z[-1][0].start()
    for to, number in out_sends:

        @pl.when(to != grid.linear)
        def _(to=to, number=number):
            out_copy(to, number, own_slot).start()

        @pl.when(to == grid.linear)
        def _(number=number):
            pltpu.make_async_copy(out_grad.at[number], out_parts.at[own_slot], own.at[0]).start()

    mix_rows(hidden, gates, columns, rows_back, output, local)
    summed = plane_sum[0].astype(F32)
    for number, (_, coming) in enumerate(along_z):
        coming.wait_recv()
        summed = summed + along_in[number].astype(F32)
    reduced[...] = summed.astype(BF16)
    placed = []
    for turn in range(1, fsdp_size):
        to = (grid.fsdp + turn) % fsdp_size
        origin = (grid.fsdp + fsdp_size - turn) % fsdp_size
        placed.append(
            links.copy(
                reduced.at[to], plane_parts.at[grid.fsdp], (grid.exp, to), plane_parts.at[origin]
            )
        )
        placed[-1][0].start()
    kept = pltpu.make_async_copy(reduced.at[grid.fsdp], plane_parts.at[grid.fsdp], own.at[1])
    kept.start()
    for going, coming in along_x + placed:
        coming.wait_recv()
    for going, _ in first_copies + along_x + along_z + placed:
        going.wait_send()
    for copies in beside_copies:
        for going, _ in copies:
            going.wait_send()
    kept.wait()
    for origin, slot in out_origins:

        @pl.when(origin != grid.linear)
        def _(origin=origin, slot=slot):
            out_copy(origin, 0, slot).wait_recv()

    for to, number in out_sends:

        @pl.when(to != grid.linear)
        def _(to=to, number=number):
            out_copy(to, number, own_slot).wait_send()

        @pl.when(to == grid.linear)
        def _(number=number):
            pltpu.make_async_copy(out_grad.at[number], out_parts.at[own_slot], own.at[0]).wait()


def mix_rows(hidden, gates, columns, rows_in, output, local):
    members, _, capacity, model_width = rows_in.shape
    routes, slots = int_columns(columns)
    total = hidden[...]
    picked = [jnp.zeros(hidden.shape, F32), jnp.zeros(hidden.shape, F32)]
    for index in range(local):
        picks = local_picks(routes, slots, capacity, local, index, members * capacity)
        values = rows_in[:, index].reshape(members * capacity, model_width)
        for k in range(2):
            picked[k] = picked[k] + matmul(jnp.where(picks[k], 1.0, 0.0).astype(BF16), values)
    for k in range(2):
        total = total + gates[:, k : k + 1] * picked[k]
    output[...] = total.astype(BF16)


def finish_kernel(
    first_parts, plane_parts, out_parts, tokens, grad_hidden, attention_in, attention_gain, counts,
    grad_tokens, grad_gain, grad_in, grad_out, grad_mixture, grad_router, grad_table, balance,
    *, lanes, heads, width, head_count, experts, token_total,
):
    total = jnp.sum(first_parts[...].astype(F32), axis=0).T
    inputs = tokens[...].astype(F32)
    scale = lax.rsqrt(jnp.mean(inputs * inputs, axis=1, keepdims=True) + EPSILON)
    normed = inputs * scale
    grad_tokens[...] = grad_hidden[...] + scale * (
        total - normed * jnp.mean(total * normed, axis=1, keepdims=True)
    )
    fsdp_size = plane_parts.shape[0]
    model_width = head_count * width
    sums = [plane_parts[place].astype(F32) for place in range(fsdp_size)]
    columns = []
    for kind in range(3):
        pieces = [
            sums[place][:, kind * heads * width : (kind + 1) * heads * width]
            for place in range(fsdp_size)
        ]
        columns.append(jnp.concatenate(pieces, axis=1)[:, :model_width])
    gathered = jnp.concatenate(columns, axis=1)
    feature_rows = gathered.shape[0]
    gain = jnp.sum(gathered * attention_in[...].astype(F32), axis=1, keepdims=True)
    gain = padded_rows(jnp.broadcast_to(gain, (feature_rows, 128)), 128).T
    grad_gain[...] = gain[0:1, :feature_rows]
    grad_in[...] = gathered * as_column(attention_gain[...], feature_rows)
    grad_out[...] = jnp.sum(out_parts[...].astype(F32), axis=0)
    extra = sum(part[:, lanes.base :] for part in sums)
    extra_t = padded_rows(extra, 128).T
    grad_mixture[...] = extra_t[lanes.gain : lanes.gain + 1, :feature_rows]
    grad_router[...] = extra_t[lanes.router : lanes.router + experts, :feature_rows]
    grad_table[...] = extra[: grad_table.shape[0], lanes.table : lanes.table + head_count]
    mass = jnp.broadcast_to(extra[0:1], (8, lanes.extra))
    mass = pltpu.roll(mass, lanes.extra - lanes.shift, 1)
    lane = expert_lane(mass.shape, lanes)
    terms = jnp.where((lane >= 0) & (lane < experts), mass * counts[...], 0.0)[0:1]
    balance[...] = jnp.sum(terms, axis=1, keepdims=True) * (
        experts / (2.0 * token_total * token_total)
    )


def sum_kernel(*refs, layout, local):
    outputs = refs[len(layout) :]
    early_blocks = pl.num_programs(0) // 2
    totals = {}
    number = 0
    while number < len(layout):
        index, which, halves = layout[number]
        shape = outputs[which].shape[1:]
        value = refs[number][...].reshape(shape).astype(F32)
        if halves:
            rest = refs[number + 1][...].reshape(shape).astype(F32)
            value = jnp.where(pl.program_id(0) < early_blocks, value, rest)
            number += 1
        totals[index, which] = totals[index, which] + value if (index, which) in totals else value
        number += 1
    for (index, which), total in totals.items():
        outputs[which][index] = total


def sum_grads(groups, up_shape, down_shape, blocks):
    local = len(groups)
    depth, part = up_shape[1], down_shape[1]
    sizes = ((depth, part), (part // blocks, down_shape[2]))
    arrays, specs, layout = [], [], []
    early = blocks // 2
    for index, group in enumerate(groups):
        for which, (size, (keep, taken, passed)) in enumerate(zip(sizes, group)):
            for array in (keep, taken, *passed):
                if isinstance(array, tuple):
                    arrays.extend(array)
                    specs.append(pl.BlockSpec(size, lambda c: (jnp.minimum(c, early - 1), 0)))
                    specs.append(pl.BlockSpec(size, lambda c: (jnp.maximum(c - early, 0), 0)))
                    layout.extend([(index, which, True)] * 2)
                else:
                    arrays.append(array)
                    specs.append(pl.BlockSpec(size, lambda c: (c, 0)))
                    layout.append((index, which, False))
    return pl.pallas_call(
        partial(sum_kernel, layout=layout, local=local),
        grid=(blocks,),
        in_specs=specs,
        out_specs=[
            pl.BlockSpec((local, depth, part), lambda c: (0, 0, c)),
            pl.BlockSpec((local, part // blocks, down_shape[2]), lambda c: (0, c, 0)),
        ],
        out_shape=(shape_of(up_shape, F32), shape_of(down_shape, F32)),
        compiler_params=params(),
        cost_estimate=hint(8),
        name="sum_grads",
    )(*arrays)


def over_x(array, hop):
    fsdp_size = lax.axis_size("fsdp")
    return lax.ppermute(array, "fsdp", [(i, (i + 2 * hop) % fsdp_size) for i in range(fsdp_size)])


def over_core(array):
    return lax.ppermute(array, "fsdp", [(i, i ^ 1) for i in range(lax.axis_size("fsdp"))])


def on_device(
    tokens,
    cotangent,
    segments,
    routes,
    slots,
    attention_gain,
    mixture_gain,
    attention_in,
    attention_out,
    router_weight,
    position_table,
    expert_up,
    expert_down,
):
    grid = Grid()
    exp_size, fsdp_size, chips = grid.exp_size, grid.fsdp_size, grid.x_size
    device_count = grid.device_count
    fsdp_index = lax.axis_index("fsdp")
    rows, model_width = tokens.shape
    length = rows * fsdp_size
    head_count = position_table.shape[1]
    width = model_width // head_count
    heads = -(-head_count // fsdp_size)
    padded_heads = heads * fsdp_size
    feature_rows, bucket_rows = attention_in.shape[0], position_table.shape[0]
    experts = router_weight.shape[1]
    local = expert_up.shape[0]
    capacity = 4 * rows // experts
    token_total = rows * device_count
    span = WINDOW + 2 * SKEW + QUERY_BLOCK
    lanes = Lanes(heads, width, padded_heads, experts)
    part = expert_down.shape[1]
    gain_row = attention_gain.reshape(1, feature_rows)
    late_rows = 2 * capacity // 3 if local > 1 and capacity % 48 == 0 else 0
    late = 1 if late_rows else 0

    shard_shapes = [shape_of((model_width, part), BF16), shape_of((part, model_width), BF16)]
    copies = (
        4 * fsdp_size + grid.z_size + grid.z_size * grid.y_size
        + grid.z_size + grid.y_size + grid.x_size + 1
    )
    started = pl.pallas_call(
        partial(
            start_kernel, lanes=lanes, heads=heads, width=width, head_count=head_count,
            experts=experts, capacity=capacity, local=local, late=late,
        ),
        out_shape=tuple(
            [
                shape_of((fsdp_size, rows, model_width), BF16),
                shape_of((grid.z_size, grid.y_size, fsdp_size, feature_rows, lanes.width), BF16),
                shape_of((exp_size, local * capacity - late_rows, model_width), BF16),
                shape_of((8, rows), F32),
                shape_of((rows, 128), F32),
                shape_of((grid.z_size, grid.y_size, chips, 2, feature_rows, model_width), BF16),
            ]
            + [shape_of((exp_size, late_rows, model_width), BF16)] * late
            + shard_shapes * local
        ),
        in_specs=[IN_VMEM] * 10 + [ANYWHERE] * 2,
        out_specs=tuple(
            [ANYWHERE, ANYWHERE, IN_VMEM, IN_VMEM, IN_VMEM, ANYWHERE]
            + [IN_VMEM] * late
            + [ANYWHERE] * (2 * local)
        ),
        scratch_shapes=[
            pltpu.VMEM((fsdp_size, feature_rows, lanes.width), BF16),
            pltpu.VMEM(expert_up.shape, BF16),
            pltpu.VMEM(expert_down.shape, BF16),
            dma_sems(copies),
            dma_sems(copies),
            dma_sems(3),
            dma_sems(2 * local),
            dma_sems(local * (fsdp_size + 1)),
        ],
        compiler_params=params(collective_id=0, has_side_effects=True),
        cost_estimate=hint(20),
        name="start",
    )(
        tokens, cotangent, routes.T, slots.T, gain_row, mixture_gain.reshape(1, feature_rows),
        attention_in, router_weight.T, position_table, attention_out, expert_up, expert_down,
    )
    all_tokens, all_planes, cotangent_early, position_rows, columns, full_out = started[:6]
    cotangent_late, started = started[6 : 6 + late], started[6 + late :]
    own_shards = [started[2 * index : 2 * index + 2] for index in range(local)]
    plane = all_planes.reshape(model_width, lanes.width)
    full_out = full_out.reshape(model_width, model_width)

    def along_x(array):
        return [over_x(array, -hop) for hop in range(1, chips)]

    near_up, near_down = [None] * local, [None] * local
    near_up[0] = along_x(own_shards[0][0])
    cotangent_in = lax.all_to_all(
        cotangent_early, "exp", split_axis=0, concat_axis=0, tiled=True
    )

    head_t = lambda size: pl.BlockSpec((heads, size, rows), lambda s, *_: (0, 0, s))
    head_n = lambda size: pl.BlockSpec((heads, rows, size), lambda s, *_: (0, s, 0))
    normed, query_t, key_n, query_n, value_n, key_t, value_t, bias, counts = pl.pallas_call(
        partial(
            project_kernel, heads=heads, width=width, lanes=lanes, feature_rows=feature_rows,
            bucket_rows=bucket_rows,
        ),
        grid=(fsdp_size,),
        in_specs=[
            pl.BlockSpec((1, rows, model_width), lambda s: (s, 0, 0)),
            whole((model_width, lanes.width)),
            pl.BlockSpec((1, rows), lambda s: (0, s)),
        ],
        out_specs=[
            pl.BlockSpec((rows, model_width), lambda s: (s, 0)),
            head_t(SKEW), head_n(SKEW), head_n(width), head_n(width), head_t(width), head_t(width),
            whole((heads, 1, span)),
            whole((8, lanes.extra)),
        ],
        out_shape=(
            shape_of((length, model_width), BF16),
            shape_of((heads, SKEW, length), BF16),
            shape_of((heads, length, SKEW), BF16),
            shape_of((heads, length, width), BF16),
            shape_of((heads, length, width), BF16),
            shape_of((heads, width, length), BF16),
            shape_of((heads, width, length), BF16),
            shape_of((heads, 1, span), F32),
            shape_of((8, lanes.extra), F32),
        ),
        scratch_shapes=[
            pltpu.VMEM((lanes.weights, model_width), BF16),
            pltpu.VMEM((lanes.extra, span), F32),
        ],
        compiler_params=params(),
        cost_estimate=hint(8),
        name="project",
    )(all_tokens, plane, segments.reshape(1, length))

    by_head = lambda *size: pl.BlockSpec((1,) + size, lambda h: (h, 0, 0))
    context, context_high, log_total, attended_t = pl.pallas_call(
        partial(attend_kernel, rows=rows),
        grid=(heads,),
        in_specs=[
            by_head(SKEW, length), by_head(length, SKEW), by_head(width, length), by_head(1, span),
        ],
        out_specs=[
            pl.BlockSpec((fsdp_size, width, rows), lambda h: (0, h, 0)),
            by_head(width, length),
            by_head(1, length),
            ANYWHERE,
        ],
        out_shape=(
            shape_of((fsdp_size, heads * width, rows), BF16),
            shape_of((heads, width, length), F32),
            shape_of((heads, 1, length), F32),
            shape_of((fsdp_size, heads * width, rows), BF16),
        ),
        scratch_shapes=[
            pltpu.VMEM((SKEW, span), F32),
            pltpu.VMEM((WINDOW + QUERY_BLOCK, QUERY_BLOCK), F32),
            pltpu.VMEM((heads, fsdp_size, width, rows), BF16),
            pltpu.SemaphoreType.DMA((heads, fsdp_size)),
            pltpu.SemaphoreType.DMA((heads, fsdp_size)),
            dma_sems(heads),
        ],
        compiler_params=params(collective_id=1, has_side_effects=True),
        cost_estimate=hint(13),
        name="attend",
    )(query_t, key_n, value_t, bias)

    own_down, near_up[0], attended_t = lax.optimization_barrier(
        (own_shards[0][1], near_up[0], attended_t)
    )
    near_down[0] = along_x(own_down)
    attended_t = attended_t.reshape(padded_heads * width, rows)

    later = [own_shards[index] for index in range(1, local)]
    attended_t, later = lax.optimization_barrier((attended_t, later))
    for index in range(1, local):
        near_up[index], near_down[index] = [along_x(array) for array in later[index - 1]]
    gate_lanes = -(-local * capacity // 128) * 128
    ready = [own_shards[0][0]] + near_up[0] + [own_shards[0][1]]
    copies = 2 * exp_size + len(ready)
    hidden, routed, probabilities, gates, outgoing, rows_in, gates_in, *crossed = pl.pallas_call(
        partial(
            route_kernel, experts=experts, lanes=lanes, capacity=capacity, crossing=len(ready)
        ),
        in_specs=[IN_VMEM] * 6 + [ANYWHERE] * len(ready),
        out_specs=tuple([IN_VMEM] * 5 + [ANYWHERE] * (2 + len(ready))),
        out_shape=tuple(
            [
                shape_of((rows, model_width), F32),
                shape_of((rows, model_width), BF16),
                shape_of((rows, lanes.extra), F32),
                shape_of((rows, 2), F32),
                shape_of((exp_size, local * capacity, model_width), BF16),
                shape_of((exp_size, capacity, model_width), BF16),
                shape_of((exp_size, 8, gate_lanes), F32),
            ]
            + [shape_of(array.shape, BF16) for array in ready]
        ),
        scratch_shapes=[
            pltpu.VMEM((exp_size, 8, gate_lanes), F32),
            dma_sems(copies),
            dma_sems(copies),
            dma_sems(2),
        ],
        compiler_params=params(collective_id=2, has_side_effects=True),
        cost_estimate=hint(35),
        name="route",
    )(tokens, attended_t, full_out, plane, columns, position_rows, *ready)
    outgoing = outgoing.reshape(exp_size, local, capacity, model_width)

    def down_parts(early, rest):
        return list(zip(early, rest))

    def pass_along(arrays):
        return [over_x(arrays[0][hop - 1], hop) for hop in range(1, chips)]

    swapped = (crossed[:-1], crossed[-1:])
    returned, groups, moved, outs = [], [], [], None
    late_rows_in = ()
    for index in range(local):
        final = index == local - 1
        carried = list(moved)
        if not final:
            carried.append((outgoing, index + 1))
        if index == 0 and late:
            carried.append((cotangent_late[0], None))
        result = run_expert(
            index, local, rows_in, gates_in, cotangent_in, late_rows_in if final else (),
            [own_shards[index][0]] + near_up[index], [own_shards[index][1]] + near_down[index],
            swapped, () if final else own_shards[index + 1], carried, outs, 3 + index,
        )
        (outs,) = result.rows_out
        arrived = list(result.moved_to)
        if index == 0 and late:
            late_rows_in = (arrived.pop(),)
        if not final:
            rows_in = arrived.pop()
            swapped = (result.next_swapped[:1], result.next_swapped[1:])
            moved = [(result.grad_rows[0], None), (result.grad_gates[0], None)]
        if arrived:
            returned.append(arrived)
        up_keep, up_taken, down_keep, down_taken = result.own
        if not final:
            passed = (result.pass_up, result.early_down, result.pass_down)
            passed, rows_in = lax.optimization_barrier((passed, rows_in))
            groups.append(
                [
                    (up_keep, up_taken, pass_along(passed[0])),
                    (
                        down_keep, down_taken,
                        down_parts(pass_along(passed[1]), pass_along(passed[2])),
                    ),
                ]
            )
    returned.append([result.back_rows[0], result.back_gates[0]])
    groups, returned = lax.optimization_barrier((groups, returned))

    outs, returned = lax.optimization_barrier((outs, returned))
    out_rows = lax.all_to_all(outs, "exp", split_axis=0, concat_axis=0, tiled=True)

    padded_out = full_out
    if padded_heads > head_count:
        padded_out = jnp.pad(full_out, ((0, padded_heads * width - model_width), (0, 0)))
    copies = 2 * 2 * fsdp_size
    grad_hidden, small, grad_t, grad_n, out_grad = pl.pallas_call(
        partial(
            unroute_kernel, experts=experts, local=local, token_total=token_total, lanes=lanes,
            heads=heads, width=width,
        ),
        out_shape=(
            shape_of((rows, model_width), F32),
            shape_of((model_width, lanes.extra), F32),
            shape_of((heads, width, length), BF16),
            shape_of((heads, length, width), BF16),
            shape_of((heads * width, model_width), BF16),
        ),
        in_specs=[IN_VMEM] * 8 + [ANYWHERE] + [IN_VMEM] * (1 + 2 * local),
        out_specs=tuple([IN_VMEM] * 5),
        scratch_shapes=[
            pltpu.VMEM((fsdp_size, rows, model_width), BF16),
            pltpu.VMEM((heads * width, model_width), BF16),
            pltpu.VMEM((heads * width, model_width), F32),
            dma_sems(copies),
            dma_sems(copies),
            dma_sems(1),
        ],
        compiler_params=params(collective_id=4 + local, has_side_effects=True),
        cost_estimate=hint(1),
        name="unroute",
    )(
        hidden, cotangent, routed, probabilities, gates, plane, columns, counts, padded_out, context,
        *[part[0] for part in returned], *[part[1] for part in returned],
    )
    early = pass_along(result.early_down)
    early, pass_up, pass_down, grad_t = lax.optimization_barrier(
        (early, result.pass_up, result.pass_down, grad_t)
    )
    groups.append(
        [
            (up_keep, up_taken, pass_along(pass_up)),
            (down_keep, down_taken, down_parts(early, pass_along(pass_down))),
        ]
    )

    grad_projected, grad_bias = pl.pallas_call(
        partial(attend_back_kernel, scale=width ** (-0.5)),
        grid=(heads,),
        in_specs=[
            by_head(SKEW, length), by_head(length, SKEW), by_head(length, width),
            by_head(length, width), by_head(width, length), by_head(width, length),
            by_head(length, width), by_head(width, length), by_head(1, length), by_head(1, span),
        ],
        out_specs=[
            pl.BlockSpec((3, 1, width, length), lambda h: (0, h, 0, 0)),
            by_head(1, span),
        ],
        out_shape=(
            shape_of((3, heads, width, length), BF16),
            shape_of((heads, 1, span), F32),
        ),
        scratch_shapes=[
            pltpu.VMEM((SKEW, span), F32),
            pltpu.VMEM((SKEW, span), F32),
            pltpu.VMEM((length, width), F32),
            pltpu.VMEM((length, width), F32),
        ],
        compiler_params=params(),
        cost_estimate=hint(1),
        name="attend_back",
    )(query_t, key_n, query_n, value_n, key_t, grad_t, grad_n, context_high, log_total, bias)
    grad_projected = grad_projected.reshape(lanes.weights, length)

    grad_first, grad_plane = pl.pallas_call(
        partial(
            project_back_kernel, lanes=lanes, heads=heads, feature_rows=feature_rows,
            bucket_rows=bucket_rows,
        ),
        grid=(fsdp_size,),
        in_specs=[
            pl.BlockSpec((lanes.weights, rows), lambda s: (0, s)),
            pl.BlockSpec((rows, model_width), lambda s: (s, 0)),
            whole((model_width, lanes.width)),
            whole((model_width, lanes.extra)),
            whole((rows, lanes.extra)),
            whole((heads, 1, span)),
        ],
        out_specs=[
            pl.BlockSpec((1, model_width, rows), lambda s: (s, 0, 0)),
            whole((model_width, lanes.width)),
        ],
        out_shape=(
            shape_of((fsdp_size, model_width, rows), BF16),
            shape_of((model_width, lanes.width), BF16),
        ),
        scratch_shapes=[
            pltpu.VMEM((lanes.width, model_width), F32),
            pltpu.VMEM((lanes.extra, span), F32),
        ],
        compiler_params=params(),
        cost_estimate=hint(1),
        name="project_back",
    )(grad_projected, normed, plane, small, probabilities, grad_bias)

    out_rows, grad_first = lax.optimization_barrier((out_rows, grad_first))
    spread_out = heads * width * fsdp_size != model_width
    if spread_out:
        out_grad = lax.dynamic_update_slice(
            jnp.zeros((padded_heads * width, model_width), BF16), out_grad,
            (fsdp_index * heads * width, jnp.int32(0)),
        )[:model_width]
    out_grad = out_grad.reshape(-1, feature_rows, model_width)
    out_count = device_count if spread_out else exp_size
    plane_shape = (grid.z_size, grid.y_size, fsdp_size, feature_rows, lanes.width)
    parts_shape = (fsdp_size, feature_rows, lanes.width)
    copies = 3 * fsdp_size + grid.z_size * grid.y_size + grid.z_size + out_count
    first_parts, layer_output, plane_parts, out_parts = pl.pallas_call(
        partial(last_kernel, spread_out=spread_out, local=local),
        out_shape=(
            shape_of((chips, model_width, rows), BF16),
            shape_of((rows, model_width), BF16),
            shape_of(parts_shape, BF16),
            shape_of((out_count, feature_rows, model_width), BF16),
        ),
        in_specs=[IN_VMEM] * 7,
        out_specs=(IN_VMEM, IN_VMEM, ANYWHERE, ANYWHERE),
        scratch_shapes=[
            pltpu.VMEM((chips, model_width, rows), BF16),
            pltpu.VMEM((max(chips - 1, 1), model_width, rows), BF16),
            pltpu.VMEM((max(grid.y_size - 1, 1), grid.z_size) + parts_shape, BF16),
            pltpu.VMEM((grid.z_size,) + parts_shape, BF16),
            pltpu.VMEM((max(grid.z_size - 1, 1),) + parts_shape, BF16),
            pltpu.VMEM(parts_shape, BF16),
            dma_sems(copies),
            dma_sems(copies),
            dma_sems(2),
        ],
        compiler_params=params(collective_id=5 + local, has_side_effects=True),
        cost_estimate=hint(1),
        name="last",
    )(grad_first, grad_plane.reshape(plane_shape), out_grad, hidden, gates, columns, out_rows)

    groups, first_parts = lax.optimization_barrier((groups, first_parts))
    (
        grad_tokens, gain_grad, in_grad, out_sum, mixture_gain_grad, router_grad, table_grad, balance,
    ) = pl.pallas_call(
        partial(
            finish_kernel, lanes=lanes, heads=heads, width=width, head_count=head_count,
            experts=experts, token_total=token_total,
        ),
        out_shape=(
            shape_of((rows, model_width), F32),
            shape_of((1, feature_rows), F32),
            shape_of((feature_rows, 3 * model_width), F32),
            shape_of((feature_rows, model_width), F32),
            shape_of((1, feature_rows), F32),
            shape_of((experts, feature_rows), F32),
            shape_of((bucket_rows, head_count), F32),
            shape_of((1, 1), F32),
        ),
        compiler_params=params(),
        cost_estimate=hint(6),
        name="finish",
    )(first_parts, plane_parts, out_parts, tokens, grad_hidden, attention_in, gain_row, counts)

    up_grad, down_grad = sum_grads(groups, expert_up.shape, expert_down.shape, fsdp_size)
    return (
        layer_output,
        balance.reshape(()),
        grad_tokens,
        gain_grad.reshape(feature_rows),
        mixture_gain_grad.reshape(feature_rows),
        in_grad,
        out_sum,
        router_grad.T,
        table_grad,
        up_grad,
        down_grad,
    )


def solution(mesh):
    in_specs = (
        P(("exp", "fsdp"), None),
        P(("exp", "fsdp"), None),
        P("exp"),
        P(("exp", "fsdp"), None),
        P(("exp", "fsdp"), None),
        P(("exp", "fsdp")),
        P(("exp", "fsdp")),
        P(("exp", "fsdp"), None),
        P(("exp", "fsdp"), None),
        P(("exp", "fsdp"), None),
        P(("exp", "fsdp"), None),
        P("exp", "fsdp", None),
        P("exp", "fsdp", None),
    )
    out_specs = (
        P(("exp", "fsdp"), None),
        P(),
        P(("exp", "fsdp"), None),
        P(("exp", "fsdp")),
        P(("exp", "fsdp")),
        P(("exp", "fsdp"), None),
        P(("exp", "fsdp"), None),
        P(("exp", "fsdp"), None),
        P(("exp", "fsdp"), None),
        P("exp", "fsdp", None),
        P("exp", "fsdp", None),
    )
    return jax.shard_map(
        on_device, mesh=mesh, in_specs=in_specs, out_specs=out_specs, check_vma=False
    )
```

```python
from functools import partial

import jax
import jax.numpy as jnp
from jax import lax
from jax.experimental import pallas as pl
from jax.experimental.pallas import tpu as pltpu
from jax.sharding import PartitionSpec as P

WINDOW = 1024
BUCKETS = 256

EPSILON = 1e-06
AUX_WEIGHT = 0.01
MASKED = -1e30
QUERY_BLOCK = 256
SKEW = 128
VMEM_BYTES = 58 * 1024 * 1024
MESH = pl.DeviceIdType.MESH
F32 = jnp.float32
BF16 = jnp.bfloat16


def params(**kwargs):
    return pltpu.CompilerParams(vmem_limit_bytes=VMEM_BYTES, **kwargs)


def shape_of(shape, dtype):
    return jax.ShapeDtypeStruct(shape, dtype)


def whole(shape):
    return pl.BlockSpec(shape, lambda *_: (0,) * len(shape))


def contract_last(left_side, right_side):
    return lax.dot_general(
        left_side, right_side, (((1,), (1,)), ((), ())), preferred_element_type=F32
    )


def matmul(left_side, right_side):
    return jnp.dot(left_side, right_side, preferred_element_type=F32)


def turned(value):
    return value.astype(F32).T


def bucket_index(distance):
    near_count = BUCKETS // 2
    spread = max(WINDOW - near_count, 1)
    far_bucket = (
        near_count + jnp.maximum(distance - near_count, 0) * (BUCKETS - near_count) // spread
    )
    return jnp.where(distance < near_count, distance, far_bucket)

def hint(micros):
    return pl.CostEstimate(flops=int(micros * 1.0e9), bytes_accessed=1024, transcendentals=0)


def flipped(place, other, size):
    result, bit = 0, 1
    while bit < size:
        result = result + bit * ((place // bit + other // bit) % 2)
        bit *= 2
    return result


class Grid:
    def __init__(self):
        self.exp_size, self.fsdp_size = lax.axis_size("exp"), lax.axis_size("fsdp")
        self.device_count = self.exp_size * self.fsdp_size
        self.y_size = max(
            y for y in range(1, self.exp_size + 1) if self.exp_size % y == 0 and 2 * y * y <= self.exp_size
        ) if self.exp_size > 1 else 1
        self.z_size = self.exp_size // self.y_size
        self.x_size = self.fsdp_size // 2

    def here(self):
        self.exp, self.fsdp = lax.axis_index("exp"), lax.axis_index("fsdp")
        self.z, self.y = self.exp // self.y_size, self.exp % self.y_size
        self.x, self.core = self.fsdp // 2, self.fsdp % 2
        self.linear = self.exp * self.fsdp_size + self.fsdp
        return self

    def at(self, z=None, y=None, fsdp=None):
        z = self.z if z is None else z
        y = self.y if y is None else y
        return (z * self.y_size + y, self.fsdp if fsdp is None else fsdp)

    def x_from(self, hop):
        return ((self.x + self.x_size + hop) % self.x_size) * 2 + self.core

    def source_z(self, turn):
        if self.z_size & (self.z_size - 1) == 0:
            return flipped(self.z, turn, self.z_size)
        return (self.z + turn) % self.z_size

    def target_z(self, turn):
        if self.z_size & (self.z_size - 1) == 0:
            return flipped(self.z, turn, self.z_size)
        return (self.z + self.z_size - turn) % self.z_size

    def exp_steps(self):
        turns = sorted(range(self.z_size), key=lambda turn: -turn.bit_length())
        steps = []
        for turn in turns:
            for hop in range(self.y_size):
                if turn or hop:
                    to = self.target_z(turn) * self.y_size + (self.y + self.y_size - hop) % self.y_size
                    origin = self.source_z(turn) * self.y_size + (self.y + hop) % self.y_size
                    steps.append((to, origin))
        return steps

    def sibling(self, fsdp):
        return fsdp + 1 - 2 * (fsdp % 2)


class Links:
    def __init__(self, send, receive):
        self.send, self.receive, self.used = send, receive, 0

    def copy(self, source, target, device, landing):
        index = self.used
        self.used += 1
        going = pltpu.make_async_remote_copy(
            src_ref=source, dst_ref=target, send_sem=self.send.at[index],
            recv_sem=self.receive.at[index], device_id=device, device_id_type=MESH,
        )
        coming = pltpu.make_async_remote_copy(
            src_ref=landing, dst_ref=landing, send_sem=self.send.at[index],
            recv_sem=self.receive.at[index], device_id=device, device_id_type=MESH,
        )
        return going, coming


def greet(devices):
    barrier = pltpu.get_barrier_semaphore()
    for device in devices:
        pl.semaphore_signal(barrier, inc=1, device_id=device, device_id_type=MESH)
    pl.semaphore_wait(barrier, len(devices))


def chip_peers(grid):
    peers = [(grid.exp, grid.sibling(grid.fsdp))]
    return peers + [(grid.exp, grid.x_from(hop)) for hop in range(1, grid.x_size)]


class ChipGather:
    def __init__(self, grid, links, own_sem, source, target):
        self.grid, self.links, self.target = grid, links, target
        self.own = pltpu.make_async_copy(source, target.at[grid.fsdp], own_sem)
        sibling = grid.sibling(grid.fsdp)
        self.along_x, self.across = [], []
        for hop in range(1, grid.x_size):
            self.along_x.append(
                links.copy(
                    source, target.at[grid.fsdp], (grid.exp, grid.x_from(hop)),
                    target.at[grid.x_from(-hop)],
                )
            )
        self.across.append(
            links.copy(source, target.at[grid.fsdp], (grid.exp, sibling), target.at[sibling])
        )

    def start(self):
        for going, _ in self.along_x + self.across:
            going.start()
        self.own.start()

    def forward(self):
        grid = self.grid
        for hop in range(1, grid.x_size):
            self.along_x[hop - 1][1].wait_recv()
            held = grid.x_from(-hop)
            other = grid.sibling(held)
            self.across.append(
                self.links.copy(
                    self.target.at[held], self.target.at[held],
                    (grid.exp, grid.sibling(grid.fsdp)), self.target.at[other],
                )
            )
            self.across[-1][0].start()

    def finish(self):
        for _, coming in self.across:
            coming.wait_recv()
        for going, _ in self.along_x + self.across:
            going.wait_send()
        self.own.wait()


class Exchange:
    def __init__(self, grid, links, own_sems, pairs):
        self.steps = grid.exp_steps()
        self.peers = [(to, grid.fsdp) for to, _ in self.steps]
        self.copies, self.own = [], []
        for index, (source, target) in enumerate(pairs):
            for to, origin in self.steps:
                self.copies.append(
                    links.copy(
                        source(to), target.at[grid.exp], (to, grid.fsdp), target.at[origin]
                    )
                )
            self.own.append(
                pltpu.make_async_copy(source(grid.exp), target.at[grid.exp], own_sems.at[index])
            )

    def start(self):
        for going, _ in self.copies:
            going.start()
        for own in self.own:
            own.start()

    def finish(self):
        for going, coming in self.copies:
            coming.wait_recv()
            going.wait_send()
        for own in self.own:
            own.wait()


ANYWHERE = pl.BlockSpec(memory_space=pl.ANY)
IN_VMEM = pl.BlockSpec(memory_space=pltpu.VMEM)


def dma_sems(count):
    return pltpu.SemaphoreType.DMA((count,))


def plane_of(source, part, to):
    return source.at[to] if part is None else source.at[to, part]


class Lanes:
    def __init__(self, heads, width, padded_heads, experts):
        self.weights = 3 * heads * width
        self.base = self.weights // 128 * 128
        self.router = self.weights - self.base
        self.gain = self.router + experts
        self.table = self.gain + 1
        self.count = self.table + padded_heads
        self.width = -(-(self.weights + 2 * experts + 1 + padded_heads) // 128) * 128
        self.extra = self.width - self.base
        self.shift = self.count - self.router


def bucket_rows_select(features, feature_rows, bucket_rows, span):
    row = lax.broadcasted_iota(jnp.int32, (features, 1), 0)
    within = lax.rem(row, feature_rows)
    bucket = jnp.where(
        within < bucket_rows, lax.div(row, feature_rows) * bucket_rows + within, -1
    )
    distance = lax.broadcasted_iota(jnp.int32, (1, span), 1) - SKEW
    near = BUCKETS // 2
    spread = max(WINDOW - near, 1)
    far = near + lax.div(jnp.maximum(distance - near, 0) * (BUCKETS - near), spread)
    wanted = jnp.where(distance < near, distance, far)
    reachable = (distance >= 0) & (distance < WINDOW)
    wanted = jnp.where(reachable, wanted, -2)
    return jnp.where(bucket == wanted, 1.0, 0.0).astype(BF16), reachable


def as_column(row, size):
    row_place = lax.broadcasted_iota(jnp.int32, (size, size), 0)
    lane = lax.broadcasted_iota(jnp.int32, (size, size), 1)
    spread = jnp.broadcast_to(row.astype(F32), (size, size))
    return jnp.sum(jnp.where(row_place == lane, spread, 0.0), axis=1, keepdims=True)


def padded_rows(value, rows):
    if value.shape[0] == rows:
        return value
    return jnp.concatenate([value, jnp.zeros((rows - value.shape[0], value.shape[1]), F32)], axis=0)


def padded_lanes(value, lanes):
    if value.shape[1] == lanes:
        return value
    return jnp.concatenate([value, jnp.zeros((value.shape[0], lanes - value.shape[1]), F32)], axis=1)


class Wide:
    def __init__(self, grid, links, own_sem, source, target):
        self.grid, self.links, self.target = grid, links, target
        self.own = pltpu.make_async_copy(
            source, target.at[grid.z, grid.y, grid.x, grid.core], own_sem
        )
        stage = []
        for hop in range(1, grid.z_size):
            origin = (grid.z + grid.z_size - hop) % grid.z_size
            stage.append(
                links.copy(
                    source, target.at[grid.z, grid.y, grid.x, grid.core],
                    grid.at(z=(grid.z + hop) % grid.z_size),
                    target.at[origin, grid.y, grid.x, grid.core],
                )
            )
        self.stages = [stage]

    def start(self):
        self.own.start()
        for going, _ in self.stages[0]:
            going.start()

    def turn(self, axis):
        grid, target = self.grid, self.target
        for _, coming in self.stages[-1]:
            coming.wait_recv()
        stage = []
        if axis == 0:
            self.own.wait()
            held = target.at[:, grid.y, grid.x, grid.core]
            for hop in range(1, grid.y_size):
                origin = (grid.y + grid.y_size - hop) % grid.y_size
                stage.append(
                    self.links.copy(
                        held, held, grid.at(y=(grid.y + hop) % grid.y_size),
                        target.at[:, origin, grid.x, grid.core],
                    )
                )
        elif axis == 1:
            held = target.at[:, :, grid.x, grid.core]
            for hop in range(1, grid.x_size):
                origin = (grid.x + grid.x_size - hop) % grid.x_size
                stage.append(
                    self.links.copy(
                        held, held, (grid.exp, grid.x_from(hop)),
                        target.at[:, :, origin, grid.core],
                    )
                )
        else:
            held = target.at[:, :, :, grid.core]
            stage.append(
                self.links.copy(
                    held, held, (grid.exp, grid.sibling(grid.fsdp)), target.at[:, :, :, 1 - grid.core]
                )
            )
        for going, _ in stage:
            going.start()
        self.stages.append(stage)

    def finish(self):
        for _, coming in self.stages[-1]:
            coming.wait_recv()
        for stage in self.stages:
            for going, _ in stage:
                going.wait_send()


def start_kernel(
    tokens, cotangent, routes_t, slots_t, attention_gain, mixture_gain, attention_in, router_t, table,
    attention_out, expert_up, expert_down, *refs, lanes, heads, width, head_count, experts, capacity,
    local, late,
):
    all_tokens, all_planes, cotangent_early, position_rows, columns, full_out = refs[:6]
    cotangent_late, refs = refs[6 : 6 + late], refs[6 + late :]
    shards = refs[: 2 * local]
    planes, up_stage, down_stage, send, receive, own, fetch, split = refs[2 * local :]
    grid = Grid().here()
    links = Links(send, receive)
    z_size, y_size, fsdp_size = grid.z_size, grid.y_size, grid.fsdp_size
    near = [
        (grid.exp, (grid.fsdp + turn) % fsdp_size) for turn in range(1, fsdp_size)
    ] + [grid.at(z=(grid.z + hop) % z_size) for hop in range(1, z_size)]
    beside = [grid.at(y=(grid.y + hop) % y_size) for hop in range(1, y_size)]
    gathered = ChipGather(grid, links, own.at[0], tokens, all_tokens)
    widely = Wide(grid, links, own.at[2], attention_out, full_out)
    part = expert_down.shape[1]
    depth = expert_up.shape[1]
    fetches = []
    for index in range(local):
        fetches.append(
            pltpu.make_async_copy(expert_up.at[index], up_stage.at[index], fetch.at[2 * index])
        )
        fetches.append(
            pltpu.make_async_copy(
                expert_down.at[index], down_stage.at[index], fetch.at[2 * index + 1]
            )
        )
    greet(near + beside)
    widely.start()
    for copy in fetches:
        copy.start()

    feature_rows = attention_in.shape[0]
    model_width = head_count * width
    gained = attention_in[...].astype(F32) * as_column(attention_gain[...], feature_rows)
    route_rows, slot_rows = routes_t[...].astype(F32), slots_t[...].astype(F32)
    columns[...] = padded_rows(jnp.concatenate([route_rows, slot_rows], axis=0), 128).T
    row_count = columns.shape[0]
    expert_lanes = lax.broadcasted_iota(jnp.int32, (row_count, experts), 1).astype(F32)
    named = jnp.zeros((row_count, experts), F32)
    for k in range(2):
        named = named + jnp.where(expert_lanes == columns[:, k : k + 1], 1.0, 0.0)
    named = jnp.sum(named, axis=0, keepdims=True)
    place = lax.broadcasted_iota(jnp.int32, (feature_rows, feature_rows), 0)
    same = place == lax.broadcasted_iota(jnp.int32, (feature_rows, feature_rows), 1)
    router = contract_last(jnp.where(same, 1.0, 0.0).astype(BF16), router_t[...])
    pieces = [
        router,
        as_column(mixture_gain[...], feature_rows),
        padded_rows(padded_lanes(table[...].astype(F32), heads * fsdp_size), feature_rows),
        padded_rows(named, feature_rows),
    ]
    taken = sum(piece.shape[1] for piece in pieces)
    if lanes.width > lanes.weights + taken:
        pieces.append(jnp.zeros((feature_rows, lanes.width - lanes.weights - taken), F32))
    for place in range(fsdp_size):
        first, last = place * heads * width, min((place + 1) * heads * width, model_width)
        own_pieces = []
        for kind in range(3):
            if last > first:
                own_pieces.append(gained[:, kind * model_width + first : kind * model_width + last])
            if last - first < heads * width:
                own_pieces.append(
                    jnp.zeros((feature_rows, heads * width - max(last - first, 0)), F32)
                )
        planes[place] = jnp.concatenate(own_pieces + pieces, axis=1).astype(BF16)
    placed = []
    for turn in range(1, fsdp_size):
        to = (grid.fsdp + turn) % fsdp_size
        origin = (grid.fsdp + fsdp_size - turn) % fsdp_size
        placed.append(
            links.copy(
                planes.at[to], all_planes.at[grid.z, grid.y, grid.fsdp], (grid.exp, to),
                all_planes.at[grid.z, grid.y, origin],
            )
        )
        placed[-1][0].start()
    kept = pltpu.make_async_copy(
        planes.at[grid.fsdp], all_planes.at[grid.z, grid.y, grid.fsdp], own.at[1]
    )
    kept.start()
    gathered.start()
    for _, coming in placed:
        coming.wait_recv()
    kept.wait()

    def over_y(z):
        for turn in range(1, y_size):
            forwarded.append(
                links.copy(
                    all_planes.at[z, grid.y],
                    all_planes.at[z, grid.y],
                    grid.at(y=(grid.y + turn) % y_size),
                    all_planes.at[z, (grid.y + y_size - turn) % y_size],
                )
            )
            forwarded[-1][0].start()

    along_z, forwarded = [], []
    for hop in range(1, z_size):
        along_z.append(
            links.copy(
                all_planes.at[grid.z, grid.y],
                all_planes.at[grid.z, grid.y],
                grid.at(z=(grid.z + hop) % z_size),
                all_planes.at[(grid.z + z_size - hop) % z_size, grid.y],
            )
        )
        along_z[-1][0].start()
    over_y(grid.z)
    widely.turn(0)

    for copy in fetches:
        copy.wait()
    splits = []
    for index in range(local):
        up, down = shards[2 * index : 2 * index + 2]
        stores = [
            (
                up_stage.at[index, :, pl.ds(block * part, part)],
                up.at[pl.ds(block * depth, depth), :],
            )
            for block in range(fsdp_size)
        ]
        for source, target in stores + [(down_stage.at[index], down)]:
            splits.append(pltpu.make_async_copy(source, target, split.at[len(splits)]))
            splits[-1].start()

    widely.turn(1)

    place = route_rows * capacity + slot_rows
    position_rows[...] = padded_rows(place, 8)
    select_rows([cotangent_early] + list(cotangent_late), place, cotangent[...])

    for hop in range(1, z_size):
        along_z[hop - 1][1].wait_recv()
        over_y((grid.z + z_size - hop) % z_size)
    gathered.forward()
    widely.turn(2)
    for going, coming in forwarded:
        coming.wait_recv()
        going.wait_send()
    for going, _ in placed + along_z:
        going.wait_send()
    gathered.finish()
    widely.finish()
    for copy in splits:
        copy.wait()


def project_kernel(
    tokens, plane, segments, normed, query_t, key_n, query_n, value_n, key_t, value_t, bias, counts,
    weight_t, table_t, *, heads, width, lanes, feature_rows, bucket_rows,
):
    @pl.when(pl.program_id(0) == 0)
    def _():
        weight_t[...] = turned(plane[:, : lanes.weights]).astype(BF16)
        extra = plane[:, lanes.base :]
        span = bias.shape[2]
        select, reachable = bucket_rows_select(plane.shape[0], feature_rows, bucket_rows, span)
        table_t[...] = lax.dot_general(
            extra, select, (((0,), (0,)), ((), ())), preferred_element_type=F32
        )
        first = lanes.table + lax.axis_index("fsdp") * heads
        for head in range(heads):
            bias[head] = jnp.where(reachable, table_t[pl.ds(first + head, 1), :], MASKED)
        summed = jnp.sum(extra.astype(F32), axis=0, keepdims=True)
        counts[...] = pltpu.roll(
            jnp.broadcast_to(summed, counts.shape), lanes.extra - lanes.shift, 1
        )

    inputs = tokens[0].astype(F32)
    scale = lax.rsqrt(jnp.mean(inputs * inputs, axis=1, keepdims=True) + EPSILON)
    low = (inputs * scale).astype(BF16)
    normed[...] = low
    rows = low.shape[0]
    projected = contract_last(weight_t[...], low).astype(BF16).astype(F32)
    document = segments[...] % 4
    places = lax.broadcasted_iota(jnp.int32, (8, rows), 0)
    same = places == document
    hot = jnp.where(same, 1.0, 0.0)
    barred = jnp.where(same | (places >= 4), 0.0, MASKED)
    filler = jnp.zeros((SKEW - 8 - width, rows), F32)
    for head in range(heads):
        query = projected[head * width : (head + 1) * width] * width ** (-0.5)
        key = projected[(heads + head) * width : (heads + head + 1) * width]
        value = projected[(2 * heads + head) * width : (2 * heads + head + 1) * width]
        query_t[head] = jnp.concatenate([query, barred, filler], axis=0).astype(BF16)
        key_n[head] = jnp.concatenate([key, hot, filler], axis=0).T.astype(BF16)
        query_n[head] = query.T.astype(BF16)
        value_n[head] = value.T.astype(BF16)
        key_t[head] = key.astype(BF16)
        value_t[head] = value.astype(BF16)


def spans(length):
    for query_start in range(0, length, QUERY_BLOCK):
        key_start = max(0, query_start - WINDOW)
        yield query_start, key_start, query_start + QUERY_BLOCK - key_start


def spread_bias(bias, skew):
    skew[...] = pltpu.roll(
        jnp.broadcast_to(bias[0], skew.shape), 0, 1, stride=1, stride_axis=0
    )


def attend_kernel(
    query_t, key_n, value_t, bias, context, context_high, log_total, attended, skew, scores, held,
    send, receive, own, *, rows,
):
    head = pl.program_id(0)
    width = value_t.shape[1]
    grid = Grid().here()
    fsdp_size = grid.fsdp_size

    def leave(number):
        place = pl.ds(pl.multiple_of(number * width, 16), width)
        copies = []
        for turn in range(1, fsdp_size):
            to = (grid.fsdp + turn) % fsdp_size
            origin = (grid.fsdp + fsdp_size - turn) % fsdp_size
            sems = dict(
                send_sem=send.at[number, turn], recv_sem=receive.at[number, turn],
                device_id=(grid.exp, to), device_id_type=MESH,
            )
            copies.append(
                (
                    pltpu.make_async_remote_copy(
                        src_ref=held.at[number, to], dst_ref=attended.at[grid.fsdp, place, :], **sems
                    ),
                    pltpu.make_async_remote_copy(
                        src_ref=attended.at[origin, place, :], dst_ref=attended.at[origin, place, :],
                        **sems,
                    ),
                )
            )
        kept = pltpu.make_async_copy(
            held.at[number, grid.fsdp], attended.at[grid.fsdp, place, :], own.at[number]
        )
        return copies, kept

    @pl.when(head == 0)
    def _():
        greet([(grid.exp, (grid.fsdp + turn) % fsdp_size) for turn in range(1, fsdp_size)])

    spread_bias(bias, skew)
    for query_start, key_start, key_count in spans(query_t.shape[2]):
        queries = slice(query_start, query_start + QUERY_BLOCK)
        keys = slice(key_start, key_start + key_count)
        raw = matmul(key_n[0, keys, :], query_t[0, :, queries])
        for start in range(0, key_count, SKEW):
            offset = query_start - key_start - start + SKEW
            scores[start : start + SKEW, :] = (
                raw[start : start + SKEW] + skew[:, offset : offset + QUERY_BLOCK]
            )
        high = jnp.max(scores[:key_count, :], axis=0, keepdims=True)
        weights = jnp.exp(scores[:key_count, :] - high)
        total = jnp.sum(weights, axis=0, keepdims=True)
        gathered = matmul(value_t[0, :, keys], weights.astype(BF16)) / total
        context_high[0, :, queries] = gathered
        log_total[0, :, queries] = high + jnp.log(total)
        for start in range(0, QUERY_BLOCK, 128):
            place = query_start + start
            piece = gathered[:, start : start + 128].astype(BF16)
            context[place // rows, :, place % rows : place % rows + 128] = piece
            held[head, place // rows, :, place % rows : place % rows + 128] = piece
    copies, kept = leave(head)
    for going, _ in copies:
        going.start()
    kept.start()

    @pl.when(head == pl.num_programs(0) - 1)
    def _():
        def finish(number, carry):
            copies, kept = leave(number)
            for going, coming in copies:
                coming.wait_recv()
                going.wait_send()
            kept.wait()
            return carry

        lax.fori_loop(0, pl.num_programs(0), finish, 0)


def attend_back_kernel(
    query_t, key_n, query_n, value_n, key_t, grad_t, grad_n, context_high, log_total, bias,
    grad_projected, grad_bias, skew, grad_skew, grad_key, grad_value, *, scale,
):
    spread_bias(bias, skew)
    grad_skew[...] = jnp.zeros_like(grad_skew)
    grad_key[...] = jnp.zeros_like(grad_key)
    grad_value[...] = jnp.zeros_like(grad_value)
    inner = jnp.sum(grad_t[0].astype(F32) * context_high[0], axis=0, keepdims=True)
    for query_start, key_start, key_count in spans(query_t.shape[2]):
        queries = slice(query_start, query_start + QUERY_BLOCK)
        keys = slice(key_start, key_start + key_count)
        raw = matmul(key_n[0, keys, :], query_t[0, :, queries])
        grad_weights = matmul(value_n[0, keys, :], grad_t[0, :, queries])
        weights_low, grad_low = [], []
        for start in range(0, key_count, SKEW):
            offset = query_start - key_start - start + SKEW
            part = slice(start, start + SKEW)
            weights = jnp.exp(
                raw[part] + skew[:, offset : offset + QUERY_BLOCK] - log_total[0, :, queries]
            )
            grad_scores = weights * (grad_weights[part] - inner[:, queries])
            grad_skew[:, offset : offset + QUERY_BLOCK] += grad_scores
            weights_low.append(weights.astype(BF16))
            grad_low.append(grad_scores.astype(BF16))
        weights_low = jnp.concatenate(weights_low, axis=0)
        grad_low = jnp.concatenate(grad_low, axis=0)
        grad_projected[0, 0, :, queries] = (matmul(key_t[0, :, keys], grad_low) * scale).astype(BF16)
        grad_key[keys, :] += matmul(grad_low, query_n[0, queries, :])
        grad_value[keys, :] += matmul(weights_low, grad_n[0, queries, :])
    grad_projected[1, 0] = grad_key[...].T.astype(BF16)
    grad_projected[2, 0] = grad_value[...].T.astype(BF16)
    count = SKEW
    span = skew.shape[1]
    while count > 8:
        count //= 2
        grad_skew[:count, :] += pltpu.roll(grad_skew[count : 2 * count, :], span - count, 1)
    summed = grad_skew[0:1, :]
    for row in range(1, 8):
        summed = summed + pltpu.roll(grad_skew[row : row + 1, :], span - row, 1)
    grad_bias[0] = summed

def expert_lane(shape, lanes):
    return lax.broadcasted_iota(jnp.int32, shape, 1) - lanes.router


def int_columns(columns):
    values = columns[:, 0:4].astype(jnp.int32)
    return values[:, 0:2], values[:, 2:4]


def route_kernel(
    tokens, attended_t, attention_out, plane, columns, position_rows, *refs,
    experts, lanes, capacity, crossing,
):
    over, refs = refs[:crossing], refs[crossing:]
    hidden, routed, probabilities, gates, outgoing, rows_in, gates_in = refs[:7]
    landed, refs = refs[7 : 7 + crossing], refs[7 + crossing :]
    slot_gates, send, receive, own = refs
    grid = Grid().here()
    links = Links(send, receive)
    exp_size = grid.exp_size
    sibling = (grid.exp, grid.sibling(grid.fsdp))
    greet([((grid.exp + hop) % exp_size, grid.fsdp) for hop in range(1, exp_size)] + [sibling])
    swaps = [links.copy(source, target, sibling, target) for source, target in zip(over, landed)]
    for going, _ in swaps:
        going.start()
    rows, model_width = tokens.shape
    routes, slots = int_columns(columns)
    attended_low = turned(attended_t[:model_width]).astype(BF16)
    hidden_state = tokens[...].astype(F32) + matmul(attended_low, attention_out[...])
    hidden[...] = hidden_state
    scale = lax.rsqrt(jnp.mean(hidden_state * hidden_state, axis=1, keepdims=True) + EPSILON)
    extra = plane[:, lanes.base :]
    gain = extra.astype(F32).T[lanes.gain : lanes.gain + 1]
    low = (hidden_state * scale * gain).astype(BF16)
    routed[...] = low
    member_slots = experts // exp_size * capacity
    work = Exchange(
        grid, links, own,
        [
            (lambda to: outgoing.at[to, pl.ds(0, capacity), :], rows_in),
            (partial(plane_of, slot_gates, None), gates_in),
        ],
    )
    for number, to in enumerate([to for to, _ in work.steps] + [grid.exp]):
        slot = lax.broadcasted_iota(jnp.int32, (member_slots, rows), 0) + to * member_slots
        slot = slot.astype(F32)
        picked = (slot == position_rows[0:1, :]) | (slot == position_rows[1:2, :])
        outgoing[to] = matmul(jnp.where(picked, 1.0, 0.0).astype(BF16), low).astype(BF16)
        (work.copies[number][0] if number < len(work.steps) else work.own[0]).start()
    logits = matmul(low, extra)
    lane = expert_lane(logits.shape, lanes)
    logits = jnp.where((lane >= 0) & (lane < experts), logits, MASKED)
    powers = jnp.exp(logits - jnp.max(logits, axis=1, keepdims=True))
    powers = powers / jnp.sum(powers, axis=1, keepdims=True)
    probabilities[...] = powers
    chosen = [
        jnp.sum(jnp.where(lane == routes[:, k : k + 1], powers, 0.0), axis=1, keepdims=True)
        for k in range(2)
    ]
    total = chosen[0] + chosen[1]
    gate_values = [chosen[k] / total for k in range(2)]
    pair = lax.broadcasted_iota(jnp.int32, (rows, 2), 1)
    gates[...] = jnp.where(pair == 0, gate_values[0], gate_values[1])
    gate_lanes = slot_gates.shape[2]
    slot_lanes = lax.broadcasted_iota(jnp.int32, (rows, gate_lanes), 1)
    inside = slot_lanes < member_slots
    places = routes * capacity + slots
    for member in range(exp_size):
        by_slot = jnp.zeros((rows, gate_lanes), F32)
        for k in range(2):
            hit = (slot_lanes + member * member_slots == places[:, k : k + 1]) & inside
            by_slot = by_slot + jnp.where(hit, gate_values[k], 0.0)
        slot_gates[member] = jnp.broadcast_to(
            jnp.sum(by_slot, axis=0, keepdims=True), slot_gates.shape[1:]
        )
    for going, _ in work.copies[exp_size - 1 :]:
        going.start()
    work.own[1].start()
    work.finish()
    for going, coming in swaps:
        coming.wait_recv()
        going.wait_send()


def select_rows(outgoing, position_rows, values):
    rows = values.shape[0]
    sizes = [array.shape[1] for array in outgoing]
    for member in range(outgoing[0].shape[0]):
        slots = lax.broadcasted_iota(jnp.int32, (sum(sizes), rows), 0) + member * sum(sizes)
        slots = slots.astype(F32)
        picked = (slots == position_rows[0:1, :]) | (slots == position_rows[1:2, :])
        found = matmul(jnp.where(picked, 1.0, 0.0).astype(BF16), values).astype(BF16)
        first = 0
        for array, size in zip(outgoing, sizes):
            array[member] = found[first : first + size]
            first += size


def gelu_parts(value):
    magnitude = jnp.abs(value)
    power = jnp.exp2(value * value * -0.7213475204444817)
    base = 1.0 + (0.3275911 * 0.7071067811865476) * magnitude
    step = pl.reciprocal(base, approx=True)
    step = step * (2.0 - base * step)
    series = step * (
        0.127414796
        + step * (-0.142248368 + step * (0.7107068705 + step * (-0.7265760135 + step * 0.5307027145)))
    )
    tail = series * power
    normal = jnp.where(value < 0.0, tail, 1.0 - tail)
    return value * normal, normal + value * (power * 0.3989422804014327)


def expert_kernel(*refs, layout, index, local, half, capacity, parts):
    shards = 2 * half
    refs = Bag(layout, refs)
    grid = Grid().here()
    z_size, y_size = grid.z_size, grid.y_size
    last = index == local - 1
    sibling = (grid.exp, grid.sibling(grid.fsdp))
    links = Links(refs.send[0], refs.receive[0])
    rows_all, cot, up_all, down_all = (
        refs.rows_all[0], refs.cot[0], refs.up_all[0], refs.down_all[0]
    )
    total = refs.total[0]
    if last:
        active, grad_hidden, unscaled = refs.active[0], refs.grad_hidden[0], refs.unscaled[0]
    else:
        grad_total, slot_grad = refs.grad_total[0], refs.slot_grad[0]
    gates, gate_column = refs.gates[0], refs.gate_column[0]
    rows_t, slot_t = refs.rows_t[0], refs.slot_t[0]
    grad_up, grad_down = refs.grad_up[0], refs.grad_down[0]
    grad_rows, grad_gates = refs.grad_rows[0], refs.grad_gates[0]
    up_keep, up_taken, down_keep, down_taken = refs.own
    keep_up = [up_keep] + list(refs.far_keep_up)
    taken_up = [up_taken] + list(refs.far_taken_up)
    keep_down = [down_keep] + list(refs.far_keep_down)
    taken_down = [down_taken] + list(refs.far_taken_down)
    load_sem, fetch_sem, store_sem = refs.load_sem[0], refs.fetch_sem[0], refs.store_sem[0]
    store_there, stored_here = refs.store_there[0], refs.stored_here[0]
    pass_sem = refs.pass_sem[0]
    blocks, _, model_width = rows_all.shape
    part = up_all.shape[2]
    count = blocks * capacity
    depth = model_width // shards
    power = z_size & (z_size - 1) == 0
    together = 2 if power and z_size > 1 else 1
    group_rows = together * y_size * capacity

    source_z, target_z = grid.source_z, grid.target_z

    def owner(place, core):
        return ((grid.x + place % half) % half) * 2 + (core + place // half) % 2

    def rows_of(place, core=None):
        core = grid.core if core is None else core
        return pl.ds(pl.multiple_of(owner(place, core) * depth, 16), depth)

    loads = [pltpu.make_async_copy(refs.rows_in[0], rows_all, load_sem.at[1])]
    late_count = 0
    if last and refs.cot_late:
        late_count = refs.cot_late[0].shape[1]
        loads.append(
            pltpu.make_async_copy(
                refs.cot_late[0], cot.at[:, pl.ds(capacity - late_count, late_count)], load_sem.at[4]
            )
        )
    loads.append(
        pltpu.make_async_copy(
            refs.cot_in[0].at[:, pl.ds(index * capacity, capacity - late_count)],
            cot.at[:, pl.ds(0, capacity - late_count)], load_sem.at[0],
        )
    )
    my_up, my_down = refs.my_up, refs.my_down
    swapped_up, swapped_down = refs.swapped_up, refs.swapped_down
    local_up = list(enumerate(my_up)) + [
        (half + number, array) for number, array in enumerate(swapped_up)
    ]
    local_down = list(enumerate(my_down)) + [
        (half + number, array) for number, array in enumerate(swapped_down)
    ]

    def fetch_up(place):
        return [
            pltpu.make_async_copy(
                array.at[rows_of(place), :], up_all.at[place, rows_of(shard), :],
                fetch_sem.at[place, number],
            )
            for number, (shard, array) in enumerate(local_up)
        ]

    fetched_down = {
        shard: pltpu.make_async_copy(
            array, down_all.at[shard], fetch_sem.at[shards + number, 0]
        )
        for number, (shard, array) in enumerate(local_down)
    }
    cross_down = {
        half + shard: links.copy(
            my_down[shard], down_all.at[half + shard], sibling, down_all.at[half + shard]
        )
        for shard in range(len(swapped_down), half)
    }
    cross_up = [
        links.copy(
            my_up[shard].at[rows_of(place, 1 - grid.core), :],
            up_all.at[place, rows_of(shard), :], sibling,
            up_all.at[place, rows_of(half + shard), :],
        )
        for shard in range(len(swapped_up), half)
        for place in range(shards)
    ]
    cross_next = [
        links.copy(source, target, sibling, target)
        for source, target in zip(refs.next_mine, refs.next_swapped)
    ]
    work = Exchange(
        grid, links, refs.own_sem[0],
        [
            (partial(plane_of, source, place), target)
            for source, place, target in zip(refs.moved_from, parts, refs.moved_to)
        ],
    )
    def member(z, y):
        return z * y_size + y

    def give_back(turn, hop):
        to = member(source_z(turn), (grid.y + hop) % y_size)
        origin = member(target_z(turn), (grid.y + y_size - hop) % y_size)
        pairs = []
        for number, (held, target) in enumerate(
            ((grad_rows, refs.back_rows[0]), (grad_gates, refs.back_gates[0]))
        ):
            sems = dict(
                send_sem=refs.back_send[0].at[number, turn, hop],
                recv_sem=refs.back_receive[0].at[number, turn, hop],
                device_id=(to, grid.fsdp), device_id_type=MESH,
            )
            pairs.append(
                (
                    pltpu.make_async_remote_copy(
                        src_ref=held.at[to], dst_ref=target.at[grid.exp], **sems
                    ),
                    pltpu.make_async_remote_copy(
                        src_ref=target.at[origin], dst_ref=target.at[origin], **sems
                    ),
                )
            )
        return pairs

    steps = [(turn, hop) for turn in range(z_size) for hop in range(y_size)]
    own_back = []
    if last:
        own_back = [
            pltpu.make_async_copy(held.at[grid.exp], target.at[grid.exp], load_sem.at[2 + number])
            for number, (held, target) in enumerate(
                ((grad_rows, refs.back_rows[0]), (grad_gates, refs.back_gates[0]))
            )
        ]

    for copy in loads:
        copy.start()
    order = list(range(shards))
    if not last:
        order = [(pair + 1) % half + side * half for pair in range(half) for side in (1, 0)]
    if last:
        for copy in fetched_down.values():
            copy.start()
    for place in order:
        if not last and place in fetched_down:
            fetched_down[place].start()
        for copy in fetch_up(place):
            copy.start()
    greet(
        [((grid.exp + hop) % grid.exp_size, grid.fsdp) for hop in range(1, grid.exp_size)]
        + chip_peers(grid)
    )
    for going, _ in list(cross_down.values()) + cross_up + cross_next:
        going.start()
    work.start()

    def place_at(position):
        hop = (position // 2 + 1) % half
        return hop + half * (1 - position % 2)

    def slot_rows():
        columns = gates[:, 0, :].T
        for block in range(blocks):
            piece = slice(block * capacity, (block + 1) * capacity)
            gate = columns[index * capacity : (index + 1) * capacity, block : block + 1]
            gate_column[piece, :] = gate
        slot_values = gate_column[...] * cot[...].reshape(count, model_width).astype(F32)
        slot_t[...] = slot_values.T.astype(BF16)
        if not last:
            slot_grad[...] = slot_values.astype(BF16)

    def wait_down(place):
        if place in fetched_down:
            fetched_down[place].wait()
        else:
            cross_down[place][1].wait_recv()

    def wait_crossed():
        for _, coming in cross_up:
            coming.wait_recv()

    def folded(value):
        return sum(value[:, start : start + 128] for start in range(0, value.shape[1], 128))

    def gate_rows(found, block):
        ones = jnp.ones((8, 128), F32)
        grad_gates[block] = lax.dot_general(
            ones, found, (((1,), (1,)), ((), ())), precision=lax.Precision.HIGHEST,
            preferred_element_type=F32,
        )

    def up_target(targets, hop, place):
        if hop == 0:
            return targets[0].at[rows_of(place), :]
        return targets[1].at[hop - 1, rows_of(place), :]

    def keep_stores(place, slot):
        return [
            pltpu.make_async_copy(
                grad_up.at[slot, rows_of(hop), :], up_target(keep_up, hop, place),
                store_sem.at[slot, hop],
            )
            for hop in range(half)
        ]

    def give_stores(place, slot):
        return [
            pltpu.make_async_remote_copy(
                src_ref=grad_up.at[slot, rows_of(half + hop), :],
                dst_ref=up_target(taken_up, hop, place),
                send_sem=store_there.at[slot, hop], recv_sem=stored_here.at[place, hop],
                device_id=sibling, device_id_type=MESH,
            )
            for hop in range(half)
        ]

    def down_store(slot):
        return pltpu.make_async_copy(grad_down.at[slot], keep_down[0], store_sem.at[slot, half])

    def down_give(hop, slot):
        target = taken_down[0] if hop == 0 else taken_down[1].at[hop - 1]
        return pltpu.make_async_remote_copy(
            src_ref=grad_down.at[slot], dst_ref=target,
            send_sem=store_there.at[slot, half], recv_sem=stored_here.at[hop, half],
            device_id=sibling, device_id_type=MESH,
        )

    def start_store(place, slot):
        for copy in keep_stores(place, slot) + give_stores(place, slot):
            copy.start()

        @pl.when(place == 0)
        def _():
            down_store(slot).start()

        for hop in range(half):

            @pl.when(place == half + hop)
            def _(hop=hop):
                down_give(hop, slot).start()

            if hop > 0:

                @pl.when(place == hop)
                def _(hop=hop):
                    keep_down[1][hop - 1] = grad_down[slot]

    def wait_store(place, slot):
        for copy in keep_stores(place, slot):
            copy.wait()
        for copy in give_stores(place, slot):
            copy.wait_send()

        @pl.when(place == 0)
        def _():
            down_store(slot).wait()

        for hop in range(half):

            @pl.when(place == half + hop)
            def _(hop=hop):
                down_give(hop, slot).wait_send()

    def fused(position, carry):
        place, slot = place_at(position), position % 2
        for copy in fetch_up(place):
            copy.wait()
        for which in range(shards):

            @pl.when(place == which)
            def _(which=which):
                wait_down(which)

        up, down = up_all[place], down_all[place]
        rows = rows_all[...].reshape(count, model_width)
        pieces = [slice(start, start + 256) for start in range(0, count, 256)]

        def products_of(piece):
            return matmul(rows[piece], up), contract_last(slot_grad[piece, :], down)

        raw = products_of(pieces[0])
        active_low, grad_low = [], []
        for number, piece in enumerate(pieces):
            hidden, grad_active = raw
            if number + 1 < len(pieces):
                raw = products_of(pieces[number + 1])
            activated, slope = gelu_parts(hidden)
            active_low.append(activated.astype(BF16))
            grad_low.append((grad_active * slope).astype(BF16))
            total[piece, :] += matmul(active_low[number], down)
            grad_total[piece, :] += contract_last(grad_low[number], up)
        active_low = jnp.concatenate(active_low, axis=0)
        grad_low = jnp.concatenate(grad_low, axis=0)

        @pl.when(position >= 2)
        def _():
            wait_store(place_at(position - 2), slot)

        grad_up[slot] = matmul(rows_t[...], grad_low).astype(BF16)
        grad_down[slot] = matmul(slot_t[...], active_low).T.astype(BF16)
        start_store(place, slot)
        return carry

    def group(step, carry):
        number = z_size // together - 1 - step
        turns = [number * together + more for more in range(together)]
        if together == 2:
            place_of_group = flipped(grid.z // 2, number, z_size // 2)
        else:
            place_of_group = source_z(number)
        members = pl.ds(place_of_group * together * y_size, together * y_size)
        span = pl.ds(pl.multiple_of(place_of_group * group_rows, 16), group_rows)
        rows = rows_all[members].reshape(group_rows, model_width)
        gate = gate_column[span, :]
        grad = jnp.zeros((group_rows, model_width), F32)
        products = jnp.zeros((group_rows, 128), F32)
        ahead = matmul(rows, up_all[0])
        for place in range(shards):
            hidden = ahead
            if place + 1 < shards:
                ahead = matmul(rows, up_all[place + 1])
            base = unscaled[place, span, :].astype(F32)
            activated, slope = gelu_parts(hidden)
            products = products + folded(activated * base)
            active_low = activated.astype(BF16)
            active[place, span, :] = active_low
            low = (gate * base * slope).astype(BF16)
            grad_hidden[place, span, :] = low
            grad = grad + contract_last(low, up_all[place])
            total[span, :] += matmul(active_low, down_all[place])
        grad_rows[members] = grad.astype(BF16).reshape(together * y_size, capacity, model_width)
        for hop in range(together * y_size):
            gate_rows(
                products[hop * capacity : (hop + 1) * capacity],
                place_of_group * together * y_size + hop,
            )
        for turn in turns:
            for hop in range(y_size):

                @pl.when(turn + hop > 0)
                def _(turn=turn, hop=hop):
                    for going, _ in give_back(turn, hop):
                        going.start()

        return carry

    def column(position, carry):
        place, slot = place_at(position), position % 2
        @pl.when(position >= 2)
        def _():
            wait_store(place_at(position - 2), slot)

        grad_up[slot] = matmul(rows_t[...], grad_hidden[place]).astype(BF16)
        grad_down[slot] = matmul(slot_t[...], active[place]).T.astype(BF16)
        start_store(place, slot)
        return carry

    for copy in loads[1:]:
        copy.wait()
    total[...] = jnp.zeros_like(total)
    slot_rows()
    if last:
        for place in range(shards):
            wait_down(place)
            unscaled[place] = contract_last(
                cot[...].reshape(count, model_width), down_all[place]
            ).astype(BF16)
        loads[0].wait()
        for place in range(shards):
            for copy in fetch_up(place):
                copy.wait()
        wait_crossed()
        lax.fori_loop(0, z_size // together, group, 0)
        for copy in own_back:
            copy.start()
        rows_t[...] = turned(rows_all[...].reshape(count, model_width)).astype(BF16)
        lax.fori_loop(0, shards, column, 0)
    else:
        loads[0].wait()
        rows_t[...] = turned(rows_all[...].reshape(count, model_width)).astype(BF16)
        grad_total[...] = jnp.zeros_like(grad_total)
        wait_crossed()
        lax.fori_loop(0, shards, fused, 0)
        grad_rows[...] = grad_total[...].astype(BF16).reshape(grad_rows.shape)
        for block in range(blocks):
            rows = total[block * capacity : (block + 1) * capacity, :].astype(BF16).astype(F32)
            gate_rows(folded(rows * cot[block].astype(F32)), block)

    rows_out = refs.rows_out[0]
    cot[...] = total[...].astype(BF16).reshape(blocks, capacity, model_width)
    out_copies = [pltpu.make_async_copy(cot, rows_out.at[:, index], load_sem.at[0])]
    for before in refs.outs_before:
        out_copies.append(
            pltpu.make_async_copy(before, rows_out.at[:, pl.ds(0, index)], load_sem.at[1])
        )
    for copy in out_copies:
        copy.start()
    for position in range(max(shards - 2, 0), shards):
        wait_store(place_at(position), position % 2)
    for place in range(shards):
        for copy in give_stores(place, 0):
            copy.wait_recv()
    for hop in range(half):
        down_give(hop, 0).wait_recv()
    if half > 1:
        for kept, taken in ((keep_up[1], taken_up[1]), (keep_down[1], taken_down[1])):
            kept[...] = (kept[...].astype(F32) + taken[...].astype(F32)).astype(BF16)
        early_rows = part // 2 if last else 0
        passed = [
            (keep_up[1], refs.pass_up[0], 0),
            (keep_down[1].at[:, pl.ds(early_rows, part - early_rows), :], refs.pass_down[0], 1),
        ]
        if last:
            passed.append((keep_down[1].at[:, pl.ds(0, early_rows), :], refs.early_down[0], 2))
        for source, target, number in passed:
            out_copies.append(pltpu.make_async_copy(source, target, pass_sem.at[number]))
            out_copies[-1].start()
    for copy in out_copies:
        copy.wait()
    for going, coming in cross_next:
        coming.wait_recv()
        going.wait_send()
    for going, _ in list(cross_down.values()) + cross_up:
        going.wait_send()
    work.finish()
    if last:
        for turn, hop in steps[1:]:
            for going, coming in give_back(turn, hop):
                coming.wait_recv()
                going.wait_send()
        for copy in own_back:
            copy.wait()


class Bag:
    def __init__(self, layout, refs):
        start = 0
        for name, size in layout.items():
            setattr(self, name, refs[start : start + size])
            start += size


class Wanted:
    def groups(self):
        return list(self.__dict__.values())

    def layout(self):
        return {name: len(group) for name, group in self.__dict__.items()}


def run_expert(index, local, rows_in, gates, cotangent, cotangent_late, ups, downs, swapped, next_mine,
               moved, outs_before, collective_id):
    grid = Grid()
    half = len(ups)
    shards = 2 * half
    last = index == local - 1
    blocks, capacity, model_width = rows_in.shape
    part = downs[0].shape[0]
    count = blocks * capacity
    inputs, outputs, scratch = Wanted(), Wanted(), Wanted()
    inputs.cot_in = [(cotangent, ANYWHERE)]
    inputs.cot_late = [(array, ANYWHERE) for array in cotangent_late]
    inputs.rows_in = [(rows_in, ANYWHERE)]
    inputs.gates = [(gates, IN_VMEM)]
    inputs.my_up = [(array, ANYWHERE) for array in ups]
    inputs.my_down = [(array, ANYWHERE) for array in downs]
    inputs.swapped_up = [(array, ANYWHERE) for array in swapped[0]]
    inputs.swapped_down = [(array, ANYWHERE) for array in swapped[1]]
    inputs.next_mine = [(array, ANYWHERE) for array in next_mine]
    inputs.moved_from = [(array, ANYWHERE) for array, _ in moved]
    inputs.outs_before = [] if outs_before is None else [(outs_before, IN_VMEM)]

    up_shape, down_shape = (model_width, part), (part, model_width)
    outputs.rows_out = [(shape_of((blocks, index + 1, capacity, model_width), BF16), ANYWHERE)]
    own_up, own_down = shape_of(up_shape, BF16), shape_of(down_shape, BF16)
    outputs.own = [(own_up, ANYWHERE), (own_up, ANYWHERE), (own_down, ANYWHERE), (own_down, ANYWHERE)]
    outputs.pass_up = [(shape_of((half - 1,) + up_shape, BF16), ANYWHERE)] if half > 1 else []
    early_rows = part // 2 if last else 0
    late_down = (half - 1, part - early_rows, model_width)
    early_down = (half - 1, early_rows, model_width)
    outputs.pass_down = [(shape_of(late_down, BF16), ANYWHERE)] if half > 1 else []
    outputs.early_down = [(shape_of(early_down, BF16), ANYWHERE)] if half > 1 and last else []
    outputs.next_swapped = [(shape_of(array.shape, BF16), ANYWHERE) for array in next_mine]
    outputs.moved_to = [
        (
            shape_of((grid.exp_size,) + array.shape[(1 if place is None else 2) :], array.dtype),
            ANYWHERE,
        )
        for array, place in moved
    ]
    rows_shape, gate_shape = (blocks, capacity, model_width), (blocks, 8, capacity)
    if last:
        outputs.back_rows = [(shape_of(rows_shape, BF16), ANYWHERE)]
        outputs.back_gates = [(shape_of(gate_shape, F32), ANYWHERE)]
    else:
        outputs.grad_rows = [(shape_of(rows_shape, BF16), IN_VMEM)]
        outputs.grad_gates = [(shape_of(gate_shape, F32), IN_VMEM)]

    sems = lambda *shape: pltpu.SemaphoreType.DMA(shape)
    scratch.rows_all = [pltpu.VMEM(rows_shape, BF16)]
    scratch.cot = [pltpu.VMEM(rows_shape, BF16)]
    scratch.up_all = [pltpu.VMEM((shards,) + up_shape, BF16)]
    scratch.down_all = [pltpu.VMEM((shards,) + down_shape, BF16)]
    scratch.total = [pltpu.VMEM((count, model_width), F32)]
    if last:
        scratch.active = [pltpu.VMEM((shards, count, part), BF16)]
        scratch.grad_hidden = [pltpu.VMEM((shards, count, part), BF16)]
        scratch.unscaled = [pltpu.VMEM((shards, count, part), BF16)]
    else:
        scratch.grad_total = [pltpu.VMEM((count, model_width), F32)]
        scratch.slot_grad = [pltpu.VMEM((count, model_width), BF16)]
    if last:
        scratch.grad_rows = [pltpu.VMEM(rows_shape, BF16)]
        scratch.grad_gates = [pltpu.VMEM(gate_shape, F32)]
        scratch.back_send = [sems(2, grid.z_size, grid.y_size)]
        scratch.back_receive = [sems(2, grid.z_size, grid.y_size)]
    scratch.gate_column = [pltpu.VMEM((count, 1), F32)]
    scratch.rows_t = [pltpu.VMEM((model_width, count), BF16)]
    scratch.slot_t = [pltpu.VMEM((model_width, count), BF16)]
    scratch.grad_up = [pltpu.VMEM((2,) + up_shape, BF16)]
    scratch.grad_down = [pltpu.VMEM((2,) + down_shape, BF16)]
    far_up = [pltpu.VMEM((half - 1,) + up_shape, BF16)] * (1 if half > 1 else 0)
    far_down = [pltpu.VMEM((half - 1,) + down_shape, BF16)] * (1 if half > 1 else 0)
    scratch.far_keep_up, scratch.far_taken_up = far_up, far_up
    scratch.far_keep_down, scratch.far_taken_down = far_down, far_down
    scratch.load_sem = [sems(5)]
    scratch.pass_sem = [sems(3)]
    scratch.fetch_sem = [sems(2 * shards, shards)]
    scratch.store_sem = [sems(2, half + 1)]
    scratch.store_there = [sems(2, half + 1)]
    scratch.stored_here = [sems(shards, half + 1)]
    copies = len(moved) * grid.exp_size + half * (shards + 2) + len(next_mine)
    scratch.send = [sems(copies)]
    scratch.receive = [sems(copies)]
    scratch.own_sem = [sems(max(len(moved), 1))]

    layout = {**inputs.layout(), **outputs.layout(), **scratch.layout()}

    def body(*refs):
        expert_kernel(
            *refs, layout=layout, index=index, local=local, half=half, capacity=capacity,
            parts=[place for _, place in moved],
        )

    results = pl.pallas_call(
        body,
        in_specs=[spec for group in inputs.groups() for _, spec in group],
        out_specs=tuple(spec for group in outputs.groups() for _, spec in group),
        out_shape=tuple(shape for group in outputs.groups() for shape, _ in group),
        scratch_shapes=[item for group in scratch.groups() for item in group],
        compiler_params=params(collective_id=collective_id, has_side_effects=True),
        cost_estimate=hint(45),
        name=f"expert_{index}",
    )(*[array for group in inputs.groups() for array, _ in group])
    return Bag(outputs.layout(), results)


def local_picks(routes, slots, capacity, local, index, slot_count):
    member, which = lax.div(routes, local), lax.rem(routes, local)
    places = jnp.where(which == index, member * capacity + slots, -1)
    lane = lax.broadcasted_iota(jnp.int32, (routes.shape[0], slot_count), 1)
    return [lane == places[:, k : k + 1] for k in range(2)]


def unroute_kernel(
    hidden, cotangent, routed, probabilities, gates, plane, columns, counts, attention_out, context,
    *refs, experts, local, token_total, lanes, heads, width,
):
    grads, gate_grads = refs[:local], refs[local : 2 * local]
    (
        grad_hidden, small, grad_t, grad_n, grad_out, branches, own_out, total, send, receive, own_sem,
    ) = refs[2 * local :]
    grid = Grid().here()
    links = Links(send, receive)
    rows, model_width = hidden.shape
    members, capacity = grads[0].shape[0], grads[0].shape[1]
    head_rows = heads * width
    fetch = pltpu.make_async_copy(
        attention_out.at[pl.ds(pl.multiple_of(grid.fsdp * head_rows, 16), head_rows), :], own_out,
        own_sem.at[0],
    )
    fetch.start()
    greet(chip_peers(grid))
    extra = plane[:, lanes.base :]
    gains = extra.astype(F32).T[lanes.gain : lanes.gain + 1]
    half_rows = rows // 2
    sibling = grid.sibling(grid.fsdp)
    small_t = jnp.zeros((lanes.extra, model_width), F32)
    gain_grad = jnp.zeros((1, model_width), F32)
    along_x, across = [], []
    for half in range(2):
        here = slice(half * half_rows, (half + 1) * half_rows)
        grad_output = cotangent[here, :].astype(F32)
        routes = columns[here, 0:2].astype(jnp.int32)
        slots = columns[here, 2:4].astype(jnp.int32)
        member, which = lax.div(routes, local), lax.rem(routes, local)
        lane = lax.broadcasted_iota(jnp.int32, (half_rows, capacity), 1)
        grad_routed = jnp.zeros((half_rows, model_width), F32)
        found = [jnp.zeros((half_rows, capacity), F32), jnp.zeros((half_rows, capacity), F32)]
        for index in range(local):
            picks = local_picks(routes, slots, capacity, local, index, members * capacity)
            grad_routed = grad_routed + matmul(
                jnp.where(picks[0] | picks[1], 1.0, 0.0).astype(BF16),
                grads[index][...].reshape(members * capacity, model_width),
            )
            for place in range(members):
                spots = jnp.where((which == index) & (member == place), slots, -1)
                for k in range(2):
                    found[k] = found[k] + jnp.where(
                        lane == spots[:, k : k + 1], gate_grads[index][place, 0:1, :], 0.0
                    )
        grad_gates = [jnp.sum(found[k], axis=1, keepdims=True) for k in range(2)]
        powers = probabilities[here, :]
        lane = expert_lane(powers.shape, lanes)
        inside = (lane >= 0) & (lane < experts)
        picked = [lane == routes[:, k : k + 1] for k in range(2)]
        chosen_total = sum(
            jnp.sum(jnp.where(picked[k], powers, 0.0), axis=1, keepdims=True) for k in range(2)
        )
        weighted = grad_gates[0] * gates[here, 0:1] + grad_gates[1] * gates[here, 1:2]
        grad_mass = (AUX_WEIGHT * experts / (2.0 * token_total * token_total)) * counts[0:1, :]
        grad_mass = jnp.where(inside, grad_mass, 0.0)
        for k in range(2):
            grad_mass = grad_mass + jnp.where(
                picked[k], (grad_gates[k] - weighted) / chosen_total, 0.0
            )
        grad_logits = powers * (grad_mass - jnp.sum(powers * grad_mass, axis=1, keepdims=True))
        grad_routed = grad_routed + contract_last(grad_logits.astype(BF16), extra)
        hidden_state = hidden[here, :]
        scale = lax.rsqrt(jnp.mean(hidden_state * hidden_state, axis=1, keepdims=True) + EPSILON)
        normed = hidden_state * scale
        product = grad_routed * normed
        grad = scale * (
            grad_routed * gains - normed * jnp.mean(product * gains, axis=1, keepdims=True)
        ) + grad_output
        grad_hidden[here, :] = grad
        branches[grid.fsdp, here, :] = grad.astype(BF16)
        mine = branches.at[grid.fsdp, here, :]
        for hop in range(1, grid.x_size):
            along_x.append(
                links.copy(
                    mine, mine, (grid.exp, grid.x_from(hop)),
                    branches.at[grid.x_from(-hop), here, :],
                )
            )
            along_x[-1][0].start()
        across.append(
            links.copy(mine, mine, (grid.exp, sibling), branches.at[sibling, here, :])
        )
        across[-1][0].start()
        gain_grad = gain_grad + jnp.sum(product, axis=0, keepdims=True)
        small_t = small_t + matmul(grad_logits.T.astype(BF16), routed[here, :])

    def context_grad(place):
        branch = branches[place]
        grad = contract_last(own_out[...], branch).astype(BF16)
        columns_here = pl.ds(pl.multiple_of(place * rows, 128), rows)
        rows_here = pl.ds(pl.multiple_of(place * rows, 16), rows)
        for head in range(heads):
            piece = grad[head * width : (head + 1) * width]
            grad_t[head, :, columns_here] = piece
            grad_n[head, rows_here, :] = turned(piece).astype(BF16)
        total[...] += matmul(context[place], branch)

    total[...] = jnp.zeros_like(total)
    fetch.wait()
    context_grad(grid.fsdp)
    forwards = []
    for half in range(2):
        here = slice(half * half_rows, (half + 1) * half_rows)
        for hop in range(1, grid.x_size):
            along_x[half * (grid.x_size - 1) + hop - 1][1].wait_recv()
            held = grid.x_from(-hop)
            forwards.append(
                links.copy(
                    branches.at[held, here, :], branches.at[held, here, :], (grid.exp, sibling),
                    branches.at[grid.sibling(held), here, :],
                )
            )
            forwards[-1][0].start()
    row = lax.broadcasted_iota(jnp.int32, small_t.shape, 0)
    small[...] = jnp.where(row == lanes.gain, gain_grad, small_t).T
    for _, coming in across:
        coming.wait_recv()
    context_grad(sibling)
    for hop in range(1, grid.x_size):
        context_grad(grid.x_from(-hop))
    for _, coming in forwards:
        coming.wait_recv()
    for hop in range(1, grid.x_size):
        context_grad(grid.sibling(grid.x_from(-hop)))
    grad_out[...] = total[...].astype(BF16)
    for going, _ in along_x + across + forwards:
        going.wait_send()


def project_back_kernel(
    grad_projected, normed, plane, small, probabilities, grad_bias, grad_first, grad_plane, total,
    bias_t, *, lanes, heads, feature_rows, bucket_rows,
):
    step = pl.program_id(0)

    @pl.when(step == 0)
    def _():
        total[...] = jnp.zeros_like(total)

    grad = grad_projected[...]
    grad_first[0] = matmul(plane[:, : lanes.weights], grad).astype(BF16)
    total[: lanes.weights, :] += matmul(grad, normed[...])

    @pl.when(step == pl.num_programs(0) - 1)
    def _():
        grad_plane[...] = total[...].T.astype(BF16)
        span = grad_bias.shape[2]
        select, _ = bucket_rows_select(plane.shape[0], feature_rows, bucket_rows, span)
        bias_t[...] = jnp.zeros_like(bias_t)
        first = lanes.table + lax.axis_index("fsdp") * heads
        for head in range(heads):
            bias_t[pl.ds(first + head, 1), :] = grad_bias[head]
        high = bias_t[...].astype(BF16)
        rest = (bias_t[...] - high.astype(F32)).astype(BF16)
        table = contract_last(select, high) + contract_last(select, rest)
        mass = jnp.sum(probabilities[...], axis=0, keepdims=True)
        mass = pltpu.roll(jnp.broadcast_to(mass, (8, lanes.extra)), lanes.shift, 1)[0:1]
        lane = lax.broadcasted_iota(jnp.int32, table.shape, 1)
        row = lax.broadcasted_iota(jnp.int32, table.shape, 0)
        is_small = (lane >= lanes.router) & (lane < lanes.table)
        is_mass = (lane >= lanes.count) & (lax.rem(row, feature_rows) == 0)
        extra = table + jnp.where(is_small, small[...], 0.0) + jnp.where(is_mass, mass, 0.0)
        grad_plane[:, lanes.base :] = (total[lanes.base :, :].T + extra).astype(BF16)


def last_kernel(
    first, planes, out_grad, hidden, gates, columns, rows_back, first_parts, output, plane_parts,
    out_parts, first_in, first_sum, planes_in, plane_sum, along_in, reduced, send, receive, own,
    *, spread_out, local,
):
    grid = Grid().here()
    links = Links(send, receive)
    z_size, y_size, x_size, fsdp_size = grid.z_size, grid.y_size, grid.x_size, grid.fsdp_size
    exp_size = grid.exp_size
    sibling = grid.sibling(grid.fsdp)
    near = [
        (grid.exp, (grid.fsdp + turn) % fsdp_size) for turn in range(1, fsdp_size)
    ] + [grid.at(z=(grid.z + hop) % z_size) for hop in range(1, z_size)]
    beside = [grid.at(y=(grid.y + hop) % y_size) for hop in range(1, y_size)]

    per_sender = grid.device_count if spread_out else exp_size
    base = 0 if spread_out else grid.fsdp * exp_size
    out_sends = []
    for number in range(per_sender):
        to = base + number
        out_sends.append((to, number))
    if spread_out:
        out_origins = [(origin, origin) for origin in range(grid.device_count)]
    else:
        out_origins = [
            (member * fsdp_size + grid.linear // exp_size, member) for member in range(exp_size)
        ]
    own_slot = grid.linear if spread_out else grid.exp
    out_base = links.used
    links.used += per_sender

    def place_of(linear):
        return (linear // fsdp_size, linear % fsdp_size)

    def out_copy(to, number, slot):
        return pltpu.make_async_remote_copy(
            src_ref=out_grad.at[number], dst_ref=out_parts.at[slot],
            send_sem=send.at[out_base + number], recv_sem=receive.at[out_base + slot],
            device_id=place_of(to), device_id_type=MESH,
        )

    barrier = pltpu.get_barrier_semaphore()
    for device in near + beside:
        pl.semaphore_signal(barrier, inc=1, device_id=device, device_id_type=MESH)
    for origin, _ in out_origins:

        @pl.when(origin != grid.linear)
        def _(origin=origin):
            pl.semaphore_signal(
                barrier, inc=1, device_id=place_of(origin), device_id_type=MESH
            )

    to_self = (
        1 if spread_out else jnp.where(grid.linear // exp_size == grid.fsdp, 1, 0)
    )
    pl.semaphore_wait(barrier, len(near) + len(beside) + per_sender - to_self)

    first_copies = []
    for hop in range(x_size):
        mine = grid.x_from(hop)
        first_copies.append(
            links.copy(
                first.at[grid.sibling(mine)], first_in.at[hop], (grid.exp, sibling), first_in.at[hop]
            )
        )
        first_copies[-1][0].start()
    z_hops = list(range(1, z_size)) + [0]
    beside_copies = []
    for z_hop in z_hops:
        beside_copies.append([])
        for hop in range(1, y_size):
            to = (grid.y + hop) % y_size
            landing = planes_in.at[hop - 1, z_hop]
            beside_copies[-1].append(
                links.copy(
                    planes.at[(grid.z + z_hop) % z_size, to], landing, grid.at(y=to), landing
                )
            )
            beside_copies[-1][-1][0].start()
    along_x = []
    features = first.shape[1]
    pieces = [pl.ds(0, features // 2), pl.ds(features // 2, features // 2)]
    for hop in range(x_size):
        first_copies[hop][1].wait_recv()
        summed = first[grid.x_from(hop)].astype(F32) + first_in[hop].astype(F32)
        if hop == 0:
            first_parts[0] = summed.astype(BF16)
        else:
            first_sum[hop - 1] = summed.astype(BF16)
            for piece in pieces:
                along_x.append(
                    links.copy(
                        first_sum.at[hop - 1, piece, :], first_parts.at[hop, piece, :],
                        (grid.exp, grid.x_from(hop)), first_parts.at[hop, piece, :],
                    )
                )
            along_x[-2][0].start()
    along_z = []
    for z_hop, copies in zip(z_hops, beside_copies):
        to_z = (grid.z + z_hop) % z_size
        summed = planes[to_z, grid.y].astype(F32)
        for number, (_, coming) in enumerate(copies):
            coming.wait_recv()
            summed = summed + planes_in[number, z_hop].astype(F32)
        plane_sum[z_hop] = summed.astype(BF16)
        if z_hop > 0:
            along_z.append(
                links.copy(
                    plane_sum.at[z_hop], along_in.at[z_hop - 1], grid.at(z=to_z),
                    along_in.at[z_hop - 1],
                )
            )
            along_z[-1][0].start()
    for to, number in out_sends:

        @pl.when(to != grid.linear)
        def _(to=to, number=number):
            out_copy(to, number, own_slot).start()

        @pl.when(to == grid.linear)
        def _(number=number):
            pltpu.make_async_copy(out_grad.at[number], out_parts.at[own_slot], own.at[0]).start()

    mix_rows(hidden, gates, columns, rows_back, output, local)
    summed = plane_sum[0].astype(F32)
    for number, (_, coming) in enumerate(along_z):
        coming.wait_recv()
        summed = summed + along_in[number].astype(F32)
    reduced[...] = summed.astype(BF16)
    placed = []
    for turn in range(1, fsdp_size):
        to = (grid.fsdp + turn) % fsdp_size
        origin = (grid.fsdp + fsdp_size - turn) % fsdp_size
        placed.append(
            links.copy(
                reduced.at[to], plane_parts.at[grid.fsdp], (grid.exp, to), plane_parts.at[origin]
            )
        )
        placed[-1][0].start()
    for going, _ in along_x[1::2]:
        going.start()
    kept = pltpu.make_async_copy(reduced.at[grid.fsdp], plane_parts.at[grid.fsdp], own.at[1])
    kept.start()
    for going, coming in along_x + placed:
        coming.wait_recv()
    for going, _ in first_copies + along_x + along_z + placed:
        going.wait_send()
    for copies in beside_copies:
        for going, _ in copies:
            going.wait_send()
    kept.wait()
    for origin, slot in out_origins:

        @pl.when(origin != grid.linear)
        def _(origin=origin, slot=slot):
            out_copy(origin, 0, slot).wait_recv()

    for to, number in out_sends:

        @pl.when(to != grid.linear)
        def _(to=to, number=number):
            out_copy(to, number, own_slot).wait_send()

        @pl.when(to == grid.linear)
        def _(number=number):
            pltpu.make_async_copy(out_grad.at[number], out_parts.at[own_slot], own.at[0]).wait()


def mix_rows(hidden, gates, columns, rows_in, output, local):
    members, _, capacity, model_width = rows_in.shape
    routes, slots = int_columns(columns)
    total = hidden[...]
    picked = [jnp.zeros(hidden.shape, F32), jnp.zeros(hidden.shape, F32)]
    for index in range(local):
        picks = local_picks(routes, slots, capacity, local, index, members * capacity)
        values = rows_in[:, index].reshape(members * capacity, model_width)
        for k in range(2):
            picked[k] = picked[k] + matmul(jnp.where(picks[k], 1.0, 0.0).astype(BF16), values)
    for k in range(2):
        total = total + gates[:, k : k + 1] * picked[k]
    output[...] = total.astype(BF16)


def finish_kernel(
    first_parts, plane_parts, out_parts, tokens, grad_hidden, attention_in, attention_gain, counts,
    grad_tokens, grad_gain, grad_in, grad_out, grad_mixture, grad_router, grad_table, balance,
    *, lanes, heads, width, head_count, experts, token_total,
):
    total = jnp.sum(first_parts[...].astype(F32), axis=0).T
    inputs = tokens[...].astype(F32)
    scale = lax.rsqrt(jnp.mean(inputs * inputs, axis=1, keepdims=True) + EPSILON)
    normed = inputs * scale
    grad_tokens[...] = grad_hidden[...] + scale * (
        total - normed * jnp.mean(total * normed, axis=1, keepdims=True)
    )
    fsdp_size = plane_parts.shape[0]
    model_width = head_count * width
    sums = [plane_parts[place].astype(F32) for place in range(fsdp_size)]
    columns = []
    for kind in range(3):
        pieces = [
            sums[place][:, kind * heads * width : (kind + 1) * heads * width]
            for place in range(fsdp_size)
        ]
        columns.append(jnp.concatenate(pieces, axis=1)[:, :model_width])
    gathered = jnp.concatenate(columns, axis=1)
    feature_rows = gathered.shape[0]
    gain = jnp.sum(gathered * attention_in[...].astype(F32), axis=1, keepdims=True)
    gain = padded_rows(jnp.broadcast_to(gain, (feature_rows, 128)), 128).T
    grad_gain[...] = gain[0:1, :feature_rows]
    grad_in[...] = gathered * as_column(attention_gain[...], feature_rows)
    grad_out[...] = jnp.sum(out_parts[...].astype(F32), axis=0)
    extra = sum(part[:, lanes.base :] for part in sums)
    extra_t = padded_rows(extra, 128).T
    grad_mixture[...] = extra_t[lanes.gain : lanes.gain + 1, :feature_rows]
    grad_router[...] = extra_t[lanes.router : lanes.router + experts, :feature_rows]
    grad_table[...] = extra[: grad_table.shape[0], lanes.table : lanes.table + head_count]
    mass = jnp.broadcast_to(extra[0:1], (8, lanes.extra))
    mass = pltpu.roll(mass, lanes.extra - lanes.shift, 1)
    lane = expert_lane(mass.shape, lanes)
    terms = jnp.where((lane >= 0) & (lane < experts), mass * counts[...], 0.0)[0:1]
    balance[...] = jnp.sum(terms, axis=1, keepdims=True) * (
        experts / (2.0 * token_total * token_total)
    )


def sum_kernel(*refs, layout, local):
    outputs = refs[len(layout) :]
    early_blocks = pl.num_programs(0) // 2
    totals = {}
    number = 0
    while number < len(layout):
        index, which, halves = layout[number]
        shape = outputs[which].shape[1:]
        value = refs[number][...].reshape(shape).astype(F32)
        if halves:
            rest = refs[number + 1][...].reshape(shape).astype(F32)
            value = jnp.where(pl.program_id(0) < early_blocks, value, rest)
            number += 1
        totals[index, which] = totals[index, which] + value if (index, which) in totals else value
        number += 1
    for (index, which), total in totals.items():
        outputs[which][index] = total


def sum_grads(groups, up_shape, down_shape, blocks):
    local = len(groups)
    depth, part = up_shape[1], down_shape[1]
    finer = 2 if depth % 32 == 0 and part // blocks % 32 == 0 else 1
    blocks = blocks * finer
    sizes = ((depth // finer, part), (part // blocks, down_shape[2]))
    arrays, specs, layout = [], [], []
    early = blocks // 2
    for index, group in enumerate(groups):
        for which, (size, (keep, taken, passed)) in enumerate(zip(sizes, group)):
            for array in (keep, taken, *passed):
                if isinstance(array, tuple):
                    arrays.extend(array)
                    specs.append(pl.BlockSpec(size, lambda c: (jnp.minimum(c, early - 1), 0)))
                    specs.append(pl.BlockSpec(size, lambda c: (jnp.maximum(c - early, 0), 0)))
                    layout.extend([(index, which, True)] * 2)
                else:
                    arrays.append(array)
                    specs.append(pl.BlockSpec(size, lambda c: (c, 0)))
                    layout.append((index, which, False))
    return pl.pallas_call(
        partial(sum_kernel, layout=layout, local=local),
        grid=(blocks,),
        in_specs=specs,
        out_specs=[
            pl.BlockSpec((local, depth // finer, part), lambda c: (0, c % finer, c // finer)),
            pl.BlockSpec((local, part // blocks, down_shape[2]), lambda c: (0, c, 0)),
        ],
        out_shape=(shape_of(up_shape, F32), shape_of(down_shape, F32)),
        compiler_params=params(),
        cost_estimate=hint(8),
        name="sum_grads",
    )(*arrays)


def over_x(array, hop):
    fsdp_size = lax.axis_size("fsdp")
    return lax.ppermute(array, "fsdp", [(i, (i + 2 * hop) % fsdp_size) for i in range(fsdp_size)])


def over_core(array):
    return lax.ppermute(array, "fsdp", [(i, i ^ 1) for i in range(lax.axis_size("fsdp"))])


def on_device(
    tokens,
    cotangent,
    segments,
    routes,
    slots,
    attention_gain,
    mixture_gain,
    attention_in,
    attention_out,
    router_weight,
    position_table,
    expert_up,
    expert_down,
):
    grid = Grid()
    exp_size, fsdp_size, chips = grid.exp_size, grid.fsdp_size, grid.x_size
    device_count = grid.device_count
    fsdp_index = lax.axis_index("fsdp")
    rows, model_width = tokens.shape
    length = rows * fsdp_size
    head_count = position_table.shape[1]
    width = model_width // head_count
    heads = -(-head_count // fsdp_size)
    padded_heads = heads * fsdp_size
    feature_rows, bucket_rows = attention_in.shape[0], position_table.shape[0]
    experts = router_weight.shape[1]
    local = expert_up.shape[0]
    capacity = 4 * rows // experts
    token_total = rows * device_count
    span = WINDOW + 2 * SKEW + QUERY_BLOCK
    lanes = Lanes(heads, width, padded_heads, experts)
    part = expert_down.shape[1]
    gain_row = attention_gain.reshape(1, feature_rows)
    late_rows = 2 * capacity // 3 if local > 1 and capacity % 48 == 0 else 0
    late = 1 if late_rows else 0

    shard_shapes = [shape_of((model_width, part), BF16), shape_of((part, model_width), BF16)]
    copies = (
        4 * fsdp_size + grid.z_size + grid.z_size * grid.y_size
        + grid.z_size + grid.y_size + grid.x_size + 1
    )
    started = pl.pallas_call(
        partial(
            start_kernel, lanes=lanes, heads=heads, width=width, head_count=head_count,
            experts=experts, capacity=capacity, local=local, late=late,
        ),
        out_shape=tuple(
            [
                shape_of((fsdp_size, rows, model_width), BF16),
                shape_of((grid.z_size, grid.y_size, fsdp_size, feature_rows, lanes.width), BF16),
                shape_of((exp_size, local * capacity - late_rows, model_width), BF16),
                shape_of((8, rows), F32),
                shape_of((rows, 128), F32),
                shape_of((grid.z_size, grid.y_size, chips, 2, feature_rows, model_width), BF16),
            ]
            + [shape_of((exp_size, late_rows, model_width), BF16)] * late
            + shard_shapes * local
        ),
        in_specs=[IN_VMEM] * 10 + [ANYWHERE] * 2,
        out_specs=tuple(
            [ANYWHERE, ANYWHERE, IN_VMEM, IN_VMEM, IN_VMEM, ANYWHERE]
            + [IN_VMEM] * late
            + [ANYWHERE] * (2 * local)
        ),
        scratch_shapes=[
            pltpu.VMEM((fsdp_size, feature_rows, lanes.width), BF16),
            pltpu.VMEM(expert_up.shape, BF16),
            pltpu.VMEM(expert_down.shape, BF16),
            dma_sems(copies),
            dma_sems(copies),
            dma_sems(3),
            dma_sems(2 * local),
            dma_sems(local * (fsdp_size + 1)),
        ],
        compiler_params=params(collective_id=0, has_side_effects=True),
        cost_estimate=hint(20),
        name="start",
    )(
        tokens, cotangent, routes.T, slots.T, gain_row, mixture_gain.reshape(1, feature_rows),
        attention_in, router_weight.T, position_table, attention_out, expert_up, expert_down,
    )
    all_tokens, all_planes, cotangent_early, position_rows, columns, full_out = started[:6]
    cotangent_late, started = started[6 : 6 + late], started[6 + late :]
    own_shards = [started[2 * index : 2 * index + 2] for index in range(local)]
    plane = all_planes.reshape(model_width, lanes.width)
    full_out = full_out.reshape(model_width, model_width)

    def along_x(array):
        return [over_x(array, -hop) for hop in range(1, chips)]

    near_up, near_down = [None] * local, [None] * local
    near_up[0] = along_x(own_shards[0][0])
    cotangent_in = lax.all_to_all(
        cotangent_early, "exp", split_axis=0, concat_axis=0, tiled=True
    )

    head_t = lambda size: pl.BlockSpec((heads, size, rows), lambda s, *_: (0, 0, s))
    head_n = lambda size: pl.BlockSpec((heads, rows, size), lambda s, *_: (0, s, 0))
    normed, query_t, key_n, query_n, value_n, key_t, value_t, bias, counts = pl.pallas_call(
        partial(
            project_kernel, heads=heads, width=width, lanes=lanes, feature_rows=feature_rows,
            bucket_rows=bucket_rows,
        ),
        grid=(fsdp_size,),
        in_specs=[
            pl.BlockSpec((1, rows, model_width), lambda s: (s, 0, 0)),
            whole((model_width, lanes.width)),
            pl.BlockSpec((1, rows), lambda s: (0, s)),
        ],
        out_specs=[
            pl.BlockSpec((rows, model_width), lambda s: (s, 0)),
            head_t(SKEW), head_n(SKEW), head_n(width), head_n(width), head_t(width), head_t(width),
            whole((heads, 1, span)),
            whole((8, lanes.extra)),
        ],
        out_shape=(
            shape_of((length, model_width), BF16),
            shape_of((heads, SKEW, length), BF16),
            shape_of((heads, length, SKEW), BF16),
            shape_of((heads, length, width), BF16),
            shape_of((heads, length, width), BF16),
            shape_of((heads, width, length), BF16),
            shape_of((heads, width, length), BF16),
            shape_of((heads, 1, span), F32),
            shape_of((8, lanes.extra), F32),
        ),
        scratch_shapes=[
            pltpu.VMEM((lanes.weights, model_width), BF16),
            pltpu.VMEM((lanes.extra, span), F32),
        ],
        compiler_params=params(),
        cost_estimate=hint(8),
        name="project",
    )(all_tokens, plane, segments.reshape(1, length))

    by_head = lambda *size: pl.BlockSpec((1,) + size, lambda h: (h, 0, 0))
    context, context_high, log_total, attended_t = pl.pallas_call(
        partial(attend_kernel, rows=rows),
        grid=(heads,),
        in_specs=[
            by_head(SKEW, length), by_head(length, SKEW), by_head(width, length), by_head(1, span),
        ],
        out_specs=[
            pl.BlockSpec((fsdp_size, width, rows), lambda h: (0, h, 0)),
            by_head(width, length),
            by_head(1, length),
            ANYWHERE,
        ],
        out_shape=(
            shape_of((fsdp_size, heads * width, rows), BF16),
            shape_of((heads, width, length), F32),
            shape_of((heads, 1, length), F32),
            shape_of((fsdp_size, heads * width, rows), BF16),
        ),
        scratch_shapes=[
            pltpu.VMEM((SKEW, span), F32),
            pltpu.VMEM((WINDOW + QUERY_BLOCK, QUERY_BLOCK), F32),
            pltpu.VMEM((heads, fsdp_size, width, rows), BF16),
            pltpu.SemaphoreType.DMA((heads, fsdp_size)),
            pltpu.SemaphoreType.DMA((heads, fsdp_size)),
            dma_sems(heads),
        ],
        compiler_params=params(collective_id=1, has_side_effects=True),
        cost_estimate=hint(13),
        name="attend",
    )(query_t, key_n, value_t, bias)

    own_down, near_up[0], attended_t = lax.optimization_barrier(
        (own_shards[0][1], near_up[0], attended_t)
    )
    near_down[0] = along_x(own_down)
    attended_t = attended_t.reshape(padded_heads * width, rows)

    later = [own_shards[index] for index in range(1, local)]
    attended_t, later = lax.optimization_barrier((attended_t, later))
    for index in range(1, local):
        near_up[index], near_down[index] = [along_x(array) for array in later[index - 1]]
    gate_lanes = -(-local * capacity // 128) * 128
    ready = [own_shards[0][0]] + near_up[0] + [own_shards[0][1]]
    copies = 2 * exp_size + len(ready)
    hidden, routed, probabilities, gates, outgoing, rows_in, gates_in, *crossed = pl.pallas_call(
        partial(
            route_kernel, experts=experts, lanes=lanes, capacity=capacity, crossing=len(ready)
        ),
        in_specs=[IN_VMEM] * 6 + [ANYWHERE] * len(ready),
        out_specs=tuple([IN_VMEM] * 5 + [ANYWHERE] * (2 + len(ready))),
        out_shape=tuple(
            [
                shape_of((rows, model_width), F32),
                shape_of((rows, model_width), BF16),
                shape_of((rows, lanes.extra), F32),
                shape_of((rows, 2), F32),
                shape_of((exp_size, local * capacity, model_width), BF16),
                shape_of((exp_size, capacity, model_width), BF16),
                shape_of((exp_size, 8, gate_lanes), F32),
            ]
            + [shape_of(array.shape, BF16) for array in ready]
        ),
        scratch_shapes=[
            pltpu.VMEM((exp_size, 8, gate_lanes), F32),
            dma_sems(copies),
            dma_sems(copies),
            dma_sems(2),
        ],
        compiler_params=params(collective_id=2, has_side_effects=True),
        cost_estimate=hint(35),
        name="route",
    )(tokens, attended_t, full_out, plane, columns, position_rows, *ready)
    outgoing = outgoing.reshape(exp_size, local, capacity, model_width)

    def down_parts(early, rest):
        return list(zip(early, rest))

    def pass_along(arrays):
        return [over_x(arrays[0][hop - 1], hop) for hop in range(1, chips)]

    swapped = (crossed[:-1], crossed[-1:])
    returned, groups, moved, outs = [], [], [], None
    late_rows_in = ()
    for index in range(local):
        final = index == local - 1
        carried = list(moved)
        if not final:
            carried.append((outgoing, index + 1))
        if index == 0 and late:
            carried.append((cotangent_late[0], None))
        result = run_expert(
            index, local, rows_in, gates_in, cotangent_in, late_rows_in if final else (),
            [own_shards[index][0]] + near_up[index], [own_shards[index][1]] + near_down[index],
            swapped, () if final else own_shards[index + 1], carried, outs, 3 + index,
        )
        (outs,) = result.rows_out
        arrived = list(result.moved_to)
        if index == 0 and late:
            late_rows_in = (arrived.pop(),)
        if not final:
            rows_in = arrived.pop()
            swapped = (result.next_swapped[:1], result.next_swapped[1:])
            moved = [(result.grad_rows[0], None), (result.grad_gates[0], None)]
        if arrived:
            returned.append(arrived)
        up_keep, up_taken, down_keep, down_taken = result.own
        if not final:
            passed = (result.pass_up, result.pass_down)
            passed, rows_in = lax.optimization_barrier((passed, rows_in))
            groups.append(
                [
                    (up_keep, up_taken, pass_along(passed[0])),
                    (down_keep, down_taken, pass_along(passed[1])),
                ]
            )
    returned.append([result.back_rows[0], result.back_gates[0]])
    groups, returned = lax.optimization_barrier((groups, returned))

    outs, returned = lax.optimization_barrier((outs, returned))
    out_rows = lax.all_to_all(outs, "exp", split_axis=0, concat_axis=0, tiled=True)

    padded_out = full_out
    if padded_heads > head_count:
        padded_out = jnp.pad(full_out, ((0, padded_heads * width - model_width), (0, 0)))
    copies = 2 * 2 * fsdp_size
    grad_hidden, small, grad_t, grad_n, out_grad = pl.pallas_call(
        partial(
            unroute_kernel, experts=experts, local=local, token_total=token_total, lanes=lanes,
            heads=heads, width=width,
        ),
        out_shape=(
            shape_of((rows, model_width), F32),
            shape_of((model_width, lanes.extra), F32),
            shape_of((heads, width, length), BF16),
            shape_of((heads, length, width), BF16),
            shape_of((heads * width, model_width), BF16),
        ),
        in_specs=[IN_VMEM] * 8 + [ANYWHERE] + [IN_VMEM] * (1 + 2 * local),
        out_specs=tuple([IN_VMEM] * 5),
        scratch_shapes=[
            pltpu.VMEM((fsdp_size, rows, model_width), BF16),
            pltpu.VMEM((heads * width, model_width), BF16),
            pltpu.VMEM((heads * width, model_width), F32),
            dma_sems(copies),
            dma_sems(copies),
            dma_sems(1),
        ],
        compiler_params=params(collective_id=4 + local, has_side_effects=True),
        cost_estimate=hint(1),
        name="unroute",
    )(
        hidden, cotangent, routed, probabilities, gates, plane, columns, counts, padded_out, context,
        *[part[0] for part in returned], *[part[1] for part in returned],
    )
    early = pass_along(result.early_down)
    early, pass_up, pass_down, grad_t = lax.optimization_barrier(
        (early, result.pass_up, result.pass_down, grad_t)
    )
    groups.append(
        [
            (up_keep, up_taken, pass_along(pass_up)),
            (down_keep, down_taken, down_parts(early, pass_along(pass_down))),
        ]
    )

    grad_projected, grad_bias = pl.pallas_call(
        partial(attend_back_kernel, scale=width ** (-0.5)),
        grid=(heads,),
        in_specs=[
            by_head(SKEW, length), by_head(length, SKEW), by_head(length, width),
            by_head(length, width), by_head(width, length), by_head(width, length),
            by_head(length, width), by_head(width, length), by_head(1, length), by_head(1, span),
        ],
        out_specs=[
            pl.BlockSpec((3, 1, width, length), lambda h: (0, h, 0, 0)),
            by_head(1, span),
        ],
        out_shape=(
            shape_of((3, heads, width, length), BF16),
            shape_of((heads, 1, span), F32),
        ),
        scratch_shapes=[
            pltpu.VMEM((SKEW, span), F32),
            pltpu.VMEM((SKEW, span), F32),
            pltpu.VMEM((length, width), F32),
            pltpu.VMEM((length, width), F32),
        ],
        compiler_params=params(),
        cost_estimate=hint(1),
        name="attend_back",
    )(query_t, key_n, query_n, value_n, key_t, grad_t, grad_n, context_high, log_total, bias)
    grad_projected = grad_projected.reshape(lanes.weights, length)

    grad_first, grad_plane = pl.pallas_call(
        partial(
            project_back_kernel, lanes=lanes, heads=heads, feature_rows=feature_rows,
            bucket_rows=bucket_rows,
        ),
        grid=(fsdp_size,),
        in_specs=[
            pl.BlockSpec((lanes.weights, rows), lambda s: (0, s)),
            pl.BlockSpec((rows, model_width), lambda s: (s, 0)),
            whole((model_width, lanes.width)),
            whole((model_width, lanes.extra)),
            whole((rows, lanes.extra)),
            whole((heads, 1, span)),
        ],
        out_specs=[
            pl.BlockSpec((1, model_width, rows), lambda s: (s, 0, 0)),
            whole((model_width, lanes.width)),
        ],
        out_shape=(
            shape_of((fsdp_size, model_width, rows), BF16),
            shape_of((model_width, lanes.width), BF16),
        ),
        scratch_shapes=[
            pltpu.VMEM((lanes.width, model_width), F32),
            pltpu.VMEM((lanes.extra, span), F32),
        ],
        compiler_params=params(),
        cost_estimate=hint(1),
        name="project_back",
    )(grad_projected, normed, plane, small, probabilities, grad_bias)

    out_rows, grad_first = lax.optimization_barrier((out_rows, grad_first))
    spread_out = heads * width * fsdp_size != model_width
    if spread_out:
        out_grad = lax.dynamic_update_slice(
            jnp.zeros((padded_heads * width, model_width), BF16), out_grad,
            (fsdp_index * heads * width, jnp.int32(0)),
        )[:model_width]
    out_grad = out_grad.reshape(-1, feature_rows, model_width)
    out_count = device_count if spread_out else exp_size
    plane_shape = (grid.z_size, grid.y_size, fsdp_size, feature_rows, lanes.width)
    parts_shape = (fsdp_size, feature_rows, lanes.width)
    copies = 4 * fsdp_size + grid.z_size * grid.y_size + grid.z_size + out_count
    first_parts, layer_output, plane_parts, out_parts = pl.pallas_call(
        partial(last_kernel, spread_out=spread_out, local=local),
        out_shape=(
            shape_of((chips, model_width, rows), BF16),
            shape_of((rows, model_width), BF16),
            shape_of(parts_shape, BF16),
            shape_of((out_count, feature_rows, model_width), BF16),
        ),
        in_specs=[IN_VMEM] * 7,
        out_specs=(IN_VMEM, IN_VMEM, ANYWHERE, ANYWHERE),
        scratch_shapes=[
            pltpu.VMEM((chips, model_width, rows), BF16),
            pltpu.VMEM((max(chips - 1, 1), model_width, rows), BF16),
            pltpu.VMEM((max(grid.y_size - 1, 1), grid.z_size) + parts_shape, BF16),
            pltpu.VMEM((grid.z_size,) + parts_shape, BF16),
            pltpu.VMEM((max(grid.z_size - 1, 1),) + parts_shape, BF16),
            pltpu.VMEM(parts_shape, BF16),
            dma_sems(copies),
            dma_sems(copies),
            dma_sems(2),
        ],
        compiler_params=params(collective_id=5 + local, has_side_effects=True),
        cost_estimate=hint(1),
        name="last",
    )(grad_first, grad_plane.reshape(plane_shape), out_grad, hidden, gates, columns, out_rows)

    groups, first_parts = lax.optimization_barrier((groups, first_parts))
    (
        grad_tokens, gain_grad, in_grad, out_sum, mixture_gain_grad, router_grad, table_grad, balance,
    ) = pl.pallas_call(
        partial(
            finish_kernel, lanes=lanes, heads=heads, width=width, head_count=head_count,
            experts=experts, token_total=token_total,
        ),
        out_shape=(
            shape_of((rows, model_width), F32),
            shape_of((1, feature_rows), F32),
            shape_of((feature_rows, 3 * model_width), F32),
            shape_of((feature_rows, model_width), F32),
            shape_of((1, feature_rows), F32),
            shape_of((experts, feature_rows), F32),
            shape_of((bucket_rows, head_count), F32),
            shape_of((1, 1), F32),
        ),
        compiler_params=params(),
        cost_estimate=hint(6),
        name="finish",
    )(first_parts, plane_parts, out_parts, tokens, grad_hidden, attention_in, gain_row, counts)

    up_grad, down_grad = sum_grads(groups, expert_up.shape, expert_down.shape, fsdp_size)
    return (
        layer_output,
        balance.reshape(()),
        grad_tokens,
        gain_grad.reshape(feature_rows),
        mixture_gain_grad.reshape(feature_rows),
        in_grad,
        out_sum,
        router_grad.T,
        table_grad,
        up_grad,
        down_grad,
    )


def solution(mesh):
    in_specs = (
        P(("exp", "fsdp"), None),
        P(("exp", "fsdp"), None),
        P("exp"),
        P(("exp", "fsdp"), None),
        P(("exp", "fsdp"), None),
        P(("exp", "fsdp")),
        P(("exp", "fsdp")),
        P(("exp", "fsdp"), None),
        P(("exp", "fsdp"), None),
        P(("exp", "fsdp"), None),
        P(("exp", "fsdp"), None),
        P("exp", "fsdp", None),
        P("exp", "fsdp", None),
    )
    out_specs = (
        P(("exp", "fsdp"), None),
        P(),
        P(("exp", "fsdp"), None),
        P(("exp", "fsdp")),
        P(("exp", "fsdp")),
        P(("exp", "fsdp"), None),
        P(("exp", "fsdp"), None),
        P(("exp", "fsdp"), None),
        P(("exp", "fsdp"), None),
        P("exp", "fsdp", None),
        P("exp", "fsdp", None),
    )
    return jax.shard_map(
        on_device, mesh=mesh, in_specs=in_specs, out_specs=out_specs, check_vma=False
    )
```

```python
from functools import partial

import jax
import jax.numpy as jnp
from jax import lax
from jax.experimental import pallas as pl
from jax.experimental.pallas import tpu as pltpu
from jax.sharding import PartitionSpec as P

WINDOW = 1024
BUCKETS = 256

EPSILON = 1e-06
AUX_WEIGHT = 0.01
MASKED = -1e30
QUERY_BLOCK = 256
SKEW = 128
VMEM_BYTES = 58 * 1024 * 1024
MESH = pl.DeviceIdType.MESH
F32 = jnp.float32
BF16 = jnp.bfloat16


def params(**kwargs):
    return pltpu.CompilerParams(vmem_limit_bytes=VMEM_BYTES, **kwargs)


def shape_of(shape, dtype):
    return jax.ShapeDtypeStruct(shape, dtype)


def whole(shape):
    return pl.BlockSpec(shape, lambda *_: (0,) * len(shape))


def contract_last(left_side, right_side):
    return lax.dot_general(
        left_side, right_side, (((1,), (1,)), ((), ())), preferred_element_type=F32
    )


def matmul(left_side, right_side):
    return jnp.dot(left_side, right_side, preferred_element_type=F32)


def turned(value):
    return value.astype(F32).T


def bucket_index(distance):
    near_count = BUCKETS // 2
    spread = max(WINDOW - near_count, 1)
    far_bucket = (
        near_count + jnp.maximum(distance - near_count, 0) * (BUCKETS - near_count) // spread
    )
    return jnp.where(distance < near_count, distance, far_bucket)

def hint(micros):
    return pl.CostEstimate(flops=int(micros * 1.0e9), bytes_accessed=1024, transcendentals=0)


def flipped(place, other, size):
    result, bit = 0, 1
    while bit < size:
        result = result + bit * ((place // bit + other // bit) % 2)
        bit *= 2
    return result


class Grid:
    def __init__(self):
        self.exp_size, self.fsdp_size = lax.axis_size("exp"), lax.axis_size("fsdp")
        self.device_count = self.exp_size * self.fsdp_size
        self.y_size = max(
            y for y in range(1, self.exp_size + 1) if self.exp_size % y == 0 and 2 * y * y <= self.exp_size
        ) if self.exp_size > 1 else 1
        self.z_size = self.exp_size // self.y_size
        self.x_size = self.fsdp_size // 2

    def here(self):
        self.exp, self.fsdp = lax.axis_index("exp"), lax.axis_index("fsdp")
        self.z, self.y = self.exp // self.y_size, self.exp % self.y_size
        self.x, self.core = self.fsdp // 2, self.fsdp % 2
        self.linear = self.exp * self.fsdp_size + self.fsdp
        return self

    def at(self, z=None, y=None, fsdp=None):
        z = self.z if z is None else z
        y = self.y if y is None else y
        return (z * self.y_size + y, self.fsdp if fsdp is None else fsdp)

    def x_from(self, hop):
        return ((self.x + self.x_size + hop) % self.x_size) * 2 + self.core

    def source_z(self, turn):
        if self.z_size & (self.z_size - 1) == 0:
            return flipped(self.z, turn, self.z_size)
        return (self.z + turn) % self.z_size

    def target_z(self, turn):
        if self.z_size & (self.z_size - 1) == 0:
            return flipped(self.z, turn, self.z_size)
        return (self.z + self.z_size - turn) % self.z_size

    def exp_steps(self):
        turns = sorted(range(self.z_size), key=lambda turn: -turn.bit_length())
        steps = []
        for turn in turns:
            for hop in range(self.y_size):
                if turn or hop:
                    to = self.target_z(turn) * self.y_size + (self.y + self.y_size - hop) % self.y_size
                    origin = self.source_z(turn) * self.y_size + (self.y + hop) % self.y_size
                    steps.append((to, origin))
        return steps

    def sibling(self, fsdp):
        return fsdp + 1 - 2 * (fsdp % 2)


class Links:
    def __init__(self, send, receive):
        self.send, self.receive, self.used = send, receive, 0

    def copy(self, source, target, device, landing):
        index = self.used
        self.used += 1
        going = pltpu.make_async_remote_copy(
            src_ref=source, dst_ref=target, send_sem=self.send.at[index],
            recv_sem=self.receive.at[index], device_id=device, device_id_type=MESH,
        )
        coming = pltpu.make_async_remote_copy(
            src_ref=landing, dst_ref=landing, send_sem=self.send.at[index],
            recv_sem=self.receive.at[index], device_id=device, device_id_type=MESH,
        )
        return going, coming


def greet(devices):
    barrier = pltpu.get_barrier_semaphore()
    for device in devices:
        pl.semaphore_signal(barrier, inc=1, device_id=device, device_id_type=MESH)
    pl.semaphore_wait(barrier, len(devices))


def chip_peers(grid):
    peers = [(grid.exp, grid.sibling(grid.fsdp))]
    return peers + [(grid.exp, grid.x_from(hop)) for hop in range(1, grid.x_size)]


class ChipGather:
    def __init__(self, grid, links, own_sem, source, target):
        self.grid, self.links, self.target = grid, links, target
        self.own = pltpu.make_async_copy(source, target.at[grid.fsdp], own_sem)
        sibling = grid.sibling(grid.fsdp)
        self.along_x, self.across = [], []
        for hop in range(1, grid.x_size):
            self.along_x.append(
                links.copy(
                    source, target.at[grid.fsdp], (grid.exp, grid.x_from(hop)),
                    target.at[grid.x_from(-hop)],
                )
            )
        self.across.append(
            links.copy(source, target.at[grid.fsdp], (grid.exp, sibling), target.at[sibling])
        )

    def start(self):
        for going, _ in self.along_x + self.across:
            going.start()
        self.own.start()

    def forward(self):
        grid = self.grid
        for hop in range(1, grid.x_size):
            self.along_x[hop - 1][1].wait_recv()
            held = grid.x_from(-hop)
            other = grid.sibling(held)
            self.across.append(
                self.links.copy(
                    self.target.at[held], self.target.at[held],
                    (grid.exp, grid.sibling(grid.fsdp)), self.target.at[other],
                )
            )
            self.across[-1][0].start()

    def finish(self):
        for _, coming in self.across:
            coming.wait_recv()
        for going, _ in self.along_x + self.across:
            going.wait_send()
        self.own.wait()


class Exchange:
    def __init__(self, grid, links, own_sems, pairs):
        self.steps = grid.exp_steps()
        self.peers = [(to, grid.fsdp) for to, _ in self.steps]
        self.copies, self.own = [], []
        for index, (source, target) in enumerate(pairs):
            for to, origin in self.steps:
                self.copies.append(
                    links.copy(
                        source(to), target.at[grid.exp], (to, grid.fsdp), target.at[origin]
                    )
                )
            self.own.append(
                pltpu.make_async_copy(source(grid.exp), target.at[grid.exp], own_sems.at[index])
            )

    def start(self):
        for going, _ in self.copies:
            going.start()
        for own in self.own:
            own.start()

    def finish(self):
        for going, coming in self.copies:
            coming.wait_recv()
            going.wait_send()
        for own in self.own:
            own.wait()


ANYWHERE = pl.BlockSpec(memory_space=pl.ANY)
IN_VMEM = pl.BlockSpec(memory_space=pltpu.VMEM)


def dma_sems(count):
    return pltpu.SemaphoreType.DMA((count,))


def plane_of(source, part, to):
    return source.at[to] if part is None else source.at[to, part]


class Lanes:
    def __init__(self, heads, width, padded_heads, experts):
        self.weights = 3 * heads * width
        self.base = self.weights // 128 * 128
        self.router = self.weights - self.base
        self.gain = self.router + experts
        self.table = self.gain + 1
        self.count = self.table + padded_heads
        self.width = -(-(self.weights + 2 * experts + 1 + padded_heads) // 128) * 128
        self.extra = self.width - self.base
        self.shift = self.count - self.router


def bucket_rows_select(features, feature_rows, bucket_rows, span):
    row = lax.broadcasted_iota(jnp.int32, (features, 1), 0)
    within = lax.rem(row, feature_rows)
    bucket = jnp.where(
        within < bucket_rows, lax.div(row, feature_rows) * bucket_rows + within, -1
    )
    distance = lax.broadcasted_iota(jnp.int32, (1, span), 1) - SKEW
    near = BUCKETS // 2
    spread = max(WINDOW - near, 1)
    far = near + lax.div(jnp.maximum(distance - near, 0) * (BUCKETS - near), spread)
    wanted = jnp.where(distance < near, distance, far)
    reachable = (distance >= 0) & (distance < WINDOW)
    wanted = jnp.where(reachable, wanted, -2)
    return jnp.where(bucket == wanted, 1.0, 0.0).astype(BF16), reachable


def as_column(row, size):
    row_place = lax.broadcasted_iota(jnp.int32, (size, size), 0)
    lane = lax.broadcasted_iota(jnp.int32, (size, size), 1)
    spread = jnp.broadcast_to(row.astype(F32), (size, size))
    return jnp.sum(jnp.where(row_place == lane, spread, 0.0), axis=1, keepdims=True)


def padded_rows(value, rows):
    if value.shape[0] == rows:
        return value
    return jnp.concatenate([value, jnp.zeros((rows - value.shape[0], value.shape[1]), F32)], axis=0)


def padded_lanes(value, lanes):
    if value.shape[1] == lanes:
        return value
    return jnp.concatenate([value, jnp.zeros((value.shape[0], lanes - value.shape[1]), F32)], axis=1)


class Wide:
    def __init__(self, grid, links, own_sem, source, target):
        self.grid, self.links, self.target = grid, links, target
        self.own = pltpu.make_async_copy(
            source, target.at[grid.z, grid.y, grid.x, grid.core], own_sem
        )
        stage = []
        for hop in range(1, grid.z_size):
            origin = (grid.z + grid.z_size - hop) % grid.z_size
            stage.append(
                links.copy(
                    source, target.at[grid.z, grid.y, grid.x, grid.core],
                    grid.at(z=(grid.z + hop) % grid.z_size),
                    target.at[origin, grid.y, grid.x, grid.core],
                )
            )
        self.stages = [stage]

    def start(self):
        self.own.start()
        for going, _ in self.stages[0]:
            going.start()

    def turn(self, axis):
        grid, target = self.grid, self.target
        for _, coming in self.stages[-1]:
            coming.wait_recv()
        stage = []
        if axis == 0:
            self.own.wait()
            held = target.at[:, grid.y, grid.x, grid.core]
            for hop in range(1, grid.y_size):
                origin = (grid.y + grid.y_size - hop) % grid.y_size
                stage.append(
                    self.links.copy(
                        held, held, grid.at(y=(grid.y + hop) % grid.y_size),
                        target.at[:, origin, grid.x, grid.core],
                    )
                )
        elif axis == 1:
            held = target.at[:, :, grid.x, grid.core]
            for hop in range(1, grid.x_size):
                origin = (grid.x + grid.x_size - hop) % grid.x_size
                stage.append(
                    self.links.copy(
                        held, held, (grid.exp, grid.x_from(hop)),
                        target.at[:, :, origin, grid.core],
                    )
                )
        else:
            held = target.at[:, :, :, grid.core]
            stage.append(
                self.links.copy(
                    held, held, (grid.exp, grid.sibling(grid.fsdp)), target.at[:, :, :, 1 - grid.core]
                )
            )
        for going, _ in stage:
            going.start()
        self.stages.append(stage)

    def finish(self):
        for _, coming in self.stages[-1]:
            coming.wait_recv()
        for stage in self.stages:
            for going, _ in stage:
                going.wait_send()


def start_kernel(
    tokens, cotangent, routes_t, slots_t, attention_gain, mixture_gain, attention_in, router_t, table,
    attention_out, expert_up, expert_down, *refs, lanes, heads, width, head_count, experts, capacity,
    local, late,
):
    all_tokens, all_planes, cotangent_early, position_rows, columns, full_out = refs[:6]
    cotangent_late, refs = refs[6 : 6 + late], refs[6 + late :]
    shards = refs[: 2 * local]
    planes, up_stage, down_stage, send, receive, own, fetch, split = refs[2 * local :]
    grid = Grid().here()
    links = Links(send, receive)
    z_size, y_size, fsdp_size = grid.z_size, grid.y_size, grid.fsdp_size
    near = [
        (grid.exp, (grid.fsdp + turn) % fsdp_size) for turn in range(1, fsdp_size)
    ] + [grid.at(z=(grid.z + hop) % z_size) for hop in range(1, z_size)]
    beside = [grid.at(y=(grid.y + hop) % y_size) for hop in range(1, y_size)]
    gathered = ChipGather(grid, links, own.at[0], tokens, all_tokens)
    widely = Wide(grid, links, own.at[2], attention_out, full_out)
    part = expert_down.shape[1]
    depth = expert_up.shape[1]
    fetches = []
    for index in range(local):
        fetches.append(
            pltpu.make_async_copy(expert_up.at[index], up_stage.at[index], fetch.at[2 * index])
        )
        fetches.append(
            pltpu.make_async_copy(
                expert_down.at[index], down_stage.at[index], fetch.at[2 * index + 1]
            )
        )
    greet(near + beside)
    widely.start()
    for copy in fetches:
        copy.start()

    feature_rows = attention_in.shape[0]
    model_width = head_count * width
    gained = attention_in[...].astype(F32) * as_column(attention_gain[...], feature_rows)
    route_rows, slot_rows = routes_t[...].astype(F32), slots_t[...].astype(F32)
    columns[...] = padded_rows(jnp.concatenate([route_rows, slot_rows], axis=0), 128).T
    row_count = columns.shape[0]
    expert_lanes = lax.broadcasted_iota(jnp.int32, (row_count, experts), 1).astype(F32)
    named = jnp.zeros((row_count, experts), F32)
    for k in range(2):
        named = named + jnp.where(expert_lanes == columns[:, k : k + 1], 1.0, 0.0)
    named = jnp.sum(named, axis=0, keepdims=True)
    place = lax.broadcasted_iota(jnp.int32, (feature_rows, feature_rows), 0)
    same = place == lax.broadcasted_iota(jnp.int32, (feature_rows, feature_rows), 1)
    router = contract_last(jnp.where(same, 1.0, 0.0).astype(BF16), router_t[...])
    pieces = [
        router,
        as_column(mixture_gain[...], feature_rows),
        padded_rows(padded_lanes(table[...].astype(F32), heads * fsdp_size), feature_rows),
        padded_rows(named, feature_rows),
    ]
    taken = sum(piece.shape[1] for piece in pieces)
    if lanes.width > lanes.weights + taken:
        pieces.append(jnp.zeros((feature_rows, lanes.width - lanes.weights - taken), F32))
    for place in range(fsdp_size):
        first, last = place * heads * width, min((place + 1) * heads * width, model_width)
        own_pieces = []
        for kind in range(3):
            if last > first:
                own_pieces.append(gained[:, kind * model_width + first : kind * model_width + last])
            if last - first < heads * width:
                own_pieces.append(
                    jnp.zeros((feature_rows, heads * width - max(last - first, 0)), F32)
                )
        planes[place] = jnp.concatenate(own_pieces + pieces, axis=1).astype(BF16)
    placed = []
    for turn in range(1, fsdp_size):
        to = (grid.fsdp + turn) % fsdp_size
        origin = (grid.fsdp + fsdp_size - turn) % fsdp_size
        placed.append(
            links.copy(
                planes.at[to], all_planes.at[grid.z, grid.y, grid.fsdp], (grid.exp, to),
                all_planes.at[grid.z, grid.y, origin],
            )
        )
        placed[-1][0].start()
    kept = pltpu.make_async_copy(
        planes.at[grid.fsdp], all_planes.at[grid.z, grid.y, grid.fsdp], own.at[1]
    )
    kept.start()
    gathered.start()
    for _, coming in placed:
        coming.wait_recv()
    kept.wait()

    def over_y(z):
        for turn in range(1, y_size):
            forwarded.append(
                links.copy(
                    all_planes.at[z, grid.y],
                    all_planes.at[z, grid.y],
                    grid.at(y=(grid.y + turn) % y_size),
                    all_planes.at[z, (grid.y + y_size - turn) % y_size],
                )
            )
            forwarded[-1][0].start()

    along_z, forwarded = [], []
    for hop in range(1, z_size):
        along_z.append(
            links.copy(
                all_planes.at[grid.z, grid.y],
                all_planes.at[grid.z, grid.y],
                grid.at(z=(grid.z + hop) % z_size),
                all_planes.at[(grid.z + z_size - hop) % z_size, grid.y],
            )
        )
        along_z[-1][0].start()
    over_y(grid.z)
    widely.turn(0)

    for copy in fetches:
        copy.wait()
    splits = []
    for index in range(local):
        up, down = shards[2 * index : 2 * index + 2]
        stores = [
            (
                up_stage.at[index, :, pl.ds(block * part, part)],
                up.at[pl.ds(block * depth, depth), :],
            )
            for block in range(fsdp_size)
        ]
        for source, target in stores + [(down_stage.at[index], down)]:
            splits.append(pltpu.make_async_copy(source, target, split.at[len(splits)]))
            splits[-1].start()

    widely.turn(1)

    place = route_rows * capacity + slot_rows
    position_rows[...] = padded_rows(place, 8)
    select_rows([cotangent_early] + list(cotangent_late), place, cotangent[...])

    for hop in range(1, z_size):
        along_z[hop - 1][1].wait_recv()
        over_y((grid.z + z_size - hop) % z_size)
    gathered.forward()
    widely.turn(2)
    for going, coming in forwarded:
        coming.wait_recv()
        going.wait_send()
    for going, _ in placed + along_z:
        going.wait_send()
    gathered.finish()
    widely.finish()
    for copy in splits:
        copy.wait()


def project_kernel(
    tokens, plane, segments, normed, query_t, key_n, query_n, value_n, key_t, value_t, bias, counts,
    weight_t, table_t, *, heads, width, lanes, feature_rows, bucket_rows,
):
    @pl.when(pl.program_id(0) == 0)
    def _():
        weight_t[...] = turned(plane[:, : lanes.weights]).astype(BF16)
        extra = plane[:, lanes.base :]
        span = bias.shape[2]
        select, reachable = bucket_rows_select(plane.shape[0], feature_rows, bucket_rows, span)
        table_t[...] = lax.dot_general(
            extra, select, (((0,), (0,)), ((), ())), preferred_element_type=F32
        )
        first = lanes.table + lax.axis_index("fsdp") * heads
        for head in range(heads):
            bias[head] = jnp.where(reachable, table_t[pl.ds(first + head, 1), :], MASKED)
        summed = jnp.sum(extra.astype(F32), axis=0, keepdims=True)
        counts[...] = pltpu.roll(
            jnp.broadcast_to(summed, counts.shape), lanes.extra - lanes.shift, 1
        )

    inputs = tokens[0].astype(F32)
    scale = lax.rsqrt(jnp.mean(inputs * inputs, axis=1, keepdims=True) + EPSILON)
    low = (inputs * scale).astype(BF16)
    normed[...] = low
    rows = low.shape[0]
    projected = contract_last(weight_t[...], low).astype(BF16).astype(F32)
    document = segments[...] % 4
    places = lax.broadcasted_iota(jnp.int32, (8, rows), 0)
    same = places == document
    hot = jnp.where(same, 1.0, 0.0)
    barred = jnp.where(same | (places >= 4), 0.0, MASKED)
    filler = jnp.zeros((SKEW - 8 - width, rows), F32)
    for head in range(heads):
        query = projected[head * width : (head + 1) * width] * width ** (-0.5)
        key = projected[(heads + head) * width : (heads + head + 1) * width]
        value = projected[(2 * heads + head) * width : (2 * heads + head + 1) * width]
        query_t[head] = jnp.concatenate([query, barred, filler], axis=0).astype(BF16)
        key_n[head] = jnp.concatenate([key, hot, filler], axis=0).T.astype(BF16)
        query_n[head] = query.T.astype(BF16)
        value_n[head] = value.T.astype(BF16)
        key_t[head] = key.astype(BF16)
        value_t[head] = value.astype(BF16)


def spans(length):
    for query_start in range(0, length, QUERY_BLOCK):
        key_start = max(0, query_start - WINDOW)
        yield query_start, key_start, query_start + QUERY_BLOCK - key_start


def spread_bias(bias, skew):
    skew[...] = pltpu.roll(
        jnp.broadcast_to(bias[0], skew.shape), 0, 1, stride=1, stride_axis=0
    )


def attend_kernel(
    query_t, key_n, value_t, bias, context, context_high, log_total, attended, skew, scores, held,
    send, receive, own, *, rows,
):
    head = pl.program_id(0)
    width = value_t.shape[1]
    grid = Grid().here()
    fsdp_size = grid.fsdp_size

    def leave(number):
        place = pl.ds(pl.multiple_of(number * width, 16), width)
        copies = []
        for turn in range(1, fsdp_size):
            to = (grid.fsdp + turn) % fsdp_size
            origin = (grid.fsdp + fsdp_size - turn) % fsdp_size
            sems = dict(
                send_sem=send.at[number, turn], recv_sem=receive.at[number, turn],
                device_id=(grid.exp, to), device_id_type=MESH,
            )
            copies.append(
                (
                    pltpu.make_async_remote_copy(
                        src_ref=held.at[number, to], dst_ref=attended.at[grid.fsdp, place, :], **sems
                    ),
                    pltpu.make_async_remote_copy(
                        src_ref=attended.at[origin, place, :], dst_ref=attended.at[origin, place, :],
                        **sems,
                    ),
                )
            )
        kept = pltpu.make_async_copy(
            held.at[number, grid.fsdp], attended.at[grid.fsdp, place, :], own.at[number]
        )
        return copies, kept

    @pl.when(head == 0)
    def _():
        greet([(grid.exp, (grid.fsdp + turn) % fsdp_size) for turn in range(1, fsdp_size)])

    spread_bias(bias, skew)
    for query_start, key_start, key_count in spans(query_t.shape[2]):
        queries = slice(query_start, query_start + QUERY_BLOCK)
        keys = slice(key_start, key_start + key_count)
        raw = matmul(key_n[0, keys, :], query_t[0, :, queries])
        for start in range(0, key_count, SKEW):
            offset = query_start - key_start - start + SKEW
            scores[start : start + SKEW, :] = (
                raw[start : start + SKEW] + skew[:, offset : offset + QUERY_BLOCK]
            )
        high = jnp.max(scores[:key_count, :], axis=0, keepdims=True)
        weights = jnp.exp(scores[:key_count, :] - high)
        total = jnp.sum(weights, axis=0, keepdims=True)
        gathered = matmul(value_t[0, :, keys], weights.astype(BF16)) / total
        context_high[0, :, queries] = gathered
        log_total[0, :, queries] = high + jnp.log(total)
        for start in range(0, QUERY_BLOCK, 128):
            place = query_start + start
            piece = gathered[:, start : start + 128].astype(BF16)
            context[place // rows, :, place % rows : place % rows + 128] = piece
            held[head, place // rows, :, place % rows : place % rows + 128] = piece
    copies, kept = leave(head)
    for going, _ in copies:
        going.start()
    kept.start()

    @pl.when(head == pl.num_programs(0) - 1)
    def _():
        def finish(number, carry):
            copies, kept = leave(number)
            for going, coming in copies:
                coming.wait_recv()
                going.wait_send()
            kept.wait()
            return carry

        lax.fori_loop(0, pl.num_programs(0), finish, 0)


def attend_back_kernel(
    query_t, key_n, query_n, value_n, key_t, grad_t, grad_n, context_high, log_total, bias,
    grad_projected, grad_bias, skew, grad_skew, grad_key, grad_value, *, scale,
):
    spread_bias(bias, skew)
    grad_skew[...] = jnp.zeros_like(grad_skew)
    grad_key[...] = jnp.zeros_like(grad_key)
    grad_value[...] = jnp.zeros_like(grad_value)
    inner = jnp.sum(grad_t[0].astype(F32) * context_high[0], axis=0, keepdims=True)
    for query_start, key_start, key_count in spans(query_t.shape[2]):
        queries = slice(query_start, query_start + QUERY_BLOCK)
        keys = slice(key_start, key_start + key_count)
        raw = matmul(key_n[0, keys, :], query_t[0, :, queries])
        grad_weights = matmul(value_n[0, keys, :], grad_t[0, :, queries])
        weights_low, grad_low = [], []
        for start in range(0, key_count, SKEW):
            offset = query_start - key_start - start + SKEW
            part = slice(start, start + SKEW)
            weights = jnp.exp(
                raw[part] + skew[:, offset : offset + QUERY_BLOCK] - log_total[0, :, queries]
            )
            grad_scores = weights * (grad_weights[part] - inner[:, queries])
            grad_skew[:, offset : offset + QUERY_BLOCK] += grad_scores
            weights_low.append(weights.astype(BF16))
            grad_low.append(grad_scores.astype(BF16))
        weights_low = jnp.concatenate(weights_low, axis=0)
        grad_low = jnp.concatenate(grad_low, axis=0)
        grad_projected[0, 0, :, queries] = (matmul(key_t[0, :, keys], grad_low) * scale).astype(BF16)
        grad_key[keys, :] += matmul(grad_low, query_n[0, queries, :])
        grad_value[keys, :] += matmul(weights_low, grad_n[0, queries, :])
    grad_projected[1, 0] = grad_key[...].T.astype(BF16)
    grad_projected[2, 0] = grad_value[...].T.astype(BF16)
    count = SKEW
    span = skew.shape[1]
    while count > 8:
        count //= 2
        grad_skew[:count, :] += pltpu.roll(grad_skew[count : 2 * count, :], span - count, 1)
    summed = grad_skew[0:1, :]
    for row in range(1, 8):
        summed = summed + pltpu.roll(grad_skew[row : row + 1, :], span - row, 1)
    grad_bias[0] = summed

def expert_lane(shape, lanes):
    return lax.broadcasted_iota(jnp.int32, shape, 1) - lanes.router


def int_columns(columns):
    values = columns[:, 0:4].astype(jnp.int32)
    return values[:, 0:2], values[:, 2:4]


def route_kernel(
    tokens, attended_t, attention_out, plane, columns, position_rows, *refs,
    experts, lanes, capacity, crossing,
):
    over, refs = refs[:crossing], refs[crossing:]
    hidden, routed, probabilities, gates, outgoing, rows_in, gates_in = refs[:7]
    landed, refs = refs[7 : 7 + crossing], refs[7 + crossing :]
    slot_gates, send, receive, own = refs
    grid = Grid().here()
    links = Links(send, receive)
    exp_size = grid.exp_size
    sibling = (grid.exp, grid.sibling(grid.fsdp))
    greet([((grid.exp + hop) % exp_size, grid.fsdp) for hop in range(1, exp_size)] + [sibling])
    swaps = [links.copy(source, target, sibling, target) for source, target in zip(over, landed)]
    for going, _ in swaps:
        going.start()
    rows, model_width = tokens.shape
    routes, slots = int_columns(columns)
    attended_low = turned(attended_t[:model_width]).astype(BF16)
    hidden_state = tokens[...].astype(F32) + matmul(attended_low, attention_out[...])
    hidden[...] = hidden_state
    scale = lax.rsqrt(jnp.mean(hidden_state * hidden_state, axis=1, keepdims=True) + EPSILON)
    extra = plane[:, lanes.base :]
    gain = extra.astype(F32).T[lanes.gain : lanes.gain + 1]
    low = (hidden_state * scale * gain).astype(BF16)
    routed[...] = low
    member_slots = experts // exp_size * capacity
    work = Exchange(
        grid, links, own,
        [
            (lambda to: outgoing.at[to, pl.ds(0, capacity), :], rows_in),
            (partial(plane_of, slot_gates, None), gates_in),
        ],
    )
    for number, to in enumerate([to for to, _ in work.steps] + [grid.exp]):
        slot = lax.broadcasted_iota(jnp.int32, (member_slots, rows), 0) + to * member_slots
        slot = slot.astype(F32)
        picked = (slot == position_rows[0:1, :]) | (slot == position_rows[1:2, :])
        outgoing[to] = matmul(jnp.where(picked, 1.0, 0.0).astype(BF16), low).astype(BF16)
        (work.copies[number][0] if number < len(work.steps) else work.own[0]).start()
    logits = matmul(low, extra)
    lane = expert_lane(logits.shape, lanes)
    logits = jnp.where((lane >= 0) & (lane < experts), logits, MASKED)
    powers = jnp.exp(logits - jnp.max(logits, axis=1, keepdims=True))
    powers = powers / jnp.sum(powers, axis=1, keepdims=True)
    probabilities[...] = powers
    chosen = [
        jnp.sum(jnp.where(lane == routes[:, k : k + 1], powers, 0.0), axis=1, keepdims=True)
        for k in range(2)
    ]
    total = chosen[0] + chosen[1]
    gate_values = [chosen[k] / total for k in range(2)]
    pair = lax.broadcasted_iota(jnp.int32, (rows, 2), 1)
    gates[...] = jnp.where(pair == 0, gate_values[0], gate_values[1])
    gate_lanes = slot_gates.shape[2]
    slot_lanes = lax.broadcasted_iota(jnp.int32, (rows, gate_lanes), 1)
    inside = slot_lanes < member_slots
    places = routes * capacity + slots
    for member in range(exp_size):
        by_slot = jnp.zeros((rows, gate_lanes), F32)
        for k in range(2):
            hit = (slot_lanes + member * member_slots == places[:, k : k + 1]) & inside
            by_slot = by_slot + jnp.where(hit, gate_values[k], 0.0)
        slot_gates[member] = jnp.broadcast_to(
            jnp.sum(by_slot, axis=0, keepdims=True), slot_gates.shape[1:]
        )
    for going, _ in work.copies[exp_size - 1 :]:
        going.start()
    work.own[1].start()
    work.finish()
    for going, coming in swaps:
        coming.wait_recv()
        going.wait_send()


def select_rows(outgoing, position_rows, values):
    rows = values.shape[0]
    sizes = [array.shape[1] for array in outgoing]
    for member in range(outgoing[0].shape[0]):
        slots = lax.broadcasted_iota(jnp.int32, (sum(sizes), rows), 0) + member * sum(sizes)
        slots = slots.astype(F32)
        picked = (slots == position_rows[0:1, :]) | (slots == position_rows[1:2, :])
        found = matmul(jnp.where(picked, 1.0, 0.0).astype(BF16), values).astype(BF16)
        first = 0
        for array, size in zip(outgoing, sizes):
            array[member] = found[first : first + size]
            first += size


def gelu_parts(value):
    magnitude = jnp.abs(value)
    power = jnp.exp2(value * value * -0.7213475204444817)
    base = 1.0 + (0.3275911 * 0.7071067811865476) * magnitude
    step = pl.reciprocal(base, approx=True)
    step = step * (2.0 - base * step)
    series = step * (
        0.127414796
        + step * (-0.142248368 + step * (0.7107068705 + step * (-0.7265760135 + step * 0.5307027145)))
    )
    tail = series * power
    normal = jnp.where(value < 0.0, tail, 1.0 - tail)
    return value * normal, normal + value * (power * 0.3989422804014327)


def expert_kernel(*refs, layout, index, local, half, capacity, parts):
    shards = 2 * half
    refs = Bag(layout, refs)
    grid = Grid().here()
    z_size, y_size = grid.z_size, grid.y_size
    last = index == local - 1
    sibling = (grid.exp, grid.sibling(grid.fsdp))
    links = Links(refs.send[0], refs.receive[0])
    rows_all, cot, up_all, down_all = (
        refs.rows_all[0], refs.cot[0], refs.up_all[0], refs.down_all[0]
    )
    total = refs.total[0]
    if last:
        active, grad_hidden, unscaled = refs.active[0], refs.grad_hidden[0], refs.unscaled[0]
    else:
        grad_total, slot_grad = refs.grad_total[0], refs.slot_grad[0]
    gates, gate_column = refs.gates[0], refs.gate_column[0]
    rows_t, slot_t = refs.rows_t[0], refs.slot_t[0]
    grad_up, grad_down = refs.grad_up[0], refs.grad_down[0]
    grad_rows, grad_gates = refs.grad_rows[0], refs.grad_gates[0]
    up_keep, up_taken, down_keep, down_taken = refs.own
    keep_up = [up_keep] + list(refs.far_keep_up)
    taken_up = [up_taken] + list(refs.far_taken_up)
    keep_down = [down_keep] + list(refs.far_keep_down)
    taken_down = [down_taken] + list(refs.far_taken_down)
    load_sem, fetch_sem, store_sem = refs.load_sem[0], refs.fetch_sem[0], refs.store_sem[0]
    store_there, stored_here = refs.store_there[0], refs.stored_here[0]
    pass_sem = refs.pass_sem[0]
    blocks, _, model_width = rows_all.shape
    part = up_all.shape[2]
    count = blocks * capacity
    depth = model_width // shards
    power = z_size & (z_size - 1) == 0
    together = 2 if power and z_size > 1 else 1
    group_rows = together * y_size * capacity

    source_z, target_z = grid.source_z, grid.target_z

    def owner(place, core):
        return ((grid.x + place % half) % half) * 2 + (core + place // half) % 2

    def rows_of(place, core=None):
        core = grid.core if core is None else core
        return pl.ds(pl.multiple_of(owner(place, core) * depth, 16), depth)

    loads = [pltpu.make_async_copy(refs.rows_in[0], rows_all, load_sem.at[1])]
    late_count = 0
    if last and refs.cot_late:
        late_count = refs.cot_late[0].shape[1]
        loads.append(
            pltpu.make_async_copy(
                refs.cot_late[0], cot.at[:, pl.ds(capacity - late_count, late_count)], load_sem.at[4]
            )
        )
    loads.append(
        pltpu.make_async_copy(
            refs.cot_in[0].at[:, pl.ds(index * capacity, capacity - late_count)],
            cot.at[:, pl.ds(0, capacity - late_count)], load_sem.at[0],
        )
    )
    my_up, my_down = refs.my_up, refs.my_down
    swapped_up, swapped_down = refs.swapped_up, refs.swapped_down
    local_up = list(enumerate(my_up)) + [
        (half + number, array) for number, array in enumerate(swapped_up)
    ]
    local_down = list(enumerate(my_down)) + [
        (half + number, array) for number, array in enumerate(swapped_down)
    ]

    def fetch_up(place):
        return [
            pltpu.make_async_copy(
                array.at[rows_of(place), :], up_all.at[place, rows_of(shard), :],
                fetch_sem.at[place, number],
            )
            for number, (shard, array) in enumerate(local_up)
        ]

    fetched_down = {
        shard: pltpu.make_async_copy(
            array, down_all.at[shard], fetch_sem.at[shards + number, 0]
        )
        for number, (shard, array) in enumerate(local_down)
    }
    cross_down = {
        half + shard: links.copy(
            my_down[shard], down_all.at[half + shard], sibling, down_all.at[half + shard]
        )
        for shard in range(len(swapped_down), half)
    }
    cross_up = [
        links.copy(
            my_up[shard].at[rows_of(place, 1 - grid.core), :],
            up_all.at[place, rows_of(shard), :], sibling,
            up_all.at[place, rows_of(half + shard), :],
        )
        for shard in range(len(swapped_up), half)
        for place in range(shards)
    ]
    cross_next = [
        links.copy(source, target, sibling, target)
        for source, target in zip(refs.next_mine, refs.next_swapped)
    ]
    work = Exchange(
        grid, links, refs.own_sem[0],
        [
            (partial(plane_of, source, place), target)
            for source, place, target in zip(refs.moved_from, parts, refs.moved_to)
        ],
    )
    def member(z, y):
        return z * y_size + y

    def give_back(turn, hop):
        to = member(source_z(turn), (grid.y + hop) % y_size)
        origin = member(target_z(turn), (grid.y + y_size - hop) % y_size)
        pairs = []
        for number, (held, target) in enumerate(
            ((grad_rows, refs.back_rows[0]), (grad_gates, refs.back_gates[0]))
        ):
            sems = dict(
                send_sem=refs.back_send[0].at[number, turn, hop],
                recv_sem=refs.back_receive[0].at[number, turn, hop],
                device_id=(to, grid.fsdp), device_id_type=MESH,
            )
            pairs.append(
                (
                    pltpu.make_async_remote_copy(
                        src_ref=held.at[to], dst_ref=target.at[grid.exp], **sems
                    ),
                    pltpu.make_async_remote_copy(
                        src_ref=target.at[origin], dst_ref=target.at[origin], **sems
                    ),
                )
            )
        return pairs

    steps = [(turn, hop) for turn in range(z_size) for hop in range(y_size)]
    own_back = []
    if last:
        own_back = [
            pltpu.make_async_copy(held.at[grid.exp], target.at[grid.exp], load_sem.at[2 + number])
            for number, (held, target) in enumerate(
                ((grad_rows, refs.back_rows[0]), (grad_gates, refs.back_gates[0]))
            )
        ]

    for copy in loads:
        copy.start()
    order = list(range(shards))
    if not last:
        order = [(pair + 1) % half + side * half for pair in range(half) for side in (1, 0)]
    if last:
        for copy in fetched_down.values():
            copy.start()
    for place in order:
        if not last and place in fetched_down:
            fetched_down[place].start()
        for copy in fetch_up(place):
            copy.start()
    greet(
        [((grid.exp + hop) % grid.exp_size, grid.fsdp) for hop in range(1, grid.exp_size)]
        + chip_peers(grid)
    )
    for going, _ in list(cross_down.values()) + cross_up + cross_next:
        going.start()
    work.start()

    def place_at(position):
        hop = (position // 2 + 1) % half
        return hop + half * (1 - position % 2)

    def slot_rows():
        columns = gates[:, 0, :].T
        for block in range(blocks):
            piece = slice(block * capacity, (block + 1) * capacity)
            gate = columns[index * capacity : (index + 1) * capacity, block : block + 1]
            gate_column[piece, :] = gate
        slot_values = gate_column[...] * cot[...].reshape(count, model_width).astype(F32)
        slot_t[...] = slot_values.T.astype(BF16)
        if not last:
            slot_grad[...] = slot_values.astype(BF16)

    def wait_down(place):
        if place in fetched_down:
            fetched_down[place].wait()
        else:
            cross_down[place][1].wait_recv()

    def wait_crossed():
        for _, coming in cross_up:
            coming.wait_recv()

    def folded(value):
        return sum(value[:, start : start + 128] for start in range(0, value.shape[1], 128))

    def gate_rows(found, block):
        ones = jnp.ones((8, 128), F32)
        grad_gates[block] = lax.dot_general(
            ones, found, (((1,), (1,)), ((), ())), precision=lax.Precision.HIGHEST,
            preferred_element_type=F32,
        )

    def up_target(targets, hop, place):
        if hop == 0:
            return targets[0].at[rows_of(place), :]
        return targets[1].at[hop - 1, rows_of(place), :]

    def keep_stores(place, slot):
        return [
            pltpu.make_async_copy(
                grad_up.at[slot, rows_of(hop), :], up_target(keep_up, hop, place),
                store_sem.at[slot, hop],
            )
            for hop in range(half)
        ]

    def give_stores(place, slot):
        return [
            pltpu.make_async_remote_copy(
                src_ref=grad_up.at[slot, rows_of(half + hop), :],
                dst_ref=up_target(taken_up, hop, place),
                send_sem=store_there.at[slot, hop], recv_sem=stored_here.at[place, hop],
                device_id=sibling, device_id_type=MESH,
            )
            for hop in range(half)
        ]

    def down_store(slot):
        return pltpu.make_async_copy(grad_down.at[slot], keep_down[0], store_sem.at[slot, half])

    def down_give(hop, slot):
        target = taken_down[0] if hop == 0 else taken_down[1].at[hop - 1]
        return pltpu.make_async_remote_copy(
            src_ref=grad_down.at[slot], dst_ref=target,
            send_sem=store_there.at[slot, half], recv_sem=stored_here.at[hop, half],
            device_id=sibling, device_id_type=MESH,
        )

    def start_store(place, slot):
        for copy in keep_stores(place, slot) + give_stores(place, slot):
            copy.start()

        @pl.when(place == 0)
        def _():
            down_store(slot).start()

        for hop in range(half):

            @pl.when(place == half + hop)
            def _(hop=hop):
                down_give(hop, slot).start()

            if hop > 0:

                @pl.when(place == hop)
                def _(hop=hop):
                    keep_down[1][hop - 1] = grad_down[slot]

    def wait_store(place, slot):
        for copy in keep_stores(place, slot):
            copy.wait()
        for copy in give_stores(place, slot):
            copy.wait_send()

        @pl.when(place == 0)
        def _():
            down_store(slot).wait()

        for hop in range(half):

            @pl.when(place == half + hop)
            def _(hop=hop):
                down_give(hop, slot).wait_send()

    def fused(position, carry):
        place, slot = place_at(position), position % 2
        for copy in fetch_up(place):
            copy.wait()
        for which in range(shards):

            @pl.when(place == which)
            def _(which=which):
                wait_down(which)

        up, down = up_all[place], down_all[place]
        rows = rows_all[...].reshape(count, model_width)
        pieces = [slice(start, start + 256) for start in range(0, count, 256)]

        def products_of(piece):
            return matmul(rows[piece], up), contract_last(slot_grad[piece, :], down)

        raw = products_of(pieces[0])
        active_low, grad_low = [], []
        for number, piece in enumerate(pieces):
            hidden, grad_active = raw
            if number + 1 < len(pieces):
                raw = products_of(pieces[number + 1])
            activated, slope = gelu_parts(hidden)
            active_low.append(activated.astype(BF16))
            grad_low.append((grad_active * slope).astype(BF16))
            total[piece, :] += matmul(active_low[number], down)
            grad_total[piece, :] += contract_last(grad_low[number], up)
        active_low = jnp.concatenate(active_low, axis=0)
        grad_low = jnp.concatenate(grad_low, axis=0)

        @pl.when(position >= 2)
        def _():
            wait_store(place_at(position - 2), slot)

        grad_up[slot] = matmul(rows_t[...], grad_low).astype(BF16)
        grad_down[slot] = matmul(slot_t[...], active_low).T.astype(BF16)
        start_store(place, slot)
        return carry

    def group(step, carry):
        number = z_size // together - 1 - step
        turns = [number * together + more for more in range(together)]
        if together == 2:
            place_of_group = flipped(grid.z // 2, number, z_size // 2)
        else:
            place_of_group = source_z(number)
        members = pl.ds(place_of_group * together * y_size, together * y_size)
        span = pl.ds(pl.multiple_of(place_of_group * group_rows, 16), group_rows)
        rows = rows_all[members].reshape(group_rows, model_width)
        gate = gate_column[span, :]
        grad = jnp.zeros((group_rows, model_width), F32)
        products = jnp.zeros((group_rows, 128), F32)
        ahead = matmul(rows, up_all[0])
        for place in range(shards):
            hidden = ahead
            if place + 1 < shards:
                ahead = matmul(rows, up_all[place + 1])
            base = unscaled[place, span, :].astype(F32)
            activated, slope = gelu_parts(hidden)
            products = products + folded(activated * base)
            active_low = activated.astype(BF16)
            active[place, span, :] = active_low
            low = (gate * base * slope).astype(BF16)
            grad_hidden[place, span, :] = low
            grad = grad + contract_last(low, up_all[place])
            total[span, :] += matmul(active_low, down_all[place])
        grad_rows[members] = grad.astype(BF16).reshape(together * y_size, capacity, model_width)
        for hop in range(together * y_size):
            gate_rows(
                products[hop * capacity : (hop + 1) * capacity],
                place_of_group * together * y_size + hop,
            )
        for turn in turns:
            for hop in range(y_size):

                @pl.when(turn + hop > 0)
                def _(turn=turn, hop=hop):
                    for going, _ in give_back(turn, hop):
                        going.start()

        return carry

    def column(position, carry):
        place, slot = place_at(position), position % 2
        @pl.when(position >= 2)
        def _():
            wait_store(place_at(position - 2), slot)

        grad_up[slot] = matmul(rows_t[...], grad_hidden[place]).astype(BF16)
        grad_down[slot] = matmul(slot_t[...], active[place]).T.astype(BF16)
        start_store(place, slot)
        return carry

    for copy in loads[1:]:
        copy.wait()
    total[...] = jnp.zeros_like(total)
    slot_rows()
    if last:
        for place in range(shards):
            wait_down(place)
            unscaled[place] = contract_last(
                cot[...].reshape(count, model_width), down_all[place]
            ).astype(BF16)
        loads[0].wait()
        for place in range(shards):
            for copy in fetch_up(place):
                copy.wait()
        wait_crossed()
        lax.fori_loop(0, z_size // together, group, 0)
        for copy in own_back:
            copy.start()
        rows_t[...] = turned(rows_all[...].reshape(count, model_width)).astype(BF16)
        lax.fori_loop(0, shards, column, 0)
    else:
        loads[0].wait()
        rows_t[...] = turned(rows_all[...].reshape(count, model_width)).astype(BF16)
        grad_total[...] = jnp.zeros_like(grad_total)
        wait_crossed()
        lax.fori_loop(0, shards, fused, 0)
        grad_rows[...] = grad_total[...].astype(BF16).reshape(grad_rows.shape)
        for block in range(blocks):
            rows = total[block * capacity : (block + 1) * capacity, :].astype(BF16).astype(F32)
            gate_rows(folded(rows * cot[block].astype(F32)), block)

    rows_out = refs.rows_out[0]
    cot[...] = total[...].astype(BF16).reshape(blocks, capacity, model_width)
    out_copies = [pltpu.make_async_copy(cot, rows_out.at[:, index], load_sem.at[0])]
    for before in refs.outs_before:
        out_copies.append(
            pltpu.make_async_copy(before, rows_out.at[:, pl.ds(0, index)], load_sem.at[1])
        )
    for copy in out_copies:
        copy.start()
    for position in range(max(shards - 2, 0), shards):
        wait_store(place_at(position), position % 2)
    for place in range(shards):
        for copy in give_stores(place, 0):
            copy.wait_recv()
    for hop in range(half):
        down_give(hop, 0).wait_recv()
    if half > 1:
        for kept, taken in ((keep_up[1], taken_up[1]), (keep_down[1], taken_down[1])):
            kept[...] = (kept[...].astype(F32) + taken[...].astype(F32)).astype(BF16)
        early_rows = part // 2 if last else 0
        passed = [
            (keep_up[1], refs.pass_up[0], 0),
            (keep_down[1].at[:, pl.ds(early_rows, part - early_rows), :], refs.pass_down[0], 1),
        ]
        if last:
            passed.append((keep_down[1].at[:, pl.ds(0, early_rows), :], refs.early_down[0], 2))
        for source, target, number in passed:
            out_copies.append(pltpu.make_async_copy(source, target, pass_sem.at[number]))
            out_copies[-1].start()
    for copy in out_copies:
        copy.wait()
    for going, coming in cross_next:
        coming.wait_recv()
        going.wait_send()
    for going, _ in list(cross_down.values()) + cross_up:
        going.wait_send()
    work.finish()
    if last:
        for turn, hop in steps[1:]:
            for going, coming in give_back(turn, hop):
                coming.wait_recv()
                going.wait_send()
        for copy in own_back:
            copy.wait()


class Bag:
    def __init__(self, layout, refs):
        start = 0
        for name, size in layout.items():
            setattr(self, name, refs[start : start + size])
            start += size


class Wanted:
    def groups(self):
        return list(self.__dict__.values())

    def layout(self):
        return {name: len(group) for name, group in self.__dict__.items()}


def run_expert(index, local, rows_in, gates, cotangent, cotangent_late, ups, downs, swapped, next_mine,
               moved, outs_before, collective_id):
    grid = Grid()
    half = len(ups)
    shards = 2 * half
    last = index == local - 1
    blocks, capacity, model_width = rows_in.shape
    part = downs[0].shape[0]
    count = blocks * capacity
    inputs, outputs, scratch = Wanted(), Wanted(), Wanted()
    inputs.cot_in = [(cotangent, ANYWHERE)]
    inputs.cot_late = [(array, ANYWHERE) for array in cotangent_late]
    inputs.rows_in = [(rows_in, ANYWHERE)]
    inputs.gates = [(gates, IN_VMEM)]
    inputs.my_up = [(array, ANYWHERE) for array in ups]
    inputs.my_down = [(array, ANYWHERE) for array in downs]
    inputs.swapped_up = [(array, ANYWHERE) for array in swapped[0]]
    inputs.swapped_down = [(array, ANYWHERE) for array in swapped[1]]
    inputs.next_mine = [(array, ANYWHERE) for array in next_mine]
    inputs.moved_from = [(array, ANYWHERE) for array, _ in moved]
    inputs.outs_before = [] if outs_before is None else [(outs_before, IN_VMEM)]

    up_shape, down_shape = (model_width, part), (part, model_width)
    outputs.rows_out = [(shape_of((blocks, index + 1, capacity, model_width), BF16), ANYWHERE)]
    own_up, own_down = shape_of(up_shape, BF16), shape_of(down_shape, BF16)
    outputs.own = [(own_up, ANYWHERE), (own_up, ANYWHERE), (own_down, ANYWHERE), (own_down, ANYWHERE)]
    outputs.pass_up = [(shape_of((half - 1,) + up_shape, BF16), ANYWHERE)] if half > 1 else []
    early_rows = part // 2 if last else 0
    late_down = (half - 1, part - early_rows, model_width)
    early_down = (half - 1, early_rows, model_width)
    outputs.pass_down = [(shape_of(late_down, BF16), ANYWHERE)] if half > 1 else []
    outputs.early_down = [(shape_of(early_down, BF16), ANYWHERE)] if half > 1 and last else []
    outputs.next_swapped = [(shape_of(array.shape, BF16), ANYWHERE) for array in next_mine]
    outputs.moved_to = [
        (
            shape_of((grid.exp_size,) + array.shape[(1 if place is None else 2) :], array.dtype),
            ANYWHERE,
        )
        for array, place in moved
    ]
    rows_shape, gate_shape = (blocks, capacity, model_width), (blocks, 8, capacity)
    if last:
        outputs.back_rows = [(shape_of(rows_shape, BF16), ANYWHERE)]
        outputs.back_gates = [(shape_of(gate_shape, F32), ANYWHERE)]
    else:
        outputs.grad_rows = [(shape_of(rows_shape, BF16), IN_VMEM)]
        outputs.grad_gates = [(shape_of(gate_shape, F32), IN_VMEM)]

    sems = lambda *shape: pltpu.SemaphoreType.DMA(shape)
    scratch.rows_all = [pltpu.VMEM(rows_shape, BF16)]
    scratch.cot = [pltpu.VMEM(rows_shape, BF16)]
    scratch.up_all = [pltpu.VMEM((shards,) + up_shape, BF16)]
    scratch.down_all = [pltpu.VMEM((shards,) + down_shape, BF16)]
    scratch.total = [pltpu.VMEM((count, model_width), F32)]
    if last:
        scratch.active = [pltpu.VMEM((shards, count, part), BF16)]
        scratch.grad_hidden = [pltpu.VMEM((shards, count, part), BF16)]
        scratch.unscaled = [pltpu.VMEM((shards, count, part), BF16)]
    else:
        scratch.grad_total = [pltpu.VMEM((count, model_width), F32)]
        scratch.slot_grad = [pltpu.VMEM((count, model_width), BF16)]
    if last:
        scratch.grad_rows = [pltpu.VMEM(rows_shape, BF16)]
        scratch.grad_gates = [pltpu.VMEM(gate_shape, F32)]
        scratch.back_send = [sems(2, grid.z_size, grid.y_size)]
        scratch.back_receive = [sems(2, grid.z_size, grid.y_size)]
    scratch.gate_column = [pltpu.VMEM((count, 1), F32)]
    scratch.rows_t = [pltpu.VMEM((model_width, count), BF16)]
    scratch.slot_t = [pltpu.VMEM((model_width, count), BF16)]
    scratch.grad_up = [pltpu.VMEM((2,) + up_shape, BF16)]
    scratch.grad_down = [pltpu.VMEM((2,) + down_shape, BF16)]
    far_up = [pltpu.VMEM((half - 1,) + up_shape, BF16)] * (1 if half > 1 else 0)
    far_down = [pltpu.VMEM((half - 1,) + down_shape, BF16)] * (1 if half > 1 else 0)
    scratch.far_keep_up, scratch.far_taken_up = far_up, far_up
    scratch.far_keep_down, scratch.far_taken_down = far_down, far_down
    scratch.load_sem = [sems(5)]
    scratch.pass_sem = [sems(3)]
    scratch.fetch_sem = [sems(2 * shards, shards)]
    scratch.store_sem = [sems(2, half + 1)]
    scratch.store_there = [sems(2, half + 1)]
    scratch.stored_here = [sems(shards, half + 1)]
    copies = len(moved) * grid.exp_size + half * (shards + 2) + len(next_mine)
    scratch.send = [sems(copies)]
    scratch.receive = [sems(copies)]
    scratch.own_sem = [sems(max(len(moved), 1))]

    layout = {**inputs.layout(), **outputs.layout(), **scratch.layout()}

    def body(*refs):
        expert_kernel(
            *refs, layout=layout, index=index, local=local, half=half, capacity=capacity,
            parts=[place for _, place in moved],
        )

    results = pl.pallas_call(
        body,
        in_specs=[spec for group in inputs.groups() for _, spec in group],
        out_specs=tuple(spec for group in outputs.groups() for _, spec in group),
        out_shape=tuple(shape for group in outputs.groups() for shape, _ in group),
        scratch_shapes=[item for group in scratch.groups() for item in group],
        compiler_params=params(collective_id=collective_id, has_side_effects=True),
        cost_estimate=hint(45),
        name=f"expert_{index}",
    )(*[array for group in inputs.groups() for array, _ in group])
    return Bag(outputs.layout(), results)


def local_picks(routes, slots, capacity, local, index, slot_count):
    member, which = lax.div(routes, local), lax.rem(routes, local)
    places = jnp.where(which == index, member * capacity + slots, -1)
    lane = lax.broadcasted_iota(jnp.int32, (routes.shape[0], slot_count), 1)
    return [lane == places[:, k : k + 1] for k in range(2)]


def unroute_kernel(
    hidden, cotangent, routed, probabilities, gates, plane, columns, counts, attention_out, context,
    *refs, experts, local, token_total, lanes, heads, width,
):
    grads, gate_grads = refs[:local], refs[local : 2 * local]
    (
        grad_hidden, small, grad_t, grad_n, grad_out, branches, own_out, total, send, receive, own_sem,
    ) = refs[2 * local :]
    grid = Grid().here()
    links = Links(send, receive)
    rows, model_width = hidden.shape
    members, capacity = grads[0].shape[0], grads[0].shape[1]
    head_rows = heads * width
    fetch = pltpu.make_async_copy(
        attention_out.at[pl.ds(pl.multiple_of(grid.fsdp * head_rows, 16), head_rows), :], own_out,
        own_sem.at[0],
    )
    fetch.start()
    greet(chip_peers(grid))
    extra = plane[:, lanes.base :]
    gains = extra.astype(F32).T[lanes.gain : lanes.gain + 1]
    half_rows = rows // 2
    sibling = grid.sibling(grid.fsdp)
    small_t = jnp.zeros((lanes.extra, model_width), F32)
    gain_grad = jnp.zeros((1, model_width), F32)
    along_x, across = [], []
    for half in range(2):
        here = slice(half * half_rows, (half + 1) * half_rows)
        grad_output = cotangent[here, :].astype(F32)
        routes = columns[here, 0:2].astype(jnp.int32)
        slots = columns[here, 2:4].astype(jnp.int32)
        member, which = lax.div(routes, local), lax.rem(routes, local)
        lane = lax.broadcasted_iota(jnp.int32, (half_rows, capacity), 1)
        grad_routed = jnp.zeros((half_rows, model_width), F32)
        found = [jnp.zeros((half_rows, capacity), F32), jnp.zeros((half_rows, capacity), F32)]
        for index in range(local):
            picks = local_picks(routes, slots, capacity, local, index, members * capacity)
            grad_routed = grad_routed + matmul(
                jnp.where(picks[0] | picks[1], 1.0, 0.0).astype(BF16),
                grads[index][...].reshape(members * capacity, model_width),
            )
            for place in range(members):
                spots = jnp.where((which == index) & (member == place), slots, -1)
                for k in range(2):
                    found[k] = found[k] + jnp.where(
                        lane == spots[:, k : k + 1], gate_grads[index][place, 0:1, :], 0.0
                    )
        grad_gates = [jnp.sum(found[k], axis=1, keepdims=True) for k in range(2)]
        powers = probabilities[here, :]
        lane = expert_lane(powers.shape, lanes)
        inside = (lane >= 0) & (lane < experts)
        picked = [lane == routes[:, k : k + 1] for k in range(2)]
        chosen_total = sum(
            jnp.sum(jnp.where(picked[k], powers, 0.0), axis=1, keepdims=True) for k in range(2)
        )
        weighted = grad_gates[0] * gates[here, 0:1] + grad_gates[1] * gates[here, 1:2]
        grad_mass = (AUX_WEIGHT * experts / (2.0 * token_total * token_total)) * counts[0:1, :]
        grad_mass = jnp.where(inside, grad_mass, 0.0)
        for k in range(2):
            grad_mass = grad_mass + jnp.where(
                picked[k], (grad_gates[k] - weighted) / chosen_total, 0.0
            )
        grad_logits = powers * (grad_mass - jnp.sum(powers * grad_mass, axis=1, keepdims=True))
        grad_routed = grad_routed + contract_last(grad_logits.astype(BF16), extra)
        hidden_state = hidden[here, :]
        scale = lax.rsqrt(jnp.mean(hidden_state * hidden_state, axis=1, keepdims=True) + EPSILON)
        normed = hidden_state * scale
        product = grad_routed * normed
        grad = scale * (
            grad_routed * gains - normed * jnp.mean(product * gains, axis=1, keepdims=True)
        ) + grad_output
        grad_hidden[here, :] = grad
        branches[grid.fsdp, here, :] = grad.astype(BF16)
        mine = branches.at[grid.fsdp, here, :]
        for hop in range(1, grid.x_size):
            along_x.append(
                links.copy(
                    mine, mine, (grid.exp, grid.x_from(hop)),
                    branches.at[grid.x_from(-hop), here, :],
                )
            )
            along_x[-1][0].start()
        across.append(
            links.copy(mine, mine, (grid.exp, sibling), branches.at[sibling, here, :])
        )
        across[-1][0].start()
        gain_grad = gain_grad + jnp.sum(product, axis=0, keepdims=True)
        small_t = small_t + matmul(grad_logits.T.astype(BF16), routed[here, :])

    def context_grad(place):
        branch = branches[place]
        grad = contract_last(own_out[...], branch).astype(BF16)
        columns_here = pl.ds(pl.multiple_of(place * rows, 128), rows)
        rows_here = pl.ds(pl.multiple_of(place * rows, 16), rows)
        for head in range(heads):
            piece = grad[head * width : (head + 1) * width]
            grad_t[head, :, columns_here] = piece
            grad_n[head, rows_here, :] = turned(piece).astype(BF16)
        total[...] += matmul(context[place], branch)

    total[...] = jnp.zeros_like(total)
    fetch.wait()
    context_grad(grid.fsdp)
    forwards = []
    for half in range(2):
        here = slice(half * half_rows, (half + 1) * half_rows)
        for hop in range(1, grid.x_size):
            along_x[half * (grid.x_size - 1) + hop - 1][1].wait_recv()
            held = grid.x_from(-hop)
            forwards.append(
                links.copy(
                    branches.at[held, here, :], branches.at[held, here, :], (grid.exp, sibling),
                    branches.at[grid.sibling(held), here, :],
                )
            )
            forwards[-1][0].start()
    row = lax.broadcasted_iota(jnp.int32, small_t.shape, 0)
    small[...] = jnp.where(row == lanes.gain, gain_grad, small_t).T
    for _, coming in across:
        coming.wait_recv()
    context_grad(sibling)
    for hop in range(1, grid.x_size):
        context_grad(grid.x_from(-hop))
    for _, coming in forwards:
        coming.wait_recv()
    for hop in range(1, grid.x_size):
        context_grad(grid.sibling(grid.x_from(-hop)))
    grad_out[...] = total[...].astype(BF16)
    for going, _ in along_x + across + forwards:
        going.wait_send()


def project_back_kernel(
    grad_projected, normed, plane, small, probabilities, grad_bias, grad_first, grad_plane, total,
    bias_t, *, lanes, heads, feature_rows, bucket_rows,
):
    step = pl.program_id(0)

    @pl.when(step == 0)
    def _():
        total[...] = jnp.zeros_like(total)

    grad = grad_projected[...]
    grad_first[0] = matmul(plane[:, : lanes.weights], grad).astype(BF16)
    total[: lanes.weights, :] += matmul(grad, normed[...])

    @pl.when(step == pl.num_programs(0) - 1)
    def _():
        grad_plane[...] = total[...].T.astype(BF16)
        span = grad_bias.shape[2]
        select, _ = bucket_rows_select(plane.shape[0], feature_rows, bucket_rows, span)
        bias_t[...] = jnp.zeros_like(bias_t)
        first = lanes.table + lax.axis_index("fsdp") * heads
        for head in range(heads):
            bias_t[pl.ds(first + head, 1), :] = grad_bias[head]
        high = bias_t[...].astype(BF16)
        rest = (bias_t[...] - high.astype(F32)).astype(BF16)
        table = contract_last(select, high) + contract_last(select, rest)
        mass = jnp.sum(probabilities[...], axis=0, keepdims=True)
        mass = pltpu.roll(jnp.broadcast_to(mass, (8, lanes.extra)), lanes.shift, 1)[0:1]
        lane = lax.broadcasted_iota(jnp.int32, table.shape, 1)
        row = lax.broadcasted_iota(jnp.int32, table.shape, 0)
        is_small = (lane >= lanes.router) & (lane < lanes.table)
        is_mass = (lane >= lanes.count) & (lax.rem(row, feature_rows) == 0)
        extra = table + jnp.where(is_small, small[...], 0.0) + jnp.where(is_mass, mass, 0.0)
        grad_plane[:, lanes.base :] = (total[lanes.base :, :].T + extra).astype(BF16)


def last_kernel(
    first, planes, out_grad, hidden, gates, columns, rows_back, first_parts, output, plane_parts,
    out_parts, first_in, first_sum, planes_in, plane_sum, along_in, reduced, send, receive, own,
    *, spread_out, local,
):
    grid = Grid().here()
    links = Links(send, receive)
    z_size, y_size, x_size, fsdp_size = grid.z_size, grid.y_size, grid.x_size, grid.fsdp_size
    exp_size = grid.exp_size
    sibling = grid.sibling(grid.fsdp)
    near = [
        (grid.exp, (grid.fsdp + turn) % fsdp_size) for turn in range(1, fsdp_size)
    ] + [grid.at(z=(grid.z + hop) % z_size) for hop in range(1, z_size)]
    beside = [grid.at(y=(grid.y + hop) % y_size) for hop in range(1, y_size)]

    per_sender = grid.device_count if spread_out else exp_size
    base = 0 if spread_out else grid.fsdp * exp_size
    out_sends = []
    for number in range(per_sender):
        to = base + number
        out_sends.append((to, number))
    if spread_out:
        out_origins = [(origin, origin) for origin in range(grid.device_count)]
    else:
        out_origins = [
            (member * fsdp_size + grid.linear // exp_size, member) for member in range(exp_size)
        ]
    own_slot = grid.linear if spread_out else grid.exp
    out_base = links.used
    links.used += per_sender

    def place_of(linear):
        return (linear // fsdp_size, linear % fsdp_size)

    def out_copy(to, number, slot):
        return pltpu.make_async_remote_copy(
            src_ref=out_grad.at[number], dst_ref=out_parts.at[slot],
            send_sem=send.at[out_base + number], recv_sem=receive.at[out_base + slot],
            device_id=place_of(to), device_id_type=MESH,
        )

    barrier = pltpu.get_barrier_semaphore()
    for device in near + beside:
        pl.semaphore_signal(barrier, inc=1, device_id=device, device_id_type=MESH)
    for origin, _ in out_origins:

        @pl.when(origin != grid.linear)
        def _(origin=origin):
            pl.semaphore_signal(
                barrier, inc=1, device_id=place_of(origin), device_id_type=MESH
            )

    to_self = (
        1 if spread_out else jnp.where(grid.linear // exp_size == grid.fsdp, 1, 0)
    )
    pl.semaphore_wait(barrier, len(near) + len(beside) + per_sender - to_self)

    first_copies = []
    for hop in range(x_size):
        mine = grid.x_from(hop)
        first_copies.append(
            links.copy(
                first.at[grid.sibling(mine)], first_in.at[hop], (grid.exp, sibling), first_in.at[hop]
            )
        )
        first_copies[-1][0].start()
    z_hops = list(range(1, z_size)) + [0]
    beside_copies = []
    for z_hop in z_hops:
        beside_copies.append([])
        for hop in range(1, y_size):
            to = (grid.y + hop) % y_size
            landing = planes_in.at[hop - 1, z_hop]
            beside_copies[-1].append(
                links.copy(
                    planes.at[(grid.z + z_hop) % z_size, to], landing, grid.at(y=to), landing
                )
            )
            beside_copies[-1][-1][0].start()
    along_x = []
    for hop in range(x_size):
        first_copies[hop][1].wait_recv()
        summed = first[grid.x_from(hop)].astype(F32) + first_in[hop].astype(F32)
        if hop == 0:
            first_parts[0] = summed.astype(BF16)
        else:
            first_sum[hop - 1] = summed.astype(BF16)
            along_x.append(
                links.copy(
                    first_sum.at[hop - 1], first_parts.at[hop], (grid.exp, grid.x_from(hop)),
                    first_parts.at[hop],
                )
            )
            along_x[-1][0].start()
    along_z = []
    for z_hop, copies in zip(z_hops, beside_copies):
        to_z = (grid.z + z_hop) % z_size
        summed = planes[to_z, grid.y].astype(F32)
        for number, (_, coming) in enumerate(copies):
            coming.wait_recv()
            summed = summed + planes_in[number, z_hop].astype(F32)
        plane_sum[z_hop] = summed.astype(BF16)
        if z_hop > 0:
            along_z.append(
                links.copy(
                    plane_sum.at[z_hop], along_in.at[z_hop - 1], grid.at(z=to_z),
                    along_in.at[z_hop - 1],
                )
            )
            along_z[-1][0].start()
    for to, number in out_sends:

        @pl.when(to != grid.linear)
        def _(to=to, number=number):
            out_copy(to, number, own_slot).start()

        @pl.when(to == grid.linear)
        def _(number=number):
            pltpu.make_async_copy(out_grad.at[number], out_parts.at[own_slot], own.at[0]).start()

    mix_rows(hidden, gates, columns, rows_back, output, local)
    summed = plane_sum[0].astype(F32)
    for number, (_, coming) in enumerate(along_z):
        coming.wait_recv()
        summed = summed + along_in[number].astype(F32)
    reduced[...] = summed.astype(BF16)
    placed = []
    for turn in range(1, fsdp_size):
        to = (grid.fsdp + turn) % fsdp_size
        origin = (grid.fsdp + fsdp_size - turn) % fsdp_size
        placed.append(
            links.copy(
                reduced.at[to], plane_parts.at[grid.fsdp], (grid.exp, to), plane_parts.at[origin]
            )
        )
        placed[-1][0].start()
    kept = pltpu.make_async_copy(reduced.at[grid.fsdp], plane_parts.at[grid.fsdp], own.at[1])
    kept.start()
    for going, coming in along_x + placed:
        coming.wait_recv()
    for going, _ in first_copies + along_x + along_z + placed:
        going.wait_send()
    for copies in beside_copies:
        for going, _ in copies:
            going.wait_send()
    kept.wait()
    for origin, slot in out_origins:

        @pl.when(origin != grid.linear)
        def _(origin=origin, slot=slot):
            out_copy(origin, 0, slot).wait_recv()

    for to, number in out_sends:

        @pl.when(to != grid.linear)
        def _(to=to, number=number):
            out_copy(to, number, own_slot).wait_send()

        @pl.when(to == grid.linear)
        def _(number=number):
            pltpu.make_async_copy(out_grad.at[number], out_parts.at[own_slot], own.at[0]).wait()


def mix_rows(hidden, gates, columns, rows_in, output, local):
    members, _, capacity, model_width = rows_in.shape
    routes, slots = int_columns(columns)
    total = hidden[...]
    picked = [jnp.zeros(hidden.shape, F32), jnp.zeros(hidden.shape, F32)]
    for index in range(local):
        picks = local_picks(routes, slots, capacity, local, index, members * capacity)
        values = rows_in[:, index].reshape(members * capacity, model_width)
        for k in range(2):
            picked[k] = picked[k] + matmul(jnp.where(picks[k], 1.0, 0.0).astype(BF16), values)
    for k in range(2):
        total = total + gates[:, k : k + 1] * picked[k]
    output[...] = total.astype(BF16)


def finish_kernel(
    first_parts, plane_parts, out_parts, tokens, grad_hidden, attention_in, attention_gain, counts,
    grad_tokens, grad_gain, grad_in, grad_out, grad_mixture, grad_router, grad_table, balance,
    *, lanes, heads, width, head_count, experts, token_total,
):
    total = jnp.sum(first_parts[...].astype(F32), axis=0).T
    inputs = tokens[...].astype(F32)
    scale = lax.rsqrt(jnp.mean(inputs * inputs, axis=1, keepdims=True) + EPSILON)
    normed = inputs * scale
    grad_tokens[...] = grad_hidden[...] + scale * (
        total - normed * jnp.mean(total * normed, axis=1, keepdims=True)
    )
    fsdp_size = plane_parts.shape[0]
    model_width = head_count * width
    sums = [plane_parts[place].astype(F32) for place in range(fsdp_size)]
    columns = []
    for kind in range(3):
        pieces = [
            sums[place][:, kind * heads * width : (kind + 1) * heads * width]
            for place in range(fsdp_size)
        ]
        columns.append(jnp.concatenate(pieces, axis=1)[:, :model_width])
    gathered = jnp.concatenate(columns, axis=1)
    feature_rows = gathered.shape[0]
    gain = jnp.sum(gathered * attention_in[...].astype(F32), axis=1, keepdims=True)
    gain = padded_rows(jnp.broadcast_to(gain, (feature_rows, 128)), 128).T
    grad_gain[...] = gain[0:1, :feature_rows]
    grad_in[...] = gathered * as_column(attention_gain[...], feature_rows)
    grad_out[...] = jnp.sum(out_parts[...].astype(F32), axis=0)
    extra = sum(part[:, lanes.base :] for part in sums)
    extra_t = padded_rows(extra, 128).T
    grad_mixture[...] = extra_t[lanes.gain : lanes.gain + 1, :feature_rows]
    grad_router[...] = extra_t[lanes.router : lanes.router + experts, :feature_rows]
    grad_table[...] = extra[: grad_table.shape[0], lanes.table : lanes.table + head_count]
    mass = jnp.broadcast_to(extra[0:1], (8, lanes.extra))
    mass = pltpu.roll(mass, lanes.extra - lanes.shift, 1)
    lane = expert_lane(mass.shape, lanes)
    terms = jnp.where((lane >= 0) & (lane < experts), mass * counts[...], 0.0)[0:1]
    balance[...] = jnp.sum(terms, axis=1, keepdims=True) * (
        experts / (2.0 * token_total * token_total)
    )


def sum_kernel(*refs, layout, local):
    outputs = refs[len(layout) :]
    early_blocks = pl.num_programs(0) // 2
    totals = {}
    number = 0
    while number < len(layout):
        index, which, halves = layout[number]
        shape = outputs[which].shape[1:]
        value = refs[number][...].reshape(shape).astype(F32)
        if halves:
            rest = refs[number + 1][...].reshape(shape).astype(F32)
            value = jnp.where(pl.program_id(0) < early_blocks, value, rest)
            number += 1
        totals[index, which] = totals[index, which] + value if (index, which) in totals else value
        number += 1
    for (index, which), total in totals.items():
        outputs[which][index] = total


def sum_grads(groups, up_shape, down_shape, blocks):
    local = len(groups)
    depth, part = up_shape[1], down_shape[1]
    sizes = ((depth, part), (part // blocks, down_shape[2]))
    arrays, specs, layout = [], [], []
    early = blocks // 2
    for index, group in enumerate(groups):
        for which, (size, (keep, taken, passed)) in enumerate(zip(sizes, group)):
            for array in (keep, taken, *passed):
                if isinstance(array, tuple):
                    arrays.extend(array)
                    specs.append(pl.BlockSpec(size, lambda c: (jnp.minimum(c, early - 1), 0)))
                    specs.append(pl.BlockSpec(size, lambda c: (jnp.maximum(c - early, 0), 0)))
                    layout.extend([(index, which, True)] * 2)
                else:
                    arrays.append(array)
                    specs.append(pl.BlockSpec(size, lambda c: (c, 0)))
                    layout.append((index, which, False))
    return pl.pallas_call(
        partial(sum_kernel, layout=layout, local=local),
        grid=(blocks,),
        in_specs=specs,
        out_specs=[
            pl.BlockSpec((local, depth, part), lambda c: (0, 0, c)),
            pl.BlockSpec((local, part // blocks, down_shape[2]), lambda c: (0, c, 0)),
        ],
        out_shape=(shape_of(up_shape, F32), shape_of(down_shape, F32)),
        compiler_params=params(),
        cost_estimate=hint(8),
        name="sum_grads",
    )(*arrays)


def over_x(array, hop):
    fsdp_size = lax.axis_size("fsdp")
    return lax.ppermute(array, "fsdp", [(i, (i + 2 * hop) % fsdp_size) for i in range(fsdp_size)])


def over_core(array):
    return lax.ppermute(array, "fsdp", [(i, i ^ 1) for i in range(lax.axis_size("fsdp"))])


def on_device(
    tokens,
    cotangent,
    segments,
    routes,
    slots,
    attention_gain,
    mixture_gain,
    attention_in,
    attention_out,
    router_weight,
    position_table,
    expert_up,
    expert_down,
):
    grid = Grid()
    exp_size, fsdp_size, chips = grid.exp_size, grid.fsdp_size, grid.x_size
    device_count = grid.device_count
    fsdp_index = lax.axis_index("fsdp")
    rows, model_width = tokens.shape
    length = rows * fsdp_size
    head_count = position_table.shape[1]
    width = model_width // head_count
    heads = -(-head_count // fsdp_size)
    padded_heads = heads * fsdp_size
    feature_rows, bucket_rows = attention_in.shape[0], position_table.shape[0]
    experts = router_weight.shape[1]
    local = expert_up.shape[0]
    capacity = 4 * rows // experts
    token_total = rows * device_count
    span = WINDOW + 2 * SKEW + QUERY_BLOCK
    lanes = Lanes(heads, width, padded_heads, experts)
    part = expert_down.shape[1]
    gain_row = attention_gain.reshape(1, feature_rows)
    late_rows = 2 * capacity // 3 if local > 1 and capacity % 48 == 0 else 0
    late = 1 if late_rows else 0

    shard_shapes = [shape_of((model_width, part), BF16), shape_of((part, model_width), BF16)]
    copies = (
        4 * fsdp_size + grid.z_size + grid.z_size * grid.y_size
        + grid.z_size + grid.y_size + grid.x_size + 1
    )
    started = pl.pallas_call(
        partial(
            start_kernel, lanes=lanes, heads=heads, width=width, head_count=head_count,
            experts=experts, capacity=capacity, local=local, late=late,
        ),
        out_shape=tuple(
            [
                shape_of((fsdp_size, rows, model_width), BF16),
                shape_of((grid.z_size, grid.y_size, fsdp_size, feature_rows, lanes.width), BF16),
                shape_of((exp_size, local * capacity - late_rows, model_width), BF16),
                shape_of((8, rows), F32),
                shape_of((rows, 128), F32),
                shape_of((grid.z_size, grid.y_size, chips, 2, feature_rows, model_width), BF16),
            ]
            + [shape_of((exp_size, late_rows, model_width), BF16)] * late
            + shard_shapes * local
        ),
        in_specs=[IN_VMEM] * 10 + [ANYWHERE] * 2,
        out_specs=tuple(
            [ANYWHERE, ANYWHERE, IN_VMEM, IN_VMEM, IN_VMEM, ANYWHERE]
            + [IN_VMEM] * late
            + [ANYWHERE] * (2 * local)
        ),
        scratch_shapes=[
            pltpu.VMEM((fsdp_size, feature_rows, lanes.width), BF16),
            pltpu.VMEM(expert_up.shape, BF16),
            pltpu.VMEM(expert_down.shape, BF16),
            dma_sems(copies),
            dma_sems(copies),
            dma_sems(3),
            dma_sems(2 * local),
            dma_sems(local * (fsdp_size + 1)),
        ],
        compiler_params=params(collective_id=0, has_side_effects=True),
        cost_estimate=hint(20),
        name="start",
    )(
        tokens, cotangent, routes.T, slots.T, gain_row, mixture_gain.reshape(1, feature_rows),
        attention_in, router_weight.T, position_table, attention_out, expert_up, expert_down,
    )
    all_tokens, all_planes, cotangent_early, position_rows, columns, full_out = started[:6]
    cotangent_late, started = started[6 : 6 + late], started[6 + late :]
    own_shards = [started[2 * index : 2 * index + 2] for index in range(local)]
    plane = all_planes.reshape(model_width, lanes.width)
    full_out = full_out.reshape(model_width, model_width)

    def along_x(array):
        return [over_x(array, -hop) for hop in range(1, chips)]

    near_up, near_down = [None] * local, [None] * local
    near_up[0] = along_x(own_shards[0][0])
    cotangent_in = lax.all_to_all(
        cotangent_early, "exp", split_axis=0, concat_axis=0, tiled=True
    )

    head_t = lambda size: pl.BlockSpec((heads, size, rows), lambda s, *_: (0, 0, s))
    head_n = lambda size: pl.BlockSpec((heads, rows, size), lambda s, *_: (0, s, 0))
    normed, query_t, key_n, query_n, value_n, key_t, value_t, bias, counts = pl.pallas_call(
        partial(
            project_kernel, heads=heads, width=width, lanes=lanes, feature_rows=feature_rows,
            bucket_rows=bucket_rows,
        ),
        grid=(fsdp_size,),
        in_specs=[
            pl.BlockSpec((1, rows, model_width), lambda s: (s, 0, 0)),
            whole((model_width, lanes.width)),
            pl.BlockSpec((1, rows), lambda s: (0, s)),
        ],
        out_specs=[
            pl.BlockSpec((rows, model_width), lambda s: (s, 0)),
            head_t(SKEW), head_n(SKEW), head_n(width), head_n(width), head_t(width), head_t(width),
            whole((heads, 1, span)),
            whole((8, lanes.extra)),
        ],
        out_shape=(
            shape_of((length, model_width), BF16),
            shape_of((heads, SKEW, length), BF16),
            shape_of((heads, length, SKEW), BF16),
            shape_of((heads, length, width), BF16),
            shape_of((heads, length, width), BF16),
            shape_of((heads, width, length), BF16),
            shape_of((heads, width, length), BF16),
            shape_of((heads, 1, span), F32),
            shape_of((8, lanes.extra), F32),
        ),
        scratch_shapes=[
            pltpu.VMEM((lanes.weights, model_width), BF16),
            pltpu.VMEM((lanes.extra, span), F32),
        ],
        compiler_params=params(),
        cost_estimate=hint(8),
        name="project",
    )(all_tokens, plane, segments.reshape(1, length))

    by_head = lambda *size: pl.BlockSpec((1,) + size, lambda h: (h, 0, 0))
    context, context_high, log_total, attended_t = pl.pallas_call(
        partial(attend_kernel, rows=rows),
        grid=(heads,),
        in_specs=[
            by_head(SKEW, length), by_head(length, SKEW), by_head(width, length), by_head(1, span),
        ],
        out_specs=[
            pl.BlockSpec((fsdp_size, width, rows), lambda h: (0, h, 0)),
            by_head(width, length),
            by_head(1, length),
            ANYWHERE,
        ],
        out_shape=(
            shape_of((fsdp_size, heads * width, rows), BF16),
            shape_of((heads, width, length), F32),
            shape_of((heads, 1, length), F32),
            shape_of((fsdp_size, heads * width, rows), BF16),
        ),
        scratch_shapes=[
            pltpu.VMEM((SKEW, span), F32),
            pltpu.VMEM((WINDOW + QUERY_BLOCK, QUERY_BLOCK), F32),
            pltpu.VMEM((heads, fsdp_size, width, rows), BF16),
            pltpu.SemaphoreType.DMA((heads, fsdp_size)),
            pltpu.SemaphoreType.DMA((heads, fsdp_size)),
            dma_sems(heads),
        ],
        compiler_params=params(collective_id=1, has_side_effects=True),
        cost_estimate=hint(13),
        name="attend",
    )(query_t, key_n, value_t, bias)

    own_down, near_up[0], attended_t = lax.optimization_barrier(
        (own_shards[0][1], near_up[0], attended_t)
    )
    near_down[0] = along_x(own_down)
    attended_t = attended_t.reshape(padded_heads * width, rows)

    later = [own_shards[index] for index in range(1, local)]
    attended_t, later = lax.optimization_barrier((attended_t, later))
    for index in range(1, local):
        near_up[index], near_down[index] = [along_x(array) for array in later[index - 1]]
    gate_lanes = -(-local * capacity // 128) * 128
    ready = [own_shards[0][0]] + near_up[0] + [own_shards[0][1]]
    copies = 2 * exp_size + len(ready)
    hidden, routed, probabilities, gates, outgoing, rows_in, gates_in, *crossed = pl.pallas_call(
        partial(
            route_kernel, experts=experts, lanes=lanes, capacity=capacity, crossing=len(ready)
        ),
        in_specs=[IN_VMEM] * 6 + [ANYWHERE] * len(ready),
        out_specs=tuple([IN_VMEM] * 5 + [ANYWHERE] * (2 + len(ready))),
        out_shape=tuple(
            [
                shape_of((rows, model_width), F32),
                shape_of((rows, model_width), BF16),
                shape_of((rows, lanes.extra), F32),
                shape_of((rows, 2), F32),
                shape_of((exp_size, local * capacity, model_width), BF16),
                shape_of((exp_size, capacity, model_width), BF16),
                shape_of((exp_size, 8, gate_lanes), F32),
            ]
            + [shape_of(array.shape, BF16) for array in ready]
        ),
        scratch_shapes=[
            pltpu.VMEM((exp_size, 8, gate_lanes), F32),
            dma_sems(copies),
            dma_sems(copies),
            dma_sems(2),
        ],
        compiler_params=params(collective_id=2, has_side_effects=True),
        cost_estimate=hint(35),
        name="route",
    )(tokens, attended_t, full_out, plane, columns, position_rows, *ready)
    outgoing = outgoing.reshape(exp_size, local, capacity, model_width)

    def down_parts(early, rest):
        return list(zip(early, rest))

    def pass_along(arrays):
        return [over_x(arrays[0][hop - 1], hop) for hop in range(1, chips)]

    swapped = (crossed[:-1], crossed[-1:])
    returned, groups, moved, outs = [], [], [], None
    late_rows_in = ()
    for index in range(local):
        final = index == local - 1
        carried = list(moved)
        if not final:
            carried.append((outgoing, index + 1))
        if index == 0 and late:
            carried.append((cotangent_late[0], None))
        result = run_expert(
            index, local, rows_in, gates_in, cotangent_in, late_rows_in if final else (),
            [own_shards[index][0]] + near_up[index], [own_shards[index][1]] + near_down[index],
            swapped, () if final else own_shards[index + 1], carried, outs, 3 + index,
        )
        (outs,) = result.rows_out
        arrived = list(result.moved_to)
        if index == 0 and late:
            late_rows_in = (arrived.pop(),)
        if not final:
            rows_in = arrived.pop()
            swapped = (result.next_swapped[:1], result.next_swapped[1:])
            moved = [(result.grad_rows[0], None), (result.grad_gates[0], None)]
        if arrived:
            returned.append(arrived)
        up_keep, up_taken, down_keep, down_taken = result.own
        if not final:
            passed = (result.pass_up, result.pass_down)
            passed, rows_in = lax.optimization_barrier((passed, rows_in))
            groups.append(
                [
                    (up_keep, up_taken, pass_along(passed[0])),
                    (down_keep, down_taken, pass_along(passed[1])),
                ]
            )
    returned.append([result.back_rows[0], result.back_gates[0]])
    early = pass_along(result.early_down)
    groups, early, returned = lax.optimization_barrier((groups, early, returned))

    out_rows = lax.all_to_all(outs, "exp", split_axis=0, concat_axis=0, tiled=True)

    padded_out = full_out
    if padded_heads > head_count:
        padded_out = jnp.pad(full_out, ((0, padded_heads * width - model_width), (0, 0)))
    copies = 2 * 2 * fsdp_size
    grad_hidden, small, grad_t, grad_n, out_grad = pl.pallas_call(
        partial(
            unroute_kernel, experts=experts, local=local, token_total=token_total, lanes=lanes,
            heads=heads, width=width,
        ),
        out_shape=(
            shape_of((rows, model_width), F32),
            shape_of((model_width, lanes.extra), F32),
            shape_of((heads, width, length), BF16),
            shape_of((heads, length, width), BF16),
            shape_of((heads * width, model_width), BF16),
        ),
        in_specs=[IN_VMEM] * 8 + [ANYWHERE] + [IN_VMEM] * (1 + 2 * local),
        out_specs=tuple([IN_VMEM] * 5),
        scratch_shapes=[
            pltpu.VMEM((fsdp_size, rows, model_width), BF16),
            pltpu.VMEM((heads * width, model_width), BF16),
            pltpu.VMEM((heads * width, model_width), F32),
            dma_sems(copies),
            dma_sems(copies),
            dma_sems(1),
        ],
        compiler_params=params(collective_id=4 + local, has_side_effects=True),
        cost_estimate=hint(1),
        name="unroute",
    )(
        hidden, cotangent, routed, probabilities, gates, plane, columns, counts, padded_out, context,
        *[part[0] for part in returned], *[part[1] for part in returned],
    )
    pass_up, pass_down, grad_t = lax.optimization_barrier(
        (result.pass_up, result.pass_down, grad_t)
    )
    groups.append(
        [
            (up_keep, up_taken, pass_along(pass_up)),
            (down_keep, down_taken, down_parts(early, pass_along(pass_down))),
        ]
    )

    grad_projected, grad_bias = pl.pallas_call(
        partial(attend_back_kernel, scale=width ** (-0.5)),
        grid=(heads,),
        in_specs=[
            by_head(SKEW, length), by_head(length, SKEW), by_head(length, width),
            by_head(length, width), by_head(width, length), by_head(width, length),
            by_head(length, width), by_head(width, length), by_head(1, length), by_head(1, span),
        ],
        out_specs=[
            pl.BlockSpec((3, 1, width, length), lambda h: (0, h, 0, 0)),
            by_head(1, span),
        ],
        out_shape=(
            shape_of((3, heads, width, length), BF16),
            shape_of((heads, 1, span), F32),
        ),
        scratch_shapes=[
            pltpu.VMEM((SKEW, span), F32),
            pltpu.VMEM((SKEW, span), F32),
            pltpu.VMEM((length, width), F32),
            pltpu.VMEM((length, width), F32),
        ],
        compiler_params=params(),
        cost_estimate=hint(1),
        name="attend_back",
    )(query_t, key_n, query_n, value_n, key_t, grad_t, grad_n, context_high, log_total, bias)
    grad_projected = grad_projected.reshape(lanes.weights, length)

    grad_first, grad_plane = pl.pallas_call(
        partial(
            project_back_kernel, lanes=lanes, heads=heads, feature_rows=feature_rows,
            bucket_rows=bucket_rows,
        ),
        grid=(fsdp_size,),
        in_specs=[
            pl.BlockSpec((lanes.weights, rows), lambda s: (0, s)),
            pl.BlockSpec((rows, model_width), lambda s: (s, 0)),
            whole((model_width, lanes.width)),
            whole((model_width, lanes.extra)),
            whole((rows, lanes.extra)),
            whole((heads, 1, span)),
        ],
        out_specs=[
            pl.BlockSpec((1, model_width, rows), lambda s: (s, 0, 0)),
            whole((model_width, lanes.width)),
        ],
        out_shape=(
            shape_of((fsdp_size, model_width, rows), BF16),
            shape_of((model_width, lanes.width), BF16),
        ),
        scratch_shapes=[
            pltpu.VMEM((lanes.width, model_width), F32),
            pltpu.VMEM((lanes.extra, span), F32),
        ],
        compiler_params=params(),
        cost_estimate=hint(1),
        name="project_back",
    )(grad_projected, normed, plane, small, probabilities, grad_bias)

    out_rows, grad_first = lax.optimization_barrier((out_rows, grad_first))
    spread_out = heads * width * fsdp_size != model_width
    if spread_out:
        out_grad = lax.dynamic_update_slice(
            jnp.zeros((padded_heads * width, model_width), BF16), out_grad,
            (fsdp_index * heads * width, jnp.int32(0)),
        )[:model_width]
    out_grad = out_grad.reshape(-1, feature_rows, model_width)
    out_count = device_count if spread_out else exp_size
    plane_shape = (grid.z_size, grid.y_size, fsdp_size, feature_rows, lanes.width)
    parts_shape = (fsdp_size, feature_rows, lanes.width)
    copies = 4 * fsdp_size + grid.z_size * grid.y_size + grid.z_size + out_count
    first_parts, layer_output, plane_parts, out_parts = pl.pallas_call(
        partial(last_kernel, spread_out=spread_out, local=local),
        out_shape=(
            shape_of((chips, model_width, rows), BF16),
            shape_of((rows, model_width), BF16),
            shape_of(parts_shape, BF16),
            shape_of((out_count, feature_rows, model_width), BF16),
        ),
        in_specs=[IN_VMEM] * 7,
        out_specs=(IN_VMEM, IN_VMEM, ANYWHERE, ANYWHERE),
        scratch_shapes=[
            pltpu.VMEM((chips, model_width, rows), BF16),
            pltpu.VMEM((max(chips - 1, 1), model_width, rows), BF16),
            pltpu.VMEM((max(grid.y_size - 1, 1), grid.z_size) + parts_shape, BF16),
            pltpu.VMEM((grid.z_size,) + parts_shape, BF16),
            pltpu.VMEM((max(grid.z_size - 1, 1),) + parts_shape, BF16),
            pltpu.VMEM(parts_shape, BF16),
            dma_sems(copies),
            dma_sems(copies),
            dma_sems(2),
        ],
        compiler_params=params(collective_id=5 + local, has_side_effects=True),
        cost_estimate=hint(1),
        name="last",
    )(grad_first, grad_plane.reshape(plane_shape), out_grad, hidden, gates, columns, out_rows)

    groups, first_parts = lax.optimization_barrier((groups, first_parts))
    (
        grad_tokens, gain_grad, in_grad, out_sum, mixture_gain_grad, router_grad, table_grad, balance,
    ) = pl.pallas_call(
        partial(
            finish_kernel, lanes=lanes, heads=heads, width=width, head_count=head_count,
            experts=experts, token_total=token_total,
        ),
        out_shape=(
            shape_of((rows, model_width), F32),
            shape_of((1, feature_rows), F32),
            shape_of((feature_rows, 3 * model_width), F32),
            shape_of((feature_rows, model_width), F32),
            shape_of((1, feature_rows), F32),
            shape_of((experts, feature_rows), F32),
            shape_of((bucket_rows, head_count), F32),
            shape_of((1, 1), F32),
        ),
        compiler_params=params(),
        cost_estimate=hint(6),
        name="finish",
    )(first_parts, plane_parts, out_parts, tokens, grad_hidden, attention_in, gain_row, counts)

    up_grad, down_grad = sum_grads(groups, expert_up.shape, expert_down.shape, fsdp_size)
    return (
        layer_output,
        balance.reshape(()),
        grad_tokens,
        gain_grad.reshape(feature_rows),
        mixture_gain_grad.reshape(feature_rows),
        in_grad,
        out_sum,
        router_grad.T,
        table_grad,
        up_grad,
        down_grad,
    )


def solution(mesh):
    in_specs = (
        P(("exp", "fsdp"), None),
        P(("exp", "fsdp"), None),
        P("exp"),
        P(("exp", "fsdp"), None),
        P(("exp", "fsdp"), None),
        P(("exp", "fsdp")),
        P(("exp", "fsdp")),
        P(("exp", "fsdp"), None),
        P(("exp", "fsdp"), None),
        P(("exp", "fsdp"), None),
        P(("exp", "fsdp"), None),
        P("exp", "fsdp", None),
        P("exp", "fsdp", None),
    )
    out_specs = (
        P(("exp", "fsdp"), None),
        P(),
        P(("exp", "fsdp"), None),
        P(("exp", "fsdp")),
        P(("exp", "fsdp")),
        P(("exp", "fsdp"), None),
        P(("exp", "fsdp"), None),
        P(("exp", "fsdp"), None),
        P(("exp", "fsdp"), None),
        P("exp", "fsdp", None),
        P("exp", "fsdp", None),
    )
    return jax.shard_map(
        on_device, mesh=mesh, in_specs=in_specs, out_specs=out_specs, check_vma=False
    )
```

```python
from functools import partial

import jax
import jax.numpy as jnp
from jax import lax
from jax.experimental import pallas as pl
from jax.experimental.pallas import tpu as pltpu
from jax.sharding import PartitionSpec as P

WINDOW = 1024
BUCKETS = 256

EPSILON = 1e-06
AUX_WEIGHT = 0.01
MASKED = -1e30
QUERY_BLOCK = 256
SKEW = 128
VMEM_BYTES = 58 * 1024 * 1024
MESH = pl.DeviceIdType.MESH
F32 = jnp.float32
BF16 = jnp.bfloat16


def params(**kwargs):
    return pltpu.CompilerParams(vmem_limit_bytes=VMEM_BYTES, **kwargs)


def shape_of(shape, dtype):
    return jax.ShapeDtypeStruct(shape, dtype)


def whole(shape):
    return pl.BlockSpec(shape, lambda *_: (0,) * len(shape))


def contract_last(left_side, right_side):
    return lax.dot_general(
        left_side, right_side, (((1,), (1,)), ((), ())), preferred_element_type=F32
    )


def matmul(left_side, right_side):
    return jnp.dot(left_side, right_side, preferred_element_type=F32)


def turned(value):
    return value.astype(F32).T


def bucket_index(distance):
    near_count = BUCKETS // 2
    spread = max(WINDOW - near_count, 1)
    far_bucket = (
        near_count + jnp.maximum(distance - near_count, 0) * (BUCKETS - near_count) // spread
    )
    return jnp.where(distance < near_count, distance, far_bucket)

def hint(micros):
    return pl.CostEstimate(flops=int(micros * 1.0e9), bytes_accessed=1024, transcendentals=0)


def flipped(place, other, size):
    result, bit = 0, 1
    while bit < size:
        result = result + bit * ((place // bit + other // bit) % 2)
        bit *= 2
    return result


class Grid:
    def __init__(self):
        self.exp_size, self.fsdp_size = lax.axis_size("exp"), lax.axis_size("fsdp")
        self.device_count = self.exp_size * self.fsdp_size
        self.y_size = max(
            y for y in range(1, self.exp_size + 1) if self.exp_size % y == 0 and 2 * y * y <= self.exp_size
        ) if self.exp_size > 1 else 1
        self.z_size = self.exp_size // self.y_size
        self.x_size = self.fsdp_size // 2

    def here(self):
        self.exp, self.fsdp = lax.axis_index("exp"), lax.axis_index("fsdp")
        self.z, self.y = self.exp // self.y_size, self.exp % self.y_size
        self.x, self.core = self.fsdp // 2, self.fsdp % 2
        self.linear = self.exp * self.fsdp_size + self.fsdp
        return self

    def at(self, z=None, y=None, fsdp=None):
        z = self.z if z is None else z
        y = self.y if y is None else y
        return (z * self.y_size + y, self.fsdp if fsdp is None else fsdp)

    def x_from(self, hop):
        return ((self.x + self.x_size + hop) % self.x_size) * 2 + self.core

    def source_z(self, turn):
        if self.z_size & (self.z_size - 1) == 0:
            return flipped(self.z, turn, self.z_size)
        return (self.z + turn) % self.z_size

    def target_z(self, turn):
        if self.z_size & (self.z_size - 1) == 0:
            return flipped(self.z, turn, self.z_size)
        return (self.z + self.z_size - turn) % self.z_size

    def exp_steps(self):
        turns = sorted(range(self.z_size), key=lambda turn: -turn.bit_length())
        steps = []
        for turn in turns:
            for hop in range(self.y_size):
                if turn or hop:
                    to = self.target_z(turn) * self.y_size + (self.y + self.y_size - hop) % self.y_size
                    origin = self.source_z(turn) * self.y_size + (self.y + hop) % self.y_size
                    steps.append((to, origin))
        return steps

    def sibling(self, fsdp):
        return fsdp + 1 - 2 * (fsdp % 2)


class Links:
    def __init__(self, send, receive):
        self.send, self.receive, self.used = send, receive, 0

    def copy(self, source, target, device, landing):
        index = self.used
        self.used += 1
        going = pltpu.make_async_remote_copy(
            src_ref=source, dst_ref=target, send_sem=self.send.at[index],
            recv_sem=self.receive.at[index], device_id=device, device_id_type=MESH,
        )
        coming = pltpu.make_async_remote_copy(
            src_ref=landing, dst_ref=landing, send_sem=self.send.at[index],
            recv_sem=self.receive.at[index], device_id=device, device_id_type=MESH,
        )
        return going, coming


def greet(devices):
    barrier = pltpu.get_barrier_semaphore()
    for device in devices:
        pl.semaphore_signal(barrier, inc=1, device_id=device, device_id_type=MESH)
    pl.semaphore_wait(barrier, len(devices))


def chip_peers(grid):
    peers = [(grid.exp, grid.sibling(grid.fsdp))]
    return peers + [(grid.exp, grid.x_from(hop)) for hop in range(1, grid.x_size)]


class ChipGather:
    def __init__(self, grid, links, own_sem, source, target):
        self.grid, self.links, self.target = grid, links, target
        self.own = pltpu.make_async_copy(source, target.at[grid.fsdp], own_sem)
        sibling = grid.sibling(grid.fsdp)
        self.along_x, self.across = [], []
        for hop in range(1, grid.x_size):
            self.along_x.append(
                links.copy(
                    source, target.at[grid.fsdp], (grid.exp, grid.x_from(hop)),
                    target.at[grid.x_from(-hop)],
                )
            )
        self.across.append(
            links.copy(source, target.at[grid.fsdp], (grid.exp, sibling), target.at[sibling])
        )

    def start(self):
        for going, _ in self.along_x + self.across:
            going.start()
        self.own.start()

    def forward(self):
        grid = self.grid
        for hop in range(1, grid.x_size):
            self.along_x[hop - 1][1].wait_recv()
            held = grid.x_from(-hop)
            other = grid.sibling(held)
            self.across.append(
                self.links.copy(
                    self.target.at[held], self.target.at[held],
                    (grid.exp, grid.sibling(grid.fsdp)), self.target.at[other],
                )
            )
            self.across[-1][0].start()

    def finish(self):
        for _, coming in self.across:
            coming.wait_recv()
        for going, _ in self.along_x + self.across:
            going.wait_send()
        self.own.wait()


class Exchange:
    def __init__(self, grid, links, own_sems, pairs):
        self.steps = grid.exp_steps()
        self.peers = [(to, grid.fsdp) for to, _ in self.steps]
        self.copies, self.own = [], []
        for index, (source, target) in enumerate(pairs):
            for to, origin in self.steps:
                self.copies.append(
                    links.copy(
                        source(to), target.at[grid.exp], (to, grid.fsdp), target.at[origin]
                    )
                )
            self.own.append(
                pltpu.make_async_copy(source(grid.exp), target.at[grid.exp], own_sems.at[index])
            )

    def start(self):
        for going, _ in self.copies:
            going.start()
        for own in self.own:
            own.start()

    def finish(self):
        for going, coming in self.copies:
            coming.wait_recv()
            going.wait_send()
        for own in self.own:
            own.wait()


ANYWHERE = pl.BlockSpec(memory_space=pl.ANY)
IN_VMEM = pl.BlockSpec(memory_space=pltpu.VMEM)


def dma_sems(count):
    return pltpu.SemaphoreType.DMA((count,))


def plane_of(source, part, to):
    return source.at[to] if part is None else source.at[to, part]


class Lanes:
    def __init__(self, heads, width, padded_heads, experts):
        self.weights = 3 * heads * width
        self.base = self.weights // 128 * 128
        self.router = self.weights - self.base
        self.gain = self.router + experts
        self.table = self.gain + 1
        self.count = self.table + padded_heads
        self.width = -(-(self.weights + 2 * experts + 1 + padded_heads) // 128) * 128
        self.extra = self.width - self.base
        self.shift = self.count - self.router


def bucket_rows_select(features, feature_rows, bucket_rows, span):
    row = lax.broadcasted_iota(jnp.int32, (features, 1), 0)
    within = lax.rem(row, feature_rows)
    bucket = jnp.where(
        within < bucket_rows, lax.div(row, feature_rows) * bucket_rows + within, -1
    )
    distance = lax.broadcasted_iota(jnp.int32, (1, span), 1) - SKEW
    near = BUCKETS // 2
    spread = max(WINDOW - near, 1)
    far = near + lax.div(jnp.maximum(distance - near, 0) * (BUCKETS - near), spread)
    wanted = jnp.where(distance < near, distance, far)
    reachable = (distance >= 0) & (distance < WINDOW)
    wanted = jnp.where(reachable, wanted, -2)
    return jnp.where(bucket == wanted, 1.0, 0.0).astype(BF16), reachable


def as_column(row, size):
    row_place = lax.broadcasted_iota(jnp.int32, (size, size), 0)
    lane = lax.broadcasted_iota(jnp.int32, (size, size), 1)
    spread = jnp.broadcast_to(row.astype(F32), (size, size))
    return jnp.sum(jnp.where(row_place == lane, spread, 0.0), axis=1, keepdims=True)


def padded_rows(value, rows):
    if value.shape[0] == rows:
        return value
    return jnp.concatenate([value, jnp.zeros((rows - value.shape[0], value.shape[1]), F32)], axis=0)


def padded_lanes(value, lanes):
    if value.shape[1] == lanes:
        return value
    return jnp.concatenate([value, jnp.zeros((value.shape[0], lanes - value.shape[1]), F32)], axis=1)


class Wide:
    def __init__(self, grid, links, own_sem, source, target):
        self.grid, self.links, self.target = grid, links, target
        self.own = pltpu.make_async_copy(
            source, target.at[grid.z, grid.y, grid.x, grid.core], own_sem
        )
        stage = []
        for hop in range(1, grid.z_size):
            origin = (grid.z + grid.z_size - hop) % grid.z_size
            stage.append(
                links.copy(
                    source, target.at[grid.z, grid.y, grid.x, grid.core],
                    grid.at(z=(grid.z + hop) % grid.z_size),
                    target.at[origin, grid.y, grid.x, grid.core],
                )
            )
        self.stages = [stage]

    def start(self):
        self.own.start()
        for going, _ in self.stages[0]:
            going.start()

    def turn(self, axis):
        grid, target = self.grid, self.target
        for _, coming in self.stages[-1]:
            coming.wait_recv()
        stage = []
        if axis == 0:
            self.own.wait()
            held = target.at[:, grid.y, grid.x, grid.core]
            for hop in range(1, grid.y_size):
                origin = (grid.y + grid.y_size - hop) % grid.y_size
                stage.append(
                    self.links.copy(
                        held, held, grid.at(y=(grid.y + hop) % grid.y_size),
                        target.at[:, origin, grid.x, grid.core],
                    )
                )
        elif axis == 1:
            held = target.at[:, :, grid.x, grid.core]
            for hop in range(1, grid.x_size):
                origin = (grid.x + grid.x_size - hop) % grid.x_size
                stage.append(
                    self.links.copy(
                        held, held, (grid.exp, grid.x_from(hop)),
                        target.at[:, :, origin, grid.core],
                    )
                )
        else:
            held = target.at[:, :, :, grid.core]
            stage.append(
                self.links.copy(
                    held, held, (grid.exp, grid.sibling(grid.fsdp)), target.at[:, :, :, 1 - grid.core]
                )
            )
        for going, _ in stage:
            going.start()
        self.stages.append(stage)

    def finish(self):
        for _, coming in self.stages[-1]:
            coming.wait_recv()
        for stage in self.stages:
            for going, _ in stage:
                going.wait_send()


def start_kernel(
    tokens, cotangent, routes_t, slots_t, attention_gain, mixture_gain, attention_in, router_t, table,
    attention_out, expert_up, expert_down, *refs, lanes, heads, width, head_count, experts, capacity,
    local, late,
):
    all_tokens, all_planes, cotangent_early, position_rows, columns, full_out = refs[:6]
    cotangent_late, refs = refs[6 : 6 + late], refs[6 + late :]
    shards = refs[: 2 * local]
    planes, up_stage, down_stage, send, receive, own, fetch, split = refs[2 * local :]
    grid = Grid().here()
    links = Links(send, receive)
    z_size, y_size, fsdp_size = grid.z_size, grid.y_size, grid.fsdp_size
    near = [
        (grid.exp, (grid.fsdp + turn) % fsdp_size) for turn in range(1, fsdp_size)
    ] + [grid.at(z=(grid.z + hop) % z_size) for hop in range(1, z_size)]
    beside = [grid.at(y=(grid.y + hop) % y_size) for hop in range(1, y_size)]
    gathered = ChipGather(grid, links, own.at[0], tokens, all_tokens)
    widely = Wide(grid, links, own.at[2], attention_out, full_out)
    part = expert_down.shape[1]
    depth = expert_up.shape[1]
    fetches = []
    for index in range(local):
        fetches.append(
            pltpu.make_async_copy(expert_up.at[index], up_stage.at[index], fetch.at[2 * index])
        )
        fetches.append(
            pltpu.make_async_copy(
                expert_down.at[index], down_stage.at[index], fetch.at[2 * index + 1]
            )
        )
    greet(near + beside)
    widely.start()
    for copy in fetches:
        copy.start()

    feature_rows = attention_in.shape[0]
    model_width = head_count * width
    gained = attention_in[...].astype(F32) * as_column(attention_gain[...], feature_rows)
    route_rows, slot_rows = routes_t[...].astype(F32), slots_t[...].astype(F32)
    columns[...] = padded_rows(jnp.concatenate([route_rows, slot_rows], axis=0), 128).T
    row_count = columns.shape[0]
    expert_lanes = lax.broadcasted_iota(jnp.int32, (row_count, experts), 1).astype(F32)
    named = jnp.zeros((row_count, experts), F32)
    for k in range(2):
        named = named + jnp.where(expert_lanes == columns[:, k : k + 1], 1.0, 0.0)
    named = jnp.sum(named, axis=0, keepdims=True)
    place = lax.broadcasted_iota(jnp.int32, (feature_rows, feature_rows), 0)
    same = place == lax.broadcasted_iota(jnp.int32, (feature_rows, feature_rows), 1)
    router = contract_last(jnp.where(same, 1.0, 0.0).astype(BF16), router_t[...])
    pieces = [
        router,
        as_column(mixture_gain[...], feature_rows),
        padded_rows(padded_lanes(table[...].astype(F32), heads * fsdp_size), feature_rows),
        padded_rows(named, feature_rows),
    ]
    taken = sum(piece.shape[1] for piece in pieces)
    if lanes.width > lanes.weights + taken:
        pieces.append(jnp.zeros((feature_rows, lanes.width - lanes.weights - taken), F32))
    for place in range(fsdp_size):
        first, last = place * heads * width, min((place + 1) * heads * width, model_width)
        own_pieces = []
        for kind in range(3):
            if last > first:
                own_pieces.append(gained[:, kind * model_width + first : kind * model_width + last])
            if last - first < heads * width:
                own_pieces.append(
                    jnp.zeros((feature_rows, heads * width - max(last - first, 0)), F32)
                )
        planes[place] = jnp.concatenate(own_pieces + pieces, axis=1).astype(BF16)
    placed = []
    for turn in range(1, fsdp_size):
        to = (grid.fsdp + turn) % fsdp_size
        origin = (grid.fsdp + fsdp_size - turn) % fsdp_size
        placed.append(
            links.copy(
                planes.at[to], all_planes.at[grid.z, grid.y, grid.fsdp], (grid.exp, to),
                all_planes.at[grid.z, grid.y, origin],
            )
        )
        placed[-1][0].start()
    kept = pltpu.make_async_copy(
        planes.at[grid.fsdp], all_planes.at[grid.z, grid.y, grid.fsdp], own.at[1]
    )
    kept.start()
    gathered.start()
    for _, coming in placed:
        coming.wait_recv()
    kept.wait()

    def over_y(z):
        for turn in range(1, y_size):
            forwarded.append(
                links.copy(
                    all_planes.at[z, grid.y],
                    all_planes.at[z, grid.y],
                    grid.at(y=(grid.y + turn) % y_size),
                    all_planes.at[z, (grid.y + y_size - turn) % y_size],
                )
            )
            forwarded[-1][0].start()

    along_z, forwarded = [], []
    for hop in range(1, z_size):
        along_z.append(
            links.copy(
                all_planes.at[grid.z, grid.y],
                all_planes.at[grid.z, grid.y],
                grid.at(z=(grid.z + hop) % z_size),
                all_planes.at[(grid.z + z_size - hop) % z_size, grid.y],
            )
        )
        along_z[-1][0].start()
    over_y(grid.z)
    widely.turn(0)

    for copy in fetches:
        copy.wait()
    splits = []
    for index in range(local):
        up, down = shards[2 * index : 2 * index + 2]
        stores = [
            (
                up_stage.at[index, :, pl.ds(block * part, part)],
                up.at[pl.ds(block * depth, depth), :],
            )
            for block in range(fsdp_size)
        ]
        for source, target in stores + [(down_stage.at[index], down)]:
            splits.append(pltpu.make_async_copy(source, target, split.at[len(splits)]))
            splits[-1].start()

    widely.turn(1)

    place = route_rows * capacity + slot_rows
    position_rows[...] = padded_rows(place, 8)
    select_rows([cotangent_early] + list(cotangent_late), place, cotangent[...])

    for hop in range(1, z_size):
        along_z[hop - 1][1].wait_recv()
        over_y((grid.z + z_size - hop) % z_size)
    gathered.forward()
    widely.turn(2)
    for going, coming in forwarded:
        coming.wait_recv()
        going.wait_send()
    for going, _ in placed + along_z:
        going.wait_send()
    gathered.finish()
    widely.finish()
    for copy in splits:
        copy.wait()


def project_kernel(
    tokens, plane, segments, normed, query_t, key_n, query_n, value_n, key_t, value_t, bias, counts,
    weight_t, table_t, *, heads, width, lanes, feature_rows, bucket_rows,
):
    @pl.when(pl.program_id(0) == 0)
    def _():
        weight_t[...] = turned(plane[:, : lanes.weights]).astype(BF16)
        extra = plane[:, lanes.base :]
        span = bias.shape[2]
        select, reachable = bucket_rows_select(plane.shape[0], feature_rows, bucket_rows, span)
        table_t[...] = lax.dot_general(
            extra, select, (((0,), (0,)), ((), ())), preferred_element_type=F32
        )
        first = lanes.table + lax.axis_index("fsdp") * heads
        for head in range(heads):
            bias[head] = jnp.where(reachable, table_t[pl.ds(first + head, 1), :], MASKED)
        summed = jnp.sum(extra.astype(F32), axis=0, keepdims=True)
        counts[...] = pltpu.roll(
            jnp.broadcast_to(summed, counts.shape), lanes.extra - lanes.shift, 1
        )

    inputs = tokens[0].astype(F32)
    scale = lax.rsqrt(jnp.mean(inputs * inputs, axis=1, keepdims=True) + EPSILON)
    low = (inputs * scale).astype(BF16)
    normed[...] = low
    rows = low.shape[0]
    projected = contract_last(weight_t[...], low).astype(BF16).astype(F32)
    document = segments[...] % 4
    places = lax.broadcasted_iota(jnp.int32, (8, rows), 0)
    same = places == document
    hot = jnp.where(same, 1.0, 0.0)
    barred = jnp.where(same | (places >= 4), 0.0, MASKED)
    filler = jnp.zeros((SKEW - 8 - width, rows), F32)
    for head in range(heads):
        query = projected[head * width : (head + 1) * width] * width ** (-0.5)
        key = projected[(heads + head) * width : (heads + head + 1) * width]
        value = projected[(2 * heads + head) * width : (2 * heads + head + 1) * width]
        query_t[head] = jnp.concatenate([query, barred, filler], axis=0).astype(BF16)
        key_n[head] = jnp.concatenate([key, hot, filler], axis=0).T.astype(BF16)
        query_n[head] = query.T.astype(BF16)
        value_n[head] = value.T.astype(BF16)
        key_t[head] = key.astype(BF16)
        value_t[head] = value.astype(BF16)


def spans(length):
    for query_start in range(0, length, QUERY_BLOCK):
        key_start = max(0, query_start - WINDOW)
        yield query_start, key_start, query_start + QUERY_BLOCK - key_start


def spread_bias(bias, skew):
    skew[...] = pltpu.roll(
        jnp.broadcast_to(bias[0], skew.shape), 0, 1, stride=1, stride_axis=0
    )


def attend_kernel(
    query_t, key_n, value_t, bias, context, context_high, log_total, attended, skew, scores, held,
    send, receive, own, *, rows,
):
    head = pl.program_id(0)
    width = value_t.shape[1]
    grid = Grid().here()
    fsdp_size = grid.fsdp_size

    def leave(number):
        place = pl.ds(pl.multiple_of(number * width, 16), width)
        copies = []
        for turn in range(1, fsdp_size):
            to = (grid.fsdp + turn) % fsdp_size
            origin = (grid.fsdp + fsdp_size - turn) % fsdp_size
            sems = dict(
                send_sem=send.at[number, turn], recv_sem=receive.at[number, turn],
                device_id=(grid.exp, to), device_id_type=MESH,
            )
            copies.append(
                (
                    pltpu.make_async_remote_copy(
                        src_ref=held.at[number, to], dst_ref=attended.at[grid.fsdp, place, :], **sems
                    ),
                    pltpu.make_async_remote_copy(
                        src_ref=attended.at[origin, place, :], dst_ref=attended.at[origin, place, :],
                        **sems,
                    ),
                )
            )
        kept = pltpu.make_async_copy(
            held.at[number, grid.fsdp], attended.at[grid.fsdp, place, :], own.at[number]
        )
        return copies, kept

    @pl.when(head == 0)
    def _():
        greet([(grid.exp, (grid.fsdp + turn) % fsdp_size) for turn in range(1, fsdp_size)])

    spread_bias(bias, skew)
    for query_start, key_start, key_count in spans(query_t.shape[2]):
        queries = slice(query_start, query_start + QUERY_BLOCK)
        keys = slice(key_start, key_start + key_count)
        raw = matmul(key_n[0, keys, :], query_t[0, :, queries])
        for start in range(0, key_count, SKEW):
            offset = query_start - key_start - start + SKEW
            scores[start : start + SKEW, :] = (
                raw[start : start + SKEW] + skew[:, offset : offset + QUERY_BLOCK]
            )
        high = jnp.max(scores[:key_count, :], axis=0, keepdims=True)
        weights = jnp.exp(scores[:key_count, :] - high)
        total = jnp.sum(weights, axis=0, keepdims=True)
        gathered = matmul(value_t[0, :, keys], weights.astype(BF16)) / total
        context_high[0, :, queries] = gathered
        log_total[0, :, queries] = high + jnp.log(total)
        for start in range(0, QUERY_BLOCK, 128):
            place = query_start + start
            piece = gathered[:, start : start + 128].astype(BF16)
            context[place // rows, :, place % rows : place % rows + 128] = piece
            held[head, place // rows, :, place % rows : place % rows + 128] = piece
    copies, kept = leave(head)
    for going, _ in copies:
        going.start()
    kept.start()

    @pl.when(head == pl.num_programs(0) - 1)
    def _():
        def finish(number, carry):
            copies, kept = leave(number)
            for going, coming in copies:
                coming.wait_recv()
                going.wait_send()
            kept.wait()
            return carry

        lax.fori_loop(0, pl.num_programs(0), finish, 0)


def attend_back_kernel(
    query_t, key_n, query_n, value_n, key_t, grad_t, grad_n, context_high, log_total, bias,
    grad_projected, grad_bias, skew, grad_skew, grad_key, grad_value, *, scale,
):
    spread_bias(bias, skew)
    grad_skew[...] = jnp.zeros_like(grad_skew)
    grad_key[...] = jnp.zeros_like(grad_key)
    grad_value[...] = jnp.zeros_like(grad_value)
    inner = jnp.sum(grad_t[0].astype(F32) * context_high[0], axis=0, keepdims=True)
    for query_start, key_start, key_count in spans(query_t.shape[2]):
        queries = slice(query_start, query_start + QUERY_BLOCK)
        keys = slice(key_start, key_start + key_count)
        raw = matmul(key_n[0, keys, :], query_t[0, :, queries])
        grad_weights = matmul(value_n[0, keys, :], grad_t[0, :, queries])
        weights_low, grad_low = [], []
        for start in range(0, key_count, SKEW):
            offset = query_start - key_start - start + SKEW
            part = slice(start, start + SKEW)
            weights = jnp.exp(
                raw[part] + skew[:, offset : offset + QUERY_BLOCK] - log_total[0, :, queries]
            )
            grad_scores = weights * (grad_weights[part] - inner[:, queries])
            grad_skew[:, offset : offset + QUERY_BLOCK] += grad_scores
            weights_low.append(weights.astype(BF16))
            grad_low.append(grad_scores.astype(BF16))
        weights_low = jnp.concatenate(weights_low, axis=0)
        grad_low = jnp.concatenate(grad_low, axis=0)
        grad_projected[0, 0, :, queries] = (matmul(key_t[0, :, keys], grad_low) * scale).astype(BF16)
        grad_key[keys, :] += matmul(grad_low, query_n[0, queries, :])
        grad_value[keys, :] += matmul(weights_low, grad_n[0, queries, :])
    grad_projected[1, 0] = grad_key[...].T.astype(BF16)
    grad_projected[2, 0] = grad_value[...].T.astype(BF16)
    count = SKEW
    span = skew.shape[1]
    while count > 8:
        count //= 2
        grad_skew[:count, :] += pltpu.roll(grad_skew[count : 2 * count, :], span - count, 1)
    summed = grad_skew[0:1, :]
    for row in range(1, 8):
        summed = summed + pltpu.roll(grad_skew[row : row + 1, :], span - row, 1)
    grad_bias[0] = summed

def expert_lane(shape, lanes):
    return lax.broadcasted_iota(jnp.int32, shape, 1) - lanes.router


def int_columns(columns):
    values = columns[:, 0:4].astype(jnp.int32)
    return values[:, 0:2], values[:, 2:4]


def route_kernel(
    tokens, attended_t, attention_out, plane, columns, position_rows, *refs,
    experts, lanes, capacity, crossing,
):
    over, refs = refs[:crossing], refs[crossing:]
    hidden, routed, probabilities, gates, outgoing, rows_in, gates_in = refs[:7]
    landed, refs = refs[7 : 7 + crossing], refs[7 + crossing :]
    slot_gates, send, receive, own = refs
    grid = Grid().here()
    links = Links(send, receive)
    exp_size = grid.exp_size
    sibling = (grid.exp, grid.sibling(grid.fsdp))
    greet([((grid.exp + hop) % exp_size, grid.fsdp) for hop in range(1, exp_size)] + [sibling])
    swaps = [links.copy(source, target, sibling, target) for source, target in zip(over, landed)]
    for going, _ in swaps:
        going.start()
    rows, model_width = tokens.shape
    routes, slots = int_columns(columns)
    attended_low = turned(attended_t[:model_width]).astype(BF16)
    hidden_state = tokens[...].astype(F32) + matmul(attended_low, attention_out[...])
    hidden[...] = hidden_state
    scale = lax.rsqrt(jnp.mean(hidden_state * hidden_state, axis=1, keepdims=True) + EPSILON)
    extra = plane[:, lanes.base :]
    gain = extra.astype(F32).T[lanes.gain : lanes.gain + 1]
    low = (hidden_state * scale * gain).astype(BF16)
    routed[...] = low
    member_slots = experts // exp_size * capacity
    work = Exchange(
        grid, links, own,
        [
            (lambda to: outgoing.at[to, pl.ds(0, capacity), :], rows_in),
            (partial(plane_of, slot_gates, None), gates_in),
        ],
    )
    for number, to in enumerate([to for to, _ in work.steps] + [grid.exp]):
        slot = lax.broadcasted_iota(jnp.int32, (member_slots, rows), 0) + to * member_slots
        slot = slot.astype(F32)
        picked = (slot == position_rows[0:1, :]) | (slot == position_rows[1:2, :])
        outgoing[to] = matmul(jnp.where(picked, 1.0, 0.0).astype(BF16), low).astype(BF16)
        (work.copies[number][0] if number < len(work.steps) else work.own[0]).start()
    logits = matmul(low, extra)
    lane = expert_lane(logits.shape, lanes)
    logits = jnp.where((lane >= 0) & (lane < experts), logits, MASKED)
    powers = jnp.exp(logits - jnp.max(logits, axis=1, keepdims=True))
    powers = powers / jnp.sum(powers, axis=1, keepdims=True)
    probabilities[...] = powers
    chosen = [
        jnp.sum(jnp.where(lane == routes[:, k : k + 1], powers, 0.0), axis=1, keepdims=True)
        for k in range(2)
    ]
    total = chosen[0] + chosen[1]
    gate_values = [chosen[k] / total for k in range(2)]
    pair = lax.broadcasted_iota(jnp.int32, (rows, 2), 1)
    gates[...] = jnp.where(pair == 0, gate_values[0], gate_values[1])
    gate_lanes = slot_gates.shape[2]
    slot_lanes = lax.broadcasted_iota(jnp.int32, (rows, gate_lanes), 1)
    inside = slot_lanes < member_slots
    places = routes * capacity + slots
    for member in range(exp_size):
        by_slot = jnp.zeros((rows, gate_lanes), F32)
        for k in range(2):
            hit = (slot_lanes + member * member_slots == places[:, k : k + 1]) & inside
            by_slot = by_slot + jnp.where(hit, gate_values[k], 0.0)
        slot_gates[member] = jnp.broadcast_to(
            jnp.sum(by_slot, axis=0, keepdims=True), slot_gates.shape[1:]
        )
    for going, _ in work.copies[exp_size - 1 :]:
        going.start()
    work.own[1].start()
    work.finish()
    for going, coming in swaps:
        coming.wait_recv()
        going.wait_send()


def select_rows(outgoing, position_rows, values):
    rows = values.shape[0]
    sizes = [array.shape[1] for array in outgoing]
    for member in range(outgoing[0].shape[0]):
        slots = lax.broadcasted_iota(jnp.int32, (sum(sizes), rows), 0) + member * sum(sizes)
        slots = slots.astype(F32)
        picked = (slots == position_rows[0:1, :]) | (slots == position_rows[1:2, :])
        found = matmul(jnp.where(picked, 1.0, 0.0).astype(BF16), values).astype(BF16)
        first = 0
        for array, size in zip(outgoing, sizes):
            array[member] = found[first : first + size]
            first += size


def gelu_parts(value):
    magnitude = jnp.abs(value)
    power = jnp.exp2(value * value * -0.7213475204444817)
    base = 1.0 + (0.3275911 * 0.7071067811865476) * magnitude
    step = pl.reciprocal(base, approx=True)
    step = step * (2.0 - base * step)
    series = step * (
        0.127414796
        + step * (-0.142248368 + step * (0.7107068705 + step * (-0.7265760135 + step * 0.5307027145)))
    )
    tail = series * power
    normal = jnp.where(value < 0.0, tail, 1.0 - tail)
    return value * normal, normal + value * (power * 0.3989422804014327)


def expert_kernel(*refs, layout, index, local, half, capacity, parts):
    shards = 2 * half
    refs = Bag(layout, refs)
    grid = Grid().here()
    z_size, y_size = grid.z_size, grid.y_size
    last = index == local - 1
    sibling = (grid.exp, grid.sibling(grid.fsdp))
    links = Links(refs.send[0], refs.receive[0])
    rows_all, cot, up_all, down_all = (
        refs.rows_all[0], refs.cot[0], refs.up_all[0], refs.down_all[0]
    )
    total = refs.total[0]
    if last:
        active, grad_hidden, unscaled = refs.active[0], refs.grad_hidden[0], refs.unscaled[0]
    else:
        grad_total, slot_grad = refs.grad_total[0], refs.slot_grad[0]
    gates, gate_column = refs.gates[0], refs.gate_column[0]
    rows_t, slot_t = refs.rows_t[0], refs.slot_t[0]
    grad_up, grad_down = refs.grad_up[0], refs.grad_down[0]
    grad_rows, grad_gates = refs.grad_rows[0], refs.grad_gates[0]
    up_keep, up_taken, down_keep, down_taken = refs.own
    keep_up = [up_keep] + list(refs.far_keep_up)
    taken_up = [up_taken] + list(refs.far_taken_up)
    keep_down = [down_keep] + list(refs.far_keep_down)
    taken_down = [down_taken] + list(refs.far_taken_down)
    load_sem, fetch_sem, store_sem = refs.load_sem[0], refs.fetch_sem[0], refs.store_sem[0]
    store_there, stored_here = refs.store_there[0], refs.stored_here[0]
    pass_sem = refs.pass_sem[0]
    blocks, _, model_width = rows_all.shape
    part = up_all.shape[2]
    count = blocks * capacity
    depth = model_width // shards
    power = z_size & (z_size - 1) == 0
    together = 2 if power and z_size > 1 else 1
    group_rows = together * y_size * capacity

    source_z, target_z = grid.source_z, grid.target_z

    def owner(place, core):
        return ((grid.x + place % half) % half) * 2 + (core + place // half) % 2

    def rows_of(place, core=None):
        core = grid.core if core is None else core
        return pl.ds(pl.multiple_of(owner(place, core) * depth, 16), depth)

    loads = [pltpu.make_async_copy(refs.rows_in[0], rows_all, load_sem.at[1])]
    late_count = 0
    if last and refs.cot_late:
        late_count = refs.cot_late[0].shape[1]
        loads.append(
            pltpu.make_async_copy(
                refs.cot_late[0], cot.at[:, pl.ds(capacity - late_count, late_count)], load_sem.at[4]
            )
        )
    loads.append(
        pltpu.make_async_copy(
            refs.cot_in[0].at[:, pl.ds(index * capacity, capacity - late_count)],
            cot.at[:, pl.ds(0, capacity - late_count)], load_sem.at[0],
        )
    )
    my_up, my_down = refs.my_up, refs.my_down
    swapped_up, swapped_down = refs.swapped_up, refs.swapped_down
    local_up = list(enumerate(my_up)) + [
        (half + number, array) for number, array in enumerate(swapped_up)
    ]
    local_down = list(enumerate(my_down)) + [
        (half + number, array) for number, array in enumerate(swapped_down)
    ]

    def fetch_up(place):
        return [
            pltpu.make_async_copy(
                array.at[rows_of(place), :], up_all.at[place, rows_of(shard), :],
                fetch_sem.at[place, number],
            )
            for number, (shard, array) in enumerate(local_up)
        ]

    fetched_down = {
        shard: pltpu.make_async_copy(
            array, down_all.at[shard], fetch_sem.at[shards + number, 0]
        )
        for number, (shard, array) in enumerate(local_down)
    }
    cross_down = {
        half + shard: links.copy(
            my_down[shard], down_all.at[half + shard], sibling, down_all.at[half + shard]
        )
        for shard in range(len(swapped_down), half)
    }
    cross_up = [
        links.copy(
            my_up[shard].at[rows_of(place, 1 - grid.core), :],
            up_all.at[place, rows_of(shard), :], sibling,
            up_all.at[place, rows_of(half + shard), :],
        )
        for shard in range(len(swapped_up), half)
        for place in range(shards)
    ]
    cross_next = [
        links.copy(source, target, sibling, target)
        for source, target in zip(refs.next_mine, refs.next_swapped)
    ]
    work = Exchange(
        grid, links, refs.own_sem[0],
        [
            (partial(plane_of, source, place), target)
            for source, place, target in zip(refs.moved_from, parts, refs.moved_to)
        ],
    )
    def member(z, y):
        return z * y_size + y

    def give_back(turn, hop):
        to = member(source_z(turn), (grid.y + hop) % y_size)
        origin = member(target_z(turn), (grid.y + y_size - hop) % y_size)
        pairs = []
        for number, (held, target) in enumerate(
            ((grad_rows, refs.back_rows[0]), (grad_gates, refs.back_gates[0]))
        ):
            sems = dict(
                send_sem=refs.back_send[0].at[number, turn, hop],
                recv_sem=refs.back_receive[0].at[number, turn, hop],
                device_id=(to, grid.fsdp), device_id_type=MESH,
            )
            pairs.append(
                (
                    pltpu.make_async_remote_copy(
                        src_ref=held.at[to], dst_ref=target.at[grid.exp], **sems
                    ),
                    pltpu.make_async_remote_copy(
                        src_ref=target.at[origin], dst_ref=target.at[origin], **sems
                    ),
                )
            )
        return pairs

    steps = [(turn, hop) for turn in range(z_size) for hop in range(y_size)]
    own_back = []
    if last:
        own_back = [
            pltpu.make_async_copy(held.at[grid.exp], target.at[grid.exp], load_sem.at[2 + number])
            for number, (held, target) in enumerate(
                ((grad_rows, refs.back_rows[0]), (grad_gates, refs.back_gates[0]))
            )
        ]

    for copy in loads:
        copy.start()
    order = list(range(shards))
    if not last:
        order = [(pair + 1) % half + side * half for pair in range(half) for side in (1, 0)]
    if last:
        for copy in fetched_down.values():
            copy.start()
    for place in order:
        if not last and place in fetched_down:
            fetched_down[place].start()
        for copy in fetch_up(place):
            copy.start()
    greet(
        [((grid.exp + hop) % grid.exp_size, grid.fsdp) for hop in range(1, grid.exp_size)]
        + chip_peers(grid)
    )
    for going, _ in list(cross_down.values()) + cross_up + cross_next:
        going.start()
    work.start()

    def place_at(position):
        hop = (position // 2 + 1) % half
        return hop + half * (1 - position % 2)

    def slot_rows():
        columns = gates[:, 0, :].T
        for block in range(blocks):
            piece = slice(block * capacity, (block + 1) * capacity)
            gate = columns[index * capacity : (index + 1) * capacity, block : block + 1]
            gate_column[piece, :] = gate
        slot_values = gate_column[...] * cot[...].reshape(count, model_width).astype(F32)
        slot_t[...] = slot_values.T.astype(BF16)
        if not last:
            slot_grad[...] = slot_values.astype(BF16)

    def wait_down(place):
        if place in fetched_down:
            fetched_down[place].wait()
        else:
            cross_down[place][1].wait_recv()

    def wait_crossed():
        for _, coming in cross_up:
            coming.wait_recv()

    def folded(value):
        return sum(value[:, start : start + 128] for start in range(0, value.shape[1], 128))

    def gate_rows(found, block):
        ones = jnp.ones((8, 128), F32)
        grad_gates[block] = lax.dot_general(
            ones, found, (((1,), (1,)), ((), ())), precision=lax.Precision.HIGHEST,
            preferred_element_type=F32,
        )

    def up_target(targets, hop, place):
        if hop == 0:
            return targets[0].at[rows_of(place), :]
        return targets[1].at[hop - 1, rows_of(place), :]

    def keep_stores(place, slot):
        return [
            pltpu.make_async_copy(
                grad_up.at[slot, rows_of(hop), :], up_target(keep_up, hop, place),
                store_sem.at[slot, hop],
            )
            for hop in range(half)
        ]

    def give_stores(place, slot):
        return [
            pltpu.make_async_remote_copy(
                src_ref=grad_up.at[slot, rows_of(half + hop), :],
                dst_ref=up_target(taken_up, hop, place),
                send_sem=store_there.at[slot, hop], recv_sem=stored_here.at[place, hop],
                device_id=sibling, device_id_type=MESH,
            )
            for hop in range(half)
        ]

    def down_store(slot):
        return pltpu.make_async_copy(grad_down.at[slot], keep_down[0], store_sem.at[slot, half])

    def down_give(hop, slot):
        target = taken_down[0] if hop == 0 else taken_down[1].at[hop - 1]
        return pltpu.make_async_remote_copy(
            src_ref=grad_down.at[slot], dst_ref=target,
            send_sem=store_there.at[slot, half], recv_sem=stored_here.at[hop, half],
            device_id=sibling, device_id_type=MESH,
        )

    def start_store(place, slot):
        for copy in keep_stores(place, slot) + give_stores(place, slot):
            copy.start()

        @pl.when(place == 0)
        def _():
            down_store(slot).start()

        for hop in range(half):

            @pl.when(place == half + hop)
            def _(hop=hop):
                down_give(hop, slot).start()

            if hop > 0:

                @pl.when(place == hop)
                def _(hop=hop):
                    keep_down[1][hop - 1] = grad_down[slot]

    def wait_store(place, slot):
        for copy in keep_stores(place, slot):
            copy.wait()
        for copy in give_stores(place, slot):
            copy.wait_send()

        @pl.when(place == 0)
        def _():
            down_store(slot).wait()

        for hop in range(half):

            @pl.when(place == half + hop)
            def _(hop=hop):
                down_give(hop, slot).wait_send()

    early_rows = part // 2 if last else 0
    early = []
    if last:
        early = [
            links.copy(
                keep_down[1].at[hop - 1, pl.ds(0, early_rows), :], refs.early_down[0].at[hop - 1],
                (grid.exp, grid.x_from(hop)), refs.early_down[0].at[hop - 1],
            )
            for hop in range(1, half)
        ]

    def sum_down():
        for hop in range(1, half):
            down_give(hop, 0).wait_recv()
            keep_down[1][hop - 1] = (
                keep_down[1][hop - 1].astype(F32) + taken_down[1][hop - 1].astype(F32)
            ).astype(BF16)
            if last:
                early[hop - 1][0].start()

    def fused(position, carry):
        place, slot = place_at(position), position % 2
        for copy in fetch_up(place):
            copy.wait()
        for which in range(shards):

            @pl.when(place == which)
            def _(which=which):
                wait_down(which)

        up, down = up_all[place], down_all[place]
        rows = rows_all[...].reshape(count, model_width)
        pieces = [slice(start, start + 256) for start in range(0, count, 256)]

        def products_of(piece):
            return matmul(rows[piece], up), contract_last(slot_grad[piece, :], down)

        raw = products_of(pieces[0])
        active_low, grad_low = [], []
        for number, piece in enumerate(pieces):
            hidden, grad_active = raw
            if number + 1 < len(pieces):
                raw = products_of(pieces[number + 1])
            activated, slope = gelu_parts(hidden)
            active_low.append(activated.astype(BF16))
            grad_low.append((grad_active * slope).astype(BF16))
            total[piece, :] += matmul(active_low[number], down)
            grad_total[piece, :] += contract_last(grad_low[number], up)
        active_low = jnp.concatenate(active_low, axis=0)
        grad_low = jnp.concatenate(grad_low, axis=0)

        @pl.when(position >= 2)
        def _():
            wait_store(place_at(position - 2), slot)

        grad_up[slot] = matmul(rows_t[...], grad_low).astype(BF16)
        grad_down[slot] = matmul(slot_t[...], active_low).T.astype(BF16)
        start_store(place, slot)
        return carry

    def group(step, carry):
        number = z_size // together - 1 - step
        turns = [number * together + more for more in range(together)]
        if together == 2:
            place_of_group = flipped(grid.z // 2, number, z_size // 2)
        else:
            place_of_group = source_z(number)
        members = pl.ds(place_of_group * together * y_size, together * y_size)
        span = pl.ds(pl.multiple_of(place_of_group * group_rows, 16), group_rows)
        rows = rows_all[members].reshape(group_rows, model_width)
        gate = gate_column[span, :]
        grad = jnp.zeros((group_rows, model_width), F32)
        products = jnp.zeros((group_rows, 128), F32)
        ahead = matmul(rows, up_all[0])
        for place in range(shards):
            hidden = ahead
            if place + 1 < shards:
                ahead = matmul(rows, up_all[place + 1])
            base = unscaled[place, span, :].astype(F32)
            activated, slope = gelu_parts(hidden)
            products = products + folded(activated * base)
            active_low = activated.astype(BF16)
            active[place, span, :] = active_low
            low = (gate * base * slope).astype(BF16)
            grad_hidden[place, span, :] = low
            grad = grad + contract_last(low, up_all[place])
            total[span, :] += matmul(active_low, down_all[place])
        grad_rows[members] = grad.astype(BF16).reshape(together * y_size, capacity, model_width)
        for hop in range(together * y_size):
            gate_rows(
                products[hop * capacity : (hop + 1) * capacity],
                place_of_group * together * y_size + hop,
            )
        for turn in turns:
            for hop in range(y_size):

                @pl.when(turn + hop > 0)
                def _(turn=turn, hop=hop):
                    for going, _ in give_back(turn, hop):
                        going.start()

        return carry

    def column(position, carry):
        place, slot = place_at(position), position % 2
        if half > 1:

            @pl.when(position == shards - 1)
            def _():
                sum_down()

        @pl.when(position >= 2)
        def _():
            wait_store(place_at(position - 2), slot)

        grad_up[slot] = matmul(rows_t[...], grad_hidden[place]).astype(BF16)
        grad_down[slot] = matmul(slot_t[...], active[place]).T.astype(BF16)
        start_store(place, slot)
        return carry

    for copy in loads[1:]:
        copy.wait()
    total[...] = jnp.zeros_like(total)
    slot_rows()
    if last:
        for place in range(shards):
            wait_down(place)
            unscaled[place] = contract_last(
                cot[...].reshape(count, model_width), down_all[place]
            ).astype(BF16)
        loads[0].wait()
        for place in range(shards):
            for copy in fetch_up(place):
                copy.wait()
        wait_crossed()
        lax.fori_loop(0, z_size // together, group, 0)
        for copy in own_back:
            copy.start()
        rows_t[...] = turned(rows_all[...].reshape(count, model_width)).astype(BF16)
        lax.fori_loop(0, shards, column, 0)
    else:
        loads[0].wait()
        rows_t[...] = turned(rows_all[...].reshape(count, model_width)).astype(BF16)
        grad_total[...] = jnp.zeros_like(grad_total)
        wait_crossed()
        lax.fori_loop(0, shards, fused, 0)
        grad_rows[...] = grad_total[...].astype(BF16).reshape(grad_rows.shape)
        for block in range(blocks):
            rows = total[block * capacity : (block + 1) * capacity, :].astype(BF16).astype(F32)
            gate_rows(folded(rows * cot[block].astype(F32)), block)

    rows_out = refs.rows_out[0]
    cot[...] = total[...].astype(BF16).reshape(blocks, capacity, model_width)
    out_copies = [pltpu.make_async_copy(cot, rows_out.at[:, index], load_sem.at[0])]
    for before in refs.outs_before:
        out_copies.append(
            pltpu.make_async_copy(before, rows_out.at[:, pl.ds(0, index)], load_sem.at[1])
        )
    for copy in out_copies:
        copy.start()
    for position in range(max(shards - 2, 0), shards):
        wait_store(place_at(position), position % 2)
    for place in range(shards):
        for copy in give_stores(place, 0):
            copy.wait_recv()
    down_give(0, 0).wait_recv()
    if half > 1:
        if not last:
            sum_down()
        keep_up[1][...] = (keep_up[1][...].astype(F32) + taken_up[1][...].astype(F32)).astype(BF16)
        passed = [
            (keep_up[1], refs.pass_up[0], 0),
            (keep_down[1].at[:, pl.ds(early_rows, part - early_rows), :], refs.pass_down[0], 1),
        ]
        for source, target, number in passed:
            out_copies.append(pltpu.make_async_copy(source, target, pass_sem.at[number]))
            out_copies[-1].start()
    for copy in out_copies:
        copy.wait()
    for going, coming in early:
        coming.wait_recv()
        going.wait_send()
    for going, coming in cross_next:
        coming.wait_recv()
        going.wait_send()
    for going, _ in list(cross_down.values()) + cross_up:
        going.wait_send()
    work.finish()
    if last:
        for turn, hop in steps[1:]:
            for going, coming in give_back(turn, hop):
                coming.wait_recv()
                going.wait_send()
        for copy in own_back:
            copy.wait()


class Bag:
    def __init__(self, layout, refs):
        start = 0
        for name, size in layout.items():
            setattr(self, name, refs[start : start + size])
            start += size


class Wanted:
    def groups(self):
        return list(self.__dict__.values())

    def layout(self):
        return {name: len(group) for name, group in self.__dict__.items()}


def run_expert(index, local, rows_in, gates, cotangent, cotangent_late, ups, downs, swapped, next_mine,
               moved, outs_before, collective_id):
    grid = Grid()
    half = len(ups)
    shards = 2 * half
    last = index == local - 1
    blocks, capacity, model_width = rows_in.shape
    part = downs[0].shape[0]
    count = blocks * capacity
    inputs, outputs, scratch = Wanted(), Wanted(), Wanted()
    inputs.cot_in = [(cotangent, ANYWHERE)]
    inputs.cot_late = [(array, ANYWHERE) for array in cotangent_late]
    inputs.rows_in = [(rows_in, ANYWHERE)]
    inputs.gates = [(gates, IN_VMEM)]
    inputs.my_up = [(array, ANYWHERE) for array in ups]
    inputs.my_down = [(array, ANYWHERE) for array in downs]
    inputs.swapped_up = [(array, ANYWHERE) for array in swapped[0]]
    inputs.swapped_down = [(array, ANYWHERE) for array in swapped[1]]
    inputs.next_mine = [(array, ANYWHERE) for array in next_mine]
    inputs.moved_from = [(array, ANYWHERE) for array, _ in moved]
    inputs.outs_before = [] if outs_before is None else [(outs_before, IN_VMEM)]

    up_shape, down_shape = (model_width, part), (part, model_width)
    outputs.rows_out = [(shape_of((blocks, index + 1, capacity, model_width), BF16), ANYWHERE)]
    own_up, own_down = shape_of(up_shape, BF16), shape_of(down_shape, BF16)
    outputs.own = [(own_up, ANYWHERE), (own_up, ANYWHERE), (own_down, ANYWHERE), (own_down, ANYWHERE)]
    outputs.pass_up = [(shape_of((half - 1,) + up_shape, BF16), ANYWHERE)] if half > 1 else []
    early_rows = part // 2 if last else 0
    late_down = (half - 1, part - early_rows, model_width)
    early_down = (half - 1, early_rows, model_width)
    outputs.pass_down = [(shape_of(late_down, BF16), ANYWHERE)] if half > 1 else []
    outputs.early_down = [(shape_of(early_down, BF16), ANYWHERE)] if half > 1 and last else []
    outputs.next_swapped = [(shape_of(array.shape, BF16), ANYWHERE) for array in next_mine]
    outputs.moved_to = [
        (
            shape_of((grid.exp_size,) + array.shape[(1 if place is None else 2) :], array.dtype),
            ANYWHERE,
        )
        for array, place in moved
    ]
    rows_shape, gate_shape = (blocks, capacity, model_width), (blocks, 8, capacity)
    if last:
        outputs.back_rows = [(shape_of(rows_shape, BF16), ANYWHERE)]
        outputs.back_gates = [(shape_of(gate_shape, F32), ANYWHERE)]
    else:
        outputs.grad_rows = [(shape_of(rows_shape, BF16), IN_VMEM)]
        outputs.grad_gates = [(shape_of(gate_shape, F32), IN_VMEM)]

    sems = lambda *shape: pltpu.SemaphoreType.DMA(shape)
    scratch.rows_all = [pltpu.VMEM(rows_shape, BF16)]
    scratch.cot = [pltpu.VMEM(rows_shape, BF16)]
    scratch.up_all = [pltpu.VMEM((shards,) + up_shape, BF16)]
    scratch.down_all = [pltpu.VMEM((shards,) + down_shape, BF16)]
    scratch.total = [pltpu.VMEM((count, model_width), F32)]
    if last:
        scratch.active = [pltpu.VMEM((shards, count, part), BF16)]
        scratch.grad_hidden = [pltpu.VMEM((shards, count, part), BF16)]
        scratch.unscaled = [pltpu.VMEM((shards, count, part), BF16)]
    else:
        scratch.grad_total = [pltpu.VMEM((count, model_width), F32)]
        scratch.slot_grad = [pltpu.VMEM((count, model_width), BF16)]
    if last:
        scratch.grad_rows = [pltpu.VMEM(rows_shape, BF16)]
        scratch.grad_gates = [pltpu.VMEM(gate_shape, F32)]
        scratch.back_send = [sems(2, grid.z_size, grid.y_size)]
        scratch.back_receive = [sems(2, grid.z_size, grid.y_size)]
    scratch.gate_column = [pltpu.VMEM((count, 1), F32)]
    scratch.rows_t = [pltpu.VMEM((model_width, count), BF16)]
    scratch.slot_t = [pltpu.VMEM((model_width, count), BF16)]
    scratch.grad_up = [pltpu.VMEM((2,) + up_shape, BF16)]
    scratch.grad_down = [pltpu.VMEM((2,) + down_shape, BF16)]
    far_up = [pltpu.VMEM((half - 1,) + up_shape, BF16)] * (1 if half > 1 else 0)
    far_down = [pltpu.VMEM((half - 1,) + down_shape, BF16)] * (1 if half > 1 else 0)
    scratch.far_keep_up, scratch.far_taken_up = far_up, far_up
    scratch.far_keep_down, scratch.far_taken_down = far_down, far_down
    scratch.load_sem = [sems(5)]
    scratch.pass_sem = [sems(3)]
    scratch.fetch_sem = [sems(2 * shards, shards)]
    scratch.store_sem = [sems(2, half + 1)]
    scratch.store_there = [sems(2, half + 1)]
    scratch.stored_here = [sems(shards, half + 1)]
    copies = len(moved) * grid.exp_size + half * (shards + 2) + len(next_mine)
    scratch.send = [sems(copies)]
    scratch.receive = [sems(copies)]
    scratch.own_sem = [sems(max(len(moved), 1))]

    layout = {**inputs.layout(), **outputs.layout(), **scratch.layout()}

    def body(*refs):
        expert_kernel(
            *refs, layout=layout, index=index, local=local, half=half, capacity=capacity,
            parts=[place for _, place in moved],
        )

    results = pl.pallas_call(
        body,
        in_specs=[spec for group in inputs.groups() for _, spec in group],
        out_specs=tuple(spec for group in outputs.groups() for _, spec in group),
        out_shape=tuple(shape for group in outputs.groups() for shape, _ in group),
        scratch_shapes=[item for group in scratch.groups() for item in group],
        compiler_params=params(collective_id=collective_id, has_side_effects=True),
        cost_estimate=hint(45),
        name=f"expert_{index}",
    )(*[array for group in inputs.groups() for array, _ in group])
    return Bag(outputs.layout(), results)


def local_picks(routes, slots, capacity, local, index, slot_count):
    member, which = lax.div(routes, local), lax.rem(routes, local)
    places = jnp.where(which == index, member * capacity + slots, -1)
    lane = lax.broadcasted_iota(jnp.int32, (routes.shape[0], slot_count), 1)
    return [lane == places[:, k : k + 1] for k in range(2)]


def unroute_kernel(
    hidden, cotangent, routed, probabilities, gates, plane, columns, counts, attention_out, context,
    *refs, experts, local, token_total, lanes, heads, width,
):
    grads, gate_grads = refs[:local], refs[local : 2 * local]
    (
        grad_hidden, small, grad_t, grad_n, grad_out, branches, own_out, total, send, receive, own_sem,
    ) = refs[2 * local :]
    grid = Grid().here()
    links = Links(send, receive)
    rows, model_width = hidden.shape
    members, capacity = grads[0].shape[0], grads[0].shape[1]
    head_rows = heads * width
    fetch = pltpu.make_async_copy(
        attention_out.at[pl.ds(pl.multiple_of(grid.fsdp * head_rows, 16), head_rows), :], own_out,
        own_sem.at[0],
    )
    fetch.start()
    greet(chip_peers(grid))
    extra = plane[:, lanes.base :]
    gains = extra.astype(F32).T[lanes.gain : lanes.gain + 1]
    half_rows = rows // 2
    sibling = grid.sibling(grid.fsdp)
    small_t = jnp.zeros((lanes.extra, model_width), F32)
    gain_grad = jnp.zeros((1, model_width), F32)
    along_x, across = [], []
    for half in range(2):
        here = slice(half * half_rows, (half + 1) * half_rows)
        grad_output = cotangent[here, :].astype(F32)
        routes = columns[here, 0:2].astype(jnp.int32)
        slots = columns[here, 2:4].astype(jnp.int32)
        member, which = lax.div(routes, local), lax.rem(routes, local)
        lane = lax.broadcasted_iota(jnp.int32, (half_rows, capacity), 1)
        grad_routed = jnp.zeros((half_rows, model_width), F32)
        found = [jnp.zeros((half_rows, capacity), F32), jnp.zeros((half_rows, capacity), F32)]
        for index in range(local):
            picks = local_picks(routes, slots, capacity, local, index, members * capacity)
            grad_routed = grad_routed + matmul(
                jnp.where(picks[0] | picks[1], 1.0, 0.0).astype(BF16),
                grads[index][...].reshape(members * capacity, model_width),
            )
            for place in range(members):
                spots = jnp.where((which == index) & (member == place), slots, -1)
                for k in range(2):
                    found[k] = found[k] + jnp.where(
                        lane == spots[:, k : k + 1], gate_grads[index][place, 0:1, :], 0.0
                    )
        grad_gates = [jnp.sum(found[k], axis=1, keepdims=True) for k in range(2)]
        powers = probabilities[here, :]
        lane = expert_lane(powers.shape, lanes)
        inside = (lane >= 0) & (lane < experts)
        picked = [lane == routes[:, k : k + 1] for k in range(2)]
        chosen_total = sum(
            jnp.sum(jnp.where(picked[k], powers, 0.0), axis=1, keepdims=True) for k in range(2)
        )
        weighted = grad_gates[0] * gates[here, 0:1] + grad_gates[1] * gates[here, 1:2]
        grad_mass = (AUX_WEIGHT * experts / (2.0 * token_total * token_total)) * counts[0:1, :]
        grad_mass = jnp.where(inside, grad_mass, 0.0)
        for k in range(2):
            grad_mass = grad_mass + jnp.where(
                picked[k], (grad_gates[k] - weighted) / chosen_total, 0.0
            )
        grad_logits = powers * (grad_mass - jnp.sum(powers * grad_mass, axis=1, keepdims=True))
        grad_routed = grad_routed + contract_last(grad_logits.astype(BF16), extra)
        hidden_state = hidden[here, :]
        scale = lax.rsqrt(jnp.mean(hidden_state * hidden_state, axis=1, keepdims=True) + EPSILON)
        normed = hidden_state * scale
        product = grad_routed * normed
        grad = scale * (
            grad_routed * gains - normed * jnp.mean(product * gains, axis=1, keepdims=True)
        ) + grad_output
        grad_hidden[here, :] = grad
        branches[grid.fsdp, here, :] = grad.astype(BF16)
        mine = branches.at[grid.fsdp, here, :]
        for hop in range(1, grid.x_size):
            along_x.append(
                links.copy(
                    mine, mine, (grid.exp, grid.x_from(hop)),
                    branches.at[grid.x_from(-hop), here, :],
                )
            )
            along_x[-1][0].start()
        across.append(
            links.copy(mine, mine, (grid.exp, sibling), branches.at[sibling, here, :])
        )
        across[-1][0].start()
        gain_grad = gain_grad + jnp.sum(product, axis=0, keepdims=True)
        small_t = small_t + matmul(grad_logits.T.astype(BF16), routed[here, :])

    def context_grad(place):
        branch = branches[place]
        grad = contract_last(own_out[...], branch).astype(BF16)
        columns_here = pl.ds(pl.multiple_of(place * rows, 128), rows)
        rows_here = pl.ds(pl.multiple_of(place * rows, 16), rows)
        for head in range(heads):
            piece = grad[head * width : (head + 1) * width]
            grad_t[head, :, columns_here] = piece
            grad_n[head, rows_here, :] = turned(piece).astype(BF16)
        total[...] += matmul(context[place], branch)

    total[...] = jnp.zeros_like(total)
    fetch.wait()
    context_grad(grid.fsdp)
    forwards = []
    for half in range(2):
        here = slice(half * half_rows, (half + 1) * half_rows)
        for hop in range(1, grid.x_size):
            along_x[half * (grid.x_size - 1) + hop - 1][1].wait_recv()
            held = grid.x_from(-hop)
            forwards.append(
                links.copy(
                    branches.at[held, here, :], branches.at[held, here, :], (grid.exp, sibling),
                    branches.at[grid.sibling(held), here, :],
                )
            )
            forwards[-1][0].start()
    row = lax.broadcasted_iota(jnp.int32, small_t.shape, 0)
    small[...] = jnp.where(row == lanes.gain, gain_grad, small_t).T
    for _, coming in across:
        coming.wait_recv()
    context_grad(sibling)
    for hop in range(1, grid.x_size):
        context_grad(grid.x_from(-hop))
    for _, coming in forwards:
        coming.wait_recv()
    for hop in range(1, grid.x_size):
        context_grad(grid.sibling(grid.x_from(-hop)))
    grad_out[...] = total[...].astype(BF16)
    for going, _ in along_x + across + forwards:
        going.wait_send()


def project_back_kernel(
    grad_projected, normed, plane, small, probabilities, grad_bias, grad_first, grad_plane, total,
    bias_t, *, lanes, heads, feature_rows, bucket_rows,
):
    step = pl.program_id(0)

    @pl.when(step == 0)
    def _():
        total[...] = jnp.zeros_like(total)

    grad = grad_projected[...]
    grad_first[0] = matmul(plane[:, : lanes.weights], grad).astype(BF16)
    total[: lanes.weights, :] += matmul(grad, normed[...])

    @pl.when(step == pl.num_programs(0) - 1)
    def _():
        grad_plane[...] = total[...].T.astype(BF16)
        span = grad_bias.shape[2]
        select, _ = bucket_rows_select(plane.shape[0], feature_rows, bucket_rows, span)
        bias_t[...] = jnp.zeros_like(bias_t)
        first = lanes.table + lax.axis_index("fsdp") * heads
        for head in range(heads):
            bias_t[pl.ds(first + head, 1), :] = grad_bias[head]
        high = bias_t[...].astype(BF16)
        rest = (bias_t[...] - high.astype(F32)).astype(BF16)
        table = contract_last(select, high) + contract_last(select, rest)
        mass = jnp.sum(probabilities[...], axis=0, keepdims=True)
        mass = pltpu.roll(jnp.broadcast_to(mass, (8, lanes.extra)), lanes.shift, 1)[0:1]
        lane = lax.broadcasted_iota(jnp.int32, table.shape, 1)
        row = lax.broadcasted_iota(jnp.int32, table.shape, 0)
        is_small = (lane >= lanes.router) & (lane < lanes.table)
        is_mass = (lane >= lanes.count) & (lax.rem(row, feature_rows) == 0)
        extra = table + jnp.where(is_small, small[...], 0.0) + jnp.where(is_mass, mass, 0.0)
        grad_plane[:, lanes.base :] = (total[lanes.base :, :].T + extra).astype(BF16)


def last_kernel(
    first, planes, out_grad, hidden, gates, columns, rows_back, first_parts, output, plane_parts,
    out_parts, first_in, first_sum, planes_in, plane_sum, along_in, reduced, rows_held, send, receive,
    own, *, spread_out, local,
):
    fetch = pltpu.make_async_copy(rows_back, rows_held, own.at[2])
    fetch.start()
    grid = Grid().here()
    links = Links(send, receive)
    z_size, y_size, x_size, fsdp_size = grid.z_size, grid.y_size, grid.x_size, grid.fsdp_size
    exp_size = grid.exp_size
    sibling = grid.sibling(grid.fsdp)
    near = [
        (grid.exp, (grid.fsdp + turn) % fsdp_size) for turn in range(1, fsdp_size)
    ] + [grid.at(z=(grid.z + hop) % z_size) for hop in range(1, z_size)]
    beside = [grid.at(y=(grid.y + hop) % y_size) for hop in range(1, y_size)]

    per_sender = grid.device_count if spread_out else exp_size
    base = 0 if spread_out else grid.fsdp * exp_size
    out_sends = []
    for number in range(per_sender):
        to = base + number
        out_sends.append((to, number))
    if spread_out:
        out_origins = [(origin, origin) for origin in range(grid.device_count)]
    else:
        out_origins = [
            (member * fsdp_size + grid.linear // exp_size, member) for member in range(exp_size)
        ]
    own_slot = grid.linear if spread_out else grid.exp
    out_base = links.used
    links.used += per_sender

    def place_of(linear):
        return (linear // fsdp_size, linear % fsdp_size)

    def out_copy(to, number, slot):
        return pltpu.make_async_remote_copy(
            src_ref=out_grad.at[number], dst_ref=out_parts.at[slot],
            send_sem=send.at[out_base + number], recv_sem=receive.at[out_base + slot],
            device_id=place_of(to), device_id_type=MESH,
        )

    barrier = pltpu.get_barrier_semaphore()
    for device in near + beside:
        pl.semaphore_signal(barrier, inc=1, device_id=device, device_id_type=MESH)
    for origin, _ in out_origins:

        @pl.when(origin != grid.linear)
        def _(origin=origin):
            pl.semaphore_signal(
                barrier, inc=1, device_id=place_of(origin), device_id_type=MESH
            )

    to_self = (
        1 if spread_out else jnp.where(grid.linear // exp_size == grid.fsdp, 1, 0)
    )
    pl.semaphore_wait(barrier, len(near) + len(beside) + per_sender - to_self)

    first_copies = []
    for hop in range(x_size):
        mine = grid.x_from(hop)
        first_copies.append(
            links.copy(
                first.at[grid.sibling(mine)], first_in.at[hop], (grid.exp, sibling), first_in.at[hop]
            )
        )
        first_copies[-1][0].start()
    z_hops = list(range(1, z_size)) + [0]
    beside_copies = []
    for z_hop in z_hops:
        beside_copies.append([])
        for hop in range(1, y_size):
            to = (grid.y + hop) % y_size
            landing = planes_in.at[hop - 1, z_hop]
            beside_copies[-1].append(
                links.copy(
                    planes.at[(grid.z + z_hop) % z_size, to], landing, grid.at(y=to), landing
                )
            )
            beside_copies[-1][-1][0].start()
    along_x = []
    for hop in range(x_size):
        first_copies[hop][1].wait_recv()
        summed = first[grid.x_from(hop)].astype(F32) + first_in[hop].astype(F32)
        if hop == 0:
            first_parts[0] = summed.astype(BF16)
        else:
            first_sum[hop - 1] = summed.astype(BF16)
            along_x.append(
                links.copy(
                    first_sum.at[hop - 1], first_parts.at[hop], (grid.exp, grid.x_from(hop)),
                    first_parts.at[hop],
                )
            )
            along_x[-1][0].start()
    along_z = []
    for z_hop, copies in zip(z_hops, beside_copies):
        to_z = (grid.z + z_hop) % z_size
        summed = planes[to_z, grid.y].astype(F32)
        for number, (_, coming) in enumerate(copies):
            coming.wait_recv()
            summed = summed + planes_in[number, z_hop].astype(F32)
        plane_sum[z_hop] = summed.astype(BF16)
        if z_hop > 0:
            along_z.append(
                links.copy(
                    plane_sum.at[z_hop], along_in.at[z_hop - 1], grid.at(z=to_z),
                    along_in.at[z_hop - 1],
                )
            )
            along_z[-1][0].start()
    for to, number in out_sends:

        @pl.when(to != grid.linear)
        def _(to=to, number=number):
            out_copy(to, number, own_slot).start()

        @pl.when(to == grid.linear)
        def _(number=number):
            pltpu.make_async_copy(out_grad.at[number], out_parts.at[own_slot], own.at[0]).start()

    fetch.wait()
    mix_rows(hidden, gates, columns, rows_held, output, local)
    summed = plane_sum[0].astype(F32)
    for number, (_, coming) in enumerate(along_z):
        coming.wait_recv()
        summed = summed + along_in[number].astype(F32)
    reduced[...] = summed.astype(BF16)
    placed = []
    for turn in range(1, fsdp_size):
        to = (grid.fsdp + turn) % fsdp_size
        origin = (grid.fsdp + fsdp_size - turn) % fsdp_size
        placed.append(
            links.copy(
                reduced.at[to], plane_parts.at[grid.fsdp], (grid.exp, to), plane_parts.at[origin]
            )
        )
        placed[-1][0].start()
    kept = pltpu.make_async_copy(reduced.at[grid.fsdp], plane_parts.at[grid.fsdp], own.at[1])
    kept.start()
    for going, coming in along_x + placed:
        coming.wait_recv()
    for going, _ in first_copies + along_x + along_z + placed:
        going.wait_send()
    for copies in beside_copies:
        for going, _ in copies:
            going.wait_send()
    kept.wait()
    for origin, slot in out_origins:

        @pl.when(origin != grid.linear)
        def _(origin=origin, slot=slot):
            out_copy(origin, 0, slot).wait_recv()

    for to, number in out_sends:

        @pl.when(to != grid.linear)
        def _(to=to, number=number):
            out_copy(to, number, own_slot).wait_send()

        @pl.when(to == grid.linear)
        def _(number=number):
            pltpu.make_async_copy(out_grad.at[number], out_parts.at[own_slot], own.at[0]).wait()


def mix_rows(hidden, gates, columns, rows_in, output, local):
    members, _, capacity, model_width = rows_in.shape
    routes, slots = int_columns(columns)
    total = hidden[...]
    picked = [jnp.zeros(hidden.shape, F32), jnp.zeros(hidden.shape, F32)]
    for index in range(local):
        picks = local_picks(routes, slots, capacity, local, index, members * capacity)
        values = rows_in[:, index].reshape(members * capacity, model_width)
        for k in range(2):
            picked[k] = picked[k] + matmul(jnp.where(picks[k], 1.0, 0.0).astype(BF16), values)
    for k in range(2):
        total = total + gates[:, k : k + 1] * picked[k]
    output[...] = total.astype(BF16)


def finish_kernel(
    first_parts, plane_parts, out_parts, tokens, grad_hidden, attention_in, attention_gain, counts,
    grad_tokens, grad_gain, grad_in, grad_out, grad_mixture, grad_router, grad_table, balance,
    *, lanes, heads, width, head_count, experts, token_total,
):
    total = jnp.sum(first_parts[...].astype(F32), axis=0).T
    inputs = tokens[...].astype(F32)
    scale = lax.rsqrt(jnp.mean(inputs * inputs, axis=1, keepdims=True) + EPSILON)
    normed = inputs * scale
    grad_tokens[...] = grad_hidden[...] + scale * (
        total - normed * jnp.mean(total * normed, axis=1, keepdims=True)
    )
    fsdp_size = plane_parts.shape[0]
    model_width = head_count * width
    sums = [plane_parts[place].astype(F32) for place in range(fsdp_size)]
    columns = []
    for kind in range(3):
        pieces = [
            sums[place][:, kind * heads * width : (kind + 1) * heads * width]
            for place in range(fsdp_size)
        ]
        columns.append(jnp.concatenate(pieces, axis=1)[:, :model_width])
    gathered = jnp.concatenate(columns, axis=1)
    feature_rows = gathered.shape[0]
    gain = jnp.sum(gathered * attention_in[...].astype(F32), axis=1, keepdims=True)
    gain = padded_rows(jnp.broadcast_to(gain, (feature_rows, 128)), 128).T
    grad_gain[...] = gain[0:1, :feature_rows]
    grad_in[...] = gathered * as_column(attention_gain[...], feature_rows)
    grad_out[...] = jnp.sum(out_parts[...].astype(F32), axis=0)
    extra = sum(part[:, lanes.base :] for part in sums)
    extra_t = padded_rows(extra, 128).T
    grad_mixture[...] = extra_t[lanes.gain : lanes.gain + 1, :feature_rows]
    grad_router[...] = extra_t[lanes.router : lanes.router + experts, :feature_rows]
    grad_table[...] = extra[: grad_table.shape[0], lanes.table : lanes.table + head_count]
    mass = jnp.broadcast_to(extra[0:1], (8, lanes.extra))
    mass = pltpu.roll(mass, lanes.extra - lanes.shift, 1)
    lane = expert_lane(mass.shape, lanes)
    terms = jnp.where((lane >= 0) & (lane < experts), mass * counts[...], 0.0)[0:1]
    balance[...] = jnp.sum(terms, axis=1, keepdims=True) * (
        experts / (2.0 * token_total * token_total)
    )


def sum_kernel(*refs, layout, local):
    outputs = refs[len(layout) :]
    early_blocks = pl.num_programs(0) // 2
    totals = {}
    number = 0
    while number < len(layout):
        index, which, halves = layout[number]
        shape = outputs[which].shape[1:]
        value = refs[number][...].reshape(shape).astype(F32)
        if halves:
            rest = refs[number + 1][...].reshape(shape).astype(F32)
            value = jnp.where(pl.program_id(0) < early_blocks, value, rest)
            number += 1
        totals[index, which] = totals[index, which] + value if (index, which) in totals else value
        number += 1
    for (index, which), total in totals.items():
        outputs[which][index] = total


def sum_grads(groups, up_shape, down_shape, blocks):
    local = len(groups)
    depth, part = up_shape[1], down_shape[1]
    sizes = ((depth, part), (part // blocks, down_shape[2]))
    arrays, specs, layout = [], [], []
    early = blocks // 2
    for index, group in enumerate(groups):
        for which, (size, (keep, taken, passed)) in enumerate(zip(sizes, group)):
            for array in (keep, taken, *passed):
                if isinstance(array, tuple):
                    arrays.extend(array)
                    specs.append(pl.BlockSpec(size, lambda c: (jnp.minimum(c, early - 1), 0)))
                    specs.append(pl.BlockSpec(size, lambda c: (jnp.maximum(c - early, 0), 0)))
                    layout.extend([(index, which, True)] * 2)
                else:
                    arrays.append(array)
                    specs.append(pl.BlockSpec(size, lambda c: (c, 0)))
                    layout.append((index, which, False))
    return pl.pallas_call(
        partial(sum_kernel, layout=layout, local=local),
        grid=(blocks,),
        in_specs=specs,
        out_specs=[
            pl.BlockSpec((local, depth, part), lambda c: (0, 0, c)),
            pl.BlockSpec((local, part // blocks, down_shape[2]), lambda c: (0, c, 0)),
        ],
        out_shape=(shape_of(up_shape, F32), shape_of(down_shape, F32)),
        compiler_params=params(),
        cost_estimate=hint(8),
        name="sum_grads",
    )(*arrays)


def over_x(array, hop):
    fsdp_size = lax.axis_size("fsdp")
    return lax.ppermute(array, "fsdp", [(i, (i + 2 * hop) % fsdp_size) for i in range(fsdp_size)])


def over_core(array):
    return lax.ppermute(array, "fsdp", [(i, i ^ 1) for i in range(lax.axis_size("fsdp"))])


def on_device(
    tokens,
    cotangent,
    segments,
    routes,
    slots,
    attention_gain,
    mixture_gain,
    attention_in,
    attention_out,
    router_weight,
    position_table,
    expert_up,
    expert_down,
):
    grid = Grid()
    exp_size, fsdp_size, chips = grid.exp_size, grid.fsdp_size, grid.x_size
    device_count = grid.device_count
    fsdp_index = lax.axis_index("fsdp")
    rows, model_width = tokens.shape
    length = rows * fsdp_size
    head_count = position_table.shape[1]
    width = model_width // head_count
    heads = -(-head_count // fsdp_size)
    padded_heads = heads * fsdp_size
    feature_rows, bucket_rows = attention_in.shape[0], position_table.shape[0]
    experts = router_weight.shape[1]
    local = expert_up.shape[0]
    capacity = 4 * rows // experts
    token_total = rows * device_count
    span = WINDOW + 2 * SKEW + QUERY_BLOCK
    lanes = Lanes(heads, width, padded_heads, experts)
    part = expert_down.shape[1]
    gain_row = attention_gain.reshape(1, feature_rows)
    late_rows = 2 * capacity // 3 if local > 1 and capacity % 48 == 0 else 0
    late = 1 if late_rows else 0

    shard_shapes = [shape_of((model_width, part), BF16), shape_of((part, model_width), BF16)]
    copies = (
        4 * fsdp_size + grid.z_size + grid.z_size * grid.y_size
        + grid.z_size + grid.y_size + grid.x_size + 1
    )
    started = pl.pallas_call(
        partial(
            start_kernel, lanes=lanes, heads=heads, width=width, head_count=head_count,
            experts=experts, capacity=capacity, local=local, late=late,
        ),
        out_shape=tuple(
            [
                shape_of((fsdp_size, rows, model_width), BF16),
                shape_of((grid.z_size, grid.y_size, fsdp_size, feature_rows, lanes.width), BF16),
                shape_of((exp_size, local * capacity - late_rows, model_width), BF16),
                shape_of((8, rows), F32),
                shape_of((rows, 128), F32),
                shape_of((grid.z_size, grid.y_size, chips, 2, feature_rows, model_width), BF16),
            ]
            + [shape_of((exp_size, late_rows, model_width), BF16)] * late
            + shard_shapes * local
        ),
        in_specs=[IN_VMEM] * 10 + [ANYWHERE] * 2,
        out_specs=tuple(
            [ANYWHERE, ANYWHERE, IN_VMEM, IN_VMEM, IN_VMEM, ANYWHERE]
            + [IN_VMEM] * late
            + [ANYWHERE] * (2 * local)
        ),
        scratch_shapes=[
            pltpu.VMEM((fsdp_size, feature_rows, lanes.width), BF16),
            pltpu.VMEM(expert_up.shape, BF16),
            pltpu.VMEM(expert_down.shape, BF16),
            dma_sems(copies),
            dma_sems(copies),
            dma_sems(3),
            dma_sems(2 * local),
            dma_sems(local * (fsdp_size + 1)),
        ],
        compiler_params=params(collective_id=0, has_side_effects=True),
        cost_estimate=hint(20),
        name="start",
    )(
        tokens, cotangent, routes.T, slots.T, gain_row, mixture_gain.reshape(1, feature_rows),
        attention_in, router_weight.T, position_table, attention_out, expert_up, expert_down,
    )
    all_tokens, all_planes, cotangent_early, position_rows, columns, full_out = started[:6]
    cotangent_late, started = started[6 : 6 + late], started[6 + late :]
    own_shards = [started[2 * index : 2 * index + 2] for index in range(local)]
    plane = all_planes.reshape(model_width, lanes.width)
    full_out = full_out.reshape(model_width, model_width)

    def along_x(array):
        return [over_x(array, -hop) for hop in range(1, chips)]

    near_up, near_down = [None] * local, [None] * local
    near_up[0] = along_x(own_shards[0][0])
    cotangent_in = lax.all_to_all(
        cotangent_early, "exp", split_axis=0, concat_axis=0, tiled=True
    )

    head_t = lambda size: pl.BlockSpec((heads, size, rows), lambda s, *_: (0, 0, s))
    head_n = lambda size: pl.BlockSpec((heads, rows, size), lambda s, *_: (0, s, 0))
    normed, query_t, key_n, query_n, value_n, key_t, value_t, bias, counts = pl.pallas_call(
        partial(
            project_kernel, heads=heads, width=width, lanes=lanes, feature_rows=feature_rows,
            bucket_rows=bucket_rows,
        ),
        grid=(fsdp_size,),
        in_specs=[
            pl.BlockSpec((1, rows, model_width), lambda s: (s, 0, 0)),
            whole((model_width, lanes.width)),
            pl.BlockSpec((1, rows), lambda s: (0, s)),
        ],
        out_specs=[
            pl.BlockSpec((rows, model_width), lambda s: (s, 0)),
            head_t(SKEW), head_n(SKEW), head_n(width), head_n(width), head_t(width), head_t(width),
            whole((heads, 1, span)),
            whole((8, lanes.extra)),
        ],
        out_shape=(
            shape_of((length, model_width), BF16),
            shape_of((heads, SKEW, length), BF16),
            shape_of((heads, length, SKEW), BF16),
            shape_of((heads, length, width), BF16),
            shape_of((heads, length, width), BF16),
            shape_of((heads, width, length), BF16),
            shape_of((heads, width, length), BF16),
            shape_of((heads, 1, span), F32),
            shape_of((8, lanes.extra), F32),
        ),
        scratch_shapes=[
            pltpu.VMEM((lanes.weights, model_width), BF16),
            pltpu.VMEM((lanes.extra, span), F32),
        ],
        compiler_params=params(),
        cost_estimate=hint(8),
        name="project",
    )(all_tokens, plane, segments.reshape(1, length))

    by_head = lambda *size: pl.BlockSpec((1,) + size, lambda h: (h, 0, 0))
    context, context_high, log_total, attended_t = pl.pallas_call(
        partial(attend_kernel, rows=rows),
        grid=(heads,),
        in_specs=[
            by_head(SKEW, length), by_head(length, SKEW), by_head(width, length), by_head(1, span),
        ],
        out_specs=[
            pl.BlockSpec((fsdp_size, width, rows), lambda h: (0, h, 0)),
            by_head(width, length),
            by_head(1, length),
            ANYWHERE,
        ],
        out_shape=(
            shape_of((fsdp_size, heads * width, rows), BF16),
            shape_of((heads, width, length), F32),
            shape_of((heads, 1, length), F32),
            shape_of((fsdp_size, heads * width, rows), BF16),
        ),
        scratch_shapes=[
            pltpu.VMEM((SKEW, span), F32),
            pltpu.VMEM((WINDOW + QUERY_BLOCK, QUERY_BLOCK), F32),
            pltpu.VMEM((heads, fsdp_size, width, rows), BF16),
            pltpu.SemaphoreType.DMA((heads, fsdp_size)),
            pltpu.SemaphoreType.DMA((heads, fsdp_size)),
            dma_sems(heads),
        ],
        compiler_params=params(collective_id=1, has_side_effects=True),
        cost_estimate=hint(13),
        name="attend",
    )(query_t, key_n, value_t, bias)

    own_down, near_up[0], attended_t = lax.optimization_barrier(
        (own_shards[0][1], near_up[0], attended_t)
    )
    near_down[0] = along_x(own_down)
    attended_t = attended_t.reshape(padded_heads * width, rows)

    later = [own_shards[index] for index in range(1, local)]
    attended_t, later = lax.optimization_barrier((attended_t, later))
    for index in range(1, local):
        near_up[index], near_down[index] = [along_x(array) for array in later[index - 1]]
    gate_lanes = -(-local * capacity // 128) * 128
    ready = [own_shards[0][0]] + near_up[0] + [own_shards[0][1]]
    copies = 2 * exp_size + len(ready)
    hidden, routed, probabilities, gates, outgoing, rows_in, gates_in, *crossed = pl.pallas_call(
        partial(
            route_kernel, experts=experts, lanes=lanes, capacity=capacity, crossing=len(ready)
        ),
        in_specs=[IN_VMEM] * 6 + [ANYWHERE] * len(ready),
        out_specs=tuple([IN_VMEM] * 5 + [ANYWHERE] * (2 + len(ready))),
        out_shape=tuple(
            [
                shape_of((rows, model_width), F32),
                shape_of((rows, model_width), BF16),
                shape_of((rows, lanes.extra), F32),
                shape_of((rows, 2), F32),
                shape_of((exp_size, local * capacity, model_width), BF16),
                shape_of((exp_size, capacity, model_width), BF16),
                shape_of((exp_size, 8, gate_lanes), F32),
            ]
            + [shape_of(array.shape, BF16) for array in ready]
        ),
        scratch_shapes=[
            pltpu.VMEM((exp_size, 8, gate_lanes), F32),
            dma_sems(copies),
            dma_sems(copies),
            dma_sems(2),
        ],
        compiler_params=params(collective_id=2, has_side_effects=True),
        cost_estimate=hint(35),
        name="route",
    )(tokens, attended_t, full_out, plane, columns, position_rows, *ready)
    outgoing = outgoing.reshape(exp_size, local, capacity, model_width)

    def down_parts(early, rest):
        return list(zip(early, rest))

    def pass_along(arrays):
        return [over_x(arrays[0][hop - 1], hop) for hop in range(1, chips)]

    swapped = (crossed[:-1], crossed[-1:])
    returned, groups, moved, outs = [], [], [], None
    late_rows_in = ()
    for index in range(local):
        final = index == local - 1
        carried = list(moved)
        if not final:
            carried.append((outgoing, index + 1))
        if index == 0 and late:
            carried.append((cotangent_late[0], None))
        result = run_expert(
            index, local, rows_in, gates_in, cotangent_in, late_rows_in if final else (),
            [own_shards[index][0]] + near_up[index], [own_shards[index][1]] + near_down[index],
            swapped, () if final else own_shards[index + 1], carried, outs, 3 + index,
        )
        (outs,) = result.rows_out
        arrived = list(result.moved_to)
        if index == 0 and late:
            late_rows_in = (arrived.pop(),)
        if not final:
            rows_in = arrived.pop()
            swapped = (result.next_swapped[:1], result.next_swapped[1:])
            moved = [(result.grad_rows[0], None), (result.grad_gates[0], None)]
        if arrived:
            returned.append(arrived)
        up_keep, up_taken, down_keep, down_taken = result.own
        if not final:
            passed = (result.pass_up, result.pass_down)
            passed, rows_in = lax.optimization_barrier((passed, rows_in))
            groups.append(
                [
                    (up_keep, up_taken, pass_along(passed[0])),
                    (down_keep, down_taken, pass_along(passed[1])),
                ]
            )
    returned.append([result.back_rows[0], result.back_gates[0]])
    groups, returned = lax.optimization_barrier((groups, returned))

    outs, returned = lax.optimization_barrier((outs, returned))
    out_rows = lax.all_to_all(outs, "exp", split_axis=0, concat_axis=0, tiled=True)

    padded_out = full_out
    if padded_heads > head_count:
        padded_out = jnp.pad(full_out, ((0, padded_heads * width - model_width), (0, 0)))
    copies = 2 * 2 * fsdp_size
    grad_hidden, small, grad_t, grad_n, out_grad = pl.pallas_call(
        partial(
            unroute_kernel, experts=experts, local=local, token_total=token_total, lanes=lanes,
            heads=heads, width=width,
        ),
        out_shape=(
            shape_of((rows, model_width), F32),
            shape_of((model_width, lanes.extra), F32),
            shape_of((heads, width, length), BF16),
            shape_of((heads, length, width), BF16),
            shape_of((heads * width, model_width), BF16),
        ),
        in_specs=[IN_VMEM] * 8 + [ANYWHERE] + [IN_VMEM] * (1 + 2 * local),
        out_specs=tuple([IN_VMEM] * 5),
        scratch_shapes=[
            pltpu.VMEM((fsdp_size, rows, model_width), BF16),
            pltpu.VMEM((heads * width, model_width), BF16),
            pltpu.VMEM((heads * width, model_width), F32),
            dma_sems(copies),
            dma_sems(copies),
            dma_sems(1),
        ],
        compiler_params=params(collective_id=4 + local, has_side_effects=True),
        cost_estimate=hint(1),
        name="unroute",
    )(
        hidden, cotangent, routed, probabilities, gates, plane, columns, counts, padded_out, context,
        *[part[0] for part in returned], *[part[1] for part in returned],
    )
    pass_up, pass_down, grad_t = lax.optimization_barrier(
        (result.pass_up, result.pass_down, grad_t)
    )
    early = [result.early_down[0][hop] for hop in range(chips - 1)]
    groups.append(
        [
            (up_keep, up_taken, pass_along(pass_up)),
            (down_keep, down_taken, down_parts(early, pass_along(pass_down))),
        ]
    )

    grad_projected, grad_bias = pl.pallas_call(
        partial(attend_back_kernel, scale=width ** (-0.5)),
        grid=(heads,),
        in_specs=[
            by_head(SKEW, length), by_head(length, SKEW), by_head(length, width),
            by_head(length, width), by_head(width, length), by_head(width, length),
            by_head(length, width), by_head(width, length), by_head(1, length), by_head(1, span),
        ],
        out_specs=[
            pl.BlockSpec((3, 1, width, length), lambda h: (0, h, 0, 0)),
            by_head(1, span),
        ],
        out_shape=(
            shape_of((3, heads, width, length), BF16),
            shape_of((heads, 1, span), F32),
        ),
        scratch_shapes=[
            pltpu.VMEM((SKEW, span), F32),
            pltpu.VMEM((SKEW, span), F32),
            pltpu.VMEM((length, width), F32),
            pltpu.VMEM((length, width), F32),
        ],
        compiler_params=params(),
        cost_estimate=hint(1),
        name="attend_back",
    )(query_t, key_n, query_n, value_n, key_t, grad_t, grad_n, context_high, log_total, bias)
    grad_projected = grad_projected.reshape(lanes.weights, length)

    grad_first, grad_plane = pl.pallas_call(
        partial(
            project_back_kernel, lanes=lanes, heads=heads, feature_rows=feature_rows,
            bucket_rows=bucket_rows,
        ),
        grid=(fsdp_size,),
        in_specs=[
            pl.BlockSpec((lanes.weights, rows), lambda s: (0, s)),
            pl.BlockSpec((rows, model_width), lambda s: (s, 0)),
            whole((model_width, lanes.width)),
            whole((model_width, lanes.extra)),
            whole((rows, lanes.extra)),
            whole((heads, 1, span)),
        ],
        out_specs=[
            pl.BlockSpec((1, model_width, rows), lambda s: (s, 0, 0)),
            whole((model_width, lanes.width)),
        ],
        out_shape=(
            shape_of((fsdp_size, model_width, rows), BF16),
            shape_of((model_width, lanes.width), BF16),
        ),
        scratch_shapes=[
            pltpu.VMEM((lanes.width, model_width), F32),
            pltpu.VMEM((lanes.extra, span), F32),
        ],
        compiler_params=params(),
        cost_estimate=hint(1),
        name="project_back",
    )(grad_projected, normed, plane, small, probabilities, grad_bias)

    out_rows, grad_first = lax.optimization_barrier((out_rows, grad_first))
    spread_out = heads * width * fsdp_size != model_width
    if spread_out:
        out_grad = lax.dynamic_update_slice(
            jnp.zeros((padded_heads * width, model_width), BF16), out_grad,
            (fsdp_index * heads * width, jnp.int32(0)),
        )[:model_width]
    out_grad = out_grad.reshape(-1, feature_rows, model_width)
    out_count = device_count if spread_out else exp_size
    plane_shape = (grid.z_size, grid.y_size, fsdp_size, feature_rows, lanes.width)
    parts_shape = (fsdp_size, feature_rows, lanes.width)
    copies = 4 * fsdp_size + grid.z_size * grid.y_size + grid.z_size + out_count
    first_parts, layer_output, plane_parts, out_parts = pl.pallas_call(
        partial(last_kernel, spread_out=spread_out, local=local),
        out_shape=(
            shape_of((chips, model_width, rows), BF16),
            shape_of((rows, model_width), BF16),
            shape_of(parts_shape, BF16),
            shape_of((out_count, feature_rows, model_width), BF16),
        ),
        in_specs=[IN_VMEM] * 6 + [ANYWHERE],
        out_specs=(IN_VMEM, IN_VMEM, ANYWHERE, ANYWHERE),
        scratch_shapes=[
            pltpu.VMEM((chips, model_width, rows), BF16),
            pltpu.VMEM((max(chips - 1, 1), model_width, rows), BF16),
            pltpu.VMEM((max(grid.y_size - 1, 1), grid.z_size) + parts_shape, BF16),
            pltpu.VMEM((grid.z_size,) + parts_shape, BF16),
            pltpu.VMEM((max(grid.z_size - 1, 1),) + parts_shape, BF16),
            pltpu.VMEM(parts_shape, BF16),
            pltpu.VMEM(out_rows.shape, BF16),
            dma_sems(copies),
            dma_sems(copies),
            dma_sems(3),
        ],
        compiler_params=params(collective_id=5 + local, has_side_effects=True),
        cost_estimate=hint(1),
        name="last",
    )(grad_first, grad_plane.reshape(plane_shape), out_grad, hidden, gates, columns, out_rows)

    groups, first_parts = lax.optimization_barrier((groups, first_parts))
    (
        grad_tokens, gain_grad, in_grad, out_sum, mixture_gain_grad, router_grad, table_grad, balance,
    ) = pl.pallas_call(
        partial(
            finish_kernel, lanes=lanes, heads=heads, width=width, head_count=head_count,
            experts=experts, token_total=token_total,
        ),
        out_shape=(
            shape_of((rows, model_width), F32),
            shape_of((1, feature_rows), F32),
            shape_of((feature_rows, 3 * model_width), F32),
            shape_of((feature_rows, model_width), F32),
            shape_of((1, feature_rows), F32),
            shape_of((experts, feature_rows), F32),
            shape_of((bucket_rows, head_count), F32),
            shape_of((1, 1), F32),
        ),
        compiler_params=params(),
        cost_estimate=hint(6),
        name="finish",
    )(first_parts, plane_parts, out_parts, tokens, grad_hidden, attention_in, gain_row, counts)

    up_grad, down_grad = sum_grads(groups, expert_up.shape, expert_down.shape, fsdp_size)
    return (
        layer_output,
        balance.reshape(()),
        grad_tokens,
        gain_grad.reshape(feature_rows),
        mixture_gain_grad.reshape(feature_rows),
        in_grad,
        out_sum,
        router_grad.T,
        table_grad,
        up_grad,
        down_grad,
    )


def solution(mesh):
    in_specs = (
        P(("exp", "fsdp"), None),
        P(("exp", "fsdp"), None),
        P("exp"),
        P(("exp", "fsdp"), None),
        P(("exp", "fsdp"), None),
        P(("exp", "fsdp")),
        P(("exp", "fsdp")),
        P(("exp", "fsdp"), None),
        P(("exp", "fsdp"), None),
        P(("exp", "fsdp"), None),
        P(("exp", "fsdp"), None),
        P("exp", "fsdp", None),
        P("exp", "fsdp", None),
    )
    out_specs = (
        P(("exp", "fsdp"), None),
        P(),
        P(("exp", "fsdp"), None),
        P(("exp", "fsdp")),
        P(("exp", "fsdp")),
        P(("exp", "fsdp"), None),
        P(("exp", "fsdp"), None),
        P(("exp", "fsdp"), None),
        P(("exp", "fsdp"), None),
        P("exp", "fsdp", None),
        P("exp", "fsdp", None),
    )
    return jax.shard_map(
        on_device, mesh=mesh, in_specs=in_specs, out_specs=out_specs, check_vma=False
    )
```

```python
from functools import partial

import jax
import jax.numpy as jnp
from jax import lax
from jax.experimental import pallas as pl
from jax.experimental.pallas import tpu as pltpu
from jax.sharding import PartitionSpec as P

WINDOW = 1024
BUCKETS = 256

EPSILON = 1e-06
AUX_WEIGHT = 0.01
MASKED = -1e30
QUERY_BLOCK = 256
SKEW = 128
VMEM_BYTES = 58 * 1024 * 1024
MESH = pl.DeviceIdType.MESH
F32 = jnp.float32
BF16 = jnp.bfloat16


def params(**kwargs):
    return pltpu.CompilerParams(vmem_limit_bytes=VMEM_BYTES, **kwargs)


def shape_of(shape, dtype):
    return jax.ShapeDtypeStruct(shape, dtype)


def whole(shape):
    return pl.BlockSpec(shape, lambda *_: (0,) * len(shape))


def contract_last(left_side, right_side):
    return lax.dot_general(
        left_side, right_side, (((1,), (1,)), ((), ())), preferred_element_type=F32
    )


def matmul(left_side, right_side):
    return jnp.dot(left_side, right_side, preferred_element_type=F32)


def turned(value):
    return value.astype(F32).T


def bucket_index(distance):
    near_count = BUCKETS // 2
    spread = max(WINDOW - near_count, 1)
    far_bucket = (
        near_count + jnp.maximum(distance - near_count, 0) * (BUCKETS - near_count) // spread
    )
    return jnp.where(distance < near_count, distance, far_bucket)

def hint(micros):
    return pl.CostEstimate(flops=int(micros * 1.0e9), bytes_accessed=1024, transcendentals=0)


def flipped(place, other, size):
    result, bit = 0, 1
    while bit < size:
        result = result + bit * ((place // bit + other // bit) % 2)
        bit *= 2
    return result


class Grid:
    def __init__(self):
        self.exp_size, self.fsdp_size = lax.axis_size("exp"), lax.axis_size("fsdp")
        self.device_count = self.exp_size * self.fsdp_size
        self.y_size = max(
            y for y in range(1, self.exp_size + 1) if self.exp_size % y == 0 and 2 * y * y <= self.exp_size
        ) if self.exp_size > 1 else 1
        self.z_size = self.exp_size // self.y_size
        self.x_size = self.fsdp_size // 2

    def here(self):
        self.exp, self.fsdp = lax.axis_index("exp"), lax.axis_index("fsdp")
        self.z, self.y = self.exp // self.y_size, self.exp % self.y_size
        self.x, self.core = self.fsdp // 2, self.fsdp % 2
        self.linear = self.exp * self.fsdp_size + self.fsdp
        return self

    def at(self, z=None, y=None, fsdp=None):
        z = self.z if z is None else z
        y = self.y if y is None else y
        return (z * self.y_size + y, self.fsdp if fsdp is None else fsdp)

    def x_from(self, hop):
        return ((self.x + self.x_size + hop) % self.x_size) * 2 + self.core

    def source_z(self, turn):
        if self.z_size & (self.z_size - 1) == 0:
            return flipped(self.z, turn, self.z_size)
        return (self.z + turn) % self.z_size

    def target_z(self, turn):
        if self.z_size & (self.z_size - 1) == 0:
            return flipped(self.z, turn, self.z_size)
        return (self.z + self.z_size - turn) % self.z_size

    def exp_steps(self):
        turns = sorted(range(self.z_size), key=lambda turn: -turn.bit_length())
        steps = []
        for turn in turns:
            for hop in range(self.y_size):
                if turn or hop:
                    to = self.target_z(turn) * self.y_size + (self.y + self.y_size - hop) % self.y_size
                    origin = self.source_z(turn) * self.y_size + (self.y + hop) % self.y_size
                    steps.append((to, origin))
        return steps

    def sibling(self, fsdp):
        return fsdp + 1 - 2 * (fsdp % 2)


class Links:
    def __init__(self, send, receive):
        self.send, self.receive, self.used = send, receive, 0

    def copy(self, source, target, device, landing):
        index = self.used
        self.used += 1
        going = pltpu.make_async_remote_copy(
            src_ref=source, dst_ref=target, send_sem=self.send.at[index],
            recv_sem=self.receive.at[index], device_id=device, device_id_type=MESH,
        )
        coming = pltpu.make_async_remote_copy(
            src_ref=landing, dst_ref=landing, send_sem=self.send.at[index],
            recv_sem=self.receive.at[index], device_id=device, device_id_type=MESH,
        )
        return going, coming


def greet(devices):
    barrier = pltpu.get_barrier_semaphore()
    for device in devices:
        pl.semaphore_signal(barrier, inc=1, device_id=device, device_id_type=MESH)
    pl.semaphore_wait(barrier, len(devices))


def chip_peers(grid):
    peers = [(grid.exp, grid.sibling(grid.fsdp))]
    return peers + [(grid.exp, grid.x_from(hop)) for hop in range(1, grid.x_size)]


class ChipGather:
    def __init__(self, grid, links, own_sem, source, target):
        self.grid, self.links, self.target = grid, links, target
        self.own = pltpu.make_async_copy(source, target.at[grid.fsdp], own_sem)
        sibling = grid.sibling(grid.fsdp)
        self.along_x, self.across = [], []
        for hop in range(1, grid.x_size):
            self.along_x.append(
                links.copy(
                    source, target.at[grid.fsdp], (grid.exp, grid.x_from(hop)),
                    target.at[grid.x_from(-hop)],
                )
            )
        self.across.append(
            links.copy(source, target.at[grid.fsdp], (grid.exp, sibling), target.at[sibling])
        )

    def start(self):
        for going, _ in self.along_x + self.across:
            going.start()
        self.own.start()

    def forward(self):
        grid = self.grid
        for hop in range(1, grid.x_size):
            self.along_x[hop - 1][1].wait_recv()
            held = grid.x_from(-hop)
            other = grid.sibling(held)
            self.across.append(
                self.links.copy(
                    self.target.at[held], self.target.at[held],
                    (grid.exp, grid.sibling(grid.fsdp)), self.target.at[other],
                )
            )
            self.across[-1][0].start()

    def finish(self):
        for _, coming in self.across:
            coming.wait_recv()
        for going, _ in self.along_x + self.across:
            going.wait_send()
        self.own.wait()


class Exchange:
    def __init__(self, grid, links, own_sems, pairs):
        self.steps = grid.exp_steps()
        self.peers = [(to, grid.fsdp) for to, _ in self.steps]
        self.copies, self.own = [], []
        for index, (source, target) in enumerate(pairs):
            for to, origin in self.steps:
                self.copies.append(
                    links.copy(
                        source(to), target.at[grid.exp], (to, grid.fsdp), target.at[origin]
                    )
                )
            self.own.append(
                pltpu.make_async_copy(source(grid.exp), target.at[grid.exp], own_sems.at[index])
            )

    def start(self):
        for going, _ in self.copies:
            going.start()
        for own in self.own:
            own.start()

    def finish(self):
        for going, coming in self.copies:
            coming.wait_recv()
            going.wait_send()
        for own in self.own:
            own.wait()


ANYWHERE = pl.BlockSpec(memory_space=pl.ANY)
IN_VMEM = pl.BlockSpec(memory_space=pltpu.VMEM)


def dma_sems(count):
    return pltpu.SemaphoreType.DMA((count,))


def plane_of(source, part, to):
    return source.at[to] if part is None else source.at[to, part]


class Lanes:
    def __init__(self, heads, width, padded_heads, experts):
        self.weights = 3 * heads * width
        self.base = self.weights // 128 * 128
        self.router = self.weights - self.base
        self.gain = self.router + experts
        self.table = self.gain + 1
        self.count = self.table + padded_heads
        self.width = -(-(self.weights + 2 * experts + 1 + padded_heads) // 128) * 128
        self.extra = self.width - self.base
        self.shift = self.count - self.router


def bucket_rows_select(features, feature_rows, bucket_rows, span):
    row = lax.broadcasted_iota(jnp.int32, (features, 1), 0)
    within = lax.rem(row, feature_rows)
    bucket = jnp.where(
        within < bucket_rows, lax.div(row, feature_rows) * bucket_rows + within, -1
    )
    distance = lax.broadcasted_iota(jnp.int32, (1, span), 1) - SKEW
    near = BUCKETS // 2
    spread = max(WINDOW - near, 1)
    far = near + lax.div(jnp.maximum(distance - near, 0) * (BUCKETS - near), spread)
    wanted = jnp.where(distance < near, distance, far)
    reachable = (distance >= 0) & (distance < WINDOW)
    wanted = jnp.where(reachable, wanted, -2)
    return jnp.where(bucket == wanted, 1.0, 0.0).astype(BF16), reachable


def as_column(row, size):
    row_place = lax.broadcasted_iota(jnp.int32, (size, size), 0)
    lane = lax.broadcasted_iota(jnp.int32, (size, size), 1)
    spread = jnp.broadcast_to(row.astype(F32), (size, size))
    return jnp.sum(jnp.where(row_place == lane, spread, 0.0), axis=1, keepdims=True)


def padded_rows(value, rows):
    if value.shape[0] == rows:
        return value
    return jnp.concatenate([value, jnp.zeros((rows - value.shape[0], value.shape[1]), F32)], axis=0)


def padded_lanes(value, lanes):
    if value.shape[1] == lanes:
        return value
    return jnp.concatenate([value, jnp.zeros((value.shape[0], lanes - value.shape[1]), F32)], axis=1)


class Wide:
    def __init__(self, grid, links, own_sem, source, target):
        self.grid, self.links, self.target = grid, links, target
        self.own = pltpu.make_async_copy(
            source, target.at[grid.z, grid.y, grid.x, grid.core], own_sem
        )
        stage = []
        for hop in range(1, grid.z_size):
            origin = (grid.z + grid.z_size - hop) % grid.z_size
            stage.append(
                links.copy(
                    source, target.at[grid.z, grid.y, grid.x, grid.core],
                    grid.at(z=(grid.z + hop) % grid.z_size),
                    target.at[origin, grid.y, grid.x, grid.core],
                )
            )
        self.stages = [stage]

    def start(self):
        self.own.start()
        for going, _ in self.stages[0]:
            going.start()

    def turn(self, axis):
        grid, target = self.grid, self.target
        for _, coming in self.stages[-1]:
            coming.wait_recv()
        stage = []
        if axis == 0:
            self.own.wait()
            held = target.at[:, grid.y, grid.x, grid.core]
            for hop in range(1, grid.y_size):
                origin = (grid.y + grid.y_size - hop) % grid.y_size
                stage.append(
                    self.links.copy(
                        held, held, grid.at(y=(grid.y + hop) % grid.y_size),
                        target.at[:, origin, grid.x, grid.core],
                    )
                )
        elif axis == 1:
            held = target.at[:, :, grid.x, grid.core]
            for hop in range(1, grid.x_size):
                origin = (grid.x + grid.x_size - hop) % grid.x_size
                stage.append(
                    self.links.copy(
                        held, held, (grid.exp, grid.x_from(hop)),
                        target.at[:, :, origin, grid.core],
                    )
                )
        else:
            held = target.at[:, :, :, grid.core]
            stage.append(
                self.links.copy(
                    held, held, (grid.exp, grid.sibling(grid.fsdp)), target.at[:, :, :, 1 - grid.core]
                )
            )
        for going, _ in stage:
            going.start()
        self.stages.append(stage)

    def finish(self):
        for _, coming in self.stages[-1]:
            coming.wait_recv()
        for stage in self.stages:
            for going, _ in stage:
                going.wait_send()


def start_kernel(
    tokens, cotangent, routes_t, slots_t, attention_gain, mixture_gain, attention_in, router_t, table,
    attention_out, expert_up, expert_down, *refs, lanes, heads, width, head_count, experts, capacity,
    local, late,
):
    all_tokens, all_planes, cotangent_early, position_rows, columns, full_out = refs[:6]
    cotangent_late, refs = refs[6 : 6 + late], refs[6 + late :]
    shards = refs[: 2 * local]
    planes, up_stage, down_stage, send, receive, own, fetch, split = refs[2 * local :]
    grid = Grid().here()
    links = Links(send, receive)
    z_size, y_size, fsdp_size = grid.z_size, grid.y_size, grid.fsdp_size
    near = [
        (grid.exp, (grid.fsdp + turn) % fsdp_size) for turn in range(1, fsdp_size)
    ] + [grid.at(z=(grid.z + hop) % z_size) for hop in range(1, z_size)]
    beside = [grid.at(y=(grid.y + hop) % y_size) for hop in range(1, y_size)]
    gathered = ChipGather(grid, links, own.at[0], tokens, all_tokens)
    widely = Wide(grid, links, own.at[2], attention_out, full_out)
    part = expert_down.shape[1]
    depth = expert_up.shape[1]
    fetches = []
    for index in range(local):
        fetches.append(
            pltpu.make_async_copy(expert_up.at[index], up_stage.at[index], fetch.at[2 * index])
        )
        fetches.append(
            pltpu.make_async_copy(
                expert_down.at[index], down_stage.at[index], fetch.at[2 * index + 1]
            )
        )
    greet(near + beside)
    widely.start()
    for copy in fetches:
        copy.start()

    feature_rows = attention_in.shape[0]
    model_width = head_count * width
    gained = attention_in[...].astype(F32) * as_column(attention_gain[...], feature_rows)
    route_rows, slot_rows = routes_t[...].astype(F32), slots_t[...].astype(F32)
    columns[...] = padded_rows(jnp.concatenate([route_rows, slot_rows], axis=0), 128).T
    row_count = columns.shape[0]
    expert_lanes = lax.broadcasted_iota(jnp.int32, (row_count, experts), 1).astype(F32)
    named = jnp.zeros((row_count, experts), F32)
    for k in range(2):
        named = named + jnp.where(expert_lanes == columns[:, k : k + 1], 1.0, 0.0)
    named = jnp.sum(named, axis=0, keepdims=True)
    place = lax.broadcasted_iota(jnp.int32, (feature_rows, feature_rows), 0)
    same = place == lax.broadcasted_iota(jnp.int32, (feature_rows, feature_rows), 1)
    router = contract_last(jnp.where(same, 1.0, 0.0).astype(BF16), router_t[...])
    pieces = [
        router,
        as_column(mixture_gain[...], feature_rows),
        padded_rows(padded_lanes(table[...].astype(F32), heads * fsdp_size), feature_rows),
        padded_rows(named, feature_rows),
    ]
    taken = sum(piece.shape[1] for piece in pieces)
    if lanes.width > lanes.weights + taken:
        pieces.append(jnp.zeros((feature_rows, lanes.width - lanes.weights - taken), F32))
    for place in range(fsdp_size):
        first, last = place * heads * width, min((place + 1) * heads * width, model_width)
        own_pieces = []
        for kind in range(3):
            if last > first:
                own_pieces.append(gained[:, kind * model_width + first : kind * model_width + last])
            if last - first < heads * width:
                own_pieces.append(
                    jnp.zeros((feature_rows, heads * width - max(last - first, 0)), F32)
                )
        planes[place] = jnp.concatenate(own_pieces + pieces, axis=1).astype(BF16)
    placed = []
    for turn in range(1, fsdp_size):
        to = (grid.fsdp + turn) % fsdp_size
        origin = (grid.fsdp + fsdp_size - turn) % fsdp_size
        placed.append(
            links.copy(
                planes.at[to], all_planes.at[grid.z, grid.y, grid.fsdp], (grid.exp, to),
                all_planes.at[grid.z, grid.y, origin],
            )
        )
        placed[-1][0].start()
    kept = pltpu.make_async_copy(
        planes.at[grid.fsdp], all_planes.at[grid.z, grid.y, grid.fsdp], own.at[1]
    )
    kept.start()
    gathered.start()
    for _, coming in placed:
        coming.wait_recv()
    kept.wait()

    def over_y(z):
        for turn in range(1, y_size):
            forwarded.append(
                links.copy(
                    all_planes.at[z, grid.y],
                    all_planes.at[z, grid.y],
                    grid.at(y=(grid.y + turn) % y_size),
                    all_planes.at[z, (grid.y + y_size - turn) % y_size],
                )
            )
            forwarded[-1][0].start()

    along_z, forwarded = [], []
    for hop in range(1, z_size):
        along_z.append(
            links.copy(
                all_planes.at[grid.z, grid.y],
                all_planes.at[grid.z, grid.y],
                grid.at(z=(grid.z + hop) % z_size),
                all_planes.at[(grid.z + z_size - hop) % z_size, grid.y],
            )
        )
        along_z[-1][0].start()
    over_y(grid.z)
    widely.turn(0)

    for copy in fetches:
        copy.wait()
    splits = []
    for index in range(local):
        up, down = shards[2 * index : 2 * index + 2]
        stores = [
            (
                up_stage.at[index, :, pl.ds(block * part, part)],
                up.at[pl.ds(block * depth, depth), :],
            )
            for block in range(fsdp_size)
        ]
        for source, target in stores + [(down_stage.at[index], down)]:
            splits.append(pltpu.make_async_copy(source, target, split.at[len(splits)]))
            splits[-1].start()

    widely.turn(1)

    place = route_rows * capacity + slot_rows
    position_rows[...] = padded_rows(place, 8)
    select_rows([cotangent_early] + list(cotangent_late), place, cotangent[...])

    for hop in range(1, z_size):
        along_z[hop - 1][1].wait_recv()
        over_y((grid.z + z_size - hop) % z_size)
    gathered.forward()
    widely.turn(2)
    for going, coming in forwarded:
        coming.wait_recv()
        going.wait_send()
    for going, _ in placed + along_z:
        going.wait_send()
    gathered.finish()
    widely.finish()
    for copy in splits:
        copy.wait()


def project_kernel(
    tokens, plane, segments, normed, query_t, key_n, query_n, value_n, key_t, value_t, bias, counts,
    weight_t, table_t, *, heads, width, lanes, feature_rows, bucket_rows,
):
    @pl.when(pl.program_id(0) == 0)
    def _():
        weight_t[...] = turned(plane[:, : lanes.weights]).astype(BF16)
        extra = plane[:, lanes.base :]
        span = bias.shape[2]
        select, reachable = bucket_rows_select(plane.shape[0], feature_rows, bucket_rows, span)
        table_t[...] = lax.dot_general(
            extra, select, (((0,), (0,)), ((), ())), preferred_element_type=F32
        )
        first = lanes.table + lax.axis_index("fsdp") * heads
        for head in range(heads):
            bias[head] = jnp.where(reachable, table_t[pl.ds(first + head, 1), :], MASKED)
        summed = jnp.sum(extra.astype(F32), axis=0, keepdims=True)
        counts[...] = pltpu.roll(
            jnp.broadcast_to(summed, counts.shape), lanes.extra - lanes.shift, 1
        )

    inputs = tokens[0].astype(F32)
    scale = lax.rsqrt(jnp.mean(inputs * inputs, axis=1, keepdims=True) + EPSILON)
    low = (inputs * scale).astype(BF16)
    normed[...] = low
    rows = low.shape[0]
    projected = contract_last(weight_t[...], low).astype(BF16).astype(F32)
    document = segments[...] % 4
    places = lax.broadcasted_iota(jnp.int32, (8, rows), 0)
    same = places == document
    hot = jnp.where(same, 1.0, 0.0)
    barred = jnp.where(same | (places >= 4), 0.0, MASKED)
    filler = jnp.zeros((SKEW - 8 - width, rows), F32)
    for head in range(heads):
        query = projected[head * width : (head + 1) * width] * width ** (-0.5)
        key = projected[(heads + head) * width : (heads + head + 1) * width]
        value = projected[(2 * heads + head) * width : (2 * heads + head + 1) * width]
        query_t[head] = jnp.concatenate([query, barred, filler], axis=0).astype(BF16)
        key_n[head] = jnp.concatenate([key, hot, filler], axis=0).T.astype(BF16)
        query_n[head] = query.T.astype(BF16)
        value_n[head] = value.T.astype(BF16)
        key_t[head] = key.astype(BF16)
        value_t[head] = value.astype(BF16)


def spans(length):
    for query_start in range(0, length, QUERY_BLOCK):
        key_start = max(0, query_start - WINDOW)
        yield query_start, key_start, query_start + QUERY_BLOCK - key_start


def spread_bias(bias, skew):
    skew[...] = pltpu.roll(
        jnp.broadcast_to(bias[0], skew.shape), 0, 1, stride=1, stride_axis=0
    )


def attend_kernel(
    query_t, key_n, value_t, bias, context, context_high, log_total, attended, skew, scores, held,
    send, receive, own, *, rows,
):
    head = pl.program_id(0)
    width = value_t.shape[1]
    grid = Grid().here()
    fsdp_size = grid.fsdp_size

    def leave(number):
        place = pl.ds(pl.multiple_of(number * width, 16), width)
        copies = []
        for turn in range(1, fsdp_size):
            to = (grid.fsdp + turn) % fsdp_size
            origin = (grid.fsdp + fsdp_size - turn) % fsdp_size
            sems = dict(
                send_sem=send.at[number, turn], recv_sem=receive.at[number, turn],
                device_id=(grid.exp, to), device_id_type=MESH,
            )
            copies.append(
                (
                    pltpu.make_async_remote_copy(
                        src_ref=held.at[number, to], dst_ref=attended.at[grid.fsdp, place, :], **sems
                    ),
                    pltpu.make_async_remote_copy(
                        src_ref=attended.at[origin, place, :], dst_ref=attended.at[origin, place, :],
                        **sems,
                    ),
                )
            )
        kept = pltpu.make_async_copy(
            held.at[number, grid.fsdp], attended.at[grid.fsdp, place, :], own.at[number]
        )
        return copies, kept

    @pl.when(head == 0)
    def _():
        greet([(grid.exp, (grid.fsdp + turn) % fsdp_size) for turn in range(1, fsdp_size)])

    spread_bias(bias, skew)
    for query_start, key_start, key_count in spans(query_t.shape[2]):
        queries = slice(query_start, query_start + QUERY_BLOCK)
        keys = slice(key_start, key_start + key_count)
        raw = matmul(key_n[0, keys, :], query_t[0, :, queries])
        for start in range(0, key_count, SKEW):
            offset = query_start - key_start - start + SKEW
            scores[start : start + SKEW, :] = (
                raw[start : start + SKEW] + skew[:, offset : offset + QUERY_BLOCK]
            )
        high = jnp.max(scores[:key_count, :], axis=0, keepdims=True)
        weights = jnp.exp(scores[:key_count, :] - high)
        total = jnp.sum(weights, axis=0, keepdims=True)
        gathered = matmul(value_t[0, :, keys], weights.astype(BF16)) / total
        context_high[0, :, queries] = gathered
        log_total[0, :, queries] = high + jnp.log(total)
        for start in range(0, QUERY_BLOCK, 128):
            place = query_start + start
            piece = gathered[:, start : start + 128].astype(BF16)
            context[place // rows, :, place % rows : place % rows + 128] = piece
            held[head, place // rows, :, place % rows : place % rows + 128] = piece
    copies, kept = leave(head)
    for going, _ in copies:
        going.start()
    kept.start()

    @pl.when(head == pl.num_programs(0) - 1)
    def _():
        def finish(number, carry):
            copies, kept = leave(number)
            for going, coming in copies:
                coming.wait_recv()
                going.wait_send()
            kept.wait()
            return carry

        lax.fori_loop(0, pl.num_programs(0), finish, 0)


def attend_back_kernel(
    query_t, key_n, query_n, value_n, key_t, grad_t, grad_n, context_high, log_total, bias,
    grad_projected, grad_bias, skew, grad_skew, grad_key, grad_value, *, scale,
):
    spread_bias(bias, skew)
    grad_skew[...] = jnp.zeros_like(grad_skew)
    grad_key[...] = jnp.zeros_like(grad_key)
    grad_value[...] = jnp.zeros_like(grad_value)
    inner = jnp.sum(grad_t[0].astype(F32) * context_high[0], axis=0, keepdims=True)
    for query_start, key_start, key_count in spans(query_t.shape[2]):
        queries = slice(query_start, query_start + QUERY_BLOCK)
        keys = slice(key_start, key_start + key_count)
        raw = matmul(key_n[0, keys, :], query_t[0, :, queries])
        grad_weights = matmul(value_n[0, keys, :], grad_t[0, :, queries])
        weights_low, grad_low = [], []
        for start in range(0, key_count, SKEW):
            offset = query_start - key_start - start + SKEW
            part = slice(start, start + SKEW)
            weights = jnp.exp(
                raw[part] + skew[:, offset : offset + QUERY_BLOCK] - log_total[0, :, queries]
            )
            grad_scores = weights * (grad_weights[part] - inner[:, queries])
            grad_skew[:, offset : offset + QUERY_BLOCK] += grad_scores
            weights_low.append(weights.astype(BF16))
            grad_low.append(grad_scores.astype(BF16))
        weights_low = jnp.concatenate(weights_low, axis=0)
        grad_low = jnp.concatenate(grad_low, axis=0)
        grad_projected[0, 0, :, queries] = (matmul(key_t[0, :, keys], grad_low) * scale).astype(BF16)
        grad_key[keys, :] += matmul(grad_low, query_n[0, queries, :])
        grad_value[keys, :] += matmul(weights_low, grad_n[0, queries, :])
    grad_projected[1, 0] = grad_key[...].T.astype(BF16)
    grad_projected[2, 0] = grad_value[...].T.astype(BF16)
    count = SKEW
    span = skew.shape[1]
    while count > 8:
        count //= 2
        grad_skew[:count, :] += pltpu.roll(grad_skew[count : 2 * count, :], span - count, 1)
    summed = grad_skew[0:1, :]
    for row in range(1, 8):
        summed = summed + pltpu.roll(grad_skew[row : row + 1, :], span - row, 1)
    grad_bias[0] = summed

def expert_lane(shape, lanes):
    return lax.broadcasted_iota(jnp.int32, shape, 1) - lanes.router


def int_columns(columns):
    values = columns[:, 0:4].astype(jnp.int32)
    return values[:, 0:2], values[:, 2:4]


def route_kernel(
    tokens, attended_t, attention_out, plane, columns, position_rows, *refs,
    experts, lanes, capacity, crossing,
):
    over, refs = refs[:crossing], refs[crossing:]
    hidden, routed, probabilities, gates, outgoing, rows_in, gates_in = refs[:7]
    landed, refs = refs[7 : 7 + crossing], refs[7 + crossing :]
    slot_gates, send, receive, own = refs
    grid = Grid().here()
    links = Links(send, receive)
    exp_size = grid.exp_size
    sibling = (grid.exp, grid.sibling(grid.fsdp))
    greet([((grid.exp + hop) % exp_size, grid.fsdp) for hop in range(1, exp_size)] + [sibling])
    swaps = [links.copy(source, target, sibling, target) for source, target in zip(over, landed)]
    for going, _ in swaps:
        going.start()
    rows, model_width = tokens.shape
    routes, slots = int_columns(columns)
    attended_low = turned(attended_t[:model_width]).astype(BF16)
    hidden_state = tokens[...].astype(F32) + matmul(attended_low, attention_out[...])
    hidden[...] = hidden_state
    scale = lax.rsqrt(jnp.mean(hidden_state * hidden_state, axis=1, keepdims=True) + EPSILON)
    extra = plane[:, lanes.base :]
    gain = extra.astype(F32).T[lanes.gain : lanes.gain + 1]
    low = (hidden_state * scale * gain).astype(BF16)
    routed[...] = low
    member_slots = experts // exp_size * capacity
    work = Exchange(
        grid, links, own,
        [
            (lambda to: outgoing.at[to, pl.ds(0, capacity), :], rows_in),
            (partial(plane_of, slot_gates, None), gates_in),
        ],
    )
    for number, to in enumerate([to for to, _ in work.steps] + [grid.exp]):
        slot = lax.broadcasted_iota(jnp.int32, (member_slots, rows), 0) + to * member_slots
        slot = slot.astype(F32)
        picked = (slot == position_rows[0:1, :]) | (slot == position_rows[1:2, :])
        outgoing[to] = matmul(jnp.where(picked, 1.0, 0.0).astype(BF16), low).astype(BF16)
        (work.copies[number][0] if number < len(work.steps) else work.own[0]).start()
    logits = matmul(low, extra)
    lane = expert_lane(logits.shape, lanes)
    logits = jnp.where((lane >= 0) & (lane < experts), logits, MASKED)
    powers = jnp.exp(logits - jnp.max(logits, axis=1, keepdims=True))
    powers = powers / jnp.sum(powers, axis=1, keepdims=True)
    probabilities[...] = powers
    chosen = [
        jnp.sum(jnp.where(lane == routes[:, k : k + 1], powers, 0.0), axis=1, keepdims=True)
        for k in range(2)
    ]
    total = chosen[0] + chosen[1]
    gate_values = [chosen[k] / total for k in range(2)]
    pair = lax.broadcasted_iota(jnp.int32, (rows, 2), 1)
    gates[...] = jnp.where(pair == 0, gate_values[0], gate_values[1])
    gate_lanes = slot_gates.shape[2]
    slot_lanes = lax.broadcasted_iota(jnp.int32, (rows, gate_lanes), 1)
    inside = slot_lanes < member_slots
    places = routes * capacity + slots
    for member in range(exp_size):
        by_slot = jnp.zeros((rows, gate_lanes), F32)
        for k in range(2):
            hit = (slot_lanes + member * member_slots == places[:, k : k + 1]) & inside
            by_slot = by_slot + jnp.where(hit, gate_values[k], 0.0)
        slot_gates[member] = jnp.broadcast_to(
            jnp.sum(by_slot, axis=0, keepdims=True), slot_gates.shape[1:]
        )
    for going, _ in work.copies[exp_size - 1 :]:
        going.start()
    work.own[1].start()
    work.finish()
    for going, coming in swaps:
        coming.wait_recv()
        going.wait_send()


def select_rows(outgoing, position_rows, values):
    rows = values.shape[0]
    sizes = [array.shape[1] for array in outgoing]
    for member in range(outgoing[0].shape[0]):
        slots = lax.broadcasted_iota(jnp.int32, (sum(sizes), rows), 0) + member * sum(sizes)
        slots = slots.astype(F32)
        picked = (slots == position_rows[0:1, :]) | (slots == position_rows[1:2, :])
        found = matmul(jnp.where(picked, 1.0, 0.0).astype(BF16), values).astype(BF16)
        first = 0
        for array, size in zip(outgoing, sizes):
            array[member] = found[first : first + size]
            first += size


def gelu_parts(value):
    magnitude = jnp.abs(value)
    power = jnp.exp2(value * value * -0.7213475204444817)
    base = 1.0 + (0.3275911 * 0.7071067811865476) * magnitude
    step = pl.reciprocal(base, approx=True)
    step = step * (2.0 - base * step)
    series = step * (
        0.127414796
        + step * (-0.142248368 + step * (0.7107068705 + step * (-0.7265760135 + step * 0.5307027145)))
    )
    tail = series * power
    normal = jnp.where(value < 0.0, tail, 1.0 - tail)
    return value * normal, normal + value * (power * 0.3989422804014327)


def expert_kernel(*refs, layout, index, local, half, capacity, parts):
    shards = 2 * half
    refs = Bag(layout, refs)
    grid = Grid().here()
    z_size, y_size = grid.z_size, grid.y_size
    last = index == local - 1
    sibling = (grid.exp, grid.sibling(grid.fsdp))
    links = Links(refs.send[0], refs.receive[0])
    rows_all, cot, up_all, down_all = (
        refs.rows_all[0], refs.cot[0], refs.up_all[0], refs.down_all[0]
    )
    total = refs.total[0]
    if last:
        active, grad_hidden, unscaled = refs.active[0], refs.grad_hidden[0], refs.unscaled[0]
    else:
        grad_total, slot_grad = refs.grad_total[0], refs.slot_grad[0]
    gates, gate_column = refs.gates[0], refs.gate_column[0]
    rows_t, slot_t = refs.rows_t[0], refs.slot_t[0]
    grad_up, grad_down = refs.grad_up[0], refs.grad_down[0]
    grad_rows, grad_gates = refs.grad_rows[0], refs.grad_gates[0]
    up_keep, up_taken, down_keep, down_taken = refs.own
    keep_up = [up_keep] + list(refs.far_keep_up)
    taken_up = [up_taken] + list(refs.far_taken_up)
    keep_down = [down_keep] + list(refs.far_keep_down)
    taken_down = [down_taken] + list(refs.far_taken_down)
    load_sem, fetch_sem, store_sem = refs.load_sem[0], refs.fetch_sem[0], refs.store_sem[0]
    store_there, stored_here = refs.store_there[0], refs.stored_here[0]
    pass_sem = refs.pass_sem[0]
    blocks, _, model_width = rows_all.shape
    part = up_all.shape[2]
    count = blocks * capacity
    depth = model_width // shards
    power = z_size & (z_size - 1) == 0
    together = 2 if power and z_size > 1 else 1
    group_rows = together * y_size * capacity

    source_z, target_z = grid.source_z, grid.target_z

    def owner(place, core):
        return ((grid.x + place % half) % half) * 2 + (core + place // half) % 2

    def rows_of(place, core=None):
        core = grid.core if core is None else core
        return pl.ds(pl.multiple_of(owner(place, core) * depth, 16), depth)

    loads = [pltpu.make_async_copy(refs.rows_in[0], rows_all, load_sem.at[1])]
    late_count = 0
    if last and refs.cot_late:
        late_count = refs.cot_late[0].shape[1]
        loads.append(
            pltpu.make_async_copy(
                refs.cot_late[0], cot.at[:, pl.ds(capacity - late_count, late_count)], load_sem.at[4]
            )
        )
    loads.append(
        pltpu.make_async_copy(
            refs.cot_in[0].at[:, pl.ds(index * capacity, capacity - late_count)],
            cot.at[:, pl.ds(0, capacity - late_count)], load_sem.at[0],
        )
    )
    my_up, my_down = refs.my_up, refs.my_down
    swapped_up, swapped_down = refs.swapped_up, refs.swapped_down
    local_up = list(enumerate(my_up)) + [
        (half + number, array) for number, array in enumerate(swapped_up)
    ]
    local_down = list(enumerate(my_down)) + [
        (half + number, array) for number, array in enumerate(swapped_down)
    ]

    def fetch_up(place):
        return [
            pltpu.make_async_copy(
                array.at[rows_of(place), :], up_all.at[place, rows_of(shard), :],
                fetch_sem.at[place, number],
            )
            for number, (shard, array) in enumerate(local_up)
        ]

    fetched_down = {
        shard: pltpu.make_async_copy(
            array, down_all.at[shard], fetch_sem.at[shards + number, 0]
        )
        for number, (shard, array) in enumerate(local_down)
    }
    cross_down = {
        half + shard: links.copy(
            my_down[shard], down_all.at[half + shard], sibling, down_all.at[half + shard]
        )
        for shard in range(len(swapped_down), half)
    }
    cross_up = [
        links.copy(
            my_up[shard].at[rows_of(place, 1 - grid.core), :],
            up_all.at[place, rows_of(shard), :], sibling,
            up_all.at[place, rows_of(half + shard), :],
        )
        for shard in range(len(swapped_up), half)
        for place in range(shards)
    ]
    cross_next = [
        links.copy(source, target, sibling, target)
        for source, target in zip(refs.next_mine, refs.next_swapped)
    ]
    work = Exchange(
        grid, links, refs.own_sem[0],
        [
            (partial(plane_of, source, place), target)
            for source, place, target in zip(refs.moved_from, parts, refs.moved_to)
        ],
    )
    def member(z, y):
        return z * y_size + y

    def give_back(turn, hop):
        to = member(source_z(turn), (grid.y + hop) % y_size)
        origin = member(target_z(turn), (grid.y + y_size - hop) % y_size)
        pairs = []
        for number, (held, target) in enumerate(
            ((grad_rows, refs.back_rows[0]), (grad_gates, refs.back_gates[0]))
        ):
            sems = dict(
                send_sem=refs.back_send[0].at[number, turn, hop],
                recv_sem=refs.back_receive[0].at[number, turn, hop],
                device_id=(to, grid.fsdp), device_id_type=MESH,
            )
            pairs.append(
                (
                    pltpu.make_async_remote_copy(
                        src_ref=held.at[to], dst_ref=target.at[grid.exp], **sems
                    ),
                    pltpu.make_async_remote_copy(
                        src_ref=target.at[origin], dst_ref=target.at[origin], **sems
                    ),
                )
            )
        return pairs

    steps = [(turn, hop) for turn in range(z_size) for hop in range(y_size)]
    own_back = []
    if last:
        own_back = [
            pltpu.make_async_copy(held.at[grid.exp], target.at[grid.exp], load_sem.at[2 + number])
            for number, (held, target) in enumerate(
                ((grad_rows, refs.back_rows[0]), (grad_gates, refs.back_gates[0]))
            )
        ]

    for copy in loads:
        copy.start()
    order = list(range(shards))
    if not last:
        order = [(pair + 1) % half + side * half for pair in range(half) for side in (1, 0)]
    if last:
        for copy in fetched_down.values():
            copy.start()
    for place in order:
        if not last and place in fetched_down:
            fetched_down[place].start()
        for copy in fetch_up(place):
            copy.start()
    greet(
        [((grid.exp + hop) % grid.exp_size, grid.fsdp) for hop in range(1, grid.exp_size)]
        + chip_peers(grid)
    )
    for going, _ in list(cross_down.values()) + cross_up + cross_next:
        going.start()
    work.start()

    def place_at(position):
        hop = (position // 2 + 1) % half
        return hop + half * (1 - position % 2)

    def slot_rows():
        columns = gates[:, 0, :].T
        for block in range(blocks):
            piece = slice(block * capacity, (block + 1) * capacity)
            gate = columns[index * capacity : (index + 1) * capacity, block : block + 1]
            gate_column[piece, :] = gate
        slot_values = gate_column[...] * cot[...].reshape(count, model_width).astype(F32)
        slot_t[...] = slot_values.T.astype(BF16)
        if not last:
            slot_grad[...] = slot_values.astype(BF16)

    def wait_down(place):
        if place in fetched_down:
            fetched_down[place].wait()
        else:
            cross_down[place][1].wait_recv()

    def wait_crossed():
        for _, coming in cross_up:
            coming.wait_recv()

    def folded(value):
        return sum(value[:, start : start + 128] for start in range(0, value.shape[1], 128))

    def gate_rows(found, block):
        ones = jnp.ones((8, 128), F32)
        grad_gates[block] = lax.dot_general(
            ones, found, (((1,), (1,)), ((), ())), precision=lax.Precision.HIGHEST,
            preferred_element_type=F32,
        )

    def up_target(targets, hop, place):
        if hop == 0:
            return targets[0].at[rows_of(place), :]
        return targets[1].at[hop - 1, rows_of(place), :]

    def keep_stores(place, slot):
        return [
            pltpu.make_async_copy(
                grad_up.at[slot, rows_of(hop), :], up_target(keep_up, hop, place),
                store_sem.at[slot, hop],
            )
            for hop in range(half)
        ]

    def give_stores(place, slot):
        return [
            pltpu.make_async_remote_copy(
                src_ref=grad_up.at[slot, rows_of(half + hop), :],
                dst_ref=up_target(taken_up, hop, place),
                send_sem=store_there.at[slot, hop], recv_sem=stored_here.at[place, hop],
                device_id=sibling, device_id_type=MESH,
            )
            for hop in range(half)
        ]

    def down_store(slot):
        return pltpu.make_async_copy(grad_down.at[slot], keep_down[0], store_sem.at[slot, half])

    def down_give(hop, slot):
        target = taken_down[0] if hop == 0 else taken_down[1].at[hop - 1]
        return pltpu.make_async_remote_copy(
            src_ref=grad_down.at[slot], dst_ref=target,
            send_sem=store_there.at[slot, half], recv_sem=stored_here.at[hop, half],
            device_id=sibling, device_id_type=MESH,
        )

    def start_store(place, slot):
        for copy in keep_stores(place, slot) + give_stores(place, slot):
            copy.start()

        @pl.when(place == 0)
        def _():
            down_store(slot).start()

        for hop in range(half):

            @pl.when(place == half + hop)
            def _(hop=hop):
                down_give(hop, slot).start()

            if hop > 0:

                @pl.when(place == hop)
                def _(hop=hop):
                    keep_down[1][hop - 1] = grad_down[slot]

    def wait_store(place, slot):
        for copy in keep_stores(place, slot):
            copy.wait()
        for copy in give_stores(place, slot):
            copy.wait_send()

        @pl.when(place == 0)
        def _():
            down_store(slot).wait()

        for hop in range(half):

            @pl.when(place == half + hop)
            def _(hop=hop):
                down_give(hop, slot).wait_send()

    early_rows = part // 2 if last else 0
    early = []
    if last:
        early = [
            links.copy(
                keep_down[1].at[hop - 1, pl.ds(0, early_rows), :], refs.early_down[0].at[hop - 1],
                (grid.exp, grid.x_from(hop)), refs.early_down[0].at[hop - 1],
            )
            for hop in range(1, half)
        ]

    def sum_down():
        for hop in range(1, half):
            down_give(hop, 0).wait_recv()
            keep_down[1][hop - 1] = (
                keep_down[1][hop - 1].astype(F32) + taken_down[1][hop - 1].astype(F32)
            ).astype(BF16)
            if last:
                early[hop - 1][0].start()

    def fused(position, carry):
        place, slot = place_at(position), position % 2
        for copy in fetch_up(place):
            copy.wait()
        for which in range(shards):

            @pl.when(place == which)
            def _(which=which):
                wait_down(which)

        up, down = up_all[place], down_all[place]
        rows = rows_all[...].reshape(count, model_width)
        pieces = [slice(start, start + 256) for start in range(0, count, 256)]

        def products_of(piece):
            return matmul(rows[piece], up), contract_last(slot_grad[piece, :], down)

        raw = products_of(pieces[0])
        active_low, grad_low = [], []
        for number, piece in enumerate(pieces):
            hidden, grad_active = raw
            if number + 1 < len(pieces):
                raw = products_of(pieces[number + 1])
            activated, slope = gelu_parts(hidden)
            active_low.append(activated.astype(BF16))
            grad_low.append((grad_active * slope).astype(BF16))
            total[piece, :] += matmul(active_low[number], down)
            grad_total[piece, :] += contract_last(grad_low[number], up)
        active_low = jnp.concatenate(active_low, axis=0)
        grad_low = jnp.concatenate(grad_low, axis=0)

        @pl.when(position >= 2)
        def _():
            wait_store(place_at(position - 2), slot)

        grad_up[slot] = matmul(rows_t[...], grad_low).astype(BF16)
        grad_down[slot] = matmul(slot_t[...], active_low).T.astype(BF16)
        start_store(place, slot)
        return carry

    def group(step, carry):
        number = z_size // together - 1 - step
        turns = [number * together + more for more in range(together)]
        if together == 2:
            place_of_group = flipped(grid.z // 2, number, z_size // 2)
        else:
            place_of_group = source_z(number)
        members = pl.ds(place_of_group * together * y_size, together * y_size)
        span = pl.ds(pl.multiple_of(place_of_group * group_rows, 16), group_rows)
        rows = rows_all[members].reshape(group_rows, model_width)
        gate = gate_column[span, :]
        grad = jnp.zeros((group_rows, model_width), F32)
        products = jnp.zeros((group_rows, 128), F32)
        ahead = matmul(rows, up_all[0])
        for place in range(shards):
            hidden = ahead
            if place + 1 < shards:
                ahead = matmul(rows, up_all[place + 1])
            base = unscaled[place, span, :].astype(F32)
            activated, slope = gelu_parts(hidden)
            products = products + folded(activated * base)
            active_low = activated.astype(BF16)
            active[place, span, :] = active_low
            low = (gate * base * slope).astype(BF16)
            grad_hidden[place, span, :] = low
            grad = grad + contract_last(low, up_all[place])
            total[span, :] += matmul(active_low, down_all[place])
        grad_rows[members] = grad.astype(BF16).reshape(together * y_size, capacity, model_width)
        for hop in range(together * y_size):
            gate_rows(
                products[hop * capacity : (hop + 1) * capacity],
                place_of_group * together * y_size + hop,
            )
        for turn in turns:
            for hop in range(y_size):

                @pl.when(turn + hop > 0)
                def _(turn=turn, hop=hop):
                    for going, _ in give_back(turn, hop):
                        going.start()

        return carry

    def column(position, carry):
        place, slot = place_at(position), position % 2
        if half > 1:

            @pl.when(position == shards - 1)
            def _():
                sum_down()

        @pl.when(position >= 2)
        def _():
            wait_store(place_at(position - 2), slot)

        grad_up[slot] = matmul(rows_t[...], grad_hidden[place]).astype(BF16)
        grad_down[slot] = matmul(slot_t[...], active[place]).T.astype(BF16)
        start_store(place, slot)
        return carry

    for copy in loads[1:]:
        copy.wait()
    total[...] = jnp.zeros_like(total)
    slot_rows()
    if last:
        for place in range(shards):
            wait_down(place)
            unscaled[place] = contract_last(
                cot[...].reshape(count, model_width), down_all[place]
            ).astype(BF16)
        loads[0].wait()
        for place in range(shards):
            for copy in fetch_up(place):
                copy.wait()
        wait_crossed()
        lax.fori_loop(0, z_size // together, group, 0)
        for copy in own_back:
            copy.start()
        rows_t[...] = turned(rows_all[...].reshape(count, model_width)).astype(BF16)
        lax.fori_loop(0, shards, column, 0)
    else:
        loads[0].wait()
        rows_t[...] = turned(rows_all[...].reshape(count, model_width)).astype(BF16)
        grad_total[...] = jnp.zeros_like(grad_total)
        wait_crossed()
        lax.fori_loop(0, shards, fused, 0)
        grad_rows[...] = grad_total[...].astype(BF16).reshape(grad_rows.shape)
        for block in range(blocks):
            rows = total[block * capacity : (block + 1) * capacity, :].astype(BF16).astype(F32)
            gate_rows(folded(rows * cot[block].astype(F32)), block)

    rows_out = refs.rows_out[0]
    cot[...] = total[...].astype(BF16).reshape(blocks, capacity, model_width)
    out_copies = [pltpu.make_async_copy(cot, rows_out.at[:, index], load_sem.at[0])]
    for before in refs.outs_before:
        out_copies.append(
            pltpu.make_async_copy(before, rows_out.at[:, pl.ds(0, index)], load_sem.at[1])
        )
    for copy in out_copies:
        copy.start()
    for position in range(max(shards - 2, 0), shards):
        wait_store(place_at(position), position % 2)
    for place in range(shards):
        for copy in give_stores(place, 0):
            copy.wait_recv()
    down_give(0, 0).wait_recv()
    if half > 1:
        if not last:
            sum_down()
        keep_up[1][...] = (keep_up[1][...].astype(F32) + taken_up[1][...].astype(F32)).astype(BF16)
        middle_rows = part // 4 if last else 0
        done_rows = early_rows + middle_rows
        passed = [
            (keep_up[1], refs.pass_up[0], 0),
            (keep_down[1].at[:, pl.ds(done_rows, part - done_rows), :], refs.pass_down[0], 1),
        ]
        if last:
            passed.append(
                (keep_down[1].at[:, pl.ds(early_rows, middle_rows), :], refs.middle_down[0], 2)
            )
        for source, target, number in passed:
            out_copies.append(pltpu.make_async_copy(source, target, pass_sem.at[number]))
            out_copies[-1].start()
    for copy in out_copies:
        copy.wait()
    for going, coming in early:
        coming.wait_recv()
        going.wait_send()
    for going, coming in cross_next:
        coming.wait_recv()
        going.wait_send()
    for going, _ in list(cross_down.values()) + cross_up:
        going.wait_send()
    work.finish()
    if last:
        for turn, hop in steps[1:]:
            for going, coming in give_back(turn, hop):
                coming.wait_recv()
                going.wait_send()
        for copy in own_back:
            copy.wait()


class Bag:
    def __init__(self, layout, refs):
        start = 0
        for name, size in layout.items():
            setattr(self, name, refs[start : start + size])
            start += size


class Wanted:
    def groups(self):
        return list(self.__dict__.values())

    def layout(self):
        return {name: len(group) for name, group in self.__dict__.items()}


def run_expert(index, local, rows_in, gates, cotangent, cotangent_late, ups, downs, swapped, next_mine,
               moved, outs_before, collective_id):
    grid = Grid()
    half = len(ups)
    shards = 2 * half
    last = index == local - 1
    blocks, capacity, model_width = rows_in.shape
    part = downs[0].shape[0]
    count = blocks * capacity
    inputs, outputs, scratch = Wanted(), Wanted(), Wanted()
    inputs.cot_in = [(cotangent, ANYWHERE)]
    inputs.cot_late = [(array, ANYWHERE) for array in cotangent_late]
    inputs.rows_in = [(rows_in, ANYWHERE)]
    inputs.gates = [(gates, IN_VMEM)]
    inputs.my_up = [(array, ANYWHERE) for array in ups]
    inputs.my_down = [(array, ANYWHERE) for array in downs]
    inputs.swapped_up = [(array, ANYWHERE) for array in swapped[0]]
    inputs.swapped_down = [(array, ANYWHERE) for array in swapped[1]]
    inputs.next_mine = [(array, ANYWHERE) for array in next_mine]
    inputs.moved_from = [(array, ANYWHERE) for array, _ in moved]
    inputs.outs_before = [] if outs_before is None else [(outs_before, IN_VMEM)]

    up_shape, down_shape = (model_width, part), (part, model_width)
    outputs.rows_out = [(shape_of((blocks, index + 1, capacity, model_width), BF16), ANYWHERE)]
    own_up, own_down = shape_of(up_shape, BF16), shape_of(down_shape, BF16)
    outputs.own = [(own_up, ANYWHERE), (own_up, ANYWHERE), (own_down, ANYWHERE), (own_down, ANYWHERE)]
    outputs.pass_up = [(shape_of((half - 1,) + up_shape, BF16), ANYWHERE)] if half > 1 else []
    early_rows, middle_rows = (part // 2, part // 4) if last else (0, 0)
    late_down = (half - 1, part - early_rows - middle_rows, model_width)
    early_down = (half - 1, early_rows, model_width)
    middle_down = (half - 1, middle_rows, model_width)
    split = half > 1 and last
    outputs.pass_down = [(shape_of(late_down, BF16), ANYWHERE)] if half > 1 else []
    outputs.early_down = [(shape_of(early_down, BF16), ANYWHERE)] if split else []
    outputs.middle_down = [(shape_of(middle_down, BF16), ANYWHERE)] if split else []
    outputs.next_swapped = [(shape_of(array.shape, BF16), ANYWHERE) for array in next_mine]
    outputs.moved_to = [
        (
            shape_of((grid.exp_size,) + array.shape[(1 if place is None else 2) :], array.dtype),
            ANYWHERE,
        )
        for array, place in moved
    ]
    rows_shape, gate_shape = (blocks, capacity, model_width), (blocks, 8, capacity)
    if last:
        outputs.back_rows = [(shape_of(rows_shape, BF16), ANYWHERE)]
        outputs.back_gates = [(shape_of(gate_shape, F32), ANYWHERE)]
    else:
        outputs.grad_rows = [(shape_of(rows_shape, BF16), IN_VMEM)]
        outputs.grad_gates = [(shape_of(gate_shape, F32), IN_VMEM)]

    sems = lambda *shape: pltpu.SemaphoreType.DMA(shape)
    scratch.rows_all = [pltpu.VMEM(rows_shape, BF16)]
    scratch.cot = [pltpu.VMEM(rows_shape, BF16)]
    scratch.up_all = [pltpu.VMEM((shards,) + up_shape, BF16)]
    scratch.down_all = [pltpu.VMEM((shards,) + down_shape, BF16)]
    scratch.total = [pltpu.VMEM((count, model_width), F32)]
    if last:
        scratch.active = [pltpu.VMEM((shards, count, part), BF16)]
        scratch.grad_hidden = [pltpu.VMEM((shards, count, part), BF16)]
        scratch.unscaled = [pltpu.VMEM((shards, count, part), BF16)]
    else:
        scratch.grad_total = [pltpu.VMEM((count, model_width), F32)]
        scratch.slot_grad = [pltpu.VMEM((count, model_width), BF16)]
    if last:
        scratch.grad_rows = [pltpu.VMEM(rows_shape, BF16)]
        scratch.grad_gates = [pltpu.VMEM(gate_shape, F32)]
        scratch.back_send = [sems(2, grid.z_size, grid.y_size)]
        scratch.back_receive = [sems(2, grid.z_size, grid.y_size)]
    scratch.gate_column = [pltpu.VMEM((count, 1), F32)]
    scratch.rows_t = [pltpu.VMEM((model_width, count), BF16)]
    scratch.slot_t = [pltpu.VMEM((model_width, count), BF16)]
    scratch.grad_up = [pltpu.VMEM((2,) + up_shape, BF16)]
    scratch.grad_down = [pltpu.VMEM((2,) + down_shape, BF16)]
    far_up = [pltpu.VMEM((half - 1,) + up_shape, BF16)] * (1 if half > 1 else 0)
    far_down = [pltpu.VMEM((half - 1,) + down_shape, BF16)] * (1 if half > 1 else 0)
    scratch.far_keep_up, scratch.far_taken_up = far_up, far_up
    scratch.far_keep_down, scratch.far_taken_down = far_down, far_down
    scratch.load_sem = [sems(5)]
    scratch.pass_sem = [sems(3)]
    scratch.fetch_sem = [sems(2 * shards, shards)]
    scratch.store_sem = [sems(2, half + 1)]
    scratch.store_there = [sems(2, half + 1)]
    scratch.stored_here = [sems(shards, half + 1)]
    copies = len(moved) * grid.exp_size + half * (shards + 2) + len(next_mine)
    scratch.send = [sems(copies)]
    scratch.receive = [sems(copies)]
    scratch.own_sem = [sems(max(len(moved), 1))]

    layout = {**inputs.layout(), **outputs.layout(), **scratch.layout()}

    def body(*refs):
        expert_kernel(
            *refs, layout=layout, index=index, local=local, half=half, capacity=capacity,
            parts=[place for _, place in moved],
        )

    results = pl.pallas_call(
        body,
        in_specs=[spec for group in inputs.groups() for _, spec in group],
        out_specs=tuple(spec for group in outputs.groups() for _, spec in group),
        out_shape=tuple(shape for group in outputs.groups() for shape, _ in group),
        scratch_shapes=[item for group in scratch.groups() for item in group],
        compiler_params=params(collective_id=collective_id, has_side_effects=True),
        cost_estimate=hint(45),
        name=f"expert_{index}",
    )(*[array for group in inputs.groups() for array, _ in group])
    return Bag(outputs.layout(), results)


def local_picks(routes, slots, capacity, local, index, slot_count):
    member, which = lax.div(routes, local), lax.rem(routes, local)
    places = jnp.where(which == index, member * capacity + slots, -1)
    lane = lax.broadcasted_iota(jnp.int32, (routes.shape[0], slot_count), 1)
    return [lane == places[:, k : k + 1] for k in range(2)]


def unroute_kernel(
    hidden, cotangent, routed, probabilities, gates, plane, columns, counts, attention_out, context,
    *refs, experts, local, token_total, lanes, heads, width,
):
    grads, gate_grads = refs[:local], refs[local : 2 * local]
    (
        grad_hidden, small, grad_t, grad_n, grad_out, branches, own_out, total, send, receive, own_sem,
    ) = refs[2 * local :]
    grid = Grid().here()
    links = Links(send, receive)
    rows, model_width = hidden.shape
    members, capacity = grads[0].shape[0], grads[0].shape[1]
    head_rows = heads * width
    fetch = pltpu.make_async_copy(
        attention_out.at[pl.ds(pl.multiple_of(grid.fsdp * head_rows, 16), head_rows), :], own_out,
        own_sem.at[0],
    )
    fetch.start()
    greet(chip_peers(grid))
    extra = plane[:, lanes.base :]
    gains = extra.astype(F32).T[lanes.gain : lanes.gain + 1]
    half_rows = rows // 2
    sibling = grid.sibling(grid.fsdp)
    small_t = jnp.zeros((lanes.extra, model_width), F32)
    gain_grad = jnp.zeros((1, model_width), F32)
    along_x, across = [], []
    for half in range(2):
        here = slice(half * half_rows, (half + 1) * half_rows)
        grad_output = cotangent[here, :].astype(F32)
        routes = columns[here, 0:2].astype(jnp.int32)
        slots = columns[here, 2:4].astype(jnp.int32)
        member, which = lax.div(routes, local), lax.rem(routes, local)
        lane = lax.broadcasted_iota(jnp.int32, (half_rows, capacity), 1)
        grad_routed = jnp.zeros((half_rows, model_width), F32)
        found = [jnp.zeros((half_rows, capacity), F32), jnp.zeros((half_rows, capacity), F32)]
        for index in range(local):
            picks = local_picks(routes, slots, capacity, local, index, members * capacity)
            grad_routed = grad_routed + matmul(
                jnp.where(picks[0] | picks[1], 1.0, 0.0).astype(BF16),
                grads[index][...].reshape(members * capacity, model_width),
            )
            for place in range(members):
                spots = jnp.where((which == index) & (member == place), slots, -1)
                for k in range(2):
                    found[k] = found[k] + jnp.where(
                        lane == spots[:, k : k + 1], gate_grads[index][place, 0:1, :], 0.0
                    )
        grad_gates = [jnp.sum(found[k], axis=1, keepdims=True) for k in range(2)]
        powers = probabilities[here, :]
        lane = expert_lane(powers.shape, lanes)
        inside = (lane >= 0) & (lane < experts)
        picked = [lane == routes[:, k : k + 1] for k in range(2)]
        chosen_total = sum(
            jnp.sum(jnp.where(picked[k], powers, 0.0), axis=1, keepdims=True) for k in range(2)
        )
        weighted = grad_gates[0] * gates[here, 0:1] + grad_gates[1] * gates[here, 1:2]
        grad_mass = (AUX_WEIGHT * experts / (2.0 * token_total * token_total)) * counts[0:1, :]
        grad_mass = jnp.where(inside, grad_mass, 0.0)
        for k in range(2):
            grad_mass = grad_mass + jnp.where(
                picked[k], (grad_gates[k] - weighted) / chosen_total, 0.0
            )
        grad_logits = powers * (grad_mass - jnp.sum(powers * grad_mass, axis=1, keepdims=True))
        grad_routed = grad_routed + contract_last(grad_logits.astype(BF16), extra)
        hidden_state = hidden[here, :]
        scale = lax.rsqrt(jnp.mean(hidden_state * hidden_state, axis=1, keepdims=True) + EPSILON)
        normed = hidden_state * scale
        product = grad_routed * normed
        grad = scale * (
            grad_routed * gains - normed * jnp.mean(product * gains, axis=1, keepdims=True)
        ) + grad_output
        grad_hidden[here, :] = grad
        branches[grid.fsdp, here, :] = grad.astype(BF16)
        mine = branches.at[grid.fsdp, here, :]
        for hop in range(1, grid.x_size):
            along_x.append(
                links.copy(
                    mine, mine, (grid.exp, grid.x_from(hop)),
                    branches.at[grid.x_from(-hop), here, :],
                )
            )
            along_x[-1][0].start()
        across.append(
            links.copy(mine, mine, (grid.exp, sibling), branches.at[sibling, here, :])
        )
        across[-1][0].start()
        gain_grad = gain_grad + jnp.sum(product, axis=0, keepdims=True)
        small_t = small_t + matmul(grad_logits.T.astype(BF16), routed[here, :])

    def context_grad(place):
        branch = branches[place]
        grad = contract_last(own_out[...], branch).astype(BF16)
        columns_here = pl.ds(pl.multiple_of(place * rows, 128), rows)
        rows_here = pl.ds(pl.multiple_of(place * rows, 16), rows)
        for head in range(heads):
            piece = grad[head * width : (head + 1) * width]
            grad_t[head, :, columns_here] = piece
            grad_n[head, rows_here, :] = turned(piece).astype(BF16)
        total[...] += matmul(context[place], branch)

    total[...] = jnp.zeros_like(total)
    fetch.wait()
    context_grad(grid.fsdp)
    forwards = []
    for half in range(2):
        here = slice(half * half_rows, (half + 1) * half_rows)
        for hop in range(1, grid.x_size):
            along_x[half * (grid.x_size - 1) + hop - 1][1].wait_recv()
            held = grid.x_from(-hop)
            forwards.append(
                links.copy(
                    branches.at[held, here, :], branches.at[held, here, :], (grid.exp, sibling),
                    branches.at[grid.sibling(held), here, :],
                )
            )
            forwards[-1][0].start()
    row = lax.broadcasted_iota(jnp.int32, small_t.shape, 0)
    small[...] = jnp.where(row == lanes.gain, gain_grad, small_t).T
    for _, coming in across:
        coming.wait_recv()
    context_grad(sibling)
    for hop in range(1, grid.x_size):
        context_grad(grid.x_from(-hop))
    for _, coming in forwards:
        coming.wait_recv()
    for hop in range(1, grid.x_size):
        context_grad(grid.sibling(grid.x_from(-hop)))
    grad_out[...] = total[...].astype(BF16)
    for going, _ in along_x + across + forwards:
        going.wait_send()


def project_back_kernel(
    grad_projected, normed, plane, small, probabilities, grad_bias, grad_first, grad_plane, total,
    bias_t, *, lanes, heads, feature_rows, bucket_rows,
):
    step = pl.program_id(0)

    @pl.when(step == 0)
    def _():
        total[...] = jnp.zeros_like(total)

    grad = grad_projected[...]
    grad_first[0] = matmul(plane[:, : lanes.weights], grad).astype(BF16)
    total[: lanes.weights, :] += matmul(grad, normed[...])

    @pl.when(step == pl.num_programs(0) - 1)
    def _():
        grad_plane[...] = total[...].T.astype(BF16)
        span = grad_bias.shape[2]
        select, _ = bucket_rows_select(plane.shape[0], feature_rows, bucket_rows, span)
        bias_t[...] = jnp.zeros_like(bias_t)
        first = lanes.table + lax.axis_index("fsdp") * heads
        for head in range(heads):
            bias_t[pl.ds(first + head, 1), :] = grad_bias[head]
        high = bias_t[...].astype(BF16)
        rest = (bias_t[...] - high.astype(F32)).astype(BF16)
        table = contract_last(select, high) + contract_last(select, rest)
        mass = jnp.sum(probabilities[...], axis=0, keepdims=True)
        mass = pltpu.roll(jnp.broadcast_to(mass, (8, lanes.extra)), lanes.shift, 1)[0:1]
        lane = lax.broadcasted_iota(jnp.int32, table.shape, 1)
        row = lax.broadcasted_iota(jnp.int32, table.shape, 0)
        is_small = (lane >= lanes.router) & (lane < lanes.table)
        is_mass = (lane >= lanes.count) & (lax.rem(row, feature_rows) == 0)
        extra = table + jnp.where(is_small, small[...], 0.0) + jnp.where(is_mass, mass, 0.0)
        grad_plane[:, lanes.base :] = (total[lanes.base :, :].T + extra).astype(BF16)


def last_kernel(
    first, planes, out_grad, hidden, gates, columns, rows_back, first_parts, output, plane_parts,
    out_parts, first_in, first_sum, planes_in, plane_sum, along_in, reduced, rows_held, send, receive,
    own, *, spread_out, local,
):
    fetch = pltpu.make_async_copy(rows_back, rows_held, own.at[2])
    fetch.start()
    grid = Grid().here()
    links = Links(send, receive)
    z_size, y_size, x_size, fsdp_size = grid.z_size, grid.y_size, grid.x_size, grid.fsdp_size
    exp_size = grid.exp_size
    sibling = grid.sibling(grid.fsdp)
    near = [
        (grid.exp, (grid.fsdp + turn) % fsdp_size) for turn in range(1, fsdp_size)
    ] + [grid.at(z=(grid.z + hop) % z_size) for hop in range(1, z_size)]
    beside = [grid.at(y=(grid.y + hop) % y_size) for hop in range(1, y_size)]

    per_sender = grid.device_count if spread_out else exp_size
    base = 0 if spread_out else grid.fsdp * exp_size
    out_sends = []
    for number in range(per_sender):
        to = base + number
        out_sends.append((to, number))
    if spread_out:
        out_origins = [(origin, origin) for origin in range(grid.device_count)]
    else:
        out_origins = [
            (member * fsdp_size + grid.linear // exp_size, member) for member in range(exp_size)
        ]
    own_slot = grid.linear if spread_out else grid.exp
    out_base = links.used
    links.used += per_sender

    def place_of(linear):
        return (linear // fsdp_size, linear % fsdp_size)

    def out_copy(to, number, slot):
        return pltpu.make_async_remote_copy(
            src_ref=out_grad.at[number], dst_ref=out_parts.at[slot],
            send_sem=send.at[out_base + number], recv_sem=receive.at[out_base + slot],
            device_id=place_of(to), device_id_type=MESH,
        )

    barrier = pltpu.get_barrier_semaphore()
    for device in near + beside:
        pl.semaphore_signal(barrier, inc=1, device_id=device, device_id_type=MESH)
    for origin, _ in out_origins:

        @pl.when(origin != grid.linear)
        def _(origin=origin):
            pl.semaphore_signal(
                barrier, inc=1, device_id=place_of(origin), device_id_type=MESH
            )

    to_self = (
        1 if spread_out else jnp.where(grid.linear // exp_size == grid.fsdp, 1, 0)
    )
    pl.semaphore_wait(barrier, len(near) + len(beside) + per_sender - to_self)

    first_copies = []
    for hop in range(x_size):
        mine = grid.x_from(hop)
        first_copies.append(
            links.copy(
                first.at[grid.sibling(mine)], first_in.at[hop], (grid.exp, sibling), first_in.at[hop]
            )
        )
        first_copies[-1][0].start()
    z_hops = list(range(1, z_size)) + [0]
    beside_copies = []
    for z_hop in z_hops:
        beside_copies.append([])
        for hop in range(1, y_size):
            to = (grid.y + hop) % y_size
            landing = planes_in.at[hop - 1, z_hop]
            beside_copies[-1].append(
                links.copy(
                    planes.at[(grid.z + z_hop) % z_size, to], landing, grid.at(y=to), landing
                )
            )
            beside_copies[-1][-1][0].start()
    along_x = []
    for hop in range(x_size):
        first_copies[hop][1].wait_recv()
        summed = first[grid.x_from(hop)].astype(F32) + first_in[hop].astype(F32)
        if hop == 0:
            first_parts[0] = summed.astype(BF16)
        else:
            first_sum[hop - 1] = summed.astype(BF16)
            along_x.append(
                links.copy(
                    first_sum.at[hop - 1], first_parts.at[hop], (grid.exp, grid.x_from(hop)),
                    first_parts.at[hop],
                )
            )
            along_x[-1][0].start()
    along_z = []
    for z_hop, copies in zip(z_hops, beside_copies):
        to_z = (grid.z + z_hop) % z_size
        summed = planes[to_z, grid.y].astype(F32)
        for number, (_, coming) in enumerate(copies):
            coming.wait_recv()
            summed = summed + planes_in[number, z_hop].astype(F32)
        plane_sum[z_hop] = summed.astype(BF16)
        if z_hop > 0:
            along_z.append(
                links.copy(
                    plane_sum.at[z_hop], along_in.at[z_hop - 1], grid.at(z=to_z),
                    along_in.at[z_hop - 1],
                )
            )
            along_z[-1][0].start()
    for to, number in out_sends:

        @pl.when(to != grid.linear)
        def _(to=to, number=number):
            out_copy(to, number, own_slot).start()

        @pl.when(to == grid.linear)
        def _(number=number):
            pltpu.make_async_copy(out_grad.at[number], out_parts.at[own_slot], own.at[0]).start()

    fetch.wait()
    mix_rows(hidden, gates, columns, rows_held, output, local)
    summed = plane_sum[0].astype(F32)
    for number, (_, coming) in enumerate(along_z):
        coming.wait_recv()
        summed = summed + along_in[number].astype(F32)
    reduced[...] = summed.astype(BF16)
    placed = []
    for turn in range(1, fsdp_size):
        to = (grid.fsdp + turn) % fsdp_size
        origin = (grid.fsdp + fsdp_size - turn) % fsdp_size
        placed.append(
            links.copy(
                reduced.at[to], plane_parts.at[grid.fsdp], (grid.exp, to), plane_parts.at[origin]
            )
        )
        placed[-1][0].start()
    kept = pltpu.make_async_copy(reduced.at[grid.fsdp], plane_parts.at[grid.fsdp], own.at[1])
    kept.start()
    for going, coming in along_x + placed:
        coming.wait_recv()
    for going, _ in first_copies + along_x + along_z + placed:
        going.wait_send()
    for copies in beside_copies:
        for going, _ in copies:
            going.wait_send()
    kept.wait()
    for origin, slot in out_origins:

        @pl.when(origin != grid.linear)
        def _(origin=origin, slot=slot):
            out_copy(origin, 0, slot).wait_recv()

    for to, number in out_sends:

        @pl.when(to != grid.linear)
        def _(to=to, number=number):
            out_copy(to, number, own_slot).wait_send()

        @pl.when(to == grid.linear)
        def _(number=number):
            pltpu.make_async_copy(out_grad.at[number], out_parts.at[own_slot], own.at[0]).wait()


def mix_rows(hidden, gates, columns, rows_in, output, local):
    members, _, capacity, model_width = rows_in.shape
    routes, slots = int_columns(columns)
    total = hidden[...]
    picked = [jnp.zeros(hidden.shape, F32), jnp.zeros(hidden.shape, F32)]
    for index in range(local):
        picks = local_picks(routes, slots, capacity, local, index, members * capacity)
        values = rows_in[:, index].reshape(members * capacity, model_width)
        for k in range(2):
            picked[k] = picked[k] + matmul(jnp.where(picks[k], 1.0, 0.0).astype(BF16), values)
    for k in range(2):
        total = total + gates[:, k : k + 1] * picked[k]
    output[...] = total.astype(BF16)


def finish_kernel(
    first_parts, plane_parts, out_parts, tokens, grad_hidden, attention_in, attention_gain, counts,
    grad_tokens, grad_gain, grad_in, grad_out, grad_mixture, grad_router, grad_table, balance,
    *, lanes, heads, width, head_count, experts, token_total,
):
    total = jnp.sum(first_parts[...].astype(F32), axis=0).T
    inputs = tokens[...].astype(F32)
    scale = lax.rsqrt(jnp.mean(inputs * inputs, axis=1, keepdims=True) + EPSILON)
    normed = inputs * scale
    grad_tokens[...] = grad_hidden[...] + scale * (
        total - normed * jnp.mean(total * normed, axis=1, keepdims=True)
    )
    fsdp_size = plane_parts.shape[0]
    model_width = head_count * width
    sums = [plane_parts[place].astype(F32) for place in range(fsdp_size)]
    columns = []
    for kind in range(3):
        pieces = [
            sums[place][:, kind * heads * width : (kind + 1) * heads * width]
            for place in range(fsdp_size)
        ]
        columns.append(jnp.concatenate(pieces, axis=1)[:, :model_width])
    gathered = jnp.concatenate(columns, axis=1)
    feature_rows = gathered.shape[0]
    gain = jnp.sum(gathered * attention_in[...].astype(F32), axis=1, keepdims=True)
    gain = padded_rows(jnp.broadcast_to(gain, (feature_rows, 128)), 128).T
    grad_gain[...] = gain[0:1, :feature_rows]
    grad_in[...] = gathered * as_column(attention_gain[...], feature_rows)
    grad_out[...] = jnp.sum(out_parts[...].astype(F32), axis=0)
    extra = sum(part[:, lanes.base :] for part in sums)
    extra_t = padded_rows(extra, 128).T
    grad_mixture[...] = extra_t[lanes.gain : lanes.gain + 1, :feature_rows]
    grad_router[...] = extra_t[lanes.router : lanes.router + experts, :feature_rows]
    grad_table[...] = extra[: grad_table.shape[0], lanes.table : lanes.table + head_count]
    mass = jnp.broadcast_to(extra[0:1], (8, lanes.extra))
    mass = pltpu.roll(mass, lanes.extra - lanes.shift, 1)
    lane = expert_lane(mass.shape, lanes)
    terms = jnp.where((lane >= 0) & (lane < experts), mass * counts[...], 0.0)[0:1]
    balance[...] = jnp.sum(terms, axis=1, keepdims=True) * (
        experts / (2.0 * token_total * token_total)
    )


def sum_kernel(*refs, layout, local):
    outputs = refs[sum(len(starts) for _, _, starts in layout) :]
    totals = {}
    number = 0
    for index, which, starts in layout:
        shape = outputs[which].shape[1:]
        value = refs[number][...].reshape(shape).astype(F32)
        for place, start in enumerate(starts[1:], 1):
            rest = refs[number + place][...].reshape(shape).astype(F32)
            value = jnp.where(pl.program_id(0) < start, value, rest)
        number += len(starts)
        totals[index, which] = totals[index, which] + value if (index, which) in totals else value
    for (index, which), total in totals.items():
        outputs[which][index] = total


def sum_grads(groups, up_shape, down_shape, blocks):
    local = len(groups)
    depth, part = up_shape[1], down_shape[1]
    sizes = ((depth, part), (part // blocks, down_shape[2]))
    arrays, specs, layout = [], [], []
    for index, group in enumerate(groups):
        for which, (size, (keep, taken, passed)) in enumerate(zip(sizes, group)):
            for array in (keep, taken, *passed):
                pieces = array if isinstance(array, tuple) else (array,)
                starts, start = [], 0
                for piece in pieces:
                    count = piece.shape[0] // size[0]
                    arrays.append(piece)
                    specs.append(
                        pl.BlockSpec(
                            size,
                            lambda c, start=start, count=count: (jnp.clip(c - start, 0, count - 1), 0),
                        )
                    )
                    starts.append(start)
                    start += count
                layout.append((index, which, starts))
    return pl.pallas_call(
        partial(sum_kernel, layout=layout, local=local),
        grid=(blocks,),
        in_specs=specs,
        out_specs=[
            pl.BlockSpec((local, depth, part), lambda c: (0, 0, c)),
            pl.BlockSpec((local, part // blocks, down_shape[2]), lambda c: (0, c, 0)),
        ],
        out_shape=(shape_of(up_shape, F32), shape_of(down_shape, F32)),
        compiler_params=params(),
        cost_estimate=hint(8),
        name="sum_grads",
    )(*arrays)


def over_x(array, hop):
    fsdp_size = lax.axis_size("fsdp")
    return lax.ppermute(array, "fsdp", [(i, (i + 2 * hop) % fsdp_size) for i in range(fsdp_size)])


def over_core(array):
    return lax.ppermute(array, "fsdp", [(i, i ^ 1) for i in range(lax.axis_size("fsdp"))])


def on_device(
    tokens,
    cotangent,
    segments,
    routes,
    slots,
    attention_gain,
    mixture_gain,
    attention_in,
    attention_out,
    router_weight,
    position_table,
    expert_up,
    expert_down,
):
    grid = Grid()
    exp_size, fsdp_size, chips = grid.exp_size, grid.fsdp_size, grid.x_size
    device_count = grid.device_count
    fsdp_index = lax.axis_index("fsdp")
    rows, model_width = tokens.shape
    length = rows * fsdp_size
    head_count = position_table.shape[1]
    width = model_width // head_count
    heads = -(-head_count // fsdp_size)
    padded_heads = heads * fsdp_size
    feature_rows, bucket_rows = attention_in.shape[0], position_table.shape[0]
    experts = router_weight.shape[1]
    local = expert_up.shape[0]
    capacity = 4 * rows // experts
    token_total = rows * device_count
    span = WINDOW + 2 * SKEW + QUERY_BLOCK
    lanes = Lanes(heads, width, padded_heads, experts)
    part = expert_down.shape[1]
    gain_row = attention_gain.reshape(1, feature_rows)
    late_rows = 2 * capacity // 3 if local > 1 and capacity % 48 == 0 else 0
    late = 1 if late_rows else 0

    shard_shapes = [shape_of((model_width, part), BF16), shape_of((part, model_width), BF16)]
    copies = (
        4 * fsdp_size + grid.z_size + grid.z_size * grid.y_size
        + grid.z_size + grid.y_size + grid.x_size + 1
    )
    started = pl.pallas_call(
        partial(
            start_kernel, lanes=lanes, heads=heads, width=width, head_count=head_count,
            experts=experts, capacity=capacity, local=local, late=late,
        ),
        out_shape=tuple(
            [
                shape_of((fsdp_size, rows, model_width), BF16),
                shape_of((grid.z_size, grid.y_size, fsdp_size, feature_rows, lanes.width), BF16),
                shape_of((exp_size, local * capacity - late_rows, model_width), BF16),
                shape_of((8, rows), F32),
                shape_of((rows, 128), F32),
                shape_of((grid.z_size, grid.y_size, chips, 2, feature_rows, model_width), BF16),
            ]
            + [shape_of((exp_size, late_rows, model_width), BF16)] * late
            + shard_shapes * local
        ),
        in_specs=[IN_VMEM] * 10 + [ANYWHERE] * 2,
        out_specs=tuple(
            [ANYWHERE, ANYWHERE, IN_VMEM, IN_VMEM, IN_VMEM, ANYWHERE]
            + [IN_VMEM] * late
            + [ANYWHERE] * (2 * local)
        ),
        scratch_shapes=[
            pltpu.VMEM((fsdp_size, feature_rows, lanes.width), BF16),
            pltpu.VMEM(expert_up.shape, BF16),
            pltpu.VMEM(expert_down.shape, BF16),
            dma_sems(copies),
            dma_sems(copies),
            dma_sems(3),
            dma_sems(2 * local),
            dma_sems(local * (fsdp_size + 1)),
        ],
        compiler_params=params(collective_id=0, has_side_effects=True),
        cost_estimate=hint(20),
        name="start",
    )(
        tokens, cotangent, routes.T, slots.T, gain_row, mixture_gain.reshape(1, feature_rows),
        attention_in, router_weight.T, position_table, attention_out, expert_up, expert_down,
    )
    all_tokens, all_planes, cotangent_early, position_rows, columns, full_out = started[:6]
    cotangent_late, started = started[6 : 6 + late], started[6 + late :]
    own_shards = [started[2 * index : 2 * index + 2] for index in range(local)]
    plane = all_planes.reshape(model_width, lanes.width)
    full_out = full_out.reshape(model_width, model_width)

    def along_x(array):
        return [over_x(array, -hop) for hop in range(1, chips)]

    near_up, near_down = [None] * local, [None] * local
    near_up[0] = along_x(own_shards[0][0])
    cotangent_in = lax.all_to_all(
        cotangent_early, "exp", split_axis=0, concat_axis=0, tiled=True
    )

    head_t = lambda size: pl.BlockSpec((heads, size, rows), lambda s, *_: (0, 0, s))
    head_n = lambda size: pl.BlockSpec((heads, rows, size), lambda s, *_: (0, s, 0))
    normed, query_t, key_n, query_n, value_n, key_t, value_t, bias, counts = pl.pallas_call(
        partial(
            project_kernel, heads=heads, width=width, lanes=lanes, feature_rows=feature_rows,
            bucket_rows=bucket_rows,
        ),
        grid=(fsdp_size,),
        in_specs=[
            pl.BlockSpec((1, rows, model_width), lambda s: (s, 0, 0)),
            whole((model_width, lanes.width)),
            pl.BlockSpec((1, rows), lambda s: (0, s)),
        ],
        out_specs=[
            pl.BlockSpec((rows, model_width), lambda s: (s, 0)),
            head_t(SKEW), head_n(SKEW), head_n(width), head_n(width), head_t(width), head_t(width),
            whole((heads, 1, span)),
            whole((8, lanes.extra)),
        ],
        out_shape=(
            shape_of((length, model_width), BF16),
            shape_of((heads, SKEW, length), BF16),
            shape_of((heads, length, SKEW), BF16),
            shape_of((heads, length, width), BF16),
            shape_of((heads, length, width), BF16),
            shape_of((heads, width, length), BF16),
            shape_of((heads, width, length), BF16),
            shape_of((heads, 1, span), F32),
            shape_of((8, lanes.extra), F32),
        ),
        scratch_shapes=[
            pltpu.VMEM((lanes.weights, model_width), BF16),
            pltpu.VMEM((lanes.extra, span), F32),
        ],
        compiler_params=params(),
        cost_estimate=hint(8),
        name="project",
    )(all_tokens, plane, segments.reshape(1, length))

    by_head = lambda *size: pl.BlockSpec((1,) + size, lambda h: (h, 0, 0))
    context, context_high, log_total, attended_t = pl.pallas_call(
        partial(attend_kernel, rows=rows),
        grid=(heads,),
        in_specs=[
            by_head(SKEW, length), by_head(length, SKEW), by_head(width, length), by_head(1, span),
        ],
        out_specs=[
            pl.BlockSpec((fsdp_size, width, rows), lambda h: (0, h, 0)),
            by_head(width, length),
            by_head(1, length),
            ANYWHERE,
        ],
        out_shape=(
            shape_of((fsdp_size, heads * width, rows), BF16),
            shape_of((heads, width, length), F32),
            shape_of((heads, 1, length), F32),
            shape_of((fsdp_size, heads * width, rows), BF16),
        ),
        scratch_shapes=[
            pltpu.VMEM((SKEW, span), F32),
            pltpu.VMEM((WINDOW + QUERY_BLOCK, QUERY_BLOCK), F32),
            pltpu.VMEM((heads, fsdp_size, width, rows), BF16),
            pltpu.SemaphoreType.DMA((heads, fsdp_size)),
            pltpu.SemaphoreType.DMA((heads, fsdp_size)),
            dma_sems(heads),
        ],
        compiler_params=params(collective_id=1, has_side_effects=True),
        cost_estimate=hint(13),
        name="attend",
    )(query_t, key_n, value_t, bias)

    own_down, near_up[0], attended_t = lax.optimization_barrier(
        (own_shards[0][1], near_up[0], attended_t)
    )
    near_down[0] = along_x(own_down)
    attended_t = attended_t.reshape(padded_heads * width, rows)

    later = [own_shards[index] for index in range(1, local)]
    attended_t, later = lax.optimization_barrier((attended_t, later))
    for index in range(1, local):
        near_up[index], near_down[index] = [along_x(array) for array in later[index - 1]]
    gate_lanes = -(-local * capacity // 128) * 128
    ready = [own_shards[0][0]] + near_up[0] + [own_shards[0][1]]
    copies = 2 * exp_size + len(ready)
    hidden, routed, probabilities, gates, outgoing, rows_in, gates_in, *crossed = pl.pallas_call(
        partial(
            route_kernel, experts=experts, lanes=lanes, capacity=capacity, crossing=len(ready)
        ),
        in_specs=[IN_VMEM] * 6 + [ANYWHERE] * len(ready),
        out_specs=tuple([IN_VMEM] * 5 + [ANYWHERE] * (2 + len(ready))),
        out_shape=tuple(
            [
                shape_of((rows, model_width), F32),
                shape_of((rows, model_width), BF16),
                shape_of((rows, lanes.extra), F32),
                shape_of((rows, 2), F32),
                shape_of((exp_size, local * capacity, model_width), BF16),
                shape_of((exp_size, capacity, model_width), BF16),
                shape_of((exp_size, 8, gate_lanes), F32),
            ]
            + [shape_of(array.shape, BF16) for array in ready]
        ),
        scratch_shapes=[
            pltpu.VMEM((exp_size, 8, gate_lanes), F32),
            dma_sems(copies),
            dma_sems(copies),
            dma_sems(2),
        ],
        compiler_params=params(collective_id=2, has_side_effects=True),
        cost_estimate=hint(35),
        name="route",
    )(tokens, attended_t, full_out, plane, columns, position_rows, *ready)
    outgoing = outgoing.reshape(exp_size, local, capacity, model_width)

    def down_parts(*parts):
        return list(zip(*parts))

    def pass_along(arrays):
        return [over_x(arrays[0][hop - 1], hop) for hop in range(1, chips)]

    swapped = (crossed[:-1], crossed[-1:])
    returned, groups, moved, outs = [], [], [], None
    late_rows_in = ()
    for index in range(local):
        final = index == local - 1
        carried = list(moved)
        if not final:
            carried.append((outgoing, index + 1))
        if index == 0 and late:
            carried.append((cotangent_late[0], None))
        result = run_expert(
            index, local, rows_in, gates_in, cotangent_in, late_rows_in if final else (),
            [own_shards[index][0]] + near_up[index], [own_shards[index][1]] + near_down[index],
            swapped, () if final else own_shards[index + 1], carried, outs, 3 + index,
        )
        (outs,) = result.rows_out
        arrived = list(result.moved_to)
        if index == 0 and late:
            late_rows_in = (arrived.pop(),)
        if not final:
            rows_in = arrived.pop()
            swapped = (result.next_swapped[:1], result.next_swapped[1:])
            moved = [(result.grad_rows[0], None), (result.grad_gates[0], None)]
        if arrived:
            returned.append(arrived)
        up_keep, up_taken, down_keep, down_taken = result.own
        if not final:
            passed = (result.pass_up, result.pass_down)
            passed, rows_in = lax.optimization_barrier((passed, rows_in))
            groups.append(
                [
                    (up_keep, up_taken, pass_along(passed[0])),
                    (down_keep, down_taken, pass_along(passed[1])),
                ]
            )
    returned.append([result.back_rows[0], result.back_gates[0]])
    groups, returned = lax.optimization_barrier((groups, returned))

    outs, returned = lax.optimization_barrier((outs, returned))
    out_rows = lax.all_to_all(outs, "exp", split_axis=0, concat_axis=0, tiled=True)

    padded_out = full_out
    if padded_heads > head_count:
        padded_out = jnp.pad(full_out, ((0, padded_heads * width - model_width), (0, 0)))
    copies = 2 * 2 * fsdp_size
    grad_hidden, small, grad_t, grad_n, out_grad = pl.pallas_call(
        partial(
            unroute_kernel, experts=experts, local=local, token_total=token_total, lanes=lanes,
            heads=heads, width=width,
        ),
        out_shape=(
            shape_of((rows, model_width), F32),
            shape_of((model_width, lanes.extra), F32),
            shape_of((heads, width, length), BF16),
            shape_of((heads, length, width), BF16),
            shape_of((heads * width, model_width), BF16),
        ),
        in_specs=[IN_VMEM] * 8 + [ANYWHERE] + [IN_VMEM] * (1 + 2 * local),
        out_specs=tuple([IN_VMEM] * 5),
        scratch_shapes=[
            pltpu.VMEM((fsdp_size, rows, model_width), BF16),
            pltpu.VMEM((heads * width, model_width), BF16),
            pltpu.VMEM((heads * width, model_width), F32),
            dma_sems(copies),
            dma_sems(copies),
            dma_sems(1),
        ],
        compiler_params=params(collective_id=4 + local, has_side_effects=True),
        cost_estimate=hint(1),
        name="unroute",
    )(
        hidden, cotangent, routed, probabilities, gates, plane, columns, counts, padded_out, context,
        *[part[0] for part in returned], *[part[1] for part in returned],
    )
    middle = pass_along(result.middle_down)
    middle, pass_up, pass_down, grad_t = lax.optimization_barrier(
        (middle, result.pass_up, result.pass_down, grad_t)
    )
    early = [result.early_down[0][hop] for hop in range(chips - 1)]
    groups.append(
        [
            (up_keep, up_taken, pass_along(pass_up)),
            (down_keep, down_taken, down_parts(early, middle, pass_along(pass_down))),
        ]
    )

    grad_projected, grad_bias = pl.pallas_call(
        partial(attend_back_kernel, scale=width ** (-0.5)),
        grid=(heads,),
        in_specs=[
            by_head(SKEW, length), by_head(length, SKEW), by_head(length, width),
            by_head(length, width), by_head(width, length), by_head(width, length),
            by_head(length, width), by_head(width, length), by_head(1, length), by_head(1, span),
        ],
        out_specs=[
            pl.BlockSpec((3, 1, width, length), lambda h: (0, h, 0, 0)),
            by_head(1, span),
        ],
        out_shape=(
            shape_of((3, heads, width, length), BF16),
            shape_of((heads, 1, span), F32),
        ),
        scratch_shapes=[
            pltpu.VMEM((SKEW, span), F32),
            pltpu.VMEM((SKEW, span), F32),
            pltpu.VMEM((length, width), F32),
            pltpu.VMEM((length, width), F32),
        ],
        compiler_params=params(),
        cost_estimate=hint(1),
        name="attend_back",
    )(query_t, key_n, query_n, value_n, key_t, grad_t, grad_n, context_high, log_total, bias)
    grad_projected = grad_projected.reshape(lanes.weights, length)

    grad_first, grad_plane = pl.pallas_call(
        partial(
            project_back_kernel, lanes=lanes, heads=heads, feature_rows=feature_rows,
            bucket_rows=bucket_rows,
        ),
        grid=(fsdp_size,),
        in_specs=[
            pl.BlockSpec((lanes.weights, rows), lambda s: (0, s)),
            pl.BlockSpec((rows, model_width), lambda s: (s, 0)),
            whole((model_width, lanes.width)),
            whole((model_width, lanes.extra)),
            whole((rows, lanes.extra)),
            whole((heads, 1, span)),
        ],
        out_specs=[
            pl.BlockSpec((1, model_width, rows), lambda s: (s, 0, 0)),
            whole((model_width, lanes.width)),
        ],
        out_shape=(
            shape_of((fsdp_size, model_width, rows), BF16),
            shape_of((model_width, lanes.width), BF16),
        ),
        scratch_shapes=[
            pltpu.VMEM((lanes.width, model_width), F32),
            pltpu.VMEM((lanes.extra, span), F32),
        ],
        compiler_params=params(),
        cost_estimate=hint(1),
        name="project_back",
    )(grad_projected, normed, plane, small, probabilities, grad_bias)

    out_rows, grad_first = lax.optimization_barrier((out_rows, grad_first))
    spread_out = heads * width * fsdp_size != model_width
    if spread_out:
        out_grad = lax.dynamic_update_slice(
            jnp.zeros((padded_heads * width, model_width), BF16), out_grad,
            (fsdp_index * heads * width, jnp.int32(0)),
        )[:model_width]
    out_grad = out_grad.reshape(-1, feature_rows, model_width)
    out_count = device_count if spread_out else exp_size
    plane_shape = (grid.z_size, grid.y_size, fsdp_size, feature_rows, lanes.width)
    parts_shape = (fsdp_size, feature_rows, lanes.width)
    copies = 4 * fsdp_size + grid.z_size * grid.y_size + grid.z_size + out_count
    first_parts, layer_output, plane_parts, out_parts = pl.pallas_call(
        partial(last_kernel, spread_out=spread_out, local=local),
        out_shape=(
            shape_of((chips, model_width, rows), BF16),
            shape_of((rows, model_width), BF16),
            shape_of(parts_shape, BF16),
            shape_of((out_count, feature_rows, model_width), BF16),
        ),
        in_specs=[IN_VMEM] * 6 + [ANYWHERE],
        out_specs=(IN_VMEM, IN_VMEM, ANYWHERE, ANYWHERE),
        scratch_shapes=[
            pltpu.VMEM((chips, model_width, rows), BF16),
            pltpu.VMEM((max(chips - 1, 1), model_width, rows), BF16),
            pltpu.VMEM((max(grid.y_size - 1, 1), grid.z_size) + parts_shape, BF16),
            pltpu.VMEM((grid.z_size,) + parts_shape, BF16),
            pltpu.VMEM((max(grid.z_size - 1, 1),) + parts_shape, BF16),
            pltpu.VMEM(parts_shape, BF16),
            pltpu.VMEM(out_rows.shape, BF16),
            dma_sems(copies),
            dma_sems(copies),
            dma_sems(3),
        ],
        compiler_params=params(collective_id=5 + local, has_side_effects=True),
        cost_estimate=hint(1),
        name="last",
    )(grad_first, grad_plane.reshape(plane_shape), out_grad, hidden, gates, columns, out_rows)

    groups, first_parts = lax.optimization_barrier((groups, first_parts))
    (
        grad_tokens, gain_grad, in_grad, out_sum, mixture_gain_grad, router_grad, table_grad, balance,
    ) = pl.pallas_call(
        partial(
            finish_kernel, lanes=lanes, heads=heads, width=width, head_count=head_count,
            experts=experts, token_total=token_total,
        ),
        out_shape=(
            shape_of((rows, model_width), F32),
            shape_of((1, feature_rows), F32),
            shape_of((feature_rows, 3 * model_width), F32),
            shape_of((feature_rows, model_width), F32),
            shape_of((1, feature_rows), F32),
            shape_of((experts, feature_rows), F32),
            shape_of((bucket_rows, head_count), F32),
            shape_of((1, 1), F32),
        ),
        compiler_params=params(),
        cost_estimate=hint(6),
        name="finish",
    )(first_parts, plane_parts, out_parts, tokens, grad_hidden, attention_in, gain_row, counts)

    up_grad, down_grad = sum_grads(groups, expert_up.shape, expert_down.shape, fsdp_size)
    return (
        layer_output,
        balance.reshape(()),
        grad_tokens,
        gain_grad.reshape(feature_rows),
        mixture_gain_grad.reshape(feature_rows),
        in_grad,
        out_sum,
        router_grad.T,
        table_grad,
        up_grad,
        down_grad,
    )


def solution(mesh):
    in_specs = (
        P(("exp", "fsdp"), None),
        P(("exp", "fsdp"), None),
        P("exp"),
        P(("exp", "fsdp"), None),
        P(("exp", "fsdp"), None),
        P(("exp", "fsdp")),
        P(("exp", "fsdp")),
        P(("exp", "fsdp"), None),
        P(("exp", "fsdp"), None),
        P(("exp", "fsdp"), None),
        P(("exp", "fsdp"), None),
        P("exp", "fsdp", None),
        P("exp", "fsdp", None),
    )
    out_specs = (
        P(("exp", "fsdp"), None),
        P(),
        P(("exp", "fsdp"), None),
        P(("exp", "fsdp")),
        P(("exp", "fsdp")),
        P(("exp", "fsdp"), None),
        P(("exp", "fsdp"), None),
        P(("exp", "fsdp"), None),
        P(("exp", "fsdp"), None),
        P("exp", "fsdp", None),
        P("exp", "fsdp", None),
    )
    return jax.shard_map(
        on_device, mesh=mesh, in_specs=in_specs, out_specs=out_specs, check_vma=False
    )
```

```python
from functools import partial

import jax
import jax.numpy as jnp
from jax import lax
from jax.experimental import pallas as pl
from jax.experimental.pallas import tpu as pltpu
from jax.sharding import PartitionSpec as P

WINDOW = 1024
BUCKETS = 256

EPSILON = 1e-06
AUX_WEIGHT = 0.01
MASKED = -1e30
QUERY_BLOCK = 256
SKEW = 128
VMEM_BYTES = 58 * 1024 * 1024
MESH = pl.DeviceIdType.MESH
F32 = jnp.float32
BF16 = jnp.bfloat16


def params(**kwargs):
    return pltpu.CompilerParams(vmem_limit_bytes=VMEM_BYTES, **kwargs)


def shape_of(shape, dtype):
    return jax.ShapeDtypeStruct(shape, dtype)


def whole(shape):
    return pl.BlockSpec(shape, lambda *_: (0,) * len(shape))


def contract_last(left_side, right_side):
    return lax.dot_general(
        left_side, right_side, (((1,), (1,)), ((), ())), preferred_element_type=F32
    )


def matmul(left_side, right_side):
    return jnp.dot(left_side, right_side, preferred_element_type=F32)


def turned(value):
    return value.astype(F32).T


def bucket_index(distance):
    near_count = BUCKETS // 2
    spread = max(WINDOW - near_count, 1)
    far_bucket = (
        near_count + jnp.maximum(distance - near_count, 0) * (BUCKETS - near_count) // spread
    )
    return jnp.where(distance < near_count, distance, far_bucket)

def hint(micros):
    return pl.CostEstimate(flops=int(micros * 1.0e9), bytes_accessed=1024, transcendentals=0)


def flipped(place, other, size):
    result, bit = 0, 1
    while bit < size:
        result = result + bit * ((place // bit + other // bit) % 2)
        bit *= 2
    return result


class Grid:
    def __init__(self):
        self.exp_size, self.fsdp_size = lax.axis_size("exp"), lax.axis_size("fsdp")
        self.device_count = self.exp_size * self.fsdp_size
        self.y_size = max(
            y for y in range(1, self.exp_size + 1) if self.exp_size % y == 0 and 2 * y * y <= self.exp_size
        ) if self.exp_size > 1 else 1
        self.z_size = self.exp_size // self.y_size
        self.x_size = self.fsdp_size // 2

    def here(self):
        self.exp, self.fsdp = lax.axis_index("exp"), lax.axis_index("fsdp")
        self.z, self.y = self.exp // self.y_size, self.exp % self.y_size
        self.x, self.core = self.fsdp // 2, self.fsdp % 2
        self.linear = self.exp * self.fsdp_size + self.fsdp
        return self

    def at(self, z=None, y=None, fsdp=None):
        z = self.z if z is None else z
        y = self.y if y is None else y
        return (z * self.y_size + y, self.fsdp if fsdp is None else fsdp)

    def x_from(self, hop):
        return ((self.x + self.x_size + hop) % self.x_size) * 2 + self.core

    def source_z(self, turn):
        if self.z_size & (self.z_size - 1) == 0:
            return flipped(self.z, turn, self.z_size)
        return (self.z + turn) % self.z_size

    def target_z(self, turn):
        if self.z_size & (self.z_size - 1) == 0:
            return flipped(self.z, turn, self.z_size)
        return (self.z + self.z_size - turn) % self.z_size

    def exp_steps(self):
        turns = sorted(range(self.z_size), key=lambda turn: -turn.bit_length())
        steps = []
        for turn in turns:
            for hop in range(self.y_size):
                if turn or hop:
                    to = self.target_z(turn) * self.y_size + (self.y + self.y_size - hop) % self.y_size
                    origin = self.source_z(turn) * self.y_size + (self.y + hop) % self.y_size
                    steps.append((to, origin))
        return steps

    def sibling(self, fsdp):
        return fsdp + 1 - 2 * (fsdp % 2)


class Links:
    def __init__(self, send, receive):
        self.send, self.receive, self.used = send, receive, 0

    def copy(self, source, target, device, landing):
        index = self.used
        self.used += 1
        going = pltpu.make_async_remote_copy(
            src_ref=source, dst_ref=target, send_sem=self.send.at[index],
            recv_sem=self.receive.at[index], device_id=device, device_id_type=MESH,
        )
        coming = pltpu.make_async_remote_copy(
            src_ref=landing, dst_ref=landing, send_sem=self.send.at[index],
            recv_sem=self.receive.at[index], device_id=device, device_id_type=MESH,
        )
        return going, coming


def greet(devices):
    barrier = pltpu.get_barrier_semaphore()
    for device in devices:
        pl.semaphore_signal(barrier, inc=1, device_id=device, device_id_type=MESH)
    pl.semaphore_wait(barrier, len(devices))


def chip_peers(grid):
    peers = [(grid.exp, grid.sibling(grid.fsdp))]
    return peers + [(grid.exp, grid.x_from(hop)) for hop in range(1, grid.x_size)]


class ChipGather:
    def __init__(self, grid, links, own_sem, source, target):
        self.grid, self.links, self.target = grid, links, target
        self.own = pltpu.make_async_copy(source, target.at[grid.fsdp], own_sem)
        sibling = grid.sibling(grid.fsdp)
        self.along_x, self.across = [], []
        for hop in range(1, grid.x_size):
            self.along_x.append(
                links.copy(
                    source, target.at[grid.fsdp], (grid.exp, grid.x_from(hop)),
                    target.at[grid.x_from(-hop)],
                )
            )
        self.across.append(
            links.copy(source, target.at[grid.fsdp], (grid.exp, sibling), target.at[sibling])
        )

    def start(self):
        for going, _ in self.along_x + self.across:
            going.start()
        self.own.start()

    def forward(self):
        grid = self.grid
        for hop in range(1, grid.x_size):
            self.along_x[hop - 1][1].wait_recv()
            held = grid.x_from(-hop)
            other = grid.sibling(held)
            self.across.append(
                self.links.copy(
                    self.target.at[held], self.target.at[held],
                    (grid.exp, grid.sibling(grid.fsdp)), self.target.at[other],
                )
            )
            self.across[-1][0].start()

    def finish(self):
        for _, coming in self.across:
            coming.wait_recv()
        for going, _ in self.along_x + self.across:
            going.wait_send()
        self.own.wait()


class Exchange:
    def __init__(self, grid, links, own_sems, pairs):
        self.steps = grid.exp_steps()
        self.peers = [(to, grid.fsdp) for to, _ in self.steps]
        self.copies, self.own = [], []
        for index, (source, target) in enumerate(pairs):
            for to, origin in self.steps:
                self.copies.append(
                    links.copy(
                        source(to), target.at[grid.exp], (to, grid.fsdp), target.at[origin]
                    )
                )
            self.own.append(
                pltpu.make_async_copy(source(grid.exp), target.at[grid.exp], own_sems.at[index])
            )

    def start(self):
        for going, _ in self.copies:
            going.start()
        for own in self.own:
            own.start()

    def finish(self):
        for going, coming in self.copies:
            coming.wait_recv()
            going.wait_send()
        for own in self.own:
            own.wait()


ANYWHERE = pl.BlockSpec(memory_space=pl.ANY)
IN_VMEM = pl.BlockSpec(memory_space=pltpu.VMEM)


def dma_sems(count):
    return pltpu.SemaphoreType.DMA((count,))


def plane_of(source, part, to):
    return source.at[to] if part is None else source.at[to, part]


class Lanes:
    def __init__(self, heads, width, padded_heads, experts):
        self.weights = 3 * heads * width
        self.base = self.weights // 128 * 128
        self.router = self.weights - self.base
        self.gain = self.router + experts
        self.table = self.gain + 1
        self.count = self.table + padded_heads
        self.width = -(-(self.weights + 2 * experts + 1 + padded_heads) // 128) * 128
        self.extra = self.width - self.base
        self.shift = self.count - self.router


def bucket_rows_select(features, feature_rows, bucket_rows, span):
    row = lax.broadcasted_iota(jnp.int32, (features, 1), 0)
    within = lax.rem(row, feature_rows)
    bucket = jnp.where(
        within < bucket_rows, lax.div(row, feature_rows) * bucket_rows + within, -1
    )
    distance = lax.broadcasted_iota(jnp.int32, (1, span), 1) - SKEW
    near = BUCKETS // 2
    spread = max(WINDOW - near, 1)
    far = near + lax.div(jnp.maximum(distance - near, 0) * (BUCKETS - near), spread)
    wanted = jnp.where(distance < near, distance, far)
    reachable = (distance >= 0) & (distance < WINDOW)
    wanted = jnp.where(reachable, wanted, -2)
    return jnp.where(bucket == wanted, 1.0, 0.0).astype(BF16), reachable


def as_column(row, size):
    row_place = lax.broadcasted_iota(jnp.int32, (size, size), 0)
    lane = lax.broadcasted_iota(jnp.int32, (size, size), 1)
    spread = jnp.broadcast_to(row.astype(F32), (size, size))
    return jnp.sum(jnp.where(row_place == lane, spread, 0.0), axis=1, keepdims=True)


def padded_rows(value, rows):
    if value.shape[0] == rows:
        return value
    return jnp.concatenate([value, jnp.zeros((rows - value.shape[0], value.shape[1]), F32)], axis=0)


def padded_lanes(value, lanes):
    if value.shape[1] == lanes:
        return value
    return jnp.concatenate([value, jnp.zeros((value.shape[0], lanes - value.shape[1]), F32)], axis=1)


class Wide:
    def __init__(self, grid, links, own_sem, source, target):
        self.grid, self.links, self.target = grid, links, target
        self.own = pltpu.make_async_copy(
            source, target.at[grid.z, grid.y, grid.x, grid.core], own_sem
        )
        stage = []
        for hop in range(1, grid.z_size):
            origin = (grid.z + grid.z_size - hop) % grid.z_size
            stage.append(
                links.copy(
                    source, target.at[grid.z, grid.y, grid.x, grid.core],
                    grid.at(z=(grid.z + hop) % grid.z_size),
                    target.at[origin, grid.y, grid.x, grid.core],
                )
            )
        self.stages = [stage]

    def start(self):
        self.own.start()
        for going, _ in self.stages[0]:
            going.start()

    def turn(self, axis):
        grid, target = self.grid, self.target
        for _, coming in self.stages[-1]:
            coming.wait_recv()
        stage = []
        if axis == 0:
            self.own.wait()
            held = target.at[:, grid.y, grid.x, grid.core]
            for hop in range(1, grid.y_size):
                origin = (grid.y + grid.y_size - hop) % grid.y_size
                stage.append(
                    self.links.copy(
                        held, held, grid.at(y=(grid.y + hop) % grid.y_size),
                        target.at[:, origin, grid.x, grid.core],
                    )
                )
        elif axis == 1:
            held = target.at[:, :, grid.x, grid.core]
            for hop in range(1, grid.x_size):
                origin = (grid.x + grid.x_size - hop) % grid.x_size
                stage.append(
                    self.links.copy(
                        held, held, (grid.exp, grid.x_from(hop)),
                        target.at[:, :, origin, grid.core],
                    )
                )
        else:
            held = target.at[:, :, :, grid.core]
            stage.append(
                self.links.copy(
                    held, held, (grid.exp, grid.sibling(grid.fsdp)), target.at[:, :, :, 1 - grid.core]
                )
            )
        for going, _ in stage:
            going.start()
        self.stages.append(stage)

    def finish(self):
        for _, coming in self.stages[-1]:
            coming.wait_recv()
        for stage in self.stages:
            for going, _ in stage:
                going.wait_send()


def start_kernel(
    tokens, cotangent, routes_t, slots_t, attention_gain, mixture_gain, attention_in, router_t, table,
    attention_out, expert_up, expert_down, *refs, lanes, heads, width, head_count, experts, capacity,
    local, late,
):
    all_tokens, all_planes, cotangent_early, position_rows, columns, full_out = refs[:6]
    cotangent_late, refs = refs[6 : 6 + late], refs[6 + late :]
    shards = refs[: 2 * local]
    planes, up_stage, down_stage, send, receive, own, fetch, split = refs[2 * local :]
    grid = Grid().here()
    links = Links(send, receive)
    z_size, y_size, fsdp_size = grid.z_size, grid.y_size, grid.fsdp_size
    near = [
        (grid.exp, (grid.fsdp + turn) % fsdp_size) for turn in range(1, fsdp_size)
    ] + [grid.at(z=(grid.z + hop) % z_size) for hop in range(1, z_size)]
    beside = [grid.at(y=(grid.y + hop) % y_size) for hop in range(1, y_size)]
    gathered = ChipGather(grid, links, own.at[0], tokens, all_tokens)
    widely = Wide(grid, links, own.at[2], attention_out, full_out)
    part = expert_down.shape[1]
    depth = expert_up.shape[1]
    fetches = []
    for index in range(local):
        fetches.append(
            pltpu.make_async_copy(expert_up.at[index], up_stage.at[index], fetch.at[2 * index])
        )
        fetches.append(
            pltpu.make_async_copy(
                expert_down.at[index], down_stage.at[index], fetch.at[2 * index + 1]
            )
        )
    greet(near + beside)
    widely.start()
    for copy in fetches:
        copy.start()

    feature_rows = attention_in.shape[0]
    model_width = head_count * width
    gained = attention_in[...].astype(F32) * as_column(attention_gain[...], feature_rows)
    route_rows, slot_rows = routes_t[...].astype(F32), slots_t[...].astype(F32)
    columns[...] = padded_rows(jnp.concatenate([route_rows, slot_rows], axis=0), 128).T
    row_count = columns.shape[0]
    expert_lanes = lax.broadcasted_iota(jnp.int32, (row_count, experts), 1).astype(F32)
    named = jnp.zeros((row_count, experts), F32)
    for k in range(2):
        named = named + jnp.where(expert_lanes == columns[:, k : k + 1], 1.0, 0.0)
    named = jnp.sum(named, axis=0, keepdims=True)
    place = lax.broadcasted_iota(jnp.int32, (feature_rows, feature_rows), 0)
    same = place == lax.broadcasted_iota(jnp.int32, (feature_rows, feature_rows), 1)
    router = contract_last(jnp.where(same, 1.0, 0.0).astype(BF16), router_t[...])
    pieces = [
        router,
        as_column(mixture_gain[...], feature_rows),
        padded_rows(padded_lanes(table[...].astype(F32), heads * fsdp_size), feature_rows),
        padded_rows(named, feature_rows),
    ]
    taken = sum(piece.shape[1] for piece in pieces)
    if lanes.width > lanes.weights + taken:
        pieces.append(jnp.zeros((feature_rows, lanes.width - lanes.weights - taken), F32))
    for place in range(fsdp_size):
        first, last = place * heads * width, min((place + 1) * heads * width, model_width)
        own_pieces = []
        for kind in range(3):
            if last > first:
                own_pieces.append(gained[:, kind * model_width + first : kind * model_width + last])
            if last - first < heads * width:
                own_pieces.append(
                    jnp.zeros((feature_rows, heads * width - max(last - first, 0)), F32)
                )
        planes[place] = jnp.concatenate(own_pieces + pieces, axis=1).astype(BF16)
    placed = []
    for turn in range(1, fsdp_size):
        to = (grid.fsdp + turn) % fsdp_size
        origin = (grid.fsdp + fsdp_size - turn) % fsdp_size
        placed.append(
            links.copy(
                planes.at[to], all_planes.at[grid.z, grid.y, grid.fsdp], (grid.exp, to),
                all_planes.at[grid.z, grid.y, origin],
            )
        )
        placed[-1][0].start()
    kept = pltpu.make_async_copy(
        planes.at[grid.fsdp], all_planes.at[grid.z, grid.y, grid.fsdp], own.at[1]
    )
    kept.start()
    gathered.start()
    for _, coming in placed:
        coming.wait_recv()
    kept.wait()

    def over_y(z):
        for turn in range(1, y_size):
            forwarded.append(
                links.copy(
                    all_planes.at[z, grid.y],
                    all_planes.at[z, grid.y],
                    grid.at(y=(grid.y + turn) % y_size),
                    all_planes.at[z, (grid.y + y_size - turn) % y_size],
                )
            )
            forwarded[-1][0].start()

    along_z, forwarded = [], []
    for hop in range(1, z_size):
        along_z.append(
            links.copy(
                all_planes.at[grid.z, grid.y],
                all_planes.at[grid.z, grid.y],
                grid.at(z=(grid.z + hop) % z_size),
                all_planes.at[(grid.z + z_size - hop) % z_size, grid.y],
            )
        )
        along_z[-1][0].start()
    over_y(grid.z)
    widely.turn(0)

    for copy in fetches:
        copy.wait()
    splits = []
    for index in range(local):
        up, down = shards[2 * index : 2 * index + 2]
        stores = [
            (
                up_stage.at[index, :, pl.ds(block * part, part)],
                up.at[pl.ds(block * depth, depth), :],
            )
            for block in range(fsdp_size)
        ]
        for source, target in stores + [(down_stage.at[index], down)]:
            splits.append(pltpu.make_async_copy(source, target, split.at[len(splits)]))
            splits[-1].start()

    widely.turn(1)

    place = route_rows * capacity + slot_rows
    position_rows[...] = padded_rows(place, 8)
    select_rows([cotangent_early] + list(cotangent_late), place, cotangent[...])

    for hop in range(1, z_size):
        along_z[hop - 1][1].wait_recv()
        over_y((grid.z + z_size - hop) % z_size)
    gathered.forward()
    widely.turn(2)
    for going, coming in forwarded:
        coming.wait_recv()
        going.wait_send()
    for going, _ in placed + along_z:
        going.wait_send()
    gathered.finish()
    widely.finish()
    for copy in splits:
        copy.wait()


def project_kernel(
    tokens, plane, segments, normed, query_t, key_n, query_n, value_n, key_t, value_t, bias, counts,
    weight_t, table_t, *, heads, width, lanes, feature_rows, bucket_rows,
):
    @pl.when(pl.program_id(0) == 0)
    def _():
        weight_t[...] = turned(plane[:, : lanes.weights]).astype(BF16)
        extra = plane[:, lanes.base :]
        span = bias.shape[2]
        select, reachable = bucket_rows_select(plane.shape[0], feature_rows, bucket_rows, span)
        table_t[...] = lax.dot_general(
            extra, select, (((0,), (0,)), ((), ())), preferred_element_type=F32
        )
        first = lanes.table + lax.axis_index("fsdp") * heads
        for head in range(heads):
            bias[head] = jnp.where(reachable, table_t[pl.ds(first + head, 1), :], MASKED)
        summed = jnp.sum(extra.astype(F32), axis=0, keepdims=True)
        counts[...] = pltpu.roll(
            jnp.broadcast_to(summed, counts.shape), lanes.extra - lanes.shift, 1
        )

    inputs = tokens[0].astype(F32)
    scale = lax.rsqrt(jnp.mean(inputs * inputs, axis=1, keepdims=True) + EPSILON)
    low = (inputs * scale).astype(BF16)
    normed[...] = low
    rows = low.shape[0]
    projected = contract_last(weight_t[...], low).astype(BF16).astype(F32)
    document = segments[...] % 4
    places = lax.broadcasted_iota(jnp.int32, (8, rows), 0)
    same = places == document
    hot = jnp.where(same, 1.0, 0.0)
    barred = jnp.where(same | (places >= 4), 0.0, MASKED)
    filler = jnp.zeros((SKEW - 8 - width, rows), F32)
    for head in range(heads):
        query = projected[head * width : (head + 1) * width] * width ** (-0.5)
        key = projected[(heads + head) * width : (heads + head + 1) * width]
        value = projected[(2 * heads + head) * width : (2 * heads + head + 1) * width]
        query_t[head] = jnp.concatenate([query, barred, filler], axis=0).astype(BF16)
        key_n[head] = jnp.concatenate([key, hot, filler], axis=0).T.astype(BF16)
        query_n[head] = query.T.astype(BF16)
        value_n[head] = value.T.astype(BF16)
        key_t[head] = key.astype(BF16)
        value_t[head] = value.astype(BF16)


def spans(length):
    for query_start in range(0, length, QUERY_BLOCK):
        key_start = max(0, query_start - WINDOW)
        yield query_start, key_start, query_start + QUERY_BLOCK - key_start


def spread_bias(bias, skew):
    skew[...] = pltpu.roll(
        jnp.broadcast_to(bias[0], skew.shape), 0, 1, stride=1, stride_axis=0
    )


def attend_kernel(
    query_t, key_n, value_t, bias, context, context_high, log_total, attended, skew, scores, held,
    send, receive, own, *, rows,
):
    head = pl.program_id(0)
    width = value_t.shape[1]
    grid = Grid().here()
    fsdp_size = grid.fsdp_size

    def leave(number):
        place = pl.ds(pl.multiple_of(number * width, 16), width)
        copies = []
        for turn in range(1, fsdp_size):
            to = (grid.fsdp + turn) % fsdp_size
            origin = (grid.fsdp + fsdp_size - turn) % fsdp_size
            sems = dict(
                send_sem=send.at[number, turn], recv_sem=receive.at[number, turn],
                device_id=(grid.exp, to), device_id_type=MESH,
            )
            copies.append(
                (
                    pltpu.make_async_remote_copy(
                        src_ref=held.at[number, to], dst_ref=attended.at[grid.fsdp, place, :], **sems
                    ),
                    pltpu.make_async_remote_copy(
                        src_ref=attended.at[origin, place, :], dst_ref=attended.at[origin, place, :],
                        **sems,
                    ),
                )
            )
        kept = pltpu.make_async_copy(
            held.at[number, grid.fsdp], attended.at[grid.fsdp, place, :], own.at[number]
        )
        return copies, kept

    @pl.when(head == 0)
    def _():
        greet([(grid.exp, (grid.fsdp + turn) % fsdp_size) for turn in range(1, fsdp_size)])

    spread_bias(bias, skew)
    for query_start, key_start, key_count in spans(query_t.shape[2]):
        queries = slice(query_start, query_start + QUERY_BLOCK)
        keys = slice(key_start, key_start + key_count)
        raw = matmul(key_n[0, keys, :], query_t[0, :, queries])
        for start in range(0, key_count, SKEW):
            offset = query_start - key_start - start + SKEW
            scores[start : start + SKEW, :] = (
                raw[start : start + SKEW] + skew[:, offset : offset + QUERY_BLOCK]
            )
        high = jnp.max(scores[:key_count, :], axis=0, keepdims=True)
        weights = jnp.exp(scores[:key_count, :] - high)
        total = jnp.sum(weights, axis=0, keepdims=True)
        gathered = matmul(value_t[0, :, keys], weights.astype(BF16)) / total
        context_high[0, :, queries] = gathered
        log_total[0, :, queries] = high + jnp.log(total)
        for start in range(0, QUERY_BLOCK, 128):
            place = query_start + start
            piece = gathered[:, start : start + 128].astype(BF16)
            context[place // rows, :, place % rows : place % rows + 128] = piece
            held[head, place // rows, :, place % rows : place % rows + 128] = piece
    copies, kept = leave(head)
    for going, _ in copies:
        going.start()
    kept.start()

    @pl.when(head == pl.num_programs(0) - 1)
    def _():
        def finish(number, carry):
            copies, kept = leave(number)
            for going, coming in copies:
                coming.wait_recv()
                going.wait_send()
            kept.wait()
            return carry

        lax.fori_loop(0, pl.num_programs(0), finish, 0)


def attend_back_kernel(
    query_t, key_n, query_n, value_n, key_t, grad_t, grad_n, context_high, log_total, bias,
    grad_projected, grad_bias, skew, grad_skew, grad_key, grad_value, *, scale,
):
    spread_bias(bias, skew)
    grad_skew[...] = jnp.zeros_like(grad_skew)
    grad_key[...] = jnp.zeros_like(grad_key)
    grad_value[...] = jnp.zeros_like(grad_value)
    inner = jnp.sum(grad_t[0].astype(F32) * context_high[0], axis=0, keepdims=True)
    for query_start, key_start, key_count in spans(query_t.shape[2]):
        queries = slice(query_start, query_start + QUERY_BLOCK)
        keys = slice(key_start, key_start + key_count)
        raw = matmul(key_n[0, keys, :], query_t[0, :, queries])
        grad_weights = matmul(value_n[0, keys, :], grad_t[0, :, queries])
        weights_low, grad_low = [], []
        for start in range(0, key_count, SKEW):
            offset = query_start - key_start - start + SKEW
            part = slice(start, start + SKEW)
            weights = jnp.exp(
                raw[part] + skew[:, offset : offset + QUERY_BLOCK] - log_total[0, :, queries]
            )
            grad_scores = weights * (grad_weights[part] - inner[:, queries])
            grad_skew[:, offset : offset + QUERY_BLOCK] += grad_scores
            weights_low.append(weights.astype(BF16))
            grad_low.append(grad_scores.astype(BF16))
        weights_low = jnp.concatenate(weights_low, axis=0)
        grad_low = jnp.concatenate(grad_low, axis=0)
        grad_projected[0, 0, :, queries] = (matmul(key_t[0, :, keys], grad_low) * scale).astype(BF16)
        grad_key[keys, :] += matmul(grad_low, query_n[0, queries, :])
        grad_value[keys, :] += matmul(weights_low, grad_n[0, queries, :])
    grad_projected[1, 0] = grad_key[...].T.astype(BF16)
    grad_projected[2, 0] = grad_value[...].T.astype(BF16)
    count = SKEW
    span = skew.shape[1]
    while count > 8:
        count //= 2
        grad_skew[:count, :] += pltpu.roll(grad_skew[count : 2 * count, :], span - count, 1)
    summed = grad_skew[0:1, :]
    for row in range(1, 8):
        summed = summed + pltpu.roll(grad_skew[row : row + 1, :], span - row, 1)
    grad_bias[0] = summed

def expert_lane(shape, lanes):
    return lax.broadcasted_iota(jnp.int32, shape, 1) - lanes.router


def int_columns(columns):
    values = columns[:, 0:4].astype(jnp.int32)
    return values[:, 0:2], values[:, 2:4]


def route_kernel(
    tokens, attended_t, attention_out, plane, columns, position_rows, *refs,
    experts, lanes, capacity, crossing,
):
    over, refs = refs[:crossing], refs[crossing:]
    hidden, routed, probabilities, gates, outgoing, rows_in, gates_in = refs[:7]
    landed, refs = refs[7 : 7 + crossing], refs[7 + crossing :]
    slot_gates, send, receive, own = refs
    grid = Grid().here()
    links = Links(send, receive)
    exp_size = grid.exp_size
    sibling = (grid.exp, grid.sibling(grid.fsdp))
    greet([((grid.exp + hop) % exp_size, grid.fsdp) for hop in range(1, exp_size)] + [sibling])
    swaps = [links.copy(source, target, sibling, target) for source, target in zip(over, landed)]
    for going, _ in swaps:
        going.start()
    rows, model_width = tokens.shape
    routes, slots = int_columns(columns)
    attended_low = turned(attended_t[:model_width]).astype(BF16)
    hidden_state = tokens[...].astype(F32) + matmul(attended_low, attention_out[...])
    hidden[...] = hidden_state
    scale = lax.rsqrt(jnp.mean(hidden_state * hidden_state, axis=1, keepdims=True) + EPSILON)
    extra = plane[:, lanes.base :]
    gain = extra.astype(F32).T[lanes.gain : lanes.gain + 1]
    low = (hidden_state * scale * gain).astype(BF16)
    routed[...] = low
    member_slots = experts // exp_size * capacity
    work = Exchange(
        grid, links, own,
        [
            (lambda to: outgoing.at[to, pl.ds(0, capacity), :], rows_in),
            (partial(plane_of, slot_gates, None), gates_in),
        ],
    )
    for number, to in enumerate([to for to, _ in work.steps] + [grid.exp]):
        slot = lax.broadcasted_iota(jnp.int32, (member_slots, rows), 0) + to * member_slots
        slot = slot.astype(F32)
        picked = (slot == position_rows[0:1, :]) | (slot == position_rows[1:2, :])
        outgoing[to] = matmul(jnp.where(picked, 1.0, 0.0).astype(BF16), low).astype(BF16)
        (work.copies[number][0] if number < len(work.steps) else work.own[0]).start()
    logits = matmul(low, extra)
    lane = expert_lane(logits.shape, lanes)
    logits = jnp.where((lane >= 0) & (lane < experts), logits, MASKED)
    powers = jnp.exp(logits - jnp.max(logits, axis=1, keepdims=True))
    powers = powers / jnp.sum(powers, axis=1, keepdims=True)
    probabilities[...] = powers
    chosen = [
        jnp.sum(jnp.where(lane == routes[:, k : k + 1], powers, 0.0), axis=1, keepdims=True)
        for k in range(2)
    ]
    total = chosen[0] + chosen[1]
    gate_values = [chosen[k] / total for k in range(2)]
    pair = lax.broadcasted_iota(jnp.int32, (rows, 2), 1)
    gates[...] = jnp.where(pair == 0, gate_values[0], gate_values[1])
    gate_lanes = slot_gates.shape[2]
    slot_lanes = lax.broadcasted_iota(jnp.int32, (rows, gate_lanes), 1)
    inside = slot_lanes < member_slots
    places = routes * capacity + slots
    for member in range(exp_size):
        by_slot = jnp.zeros((rows, gate_lanes), F32)
        for k in range(2):
            hit = (slot_lanes + member * member_slots == places[:, k : k + 1]) & inside
            by_slot = by_slot + jnp.where(hit, gate_values[k], 0.0)
        slot_gates[member] = jnp.broadcast_to(
            jnp.sum(by_slot, axis=0, keepdims=True), slot_gates.shape[1:]
        )
    for going, _ in work.copies[exp_size - 1 :]:
        going.start()
    work.own[1].start()
    work.finish()
    for going, coming in swaps:
        coming.wait_recv()
        going.wait_send()


def select_rows(outgoing, position_rows, values):
    rows = values.shape[0]
    sizes = [array.shape[1] for array in outgoing]
    for member in range(outgoing[0].shape[0]):
        slots = lax.broadcasted_iota(jnp.int32, (sum(sizes), rows), 0) + member * sum(sizes)
        slots = slots.astype(F32)
        picked = (slots == position_rows[0:1, :]) | (slots == position_rows[1:2, :])
        found = matmul(jnp.where(picked, 1.0, 0.0).astype(BF16), values).astype(BF16)
        first = 0
        for array, size in zip(outgoing, sizes):
            array[member] = found[first : first + size]
            first += size


def gelu_parts(value):
    magnitude = jnp.abs(value)
    power = jnp.exp2(value * value * -0.7213475204444817)
    base = 1.0 + (0.3275911 * 0.7071067811865476) * magnitude
    step = pl.reciprocal(base, approx=True)
    step = step * (2.0 - base * step)
    series = step * (
        0.127414796
        + step * (-0.142248368 + step * (0.7107068705 + step * (-0.7265760135 + step * 0.5307027145)))
    )
    tail = series * power
    normal = jnp.where(value < 0.0, tail, 1.0 - tail)
    return value * normal, normal + value * (power * 0.3989422804014327)


def expert_kernel(*refs, layout, index, local, half, capacity, parts):
    shards = 2 * half
    refs = Bag(layout, refs)
    grid = Grid().here()
    z_size, y_size = grid.z_size, grid.y_size
    last = index == local - 1
    sibling = (grid.exp, grid.sibling(grid.fsdp))
    links = Links(refs.send[0], refs.receive[0])
    rows_all, cot, up_all, down_all = (
        refs.rows_all[0], refs.cot[0], refs.up_all[0], refs.down_all[0]
    )
    total = refs.total[0]
    if last:
        active, grad_hidden, unscaled = refs.active[0], refs.grad_hidden[0], refs.unscaled[0]
    else:
        grad_total, slot_grad = refs.grad_total[0], refs.slot_grad[0]
    gates, gate_column = refs.gates[0], refs.gate_column[0]
    rows_t, slot_t = refs.rows_t[0], refs.slot_t[0]
    grad_up, grad_down = refs.grad_up[0], refs.grad_down[0]
    grad_rows, grad_gates = refs.grad_rows[0], refs.grad_gates[0]
    up_keep, up_taken, down_keep, down_taken = refs.own
    keep_up = [up_keep] + list(refs.far_keep_up)
    taken_up = [up_taken] + list(refs.far_taken_up)
    keep_down = [down_keep] + list(refs.far_keep_down)
    taken_down = [down_taken] + list(refs.far_taken_down)
    load_sem, fetch_sem, store_sem = refs.load_sem[0], refs.fetch_sem[0], refs.store_sem[0]
    store_there, stored_here = refs.store_there[0], refs.stored_here[0]
    pass_sem = refs.pass_sem[0]
    blocks, _, model_width = rows_all.shape
    part = up_all.shape[2]
    count = blocks * capacity
    depth = model_width // shards
    power = z_size & (z_size - 1) == 0
    together = 2 if power and z_size > 1 else 1
    group_rows = together * y_size * capacity

    source_z, target_z = grid.source_z, grid.target_z

    def owner(place, core):
        return ((grid.x + place % half) % half) * 2 + (core + place // half) % 2

    def rows_of(place, core=None):
        core = grid.core if core is None else core
        return pl.ds(pl.multiple_of(owner(place, core) * depth, 16), depth)

    loads = [pltpu.make_async_copy(refs.rows_in[0], rows_all, load_sem.at[1])]
    late_count = 0
    if last and refs.cot_late:
        late_count = refs.cot_late[0].shape[1]
        loads.append(
            pltpu.make_async_copy(
                refs.cot_late[0], cot.at[:, pl.ds(capacity - late_count, late_count)], load_sem.at[4]
            )
        )
    loads.append(
        pltpu.make_async_copy(
            refs.cot_in[0].at[:, pl.ds(index * capacity, capacity - late_count)],
            cot.at[:, pl.ds(0, capacity - late_count)], load_sem.at[0],
        )
    )
    my_up, my_down = refs.my_up, refs.my_down
    swapped_up, swapped_down = refs.swapped_up, refs.swapped_down
    local_up = list(enumerate(my_up)) + [
        (half + number, array) for number, array in enumerate(swapped_up)
    ]
    local_down = list(enumerate(my_down)) + [
        (half + number, array) for number, array in enumerate(swapped_down)
    ]

    def fetch_up(place):
        return [
            pltpu.make_async_copy(
                array.at[rows_of(place), :], up_all.at[place, rows_of(shard), :],
                fetch_sem.at[place, number],
            )
            for number, (shard, array) in enumerate(local_up)
        ]

    fetched_down = {
        shard: pltpu.make_async_copy(
            array, down_all.at[shard], fetch_sem.at[shards + number, 0]
        )
        for number, (shard, array) in enumerate(local_down)
    }
    cross_down = {
        half + shard: links.copy(
            my_down[shard], down_all.at[half + shard], sibling, down_all.at[half + shard]
        )
        for shard in range(len(swapped_down), half)
    }
    cross_up = [
        links.copy(
            my_up[shard].at[rows_of(place, 1 - grid.core), :],
            up_all.at[place, rows_of(shard), :], sibling,
            up_all.at[place, rows_of(half + shard), :],
        )
        for shard in range(len(swapped_up), half)
        for place in range(shards)
    ]
    cross_next = [
        links.copy(source, target, sibling, target)
        for source, target in zip(refs.next_mine, refs.next_swapped)
    ]
    work = Exchange(
        grid, links, refs.own_sem[0],
        [
            (partial(plane_of, source, place), target)
            for source, place, target in zip(refs.moved_from, parts, refs.moved_to)
        ],
    )
    def member(z, y):
        return z * y_size + y

    def give_back(turn, hop):
        to = member(source_z(turn), (grid.y + hop) % y_size)
        origin = member(target_z(turn), (grid.y + y_size - hop) % y_size)
        pairs = []
        for number, (held, target) in enumerate(
            ((grad_rows, refs.back_rows[0]), (grad_gates, refs.back_gates[0]))
        ):
            sems = dict(
                send_sem=refs.back_send[0].at[number, turn, hop],
                recv_sem=refs.back_receive[0].at[number, turn, hop],
                device_id=(to, grid.fsdp), device_id_type=MESH,
            )
            pairs.append(
                (
                    pltpu.make_async_remote_copy(
                        src_ref=held.at[to], dst_ref=target.at[grid.exp], **sems
                    ),
                    pltpu.make_async_remote_copy(
                        src_ref=target.at[origin], dst_ref=target.at[origin], **sems
                    ),
                )
            )
        return pairs

    steps = [(turn, hop) for turn in range(z_size) for hop in range(y_size)]
    own_back = []
    if last:
        own_back = [
            pltpu.make_async_copy(held.at[grid.exp], target.at[grid.exp], load_sem.at[2 + number])
            for number, (held, target) in enumerate(
                ((grad_rows, refs.back_rows[0]), (grad_gates, refs.back_gates[0]))
            )
        ]

    for copy in loads:
        copy.start()
    order = list(range(shards))
    if not last:
        order = [(pair + 1) % half + side * half for pair in range(half) for side in (1, 0)]
    if last:
        for copy in fetched_down.values():
            copy.start()
    for place in order:
        if not last and place in fetched_down:
            fetched_down[place].start()
        for copy in fetch_up(place):
            copy.start()
    greet(
        [((grid.exp + hop) % grid.exp_size, grid.fsdp) for hop in range(1, grid.exp_size)]
        + chip_peers(grid)
    )
    for going, _ in list(cross_down.values()) + cross_up + cross_next:
        going.start()
    work.start()

    def place_at(position):
        hop = (position // 2 + 1) % half
        return hop + half * (1 - position % 2)

    def slot_rows():
        columns = gates[:, 0, :].T
        for block in range(blocks):
            piece = slice(block * capacity, (block + 1) * capacity)
            gate = columns[index * capacity : (index + 1) * capacity, block : block + 1]
            gate_column[piece, :] = gate
        slot_values = gate_column[...] * cot[...].reshape(count, model_width).astype(F32)
        slot_t[...] = slot_values.T.astype(BF16)
        if not last:
            slot_grad[...] = slot_values.astype(BF16)

    def wait_down(place):
        if place in fetched_down:
            fetched_down[place].wait()
        else:
            cross_down[place][1].wait_recv()

    def wait_crossed():
        for _, coming in cross_up:
            coming.wait_recv()

    def folded(value):
        return sum(value[:, start : start + 128] for start in range(0, value.shape[1], 128))

    def gate_rows(found, block):
        ones = jnp.ones((8, 128), F32)
        grad_gates[block] = lax.dot_general(
            ones, found, (((1,), (1,)), ((), ())), precision=lax.Precision.HIGHEST,
            preferred_element_type=F32,
        )

    def up_target(targets, hop, place):
        if hop == 0:
            return targets[0].at[rows_of(place), :]
        return targets[1].at[hop - 1, rows_of(place), :]

    def keep_stores(place, slot):
        return [
            pltpu.make_async_copy(
                grad_up.at[slot, rows_of(hop), :], up_target(keep_up, hop, place),
                store_sem.at[slot, hop],
            )
            for hop in range(half)
        ]

    def give_stores(place, slot):
        return [
            pltpu.make_async_remote_copy(
                src_ref=grad_up.at[slot, rows_of(half + hop), :],
                dst_ref=up_target(taken_up, hop, place),
                send_sem=store_there.at[slot, hop], recv_sem=stored_here.at[place, hop],
                device_id=sibling, device_id_type=MESH,
            )
            for hop in range(half)
        ]

    def down_store(slot):
        return pltpu.make_async_copy(grad_down.at[slot], keep_down[0], store_sem.at[slot, half])

    def down_give(hop, slot):
        target = taken_down[0] if hop == 0 else taken_down[1].at[hop - 1]
        return pltpu.make_async_remote_copy(
            src_ref=grad_down.at[slot], dst_ref=target,
            send_sem=store_there.at[slot, half], recv_sem=stored_here.at[hop, half],
            device_id=sibling, device_id_type=MESH,
        )

    def start_store(place, slot):
        for copy in keep_stores(place, slot) + give_stores(place, slot):
            copy.start()

        @pl.when(place == 0)
        def _():
            down_store(slot).start()

        for hop in range(half):

            @pl.when(place == half + hop)
            def _(hop=hop):
                down_give(hop, slot).start()

            if hop > 0:

                @pl.when(place == hop)
                def _(hop=hop):
                    keep_down[1][hop - 1] = grad_down[slot]

    def wait_store(place, slot):
        for copy in keep_stores(place, slot):
            copy.wait()
        for copy in give_stores(place, slot):
            copy.wait_send()

        @pl.when(place == 0)
        def _():
            down_store(slot).wait()

        for hop in range(half):

            @pl.when(place == half + hop)
            def _(hop=hop):
                down_give(hop, slot).wait_send()

    early_rows = part // 2 if last else 0
    early = []
    if last:
        early = [
            links.copy(
                keep_down[1].at[hop - 1, pl.ds(0, early_rows), :], refs.early_down[0].at[hop - 1],
                (grid.exp, grid.x_from(hop)), refs.early_down[0].at[hop - 1],
            )
            for hop in range(1, half)
        ]

    def sum_down():
        for hop in range(1, half):
            down_give(hop, 0).wait_recv()
            keep_down[1][hop - 1] = (
                keep_down[1][hop - 1].astype(F32) + taken_down[1][hop - 1].astype(F32)
            ).astype(BF16)
            if last:
                early[hop - 1][0].start()

    def fused(position, carry):
        place, slot = place_at(position), position % 2
        for copy in fetch_up(place):
            copy.wait()
        for which in range(shards):

            @pl.when(place == which)
            def _(which=which):
                wait_down(which)

        up, down = up_all[place], down_all[place]
        rows = rows_all[...].reshape(count, model_width)
        pieces = [slice(start, start + 256) for start in range(0, count, 256)]

        def products_of(piece):
            return matmul(rows[piece], up), contract_last(slot_grad[piece, :], down)

        raw = products_of(pieces[0])
        active_low, grad_low = [], []
        for number, piece in enumerate(pieces):
            hidden, grad_active = raw
            if number + 1 < len(pieces):
                raw = products_of(pieces[number + 1])
            activated, slope = gelu_parts(hidden)
            active_low.append(activated.astype(BF16))
            grad_low.append((grad_active * slope).astype(BF16))
            total[piece, :] += matmul(active_low[number], down)
            grad_total[piece, :] += contract_last(grad_low[number], up)
        active_low = jnp.concatenate(active_low, axis=0)
        grad_low = jnp.concatenate(grad_low, axis=0)

        @pl.when(position >= 2)
        def _():
            wait_store(place_at(position - 2), slot)

        grad_up[slot] = matmul(rows_t[...], grad_low).astype(BF16)
        grad_down[slot] = matmul(slot_t[...], active_low).T.astype(BF16)
        start_store(place, slot)
        return carry

    def group(step, carry):
        number = z_size // together - 1 - step
        turns = [number * together + more for more in range(together)]
        if together == 2:
            place_of_group = flipped(grid.z // 2, number, z_size // 2)
        else:
            place_of_group = source_z(number)
        members = pl.ds(place_of_group * together * y_size, together * y_size)
        span = pl.ds(pl.multiple_of(place_of_group * group_rows, 16), group_rows)
        rows = rows_all[members].reshape(group_rows, model_width)
        gate = gate_column[span, :]
        grad = jnp.zeros((group_rows, model_width), F32)
        products = jnp.zeros((group_rows, 128), F32)
        ahead = matmul(rows, up_all[0])
        for place in range(shards):
            hidden = ahead
            if place + 1 < shards:
                ahead = matmul(rows, up_all[place + 1])
            base = unscaled[place, span, :].astype(F32)
            activated, slope = gelu_parts(hidden)
            products = products + folded(activated * base)
            active_low = activated.astype(BF16)
            active[place, span, :] = active_low
            low = (gate * base * slope).astype(BF16)
            grad_hidden[place, span, :] = low
            grad = grad + contract_last(low, up_all[place])
            total[span, :] += matmul(active_low, down_all[place])
        grad_rows[members] = grad.astype(BF16).reshape(together * y_size, capacity, model_width)
        for hop in range(together * y_size):
            gate_rows(
                products[hop * capacity : (hop + 1) * capacity],
                place_of_group * together * y_size + hop,
            )
        for turn in turns:
            for hop in range(y_size):

                @pl.when(turn + hop > 0)
                def _(turn=turn, hop=hop):
                    for going, _ in give_back(turn, hop):
                        going.start()

        return carry

    def column(position, carry):
        place, slot = place_at(position), position % 2
        if half > 1:

            @pl.when(position == shards - 1)
            def _():
                sum_down()

        @pl.when(position >= 2)
        def _():
            wait_store(place_at(position - 2), slot)

        grad_up[slot] = matmul(rows_t[...], grad_hidden[place]).astype(BF16)
        grad_down[slot] = matmul(slot_t[...], active[place]).T.astype(BF16)
        start_store(place, slot)
        return carry

    for copy in loads[1:]:
        copy.wait()
    total[...] = jnp.zeros_like(total)
    slot_rows()
    if last:
        for place in range(shards):
            wait_down(place)
            unscaled[place] = contract_last(
                cot[...].reshape(count, model_width), down_all[place]
            ).astype(BF16)
        loads[0].wait()
        for place in range(shards):
            for copy in fetch_up(place):
                copy.wait()
        wait_crossed()
        lax.fori_loop(0, z_size // together, group, 0)
        for copy in own_back:
            copy.start()
        rows_t[...] = turned(rows_all[...].reshape(count, model_width)).astype(BF16)
        lax.fori_loop(0, shards, column, 0)
    else:
        loads[0].wait()
        rows_t[...] = turned(rows_all[...].reshape(count, model_width)).astype(BF16)
        grad_total[...] = jnp.zeros_like(grad_total)
        wait_crossed()
        lax.fori_loop(0, shards, fused, 0)
        grad_rows[...] = grad_total[...].astype(BF16).reshape(grad_rows.shape)
        for block in range(blocks):
            rows = total[block * capacity : (block + 1) * capacity, :].astype(BF16).astype(F32)
            gate_rows(folded(rows * cot[block].astype(F32)), block)

    rows_out = refs.rows_out[0]
    cot[...] = total[...].astype(BF16).reshape(blocks, capacity, model_width)
    out_copies = [pltpu.make_async_copy(cot, rows_out.at[:, index], load_sem.at[0])]
    for before in refs.outs_before:
        out_copies.append(
            pltpu.make_async_copy(before, rows_out.at[:, pl.ds(0, index)], load_sem.at[1])
        )
    for copy in out_copies:
        copy.start()
    for position in range(max(shards - 2, 0), shards):
        wait_store(place_at(position), position % 2)
    for place in range(shards):
        for copy in give_stores(place, 0):
            copy.wait_recv()
    down_give(0, 0).wait_recv()
    if half > 1:
        if not last:
            sum_down()
        keep_up[1][...] = (keep_up[1][...].astype(F32) + taken_up[1][...].astype(F32)).astype(BF16)
        passed = [
            (keep_up[1], refs.pass_up[0], 0),
            (keep_down[1].at[:, pl.ds(early_rows, part - early_rows), :], refs.pass_down[0], 1),
        ]
        for source, target, number in passed:
            out_copies.append(pltpu.make_async_copy(source, target, pass_sem.at[number]))
            out_copies[-1].start()
    for copy in out_copies:
        copy.wait()
    for going, coming in early:
        coming.wait_recv()
        going.wait_send()
    for going, coming in cross_next:
        coming.wait_recv()
        going.wait_send()
    for going, _ in list(cross_down.values()) + cross_up:
        going.wait_send()
    work.finish()
    if last:
        for turn, hop in steps[1:]:
            for going, coming in give_back(turn, hop):
                coming.wait_recv()
                going.wait_send()
        for copy in own_back:
            copy.wait()


class Bag:
    def __init__(self, layout, refs):
        start = 0
        for name, size in layout.items():
            setattr(self, name, refs[start : start + size])
            start += size


class Wanted:
    def groups(self):
        return list(self.__dict__.values())

    def layout(self):
        return {name: len(group) for name, group in self.__dict__.items()}


def run_expert(index, local, rows_in, gates, cotangent, cotangent_late, ups, downs, swapped, next_mine,
               moved, outs_before, collective_id):
    grid = Grid()
    half = len(ups)
    shards = 2 * half
    last = index == local - 1
    blocks, capacity, model_width = rows_in.shape
    part = downs[0].shape[0]
    count = blocks * capacity
    inputs, outputs, scratch = Wanted(), Wanted(), Wanted()
    inputs.cot_in = [(cotangent, ANYWHERE)]
    inputs.cot_late = [(array, ANYWHERE) for array in cotangent_late]
    inputs.rows_in = [(rows_in, ANYWHERE)]
    inputs.gates = [(gates, IN_VMEM)]
    inputs.my_up = [(array, ANYWHERE) for array in ups]
    inputs.my_down = [(array, ANYWHERE) for array in downs]
    inputs.swapped_up = [(array, ANYWHERE) for array in swapped[0]]
    inputs.swapped_down = [(array, ANYWHERE) for array in swapped[1]]
    inputs.next_mine = [(array, ANYWHERE) for array in next_mine]
    inputs.moved_from = [(array, ANYWHERE) for array, _ in moved]
    inputs.outs_before = [] if outs_before is None else [(outs_before, IN_VMEM)]

    up_shape, down_shape = (model_width, part), (part, model_width)
    outputs.rows_out = [(shape_of((blocks, index + 1, capacity, model_width), BF16), ANYWHERE)]
    own_up, own_down = shape_of(up_shape, BF16), shape_of(down_shape, BF16)
    outputs.own = [(own_up, ANYWHERE), (own_up, ANYWHERE), (own_down, ANYWHERE), (own_down, ANYWHERE)]
    outputs.pass_up = [(shape_of((half - 1,) + up_shape, BF16), ANYWHERE)] if half > 1 else []
    early_rows = part // 2 if last else 0
    late_down = (half - 1, part - early_rows, model_width)
    early_down = (half - 1, early_rows, model_width)
    outputs.pass_down = [(shape_of(late_down, BF16), ANYWHERE)] if half > 1 else []
    outputs.early_down = [(shape_of(early_down, BF16), ANYWHERE)] if half > 1 and last else []
    outputs.next_swapped = [(shape_of(array.shape, BF16), ANYWHERE) for array in next_mine]
    outputs.moved_to = [
        (
            shape_of((grid.exp_size,) + array.shape[(1 if place is None else 2) :], array.dtype),
            ANYWHERE,
        )
        for array, place in moved
    ]
    rows_shape, gate_shape = (blocks, capacity, model_width), (blocks, 8, capacity)
    if last:
        outputs.back_rows = [(shape_of(rows_shape, BF16), ANYWHERE)]
        outputs.back_gates = [(shape_of(gate_shape, F32), ANYWHERE)]
    else:
        outputs.grad_rows = [(shape_of(rows_shape, BF16), IN_VMEM)]
        outputs.grad_gates = [(shape_of(gate_shape, F32), IN_VMEM)]

    sems = lambda *shape: pltpu.SemaphoreType.DMA(shape)
    scratch.rows_all = [pltpu.VMEM(rows_shape, BF16)]
    scratch.cot = [pltpu.VMEM(rows_shape, BF16)]
    scratch.up_all = [pltpu.VMEM((shards,) + up_shape, BF16)]
    scratch.down_all = [pltpu.VMEM((shards,) + down_shape, BF16)]
    scratch.total = [pltpu.VMEM((count, model_width), F32)]
    if last:
        scratch.active = [pltpu.VMEM((shards, count, part), BF16)]
        scratch.grad_hidden = [pltpu.VMEM((shards, count, part), BF16)]
        scratch.unscaled = [pltpu.VMEM((shards, count, part), BF16)]
    else:
        scratch.grad_total = [pltpu.VMEM((count, model_width), F32)]
        scratch.slot_grad = [pltpu.VMEM((count, model_width), BF16)]
    if last:
        scratch.grad_rows = [pltpu.VMEM(rows_shape, BF16)]
        scratch.grad_gates = [pltpu.VMEM(gate_shape, F32)]
        scratch.back_send = [sems(2, grid.z_size, grid.y_size)]
        scratch.back_receive = [sems(2, grid.z_size, grid.y_size)]
    scratch.gate_column = [pltpu.VMEM((count, 1), F32)]
    scratch.rows_t = [pltpu.VMEM((model_width, count), BF16)]
    scratch.slot_t = [pltpu.VMEM((model_width, count), BF16)]
    scratch.grad_up = [pltpu.VMEM((2,) + up_shape, BF16)]
    scratch.grad_down = [pltpu.VMEM((2,) + down_shape, BF16)]
    far_up = [pltpu.VMEM((half - 1,) + up_shape, BF16)] * (1 if half > 1 else 0)
    far_down = [pltpu.VMEM((half - 1,) + down_shape, BF16)] * (1 if half > 1 else 0)
    scratch.far_keep_up, scratch.far_taken_up = far_up, far_up
    scratch.far_keep_down, scratch.far_taken_down = far_down, far_down
    scratch.load_sem = [sems(5)]
    scratch.pass_sem = [sems(3)]
    scratch.fetch_sem = [sems(2 * shards, shards)]
    scratch.store_sem = [sems(2, half + 1)]
    scratch.store_there = [sems(2, half + 1)]
    scratch.stored_here = [sems(shards, half + 1)]
    copies = len(moved) * grid.exp_size + half * (shards + 2) + len(next_mine)
    scratch.send = [sems(copies)]
    scratch.receive = [sems(copies)]
    scratch.own_sem = [sems(max(len(moved), 1))]

    layout = {**inputs.layout(), **outputs.layout(), **scratch.layout()}

    def body(*refs):
        expert_kernel(
            *refs, layout=layout, index=index, local=local, half=half, capacity=capacity,
            parts=[place for _, place in moved],
        )

    results = pl.pallas_call(
        body,
        in_specs=[spec for group in inputs.groups() for _, spec in group],
        out_specs=tuple(spec for group in outputs.groups() for _, spec in group),
        out_shape=tuple(shape for group in outputs.groups() for shape, _ in group),
        scratch_shapes=[item for group in scratch.groups() for item in group],
        compiler_params=params(collective_id=collective_id, has_side_effects=True),
        cost_estimate=hint(45),
        name=f"expert_{index}",
    )(*[array for group in inputs.groups() for array, _ in group])
    return Bag(outputs.layout(), results)


def local_picks(routes, slots, capacity, local, index, slot_count):
    member, which = lax.div(routes, local), lax.rem(routes, local)
    places = jnp.where(which == index, member * capacity + slots, -1)
    lane = lax.broadcasted_iota(jnp.int32, (routes.shape[0], slot_count), 1)
    return [lane == places[:, k : k + 1] for k in range(2)]


def unroute_kernel(
    hidden, cotangent, routed, probabilities, gates, plane, columns, counts, attention_out, context,
    *refs, experts, local, token_total, lanes, heads, width,
):
    grads, gate_grads = refs[:local], refs[local : 2 * local]
    (
        grad_hidden, small, grad_t, grad_n, grad_out, branches, own_out, total, send, receive, own_sem,
    ) = refs[2 * local :]
    grid = Grid().here()
    links = Links(send, receive)
    rows, model_width = hidden.shape
    members, capacity = grads[0].shape[0], grads[0].shape[1]
    head_rows = heads * width
    fetch = pltpu.make_async_copy(
        attention_out.at[pl.ds(pl.multiple_of(grid.fsdp * head_rows, 16), head_rows), :], own_out,
        own_sem.at[0],
    )
    fetch.start()
    greet(chip_peers(grid))
    extra = plane[:, lanes.base :]
    gains = extra.astype(F32).T[lanes.gain : lanes.gain + 1]
    half_rows = rows // 2
    sibling = grid.sibling(grid.fsdp)
    small_t = jnp.zeros((lanes.extra, model_width), F32)
    gain_grad = jnp.zeros((1, model_width), F32)
    along_x, across = [], []
    for half in range(2):
        here = slice(half * half_rows, (half + 1) * half_rows)
        grad_output = cotangent[here, :].astype(F32)
        routes = columns[here, 0:2].astype(jnp.int32)
        slots = columns[here, 2:4].astype(jnp.int32)
        member, which = lax.div(routes, local), lax.rem(routes, local)
        lane = lax.broadcasted_iota(jnp.int32, (half_rows, capacity), 1)
        grad_routed = jnp.zeros((half_rows, model_width), F32)
        found = [jnp.zeros((half_rows, capacity), F32), jnp.zeros((half_rows, capacity), F32)]
        for index in range(local):
            picks = local_picks(routes, slots, capacity, local, index, members * capacity)
            grad_routed = grad_routed + matmul(
                jnp.where(picks[0] | picks[1], 1.0, 0.0).astype(BF16),
                grads[index][...].reshape(members * capacity, model_width),
            )
            for place in range(members):
                spots = jnp.where((which == index) & (member == place), slots, -1)
                for k in range(2):
                    found[k] = found[k] + jnp.where(
                        lane == spots[:, k : k + 1], gate_grads[index][place, 0:1, :], 0.0
                    )
        grad_gates = [jnp.sum(found[k], axis=1, keepdims=True) for k in range(2)]
        powers = probabilities[here, :]
        lane = expert_lane(powers.shape, lanes)
        inside = (lane >= 0) & (lane < experts)
        picked = [lane == routes[:, k : k + 1] for k in range(2)]
        chosen_total = sum(
            jnp.sum(jnp.where(picked[k], powers, 0.0), axis=1, keepdims=True) for k in range(2)
        )
        weighted = grad_gates[0] * gates[here, 0:1] + grad_gates[1] * gates[here, 1:2]
        grad_mass = (AUX_WEIGHT * experts / (2.0 * token_total * token_total)) * counts[0:1, :]
        grad_mass = jnp.where(inside, grad_mass, 0.0)
        for k in range(2):
            grad_mass = grad_mass + jnp.where(
                picked[k], (grad_gates[k] - weighted) / chosen_total, 0.0
            )
        grad_logits = powers * (grad_mass - jnp.sum(powers * grad_mass, axis=1, keepdims=True))
        grad_routed = grad_routed + contract_last(grad_logits.astype(BF16), extra)
        hidden_state = hidden[here, :]
        scale = lax.rsqrt(jnp.mean(hidden_state * hidden_state, axis=1, keepdims=True) + EPSILON)
        normed = hidden_state * scale
        product = grad_routed * normed
        grad = scale * (
            grad_routed * gains - normed * jnp.mean(product * gains, axis=1, keepdims=True)
        ) + grad_output
        grad_hidden[here, :] = grad
        branches[grid.fsdp, here, :] = grad.astype(BF16)
        mine = branches.at[grid.fsdp, here, :]
        for hop in range(1, grid.x_size):
            along_x.append(
                links.copy(
                    mine, mine, (grid.exp, grid.x_from(hop)),
                    branches.at[grid.x_from(-hop), here, :],
                )
            )
            along_x[-1][0].start()
        across.append(
            links.copy(mine, mine, (grid.exp, sibling), branches.at[sibling, here, :])
        )
        across[-1][0].start()
        gain_grad = gain_grad + jnp.sum(product, axis=0, keepdims=True)
        small_t = small_t + matmul(grad_logits.T.astype(BF16), routed[here, :])

    def context_grad(place):
        branch = branches[place]
        grad = contract_last(own_out[...], branch).astype(BF16)
        columns_here = pl.ds(pl.multiple_of(place * rows, 128), rows)
        rows_here = pl.ds(pl.multiple_of(place * rows, 16), rows)
        for head in range(heads):
            piece = grad[head * width : (head + 1) * width]
            grad_t[head, :, columns_here] = piece
            grad_n[head, rows_here, :] = turned(piece).astype(BF16)
        total[...] += matmul(context[place], branch)

    total[...] = jnp.zeros_like(total)
    fetch.wait()
    context_grad(grid.fsdp)
    forwards = []
    for half in range(2):
        here = slice(half * half_rows, (half + 1) * half_rows)
        for hop in range(1, grid.x_size):
            along_x[half * (grid.x_size - 1) + hop - 1][1].wait_recv()
            held = grid.x_from(-hop)
            forwards.append(
                links.copy(
                    branches.at[held, here, :], branches.at[held, here, :], (grid.exp, sibling),
                    branches.at[grid.sibling(held), here, :],
                )
            )
            forwards[-1][0].start()
    row = lax.broadcasted_iota(jnp.int32, small_t.shape, 0)
    small[...] = jnp.where(row == lanes.gain, gain_grad, small_t).T
    for _, coming in across:
        coming.wait_recv()
    context_grad(sibling)
    for hop in range(1, grid.x_size):
        context_grad(grid.x_from(-hop))
    for _, coming in forwards:
        coming.wait_recv()
    for hop in range(1, grid.x_size):
        context_grad(grid.sibling(grid.x_from(-hop)))
    grad_out[...] = total[...].astype(BF16)
    for going, _ in along_x + across + forwards:
        going.wait_send()


def project_back_kernel(
    grad_projected, normed, plane, small, probabilities, grad_bias, grad_first, grad_plane, total,
    bias_t, *, lanes, heads, feature_rows, bucket_rows,
):
    step = pl.program_id(0)

    @pl.when(step == 0)
    def _():
        total[...] = jnp.zeros_like(total)

    grad = grad_projected[...]
    grad_first[0] = matmul(plane[:, : lanes.weights], grad).astype(BF16)
    total[: lanes.weights, :] += matmul(grad, normed[...])

    @pl.when(step == pl.num_programs(0) - 1)
    def _():
        grad_plane[...] = total[...].T.astype(BF16)
        span = grad_bias.shape[2]
        select, _ = bucket_rows_select(plane.shape[0], feature_rows, bucket_rows, span)
        bias_t[...] = jnp.zeros_like(bias_t)
        first = lanes.table + lax.axis_index("fsdp") * heads
        for head in range(heads):
            bias_t[pl.ds(first + head, 1), :] = grad_bias[head]
        high = bias_t[...].astype(BF16)
        rest = (bias_t[...] - high.astype(F32)).astype(BF16)
        table = contract_last(select, high) + contract_last(select, rest)
        mass = jnp.sum(probabilities[...], axis=0, keepdims=True)
        mass = pltpu.roll(jnp.broadcast_to(mass, (8, lanes.extra)), lanes.shift, 1)[0:1]
        lane = lax.broadcasted_iota(jnp.int32, table.shape, 1)
        row = lax.broadcasted_iota(jnp.int32, table.shape, 0)
        is_small = (lane >= lanes.router) & (lane < lanes.table)
        is_mass = (lane >= lanes.count) & (lax.rem(row, feature_rows) == 0)
        extra = table + jnp.where(is_small, small[...], 0.0) + jnp.where(is_mass, mass, 0.0)
        grad_plane[:, lanes.base :] = (total[lanes.base :, :].T + extra).astype(BF16)


def last_kernel(
    first, planes, out_grad, hidden, gates, columns, rows_back, first_parts, output, plane_parts,
    out_parts, first_in, first_sum, planes_in, plane_sum, along_in, reduced, rows_held, send, receive,
    own, *, spread_out, local,
):
    fetch = pltpu.make_async_copy(rows_back, rows_held, own.at[2])
    fetch.start()
    grid = Grid().here()
    links = Links(send, receive)
    z_size, y_size, x_size, fsdp_size = grid.z_size, grid.y_size, grid.x_size, grid.fsdp_size
    exp_size = grid.exp_size
    sibling = grid.sibling(grid.fsdp)
    near = [
        (grid.exp, (grid.fsdp + turn) % fsdp_size) for turn in range(1, fsdp_size)
    ] + [grid.at(z=(grid.z + hop) % z_size) for hop in range(1, z_size)]
    beside = [grid.at(y=(grid.y + hop) % y_size) for hop in range(1, y_size)]

    per_sender = grid.device_count if spread_out else exp_size
    base = 0 if spread_out else grid.fsdp * exp_size
    out_sends = []
    for number in range(per_sender):
        to = base + number
        out_sends.append((to, number))
    if spread_out:
        out_origins = [(origin, origin) for origin in range(grid.device_count)]
    else:
        out_origins = [
            (member * fsdp_size + grid.linear // exp_size, member) for member in range(exp_size)
        ]
    own_slot = grid.linear if spread_out else grid.exp
    out_base = links.used
    links.used += per_sender

    def place_of(linear):
        return (linear // fsdp_size, linear % fsdp_size)

    def out_copy(to, number, slot):
        return pltpu.make_async_remote_copy(
            src_ref=out_grad.at[number], dst_ref=out_parts.at[slot],
            send_sem=send.at[out_base + number], recv_sem=receive.at[out_base + slot],
            device_id=place_of(to), device_id_type=MESH,
        )

    barrier = pltpu.get_barrier_semaphore()
    for device in near + beside:
        pl.semaphore_signal(barrier, inc=1, device_id=device, device_id_type=MESH)
    for origin, _ in out_origins:

        @pl.when(origin != grid.linear)
        def _(origin=origin):
            pl.semaphore_signal(
                barrier, inc=1, device_id=place_of(origin), device_id_type=MESH
            )

    to_self = (
        1 if spread_out else jnp.where(grid.linear // exp_size == grid.fsdp, 1, 0)
    )
    pl.semaphore_wait(barrier, len(near) + len(beside) + per_sender - to_self)

    for to, number in out_sends:

        @pl.when(to != grid.linear)
        def _(to=to, number=number):
            out_copy(to, number, own_slot).start()

        @pl.when(to == grid.linear)
        def _(number=number):
            pltpu.make_async_copy(out_grad.at[number], out_parts.at[own_slot], own.at[0]).start()

    first_copies = []
    for hop in range(x_size):
        mine = grid.x_from(hop)
        first_copies.append(
            links.copy(
                first.at[grid.sibling(mine)], first_in.at[hop], (grid.exp, sibling), first_in.at[hop]
            )
        )
        first_copies[-1][0].start()
    z_hops = list(range(1, z_size)) + [0]
    beside_copies = []
    for z_hop in z_hops:
        beside_copies.append([])
        for hop in range(1, y_size):
            to = (grid.y + hop) % y_size
            landing = planes_in.at[hop - 1, z_hop]
            beside_copies[-1].append(
                links.copy(
                    planes.at[(grid.z + z_hop) % z_size, to], landing, grid.at(y=to), landing
                )
            )
            beside_copies[-1][-1][0].start()
    along_x = []
    for hop in range(x_size):
        first_copies[hop][1].wait_recv()
        summed = first[grid.x_from(hop)].astype(F32) + first_in[hop].astype(F32)
        if hop == 0:
            first_parts[0] = summed.astype(BF16)
        else:
            first_sum[hop - 1] = summed.astype(BF16)
            along_x.append(
                links.copy(
                    first_sum.at[hop - 1], first_parts.at[hop], (grid.exp, grid.x_from(hop)),
                    first_parts.at[hop],
                )
            )
            along_x[-1][0].start()
    along_z = []
    for z_hop, copies in zip(z_hops, beside_copies):
        to_z = (grid.z + z_hop) % z_size
        summed = planes[to_z, grid.y].astype(F32)
        for number, (_, coming) in enumerate(copies):
            coming.wait_recv()
            summed = summed + planes_in[number, z_hop].astype(F32)
        plane_sum[z_hop] = summed.astype(BF16)
        if z_hop > 0:
            along_z.append(
                links.copy(
                    plane_sum.at[z_hop], along_in.at[z_hop - 1], grid.at(z=to_z),
                    along_in.at[z_hop - 1],
                )
            )
            along_z[-1][0].start()
    fetch.wait()
    mix_rows(hidden, gates, columns, rows_held, output, local)
    summed = plane_sum[0].astype(F32)
    for number, (_, coming) in enumerate(along_z):
        coming.wait_recv()
        summed = summed + along_in[number].astype(F32)
    reduced[...] = summed.astype(BF16)
    placed = []
    for turn in range(1, fsdp_size):
        to = (grid.fsdp + turn) % fsdp_size
        origin = (grid.fsdp + fsdp_size - turn) % fsdp_size
        placed.append(
            links.copy(
                reduced.at[to], plane_parts.at[grid.fsdp], (grid.exp, to), plane_parts.at[origin]
            )
        )
        placed[-1][0].start()
    kept = pltpu.make_async_copy(reduced.at[grid.fsdp], plane_parts.at[grid.fsdp], own.at[1])
    kept.start()
    for going, coming in along_x + placed:
        coming.wait_recv()
    for going, _ in first_copies + along_x + along_z + placed:
        going.wait_send()
    for copies in beside_copies:
        for going, _ in copies:
            going.wait_send()
    kept.wait()
    for origin, slot in out_origins:

        @pl.when(origin != grid.linear)
        def _(origin=origin, slot=slot):
            out_copy(origin, 0, slot).wait_recv()

    for to, number in out_sends:

        @pl.when(to != grid.linear)
        def _(to=to, number=number):
            out_copy(to, number, own_slot).wait_send()

        @pl.when(to == grid.linear)
        def _(number=number):
            pltpu.make_async_copy(out_grad.at[number], out_parts.at[own_slot], own.at[0]).wait()


def mix_rows(hidden, gates, columns, rows_in, output, local):
    members, _, capacity, model_width = rows_in.shape
    routes, slots = int_columns(columns)
    total = hidden[...]
    picked = [jnp.zeros(hidden.shape, F32), jnp.zeros(hidden.shape, F32)]
    for index in range(local):
        picks = local_picks(routes, slots, capacity, local, index, members * capacity)
        values = rows_in[:, index].reshape(members * capacity, model_width)
        for k in range(2):
            picked[k] = picked[k] + matmul(jnp.where(picks[k], 1.0, 0.0).astype(BF16), values)
    for k in range(2):
        total = total + gates[:, k : k + 1] * picked[k]
    output[...] = total.astype(BF16)


def finish_kernel(
    first_parts, plane_parts, out_parts, tokens, grad_hidden, attention_in, attention_gain, counts,
    grad_tokens, grad_gain, grad_in, grad_out, grad_mixture, grad_router, grad_table, balance,
    *, lanes, heads, width, head_count, experts, token_total,
):
    total = jnp.sum(first_parts[...].astype(F32), axis=0).T
    inputs = tokens[...].astype(F32)
    scale = lax.rsqrt(jnp.mean(inputs * inputs, axis=1, keepdims=True) + EPSILON)
    normed = inputs * scale
    grad_tokens[...] = grad_hidden[...] + scale * (
        total - normed * jnp.mean(total * normed, axis=1, keepdims=True)
    )
    fsdp_size = plane_parts.shape[0]
    model_width = head_count * width
    sums = [plane_parts[place].astype(F32) for place in range(fsdp_size)]
    columns = []
    for kind in range(3):
        pieces = [
            sums[place][:, kind * heads * width : (kind + 1) * heads * width]
            for place in range(fsdp_size)
        ]
        columns.append(jnp.concatenate(pieces, axis=1)[:, :model_width])
    gathered = jnp.concatenate(columns, axis=1)
    feature_rows = gathered.shape[0]
    gain = jnp.sum(gathered * attention_in[...].astype(F32), axis=1, keepdims=True)
    gain = padded_rows(jnp.broadcast_to(gain, (feature_rows, 128)), 128).T
    grad_gain[...] = gain[0:1, :feature_rows]
    grad_in[...] = gathered * as_column(attention_gain[...], feature_rows)
    grad_out[...] = jnp.sum(out_parts[...].astype(F32), axis=0)
    extra = sum(part[:, lanes.base :] for part in sums)
    extra_t = padded_rows(extra, 128).T
    grad_mixture[...] = extra_t[lanes.gain : lanes.gain + 1, :feature_rows]
    grad_router[...] = extra_t[lanes.router : lanes.router + experts, :feature_rows]
    grad_table[...] = extra[: grad_table.shape[0], lanes.table : lanes.table + head_count]
    mass = jnp.broadcast_to(extra[0:1], (8, lanes.extra))
    mass = pltpu.roll(mass, lanes.extra - lanes.shift, 1)
    lane = expert_lane(mass.shape, lanes)
    terms = jnp.where((lane >= 0) & (lane < experts), mass * counts[...], 0.0)[0:1]
    balance[...] = jnp.sum(terms, axis=1, keepdims=True) * (
        experts / (2.0 * token_total * token_total)
    )


def sum_kernel(*refs, layout, local):
    outputs = refs[len(layout) :]
    early_blocks = pl.num_programs(0) // 2
    totals = {}
    number = 0
    while number < len(layout):
        index, which, halves = layout[number]
        shape = outputs[which].shape[1:]
        value = refs[number][...].reshape(shape).astype(F32)
        if halves:
            rest = refs[number + 1][...].reshape(shape).astype(F32)
            value = jnp.where(pl.program_id(0) < early_blocks, value, rest)
            number += 1
        totals[index, which] = totals[index, which] + value if (index, which) in totals else value
        number += 1
    for (index, which), total in totals.items():
        outputs[which][index] = total


def sum_grads(groups, up_shape, down_shape, blocks):
    local = len(groups)
    depth, part = up_shape[1], down_shape[1]
    sizes = ((depth, part), (part // blocks, down_shape[2]))
    arrays, specs, layout = [], [], []
    early = blocks // 2
    for index, group in enumerate(groups):
        for which, (size, (keep, taken, passed)) in enumerate(zip(sizes, group)):
            for array in (keep, taken, *passed):
                if isinstance(array, tuple):
                    arrays.extend(array)
                    specs.append(pl.BlockSpec(size, lambda c: (jnp.minimum(c, early - 1), 0)))
                    specs.append(pl.BlockSpec(size, lambda c: (jnp.maximum(c - early, 0), 0)))
                    layout.extend([(index, which, True)] * 2)
                else:
                    arrays.append(array)
                    specs.append(pl.BlockSpec(size, lambda c: (c, 0)))
                    layout.append((index, which, False))
    return pl.pallas_call(
        partial(sum_kernel, layout=layout, local=local),
        grid=(blocks,),
        in_specs=specs,
        out_specs=[
            pl.BlockSpec((local, depth, part), lambda c: (0, 0, c)),
            pl.BlockSpec((local, part // blocks, down_shape[2]), lambda c: (0, c, 0)),
        ],
        out_shape=(shape_of(up_shape, F32), shape_of(down_shape, F32)),
        compiler_params=params(),
        cost_estimate=hint(8),
        name="sum_grads",
    )(*arrays)


def over_x(array, hop):
    fsdp_size = lax.axis_size("fsdp")
    return lax.ppermute(array, "fsdp", [(i, (i + 2 * hop) % fsdp_size) for i in range(fsdp_size)])


def over_core(array):
    return lax.ppermute(array, "fsdp", [(i, i ^ 1) for i in range(lax.axis_size("fsdp"))])


def on_device(
    tokens,
    cotangent,
    segments,
    routes,
    slots,
    attention_gain,
    mixture_gain,
    attention_in,
    attention_out,
    router_weight,
    position_table,
    expert_up,
    expert_down,
):
    grid = Grid()
    exp_size, fsdp_size, chips = grid.exp_size, grid.fsdp_size, grid.x_size
    device_count = grid.device_count
    fsdp_index = lax.axis_index("fsdp")
    rows, model_width = tokens.shape
    length = rows * fsdp_size
    head_count = position_table.shape[1]
    width = model_width // head_count
    heads = -(-head_count // fsdp_size)
    padded_heads = heads * fsdp_size
    feature_rows, bucket_rows = attention_in.shape[0], position_table.shape[0]
    experts = router_weight.shape[1]
    local = expert_up.shape[0]
    capacity = 4 * rows // experts
    token_total = rows * device_count
    span = WINDOW + 2 * SKEW + QUERY_BLOCK
    lanes = Lanes(heads, width, padded_heads, experts)
    part = expert_down.shape[1]
    gain_row = attention_gain.reshape(1, feature_rows)
    late_rows = 2 * capacity // 3 if local > 1 and capacity % 48 == 0 else 0
    late = 1 if late_rows else 0

    shard_shapes = [shape_of((model_width, part), BF16), shape_of((part, model_width), BF16)]
    copies = (
        4 * fsdp_size + grid.z_size + grid.z_size * grid.y_size
        + grid.z_size + grid.y_size + grid.x_size + 1
    )
    started = pl.pallas_call(
        partial(
            start_kernel, lanes=lanes, heads=heads, width=width, head_count=head_count,
            experts=experts, capacity=capacity, local=local, late=late,
        ),
        out_shape=tuple(
            [
                shape_of((fsdp_size, rows, model_width), BF16),
                shape_of((grid.z_size, grid.y_size, fsdp_size, feature_rows, lanes.width), BF16),
                shape_of((exp_size, local * capacity - late_rows, model_width), BF16),
                shape_of((8, rows), F32),
                shape_of((rows, 128), F32),
                shape_of((grid.z_size, grid.y_size, chips, 2, feature_rows, model_width), BF16),
            ]
            + [shape_of((exp_size, late_rows, model_width), BF16)] * late
            + shard_shapes * local
        ),
        in_specs=[IN_VMEM] * 10 + [ANYWHERE] * 2,
        out_specs=tuple(
            [ANYWHERE, ANYWHERE, IN_VMEM, IN_VMEM, IN_VMEM, ANYWHERE]
            + [IN_VMEM] * late
            + [ANYWHERE] * (2 * local)
        ),
        scratch_shapes=[
            pltpu.VMEM((fsdp_size, feature_rows, lanes.width), BF16),
            pltpu.VMEM(expert_up.shape, BF16),
            pltpu.VMEM(expert_down.shape, BF16),
            dma_sems(copies),
            dma_sems(copies),
            dma_sems(3),
            dma_sems(2 * local),
            dma_sems(local * (fsdp_size + 1)),
        ],
        compiler_params=params(collective_id=0, has_side_effects=True),
        cost_estimate=hint(20),
        name="start",
    )(
        tokens, cotangent, routes.T, slots.T, gain_row, mixture_gain.reshape(1, feature_rows),
        attention_in, router_weight.T, position_table, attention_out, expert_up, expert_down,
    )
    all_tokens, all_planes, cotangent_early, position_rows, columns, full_out = started[:6]
    cotangent_late, started = started[6 : 6 + late], started[6 + late :]
    own_shards = [started[2 * index : 2 * index + 2] for index in range(local)]
    plane = all_planes.reshape(model_width, lanes.width)
    full_out = full_out.reshape(model_width, model_width)

    def along_x(array):
        return [over_x(array, -hop) for hop in range(1, chips)]

    near_up, near_down = [None] * local, [None] * local
    near_up[0] = along_x(own_shards[0][0])
    cotangent_in = lax.all_to_all(
        cotangent_early, "exp", split_axis=0, concat_axis=0, tiled=True
    )

    head_t = lambda size: pl.BlockSpec((heads, size, rows), lambda s, *_: (0, 0, s))
    head_n = lambda size: pl.BlockSpec((heads, rows, size), lambda s, *_: (0, s, 0))
    normed, query_t, key_n, query_n, value_n, key_t, value_t, bias, counts = pl.pallas_call(
        partial(
            project_kernel, heads=heads, width=width, lanes=lanes, feature_rows=feature_rows,
            bucket_rows=bucket_rows,
        ),
        grid=(fsdp_size,),
        in_specs=[
            pl.BlockSpec((1, rows, model_width), lambda s: (s, 0, 0)),
            whole((model_width, lanes.width)),
            pl.BlockSpec((1, rows), lambda s: (0, s)),
        ],
        out_specs=[
            pl.BlockSpec((rows, model_width), lambda s: (s, 0)),
            head_t(SKEW), head_n(SKEW), head_n(width), head_n(width), head_t(width), head_t(width),
            whole((heads, 1, span)),
            whole((8, lanes.extra)),
        ],
        out_shape=(
            shape_of((length, model_width), BF16),
            shape_of((heads, SKEW, length), BF16),
            shape_of((heads, length, SKEW), BF16),
            shape_of((heads, length, width), BF16),
            shape_of((heads, length, width), BF16),
            shape_of((heads, width, length), BF16),
            shape_of((heads, width, length), BF16),
            shape_of((heads, 1, span), F32),
            shape_of((8, lanes.extra), F32),
        ),
        scratch_shapes=[
            pltpu.VMEM((lanes.weights, model_width), BF16),
            pltpu.VMEM((lanes.extra, span), F32),
        ],
        compiler_params=params(),
        cost_estimate=hint(8),
        name="project",
    )(all_tokens, plane, segments.reshape(1, length))

    by_head = lambda *size: pl.BlockSpec((1,) + size, lambda h: (h, 0, 0))
    context, context_high, log_total, attended_t = pl.pallas_call(
        partial(attend_kernel, rows=rows),
        grid=(heads,),
        in_specs=[
            by_head(SKEW, length), by_head(length, SKEW), by_head(width, length), by_head(1, span),
        ],
        out_specs=[
            pl.BlockSpec((fsdp_size, width, rows), lambda h: (0, h, 0)),
            by_head(width, length),
            by_head(1, length),
            ANYWHERE,
        ],
        out_shape=(
            shape_of((fsdp_size, heads * width, rows), BF16),
            shape_of((heads, width, length), F32),
            shape_of((heads, 1, length), F32),
            shape_of((fsdp_size, heads * width, rows), BF16),
        ),
        scratch_shapes=[
            pltpu.VMEM((SKEW, span), F32),
            pltpu.VMEM((WINDOW + QUERY_BLOCK, QUERY_BLOCK), F32),
            pltpu.VMEM((heads, fsdp_size, width, rows), BF16),
            pltpu.SemaphoreType.DMA((heads, fsdp_size)),
            pltpu.SemaphoreType.DMA((heads, fsdp_size)),
            dma_sems(heads),
        ],
        compiler_params=params(collective_id=1, has_side_effects=True),
        cost_estimate=hint(13),
        name="attend",
    )(query_t, key_n, value_t, bias)

    own_down, near_up[0], attended_t = lax.optimization_barrier(
        (own_shards[0][1], near_up[0], attended_t)
    )
    near_down[0] = along_x(own_down)
    attended_t = attended_t.reshape(padded_heads * width, rows)

    later = [own_shards[index] for index in range(1, local)]
    attended_t, later = lax.optimization_barrier((attended_t, later))
    for index in range(1, local):
        near_up[index], near_down[index] = [along_x(array) for array in later[index - 1]]
    gate_lanes = -(-local * capacity // 128) * 128
    ready = [own_shards[0][0]] + near_up[0] + [own_shards[0][1]]
    copies = 2 * exp_size + len(ready)
    hidden, routed, probabilities, gates, outgoing, rows_in, gates_in, *crossed = pl.pallas_call(
        partial(
            route_kernel, experts=experts, lanes=lanes, capacity=capacity, crossing=len(ready)
        ),
        in_specs=[IN_VMEM] * 6 + [ANYWHERE] * len(ready),
        out_specs=tuple([IN_VMEM] * 5 + [ANYWHERE] * (2 + len(ready))),
        out_shape=tuple(
            [
                shape_of((rows, model_width), F32),
                shape_of((rows, model_width), BF16),
                shape_of((rows, lanes.extra), F32),
                shape_of((rows, 2), F32),
                shape_of((exp_size, local * capacity, model_width), BF16),
                shape_of((exp_size, capacity, model_width), BF16),
                shape_of((exp_size, 8, gate_lanes), F32),
            ]
            + [shape_of(array.shape, BF16) for array in ready]
        ),
        scratch_shapes=[
            pltpu.VMEM((exp_size, 8, gate_lanes), F32),
            dma_sems(copies),
            dma_sems(copies),
            dma_sems(2),
        ],
        compiler_params=params(collective_id=2, has_side_effects=True),
        cost_estimate=hint(35),
        name="route",
    )(tokens, attended_t, full_out, plane, columns, position_rows, *ready)
    outgoing = outgoing.reshape(exp_size, local, capacity, model_width)

    def down_parts(early, rest):
        return list(zip(early, rest))

    def pass_along(arrays):
        return [over_x(arrays[0][hop - 1], hop) for hop in range(1, chips)]

    swapped = (crossed[:-1], crossed[-1:])
    returned, groups, moved, outs = [], [], [], None
    late_rows_in = ()
    for index in range(local):
        final = index == local - 1
        carried = list(moved)
        if not final:
            carried.append((outgoing, index + 1))
        if index == 0 and late:
            carried.append((cotangent_late[0], None))
        result = run_expert(
            index, local, rows_in, gates_in, cotangent_in, late_rows_in if final else (),
            [own_shards[index][0]] + near_up[index], [own_shards[index][1]] + near_down[index],
            swapped, () if final else own_shards[index + 1], carried, outs, 3 + index,
        )
        (outs,) = result.rows_out
        arrived = list(result.moved_to)
        if index == 0 and late:
            late_rows_in = (arrived.pop(),)
        if not final:
            rows_in = arrived.pop()
            swapped = (result.next_swapped[:1], result.next_swapped[1:])
            moved = [(result.grad_rows[0], None), (result.grad_gates[0], None)]
        if arrived:
            returned.append(arrived)
        up_keep, up_taken, down_keep, down_taken = result.own
        if not final:
            passed = (result.pass_up, result.pass_down)
            passed, rows_in = lax.optimization_barrier((passed, rows_in))
            groups.append(
                [
                    (up_keep, up_taken, pass_along(passed[0])),
                    (down_keep, down_taken, pass_along(passed[1])),
                ]
            )
    returned.append([result.back_rows[0], result.back_gates[0]])
    groups, returned = lax.optimization_barrier((groups, returned))

    outs, returned = lax.optimization_barrier((outs, returned))
    out_rows = lax.all_to_all(outs, "exp", split_axis=0, concat_axis=0, tiled=True)

    padded_out = full_out
    if padded_heads > head_count:
        padded_out = jnp.pad(full_out, ((0, padded_heads * width - model_width), (0, 0)))
    copies = 2 * 2 * fsdp_size
    grad_hidden, small, grad_t, grad_n, out_grad = pl.pallas_call(
        partial(
            unroute_kernel, experts=experts, local=local, token_total=token_total, lanes=lanes,
            heads=heads, width=width,
        ),
        out_shape=(
            shape_of((rows, model_width), F32),
            shape_of((model_width, lanes.extra), F32),
            shape_of((heads, width, length), BF16),
            shape_of((heads, length, width), BF16),
            shape_of((heads * width, model_width), BF16),
        ),
        in_specs=[IN_VMEM] * 8 + [ANYWHERE] + [IN_VMEM] * (1 + 2 * local),
        out_specs=tuple([IN_VMEM] * 5),
        scratch_shapes=[
            pltpu.VMEM((fsdp_size, rows, model_width), BF16),
            pltpu.VMEM((heads * width, model_width), BF16),
            pltpu.VMEM((heads * width, model_width), F32),
            dma_sems(copies),
            dma_sems(copies),
            dma_sems(1),
        ],
        compiler_params=params(collective_id=4 + local, has_side_effects=True),
        cost_estimate=hint(1),
        name="unroute",
    )(
        hidden, cotangent, routed, probabilities, gates, plane, columns, counts, padded_out, context,
        *[part[0] for part in returned], *[part[1] for part in returned],
    )
    pass_up, pass_down, grad_t = lax.optimization_barrier(
        (result.pass_up, result.pass_down, grad_t)
    )
    early = [result.early_down[0][hop] for hop in range(chips - 1)]
    groups.append(
        [
            (up_keep, up_taken, pass_along(pass_up)),
            (down_keep, down_taken, down_parts(early, pass_along(pass_down))),
        ]
    )

    grad_projected, grad_bias = pl.pallas_call(
        partial(attend_back_kernel, scale=width ** (-0.5)),
        grid=(heads,),
        in_specs=[
            by_head(SKEW, length), by_head(length, SKEW), by_head(length, width),
            by_head(length, width), by_head(width, length), by_head(width, length),
            by_head(length, width), by_head(width, length), by_head(1, length), by_head(1, span),
        ],
        out_specs=[
            pl.BlockSpec((3, 1, width, length), lambda h: (0, h, 0, 0)),
            by_head(1, span),
        ],
        out_shape=(
            shape_of((3, heads, width, length), BF16),
            shape_of((heads, 1, span), F32),
        ),
        scratch_shapes=[
            pltpu.VMEM((SKEW, span), F32),
            pltpu.VMEM((SKEW, span), F32),
            pltpu.VMEM((length, width), F32),
            pltpu.VMEM((length, width), F32),
        ],
        compiler_params=params(),
        cost_estimate=hint(1),
        name="attend_back",
    )(query_t, key_n, query_n, value_n, key_t, grad_t, grad_n, context_high, log_total, bias)
    grad_projected = grad_projected.reshape(lanes.weights, length)

    grad_first, grad_plane = pl.pallas_call(
        partial(
            project_back_kernel, lanes=lanes, heads=heads, feature_rows=feature_rows,
            bucket_rows=bucket_rows,
        ),
        grid=(fsdp_size,),
        in_specs=[
            pl.BlockSpec((lanes.weights, rows), lambda s: (0, s)),
            pl.BlockSpec((rows, model_width), lambda s: (s, 0)),
            whole((model_width, lanes.width)),
            whole((model_width, lanes.extra)),
            whole((rows, lanes.extra)),
            whole((heads, 1, span)),
        ],
        out_specs=[
            pl.BlockSpec((1, model_width, rows), lambda s: (s, 0, 0)),
            whole((model_width, lanes.width)),
        ],
        out_shape=(
            shape_of((fsdp_size, model_width, rows), BF16),
            shape_of((model_width, lanes.width), BF16),
        ),
        scratch_shapes=[
            pltpu.VMEM((lanes.width, model_width), F32),
            pltpu.VMEM((lanes.extra, span), F32),
        ],
        compiler_params=params(),
        cost_estimate=hint(1),
        name="project_back",
    )(grad_projected, normed, plane, small, probabilities, grad_bias)

    out_rows, grad_first = lax.optimization_barrier((out_rows, grad_first))
    spread_out = heads * width * fsdp_size != model_width
    if spread_out:
        out_grad = lax.dynamic_update_slice(
            jnp.zeros((padded_heads * width, model_width), BF16), out_grad,
            (fsdp_index * heads * width, jnp.int32(0)),
        )[:model_width]
    out_grad = out_grad.reshape(-1, feature_rows, model_width)
    out_count = device_count if spread_out else exp_size
    plane_shape = (grid.z_size, grid.y_size, fsdp_size, feature_rows, lanes.width)
    parts_shape = (fsdp_size, feature_rows, lanes.width)
    copies = 4 * fsdp_size + grid.z_size * grid.y_size + grid.z_size + out_count
    first_parts, layer_output, plane_parts, out_parts = pl.pallas_call(
        partial(last_kernel, spread_out=spread_out, local=local),
        out_shape=(
            shape_of((chips, model_width, rows), BF16),
            shape_of((rows, model_width), BF16),
            shape_of(parts_shape, BF16),
            shape_of((out_count, feature_rows, model_width), BF16),
        ),
        in_specs=[IN_VMEM] * 6 + [ANYWHERE],
        out_specs=(IN_VMEM, IN_VMEM, ANYWHERE, ANYWHERE),
        scratch_shapes=[
            pltpu.VMEM((chips, model_width, rows), BF16),
            pltpu.VMEM((max(chips - 1, 1), model_width, rows), BF16),
            pltpu.VMEM((max(grid.y_size - 1, 1), grid.z_size) + parts_shape, BF16),
            pltpu.VMEM((grid.z_size,) + parts_shape, BF16),
            pltpu.VMEM((max(grid.z_size - 1, 1),) + parts_shape, BF16),
            pltpu.VMEM(parts_shape, BF16),
            pltpu.VMEM(out_rows.shape, BF16),
            dma_sems(copies),
            dma_sems(copies),
            dma_sems(3),
        ],
        compiler_params=params(collective_id=5 + local, has_side_effects=True),
        cost_estimate=hint(1),
        name="last",
    )(grad_first, grad_plane.reshape(plane_shape), out_grad, hidden, gates, columns, out_rows)

    groups, first_parts = lax.optimization_barrier((groups, first_parts))
    (
        grad_tokens, gain_grad, in_grad, out_sum, mixture_gain_grad, router_grad, table_grad, balance,
    ) = pl.pallas_call(
        partial(
            finish_kernel, lanes=lanes, heads=heads, width=width, head_count=head_count,
            experts=experts, token_total=token_total,
        ),
        out_shape=(
            shape_of((rows, model_width), F32),
            shape_of((1, feature_rows), F32),
            shape_of((feature_rows, 3 * model_width), F32),
            shape_of((feature_rows, model_width), F32),
            shape_of((1, feature_rows), F32),
            shape_of((experts, feature_rows), F32),
            shape_of((bucket_rows, head_count), F32),
            shape_of((1, 1), F32),
        ),
        compiler_params=params(),
        cost_estimate=hint(6),
        name="finish",
    )(first_parts, plane_parts, out_parts, tokens, grad_hidden, attention_in, gain_row, counts)

    up_grad, down_grad = sum_grads(groups, expert_up.shape, expert_down.shape, fsdp_size)
    return (
        layer_output,
        balance.reshape(()),
        grad_tokens,
        gain_grad.reshape(feature_rows),
        mixture_gain_grad.reshape(feature_rows),
        in_grad,
        out_sum,
        router_grad.T,
        table_grad,
        up_grad,
        down_grad,
    )


def solution(mesh):
    in_specs = (
        P(("exp", "fsdp"), None),
        P(("exp", "fsdp"), None),
        P("exp"),
        P(("exp", "fsdp"), None),
        P(("exp", "fsdp"), None),
        P(("exp", "fsdp")),
        P(("exp", "fsdp")),
        P(("exp", "fsdp"), None),
        P(("exp", "fsdp"), None),
        P(("exp", "fsdp"), None),
        P(("exp", "fsdp"), None),
        P("exp", "fsdp", None),
        P("exp", "fsdp", None),
    )
    out_specs = (
        P(("exp", "fsdp"), None),
        P(),
        P(("exp", "fsdp"), None),
        P(("exp", "fsdp")),
        P(("exp", "fsdp")),
        P(("exp", "fsdp"), None),
        P(("exp", "fsdp"), None),
        P(("exp", "fsdp"), None),
        P(("exp", "fsdp"), None),
        P("exp", "fsdp", None),
        P("exp", "fsdp", None),
    )
    return jax.shard_map(
        on_device, mesh=mesh, in_specs=in_specs, out_specs=out_specs, check_vma=False
    )
```
